32 devices in a mesh: dp: 2 (over y), ctx: 16 (over z, x, core).
Axes of the slice: x: 2, y: 2, z: 4, core: 2. Of those that a mesh axis runs over, the one named last changes fastest.
Arguments:
- tokens: bfloat16 [2, 2048, 896], P('dp', 'ctx'), may hold values from -6 to 6
- w_qkv: bfloat16 [896, 1152], P('dp'), may hold values from -0.1875 to 0.1875
- b_qkv: float32 [1152], replicated, may hold values from -3 to 3
- w_out: bfloat16 [896, 896], P('dp'), may hold values from -6 to 6
- gain_attn: float32 [896], replicated, may hold values from 0.5 to 1.5
- gain_mlp: float32 [896], replicated, may hold values from 0.5 to 1.5
- w_gate: bfloat16 [896, 4864], P(None, 'dp'), may hold values from -0.1875 to 0.1875
- w_up: bfloat16 [896, 4864], P(None, 'dp'), may hold values from -0.1875 to 0.1875
- w_down: bfloat16 [4864, 896], P('dp'), may hold values from -0.078125 to 0.078125
- cotangent: bfloat16 [2, 2048, 896], P('dp', 'ctx'), may hold values from -6 to 6
Outputs:
- output: bfloat16 [2, 2048, 896], P('dp', 'ctx')
- grad_tokens: float32 [2, 2048, 896], P('dp', 'ctx')
- grad_w_qkv: float32 [896, 1152], P('dp')
- grad_b_qkv: float32 [1152], replicated
- grad_w_out: float32 [896, 896], P('dp')
- grad_gain_attn: float32 [896], replicated
- grad_gain_mlp: float32 [896], replicated
- grad_w_gate: float32 [896, 4864], P(None, 'dp')
- grad_w_up: float32 [896, 4864], P(None, 'dp')
- grad_w_down: float32 [4864, 896], P('dp')
The draws below stay inside these ranges and needn't reach their ends.
All inputs are finite; a program needn't handle non-finite values.
Results may differ from the reference program's by a relative error of at most 0.015.
Values may be sent and summed in bfloat16 or wider, within the bound.
No kernel may reach another device: no remote copies, remote signals or barrier semaphores. Data moves between devices by JAX's collectives and lax.ppermute only.
A program may use at most 192 MiB of HBM per device.

```python
import jax
import jax.numpy as jnp
from jax import lax

D = 896
QH = 14
KH = 2
HD = 64
FF = 4864
BLK = 64
BLOCKS = 32
SEQ = 2048
SEQS = 2
QKV = 1152


def shard_levels(key, dims, shards, low, largest):
    def one(dim, parts):
        draws = jax.random.uniform(jax.random.fold_in(jax.random.fold_in(key, 6), dim), (parts,), jnp.float32, low / len(shards), largest / len(shards))
        return jnp.repeat(jnp.exp(draws), dims[dim] // parts).reshape((-1,) + (1,) * (len(dims) - dim - 1))

    level = one(*shards[0])
    for cut in shards[1:]:
        level = level * one(*cut)
    return level


def centred(stream_key, dims, width, most, cuts=(), held_as=jnp.bfloat16):
    level = shard_levels(stream_key, dims, cuts, -0.22, 0.18) if cuts else 1.0
    values = jax.random.normal(stream_key, dims, jnp.float32) * width * level
    return jnp.minimum(jnp.maximum(values, -most), most).astype(held_as)


def setup_inputs(seed: int = 0) -> dict:
    arg_keys = jax.random.split(jax.random.key(seed), 11)
    return {
        "tokens": centred(arg_keys[0], (SEQS, SEQ, D), 1.0, 6.0, ((0, 2), (1, 16))),
        "w_qkv": centred(arg_keys[1], (D, QKV), D ** -0.5, 0.1875, ((0, 2),)),
        "b_qkv": centred(arg_keys[2], (QKV,), 0.5, 3.0, (), jnp.float32),
        "w_out": centred(arg_keys[3], (QH * HD, D), 1 ** -0.5, 6.0, ((0, 2),)),
        "gain_attn": jnp.clip(1.0 + 0.1 * jax.random.normal(arg_keys[4], (D,), jnp.float32), 0.5, 1.5),
        "gain_mlp": jnp.clip(1.0 + 0.1 * jax.random.normal(arg_keys[5], (D,), jnp.float32), 0.5, 1.5),
        "w_gate": centred(arg_keys[6], (D, FF), D ** -0.5, 0.1875, ((1, 2),)),
        "w_up": centred(arg_keys[7], (D, FF), D ** -0.5, 0.1875, ((1, 2),)),
        "w_down": centred(arg_keys[8], (FF, D), FF ** -0.5, 0.078125, ((0, 2),)),
        "cotangent": centred(arg_keys[9], (SEQS, SEQ, D), 1.0, 6.0, ((0, 2), (1, 16))),
    }


EPS = 1e-06
ROPE_BASE = 1000000.0
HIGH = lax.Precision.HIGHEST

@jax.custom_vjp
def low(v):
    return lax.optimization_barrier(v.astype(jnp.bfloat16)).astype(jnp.float32)

@jax.custom_vjp
def low_back(v):
    return v

def low_keep(v):
    return (low(v), None)

def low_pass(kept, grad):
    return (grad,)

def back_keep(v):
    return (v, None)

def back_low(kept, grad):
    return (low(grad),)
low.defvjp(low_keep, low_pass)
low_back.defvjp(back_keep, back_low)

def positions():
    index_rows = jnp.arange(SEQ, dtype=jnp.int32)
    block_no = index_rows // BLK
    device = block_no // 2
    start = jnp.where(block_no % 2 == 0, device, BLOCKS - 1 - device)
    return (start * BLK + index_rows % BLK).astype(jnp.int32)

def rotary_tables(place):
    freq = ROPE_BASE ** (-(jnp.arange(HD // 2).astype(jnp.float32) * (2.0 / HD)))
    angle = place.astype(jnp.float32)[:, None] * freq[None, :]
    angle = jnp.concatenate([angle, angle], 1)
    return (jnp.cos(angle), jnp.sin(angle))

def rotate_apply(heads, cosine, sine):
    first = heads[..., :HD // 2]
    second = heads[..., HD // 2:]
    turned = jnp.concatenate([-second, first], -1)
    return heads * cosine[:, None, :] + turned * sine[:, None, :]

def rms_scale(values, gain):
    return values * lax.rsqrt(lax.optimization_barrier(jnp.mean(values * values, -1, keepdims=True)) + EPS) * gain

def attention(queries, keys, values, place):
    group_size = QH // KH
    query_block = min(512, SEQ)
    query_parts = queries.reshape(SEQ // query_block, query_block, KH, group_size, HD)
    place_parts = place.reshape(SEQ // query_block, query_block)

    def one_block(pieces):
        query_piece, query_place = pieces
        scores = jnp.einsum('qhgd,khd->hgqk', query_piece, keys, precision=HIGH) * HD ** (-0.5)
        scores = low_back(scores)
        allowed = place[None, None, None, :] <= query_place[None, None, :, None]
        scores = jnp.where(allowed, scores, -1e+30)
        top = lax.optimization_barrier(jnp.max(scores, -1, keepdims=True))
        expo = jnp.exp(scores - top)
        probs = low(expo / lax.optimization_barrier(jnp.sum(expo, -1, keepdims=True)))
        return jnp.einsum('hgqk,khd->qhgd', probs, values, precision=HIGH)
    result = lax.map(jax.checkpoint(one_block), (query_parts, place_parts))
    return result.reshape(SEQ, QH * HD)

def forward_sequence(seq_in, w_qkv, b_qkv, w_out, gain_attn, gain_mlp, w_gate, w_up, w_down):
    place = positions()
    cosine, sine = rotary_tables(place)
    normed = low(rms_scale(seq_in, gain_attn))
    joint = low_back(jnp.dot(normed, w_qkv, precision=HIGH) + b_qkv)
    queries = joint[:, :QH * HD].reshape(SEQ, QH, HD)
    keys = joint[:, QH * HD:(QH + KH) * HD].reshape(SEQ, KH, HD)
    values = joint[:, (QH + KH) * HD:].reshape(SEQ, KH, HD)
    queries = low(rotate_apply(queries, cosine, sine))
    keys = low(rotate_apply(keys, cosine, sine))
    values = low(values)
    attended = low(low_back(attention(queries, keys, values, place)))
    hidden = seq_in + low_back(jnp.dot(attended, w_out, precision=HIGH))
    normed_two = low(rms_scale(hidden, gain_mlp))
    gate = low_back(jnp.dot(normed_two, w_gate, precision=HIGH))
    upper = low_back(jnp.dot(normed_two, w_up, precision=HIGH))
    middle = low(jax.nn.silu(gate) * upper)
    return hidden + low_back(jnp.dot(middle, w_down, precision=HIGH))

def forward_all(tokens, w_qkv, b_qkv, w_out, gain_attn, gain_mlp, w_gate, w_up, w_down):

    def one_sequence(seq_in):
        return forward_sequence(seq_in, w_qkv, b_qkv, w_out, gain_attn, gain_mlp, w_gate, w_up, w_down)
    return lax.map(one_sequence, tokens)

def reference(tokens, w_qkv, b_qkv, w_out, gain_attn, gain_mlp, w_gate, w_up, w_down, cotangent):
    primal = (tokens.astype(jnp.float32), w_qkv.astype(jnp.float32), b_qkv.astype(jnp.float32), w_out.astype(jnp.float32), gain_attn.astype(jnp.float32), gain_mlp.astype(jnp.float32), w_gate.astype(jnp.float32), w_up.astype(jnp.float32), w_down.astype(jnp.float32))
    result, pullback = jax.vjp(forward_all, *primal)
    grads = pullback(cotangent.astype(jnp.float32))
    return (result.astype(jnp.bfloat16), grads[0], grads[1], grads[2], grads[3], grads[4], grads[5], grads[6], grads[7], grads[8])
```

```python
import jax
import jax.numpy as jnp
from jax import lax
from jax.sharding import PartitionSpec as P

D = 896
QH = 14
KH = 2
HD = 64
GROUP = QH // KH
WIDTH_Q = QH * HD
WIDTH_K = KH * HD

EPS = 1e-06
ROPE_BASE = 1000000.0

f32 = jnp.float32
bf16 = jnp.bfloat16


def rotary_tables(place):
    freq = ROPE_BASE ** (-(jnp.arange(HD // 2).astype(f32) * (2.0 / HD)))
    angle = place.astype(f32)[:, None] * freq[None, :]
    angle = jnp.concatenate([angle, angle], 1)
    return (jnp.cos(angle), jnp.sin(angle))


def rotate_apply(heads, cosine, sine):
    first = heads[..., : HD // 2]
    second = heads[..., HD // 2 :]
    turned = jnp.concatenate([-second, first], -1)
    return heads * cosine[:, None, :] + turned * sine[:, None, :]


def rotate_back(grads, cosine, sine):
    scaled = grads * sine[:, None, :]
    first = scaled[..., : HD // 2]
    second = scaled[..., HD // 2 :]
    return grads * cosine[:, None, :] + jnp.concatenate([second, -first], -1)


def ring_order(chips):
    if chips % 2:
        return list(range(chips))
    rows = chips // 2
    return [2 * i for i in range(rows)] + [2 * i + 1 for i in reversed(range(rows))]


def half_cut(rows):
    cut = (rows // 2 + 7) // 8 * 8
    return cut if cut < rows else rows // 2


class Net:
    def __init__(self):
        self.dp = lax.axis_size("dp")
        self.ctx = lax.axis_size("ctx")
        self.chips = self.ctx // 2
        self.order = ring_order(self.chips)
        self.d = lax.axis_index("dp")
        self.c = lax.axis_index("ctx")
        self.core = self.c % 2
        place = [0] * self.chips
        for spot, chip in enumerate(self.order):
            place[chip] = spot
        self.pos = jnp.array(place, jnp.int32)[self.c // 2]

    def swap(self, x):
        return lax.ppermute(x, "ctx", [(i, i ^ 1) for i in range(self.ctx)])

    def shift(self, x, step):
        n = self.dp
        return lax.ppermute(x, "dp", [(i, (i + step) % n) for i in range(n)])

    def hop(self, x, step):
        n = self.chips
        perm = []
        for spot in range(n):
            for core in range(2):
                perm.append((2 * self.order[spot] + core, 2 * self.order[(spot + step) % n] + core))
        return lax.ppermute(x, "ctx", perm)

    def owner(self, slot):
        return (self.pos - slot) % self.chips

    def group_gather(self, x):
        parts = [x] + [self.shift(x, s) for s in range(1, self.dp)]
        parts = parts + [self.swap(p) for p in parts]
        return jnp.concatenate(parts, 0)

    def group_scatter(self, x, rows):
        half = self.dp * rows
        mine = x[:half] + self.swap(x[half:].astype(bf16)).astype(f32)
        total = mine[:rows]
        for s in range(1, self.dp):
            got = self.shift(mine[s * rows : (s + 1) * rows].astype(bf16), self.dp - s)
            total = total + got.astype(f32)
        return total

    def ring_gather(self, x):
        n = self.chips
        half = n // 2
        cut = half_cut(x.shape[0])
        found = [x] + [None] * (n - 1)
        fwd, back = x, x
        for s in range(1, half):
            fwd = self.hop(fwd, 1)
            back = self.hop(back, -1)
            found[s] = fwd
            found[n - s] = back
        found[half] = jnp.concatenate([self.hop(fwd[:cut], 1), self.hop(back[cut:], -1)], 0)
        return found

    def ring_scatter(self, local):
        n = self.chips
        half = n // 2
        cut = half_cut(local[half].shape[0])

        def add(got, mine):
            return (got.astype(f32) + mine.astype(f32)).astype(bf16)

        fwd = self.hop(local[half][:cut], 1)
        back = self.hop(local[half][cut:], -1)
        for s in range(1, half):
            mine_f = local[half + s]
            mine_b = local[half - s]
            if s == 1:
                mine_f = jnp.concatenate([add(fwd, mine_f[:cut]), mine_f[cut:]], 0)
                mine_b = jnp.concatenate([mine_b[:cut], add(back, mine_b[cut:])], 0)
            else:
                mine_f = add(fwd, mine_f)
                mine_b = add(back, mine_b)
            fwd = self.hop(mine_f, 1)
            back = self.hop(mine_b, -1)
        return fwd.astype(f32) + back.astype(f32) + local[0].astype(f32)

    def full_rows(self, shard):
        rows = shard.shape[0]
        half = rows // 2
        full = jnp.zeros((rows * self.dp, shard.shape[1]), shard.dtype)
        full = lax.dynamic_update_slice(full, shard, (self.d * rows, 0))
        piece = lax.dynamic_slice(shard, (self.core * half, 0), (half, shard.shape[1]))
        for s in range(1, self.dp):
            got = self.shift(piece, s)
            other = self.swap(got)
            base = ((self.d - s) % self.dp) * rows
            full = lax.dynamic_update_slice(full, got, (base + self.core * half, 0))
            full = lax.dynamic_update_slice(full, other, (base + (1 - self.core) * half, 0))
        return full

    def total(self, x):
        x = x + self.swap(x)
        bit = 1
        while bit < self.chips:
            x = x + lax.ppermute(x, "ctx", [(i, i ^ (2 * bit)) for i in range(self.ctx)])
            bit *= 2
        bit = 1
        while bit < self.dp:
            x = x + lax.ppermute(x, "dp", [(i, i ^ bit) for i in range(self.dp)])
            bit *= 2
        return x


def local(tokens, w_qkv, b_qkv, w_out, gain_attn, gain_mlp, w_gate, w_up, w_down, cotangent):
    net = Net()
    rows = tokens.shape[1]
    half_rows = rows // 2
    ctx_count = net.ctx
    core = net.core
    chips = net.chips
    scale = HD ** (-0.5)

    w_qkv_full = net.full_rows(w_qkv)
    w_out_full = net.full_rows(w_out)
    grad_out_low = cotangent[0]
    grad_out_group = net.group_gather(grad_out_low)

    ff_loc = w_gate.shape[1]
    ff_half = ff_loc // 2
    main = (ff_half // 128) * 128
    rest = ff_half - main
    width = main + 2 * rest
    first = core * main
    own_cols = (jnp.arange(width) + first < ff_half) == (core == 0)
    wg = lax.dynamic_slice(w_gate, (0, first), (D, width))
    wu = lax.dynamic_slice(w_up, (0, first), (D, width))
    wd = lax.dynamic_slice(w_down, (first, 0), (width, D))

    resid_in = tokens[0].astype(f32)
    row_ids = jnp.arange(half_rows, dtype=jnp.int32)
    query_place = jnp.concatenate(
        [net.c * half_rows + row_ids, (2 * ctx_count - 1 - net.c) * half_rows + row_ids]
    )
    cosine, sine = rotary_tables(query_place)
    inverse_one = lax.rsqrt(jnp.mean(resid_in * resid_in, -1, keepdims=True) + EPS)
    unit_one = resid_in * inverse_one
    normed_one = (unit_one * gain_attn).astype(bf16)
    joint = jnp.dot(normed_one, w_qkv_full, preferred_element_type=f32) + b_qkv
    queries = rotate_apply(joint[:, :WIDTH_Q].reshape(rows, QH, HD), cosine, sine).astype(bf16)
    queries = queries.reshape(rows, KH, GROUP, HD)
    keys_local = rotate_apply(
        joint[:, WIDTH_Q : WIDTH_Q + WIDTH_K].reshape(rows, KH, HD), cosine, sine
    ).astype(bf16)
    values_local = joint[:, WIDTH_Q + WIDTH_K :].astype(bf16)
    local_pairs = jnp.concatenate([keys_local.reshape(rows, WIDTH_K), values_local], 1)

    slots = net.ring_gather(local_pairs)
    mine = jnp.concatenate(slots, 0)
    all_pairs = jnp.concatenate([mine, net.swap(mine)], 0)
    order = jnp.array(net.order, jnp.int32)
    chip_ids = order[(net.pos - jnp.arange(chips, dtype=jnp.int32)) % chips]
    slot_ids = jnp.concatenate([2 * chip_ids + core, 2 * chip_ids + 1 - core])
    key_place = jnp.concatenate(
        [
            slot_ids[:, None] * half_rows + row_ids[None],
            (2 * ctx_count - 1 - slot_ids)[:, None] * half_rows + row_ids[None],
        ],
        1,
    ).reshape(-1)

    total_keys = all_pairs.shape[0]
    key_block = min(1024, total_keys)
    block_count = total_keys // key_block
    pair_blocks = all_pairs.reshape(block_count, key_block, 2 * WIDTH_K)
    place_blocks = key_place.reshape(block_count, key_block)

    def block_scores(pair_block, place_block):
        key_heads = pair_block[:, :WIDTH_K].reshape(key_block, KH, HD)
        value_heads = pair_block[:, WIDTH_K:].reshape(key_block, KH, HD)
        scores = (
            jnp.einsum("qhgd,khd->hgqk", queries, key_heads, preferred_element_type=f32) * scale
        )
        allowed = place_block[None, None, None, :] <= query_place[None, None, :, None]
        return (jnp.where(allowed, scores, -1e30), key_heads, value_heads)

    def gather_stats(carry, pieces):
        run_max, run_sum = carry
        scores, key_heads, value_heads = block_scores(pieces[0], pieces[1])
        new_max = jnp.maximum(run_max, jnp.max(scores, -1, keepdims=True))
        run_sum = run_sum * jnp.exp(run_max - new_max) + jnp.sum(
            jnp.exp(scores - new_max), -1, keepdims=True
        )
        return ((new_max, run_sum), None)

    start_max = jnp.full((KH, GROUP, rows, 1), -1e30, f32)
    start_sum = jnp.zeros((KH, GROUP, rows, 1), f32)
    (run_max, run_sum), unused = lax.scan(
        gather_stats, (start_max, start_sum), (pair_blocks, place_blocks)
    )
    log_total = run_max + jnp.log(run_sum)

    def weighted_sum(acc, pieces):
        scores, key_heads, value_heads = block_scores(pieces[0], pieces[1])
        probs_low = jnp.exp(scores - log_total).astype(bf16)
        acc = acc + jnp.einsum("hgqk,khd->qhgd", probs_low, value_heads, preferred_element_type=f32)
        return (acc, None)

    attended, unused = lax.scan(
        weighted_sum, jnp.zeros((rows, KH, GROUP, HD), f32), (pair_blocks, place_blocks)
    )
    attended_low = attended.reshape(rows, WIDTH_Q).astype(bf16)
    hidden = resid_in + jnp.dot(attended_low, w_out_full, preferred_element_type=f32)
    inverse_two = lax.rsqrt(jnp.mean(hidden * hidden, -1, keepdims=True) + EPS)
    unit_two = hidden * inverse_two
    normed_two = (unit_two * gain_mlp).astype(bf16)

    normed_two_group = net.group_gather(normed_two)
    gate = jnp.dot(normed_two_group, wg, preferred_element_type=f32)
    upper = jnp.dot(normed_two_group, wu, preferred_element_type=f32)
    sigma = jax.nn.sigmoid(gate)
    activated = gate * sigma
    middle = jnp.where(own_cols, activated * upper, 0.0).astype(bf16)
    grad_middle = jnp.einsum("td,fd->tf", grad_out_group, wd, preferred_element_type=f32)
    slope = sigma * (1.0 + gate * (1.0 - sigma))
    grad_gate_low = jnp.where(own_cols, grad_middle * upper * slope, 0.0).astype(bf16)
    grad_up_low = jnp.where(own_cols, grad_middle * activated, 0.0).astype(bf16)

    part_down = jnp.einsum(
        "tf,td->fd", middle, grad_out_group, preferred_element_type=f32
    ).astype(bf16)
    part_down = lax.dynamic_slice(part_down, (core * rest, 0), (ff_half, D))
    down_rows = ff_half // chips

    def down_chunk(slot):
        return lax.dynamic_slice(part_down, (net.owner(slot) * down_rows, 0), (down_rows, D))

    sum_down = net.ring_scatter([down_chunk(s) for s in range(chips)]).astype(bf16)
    sum_down = lax.optimization_barrier(sum_down)

    def split_main(x):
        left = (x[:, :main], x[:, main:])
        right = (x[:, 2 * rest :], x[:, : 2 * rest])
        return (
            jnp.where(core == 0, left[0], right[0]),
            jnp.where(core == 0, left[1], right[1]),
        )

    gate_main, gate_tile = split_main(grad_gate_low)
    up_main, up_tile = split_main(grad_up_low)
    packed = jnp.concatenate(
        [gate_main, up_main, gate_tile + jnp.roll(up_tile, rest, 1)], 1
    )
    part_mlp = jnp.einsum(
        "td,tf->df", normed_two_group, packed, preferred_element_type=f32
    ).astype(bf16)
    mlp_rows = D // chips

    def mlp_chunk(slot):
        return lax.dynamic_slice(
            part_mlp, (net.owner(slot) * mlp_rows, 0), (mlp_rows, 2 * ff_half)
        )

    sum_mlp = net.ring_scatter([mlp_chunk(s) for s in range(chips)]).astype(bf16)
    sum_mlp = lax.optimization_barrier(sum_mlp)

    grad_normed_two = jnp.einsum(
        "tf,df->td", grad_gate_low, wg, preferred_element_type=f32
    ) + jnp.einsum("tf,df->td", grad_up_low, wu, preferred_element_type=f32)
    grad_normed_two = net.group_scatter(grad_normed_two, rows)
    mlp_out = jnp.dot(middle, wd, preferred_element_type=f32)
    output = (hidden + net.group_scatter(mlp_out, rows)).astype(bf16)
    grad_out = grad_out_low.astype(f32)
    grad_gain_two = jnp.sum(grad_normed_two * unit_two, 0)
    scaled_two = grad_normed_two * gain_mlp
    grad_hidden = grad_out + inverse_two * (
        scaled_two - unit_two * jnp.mean(scaled_two * unit_two, -1, keepdims=True)
    )
    grad_attn_low = grad_hidden.astype(bf16)
    grad_heads = jnp.einsum(
        "td,cd->tc", grad_attn_low, w_out_full, preferred_element_type=f32
    ).astype(bf16)
    grad_heads = grad_heads.reshape(rows, KH, GROUP, HD)
    delta = jnp.sum(grad_heads.astype(f32) * attended, -1)
    delta = jnp.transpose(delta, (1, 2, 0))[..., None]

    def attention_back(grad_queries, pieces):
        scores, key_heads, value_heads = block_scores(pieces[0], pieces[1])
        probs = jnp.exp(scores - log_total)
        probs_low = probs.astype(bf16)
        grad_probs = jnp.einsum(
            "qhgd,khd->hgqk", grad_heads, value_heads, preferred_element_type=f32
        )
        grad_scores = (probs * (grad_probs - delta)).astype(bf16)
        grad_queries = grad_queries + jnp.einsum(
            "hgqk,khd->qhgd", grad_scores, key_heads, preferred_element_type=f32
        )
        grad_keys = (
            jnp.einsum("hgqk,qhgd->khd", grad_scores, queries, preferred_element_type=f32) * scale
        )
        grad_values = jnp.einsum(
            "hgqk,qhgd->khd", probs_low, grad_heads, preferred_element_type=f32
        )
        joined = jnp.concatenate(
            [grad_keys.reshape(key_block, WIDTH_K), grad_values.reshape(key_block, WIDTH_K)], 1
        )
        return (grad_queries, joined)

    grad_queries, pair_terms = lax.scan(
        attention_back, jnp.zeros((rows, KH, GROUP, HD), f32), (pair_blocks, place_blocks)
    )
    pair_terms = pair_terms.reshape(2, chips, rows, 2 * WIDTH_K)
    pair_sums = pair_terms[0] + net.swap(pair_terms[1].astype(bf16)).astype(f32)
    pair_sums = pair_sums.astype(bf16)
    grad_pairs = net.ring_scatter([pair_sums[s] for s in range(chips)])
    grad_queries = rotate_back((grad_queries * scale).reshape(rows, QH, HD), cosine, sine)
    grad_keys = rotate_back(grad_pairs[:, :WIDTH_K].reshape(rows, KH, HD), cosine, sine)
    grad_joint_low = jnp.concatenate(
        [
            grad_queries.reshape(rows, WIDTH_Q),
            grad_keys.reshape(rows, WIDTH_K),
            grad_pairs[:, WIDTH_K:],
        ],
        1,
    ).astype(bf16)
    grad_bias = jnp.sum(grad_joint_low.astype(f32), 0)
    grad_normed_one = jnp.einsum(
        "tc,dc->td", grad_joint_low, w_qkv_full, preferred_element_type=f32
    )
    grad_gain_one = jnp.sum(grad_normed_one * unit_one, 0)
    scaled_one = grad_normed_one * gain_attn
    grad_input = grad_hidden + inverse_one * (
        scaled_one - unit_one * jnp.mean(scaled_one * unit_one, -1, keepdims=True)
    )
    small = net.total(jnp.concatenate([grad_gain_one, grad_gain_two, grad_bias]))

    q_rows = w_qkv.shape[0] // 2
    q_first = net.d * (2 * q_rows) + core * q_rows
    attended_group = lax.dynamic_slice(
        net.group_gather(attended_low), (0, q_first), (2 * net.dp * rows, q_rows)
    )
    normed_one_group = lax.dynamic_slice(
        net.group_gather(normed_one), (0, q_first), (2 * net.dp * rows, q_rows)
    )
    part_out = jnp.einsum(
        "tc,td->cd", attended_group, net.group_gather(grad_attn_low), preferred_element_type=f32
    )
    part_joint = jnp.einsum(
        "td,tc->dc", normed_one_group, net.group_gather(grad_joint_low), preferred_element_type=f32
    )
    part_small = jnp.concatenate([part_joint, part_out], 1).astype(bf16)
    small_cols = part_small.shape[1] // chips

    def small_chunk(slot):
        return lax.dynamic_slice(part_small, (0, net.owner(slot) * small_cols), (q_rows, small_cols))

    sum_small = net.ring_scatter([small_chunk(s) for s in range(chips)]).astype(bf16)
    sum_small = lax.optimization_barrier(sum_small)

    grad_down = jnp.zeros((ff_loc, D), f32)
    for s, got in enumerate(net.ring_gather(sum_down)):
        other = net.swap(got)
        base = net.owner(s) * down_rows
        grad_down = lax.dynamic_update_slice(
            grad_down, got.astype(f32), (core * ff_half + base, 0)
        )
        grad_down = lax.dynamic_update_slice(
            grad_down, other.astype(f32), ((1 - core) * ff_half + base, 0)
        )
    grad_gate = jnp.zeros((D, ff_loc), f32)
    grad_up = jnp.zeros((D, ff_loc), f32)
    left_lane = jnp.arange(2 * rest) < rest
    for s, got in enumerate(net.ring_gather(sum_mlp)):
        other = net.swap(got)
        zero = jnp.where(core == 0, got, other).astype(f32)
        one = jnp.where(core == 0, other, got).astype(f32)
        tile_zero, tile_one = zero[:, 2 * main :], one[:, 2 * main :]
        mid_gate = jnp.where(left_lane, tile_zero, tile_one)
        mid_up = jnp.roll(jnp.where(left_lane, tile_one, tile_zero), rest, 1)
        base = net.owner(s) * mlp_rows
        grad_gate = lax.dynamic_update_slice(
            grad_gate, jnp.concatenate([zero[:, :main], mid_gate, one[:, :main]], 1), (base, 0)
        )
        grad_up = lax.dynamic_update_slice(
            grad_up,
            jnp.concatenate([zero[:, main : 2 * main], mid_up, one[:, main : 2 * main]], 1),
            (base, 0),
        )
    grad_small = jnp.zeros((2 * q_rows, part_small.shape[1]), f32)
    for s, got in enumerate(net.ring_gather(sum_small)):
        other = net.swap(got)
        base = net.owner(s) * small_cols
        grad_small = lax.dynamic_update_slice(grad_small, got.astype(f32), (core * q_rows, base))
        grad_small = lax.dynamic_update_slice(
            grad_small, other.astype(f32), ((1 - core) * q_rows, base)
        )
    qkv_cols = w_qkv.shape[1]
    return (
        output[None],
        grad_input[None],
        grad_small[:, :qkv_cols],
        small[2 * D :],
        grad_small[:, qkv_cols:],
        small[:D],
        small[D : 2 * D],
        grad_gate,
        grad_up,
        grad_down,
    )


def solution(mesh):
    placed = (
        P("dp", "ctx", None),
        P("dp", None),
        P(),
        P("dp", None),
        P(),
        P(),
        P(None, "dp"),
        P(None, "dp"),
        P("dp", None),
        P("dp", "ctx", None),
    )
    return jax.shard_map(
        local,
        mesh=mesh,
        in_specs=placed,
        out_specs=(
            P("dp", "ctx", None),
            P("dp", "ctx", None),
            P("dp", None),
            P(),
            P("dp", None),
            P(),
            P(),
            P(None, "dp"),
            P(None, "dp"),
            P("dp", None),
        ),
        check_vma=False,
    )
```

```python
import jax
import jax.numpy as jnp
from jax import lax
from jax.experimental import pallas as pl
from jax.experimental.pallas import tpu as pltpu
from jax.sharding import PartitionSpec as P

D = 896
QH = 14
KH = 2
HD = 64
GROUP = QH // KH
WIDTH_Q = QH * HD
WIDTH_K = KH * HD

EPS = 1e-06
ROPE_BASE = 1000000.0

f32 = jnp.float32
bf16 = jnp.bfloat16


def ring_order(chips):
    if chips % 2:
        return list(range(chips))
    rows = chips // 2
    return [2 * i for i in range(rows)] + [2 * i + 1 for i in reversed(range(rows))]


def half_cut(rows):
    cut = (rows // 2 + 7) // 8 * 8
    return cut if cut < rows else rows // 2


class Net:
    def __init__(self):
        self.dp = lax.axis_size("dp")
        self.ctx = lax.axis_size("ctx")
        self.chips = self.ctx // 2
        self.order = ring_order(self.chips)
        self.d = lax.axis_index("dp")
        self.c = lax.axis_index("ctx")
        self.core = self.c % 2
        place = [0] * self.chips
        for spot, chip in enumerate(self.order):
            place[chip] = spot
        self.pos = jnp.array(place, jnp.int32)[self.c // 2]

    def swap(self, x):
        return lax.ppermute(x, "ctx", [(i, i ^ 1) for i in range(self.ctx)])

    def shift(self, x, step):
        n = self.dp
        return lax.ppermute(x, "dp", [(i, (i + step) % n) for i in range(n)])

    def hop(self, x, step):
        n = self.chips
        perm = []
        for spot in range(n):
            for core in range(2):
                perm.append((2 * self.order[spot] + core, 2 * self.order[(spot + step) % n] + core))
        return lax.ppermute(x, "ctx", perm)

    def owner(self, slot):
        return (self.pos - slot) % self.chips

    def group_gather(self, x):
        chip = jnp.concatenate([x] + [self.shift(x, s) for s in range(1, self.dp)], 0)
        return jnp.concatenate([chip, self.swap(chip)], 0)

    def ring_gather(self, x):
        n = self.chips
        half = n // 2
        cut = half_cut(x.shape[0])
        found = [x] + [None] * (n - 1)
        fwd, back = x, x
        for s in range(1, half):
            fwd = self.hop(fwd, 1)
            back = self.hop(back, -1)
            found[s] = fwd
            found[n - s] = back
        found[half] = jnp.concatenate([self.hop(fwd[:cut], 1), self.hop(back[cut:], -1)], 0)
        return found

    def ring_scatter(self, local):
        n = self.chips
        half = n // 2
        cut = half_cut(local[half].shape[0])

        def add(got, mine):
            return (got.astype(f32) + mine.astype(f32)).astype(bf16)

        fwd = self.hop(local[half][:cut], 1)
        back = self.hop(local[half][cut:], -1)
        for s in range(1, half):
            mine_f = local[half + s]
            mine_b = local[half - s]
            if s == 1:
                mine_f = jnp.concatenate([add(fwd, mine_f[:cut]), mine_f[cut:]], 0)
                mine_b = jnp.concatenate([mine_b[:cut], add(back, mine_b[cut:])], 0)
            else:
                mine_f = add(fwd, mine_f)
                mine_b = add(back, mine_b)
            fwd = self.hop(mine_f, 1)
            back = self.hop(mine_b, -1)
        return fwd.astype(f32) + back.astype(f32) + local[0].astype(f32)

    def full_rows(self, shard):
        rows = shard.shape[0]
        half = rows // 2
        piece = lax.dynamic_slice(shard, (self.core * half, 0), (half, shard.shape[1]))
        blocks = [shard]
        for s in range(1, self.dp):
            got = self.shift(piece, s)
            other = self.swap(got)
            low = jnp.where(self.core == 0, got, other)
            high = jnp.where(self.core == 0, other, got)
            blocks.append(jnp.concatenate([low, high], 0))
        if self.dp == 2:
            first = jnp.where(self.d == 0, blocks[0], blocks[1])
            second = jnp.where(self.d == 0, blocks[1], blocks[0])
            return jnp.concatenate([first, second], 0)
        ranked = jnp.stack(blocks)[(self.d - jnp.arange(self.dp)) % self.dp]
        return ranked.reshape(self.dp * rows, shard.shape[1])

    def total(self, x):
        x = x + self.swap(x)
        bit = 1
        while bit < self.chips:
            x = x + lax.ppermute(x, "ctx", [(i, i ^ (2 * bit)) for i in range(self.ctx)])
            bit *= 2
        bit = 1
        while bit < self.dp:
            x = x + lax.ppermute(x, "dp", [(i, i ^ bit) for i in range(self.dp)])
            bit *= 2
        return x


VMEM_BYTES = 56 * 1024 * 1024
KEYS = 256


def full_spec(shape):
    return pl.BlockSpec(shape, lambda: (0,) * len(shape))


def call(kernel, outs, args, smem=0, scratch=(), flops=0):
    specs = [pl.BlockSpec(memory_space=pltpu.SMEM)] * smem
    specs += [pl.BlockSpec(memory_space=pltpu.VMEM)] * (len(args) - smem)
    moved = sum(x.size * x.dtype.itemsize for x in list(args) + list(outs))
    return pl.pallas_call(
        kernel,
        out_shape=list(outs),
        in_specs=specs,
        out_specs=[pl.BlockSpec(memory_space=pltpu.VMEM)] * len(outs),
        scratch_shapes=list(scratch),
        compiler_params=pltpu.CompilerParams(vmem_limit_bytes=VMEM_BYTES),
        cost_estimate=pl.CostEstimate(flops=flops, bytes_accessed=moved, transcendentals=0),
    )(*args)


def lanes(shape):
    return lax.broadcasted_iota(jnp.int32, shape, len(shape) - 1)


def dot_nt(a, b, precision=None):
    return lax.dot_general(
        a, b, (((1,), (1,)), ((), ())), preferred_element_type=f32, precision=precision
    )


def dot_tn(a, b):
    return lax.dot_general(a, b, (((0,), (0,)), ((), ())), preferred_element_type=f32)


def qkv_kernel(x_ref, gain_ref, w_ref, b_ref, cos_ref, sin_ref, norm_ref, q_ref, pair_ref):
    x = x_ref[...].astype(f32)
    inverse = lax.rsqrt(jnp.mean(x * x, -1, keepdims=True) + EPS)
    normed = (x * inverse * gain_ref[...]).astype(bf16)
    norm_ref[...] = normed
    joint = jnp.dot(normed, w_ref[...], preferred_element_type=f32) + b_ref[...]
    cosine = cos_ref[...]
    sine = sin_ref[...]
    early = lanes(cosine.shape) % HD < HD // 2
    for i in range((WIDTH_Q + WIDTH_K) // 128):
        tile = joint[:, i * 128 : (i + 1) * 128]
        turned = jnp.where(early, -pltpu.roll(tile, 96, 1), pltpu.roll(tile, 32, 1))
        turned = tile * cosine + turned * sine
        if i * 128 < WIDTH_Q:
            q_ref[:, i * 128 : (i + 1) * 128] = turned.astype(bf16)
        else:
            pair_ref[:, :WIDTH_K] = turned.astype(bf16)
    pair_ref[:, WIDTH_K:] = joint[:, WIDTH_Q + WIDTH_K :].astype(bf16)


def spread_heads(x, out_ref, factor):
    rows = x.shape[0]
    half = rows // 2
    for head in range(QH):
        kh, g = divmod(head, GROUP)
        tile = x[:, (head // 2) * 128 : (head // 2 + 1) * 128].astype(f32)
        if head % 2 != kh:
            tile = pltpu.roll(tile, HD, 1)
        tile = jnp.where(lanes(tile.shape) // HD == kh, tile * factor, 0.0).astype(out_ref.dtype)
        for part in range(2):
            start = (part * GROUP + g) * half
            out_ref[kh, start : start + half, :] = tile[part * half : (part + 1) * half]


def join_heads(src_ref, half, tile):
    sides = []
    for side in range(2):
        kh, g = divmod(2 * tile + side, GROUP)
        parts = [
            src_ref[kh, (part * GROUP + g) * half : (part * GROUP + g + 1) * half, :]
            for part in range(2)
        ]
        both = jnp.concatenate(parts, 0)
        sides.append(both if side == kh else pltpu.roll(both, HD, 1))
    return jnp.where(lanes(sides[0].shape) < HD, sides[0], sides[1])


def forward_kernel(
    ctx, meta_ref, q_ref, mine_ref, other_ref, x_ref, w_ref, gain_ref,
    low_ref, o_ref, lse_ref, spread_ref, k_ref, v_ref, hidden_ref, normed_ref,
    s_ref, max_ref, sum_ref,
):
    rows = q_ref.shape[0]
    half = rows // 2
    part_rows = GROUP * half
    me = meta_ref[0]
    chips = ctx // 2
    for j in range(ctx):
        src = mine_ref if j < chips else other_ref
        at = (j % chips) * rows
        owner = meta_ref[1 + j]
        for part in range(2):
            place = owner if part == 0 else 2 * ctx - 1 - owner
            to = pl.ds(pl.multiple_of(place * half, half), half)
            block = src[at + part * half : at + (part + 1) * half, :]
            k_ref[to, :] = block[:, :WIDTH_K]
            v_ref[to, :] = block[:, WIDTH_K:]
    spread_heads(q_ref[...], spread_ref, HD ** (-0.5))
    for kh in range(KH):
        for part in range(2):
            span = slice(part * part_rows, (part + 1) * part_rows)
            start = (me if part == 0 else 2 * ctx - 1 - me) * half
            last = start // KEYS
            queries = spread_ref[kh, span, :]

            def keys_of(ref, i):
                return ref[pl.ds(pl.multiple_of(i * KEYS, KEYS), KEYS), :]

            scores = dot_nt(queries, keys_of(k_ref, last))
            row = lax.broadcasted_iota(jnp.int32, scores.shape, 0) % half + start
            scores = jnp.where(lanes(scores.shape) + last * KEYS <= row, scores, -1e30)
            s_ref[last] = scores
            max_ref[...] = jnp.maximum(scores[:, :128], scores[:, 128:])

            def score(i, carry):
                s = dot_nt(queries, keys_of(k_ref, i))
                s_ref[i] = s
                max_ref[...] = jnp.maximum(max_ref[...], jnp.maximum(s[:, :128], s[:, 128:]))
                return carry

            lax.fori_loop(0, last, score, 0)
            top = jnp.max(max_ref[...], -1, keepdims=True)
            sum_ref[...] = jnp.zeros_like(sum_ref)
            o_ref[kh, span, :] = jnp.zeros((part_rows, 128), f32)

            def weigh(i, carry):
                p = jnp.exp(s_ref[i] - top)
                sum_ref[...] += p[:, :128] + p[:, 128:]
                o_ref[kh, span, :] += jnp.dot(
                    p.astype(bf16), keys_of(v_ref, i), preferred_element_type=f32
                )
                return carry

            lax.fori_loop(0, last + 1, weigh, 0)
            total = jnp.sum(sum_ref[...], -1, keepdims=True)
            o_ref[kh, span, :] = o_ref[kh, span, :] / total
            lse = jnp.broadcast_to(top + jnp.log(total), (part_rows, 128))
            lse_ref[kh, part] = dot_nt(
                jnp.full((8, 128), 1.0 / 128, f32), lse, lax.Precision.HIGHEST
            )
    for tile in range(WIDTH_Q // 128):
        low_ref[:, tile * 128 : (tile + 1) * 128] = join_heads(o_ref, half, tile).astype(bf16)
    hidden = x_ref[...].astype(f32) + jnp.dot(low_ref[...], w_ref[...], preferred_element_type=f32)
    hidden_ref[...] = hidden
    inverse = lax.rsqrt(jnp.mean(hidden * hidden, -1, keepdims=True) + EPS)
    normed_ref[...] = (hidden * inverse * gain_ref[...]).astype(bf16)


def backward_kernel(
    ctx, meta_ref, gn_ref, hidden_ref, gout_ref, gain_ref, w_ref, spread_ref, k_ref, v_ref, lse_ref,
    o_ref,
    gh_ref, ga_ref, gain_grad_ref, gq_ref, mine_ref, other_ref,
    go_ref, gqs_ref, gk_ref, gv_ref,
):
    rows = gn_ref.shape[0]
    half = rows // 2
    part_rows = GROUP * half
    me = meta_ref[0]
    chips = ctx // 2
    hidden = hidden_ref[...]
    inverse = lax.rsqrt(jnp.mean(hidden * hidden, -1, keepdims=True) + EPS)
    unit = hidden * inverse
    grad = gn_ref[...]
    gain_grad_ref[...] = jnp.sum(grad * unit, 0, keepdims=True)
    scaled = grad * gain_ref[...]
    gh = gout_ref[...].astype(f32) + inverse * (
        scaled - unit * jnp.mean(scaled * unit, -1, keepdims=True)
    )
    gh_ref[...] = gh
    ga = gh.astype(bf16)
    ga_ref[...] = ga
    spread_heads(dot_nt(ga, w_ref[...]).astype(bf16), go_ref, 1.0)
    gqs_ref[...] = jnp.zeros_like(gqs_ref)
    gk_ref[...] = jnp.zeros_like(gk_ref)
    gv_ref[...] = jnp.zeros_like(gv_ref)
    for kh in range(KH):
        for part in range(2):
            span = slice(part * part_rows, (part + 1) * part_rows)
            start = (me if part == 0 else 2 * ctx - 1 - me) * half
            last = start // KEYS
            queries = spread_ref[kh, span, :]
            heads = go_ref[kh, span, :]
            lse = lse_ref[kh, part][:1]
            delta = dot_nt(
                jnp.ones((8, 128), f32), heads.astype(f32) * o_ref[kh, span, :],
                lax.Precision.HIGHEST,
            )[:1]

            def step(i, masked):
                at = pl.ds(pl.multiple_of(i * KEYS, KEYS), KEYS)
                keys = k_ref[at, :]
                p = jnp.exp(dot_nt(keys, queries) - lse)
                if masked:
                    row = lanes(p.shape) % half + start
                    key = lax.broadcasted_iota(jnp.int32, p.shape, 0) + i * KEYS
                    p = jnp.where(key <= row, p, 0.0)
                gs = (p * (dot_nt(v_ref[at, :], heads) - delta)).astype(bf16)
                gv_ref[at, :] += jnp.dot(p.astype(bf16), heads, preferred_element_type=f32)
                gk_ref[at, :] += jnp.dot(gs, queries, preferred_element_type=f32)
                gqs_ref[kh, span, :] += dot_tn(gs, keys)

            def body(i, carry):
                step(i, False)
                return carry

            lax.fori_loop(0, last, body, 0)
            step(last, True)
    for tile in range(WIDTH_Q // 128):
        gq_ref[:, tile * 128 : (tile + 1) * 128] = join_heads(gqs_ref, half, tile) * HD ** (-0.5)
    for j in range(ctx):
        dst = mine_ref if j < chips else other_ref
        at = (j % chips) * rows
        owner = meta_ref[1 + j]
        for part in range(2):
            place = owner if part == 0 else 2 * ctx - 1 - owner
            frm = pl.ds(pl.multiple_of(place * half, half), half)
            to = slice(at + part * half, at + (part + 1) * half)
            dst[to, :WIDTH_K] = gk_ref[frm, :].astype(dst.dtype)
            dst[to, WIDTH_K:] = gv_ref[frm, :].astype(dst.dtype)


def finish_kernel(
    gq_ref, pair_ref, x_ref, gain_ref, w_ref, cos_ref, sin_ref, gh_ref,
    joint_ref, gx_ref, gain_grad_ref, bias_ref,
):
    cosine = cos_ref[...]
    sine = sin_ref[...]
    early = lanes(cosine.shape) % HD < HD // 2
    for i in range((WIDTH_Q + WIDTH_K) // 128):
        at = slice(i * 128, (i + 1) * 128)
        grad = gq_ref[:, at] if i * 128 < WIDTH_Q else pair_ref[:, :WIDTH_K]
        scaled = grad * sine
        turned = jnp.where(early, pltpu.roll(scaled, 96, 1), -pltpu.roll(scaled, 32, 1))
        joint_ref[:, at] = (grad * cosine + turned).astype(bf16)
    joint_ref[:, WIDTH_Q + WIDTH_K :] = pair_ref[:, WIDTH_K:].astype(bf16)
    joint = joint_ref[...]
    bias_ref[...] = jnp.sum(joint.astype(f32), 0, keepdims=True)
    grad = dot_nt(joint, w_ref[...])
    x = x_ref[...].astype(f32)
    inverse = lax.rsqrt(jnp.mean(x * x, -1, keepdims=True) + EPS)
    unit = x * inverse
    gain_grad_ref[...] = jnp.sum(grad * unit, 0, keepdims=True)
    scaled = grad * gain_ref[...]
    gx_ref[...] = gh_ref[...] + inverse * (
        scaled - unit * jnp.mean(scaled * unit, -1, keepdims=True)
    )


def place_blocks(blocks, spots, out_shape, old=None):
    shape = blocks[0].shape
    count = len(blocks)
    if shape[0] % 8 or shape[1] % 128:
        out = jnp.zeros(out_shape, f32) if old is None else old
        for block, (i, j) in zip(blocks, spots):
            out = lax.dynamic_update_slice(
                out, block.astype(f32), (i * shape[0], j * shape[1])
            )
        return out

    def kernel(spots_ref, *refs):
        step = pl.program_id(0)
        out_ref = refs[-1]
        for i in range(count):

            @pl.when(step == i)
            def write(i=i):
                out_ref[...] = refs[i][...].astype(f32)

    keep = [] if old is None else [old]
    return pl.pallas_call(
        kernel,
        out_shape=jax.ShapeDtypeStruct(out_shape, f32),
        grid_spec=pltpu.PrefetchScalarGridSpec(
            num_scalar_prefetch=1,
            grid=(count,),
            in_specs=[pl.BlockSpec(shape, lambda i, spots: (0, 0))] * count
            + [pl.BlockSpec(memory_space=pl.ANY)] * len(keep),
            out_specs=pl.BlockSpec(shape, lambda i, spots: (spots[i, 0], spots[i, 1])),
        ),
        input_output_aliases={} if old is None else {count + 1: 0},
        compiler_params=pltpu.CompilerParams(vmem_limit_bytes=VMEM_BYTES),
    )(jnp.stack([jnp.stack(s) for s in spots]).astype(jnp.int32), *blocks, *keep)


def place_mlp(pairs, owners, core, main, out_shape, old=None):
    count = len(pairs)
    rows = pairs[0][0].shape[0]
    columns = pairs[0][0].shape[1]
    blocks = [x for pair in pairs for x in pair]

    def kernel(spots_ref, *refs):
        step = pl.program_id(0)
        gate_ref, up_ref = refs[-2:]
        core_zero = spots_ref[count] == 0
        for i in range(count):

            @pl.when(step == i)
            def write(i=i):
                got = refs[2 * i][...].astype(f32)
                other = refs[2 * i + 1][...].astype(f32)
                zero = jnp.where(core_zero, got, other)
                one = jnp.where(core_zero, other, got)
                tile_zero, tile_one = zero[:, 2 * main :], one[:, 2 * main :]
                left = lanes(tile_zero.shape) < 64
                gate_ref[:, :main] = zero[:, :main]
                gate_ref[:, main : main + 128] = jnp.where(left, tile_zero, tile_one)
                gate_ref[:, main + 128 :] = one[:, :main]
                up_ref[:, :main] = zero[:, main : 2 * main]
                up_ref[:, main : main + 128] = pltpu.roll(
                    jnp.where(left, tile_one, tile_zero), 64, 1
                )
                up_ref[:, main + 128 :] = one[:, main : 2 * main]

    keep = [] if old is None else list(old)
    out_spec = pl.BlockSpec((rows, out_shape[1]), lambda i, spots: (spots[i], 0))
    return pl.pallas_call(
        kernel,
        out_shape=[jax.ShapeDtypeStruct(out_shape, f32)] * 2,
        grid_spec=pltpu.PrefetchScalarGridSpec(
            num_scalar_prefetch=1,
            grid=(count,),
            in_specs=[pl.BlockSpec((rows, columns), lambda i, spots: (0, 0))] * (2 * count)
            + [pl.BlockSpec(memory_space=pl.ANY)] * len(keep),
            out_specs=[out_spec, out_spec],
        ),
        input_output_aliases={} if old is None else {2 * count + 1: 0, 2 * count + 2: 1},
        compiler_params=pltpu.CompilerParams(vmem_limit_bytes=VMEM_BYTES),
    )(jnp.stack(list(owners) + [core]).astype(jnp.int32), *blocks, *keep)


def local(tokens, w_qkv, b_qkv, w_out, gain_attn, gain_mlp, w_gate, w_up, w_down, cotangent):
    net = Net()
    rows = tokens.shape[1]
    half_rows = rows // 2
    ctx_count = net.ctx
    core = net.core
    chips = net.chips
    part_rows = GROUP * half_rows
    x = tokens[0]
    gain_one = gain_attn[None]
    gain_two = gain_mlp[None]

    w_qkv_full = net.full_rows(w_qkv)

    ff_loc = w_gate.shape[1]
    ff_half = ff_loc // 2
    main = (ff_half // 128) * 128
    rest = ff_half - main
    width = main + 2 * rest
    first = core * main
    own_cols = (jnp.arange(width) + first < ff_half) == (core == 0)
    wg = lax.dynamic_slice(w_gate, (0, first), (D, width))
    wu = lax.dynamic_slice(w_up, (0, first), (D, width))
    wd = lax.dynamic_slice(w_down, (first, 0), (width, D))

    row_ids = jnp.arange(half_rows, dtype=jnp.int32)
    place = jnp.concatenate(
        [net.c * half_rows + row_ids, (2 * ctx_count - 1 - net.c) * half_rows + row_ids]
    )
    freq = ROPE_BASE ** (-((jnp.arange(128) % (HD // 2)).astype(f32) * (2.0 / HD)))
    angle = place.astype(f32)[:, None] * freq[None, :]
    cosine, sine = jnp.cos(angle), jnp.sin(angle)
    normed_one, queries, pairs = call(
        qkv_kernel,
        [
            jax.ShapeDtypeStruct((rows, D), bf16),
            jax.ShapeDtypeStruct((rows, WIDTH_Q), bf16),
            jax.ShapeDtypeStruct((rows, 2 * WIDTH_K), bf16),
        ],
        [x, gain_one, w_qkv_full, b_qkv[None], cosine, sine],
        flops=2 * rows * D * 1152,
    )

    slots = net.ring_gather(pairs)
    mine = jnp.concatenate(slots, 0)
    other = net.swap(mine)
    order = jnp.array(net.order, jnp.int32)
    chip_ids = order[(net.pos - jnp.arange(chips, dtype=jnp.int32)) % chips]
    meta = jnp.concatenate([net.c[None], 2 * chip_ids + core, 2 * chip_ids + 1 - core])
    meta = meta.astype(jnp.int32)

    late_w, late_g, late_n, unused = lax.optimization_barrier((w_out, cotangent[0], normed_one, pairs))
    w_out_full = net.full_rows(late_w)
    early_group = net.group_gather(jnp.concatenate([late_g, late_n], 1))
    grad_out_group = early_group[:, :D]
    normed_one_group = early_group[:, D:]

    total_keys = rows * ctx_count
    padded = (KH, 2 * part_rows, 128)
    attended_low, attended, lse, spread, keys, values, hidden, normed_two = call(
        lambda *refs: forward_kernel(ctx_count, *refs),
        [
            jax.ShapeDtypeStruct((rows, WIDTH_Q), bf16),
            jax.ShapeDtypeStruct(padded, f32),
            jax.ShapeDtypeStruct((KH, 2, 8, part_rows), f32),
            jax.ShapeDtypeStruct(padded, bf16),
            jax.ShapeDtypeStruct((total_keys, WIDTH_K), bf16),
            jax.ShapeDtypeStruct((total_keys, WIDTH_K), bf16),
            jax.ShapeDtypeStruct((rows, D), f32),
            jax.ShapeDtypeStruct((rows, D), bf16),
        ],
        [meta, queries, mine, other, x, w_out_full, gain_two],
        smem=1,
        scratch=[
            pltpu.VMEM((total_keys // KEYS, part_rows, KEYS), f32),
            pltpu.VMEM((part_rows, 128), f32),
            pltpu.VMEM((part_rows, 128), f32),
        ],
        flops=8 * KH * part_rows * total_keys * 128,
    )

    normed_two_group = net.group_gather(normed_two)
    gate = jnp.dot(normed_two_group, wg, preferred_element_type=f32)
    upper = jnp.dot(normed_two_group, wu, preferred_element_type=f32)
    sigma = jax.nn.sigmoid(gate)
    activated = gate * sigma
    middle = jnp.where(own_cols, activated * upper, 0.0).astype(bf16)
    grad_middle = jnp.einsum("td,fd->tf", grad_out_group, wd, preferred_element_type=f32)
    slope = sigma * (1.0 + gate * (1.0 - sigma))
    grad_gate_low = jnp.where(own_cols, grad_middle * upper * slope, 0.0).astype(bf16)
    grad_up_low = jnp.where(own_cols, grad_middle * activated, 0.0).astype(bf16)

    grad_normed_two = jnp.einsum(
        "tf,df->td", grad_gate_low, wg, preferred_element_type=f32
    ) + jnp.einsum("tf,df->td", grad_up_low, wu, preferred_element_type=f32)
    mlp_out = jnp.dot(middle, wd, preferred_element_type=f32)
    chip_rows = net.dp * rows
    swapped = net.swap(
        jnp.concatenate([grad_normed_two[chip_rows:], mlp_out[chip_rows:]], 0).astype(bf16)
    ).astype(f32)
    grad_chip = grad_normed_two[:chip_rows] + swapped[:chip_rows]
    mlp_chip = mlp_out[:chip_rows] + swapped[chip_rows:]
    grad_two = grad_chip[:rows]
    for s in range(1, net.dp):
        sent = grad_chip[s * rows : (s + 1) * rows].astype(bf16)
        grad_two = grad_two + net.shift(sent, net.dp - s).astype(f32)

    part_down = jnp.einsum(
        "tf,td->fd", middle, grad_out_group, preferred_element_type=f32
    ).astype(bf16)
    part_down = lax.dynamic_slice(part_down, (core * rest, 0), (ff_half, D))
    down_rows = ff_half // chips

    def down_chunk(slot):
        return lax.dynamic_slice(part_down, (net.owner(slot) * down_rows, 0), (down_rows, D))

    sum_down = net.ring_scatter([down_chunk(s) for s in range(chips)]).astype(bf16)

    def split_main(x):
        left = (x[:, :main], x[:, main:])
        right = (x[:, 2 * rest :], x[:, : 2 * rest])
        return (
            jnp.where(core == 0, left[0], right[0]),
            jnp.where(core == 0, left[1], right[1]),
        )

    gate_main, gate_tile = split_main(grad_gate_low)
    up_main, up_tile = split_main(grad_up_low)
    packed = jnp.concatenate(
        [gate_main, up_main, gate_tile + jnp.roll(up_tile, rest, 1)], 1
    )
    part_mlp = jnp.einsum(
        "td,tf->df", normed_two_group, packed, preferred_element_type=f32
    ).astype(bf16)
    mlp_rows = D // chips

    def mlp_chunk(slot):
        return lax.dynamic_slice(
            part_mlp, (net.owner(slot) * mlp_rows, 0), (mlp_rows, 2 * ff_half)
        )

    sum_mlp = net.ring_scatter([mlp_chunk(s) for s in range(chips)]).astype(bf16)
    sum_mlp = lax.optimization_barrier(sum_mlp)

    grad_hidden, grad_attn_low, grad_gain_two, grad_queries, terms_mine, terms_other = call(
        lambda *refs: backward_kernel(ctx_count, *refs),
        [
            jax.ShapeDtypeStruct((rows, D), f32),
            jax.ShapeDtypeStruct((rows, D), bf16),
            jax.ShapeDtypeStruct((1, D), f32),
            jax.ShapeDtypeStruct((rows, WIDTH_Q), f32),
            jax.ShapeDtypeStruct((chips * rows, 2 * WIDTH_K), f32),
            jax.ShapeDtypeStruct((chips * rows, 2 * WIDTH_K), bf16),
        ],
        [
            meta, grad_two, hidden, cotangent[0], gain_two, w_out_full, spread, keys, values, lse,
            attended,
        ],
        smem=1,
        scratch=[
            pltpu.VMEM(padded, bf16),
            pltpu.VMEM(padded, f32),
            pltpu.VMEM((total_keys, WIDTH_K), f32),
            pltpu.VMEM((total_keys, WIDTH_K), f32),
        ],
        flops=20 * KH * part_rows * total_keys * 128,
    )
    pair_sums = (terms_mine + net.swap(terms_other).astype(f32)).astype(bf16)
    grad_pairs = net.ring_scatter(
        [pair_sums[s * rows : (s + 1) * rows] for s in range(chips)]
    )
    grad_joint_low, grad_input, grad_gain_one, grad_bias = call(
        finish_kernel,
        [
            jax.ShapeDtypeStruct((rows, 1152), bf16),
            jax.ShapeDtypeStruct((rows, D), f32),
            jax.ShapeDtypeStruct((1, D), f32),
            jax.ShapeDtypeStruct((1, 1152), f32),
        ],
        [grad_queries, grad_pairs, x, gain_one, w_qkv_full, cosine, sine, grad_hidden],
        flops=2 * rows * D * 1152,
    )

    out_sum = mlp_chip[:rows]
    sent = jnp.concatenate([attended_low, grad_attn_low], 0)
    gathered = [sent]
    for s in range(1, net.dp):
        got = net.shift(
            jnp.concatenate([mlp_chip[s * rows : (s + 1) * rows].astype(bf16), sent], 0),
            net.dp - s,
        )
        out_sum = out_sum + got[:rows].astype(f32)
        gathered.append(got[rows:])
    output = (hidden + out_sum).astype(bf16)
    gathered = jnp.concatenate(gathered, 0)
    gathered = jnp.concatenate([gathered, net.swap(gathered)], 0).reshape(2 * net.dp, 2, rows, D)
    attended_group = gathered[:, 0].reshape(2 * net.dp * rows, D)
    grad_attn_group = gathered[:, 1].reshape(2 * net.dp * rows, D)

    q_rows = w_qkv.shape[0] // 2
    q_first = net.d * (2 * q_rows) + core * q_rows
    group_rows = 2 * net.dp * rows
    part_out = jnp.einsum(
        "tc,td->cd",
        lax.dynamic_slice(attended_group, (0, q_first), (group_rows, q_rows)),
        grad_attn_group,
        preferred_element_type=f32,
    )
    part_joint = jnp.einsum(
        "td,tc->dc",
        lax.dynamic_slice(normed_one_group, (0, q_first), (group_rows, q_rows)),
        net.group_gather(grad_joint_low),
        preferred_element_type=f32,
    )
    part_small = jnp.concatenate([part_joint, part_out], 1).astype(bf16)
    small_cols = part_small.shape[1] // chips

    def small_chunk(slot):
        return lax.dynamic_slice(part_small, (0, net.owner(slot) * small_cols), (q_rows, small_cols))

    sum_small = net.ring_scatter([small_chunk(s) for s in range(chips)]).astype(bf16)

    tall = jnp.concatenate(
        [sum_small[:, i * 128 : (i + 1) * 128] for i in range(small_cols // 128)], 0
    )
    piece = tall.shape[0] // (D // 128)
    wide = jnp.concatenate([tall[i * piece : (i + 1) * piece] for i in range(D // 128)], 1)
    both = lax.optimization_barrier(jnp.concatenate([sum_down, wide], 0))

    owners = [net.owner(s) for s in range(chips)]
    got_mlp = net.ring_gather(sum_mlp)
    got_both = net.ring_gather(both)
    pairs_mlp = [(got, net.swap(got)) for got in got_mlp]
    pairs_both = [(got, net.swap(got)) for got in got_both]

    down_blocks, down_spots, small_blocks, small_spots = [], [], [], []
    for owner, pair in zip(owners, pairs_both):
        for which, got in zip((core, 1 - core), pair):
            down_blocks.append(got[:down_rows])
            down_spots.append((which * chips + owner, jnp.int32(0)))
            wide = got[down_rows:]
            tall = jnp.concatenate([wide[:, i * 128 : (i + 1) * 128] for i in range(D // 128)], 0)
            small_blocks.append(
                jnp.concatenate(
                    [tall[i * q_rows : (i + 1) * q_rows] for i in range(small_cols // 128)], 1
                )
            )
            small_spots.append((which, owner))
    grad_down = place_blocks(down_blocks, down_spots, (ff_loc, D))
    grad_small = place_blocks(small_blocks, small_spots, (2 * q_rows, part_small.shape[1]))
    half = chips // 2
    if 2 * rest == 128:
        first_slots = [s for s in range(chips) if s != half]
        grad_mlp = place_mlp(
            [pairs_mlp[s] for s in first_slots], [owners[s] for s in first_slots], core, main,
            (D, ff_loc),
        )
        grad_gate, grad_up = place_mlp(
            [pairs_mlp[half]], [owners[half]], core, main, (D, ff_loc), grad_mlp
        )
    else:
        grad_gate = jnp.zeros((D, ff_loc), f32)
        grad_up = jnp.zeros((D, ff_loc), f32)
        left_lane = jnp.arange(2 * rest) < rest
        for owner, (got, swapped) in zip(owners, pairs_mlp):
            zero = jnp.where(core == 0, got, swapped).astype(f32)
            one = jnp.where(core == 0, swapped, got).astype(f32)
            tile_zero, tile_one = zero[:, 2 * main :], one[:, 2 * main :]
            mid_gate = jnp.where(left_lane, tile_zero, tile_one)
            mid_up = jnp.roll(jnp.where(left_lane, tile_one, tile_zero), rest, 1)
            base = owner * mlp_rows
            grad_gate = lax.dynamic_update_slice(
                grad_gate, jnp.concatenate([zero[:, :main], mid_gate, one[:, :main]], 1), (base, 0)
            )
            grad_up = lax.dynamic_update_slice(
                grad_up,
                jnp.concatenate([zero[:, main : 2 * main], mid_up, one[:, main : 2 * main]], 1),
                (base, 0),
            )

    small = net.total(jnp.concatenate([grad_gain_one, grad_gain_two, grad_bias], 1))[0]
    qkv_cols = w_qkv.shape[1]
    return (
        output[None],
        grad_input[None],
        grad_small[:, :qkv_cols],
        small[2 * D :],
        grad_small[:, qkv_cols:],
        small[:D],
        small[D : 2 * D],
        grad_gate,
        grad_up,
        grad_down,
    )


def solution(mesh):
    placed = (
        P("dp", "ctx", None),
        P("dp", None),
        P(),
        P("dp", None),
        P(),
        P(),
        P(None, "dp"),
        P(None, "dp"),
        P("dp", None),
        P("dp", "ctx", None),
    )
    return jax.shard_map(
        local,
        mesh=mesh,
        in_specs=placed,
        out_specs=(
            P("dp", "ctx", None),
            P("dp", "ctx", None),
            P("dp", None),
            P(),
            P("dp", None),
            P(),
            P(),
            P(None, "dp"),
            P(None, "dp"),
            P("dp", None),
        ),
        check_vma=False,
    )
```

```python
import jax
import jax.numpy as jnp
from jax import lax
from jax.experimental import pallas as pl
from jax.experimental.pallas import tpu as pltpu
from jax.sharding import PartitionSpec as P

D = 896
QH = 14
KH = 2
HD = 64
GROUP = QH // KH
WIDTH_Q = QH * HD
WIDTH_K = KH * HD

EPS = 1e-06
ROPE_BASE = 1000000.0

f32 = jnp.float32
bf16 = jnp.bfloat16


def ring_order(chips):
    if chips % 2:
        return list(range(chips))
    rows = chips // 2
    return [2 * i for i in range(rows)] + [2 * i + 1 for i in reversed(range(rows))]


def half_cut(rows):
    cut = (rows // 2 + 7) // 8 * 8
    return cut if cut < rows else rows // 2


class Net:
    def __init__(self):
        self.dp = lax.axis_size("dp")
        self.ctx = lax.axis_size("ctx")
        self.chips = self.ctx // 2
        self.order = ring_order(self.chips)
        self.d = lax.axis_index("dp")
        self.c = lax.axis_index("ctx")
        self.core = self.c % 2
        place = [0] * self.chips
        for spot, chip in enumerate(self.order):
            place[chip] = spot
        self.pos = jnp.array(place, jnp.int32)[self.c // 2]

    def swap(self, x):
        return lax.ppermute(x, "ctx", [(i, i ^ 1) for i in range(self.ctx)])

    def shift(self, x, step):
        n = self.dp
        return lax.ppermute(x, "dp", [(i, (i + step) % n) for i in range(n)])

    def hop(self, x, step):
        n = self.chips
        perm = []
        for spot in range(n):
            for core in range(2):
                perm.append((2 * self.order[spot] + core, 2 * self.order[(spot + step) % n] + core))
        return lax.ppermute(x, "ctx", perm)

    def owner(self, slot):
        return (self.pos - slot) % self.chips

    def group_gather(self, x):
        chip = jnp.concatenate([x] + [self.shift(x, s) for s in range(1, self.dp)], 0)
        return jnp.concatenate([chip, self.swap(chip)], 0)

    def ring_gather(self, x):
        n = self.chips
        half = n // 2
        cut = half_cut(x.shape[0])
        found = [x] + [None] * (n - 1)
        fwd, back = x, x
        for s in range(1, half):
            fwd = self.hop(fwd, 1)
            back = self.hop(back, -1)
            found[s] = fwd
            found[n - s] = back
        found[half] = jnp.concatenate([self.hop(fwd[:cut], 1), self.hop(back[cut:], -1)], 0)
        return found

    def ring_scatter(self, local):
        n = self.chips
        half = n // 2
        cut = half_cut(local[half].shape[0])

        def add(got, mine):
            return (got.astype(f32) + mine.astype(f32)).astype(bf16)

        fwd = self.hop(local[half][:cut], 1)
        back = self.hop(local[half][cut:], -1)
        for s in range(1, half):
            mine_f = local[half + s]
            mine_b = local[half - s]
            if s == 1:
                mine_f = jnp.concatenate([add(fwd, mine_f[:cut]), mine_f[cut:]], 0)
                mine_b = jnp.concatenate([mine_b[:cut], add(back, mine_b[cut:])], 0)
            else:
                mine_f = add(fwd, mine_f)
                mine_b = add(back, mine_b)
            fwd = self.hop(mine_f, 1)
            back = self.hop(mine_b, -1)
        return fwd.astype(f32) + back.astype(f32) + local[0].astype(f32)

    def full_rows(self, shard):
        rows = shard.shape[0]
        half = rows // 2
        piece = lax.dynamic_slice(shard, (self.core * half, 0), (half, shard.shape[1]))
        blocks = [shard]
        for s in range(1, self.dp):
            got = self.shift(piece, s)
            other = self.swap(got)
            low = jnp.where(self.core == 0, got, other)
            high = jnp.where(self.core == 0, other, got)
            blocks.append(jnp.concatenate([low, high], 0))
        if self.dp == 2:
            first = jnp.where(self.d == 0, blocks[0], blocks[1])
            second = jnp.where(self.d == 0, blocks[1], blocks[0])
            return jnp.concatenate([first, second], 0)
        ranked = jnp.stack(blocks)[(self.d - jnp.arange(self.dp)) % self.dp]
        return ranked.reshape(self.dp * rows, shard.shape[1])

    def total(self, x):
        x = x + self.swap(x)
        bit = 1
        while bit < self.chips:
            x = x + lax.ppermute(x, "ctx", [(i, i ^ (2 * bit)) for i in range(self.ctx)])
            bit *= 2
        bit = 1
        while bit < self.dp:
            x = x + lax.ppermute(x, "dp", [(i, i ^ bit) for i in range(self.dp)])
            bit *= 2
        return x

    def gather_both(self, a, b, place_a, place_b):
        n = self.chips
        half = n // 2
        streams = [[a, a, a, place_a, None, None], [b, b, b, place_b, None, None]]
        waiting = [([0], [x]) for x in (a, b)]
        for s in range(1, half + 1):
            for k, stream in enumerate(streams):
                own, fwd, back, place, placed, token = stream
                if token is not None:
                    fwd, back, token = lax.optimization_barrier((fwd, back, token))
                if s < half:
                    fwd, back = self.hop(fwd, 1), self.hop(back, -1)
                    arrived = ([s, n - s], [fwd, back])
                else:
                    cut = half_cut(own.shape[0])
                    far = jnp.concatenate([self.hop(fwd[:cut], 1), self.hop(back[cut:], -1)], 0)
                    arrived = ([half], [far])
                slots, blocks = waiting[k]
                out = place(slots, [(x, self.swap(x)) for x in blocks], placed)
                waiting[k] = arrived
                streams[k] = [own, fwd, back, place, out[:2], out[2]]
        results = []
        for k, stream in enumerate(streams):
            slots, blocks = waiting[k]
            out = stream[3](slots, [(x, self.swap(x)) for x in blocks], stream[4])
            results.append(out[:2])
        return results


VMEM_BYTES = 56 * 1024 * 1024
KEYS = 256


def full_spec(shape):
    return pl.BlockSpec(shape, lambda: (0,) * len(shape))


def call(kernel, outs, args, smem=0, scratch=(), flops=0):
    specs = [pl.BlockSpec(memory_space=pltpu.SMEM)] * smem
    specs += [pl.BlockSpec(memory_space=pltpu.VMEM)] * (len(args) - smem)
    moved = sum(x.size * x.dtype.itemsize for x in list(args) + list(outs))
    return pl.pallas_call(
        kernel,
        out_shape=list(outs),
        in_specs=specs,
        out_specs=[pl.BlockSpec(memory_space=pltpu.VMEM)] * len(outs),
        scratch_shapes=list(scratch),
        compiler_params=pltpu.CompilerParams(vmem_limit_bytes=VMEM_BYTES),
        cost_estimate=pl.CostEstimate(flops=flops, bytes_accessed=moved, transcendentals=0),
    )(*args)


def lanes(shape):
    return lax.broadcasted_iota(jnp.int32, shape, len(shape) - 1)


def dot_nt(a, b, precision=None):
    return lax.dot_general(
        a, b, (((1,), (1,)), ((), ())), preferred_element_type=f32, precision=precision
    )


def dot_tn(a, b):
    return lax.dot_general(a, b, (((0,), (0,)), ((), ())), preferred_element_type=f32)


def qkv_kernel(x_ref, gain_ref, w_ref, b_ref, cos_ref, sin_ref, norm_ref, q_ref, pair_ref):
    x = x_ref[...].astype(f32)
    inverse = lax.rsqrt(jnp.mean(x * x, -1, keepdims=True) + EPS)
    normed = (x * inverse * gain_ref[...]).astype(bf16)
    norm_ref[...] = normed
    joint = jnp.dot(normed, w_ref[...], preferred_element_type=f32) + b_ref[...]
    cosine = cos_ref[...]
    sine = sin_ref[...]
    early = lanes(cosine.shape) % HD < HD // 2
    for i in range((WIDTH_Q + WIDTH_K) // 128):
        tile = joint[:, i * 128 : (i + 1) * 128]
        turned = jnp.where(early, -pltpu.roll(tile, 96, 1), pltpu.roll(tile, 32, 1))
        turned = tile * cosine + turned * sine
        if i * 128 < WIDTH_Q:
            q_ref[:, i * 128 : (i + 1) * 128] = turned.astype(bf16)
        else:
            pair_ref[:, :WIDTH_K] = turned.astype(bf16)
    pair_ref[:, WIDTH_K:] = joint[:, WIDTH_Q + WIDTH_K :].astype(bf16)


def spread_heads(x, out_ref, factor):
    rows = x.shape[0]
    half = rows // 2
    for head in range(QH):
        kh, g = divmod(head, GROUP)
        tile = x[:, (head // 2) * 128 : (head // 2 + 1) * 128].astype(f32)
        if head % 2 != kh:
            tile = pltpu.roll(tile, HD, 1)
        tile = jnp.where(lanes(tile.shape) // HD == kh, tile * factor, 0.0).astype(out_ref.dtype)
        for part in range(2):
            start = (part * GROUP + g) * half
            out_ref[kh, start : start + half, :] = tile[part * half : (part + 1) * half]


def join_heads(src_ref, half, tile):
    sides = []
    for side in range(2):
        kh, g = divmod(2 * tile + side, GROUP)
        parts = [
            src_ref[kh, (part * GROUP + g) * half : (part * GROUP + g + 1) * half, :]
            for part in range(2)
        ]
        both = jnp.concatenate(parts, 0)
        sides.append(both if side == kh else pltpu.roll(both, HD, 1))
    return jnp.where(lanes(sides[0].shape) < HD, sides[0], sides[1])


def forward_kernel(
    ctx, meta_ref, q_ref, mine_ref, other_ref, x_ref, w_ref, gain_ref,
    low_ref, o_ref, lse_ref, spread_ref, k_ref, v_ref, hidden_ref, normed_ref,
    s_ref, max_ref, sum_ref,
):
    rows = q_ref.shape[0]
    half = rows // 2
    part_rows = GROUP * half
    me = meta_ref[0]
    chips = ctx // 2
    for j in range(ctx):
        src = mine_ref if j < chips else other_ref
        at = (j % chips) * rows
        owner = meta_ref[1 + j]
        for part in range(2):
            place = owner if part == 0 else 2 * ctx - 1 - owner
            to = pl.ds(pl.multiple_of(place * half, half), half)
            block = src[at + part * half : at + (part + 1) * half, :]
            k_ref[to, :] = block[:, :WIDTH_K]
            v_ref[to, :] = block[:, WIDTH_K:]
    spread_heads(q_ref[...], spread_ref, HD ** (-0.5))
    for part in range(2):
        span = slice(part * part_rows, (part + 1) * part_rows)
        start = (me if part == 0 else 2 * ctx - 1 - me) * half
        last = start // KEYS

        def keys_of(ref, i):
            return ref[pl.ds(pl.multiple_of(i * KEYS, KEYS), KEYS), :]

        for kh in range(KH):
            scores = dot_nt(spread_ref[kh, span, :], keys_of(k_ref, last))
            row = lax.broadcasted_iota(jnp.int32, scores.shape, 0) % half + start
            scores = jnp.where(lanes(scores.shape) + last * KEYS <= row, scores, -1e30)
            s_ref[kh, last] = scores
            max_ref[kh] = jnp.maximum(scores[:, :128], scores[:, 128:])

        def score(i, carry):
            for kh in range(KH):
                s = dot_nt(spread_ref[kh, span, :], keys_of(k_ref, i))
                s_ref[kh, i] = s
                max_ref[kh] = jnp.maximum(max_ref[kh], jnp.maximum(s[:, :128], s[:, 128:]))
            return carry

        lax.fori_loop(0, last, score, 0)
        for kh in range(KH):
            top = jnp.max(max_ref[kh], -1, keepdims=True)
            max_ref[kh] = jnp.broadcast_to(top, (part_rows, 128))
            sum_ref[kh] = jnp.zeros((part_rows, 128), f32)
            o_ref[kh, span, :] = jnp.zeros((part_rows, 128), f32)

        def weigh(i, carry):
            for kh in range(KH):
                s = s_ref[kh, i]
                top = max_ref[kh]
                left = jnp.exp(s[:, :128] - top)
                right = jnp.exp(s[:, 128:] - top)
                sum_ref[kh] += left + right
                o_ref[kh, span, :] += jnp.dot(
                    jnp.concatenate([left, right], 1).astype(bf16),
                    keys_of(v_ref, i),
                    preferred_element_type=f32,
                )
            return carry

        lax.fori_loop(0, last + 1, weigh, 0)
        for kh in range(KH):
            total = jnp.sum(sum_ref[kh], -1, keepdims=True)
            o_ref[kh, span, :] = o_ref[kh, span, :] / total
            lse_ref[kh, part] = dot_nt(
                jnp.full((8, 128), 1.0 / 128, f32),
                max_ref[kh] + jnp.log(total),
                lax.Precision.HIGHEST,
            )
    for tile in range(WIDTH_Q // 128):
        low_ref[:, tile * 128 : (tile + 1) * 128] = join_heads(o_ref, half, tile).astype(bf16)
    hidden = x_ref[...].astype(f32) + jnp.dot(low_ref[...], w_ref[...], preferred_element_type=f32)
    hidden_ref[...] = hidden
    inverse = lax.rsqrt(jnp.mean(hidden * hidden, -1, keepdims=True) + EPS)
    normed_ref[...] = (hidden * inverse * gain_ref[...]).astype(bf16)


def backward_kernel(
    ctx, meta_ref, gn_ref, hidden_ref, gout_ref, gain_ref, w_ref, spread_ref, k_ref, v_ref, lse_ref,
    o_ref,
    gh_ref, ga_ref, gain_grad_ref, gq_ref, mine_ref, other_ref,
    go_ref, gqs_ref, gk_ref, gv_ref,
):
    rows = gn_ref.shape[0]
    half = rows // 2
    part_rows = GROUP * half
    me = meta_ref[0]
    chips = ctx // 2
    hidden = hidden_ref[...]
    inverse = lax.rsqrt(jnp.mean(hidden * hidden, -1, keepdims=True) + EPS)
    unit = hidden * inverse
    grad = gn_ref[...]
    gain_grad_ref[...] = jnp.sum(grad * unit, 0, keepdims=True)
    scaled = grad * gain_ref[...]
    gh = gout_ref[...].astype(f32) + inverse * (
        scaled - unit * jnp.mean(scaled * unit, -1, keepdims=True)
    )
    gh_ref[...] = gh
    ga = gh.astype(bf16)
    ga_ref[...] = ga
    spread_heads(dot_nt(ga, w_ref[...]).astype(bf16), go_ref, 1.0)
    gqs_ref[...] = jnp.zeros_like(gqs_ref)
    gk_ref[...] = jnp.zeros_like(gk_ref)
    gv_ref[...] = jnp.zeros_like(gv_ref)
    for part in range(2):
        span = slice(part * part_rows, (part + 1) * part_rows)
        start = (me if part == 0 else 2 * ctx - 1 - me) * half
        last = start // KEYS
        deltas = [
            dot_nt(
                jnp.ones((8, 128), f32),
                go_ref[kh, span, :].astype(f32) * o_ref[kh, span, :],
                lax.Precision.HIGHEST,
            )[:1]
            for kh in range(KH)
        ]

        def step(i, masked):
            at = pl.ds(pl.multiple_of(i * KEYS, KEYS), KEYS)
            keys = k_ref[at, :]
            grad_k = gk_ref[at, :]
            grad_v = gv_ref[at, :]
            for kh in range(KH):
                queries = spread_ref[kh, span, :]
                heads = go_ref[kh, span, :]
                p = jnp.exp(dot_nt(keys, queries) - lse_ref[kh, part][:1])
                if masked:
                    row = lanes(p.shape) % half + start
                    key = lax.broadcasted_iota(jnp.int32, p.shape, 0) + i * KEYS
                    p = jnp.where(key <= row, p, 0.0)
                gs = (p * (dot_nt(v_ref[at, :], heads) - deltas[kh])).astype(bf16)
                grad_v += jnp.dot(p.astype(bf16), heads, preferred_element_type=f32)
                grad_k += jnp.dot(gs, queries, preferred_element_type=f32)
                gqs_ref[kh, span, :] += dot_tn(gs, keys)
            gk_ref[at, :] = grad_k
            gv_ref[at, :] = grad_v

        def body(i, carry):
            step(i, False)
            return carry

        lax.fori_loop(0, last, body, 0)
        step(last, True)
    for tile in range(WIDTH_Q // 128):
        gq_ref[:, tile * 128 : (tile + 1) * 128] = join_heads(gqs_ref, half, tile) * HD ** (-0.5)
    for j in range(ctx):
        dst = mine_ref if j < chips else other_ref
        at = (j % chips) * rows
        owner = meta_ref[1 + j]
        for part in range(2):
            place = owner if part == 0 else 2 * ctx - 1 - owner
            frm = pl.ds(pl.multiple_of(place * half, half), half)
            to = slice(at + part * half, at + (part + 1) * half)
            dst[to, :WIDTH_K] = gk_ref[frm, :].astype(dst.dtype)
            dst[to, WIDTH_K:] = gv_ref[frm, :].astype(dst.dtype)


def finish_kernel(
    gq_ref, pair_ref, x_ref, gain_ref, w_ref, cos_ref, sin_ref, gh_ref,
    joint_ref, gx_ref, gain_grad_ref, bias_ref,
):
    cosine = cos_ref[...]
    sine = sin_ref[...]
    early = lanes(cosine.shape) % HD < HD // 2
    for i in range((WIDTH_Q + WIDTH_K) // 128):
        at = slice(i * 128, (i + 1) * 128)
        grad = gq_ref[:, at] if i * 128 < WIDTH_Q else pair_ref[:, :WIDTH_K]
        scaled = grad * sine
        turned = jnp.where(early, pltpu.roll(scaled, 96, 1), -pltpu.roll(scaled, 32, 1))
        joint_ref[:, at] = (grad * cosine + turned).astype(bf16)
    joint_ref[:, WIDTH_Q + WIDTH_K :] = pair_ref[:, WIDTH_K:].astype(bf16)
    joint = joint_ref[...]
    bias_ref[...] = jnp.sum(joint.astype(f32), 0, keepdims=True)
    grad = dot_nt(joint, w_ref[...])
    x = x_ref[...].astype(f32)
    inverse = lax.rsqrt(jnp.mean(x * x, -1, keepdims=True) + EPS)
    unit = x * inverse
    gain_grad_ref[...] = jnp.sum(grad * unit, 0, keepdims=True)
    scaled = grad * gain_ref[...]
    gx_ref[...] = gh_ref[...] + inverse * (
        scaled - unit * jnp.mean(scaled * unit, -1, keepdims=True)
    )


def mlp_kernel(
    half_rows, spots_ref, x_ref, gy_ref, gate_a, gate_b, up_a, up_b, down_a, down_b,
    mid_ref, gg_ref, gu_ref, gx_ref, out_ref, send_ref, gx_acc, out_acc,
):
    step = pl.program_id(0)
    x = x_ref[...]
    gy = gy_ref[...]
    wg = jnp.concatenate([gate_a[...], gate_b[...]], 1)
    wu = jnp.concatenate([up_a[...], up_b[...]], 1)
    wd = jnp.concatenate([down_a[...], down_b[...]], 0)
    gate = jnp.dot(x, wg, preferred_element_type=f32)
    up = jnp.dot(x, wu, preferred_element_type=f32)
    grad = dot_nt(gy, wd)
    core = spots_ref[1]
    column = lanes((1, gate.shape[1])) + (step * 256 + spots_ref[2])
    own = (column < spots_ref[3]) == (core == 0)
    sigma = jax.nn.sigmoid(gate)
    active = gate * sigma
    middle = jnp.where(own, active * up, 0.0).astype(bf16)
    grad_gate = jnp.where(
        own, grad * up * (sigma * (1.0 + gate * (1.0 - sigma))), 0.0
    ).astype(bf16)
    grad_up = jnp.where(own, grad * active, 0.0).astype(bf16)
    mid_ref[...] = middle
    gg_ref[...] = grad_gate
    gu_ref[...] = grad_up
    gx = dot_nt(grad_gate, wg) + dot_nt(grad_up, wu)
    out = jnp.dot(middle, wd, preferred_element_type=f32)

    @pl.when(step == 0)
    def start():
        gx_acc[...] = gx
        out_acc[...] = out

    @pl.when(step > 0)
    def add():
        gx_acc[...] += gx
        out_acc[...] += out

    @pl.when(step == pl.num_programs(0) - 1)
    def end():
        gx_ref[...] = gx_acc[:half_rows]
        out_ref[...] = out_acc[:half_rows]
        send_ref[:half_rows] = gx_acc[half_rows:].astype(bf16)
        send_ref[half_rows:] = out_acc[half_rows:].astype(bf16)


def feed_forward(meta, x, gy, w_gate, w_up, w_down, width):
    tokens = x.shape[0]
    half = tokens // 2
    steps = width // 256
    tiles = width // 128 - 1

    def columns(j):
        return pl.BlockSpec((D, 128), lambda i, m: (0, m[1] * tiles + 2 * i + j))

    def rows(j):
        return pl.BlockSpec((128, D), lambda i, m: (m[1] * tiles + 2 * i + j, 0))

    whole = pl.BlockSpec((tokens, D), lambda i, m: (0, 0))
    halves = pl.BlockSpec((half, D), lambda i, m: (0, 0))
    tile = pl.BlockSpec((tokens, 256), lambda i, m: (0, i))
    hidden = jax.ShapeDtypeStruct((tokens, width), bf16)
    return pl.pallas_call(
        lambda *refs: mlp_kernel(half, *refs),
        out_shape=[hidden] * 3
        + [jax.ShapeDtypeStruct((half, D), f32)] * 2
        + [jax.ShapeDtypeStruct((tokens, D), bf16)],
        grid_spec=pltpu.PrefetchScalarGridSpec(
            num_scalar_prefetch=1,
            grid=(steps,),
            in_specs=[whole, whole, columns(0), columns(1), columns(0), columns(1), rows(0), rows(1)],
            out_specs=[tile, tile, tile, halves, halves, whole],
            scratch_shapes=[pltpu.VMEM((tokens, D), f32)] * 2,
        ),
        compiler_params=pltpu.CompilerParams(vmem_limit_bytes=VMEM_BYTES),
        cost_estimate=pl.CostEstimate(
            flops=12 * tokens * width * D, bytes_accessed=6 * width * D, transcendentals=0
        ),
    )(meta, x, gy, w_gate, w_gate, w_up, w_up, w_down, w_down)


def mlp_grad_kernel(
    down_rows, main, meta_ref, x_ref, gy_ref, mid_ref, gg_ref, gu_ref, out_ref, mlp_acc, down_acc
):
    step = pl.program_id(0)
    core = meta_ref[1]
    at_main = pl.ds(pl.multiple_of(core * 128, 128), main)
    at_tile = pl.ds(pl.multiple_of((1 - core) * main, 128), 128)

    @pl.when(step == 0)
    def products():
        x = x_ref[...]
        mlp_acc[:, :main] = dot_tn(x, gg_ref[:, at_main])
        mlp_acc[:, main : 2 * main] = dot_tn(x, gu_ref[:, at_main])
        mixed = gg_ref[:, at_tile].astype(f32) + pltpu.roll(gu_ref[:, at_tile].astype(f32), 64, 1)
        mlp_acc[:, 2 * main :] = dot_tn(x, mixed.astype(bf16))
        down_acc[...] = dot_tn(mid_ref[...], gy_ref[...])

    mlp_rows = mlp_acc.shape[0] // pl.num_programs(0)
    columns = mlp_acc.shape[1] // 128
    block = mlp_acc[pl.ds(pl.multiple_of(step * mlp_rows, 16), mlp_rows), :].astype(bf16)
    for j in range(columns):
        for i in range(mlp_rows // 16):
            out_ref[0, j * 16 : (j + 1) * 16, i * 128 : (i + 1) * 128] = block[
                i * 16 : (i + 1) * 16, j * 128 : (j + 1) * 128
            ]
    first = pl.multiple_of(core * 64 + step * down_rows, 8)
    out_ref[0, columns * 16 :, :] = down_acc[pl.ds(first, down_rows), :].astype(bf16)


def mlp_gradients(meta, x, gy, mid, gg, gu, chips, down_rows, main):
    tokens = x.shape[0]
    columns = (2 * main + 128) // 128
    rows = columns * 16 + down_rows
    wide = pl.BlockSpec((tokens, D), lambda i, m: (0, 0))
    tall = pl.BlockSpec((tokens, mid.shape[1]), lambda i, m: (0, 0))
    return pl.pallas_call(
        lambda *refs: mlp_grad_kernel(down_rows, main, *refs),
        out_shape=jax.ShapeDtypeStruct((chips, rows, D), bf16),
        grid_spec=pltpu.PrefetchScalarGridSpec(
            num_scalar_prefetch=1,
            grid=(chips,),
            in_specs=[wide, wide, tall, tall, tall],
            out_specs=pl.BlockSpec((1, rows, D), lambda i, m: (m[4 + i], 0, 0)),
            scratch_shapes=[
                pltpu.VMEM((D, columns * 128), f32),
                pltpu.VMEM((mid.shape[1], D), f32),
            ],
        ),
        compiler_params=pltpu.CompilerParams(vmem_limit_bytes=VMEM_BYTES),
        cost_estimate=pl.CostEstimate(
            flops=6 * tokens * mid.shape[1] * D, bytes_accessed=4 * chips * rows * D,
            transcendentals=0,
        ),
    )(meta, x, gy, mid, gg, gu)


def small_grad_kernel(chips, q_rows, meta_ref, norm_ref, joint_ref, att_ref, ga_ref, out_ref, acc):
    cols = joint_ref.shape[1]
    acc[:, :cols] = dot_tn(norm_ref[...], joint_ref[...])
    acc[:, cols:] = dot_tn(att_ref[...], ga_ref[...])
    first = (2 * meta_ref[0] + meta_ref[1]) * q_rows
    rows = acc[pl.ds(pl.multiple_of(first, 16), q_rows), :]
    count = acc.shape[1] // 128 // chips
    lanes_out = D // 128
    piece = q_rows * count // lanes_out
    for owner in range(chips):
        tall = jnp.concatenate(
            [rows[:, (owner * count + i) * 128 : (owner * count + i + 1) * 128] for i in range(count)],
            0,
        ).astype(bf16)
        slot = meta_ref[4 + owner]
        for i in range(lanes_out):
            out_ref[slot, :, i * 128 : (i + 1) * 128] = tall[i * piece : (i + 1) * piece]


def place_pairs(meta, slots, pairs, main, ff_loc, old=None):
    count = len(pairs)
    mlp_rows = D // 8
    columns = pairs[0][0].shape[0] // 16
    tiles = main // 128
    blocks = [x for pair in pairs for x in pair]

    def kernel(meta_ref, *refs):
        step = pl.program_id(0)
        gate_ref, up_ref, token_ref = refs[-3:]
        token_ref[...] = jnp.zeros(token_ref.shape, f32)
        core_zero = meta_ref[1] == 0

        def column(ref, j):
            parts = [
                ref[j * 16 : (j + 1) * 16, i * 128 : (i + 1) * 128] for i in range(mlp_rows // 16)
            ]
            return jnp.concatenate(parts, 0).astype(f32)

        for k in range(count):

            @pl.when(step == k)
            def write(k=k):
                for j in range(columns):
                    got = column(refs[2 * k], j)
                    other = column(refs[2 * k + 1], j)
                    zero = jnp.where(core_zero, got, other)
                    one = jnp.where(core_zero, other, got)
                    if j < 2 * tiles:
                        ref = gate_ref if j < tiles else up_ref
                        at = (j % tiles) * 128
                        ref[:, at : at + 128] = zero
                        ref[:, at + main + 128 : at + main + 256] = one
                    else:
                        left = lanes(zero.shape) < 64
                        gate_ref[:, main : main + 128] = jnp.where(left, zero, one)
                        up_ref[:, main : main + 128] = pltpu.roll(jnp.where(left, one, zero), 64, 1)

    keep = [] if old is None else list(old)
    out_spec = pl.BlockSpec((mlp_rows, ff_loc), lambda i, m: (m[12 + pick(slots, i)], 0))
    return pl.pallas_call(
        kernel,
        out_shape=[jax.ShapeDtypeStruct((D, ff_loc), f32)] * 2
        + [jax.ShapeDtypeStruct((8, 128), f32)],
        grid_spec=pltpu.PrefetchScalarGridSpec(
            num_scalar_prefetch=1,
            grid=(count,),
            in_specs=[pl.BlockSpec(blocks[0].shape, lambda i, m: (0, 0))] * (2 * count)
            + [pl.BlockSpec(memory_space=pl.ANY)] * len(keep),
            out_specs=[out_spec, out_spec, pl.BlockSpec((8, 128), lambda i, m: (0, 0))],
        ),
        input_output_aliases={} if old is None else {2 * count + 1: 0, 2 * count + 2: 1},
        compiler_params=pltpu.CompilerParams(vmem_limit_bytes=VMEM_BYTES),
        cost_estimate=pl.CostEstimate(
            flops=0, bytes_accessed=count * mlp_rows * ff_loc * 16, transcendentals=0
        ),
    )(meta, *blocks, *keep)


def pick(values, i):
    out = values[0]
    for k in range(1, len(values)):
        out = jnp.where(i == k, values[k], out)
    return out


def place_rest(meta, slots, pairs, down_rows, q_rows, ff_loc, cols, chips, old=None):
    count = len(pairs)
    blocks = [x for pair in pairs for x in pair]
    lanes_out = D // 128
    piece = blocks[0].shape[0] - down_rows

    def kernel(meta_ref, *refs):
        step = pl.program_id(0)
        down_ref, small_ref, token_ref = refs[-3:]
        token_ref[...] = jnp.zeros(token_ref.shape, f32)
        for k in range(2 * count):

            @pl.when(step == k)
            def write(k=k):
                ref = refs[k]
                down_ref[...] = ref[piece:, :].astype(f32)
                tall = jnp.concatenate(
                    [ref[:piece, i * 128 : (i + 1) * 128] for i in range(lanes_out)], 0
                ).astype(f32)
                for i in range(tall.shape[0] // q_rows):
                    small_ref[:, i * 128 : (i + 1) * 128] = tall[i * q_rows : (i + 1) * q_rows]

    keep = [] if old is None else list(old)

    def side(i, m):
        return jnp.where(i % 2 == 0, m[1], 1 - m[1])

    def owner(i, m):
        return m[12 + pick(slots, i // 2)]

    return pl.pallas_call(
        kernel,
        out_shape=[
            jax.ShapeDtypeStruct((ff_loc, D), f32),
            jax.ShapeDtypeStruct((2 * q_rows, cols), f32),
            jax.ShapeDtypeStruct((8, 128), f32),
        ],
        grid_spec=pltpu.PrefetchScalarGridSpec(
            num_scalar_prefetch=1,
            grid=(2 * count,),
            in_specs=[pl.BlockSpec(blocks[0].shape, lambda i, m: (0, 0))] * (2 * count)
            + [pl.BlockSpec(memory_space=pl.ANY)] * len(keep),
            out_specs=[
                pl.BlockSpec((down_rows, D), lambda i, m: (side(i, m) * chips + owner(i, m), 0)),
                pl.BlockSpec((q_rows, cols // chips), lambda i, m: (side(i, m), owner(i, m))),
                pl.BlockSpec((8, 128), lambda i, m: (0, 0)),
            ],
        ),
        input_output_aliases={} if old is None else {2 * count + 1: 0, 2 * count + 2: 1},
        compiler_params=pltpu.CompilerParams(vmem_limit_bytes=VMEM_BYTES),
        cost_estimate=pl.CostEstimate(
            flops=0, bytes_accessed=count * down_rows * D * 16, transcendentals=0
        ),
    )(meta, *blocks, *keep)


def place_blocks(blocks, spots, out_shape, old=None):
    shape = blocks[0].shape
    count = len(blocks)
    if shape[0] % 8 or shape[1] % 128:
        out = jnp.zeros(out_shape, f32) if old is None else old
        for block, (i, j) in zip(blocks, spots):
            out = lax.dynamic_update_slice(
                out, block.astype(f32), (i * shape[0], j * shape[1])
            )
        return out

    def kernel(spots_ref, *refs):
        step = pl.program_id(0)
        out_ref = refs[-1]
        for i in range(count):

            @pl.when(step == i)
            def write(i=i):
                out_ref[...] = refs[i][...].astype(f32)

    keep = [] if old is None else [old]
    return pl.pallas_call(
        kernel,
        out_shape=jax.ShapeDtypeStruct(out_shape, f32),
        grid_spec=pltpu.PrefetchScalarGridSpec(
            num_scalar_prefetch=1,
            grid=(count,),
            in_specs=[pl.BlockSpec(shape, lambda i, spots: (0, 0))] * count
            + [pl.BlockSpec(memory_space=pl.ANY)] * len(keep),
            out_specs=pl.BlockSpec(shape, lambda i, spots: (spots[i, 0], spots[i, 1])),
        ),
        input_output_aliases={} if old is None else {count + 1: 0},
        compiler_params=pltpu.CompilerParams(vmem_limit_bytes=VMEM_BYTES),
    )(jnp.stack([jnp.stack(s) for s in spots]).astype(jnp.int32), *blocks, *keep)


def local(tokens, w_qkv, b_qkv, w_out, gain_attn, gain_mlp, w_gate, w_up, w_down, cotangent):
    net = Net()
    rows = tokens.shape[1]
    half_rows = rows // 2
    ctx_count = net.ctx
    core = net.core
    chips = net.chips
    part_rows = GROUP * half_rows
    x = tokens[0]
    gain_one = gain_attn[None]
    gain_two = gain_mlp[None]

    w_qkv_full = net.full_rows(w_qkv)

    ff_loc = w_gate.shape[1]
    ff_half = ff_loc // 2
    main = (ff_half // 128) * 128
    rest = ff_half - main
    width = main + 2 * rest
    first = core * main
    tiled = 2 * rest == 128 and width % 256 == 0 and chips == 8 and (ff_half // chips) % 8 == 0
    ring = jnp.arange(chips, dtype=jnp.int32)
    owners_of = (net.pos - ring) % chips
    spots = jnp.concatenate(
        [jnp.stack([net.d, core, first, jnp.int32(ff_half)]), owners_of, owners_of]
    ).astype(jnp.int32)

    row_ids = jnp.arange(half_rows, dtype=jnp.int32)
    place = jnp.concatenate(
        [net.c * half_rows + row_ids, (2 * ctx_count - 1 - net.c) * half_rows + row_ids]
    )
    freq = ROPE_BASE ** (-((jnp.arange(128) % (HD // 2)).astype(f32) * (2.0 / HD)))
    angle = place.astype(f32)[:, None] * freq[None, :]
    cosine, sine = jnp.cos(angle), jnp.sin(angle)
    normed_one, queries, pairs = call(
        qkv_kernel,
        [
            jax.ShapeDtypeStruct((rows, D), bf16),
            jax.ShapeDtypeStruct((rows, WIDTH_Q), bf16),
            jax.ShapeDtypeStruct((rows, 2 * WIDTH_K), bf16),
        ],
        [x, gain_one, w_qkv_full, b_qkv[None], cosine, sine],
        flops=2 * rows * D * 1152,
    )

    slots = net.ring_gather(pairs)
    mine = jnp.concatenate(slots, 0)
    other = net.swap(mine)
    order = jnp.array(net.order, jnp.int32)
    chip_ids = order[(net.pos - jnp.arange(chips, dtype=jnp.int32)) % chips]
    meta = jnp.concatenate([net.c[None], 2 * chip_ids + core, 2 * chip_ids + 1 - core])
    meta = meta.astype(jnp.int32)

    late_w, late_g, late_n, unused = lax.optimization_barrier((w_out, cotangent[0], normed_one, pairs))
    w_out_full = net.full_rows(late_w)
    early_group = net.group_gather(jnp.concatenate([late_g, late_n], 1))
    grad_out_group = early_group[:, :D]
    normed_one_group = early_group[:, D:]

    total_keys = rows * ctx_count
    padded = (KH, 2 * part_rows, 128)
    attended_low, attended, lse, spread, keys, values, hidden, normed_two = call(
        lambda *refs: forward_kernel(ctx_count, *refs),
        [
            jax.ShapeDtypeStruct((rows, WIDTH_Q), bf16),
            jax.ShapeDtypeStruct(padded, f32),
            jax.ShapeDtypeStruct((KH, 2, 8, part_rows), f32),
            jax.ShapeDtypeStruct(padded, bf16),
            jax.ShapeDtypeStruct((total_keys, WIDTH_K), bf16),
            jax.ShapeDtypeStruct((total_keys, WIDTH_K), bf16),
            jax.ShapeDtypeStruct((rows, D), f32),
            jax.ShapeDtypeStruct((rows, D), bf16),
        ],
        [meta, queries, mine, other, x, w_out_full, gain_two],
        smem=1,
        scratch=[
            pltpu.VMEM((KH, total_keys // KEYS, part_rows, KEYS), f32),
            pltpu.VMEM((KH, part_rows, 128), f32),
            pltpu.VMEM((KH, part_rows, 128), f32),
        ],
        flops=8 * KH * part_rows * total_keys * 128,
    )

    normed_two_group = net.group_gather(normed_two)
    chip_rows = net.dp * rows
    down_rows = ff_half // chips
    mlp_rows = D // chips
    if tiled:
        mid, gate_low, up_low, grad_mine, out_mine, sent = feed_forward(
            spots, normed_two_group, grad_out_group, w_gate, w_up, w_down, width
        )
    else:
        own_cols = (jnp.arange(width) + first < ff_half) == (core == 0)
        wg = lax.dynamic_slice(w_gate, (0, first), (D, width))
        wu = lax.dynamic_slice(w_up, (0, first), (D, width))
        wd = lax.dynamic_slice(w_down, (first, 0), (width, D))
        gate = jnp.dot(normed_two_group, wg, preferred_element_type=f32)
        upper = jnp.dot(normed_two_group, wu, preferred_element_type=f32)
        sigma = jax.nn.sigmoid(gate)
        activated = gate * sigma
        middle = jnp.where(own_cols, activated * upper, 0.0).astype(bf16)
        grad_middle = jnp.einsum("td,fd->tf", grad_out_group, wd, preferred_element_type=f32)
        slope = sigma * (1.0 + gate * (1.0 - sigma))
        grad_gate_low = jnp.where(own_cols, grad_middle * upper * slope, 0.0).astype(bf16)
        grad_up_low = jnp.where(own_cols, grad_middle * activated, 0.0).astype(bf16)

        grad_normed_two = jnp.einsum(
            "tf,df->td", grad_gate_low, wg, preferred_element_type=f32
        ) + jnp.einsum("tf,df->td", grad_up_low, wu, preferred_element_type=f32)
        mlp_out = jnp.dot(middle, wd, preferred_element_type=f32)
        grad_mine, out_mine = grad_normed_two[:chip_rows], mlp_out[:chip_rows]
        sent = jnp.concatenate([grad_normed_two[chip_rows:], mlp_out[chip_rows:]], 0).astype(bf16)
    swapped = net.swap(sent)
    grad_chip = grad_mine + swapped[:chip_rows].astype(f32)
    mlp_chip = out_mine + swapped[chip_rows:].astype(f32)
    grad_two = grad_chip[:rows]
    for s in range(1, net.dp):
        piece = grad_chip[s * rows : (s + 1) * rows].astype(bf16)
        grad_two = grad_two + net.shift(piece, net.dp - s).astype(f32)

    if tiled:
        terms = mlp_gradients(
            spots, normed_two_group, grad_out_group, mid, gate_low, up_low, chips, down_rows, main
        )
        summed = net.ring_scatter([terms[s] for s in range(chips)]).astype(bf16)
        sum_mlp = summed[: terms.shape[1] - down_rows]
        sum_down = summed[terms.shape[1] - down_rows :]
    else:
        part_down = jnp.einsum(
            "tf,td->fd", middle, grad_out_group, preferred_element_type=f32
        ).astype(bf16)
        part_down = lax.dynamic_slice(part_down, (core * rest, 0), (ff_half, D))

        def down_chunk(slot):
            return lax.dynamic_slice(part_down, (net.owner(slot) * down_rows, 0), (down_rows, D))

        sum_down = net.ring_scatter([down_chunk(s) for s in range(chips)]).astype(bf16)

        def split_main(x):
            left = (x[:, :main], x[:, main:])
            right = (x[:, 2 * rest :], x[:, : 2 * rest])
            return (
                jnp.where(core == 0, left[0], right[0]),
                jnp.where(core == 0, left[1], right[1]),
            )

        gate_main, gate_tile = split_main(grad_gate_low)
        up_main, up_tile = split_main(grad_up_low)
        packed = jnp.concatenate(
            [gate_main, up_main, gate_tile + jnp.roll(up_tile, rest, 1)], 1
        )
        part_mlp = jnp.einsum(
            "td,tf->df", normed_two_group, packed, preferred_element_type=f32
        ).astype(bf16)

        def mlp_chunk(slot):
            return lax.dynamic_slice(
                part_mlp, (net.owner(slot) * mlp_rows, 0), (mlp_rows, 2 * ff_half)
            )

        sum_mlp = net.ring_scatter([mlp_chunk(s) for s in range(chips)]).astype(bf16)
        sum_mlp = lax.optimization_barrier(sum_mlp)

    grad_hidden, grad_attn_low, grad_gain_two, grad_queries, terms_mine, terms_other = call(
        lambda *refs: backward_kernel(ctx_count, *refs),
        [
            jax.ShapeDtypeStruct((rows, D), f32),
            jax.ShapeDtypeStruct((rows, D), bf16),
            jax.ShapeDtypeStruct((1, D), f32),
            jax.ShapeDtypeStruct((rows, WIDTH_Q), f32),
            jax.ShapeDtypeStruct((chips * rows, 2 * WIDTH_K), f32),
            jax.ShapeDtypeStruct((chips * rows, 2 * WIDTH_K), bf16),
        ],
        [
            meta, grad_two, hidden, cotangent[0], gain_two, w_out_full, spread, keys, values, lse,
            attended,
        ],
        smem=1,
        scratch=[
            pltpu.VMEM(padded, bf16),
            pltpu.VMEM(padded, f32),
            pltpu.VMEM((total_keys, WIDTH_K), f32),
            pltpu.VMEM((total_keys, WIDTH_K), f32),
        ],
        flops=20 * KH * part_rows * total_keys * 128,
    )
    pair_sums = (terms_mine + net.swap(terms_other).astype(f32)).astype(bf16)
    grad_pairs = net.ring_scatter(
        [pair_sums[s * rows : (s + 1) * rows] for s in range(chips)]
    )
    grad_joint_low, grad_input, grad_gain_one, grad_bias = call(
        finish_kernel,
        [
            jax.ShapeDtypeStruct((rows, 1152), bf16),
            jax.ShapeDtypeStruct((rows, D), f32),
            jax.ShapeDtypeStruct((1, D), f32),
            jax.ShapeDtypeStruct((1, 1152), f32),
        ],
        [grad_queries, grad_pairs, x, gain_one, w_qkv_full, cosine, sine, grad_hidden],
        flops=2 * rows * D * 1152,
    )

    out_sum = mlp_chip[:rows]
    sent = jnp.concatenate([attended_low, grad_attn_low], 0)
    gathered = [sent]
    for s in range(1, net.dp):
        got = net.shift(
            jnp.concatenate([mlp_chip[s * rows : (s + 1) * rows].astype(bf16), sent], 0),
            net.dp - s,
        )
        out_sum = out_sum + got[:rows].astype(f32)
        gathered.append(got[rows:])
    output = (hidden + out_sum).astype(bf16)
    gathered = jnp.concatenate(gathered, 0)
    gathered = jnp.concatenate([gathered, net.swap(gathered)], 0).reshape(2 * net.dp, 2, rows, D)
    attended_group = gathered[:, 0].reshape(2 * net.dp * rows, D)
    grad_attn_group = gathered[:, 1].reshape(2 * net.dp * rows, D)

    q_rows = w_qkv.shape[0] // 2
    qkv_cols = w_qkv.shape[1]
    joint_group = net.group_gather(grad_joint_low)
    if tiled:
        piece = q_rows * (qkv_cols + D) // chips // D
        terms_small = call(
            lambda *refs: small_grad_kernel(chips, q_rows, *refs),
            [jax.ShapeDtypeStruct((chips, piece, D), bf16)],
            [spots, normed_one_group, joint_group, attended_group, grad_attn_group],
            smem=1,
            scratch=[pltpu.VMEM((D, qkv_cols + D), f32)],
            flops=4 * chip_rows * D * (qkv_cols + D),
        )[0]
        sum_small = net.ring_scatter([terms_small[s] for s in range(chips)]).astype(bf16)
        rest_block = jnp.concatenate([sum_small, sum_down], 0)
        (grad_gate, grad_up), (grad_down, grad_small) = net.gather_both(
            sum_mlp,
            rest_block,
            lambda slots, pairs, old: place_pairs(spots, slots, pairs, main, ff_loc, old),
            lambda slots, pairs, old: place_rest(
                spots, slots, pairs, down_rows, q_rows, ff_loc, qkv_cols + D, chips, old
            ),
        )
    else:
        q_first = net.d * (2 * q_rows) + core * q_rows
        group_rows = 2 * net.dp * rows
        part_out = jnp.einsum(
            "tc,td->cd",
            lax.dynamic_slice(attended_group, (0, q_first), (group_rows, q_rows)),
            grad_attn_group,
            preferred_element_type=f32,
        )
        part_joint = jnp.einsum(
            "td,tc->dc",
            lax.dynamic_slice(normed_one_group, (0, q_first), (group_rows, q_rows)),
            joint_group,
            preferred_element_type=f32,
        )
        part_small = jnp.concatenate([part_joint, part_out], 1).astype(bf16)
        small_cols = part_small.shape[1] // chips

        def small_chunk(slot):
            return lax.dynamic_slice(part_small, (0, net.owner(slot) * small_cols), (q_rows, small_cols))

        sum_small = net.ring_scatter([small_chunk(s) for s in range(chips)]).astype(bf16)

        tall = jnp.concatenate(
            [sum_small[:, i * 128 : (i + 1) * 128] for i in range(small_cols // 128)], 0
        )
        piece = tall.shape[0] // (D // 128)
        wide = jnp.concatenate([tall[i * piece : (i + 1) * piece] for i in range(D // 128)], 1)
        both = lax.optimization_barrier(jnp.concatenate([sum_down, wide], 0))

        owners = [net.owner(s) for s in range(chips)]
        got_mlp = net.ring_gather(sum_mlp)
        got_both = net.ring_gather(both)
        pairs_mlp = [(got, net.swap(got)) for got in got_mlp]
        pairs_both = [(got, net.swap(got)) for got in got_both]

        down_blocks, down_spots, small_blocks, small_spots = [], [], [], []
        for owner, pair in zip(owners, pairs_both):
            for which, got in zip((core, 1 - core), pair):
                down_blocks.append(got[:down_rows])
                down_spots.append((which * chips + owner, jnp.int32(0)))
                wide = got[down_rows:]
                tall = jnp.concatenate([wide[:, i * 128 : (i + 1) * 128] for i in range(D // 128)], 0)
                small_blocks.append(
                    jnp.concatenate(
                        [tall[i * q_rows : (i + 1) * q_rows] for i in range(small_cols // 128)], 1
                    )
                )
                small_spots.append((which, owner))
        grad_down = place_blocks(down_blocks, down_spots, (ff_loc, D))
        grad_small = place_blocks(small_blocks, small_spots, (2 * q_rows, part_small.shape[1]))
        grad_gate = jnp.zeros((D, ff_loc), f32)
        grad_up = jnp.zeros((D, ff_loc), f32)
        left_lane = jnp.arange(2 * rest) < rest
        for owner, (got, swapped) in zip(owners, pairs_mlp):
            zero = jnp.where(core == 0, got, swapped).astype(f32)
            one = jnp.where(core == 0, swapped, got).astype(f32)
            tile_zero, tile_one = zero[:, 2 * main :], one[:, 2 * main :]
            mid_gate = jnp.where(left_lane, tile_zero, tile_one)
            mid_up = jnp.roll(jnp.where(left_lane, tile_one, tile_zero), rest, 1)
            base = owner * mlp_rows
            grad_gate = lax.dynamic_update_slice(
                grad_gate, jnp.concatenate([zero[:, :main], mid_gate, one[:, :main]], 1), (base, 0)
            )
            grad_up = lax.dynamic_update_slice(
                grad_up,
                jnp.concatenate([zero[:, main : 2 * main], mid_up, one[:, main : 2 * main]], 1),
                (base, 0),
            )

    small = net.total(jnp.concatenate([grad_gain_one, grad_gain_two, grad_bias], 1))[0]
    return (
        output[None],
        grad_input[None],
        grad_small[:, :qkv_cols],
        small[2 * D :],
        grad_small[:, qkv_cols:],
        small[:D],
        small[D : 2 * D],
        grad_gate,
        grad_up,
        grad_down,
    )


def solution(mesh):
    placed = (
        P("dp", "ctx", None),
        P("dp", None),
        P(),
        P("dp", None),
        P(),
        P(),
        P(None, "dp"),
        P(None, "dp"),
        P("dp", None),
        P("dp", "ctx", None),
    )
    return jax.shard_map(
        local,
        mesh=mesh,
        in_specs=placed,
        out_specs=(
            P("dp", "ctx", None),
            P("dp", "ctx", None),
            P("dp", None),
            P(),
            P("dp", None),
            P(),
            P(),
            P(None, "dp"),
            P(None, "dp"),
            P("dp", None),
        ),
        check_vma=False,
    )
```

```python
import jax
import jax.numpy as jnp
from jax import lax
from jax.experimental import pallas as pl
from jax.experimental.pallas import tpu as pltpu
from jax.sharding import PartitionSpec as P

D = 896
QH = 14
KH = 2
HD = 64
GROUP = QH // KH
WIDTH_Q = QH * HD
WIDTH_K = KH * HD

EPS = 1e-06
ROPE_BASE = 1000000.0

f32 = jnp.float32
bf16 = jnp.bfloat16


def ring_order(chips):
    if chips % 2:
        return list(range(chips))
    rows = chips // 2
    return [2 * i for i in range(rows)] + [2 * i + 1 for i in reversed(range(rows))]


def half_cut(rows):
    cut = (rows // 2 + 7) // 8 * 8
    return cut if cut < rows else rows // 2


class Net:
    def __init__(self):
        self.dp = lax.axis_size("dp")
        self.ctx = lax.axis_size("ctx")
        self.chips = self.ctx // 2
        self.order = ring_order(self.chips)
        self.d = lax.axis_index("dp")
        self.c = lax.axis_index("ctx")
        self.core = self.c % 2
        place = [0] * self.chips
        for spot, chip in enumerate(self.order):
            place[chip] = spot
        self.pos = jnp.array(place, jnp.int32)[self.c // 2]

    def swap(self, x):
        return lax.ppermute(x, "ctx", [(i, i ^ 1) for i in range(self.ctx)])

    def shift(self, x, step):
        n = self.dp
        return lax.ppermute(x, "dp", [(i, (i + step) % n) for i in range(n)])

    def hop(self, x, step):
        n = self.chips
        perm = []
        for spot in range(n):
            for core in range(2):
                perm.append((2 * self.order[spot] + core, 2 * self.order[(spot + step) % n] + core))
        return lax.ppermute(x, "ctx", perm)

    def owner(self, slot):
        return (self.pos - slot) % self.chips

    def group_gather(self, x):
        chip = jnp.concatenate([x] + [self.shift(x, s) for s in range(1, self.dp)], 0)
        return jnp.concatenate([chip, self.swap(chip)], 0)

    def ring_gather(self, x):
        n = self.chips
        half = n // 2
        cut = half_cut(x.shape[0])
        found = [x] + [None] * (n - 1)
        fwd, back = x, x
        for s in range(1, half):
            fwd = self.hop(fwd, 1)
            back = self.hop(back, -1)
            found[s] = fwd
            found[n - s] = back
        found[half] = jnp.concatenate([self.hop(fwd[:cut], 1), self.hop(back[cut:], -1)], 0)
        return found

    def ring_scatter(self, local):
        n = self.chips
        half = n // 2
        cut = half_cut(local[half].shape[0])

        def add(got, mine):
            return (got.astype(f32) + mine.astype(f32)).astype(bf16)

        fwd = self.hop(local[half][:cut], 1)
        back = self.hop(local[half][cut:], -1)
        for s in range(1, half):
            mine_f = local[half + s]
            mine_b = local[half - s]
            if s == 1:
                mine_f = jnp.concatenate([add(fwd, mine_f[:cut]), mine_f[cut:]], 0)
                mine_b = jnp.concatenate([mine_b[:cut], add(back, mine_b[cut:])], 0)
            else:
                mine_f = add(fwd, mine_f)
                mine_b = add(back, mine_b)
            fwd = self.hop(mine_f, 1)
            back = self.hop(mine_b, -1)
        return fwd.astype(f32) + back.astype(f32) + local[0].astype(f32)

    def full_rows(self, shard):
        rows = shard.shape[0]
        half = rows // 2
        piece = lax.dynamic_slice(shard, (self.core * half, 0), (half, shard.shape[1]))
        blocks = [shard]
        for s in range(1, self.dp):
            got = self.shift(piece, s)
            other = self.swap(got)
            low = jnp.where(self.core == 0, got, other)
            high = jnp.where(self.core == 0, other, got)
            blocks.append(jnp.concatenate([low, high], 0))
        if self.dp == 2:
            first = jnp.where(self.d == 0, blocks[0], blocks[1])
            second = jnp.where(self.d == 0, blocks[1], blocks[0])
            return jnp.concatenate([first, second], 0)
        ranked = jnp.stack(blocks)[(self.d - jnp.arange(self.dp)) % self.dp]
        return ranked.reshape(self.dp * rows, shard.shape[1])

    def total(self, x):
        x = x + self.swap(x)
        bit = 1
        while bit < self.chips:
            x = x + lax.ppermute(x, "ctx", [(i, i ^ (2 * bit)) for i in range(self.ctx)])
            bit *= 2
        bit = 1
        while bit < self.dp:
            x = x + lax.ppermute(x, "dp", [(i, i ^ bit) for i in range(self.dp)])
            bit *= 2
        return x

    def send_gather(self, x):
        return [x] + [self.hop(x, s) for s in range(1, self.chips)]

    def send_scatter(self, local):
        return [self.hop(local[s], -s) for s in range(1, self.chips)]

    def ring_sum(self, head, tail, terms, split):
        n = self.chips
        half = n // 2
        fwd, back = self.hop(head, 1), self.hop(tail, -1)
        for s in range(1, half):
            fwd = self.hop(ring_add(fwd, terms, half + s, 0), 1)
            back = self.hop(ring_add(back, terms, half - s, 1), -1)
        return ring_end(fwd, back, terms, split)

    def gather_both(self, a, b, place_a, place_b):
        n = self.chips
        half = n // 2
        streams = [
            [x, x, None, ([0], [(x, self.swap(x))]), place] for x, place in ((a, place_a), (b, place_b))
        ]
        for s in range(1, half + 1):
            for stream in streams:
                fwd, back, placed, waiting, place = stream
                if s > 1:
                    placed, fwd = place(*waiting, placed, fwd)
                    pairs = [(fwd, self.swap(fwd)), (back, self.swap(back))]
                    waiting = ([s - 1, n - s + 1], pairs)
                if s < half:
                    fwd, back = self.hop(fwd, 1), self.hop(back, -1)
                else:
                    cut = half_cut(fwd.shape[0])
                    fwd, back = self.hop(fwd[:cut], 1), self.hop(back[cut:], -1)
                stream[:4] = [fwd, back, placed, waiting]
        results = []
        for fwd, back, placed, waiting, place in streams:
            far = jnp.concatenate([fwd, back], 0)
            placed, far = place(*waiting, placed, far)
            results.append(place([half], [(far, self.swap(far))], placed, None)[0])
        return results


VMEM_BYTES = 56 * 1024 * 1024
KEYS = 256


def full_spec(shape):
    return pl.BlockSpec(shape, lambda: (0,) * len(shape))


def call(kernel, outs, args, smem=0, scratch=(), flops=0):
    specs = [pl.BlockSpec(memory_space=pltpu.SMEM)] * smem
    specs += [pl.BlockSpec(memory_space=pltpu.VMEM)] * (len(args) - smem)
    moved = sum(x.size * x.dtype.itemsize for x in list(args) + list(outs))
    return pl.pallas_call(
        kernel,
        out_shape=list(outs),
        in_specs=specs,
        out_specs=[pl.BlockSpec(memory_space=pltpu.VMEM)] * len(outs),
        scratch_shapes=list(scratch),
        compiler_params=pltpu.CompilerParams(vmem_limit_bytes=VMEM_BYTES),
        cost_estimate=pl.CostEstimate(flops=flops, bytes_accessed=moved, transcendentals=0),
    )(*args)


def lanes(shape):
    return lax.broadcasted_iota(jnp.int32, shape, len(shape) - 1)


def dot_nt(a, b, precision=None):
    return lax.dot_general(
        a, b, (((1,), (1,)), ((), ())), preferred_element_type=f32, precision=precision
    )


def dot_tn(a, b):
    return lax.dot_general(a, b, (((0,), (0,)), ((), ())), preferred_element_type=f32)


def ring_add(got, terms, slot, side):
    rows, columns = terms.shape[1:]
    some = got.shape[0]

    def kernel(got_ref, term_ref, out_ref):
        first = 0 if side == 0 else rows - some
        out_ref[...] = term_ref[0]
        here = slice(first, first + some)
        total = got_ref[...].astype(f32) + term_ref[0, here, :].astype(f32)
        out_ref[here, :] = total.astype(bf16)

    return pl.pallas_call(
        kernel,
        out_shape=jax.ShapeDtypeStruct((rows, columns), bf16),
        grid=(1,),
        in_specs=[
            pl.BlockSpec(got.shape, lambda i: (0, 0)),
            pl.BlockSpec((1, rows, columns), lambda i: (slot, 0, 0)),
        ],
        out_specs=pl.BlockSpec((rows, columns), lambda i: (0, 0)),
        compiler_params=pltpu.CompilerParams(vmem_limit_bytes=VMEM_BYTES),
        cost_estimate=pl.CostEstimate(
            flops=0, bytes_accessed=6 * rows * columns, transcendentals=0
        ),
    )(got, terms)


def ring_end(fwd, back, terms, split):
    rows, columns = terms.shape[1:]

    def kernel(fwd_ref, back_ref, term_ref, first_ref, rest_ref):
        for ref, here in ((first_ref, slice(0, split)), (rest_ref, slice(split, rows))):
            total = fwd_ref[here, :].astype(f32) + back_ref[here, :].astype(f32)
            ref[...] = (total + term_ref[0, here, :].astype(f32)).astype(bf16)

    whole = pl.BlockSpec((rows, columns), lambda i: (0, 0))
    return pl.pallas_call(
        kernel,
        out_shape=[
            jax.ShapeDtypeStruct((split, columns), bf16),
            jax.ShapeDtypeStruct((rows - split, columns), bf16),
        ],
        grid=(1,),
        in_specs=[whole, whole, pl.BlockSpec((1, rows, columns), lambda i: (0, 0, 0))],
        out_specs=[
            pl.BlockSpec((split, columns), lambda i: (0, 0)),
            pl.BlockSpec((rows - split, columns), lambda i: (0, 0)),
        ],
        compiler_params=pltpu.CompilerParams(vmem_limit_bytes=VMEM_BYTES),
        cost_estimate=pl.CostEstimate(
            flops=0, bytes_accessed=8 * rows * columns, transcendentals=0
        ),
    )(fwd, back, terms)


def pair_kernel(mine_ref, got_ref, *out_refs):
    rows = out_refs[0].shape[0]
    for s, out_ref in enumerate(out_refs):
        here = slice(s * rows, (s + 1) * rows)
        out_ref[...] = (mine_ref[here, :] + got_ref[here, :].astype(f32)).astype(out_ref.dtype)


def rest_kernel(*refs):
    small = refs[0][...].astype(f32)
    for ref in refs[1:-2]:
        small = small + ref[...].astype(f32)
    out_ref = refs[-1]
    piece = small.shape[0]
    out_ref[:piece, :] = small.astype(bf16)
    out_ref[piece:, :] = refs[-2][...]


def qkv_kernel(x_ref, gain_ref, w_ref, b_ref, cos_ref, sin_ref, norm_ref, q_ref, pair_ref):
    x = x_ref[...].astype(f32)
    inverse = lax.rsqrt(jnp.mean(x * x, -1, keepdims=True) + EPS)
    normed = (x * inverse * gain_ref[...]).astype(bf16)
    norm_ref[...] = normed
    joint = jnp.dot(normed, w_ref[...], preferred_element_type=f32) + b_ref[...]
    cosine = cos_ref[...]
    sine = sin_ref[...]
    early = lanes(cosine.shape) % HD < HD // 2
    for i in range((WIDTH_Q + WIDTH_K) // 128):
        tile = joint[:, i * 128 : (i + 1) * 128]
        turned = jnp.where(early, -pltpu.roll(tile, 96, 1), pltpu.roll(tile, 32, 1))
        turned = tile * cosine + turned * sine
        if i * 128 < WIDTH_Q:
            q_ref[:, i * 128 : (i + 1) * 128] = turned.astype(bf16)
        else:
            pair_ref[:, :WIDTH_K] = turned.astype(bf16)
    pair_ref[:, WIDTH_K:] = joint[:, WIDTH_Q + WIDTH_K :].astype(bf16)


def spread_heads(x, out_ref, factor):
    rows = x.shape[0]
    half = rows // 2
    for head in range(QH):
        kh, g = divmod(head, GROUP)
        tile = x[:, (head // 2) * 128 : (head // 2 + 1) * 128].astype(f32)
        if head % 2 != kh:
            tile = pltpu.roll(tile, HD, 1)
        tile = jnp.where(lanes(tile.shape) // HD == kh, tile * factor, 0.0).astype(out_ref.dtype)
        for part in range(2):
            start = (part * GROUP + g) * half
            out_ref[kh, start : start + half, :] = tile[part * half : (part + 1) * half]


def join_heads(src_ref, half, tile):
    sides = []
    for side in range(2):
        kh, g = divmod(2 * tile + side, GROUP)
        parts = [
            src_ref[kh, (part * GROUP + g) * half : (part * GROUP + g + 1) * half, :]
            for part in range(2)
        ]
        both = jnp.concatenate(parts, 0)
        sides.append(both if side == kh else pltpu.roll(both, HD, 1))
    return jnp.where(lanes(sides[0].shape) < HD, sides[0], sides[1])


def forward_kernel(
    ctx, meta_ref, q_ref, mine_ref, other_ref, x_ref, w_ref, gain_ref,
    low_ref, o_ref, lse_ref, spread_ref, k_ref, v_ref, hidden_ref, normed_ref,
    s_ref, max_ref, sum_ref,
):
    rows = q_ref.shape[0]
    half = rows // 2
    part_rows = GROUP * half
    me = meta_ref[0]
    chips = ctx // 2
    for j in range(ctx):
        src = mine_ref if j < chips else other_ref
        at = (j % chips) * rows
        owner = meta_ref[1 + j]
        for part in range(2):
            place = owner if part == 0 else 2 * ctx - 1 - owner
            to = pl.ds(pl.multiple_of(place * half, half), half)
            block = src[at + part * half : at + (part + 1) * half, :]
            k_ref[to, :] = block[:, :WIDTH_K]
            v_ref[to, :] = block[:, WIDTH_K:]
    spread_heads(q_ref[...], spread_ref, HD ** (-0.5))
    for part in range(2):
        span = slice(part * part_rows, (part + 1) * part_rows)
        start = (me if part == 0 else 2 * ctx - 1 - me) * half
        last = start // KEYS

        def keys_of(ref, i):
            return ref[pl.ds(pl.multiple_of(i * KEYS, KEYS), KEYS), :]

        for kh in range(KH):
            scores = dot_nt(spread_ref[kh, span, :], keys_of(k_ref, last))
            row = lax.broadcasted_iota(jnp.int32, scores.shape, 0) % half + start
            scores = jnp.where(lanes(scores.shape) + last * KEYS <= row, scores, -1e30)
            s_ref[kh, last] = scores
            max_ref[kh] = jnp.maximum(scores[:, :128], scores[:, 128:])

        def score(i, carry):
            for kh in range(KH):
                s = dot_nt(spread_ref[kh, span, :], keys_of(k_ref, i))
                s_ref[kh, i] = s
                max_ref[kh] = jnp.maximum(max_ref[kh], jnp.maximum(s[:, :128], s[:, 128:]))
            return carry

        lax.fori_loop(0, last, score, 0)
        for kh in range(KH):
            top = jnp.max(max_ref[kh], -1, keepdims=True)
            max_ref[kh] = jnp.broadcast_to(top, (part_rows, 128))
            sum_ref[kh] = jnp.zeros((part_rows, 128), f32)
            o_ref[kh, span, :] = jnp.zeros((part_rows, 128), f32)

        def weigh(i, carry):
            for kh in range(KH):
                s = s_ref[kh, i]
                top = max_ref[kh]
                left = jnp.exp(s[:, :128] - top)
                right = jnp.exp(s[:, 128:] - top)
                sum_ref[kh] += left + right
                o_ref[kh, span, :] += jnp.dot(
                    jnp.concatenate([left, right], 1).astype(bf16),
                    keys_of(v_ref, i),
                    preferred_element_type=f32,
                )
            return carry

        lax.fori_loop(0, last + 1, weigh, 0)
        for kh in range(KH):
            total = jnp.sum(sum_ref[kh], -1, keepdims=True)
            o_ref[kh, span, :] = o_ref[kh, span, :] / total
            lse_ref[kh, part] = dot_nt(
                jnp.full((8, 128), 1.0 / 128, f32),
                max_ref[kh] + jnp.log(total),
                lax.Precision.HIGHEST,
            )
    for tile in range(WIDTH_Q // 128):
        low_ref[:, tile * 128 : (tile + 1) * 128] = join_heads(o_ref, half, tile).astype(bf16)
    hidden = x_ref[...].astype(f32) + jnp.dot(low_ref[...], w_ref[...], preferred_element_type=f32)
    hidden_ref[...] = hidden
    inverse = lax.rsqrt(jnp.mean(hidden * hidden, -1, keepdims=True) + EPS)
    normed_ref[...] = (hidden * inverse * gain_ref[...]).astype(bf16)


def backward_kernel(
    ctx, meta_ref, gn_ref, hidden_ref, gout_ref, gain_ref, w_ref, spread_ref, k_ref, v_ref, lse_ref,
    o_ref,
    gh_ref, ga_ref, gain_grad_ref, gq_ref, mine_ref, other_ref,
    go_ref, gqs_ref, gk_ref, gv_ref,
):
    rows = gn_ref.shape[0]
    half = rows // 2
    part_rows = GROUP * half
    me = meta_ref[0]
    chips = ctx // 2
    hidden = hidden_ref[...]
    inverse = lax.rsqrt(jnp.mean(hidden * hidden, -1, keepdims=True) + EPS)
    unit = hidden * inverse
    grad = gn_ref[...]
    gain_grad_ref[...] = jnp.sum(grad * unit, 0, keepdims=True)
    scaled = grad * gain_ref[...]
    gh = gout_ref[...].astype(f32) + inverse * (
        scaled - unit * jnp.mean(scaled * unit, -1, keepdims=True)
    )
    gh_ref[...] = gh
    ga = gh.astype(bf16)
    ga_ref[...] = ga
    spread_heads(dot_nt(ga, w_ref[...]).astype(bf16), go_ref, 1.0)
    gqs_ref[...] = jnp.zeros_like(gqs_ref)
    gk_ref[...] = jnp.zeros_like(gk_ref)
    gv_ref[...] = jnp.zeros_like(gv_ref)
    for part in range(2):
        span = slice(part * part_rows, (part + 1) * part_rows)
        start = (me if part == 0 else 2 * ctx - 1 - me) * half
        last = start // KEYS
        deltas = [
            dot_nt(
                jnp.ones((8, 128), f32),
                go_ref[kh, span, :].astype(f32) * o_ref[kh, span, :],
                lax.Precision.HIGHEST,
            )[:1]
            for kh in range(KH)
        ]

        def step(i, masked):
            at = pl.ds(pl.multiple_of(i * KEYS, KEYS), KEYS)
            keys = k_ref[at, :]
            grad_k = gk_ref[at, :]
            grad_v = gv_ref[at, :]
            for kh in range(KH):
                queries = spread_ref[kh, span, :]
                heads = go_ref[kh, span, :]
                p = jnp.exp(dot_nt(keys, queries) - lse_ref[kh, part][:1])
                if masked:
                    row = lanes(p.shape) % half + start
                    key = lax.broadcasted_iota(jnp.int32, p.shape, 0) + i * KEYS
                    p = jnp.where(key <= row, p, 0.0)
                gs = (p * (dot_nt(v_ref[at, :], heads) - deltas[kh])).astype(bf16)
                grad_v += jnp.dot(p.astype(bf16), heads, preferred_element_type=f32)
                grad_k += jnp.dot(gs, queries, preferred_element_type=f32)
                gqs_ref[kh, span, :] += dot_tn(gs, keys)
            gk_ref[at, :] = grad_k
            gv_ref[at, :] = grad_v

        def body(i, carry):
            step(i, False)
            return carry

        lax.fori_loop(0, last, body, 0)
        step(last, True)
    for tile in range(WIDTH_Q // 128):
        gq_ref[:, tile * 128 : (tile + 1) * 128] = join_heads(gqs_ref, half, tile) * HD ** (-0.5)
    for j in range(ctx):
        dst = mine_ref if j < chips else other_ref
        at = (j % chips) * rows
        owner = meta_ref[1 + j]
        for part in range(2):
            place = owner if part == 0 else 2 * ctx - 1 - owner
            frm = pl.ds(pl.multiple_of(place * half, half), half)
            to = slice(at + part * half, at + (part + 1) * half)
            dst[to, :WIDTH_K] = gk_ref[frm, :].astype(dst.dtype)
            dst[to, WIDTH_K:] = gv_ref[frm, :].astype(dst.dtype)


def finish_kernel(
    gq_ref, x_ref, gain_ref, w_ref, cos_ref, sin_ref, gh_ref, *refs
):
    joint_ref, gx_ref, gain_grad_ref, bias_ref = refs[-4:]
    pair = refs[0][...]
    for ref in refs[1:-4]:
        pair = pair + ref[...].astype(f32)
    cosine = cos_ref[...]
    sine = sin_ref[...]
    early = lanes(cosine.shape) % HD < HD // 2
    for i in range((WIDTH_Q + WIDTH_K) // 128):
        at = slice(i * 128, (i + 1) * 128)
        grad = gq_ref[:, at] if i * 128 < WIDTH_Q else pair[:, :WIDTH_K]
        scaled = grad * sine
        turned = jnp.where(early, pltpu.roll(scaled, 96, 1), -pltpu.roll(scaled, 32, 1))
        joint_ref[:, at] = (grad * cosine + turned).astype(bf16)
    joint_ref[:, WIDTH_Q + WIDTH_K :] = pair[:, WIDTH_K:].astype(bf16)
    joint = joint_ref[...]
    bias_ref[...] = jnp.sum(joint.astype(f32), 0, keepdims=True)
    grad = dot_nt(joint, w_ref[...])
    x = x_ref[...].astype(f32)
    inverse = lax.rsqrt(jnp.mean(x * x, -1, keepdims=True) + EPS)
    unit = x * inverse
    gain_grad_ref[...] = jnp.sum(grad * unit, 0, keepdims=True)
    scaled = grad * gain_ref[...]
    gx_ref[...] = gh_ref[...] + inverse * (
        scaled - unit * jnp.mean(scaled * unit, -1, keepdims=True)
    )


def mlp_kernel(
    half_rows, spots_ref, x_ref, gy_ref, gate_a, gate_b, up_a, up_b, down_a, down_b,
    mid_ref, gg_ref, gu_ref, gx_ref, out_ref, send_ref, gx_acc, out_acc,
):
    step = pl.program_id(0)
    x = x_ref[...]
    gy = gy_ref[...]
    wg = jnp.concatenate([gate_a[...], gate_b[...]], 1)
    wu = jnp.concatenate([up_a[...], up_b[...]], 1)
    wd = jnp.concatenate([down_a[...], down_b[...]], 0)
    gate = jnp.dot(x, wg, preferred_element_type=f32)
    up = jnp.dot(x, wu, preferred_element_type=f32)
    grad = dot_nt(gy, wd)
    core = spots_ref[1]
    column = lanes((1, gate.shape[1])) + (step * 256 + spots_ref[2])
    own = (column < spots_ref[3]) == (core == 0)
    sigma = jax.nn.sigmoid(gate)
    active = gate * sigma
    middle = jnp.where(own, active * up, 0.0).astype(bf16)
    grad_gate = jnp.where(
        own, grad * up * (sigma * (1.0 + gate * (1.0 - sigma))), 0.0
    ).astype(bf16)
    grad_up = jnp.where(own, grad * active, 0.0).astype(bf16)
    mid_ref[...] = middle
    gg_ref[...] = grad_gate
    gu_ref[...] = grad_up
    gx = dot_nt(grad_gate, wg) + dot_nt(grad_up, wu)
    out = jnp.dot(middle, wd, preferred_element_type=f32)

    @pl.when(step == 0)
    def start():
        gx_acc[...] = gx
        out_acc[...] = out

    @pl.when(step > 0)
    def add():
        gx_acc[...] += gx
        out_acc[...] += out

    @pl.when(step == pl.num_programs(0) - 1)
    def end():
        gx_ref[...] = gx_acc[:half_rows]
        out_ref[...] = out_acc[:half_rows]
        send_ref[:half_rows] = gx_acc[half_rows:].astype(bf16)
        send_ref[half_rows:] = out_acc[half_rows:].astype(bf16)


def feed_forward(meta, x, gy, w_gate, w_up, w_down, width):
    tokens = x.shape[0]
    half = tokens // 2
    steps = width // 256
    tiles = width // 128 - 1

    def columns(j):
        return pl.BlockSpec((D, 128), lambda i, m: (0, m[1] * tiles + 2 * i + j))

    def rows(j):
        return pl.BlockSpec((128, D), lambda i, m: (m[1] * tiles + 2 * i + j, 0))

    whole = pl.BlockSpec((tokens, D), lambda i, m: (0, 0))
    halves = pl.BlockSpec((half, D), lambda i, m: (0, 0))
    tile = pl.BlockSpec((tokens, 256), lambda i, m: (0, i))
    hidden = jax.ShapeDtypeStruct((tokens, width), bf16)
    return pl.pallas_call(
        lambda *refs: mlp_kernel(half, *refs),
        out_shape=[hidden] * 3
        + [jax.ShapeDtypeStruct((half, D), f32)] * 2
        + [jax.ShapeDtypeStruct((tokens, D), bf16)],
        grid_spec=pltpu.PrefetchScalarGridSpec(
            num_scalar_prefetch=1,
            grid=(steps,),
            in_specs=[whole, whole, columns(0), columns(1), columns(0), columns(1), rows(0), rows(1)],
            out_specs=[tile, tile, tile, halves, halves, whole],
            scratch_shapes=[pltpu.VMEM((tokens, D), f32)] * 2,
        ),
        compiler_params=pltpu.CompilerParams(vmem_limit_bytes=VMEM_BYTES),
        cost_estimate=pl.CostEstimate(
            flops=12 * tokens * width * D, bytes_accessed=6 * width * D, transcendentals=0
        ),
    )(meta, x, gy, w_gate, w_gate, w_up, w_up, w_down, w_down)


def mlp_grad_kernel(
    down_rows, main, meta_ref, x_ref, gy_ref, mid_ref, gg_ref, gu_ref,
    out_ref, head_ref, tail_ref, mlp_acc, down_acc,
):
    step = pl.program_id(0)
    core = meta_ref[1]
    at_main = pl.ds(pl.multiple_of(core * 128, 128), main)
    at_tile = pl.ds(pl.multiple_of((1 - core) * main, 128), 128)

    @pl.when(step == 0)
    def products():
        x = x_ref[...]
        mlp_acc[:, :main] = dot_tn(x, gg_ref[:, at_main])
        mlp_acc[:, main : 2 * main] = dot_tn(x, gu_ref[:, at_main])
        mixed = gg_ref[:, at_tile].astype(f32) + pltpu.roll(gu_ref[:, at_tile].astype(f32), 64, 1)
        mlp_acc[:, 2 * main :] = dot_tn(x, mixed.astype(bf16))
        down_acc[...] = dot_tn(mid_ref[...], gy_ref[...])

    mlp_rows = mlp_acc.shape[0] // pl.num_programs(0)
    columns = mlp_acc.shape[1] // 128
    block = mlp_acc[pl.ds(pl.multiple_of(step * mlp_rows, 16), mlp_rows), :].astype(bf16)
    for j in range(columns):
        for i in range(mlp_rows // 16):
            out_ref[0, j * 16 : (j + 1) * 16, i * 128 : (i + 1) * 128] = block[
                i * 16 : (i + 1) * 16, j * 128 : (j + 1) * 128
            ]
    first = pl.multiple_of(core * 64 + step * down_rows, 8)
    out_ref[0, columns * 16 :, :] = down_acc[pl.ds(first, down_rows), :].astype(bf16)

    @pl.when(meta_ref[4 + step] == pl.num_programs(0) // 2)
    def far():
        head_ref[...] = out_ref[0, : head_ref.shape[0], :]
        tail_ref[...] = out_ref[0, head_ref.shape[0] :, :]


def mlp_gradients(meta, x, gy, mid, gg, gu, chips, down_rows, main):
    tokens = x.shape[0]
    columns = (2 * main + 128) // 128
    rows = columns * 16 + down_rows
    cut = (rows // 2 + 15) // 16 * 16
    wide = pl.BlockSpec((tokens, D), lambda i, m: (0, 0))
    tall = pl.BlockSpec((tokens, mid.shape[1]), lambda i, m: (0, 0))
    return pl.pallas_call(
        lambda *refs: mlp_grad_kernel(down_rows, main, *refs),
        out_shape=[
            jax.ShapeDtypeStruct((chips, rows, D), bf16),
            jax.ShapeDtypeStruct((cut, D), bf16),
            jax.ShapeDtypeStruct((rows - cut, D), bf16),
        ],
        grid_spec=pltpu.PrefetchScalarGridSpec(
            num_scalar_prefetch=1,
            grid=(chips,),
            in_specs=[wide, wide, tall, tall, tall],
            out_specs=[
                pl.BlockSpec((1, rows, D), lambda i, m: (m[4 + i], 0, 0)),
                pl.BlockSpec((cut, D), lambda i, m: (0, 0)),
                pl.BlockSpec((rows - cut, D), lambda i, m: (0, 0)),
            ],
            scratch_shapes=[
                pltpu.VMEM((D, columns * 128), f32),
                pltpu.VMEM((mid.shape[1], D), f32),
            ],
        ),
        compiler_params=pltpu.CompilerParams(vmem_limit_bytes=VMEM_BYTES),
        cost_estimate=pl.CostEstimate(
            flops=6 * tokens * mid.shape[1] * D, bytes_accessed=4 * chips * rows * D,
            transcendentals=0,
        ),
    )(meta, x, gy, mid, gg, gu)


def small_grad_kernel(chips, q_rows, meta_ref, norm_ref, joint_ref, att_ref, ga_ref, *refs):
    out_refs, acc = refs[:-1], refs[-1]
    cols = joint_ref.shape[1]
    acc[:, :cols] = dot_tn(norm_ref[...], joint_ref[...])
    acc[:, cols:] = dot_tn(att_ref[...], ga_ref[...])
    first = pl.multiple_of((2 * meta_ref[0] + meta_ref[1]) * q_rows, 16)
    width = acc.shape[1] // chips
    for out_ref, slot in zip(out_refs, range(chips)):
        column = pl.multiple_of(meta_ref[12 + slot] * width, 128)
        block = acc[pl.ds(first, q_rows), pl.ds(column, width)]
        tall = jnp.concatenate(
            [block[:, i * 128 : (i + 1) * 128] for i in range(width // 128)], 0
        ).astype(bf16)
        piece = out_ref.shape[0]
        for i in range(D // 128):
            out_ref[:, i * 128 : (i + 1) * 128] = tall[i * piece : (i + 1) * piece]


def place_call(kernel, outs, meta, pairs, scratch, copies, old, through):
    blocks = [x for pair in pairs for x in pair]
    keep = [] if old is None else list(old)
    outs = list(outs)
    aliases = {1 + len(blocks) + i: i for i in range(len(keep))}
    if through is not None:
        aliases[1 + len(blocks) + len(keep)] = len(outs)
        keep = keep + [through]
        outs = outs + [jax.ShapeDtypeStruct(through.shape, through.dtype)]
    count = len(blocks)
    n_out = len(outs)
    n_old = len(keep)

    def body(meta_ref, *refs):
        outs_at = count + n_old
        kernel(meta_ref, refs[:count], refs[outs_at : outs_at + n_out], refs[outs_at + n_out :])

    moved = 8 * sum(x.size for x in blocks)
    result = pl.pallas_call(
        body,
        out_shape=outs,
        in_specs=[pl.BlockSpec(memory_space=pltpu.SMEM)]
        + [pl.BlockSpec(memory_space=pltpu.VMEM)] * count
        + [pl.BlockSpec(memory_space=pl.ANY)] * n_old,
        out_specs=[pl.BlockSpec(memory_space=pl.ANY)] * n_out,
        scratch_shapes=list(scratch) + [pltpu.SemaphoreType.DMA((copies,))],
        input_output_aliases=aliases,
        compiler_params=pltpu.CompilerParams(vmem_limit_bytes=VMEM_BYTES),
        cost_estimate=pl.CostEstimate(flops=0, bytes_accessed=moved, transcendentals=0),
    )(meta, *blocks, *keep)
    if through is None:
        return list(result), None
    return list(result[:-1]), result[-1]


def place_pairs(meta, slots, pairs, main, ff_loc, old, through):
    mlp_rows = D // 8
    columns = pairs[0][0].shape[0] // 16
    tiles = main // 128

    def kernel(meta_ref, refs, outs, scratch):
        gate_buf, up_buf, sems = scratch
        core_zero = meta_ref[1] == 0

        def column(ref, j):
            parts = [
                ref[j * 16 : (j + 1) * 16, i * 128 : (i + 1) * 128] for i in range(mlp_rows // 16)
            ]
            return jnp.concatenate(parts, 0).astype(f32)

        copies = []
        for k, slot in enumerate(slots):
            for j in range(columns):
                got = column(refs[2 * k], j)
                other = column(refs[2 * k + 1], j)
                zero = jnp.where(core_zero, got, other)
                one = jnp.where(core_zero, other, got)
                if j < 2 * tiles:
                    buf = gate_buf if j < tiles else up_buf
                    at = (j % tiles) * 128
                    buf[k, :, at : at + 128] = zero
                    buf[k, :, at + main + 128 : at + main + 256] = one
                else:
                    left = lanes(zero.shape) < 64
                    gate_buf[k, :, main : main + 128] = jnp.where(left, zero, one)
                    up_buf[k, :, main : main + 128] = pltpu.roll(jnp.where(left, one, zero), 64, 1)
            here = pl.ds(pl.multiple_of(meta_ref[12 + slot] * mlp_rows, 8), mlp_rows)
            for side, buf in enumerate((gate_buf, up_buf)):
                copy = pltpu.make_async_copy(
                    buf.at[k], outs[side].at[here, :], sems.at[2 * k + side]
                )
                copy.start()
                copies.append(copy)
        for copy in copies:
            copy.wait()

    count = len(slots)
    return place_call(
        kernel,
        [jax.ShapeDtypeStruct((D, ff_loc), f32)] * 2,
        meta,
        pairs,
        [pltpu.VMEM((count, mlp_rows, ff_loc), f32)] * 2,
        2 * count,
        old,
        through,
    )


def place_rest(meta, slots, pairs, down_rows, q_rows, ff_loc, cols, chips, old, through):
    lanes_out = D // 128
    piece = pairs[0][0].shape[0] - down_rows
    width = (cols + D) // chips

    def kernel(meta_ref, refs, outs, scratch):
        down_buf, small_buf, sems = scratch
        down_ref, joint_ref, out_ref = outs[:3]
        copies = []
        for k in range(2 * len(slots)):
            ref = refs[k]
            core = meta_ref[1] if k % 2 == 0 else 1 - meta_ref[1]
            owner = meta_ref[12 + slots[k // 2]]
            down_buf[k] = ref[piece:, :].astype(f32)
            here = pl.ds(pl.multiple_of((core * chips + owner) * down_rows, 8), down_rows)
            copy = pltpu.make_async_copy(down_buf.at[k], down_ref.at[here, :], sems.at[each * k])
            copy.start()
            copies.append(copy)
            tall = jnp.concatenate(
                [ref[:piece, i * 128 : (i + 1) * 128] for i in range(lanes_out)], 0
            ).astype(f32)
            rows = pl.ds(pl.multiple_of(core * q_rows, 8), q_rows)
            for i in range(width // 128):
                small_buf[k, i] = tall[i * q_rows : (i + 1) * q_rows]
                block = owner * (width // 128) + i

                @pl.when(block < cols // 128)
                def joint(k=k, i=i, rows=rows, block=block):
                    at = pl.ds(pl.multiple_of(block * 128, 128), 128)
                    pltpu.make_async_copy(
                        small_buf.at[k, i], joint_ref.at[rows, at], sems.at[each * k + 1 + i]
                    ).start()

                @pl.when(block >= cols // 128)
                def out(k=k, i=i, rows=rows, block=block):
                    at = pl.ds(pl.multiple_of((block - cols // 128) * 128, 128), 128)
                    pltpu.make_async_copy(
                        small_buf.at[k, i], out_ref.at[rows, at], sems.at[each * k + 1 + i]
                    ).start()

        for copy in copies:
            copy.wait()
        for k in range(2 * len(slots)):
            for i in range(width // 128):
                pltpu.make_async_copy(
                    small_buf.at[k, i], out_ref.at[pl.ds(0, q_rows), pl.ds(0, 128)], sems.at[each * k + 1 + i]
                ).wait()

    count = 2 * len(slots)
    each = 1 + width // 128
    return place_call(
        kernel,
        [
            jax.ShapeDtypeStruct((ff_loc, D), f32),
            jax.ShapeDtypeStruct((2 * q_rows, cols), f32),
            jax.ShapeDtypeStruct((2 * q_rows, D), f32),
        ],
        meta,
        pairs,
        [
            pltpu.VMEM((count, down_rows, D), f32),
            pltpu.VMEM((count, width // 128, q_rows, 128), f32),
        ],
        each * count,
        old,
        through,
    )


def place_blocks(blocks, spots, out_shape, old=None):
    shape = blocks[0].shape
    count = len(blocks)
    if shape[0] % 8 or shape[1] % 128:
        out = jnp.zeros(out_shape, f32) if old is None else old
        for block, (i, j) in zip(blocks, spots):
            out = lax.dynamic_update_slice(
                out, block.astype(f32), (i * shape[0], j * shape[1])
            )
        return out

    def kernel(spots_ref, *refs):
        step = pl.program_id(0)
        out_ref = refs[-1]
        for i in range(count):

            @pl.when(step == i)
            def write(i=i):
                out_ref[...] = refs[i][...].astype(f32)

    keep = [] if old is None else [old]
    return pl.pallas_call(
        kernel,
        out_shape=jax.ShapeDtypeStruct(out_shape, f32),
        grid_spec=pltpu.PrefetchScalarGridSpec(
            num_scalar_prefetch=1,
            grid=(count,),
            in_specs=[pl.BlockSpec(shape, lambda i, spots: (0, 0))] * count
            + [pl.BlockSpec(memory_space=pl.ANY)] * len(keep),
            out_specs=pl.BlockSpec(shape, lambda i, spots: (spots[i, 0], spots[i, 1])),
        ),
        input_output_aliases={} if old is None else {count + 1: 0},
        compiler_params=pltpu.CompilerParams(vmem_limit_bytes=VMEM_BYTES),
    )(jnp.stack([jnp.stack(s) for s in spots]).astype(jnp.int32), *blocks, *keep)


def local(tokens, w_qkv, b_qkv, w_out, gain_attn, gain_mlp, w_gate, w_up, w_down, cotangent):
    net = Net()
    rows = tokens.shape[1]
    half_rows = rows // 2
    ctx_count = net.ctx
    core = net.core
    chips = net.chips
    part_rows = GROUP * half_rows
    x = tokens[0]
    gain_one = gain_attn[None]
    gain_two = gain_mlp[None]

    w_qkv_full = net.full_rows(w_qkv)

    ff_loc = w_gate.shape[1]
    ff_half = ff_loc // 2
    main = (ff_half // 128) * 128
    rest = ff_half - main
    width = main + 2 * rest
    first = core * main
    tiled = 2 * rest == 128 and width % 256 == 0 and chips == 8 and (ff_half // chips) % 8 == 0
    ring = jnp.arange(chips, dtype=jnp.int32)
    owners_of = (net.pos - ring) % chips
    spots = jnp.concatenate(
        [jnp.stack([net.d, core, first, jnp.int32(ff_half)]), owners_of, owners_of]
    ).astype(jnp.int32)

    row_ids = jnp.arange(half_rows, dtype=jnp.int32)
    place = jnp.concatenate(
        [net.c * half_rows + row_ids, (2 * ctx_count - 1 - net.c) * half_rows + row_ids]
    )
    freq = ROPE_BASE ** (-((jnp.arange(128) % (HD // 2)).astype(f32) * (2.0 / HD)))
    angle = place.astype(f32)[:, None] * freq[None, :]
    cosine, sine = jnp.cos(angle), jnp.sin(angle)
    normed_one, queries, pairs = call(
        qkv_kernel,
        [
            jax.ShapeDtypeStruct((rows, D), bf16),
            jax.ShapeDtypeStruct((rows, WIDTH_Q), bf16),
            jax.ShapeDtypeStruct((rows, 2 * WIDTH_K), bf16),
        ],
        [x, gain_one, w_qkv_full, b_qkv[None], cosine, sine],
        flops=2 * rows * D * 1152,
    )

    slots = net.send_gather(pairs)
    mine = jnp.concatenate(slots, 0)
    other = net.swap(mine)
    order = jnp.array(net.order, jnp.int32)
    chip_ids = order[(net.pos - jnp.arange(chips, dtype=jnp.int32)) % chips]
    meta = jnp.concatenate([net.c[None], 2 * chip_ids + core, 2 * chip_ids + 1 - core])
    meta = meta.astype(jnp.int32)

    late_w, late_g, late_n, unused = lax.optimization_barrier((w_out, cotangent[0], normed_one, pairs))
    w_out_full = net.full_rows(late_w)
    early_group = net.group_gather(jnp.concatenate([late_g, late_n], 1))
    grad_out_group = early_group[:, :D]
    normed_one_group = early_group[:, D:]

    total_keys = rows * ctx_count
    padded = (KH, 2 * part_rows, 128)
    attended_low, attended, lse, spread, keys, values, hidden, normed_two = call(
        lambda *refs: forward_kernel(ctx_count, *refs),
        [
            jax.ShapeDtypeStruct((rows, WIDTH_Q), bf16),
            jax.ShapeDtypeStruct(padded, f32),
            jax.ShapeDtypeStruct((KH, 2, 8, part_rows), f32),
            jax.ShapeDtypeStruct(padded, bf16),
            jax.ShapeDtypeStruct((total_keys, WIDTH_K), bf16),
            jax.ShapeDtypeStruct((total_keys, WIDTH_K), bf16),
            jax.ShapeDtypeStruct((rows, D), f32),
            jax.ShapeDtypeStruct((rows, D), bf16),
        ],
        [meta, queries, mine, other, x, w_out_full, gain_two],
        smem=1,
        scratch=[
            pltpu.VMEM((KH, total_keys // KEYS, part_rows, KEYS), f32),
            pltpu.VMEM((KH, part_rows, 128), f32),
            pltpu.VMEM((KH, part_rows, 128), f32),
        ],
        flops=8 * KH * part_rows * total_keys * 128,
    )

    normed_two_group = net.group_gather(normed_two)
    chip_rows = net.dp * rows
    down_rows = ff_half // chips
    mlp_rows = D // chips
    if tiled:
        mid, gate_low, up_low, grad_mine, out_mine, sent = feed_forward(
            spots, normed_two_group, grad_out_group, w_gate, w_up, w_down, width
        )
    else:
        own_cols = (jnp.arange(width) + first < ff_half) == (core == 0)
        wg = lax.dynamic_slice(w_gate, (0, first), (D, width))
        wu = lax.dynamic_slice(w_up, (0, first), (D, width))
        wd = lax.dynamic_slice(w_down, (first, 0), (width, D))
        gate = jnp.dot(normed_two_group, wg, preferred_element_type=f32)
        upper = jnp.dot(normed_two_group, wu, preferred_element_type=f32)
        sigma = jax.nn.sigmoid(gate)
        activated = gate * sigma
        middle = jnp.where(own_cols, activated * upper, 0.0).astype(bf16)
        grad_middle = jnp.einsum("td,fd->tf", grad_out_group, wd, preferred_element_type=f32)
        slope = sigma * (1.0 + gate * (1.0 - sigma))
        grad_gate_low = jnp.where(own_cols, grad_middle * upper * slope, 0.0).astype(bf16)
        grad_up_low = jnp.where(own_cols, grad_middle * activated, 0.0).astype(bf16)

        grad_normed_two = jnp.einsum(
            "tf,df->td", grad_gate_low, wg, preferred_element_type=f32
        ) + jnp.einsum("tf,df->td", grad_up_low, wu, preferred_element_type=f32)
        mlp_out = jnp.dot(middle, wd, preferred_element_type=f32)
        grad_mine, out_mine = grad_normed_two[:chip_rows], mlp_out[:chip_rows]
        sent = jnp.concatenate([grad_normed_two[chip_rows:], mlp_out[chip_rows:]], 0).astype(bf16)
    swapped = net.swap(sent)
    grad_chip = grad_mine + swapped[:chip_rows].astype(f32)
    mlp_chip = out_mine + swapped[chip_rows:].astype(f32)
    grad_two = grad_chip[:rows]
    for s in range(1, net.dp):
        piece = grad_chip[s * rows : (s + 1) * rows].astype(bf16)
        grad_two = grad_two + net.shift(piece, net.dp - s).astype(f32)

    if tiled:
        terms, head, tail = mlp_gradients(
            spots, normed_two_group, grad_out_group, mid, gate_low, up_low, chips, down_rows, main
        )
        sum_mlp, sum_down = net.ring_sum(head, tail, terms, terms.shape[1] - down_rows)
    else:
        part_down = jnp.einsum(
            "tf,td->fd", middle, grad_out_group, preferred_element_type=f32
        ).astype(bf16)
        part_down = lax.dynamic_slice(part_down, (core * rest, 0), (ff_half, D))

        def down_chunk(slot):
            return lax.dynamic_slice(part_down, (net.owner(slot) * down_rows, 0), (down_rows, D))

        sum_down = net.ring_scatter([down_chunk(s) for s in range(chips)]).astype(bf16)

        def split_main(x):
            left = (x[:, :main], x[:, main:])
            right = (x[:, 2 * rest :], x[:, : 2 * rest])
            return (
                jnp.where(core == 0, left[0], right[0]),
                jnp.where(core == 0, left[1], right[1]),
            )

        gate_main, gate_tile = split_main(grad_gate_low)
        up_main, up_tile = split_main(grad_up_low)
        packed = jnp.concatenate(
            [gate_main, up_main, gate_tile + jnp.roll(up_tile, rest, 1)], 1
        )
        part_mlp = jnp.einsum(
            "td,tf->df", normed_two_group, packed, preferred_element_type=f32
        ).astype(bf16)

        def mlp_chunk(slot):
            return lax.dynamic_slice(
                part_mlp, (net.owner(slot) * mlp_rows, 0), (mlp_rows, 2 * ff_half)
            )

        sum_mlp = net.ring_scatter([mlp_chunk(s) for s in range(chips)]).astype(bf16)
        sum_mlp = lax.optimization_barrier(sum_mlp)

    grad_hidden, grad_attn_low, grad_gain_two, grad_queries, terms_mine, terms_other = call(
        lambda *refs: backward_kernel(ctx_count, *refs),
        [
            jax.ShapeDtypeStruct((rows, D), f32),
            jax.ShapeDtypeStruct((rows, D), bf16),
            jax.ShapeDtypeStruct((1, D), f32),
            jax.ShapeDtypeStruct((rows, WIDTH_Q), f32),
            jax.ShapeDtypeStruct((chips * rows, 2 * WIDTH_K), f32),
            jax.ShapeDtypeStruct((chips * rows, 2 * WIDTH_K), bf16),
        ],
        [
            meta, grad_two, hidden, cotangent[0], gain_two, w_out_full, spread, keys, values, lse,
            attended,
        ],
        smem=1,
        scratch=[
            pltpu.VMEM(padded, bf16),
            pltpu.VMEM(padded, f32),
            pltpu.VMEM((total_keys, WIDTH_K), f32),
            pltpu.VMEM((total_keys, WIDTH_K), f32),
        ],
        flops=20 * KH * part_rows * total_keys * 128,
    )
    pair_sums = call(
        pair_kernel,
        [jax.ShapeDtypeStruct((rows, 2 * WIDTH_K), f32)]
        + [jax.ShapeDtypeStruct((rows, 2 * WIDTH_K), bf16)] * (chips - 1),
        [terms_mine, net.swap(terms_other)],
    )
    grad_pairs = [pair_sums[0]] + net.send_scatter(pair_sums)
    grad_joint_low, grad_input, grad_gain_one, grad_bias = call(
        finish_kernel,
        [
            jax.ShapeDtypeStruct((rows, 1152), bf16),
            jax.ShapeDtypeStruct((rows, D), f32),
            jax.ShapeDtypeStruct((1, D), f32),
            jax.ShapeDtypeStruct((1, 1152), f32),
        ],
        [grad_queries, x, gain_one, w_qkv_full, cosine, sine, grad_hidden] + grad_pairs,
        flops=2 * rows * D * 1152,
    )

    out_sum = mlp_chip[:rows]
    sent = jnp.concatenate([attended_low, grad_attn_low], 0)
    gathered = [sent]
    for s in range(1, net.dp):
        got = net.shift(
            jnp.concatenate([mlp_chip[s * rows : (s + 1) * rows].astype(bf16), sent], 0),
            net.dp - s,
        )
        out_sum = out_sum + got[:rows].astype(f32)
        gathered.append(got[rows:])
    output = (hidden + out_sum).astype(bf16)
    gathered = jnp.concatenate(gathered, 0)
    gathered = jnp.concatenate([gathered, net.swap(gathered)], 0).reshape(2 * net.dp, 2, rows, D)
    attended_group = gathered[:, 0].reshape(2 * net.dp * rows, D)
    grad_attn_group = gathered[:, 1].reshape(2 * net.dp * rows, D)

    q_rows = w_qkv.shape[0] // 2
    qkv_cols = w_qkv.shape[1]
    joint_group = net.group_gather(grad_joint_low)
    if tiled:
        piece = q_rows * (qkv_cols + D) // chips // D
        terms_small = call(
            lambda *refs: small_grad_kernel(chips, q_rows, *refs),
            [jax.ShapeDtypeStruct((piece, D), bf16)] * chips,
            [spots, normed_one_group, joint_group, attended_group, grad_attn_group],
            smem=1,
            scratch=[pltpu.VMEM((D, qkv_cols + D), f32)],
            flops=4 * chip_rows * D * (qkv_cols + D),
        )
        rest_block = call(
            rest_kernel,
            [jax.ShapeDtypeStruct((piece + down_rows, D), bf16)],
            [terms_small[0]] + net.send_scatter(terms_small) + [sum_down],
        )[0]
        (grad_gate, grad_up), (grad_down, grad_joint, grad_out_proj) = net.gather_both(
            sum_mlp,
            rest_block,
            lambda *args: place_pairs(spots, *args[:2], main, ff_loc, *args[2:]),
            lambda *args: place_rest(
                spots, *args[:2], down_rows, q_rows, ff_loc, qkv_cols, chips, *args[2:]
            ),
        )
    else:
        q_first = net.d * (2 * q_rows) + core * q_rows
        group_rows = 2 * net.dp * rows
        part_out = jnp.einsum(
            "tc,td->cd",
            lax.dynamic_slice(attended_group, (0, q_first), (group_rows, q_rows)),
            grad_attn_group,
            preferred_element_type=f32,
        )
        part_joint = jnp.einsum(
            "td,tc->dc",
            lax.dynamic_slice(normed_one_group, (0, q_first), (group_rows, q_rows)),
            joint_group,
            preferred_element_type=f32,
        )
        part_small = jnp.concatenate([part_joint, part_out], 1).astype(bf16)
        small_cols = part_small.shape[1] // chips

        def small_chunk(slot):
            return lax.dynamic_slice(part_small, (0, net.owner(slot) * small_cols), (q_rows, small_cols))

        sum_small = net.ring_scatter([small_chunk(s) for s in range(chips)]).astype(bf16)

        tall = jnp.concatenate(
            [sum_small[:, i * 128 : (i + 1) * 128] for i in range(small_cols // 128)], 0
        )
        piece = tall.shape[0] // (D // 128)
        wide = jnp.concatenate([tall[i * piece : (i + 1) * piece] for i in range(D // 128)], 1)
        both = lax.optimization_barrier(jnp.concatenate([sum_down, wide], 0))

        owners = [net.owner(s) for s in range(chips)]
        got_mlp = net.ring_gather(sum_mlp)
        got_both = net.ring_gather(both)
        pairs_mlp = [(got, net.swap(got)) for got in got_mlp]
        pairs_both = [(got, net.swap(got)) for got in got_both]

        down_blocks, down_spots, small_blocks, small_spots = [], [], [], []
        for owner, pair in zip(owners, pairs_both):
            for which, got in zip((core, 1 - core), pair):
                down_blocks.append(got[:down_rows])
                down_spots.append((which * chips + owner, jnp.int32(0)))
                wide = got[down_rows:]
                tall = jnp.concatenate([wide[:, i * 128 : (i + 1) * 128] for i in range(D // 128)], 0)
                small_blocks.append(
                    jnp.concatenate(
                        [tall[i * q_rows : (i + 1) * q_rows] for i in range(small_cols // 128)], 1
                    )
                )
                small_spots.append((which, owner))
        grad_down = place_blocks(down_blocks, down_spots, (ff_loc, D))
        grad_small = place_blocks(small_blocks, small_spots, (2 * q_rows, part_small.shape[1]))
        grad_gate = jnp.zeros((D, ff_loc), f32)
        grad_up = jnp.zeros((D, ff_loc), f32)
        left_lane = jnp.arange(2 * rest) < rest
        for owner, (got, swapped) in zip(owners, pairs_mlp):
            zero = jnp.where(core == 0, got, swapped).astype(f32)
            one = jnp.where(core == 0, swapped, got).astype(f32)
            tile_zero, tile_one = zero[:, 2 * main :], one[:, 2 * main :]
            mid_gate = jnp.where(left_lane, tile_zero, tile_one)
            mid_up = jnp.roll(jnp.where(left_lane, tile_one, tile_zero), rest, 1)
            base = owner * mlp_rows
            grad_gate = lax.dynamic_update_slice(
                grad_gate, jnp.concatenate([zero[:, :main], mid_gate, one[:, :main]], 1), (base, 0)
            )
            grad_up = lax.dynamic_update_slice(
                grad_up,
                jnp.concatenate([zero[:, main : 2 * main], mid_up, one[:, main : 2 * main]], 1),
                (base, 0),
            )

        grad_joint, grad_out_proj = grad_small[:, :qkv_cols], grad_small[:, qkv_cols:]

    small = net.total(jnp.concatenate([grad_gain_one, grad_gain_two, grad_bias], 1))[0]
    return (
        output[None],
        grad_input[None],
        grad_joint,
        small[2 * D :],
        grad_out_proj,
        small[:D],
        small[D : 2 * D],
        grad_gate,
        grad_up,
        grad_down,
    )


def solution(mesh):
    placed = (
        P("dp", "ctx", None),
        P("dp", None),
        P(),
        P("dp", None),
        P(),
        P(),
        P(None, "dp"),
        P(None, "dp"),
        P("dp", None),
        P("dp", "ctx", None),
    )
    return jax.shard_map(
        local,
        mesh=mesh,
        in_specs=placed,
        out_specs=(
            P("dp", "ctx", None),
            P("dp", "ctx", None),
            P("dp", None),
            P(),
            P("dp", None),
            P(),
            P(),
            P(None, "dp"),
            P(None, "dp"),
            P("dp", None),
        ),
        check_vma=False,
    )
```

```python
import math

import jax
import jax.numpy as jnp
from jax import lax
from jax.experimental import pallas as pl
from jax.experimental.pallas import tpu as pltpu
from jax.sharding import PartitionSpec as P

D = 896
QH = 14
KH = 2
HD = 64
GROUP = QH // KH
WIDTH_Q = QH * HD
WIDTH_K = KH * HD

EPS = 1e-06
ROPE_BASE = 1000000.0

f32 = jnp.float32
bf16 = jnp.bfloat16


def ring_order(chips):
    if chips % 2:
        return list(range(chips))
    rows = chips // 2
    return [2 * i for i in range(rows)] + [2 * i + 1 for i in reversed(range(rows))]


def half_cut(rows):
    cut = (rows // 2 + 7) // 8 * 8
    return cut if cut < rows else rows // 2


class Net:
    def __init__(self):
        self.dp = lax.axis_size("dp")
        self.ctx = lax.axis_size("ctx")
        self.chips = self.ctx // 2
        self.order = ring_order(self.chips)
        self.d = lax.axis_index("dp")
        self.c = lax.axis_index("ctx")
        self.core = self.c % 2
        place = [0] * self.chips
        for spot, chip in enumerate(self.order):
            place[chip] = spot
        self.pos = jnp.array(place, jnp.int32)[self.c // 2]

    def swap(self, x):
        return lax.ppermute(x, "ctx", [(i, i ^ 1) for i in range(self.ctx)])

    def shift(self, x, step):
        n = self.dp
        return lax.ppermute(x, "dp", [(i, (i + step) % n) for i in range(n)])

    def hop(self, x, step):
        n = self.chips
        perm = []
        for spot in range(n):
            for core in range(2):
                perm.append((2 * self.order[spot] + core, 2 * self.order[(spot + step) % n] + core))
        return lax.ppermute(x, "ctx", perm)

    def owner(self, slot):
        return (self.pos - slot) % self.chips

    def group_gather(self, x):
        chip = jnp.concatenate([x] + [self.shift(x, s) for s in range(1, self.dp)], 0)
        return jnp.concatenate([chip, self.swap(chip)], 0)

    def ring_gather(self, x):
        n = self.chips
        half = n // 2
        cut = half_cut(x.shape[0])
        found = [x] + [None] * (n - 1)
        fwd, back = x, x
        for s in range(1, half):
            fwd = self.hop(fwd, 1)
            back = self.hop(back, -1)
            found[s] = fwd
            found[n - s] = back
        found[half] = jnp.concatenate([self.hop(fwd[:cut], 1), self.hop(back[cut:], -1)], 0)
        return found

    def ring_scatter(self, local):
        n = self.chips
        half = n // 2
        cut = half_cut(local[half].shape[0])

        def add(got, mine):
            return (got.astype(f32) + mine.astype(f32)).astype(bf16)

        fwd = self.hop(local[half][:cut], 1)
        back = self.hop(local[half][cut:], -1)
        for s in range(1, half):
            mine_f = local[half + s]
            mine_b = local[half - s]
            if s == 1:
                mine_f = jnp.concatenate([add(fwd, mine_f[:cut]), mine_f[cut:]], 0)
                mine_b = jnp.concatenate([mine_b[:cut], add(back, mine_b[cut:])], 0)
            else:
                mine_f = add(fwd, mine_f)
                mine_b = add(back, mine_b)
            fwd = self.hop(mine_f, 1)
            back = self.hop(mine_b, -1)
        return fwd.astype(f32) + back.astype(f32) + local[0].astype(f32)

    def full_rows(self, shard):
        rows = shard.shape[0]
        half = rows // 2
        piece = lax.dynamic_slice(shard, (self.core * half, 0), (half, shard.shape[1]))
        blocks = [shard]
        for s in range(1, self.dp):
            got = self.shift(piece, s)
            other = self.swap(got)
            low = jnp.where(self.core == 0, got, other)
            high = jnp.where(self.core == 0, other, got)
            blocks.append(jnp.concatenate([low, high], 0))
        if self.dp == 2:
            first = jnp.where(self.d == 0, blocks[0], blocks[1])
            second = jnp.where(self.d == 0, blocks[1], blocks[0])
            return jnp.concatenate([first, second], 0)
        ranked = jnp.stack(blocks)[(self.d - jnp.arange(self.dp)) % self.dp]
        return ranked.reshape(self.dp * rows, shard.shape[1])

    def total(self, x):
        x = x + self.swap(x)
        bit = 1
        while bit < self.chips:
            x = x + lax.ppermute(x, "ctx", [(i, i ^ (2 * bit)) for i in range(self.ctx)])
            bit *= 2
        bit = 1
        while bit < self.dp:
            x = x + lax.ppermute(x, "dp", [(i, i ^ bit) for i in range(self.dp)])
            bit *= 2
        return x

    def ring_parts(self, local):
        n = self.chips
        half = n // 2
        cut = half_cut(local[half].shape[0])

        def add(got, mine):
            return (got.astype(f32) + mine.astype(f32)).astype(bf16)

        fwd, back = self.hop(local[half][:cut], 1), self.hop(local[half][cut:], -1)
        for s in range(1, half):
            mine_f, mine_b = local[half + s], local[half - s]
            if s == 1:
                mine_f = jnp.concatenate([add(fwd, mine_f[:cut]), mine_f[cut:]], 0)
                mine_b = jnp.concatenate([mine_b[:cut], add(back, mine_b[cut:])], 0)
            else:
                mine_f, mine_b = add(fwd, mine_f), add(back, mine_b)
            fwd, back = self.hop(mine_f, 1), self.hop(mine_b, -1)
        return [local[0], fwd, back]

    def ring_sum(self, head, tail, terms, split, middle):
        n = self.chips
        half = n // 2
        fwd, back = self.hop(head, 1), self.hop(tail, -1)
        token = None
        for s in range(1, half):
            after = token if s == half - 1 else None
            fwd_sum = ring_add(fwd, terms, half + s, 0, after)
            back_sum = ring_add(back, terms, half - s, 1, after)
            if s == 1:
                token = middle(fwd_sum, back_sum)
            fwd, back = self.hop(fwd_sum, 1), self.hop(back_sum, -1)
        return ring_end(fwd, back, terms, split)

    def gather_placed(self, x, place):
        n = self.chips
        half = n // 2
        fwd = back = x
        placed = None
        waiting = ([0], [(x, self.swap(x))])
        for s in range(1, half + 1):
            if s > 1:
                placed, token = place(*waiting, placed)
                fwd, back = gate(token, fwd, back)
                waiting = ([s - 1, n - s + 1], [(fwd, self.swap(fwd)), (back, self.swap(back))])
            if s < half:
                fwd, back = self.hop(fwd, 1), self.hop(back, -1)
            else:
                cut = half_cut(fwd.shape[0])
                fwd, back = self.hop(fwd[:cut], 1), self.hop(back[cut:], -1)
        far = jnp.concatenate([fwd, back], 0)
        placed, token = place(*waiting, placed)
        return place([half], [(far, self.swap(far))], placed)[0]


VMEM_BYTES = 56 * 1024 * 1024
KEYS = 256
RING_ROWS = 152


def full_spec(shape):
    return pl.BlockSpec(shape, lambda: (0,) * len(shape))


def call(kernel, outs, args, smem=0, scratch=(), flops=0, loose=0):
    tight = len(args) - loose
    specs = [pl.BlockSpec(memory_space=pltpu.SMEM)] * smem
    specs += [pl.BlockSpec(memory_space=pltpu.VMEM)] * (tight - smem)
    specs += [pl.BlockSpec(memory_space=pl.ANY)] * loose

    def body(*refs):
        kernel(*refs[:tight], *refs[tight + loose :])

    moved = sum(x.size * x.dtype.itemsize for x in list(args) + list(outs))
    return pl.pallas_call(
        body,
        out_shape=list(outs),
        in_specs=specs,
        out_specs=[pl.BlockSpec(memory_space=pltpu.VMEM)] * len(outs),
        scratch_shapes=list(scratch),
        compiler_params=pltpu.CompilerParams(vmem_limit_bytes=VMEM_BYTES),
        cost_estimate=pl.CostEstimate(flops=flops, bytes_accessed=moved, transcendentals=0),
    )(*args)


def lanes(shape):
    return lax.broadcasted_iota(jnp.int32, shape, len(shape) - 1)


def dot_nt(a, b, precision=None):
    return lax.dot_general(
        a, b, (((1,), (1,)), ((), ())), preferred_element_type=f32, precision=precision
    )


def dot_tn(a, b):
    return lax.dot_general(a, b, (((0,), (0,)), ((), ())), preferred_element_type=f32)


def gate(token, *blocks):
    count = len(blocks)
    anywhere = pl.BlockSpec(memory_space=pl.ANY)

    def kernel(*refs):
        return None

    return pl.pallas_call(
        kernel,
        out_shape=[jax.ShapeDtypeStruct(x.shape, x.dtype) for x in blocks],
        in_specs=[anywhere] * (count + 1),
        out_specs=[anywhere] * count,
        input_output_aliases={i + 1: i for i in range(count)},
        cost_estimate=pl.CostEstimate(flops=0, bytes_accessed=1024, transcendentals=0),
    )(token, *blocks)


def ring_add(got, terms, slot, side, after=None):
    rows, columns = terms.shape[1:]
    some = got.shape[0]
    step = math.gcd(rows, RING_ROWS)
    steps, here = rows // step, some // step
    first = 0 if side == 0 else steps - here

    def kernel(*refs):
        got_ref, term_ref, out_ref = refs[0], refs[1], refs[-1]
        i = pl.program_id(0)
        inside = (i >= first) & (i < first + here)

        @pl.when(inside)
        def add():
            out_ref[...] = (got_ref[...].astype(f32) + term_ref[0].astype(f32)).astype(bf16)

        @pl.when(jnp.logical_not(inside))
        def keep():
            out_ref[...] = term_ref[0]

    extra = [] if after is None else [after]
    return pl.pallas_call(
        kernel,
        out_shape=jax.ShapeDtypeStruct((rows, columns), bf16),
        grid=(steps,),
        in_specs=[
            pl.BlockSpec((step, columns), lambda i: (jnp.clip(i - first, 0, here - 1), 0)),
            pl.BlockSpec((1, step, columns), lambda i: (slot, i, 0)),
        ]
        + [pl.BlockSpec(memory_space=pl.ANY)] * len(extra),
        out_specs=pl.BlockSpec((step, columns), lambda i: (i, 0)),
        compiler_params=pltpu.CompilerParams(vmem_limit_bytes=VMEM_BYTES),
        cost_estimate=pl.CostEstimate(
            flops=0, bytes_accessed=6 * rows * columns, transcendentals=0
        ),
    )(got, terms, *extra)


def ring_end(fwd, back, terms, split):
    rows, columns = terms.shape[1:]

    def kernel(fwd_ref, back_ref, term_ref, first_ref, rest_ref):
        for ref, here in ((first_ref, slice(0, split)), (rest_ref, slice(split, rows))):
            total = fwd_ref[here, :].astype(f32) + back_ref[here, :].astype(f32)
            ref[...] = (total + term_ref[0, here, :].astype(f32)).astype(bf16)

    whole = pl.BlockSpec((rows, columns), lambda i: (0, 0))
    return pl.pallas_call(
        kernel,
        out_shape=[
            jax.ShapeDtypeStruct((split, columns), bf16),
            jax.ShapeDtypeStruct((rows - split, columns), bf16),
        ],
        grid=(1,),
        in_specs=[whole, whole, pl.BlockSpec((1, rows, columns), lambda i: (0, 0, 0))],
        out_specs=[
            pl.BlockSpec((split, columns), lambda i: (0, 0)),
            pl.BlockSpec((rows - split, columns), lambda i: (0, 0)),
        ],
        compiler_params=pltpu.CompilerParams(vmem_limit_bytes=VMEM_BYTES),
        cost_estimate=pl.CostEstimate(
            flops=0, bytes_accessed=8 * rows * columns, transcendentals=0
        ),
    )(fwd, back, terms)


def pair_kernel(mine_ref, got_ref, *out_refs):
    rows = out_refs[0].shape[0]
    for s, out_ref in enumerate(out_refs):
        here = slice(s * rows, (s + 1) * rows)
        out_ref[...] = (mine_ref[here, :] + got_ref[here, :].astype(f32)).astype(out_ref.dtype)


def block_kernel(mlp_ref, down_ref, *refs):
    small = refs[0][...].astype(f32)
    for ref in refs[1:-1]:
        small = small + ref[...].astype(f32)
    out_ref = refs[-1]
    top = mlp_ref.shape[0]
    piece = small.shape[0]
    out_ref[:top, :] = mlp_ref[...]
    out_ref[top : top + piece, :] = small.astype(bf16)
    out_ref[top + piece :, :] = down_ref[...]


def qkv_kernel(x_ref, gain_ref, w_ref, b_ref, cos_ref, sin_ref, norm_ref, q_ref, pair_ref):
    x = x_ref[...].astype(f32)
    inverse = lax.rsqrt(jnp.mean(x * x, -1, keepdims=True) + EPS)
    normed = (x * inverse * gain_ref[...]).astype(bf16)
    norm_ref[...] = normed
    joint = jnp.dot(normed, w_ref[...], preferred_element_type=f32) + b_ref[...]
    cosine = cos_ref[...]
    sine = sin_ref[...]
    early = lanes(cosine.shape) % HD < HD // 2
    for i in range((WIDTH_Q + WIDTH_K) // 128):
        tile = joint[:, i * 128 : (i + 1) * 128]
        turned = jnp.where(early, -pltpu.roll(tile, 96, 1), pltpu.roll(tile, 32, 1))
        turned = tile * cosine + turned * sine
        if i * 128 < WIDTH_Q:
            q_ref[:, i * 128 : (i + 1) * 128] = turned.astype(bf16)
        else:
            pair_ref[:, :WIDTH_K] = turned.astype(bf16)
    pair_ref[:, WIDTH_K:] = joint[:, WIDTH_Q + WIDTH_K :].astype(bf16)


def spread_heads(x, out_ref, factor):
    rows = x.shape[0]
    half = rows // 2
    for head in range(QH):
        kh, g = divmod(head, GROUP)
        tile = x[:, (head // 2) * 128 : (head // 2 + 1) * 128].astype(f32)
        if head % 2 != kh:
            tile = pltpu.roll(tile, HD, 1)
        tile = jnp.where(lanes(tile.shape) // HD == kh, tile * factor, 0.0).astype(out_ref.dtype)
        for part in range(2):
            start = (part * GROUP + g) * half
            out_ref[kh, start : start + half, :] = tile[part * half : (part + 1) * half]


def join_heads(src_ref, half, tile):
    sides = []
    for side in range(2):
        kh, g = divmod(2 * tile + side, GROUP)
        parts = [
            src_ref[kh, (part * GROUP + g) * half : (part * GROUP + g + 1) * half, :]
            for part in range(2)
        ]
        both = jnp.concatenate(parts, 0)
        sides.append(both if side == kh else pltpu.roll(both, HD, 1))
    return jnp.where(lanes(sides[0].shape) < HD, sides[0], sides[1])


def forward_kernel(
    ctx, meta_ref, q_ref, mine_ref, other_ref, x_ref, w_ref, gain_ref,
    low_ref, o_ref, lse_ref, spread_ref, k_ref, v_ref, hidden_ref, normed_ref,
    s_ref, max_ref, sum_ref,
):
    rows = q_ref.shape[0]
    half = rows // 2
    part_rows = GROUP * half
    me = meta_ref[0]
    chips = ctx // 2
    for j in range(ctx):
        src = mine_ref if j < chips else other_ref
        at = (j % chips) * rows
        owner = meta_ref[1 + j]
        for part in range(2):
            place = owner if part == 0 else 2 * ctx - 1 - owner
            to = pl.ds(pl.multiple_of(place * half, half), half)
            block = src[at + part * half : at + (part + 1) * half, :]
            k_ref[to, :] = block[:, :WIDTH_K]
            v_ref[to, :] = block[:, WIDTH_K:]
    spread_heads(q_ref[...], spread_ref, HD ** (-0.5))
    for part in range(2):
        span = slice(part * part_rows, (part + 1) * part_rows)
        start = (me if part == 0 else 2 * ctx - 1 - me) * half
        last = start // KEYS

        def keys_of(ref, i):
            return ref[pl.ds(pl.multiple_of(i * KEYS, KEYS), KEYS), :]

        for kh in range(KH):
            scores = dot_nt(spread_ref[kh, span, :], keys_of(k_ref, last))
            row = lax.broadcasted_iota(jnp.int32, scores.shape, 0) % half + start
            scores = jnp.where(lanes(scores.shape) + last * KEYS <= row, scores, -1e30)
            s_ref[kh, last] = scores
            max_ref[kh] = jnp.maximum(scores[:, :128], scores[:, 128:])

        def score(i, carry):
            for kh in range(KH):
                s = dot_nt(spread_ref[kh, span, :], keys_of(k_ref, i))
                s_ref[kh, i] = s
                max_ref[kh] = jnp.maximum(max_ref[kh], jnp.maximum(s[:, :128], s[:, 128:]))
            return carry

        lax.fori_loop(0, last, score, 0)
        for kh in range(KH):
            top = jnp.max(max_ref[kh], -1, keepdims=True)
            max_ref[kh] = jnp.broadcast_to(top, (part_rows, 128))
            sum_ref[kh] = jnp.zeros((part_rows, 128), f32)
            o_ref[kh, span, :] = jnp.zeros((part_rows, 128), f32)

        def weigh(i, carry):
            for kh in range(KH):
                s = s_ref[kh, i]
                top = max_ref[kh]
                left = jnp.exp(s[:, :128] - top)
                right = jnp.exp(s[:, 128:] - top)
                sum_ref[kh] += left + right
                o_ref[kh, span, :] += jnp.dot(
                    jnp.concatenate([left, right], 1).astype(bf16),
                    keys_of(v_ref, i),
                    preferred_element_type=f32,
                )
            return carry

        lax.fori_loop(0, last + 1, weigh, 0)
        for kh in range(KH):
            total = jnp.sum(sum_ref[kh], -1, keepdims=True)
            o_ref[kh, span, :] = o_ref[kh, span, :] / total
            lse_ref[kh, part] = dot_nt(
                jnp.full((8, 128), 1.0 / 128, f32),
                max_ref[kh] + jnp.log(total),
                lax.Precision.HIGHEST,
            )
    for tile in range(WIDTH_Q // 128):
        low_ref[:, tile * 128 : (tile + 1) * 128] = join_heads(o_ref, half, tile).astype(bf16)
    hidden = x_ref[...].astype(f32) + jnp.dot(low_ref[...], w_ref[...], preferred_element_type=f32)
    hidden_ref[...] = hidden
    inverse = lax.rsqrt(jnp.mean(hidden * hidden, -1, keepdims=True) + EPS)
    normed_ref[...] = (hidden * inverse * gain_ref[...]).astype(bf16)


def backward_kernel(
    ctx, meta_ref, gn_ref, hidden_ref, gout_ref, gain_ref, w_ref, spread_ref, k_ref, v_ref, lse_ref,
    o_ref,
    gh_ref, ga_ref, gain_grad_ref, gq_ref, mine_ref, other_ref,
    go_ref, gqs_ref, gk_ref, gv_ref,
):
    rows = gn_ref.shape[0]
    half = rows // 2
    part_rows = GROUP * half
    me = meta_ref[0]
    chips = ctx // 2
    hidden = hidden_ref[...]
    inverse = lax.rsqrt(jnp.mean(hidden * hidden, -1, keepdims=True) + EPS)
    unit = hidden * inverse
    grad = gn_ref[...]
    gain_grad_ref[...] = jnp.sum(grad * unit, 0, keepdims=True)
    scaled = grad * gain_ref[...]
    gh = gout_ref[...].astype(f32) + inverse * (
        scaled - unit * jnp.mean(scaled * unit, -1, keepdims=True)
    )
    gh_ref[...] = gh
    ga = gh.astype(bf16)
    ga_ref[...] = ga
    spread_heads(dot_nt(ga, w_ref[...]).astype(bf16), go_ref, 1.0)
    gqs_ref[...] = jnp.zeros_like(gqs_ref)
    gk_ref[...] = jnp.zeros_like(gk_ref)
    gv_ref[...] = jnp.zeros_like(gv_ref)
    for part in range(2):
        span = slice(part * part_rows, (part + 1) * part_rows)
        start = (me if part == 0 else 2 * ctx - 1 - me) * half
        last = start // KEYS
        deltas = [
            dot_nt(
                jnp.ones((8, 128), f32),
                go_ref[kh, span, :].astype(f32) * o_ref[kh, span, :],
                lax.Precision.HIGHEST,
            )[:1]
            for kh in range(KH)
        ]

        def step(i, masked):
            at = pl.ds(pl.multiple_of(i * KEYS, KEYS), KEYS)
            keys = k_ref[at, :]
            grad_k = gk_ref[at, :]
            grad_v = gv_ref[at, :]
            for kh in range(KH):
                queries = spread_ref[kh, span, :]
                heads = go_ref[kh, span, :]
                p = jnp.exp(dot_nt(keys, queries) - lse_ref[kh, part][:1])
                if masked:
                    row = lanes(p.shape) % half + start
                    key = lax.broadcasted_iota(jnp.int32, p.shape, 0) + i * KEYS
                    p = jnp.where(key <= row, p, 0.0)
                gs = (p * (dot_nt(v_ref[at, :], heads) - deltas[kh])).astype(bf16)
                grad_v += jnp.dot(p.astype(bf16), heads, preferred_element_type=f32)
                grad_k += jnp.dot(gs, queries, preferred_element_type=f32)
                gqs_ref[kh, span, :] += dot_tn(gs, keys)
            gk_ref[at, :] = grad_k
            gv_ref[at, :] = grad_v

        def body(i, carry):
            step(i, False)
            return carry

        lax.fori_loop(0, last, body, 0)
        step(last, True)
    for tile in range(WIDTH_Q // 128):
        gq_ref[:, tile * 128 : (tile + 1) * 128] = join_heads(gqs_ref, half, tile) * HD ** (-0.5)
    for j in range(ctx):
        dst = mine_ref if j < chips else other_ref
        at = (j % chips) * rows
        owner = meta_ref[1 + j]
        for part in range(2):
            place = owner if part == 0 else 2 * ctx - 1 - owner
            frm = pl.ds(pl.multiple_of(place * half, half), half)
            to = slice(at + part * half, at + (part + 1) * half)
            dst[to, :WIDTH_K] = gk_ref[frm, :].astype(dst.dtype)
            dst[to, WIDTH_K:] = gv_ref[frm, :].astype(dst.dtype)


def finish_kernel(
    gq_ref, x_ref, gain_ref, w_ref, cos_ref, sin_ref, gh_ref, *refs
):
    joint_ref, gx_ref, gain_grad_ref, bias_ref = refs[-4:]
    pair = refs[0][...]
    for ref in refs[1:-4]:
        pair = pair + ref[...].astype(f32)
    cosine = cos_ref[...]
    sine = sin_ref[...]
    early = lanes(cosine.shape) % HD < HD // 2
    for i in range((WIDTH_Q + WIDTH_K) // 128):
        at = slice(i * 128, (i + 1) * 128)
        grad = gq_ref[:, at] if i * 128 < WIDTH_Q else pair[:, :WIDTH_K]
        scaled = grad * sine
        turned = jnp.where(early, pltpu.roll(scaled, 96, 1), -pltpu.roll(scaled, 32, 1))
        joint_ref[:, at] = (grad * cosine + turned).astype(bf16)
    joint_ref[:, WIDTH_Q + WIDTH_K :] = pair[:, WIDTH_K:].astype(bf16)
    joint = joint_ref[...]
    bias_ref[...] = jnp.sum(joint.astype(f32), 0, keepdims=True)
    grad = dot_nt(joint, w_ref[...])
    x = x_ref[...].astype(f32)
    inverse = lax.rsqrt(jnp.mean(x * x, -1, keepdims=True) + EPS)
    unit = x * inverse
    gain_grad_ref[...] = jnp.sum(grad * unit, 0, keepdims=True)
    scaled = grad * gain_ref[...]
    gx_ref[...] = gh_ref[...] + inverse * (
        scaled - unit * jnp.mean(scaled * unit, -1, keepdims=True)
    )


def mlp_kernel(
    half_rows, spots_ref, x_ref, gy_ref, gate_a, gate_b, up_a, up_b, down_a, down_b,
    xt_ref, midt_ref, gg_ref, gu_ref, gx_ref, out_ref, send_ref,
    wg_all, wu_all, wd_all, mid_all, gg_all, gu_all,
):
    step = pl.program_id(0)
    here = pl.ds(pl.multiple_of(step * 256, 256), 256)
    wg = jnp.concatenate([gate_a[...], gate_b[...]], 1)
    wu = jnp.concatenate([up_a[...], up_b[...]], 1)
    wd = jnp.concatenate([down_a[...], down_b[...]], 0)
    wg_all[:, here] = wg
    wu_all[:, here] = wu
    wd_all[here, :] = wd
    core = spots_ref[1]
    column = lanes((1, 256)) + (step * 256 + spots_ref[2])
    own = (column < spots_ref[3]) == (core == 0)
    tokens = x_ref.shape[0]
    for r in range(0, tokens, 256):
        rows = slice(r, r + 256)
        x = x_ref[rows, :]
        gate = jnp.dot(x, wg, preferred_element_type=f32)
        up = jnp.dot(x, wu, preferred_element_type=f32)
        grad = jnp.where(own, dot_nt(gy_ref[rows, :], wd), 0.0)
        sigma = jax.nn.sigmoid(gate)
        active = gate * sigma
        middle = jnp.where(own, active * up, 0.0).astype(bf16)
        grad_gate = (grad * up * (sigma + active * (1.0 - sigma))).astype(bf16)
        grad_up = (grad * active).astype(bf16)
        midt_ref[:, rows] = middle.T
        gg_ref[rows, :] = grad_gate
        gu_ref[rows, :] = grad_up
        mid_all[rows, here] = middle
        gg_all[rows, here] = grad_gate
        gu_all[rows, here] = grad_up

    @pl.when(step == 0)
    def transpose():
        xt_ref[...] = x_ref[...].T

    @pl.when(step == pl.num_programs(0) - 1)
    def end():
        gx = dot_nt(gg_all[...], wg_all[...]) + dot_nt(gu_all[...], wu_all[...])
        gx_ref[...] = gx[:half_rows]
        send_ref[:half_rows] = gx[half_rows:].astype(bf16)
        out = jnp.dot(mid_all[...], wd_all[...], preferred_element_type=f32)
        out_ref[...] = out[:half_rows]
        send_ref[half_rows:] = out[half_rows:].astype(bf16)


def feed_forward(meta, x, gy, w_gate, w_up, w_down, width):
    tokens = x.shape[0]
    half = tokens // 2
    steps = width // 256
    tiles = width // 128 - 1

    def columns(j):
        return pl.BlockSpec((D, 128), lambda i, m: (0, m[1] * tiles + 2 * i + j))

    def rows(j):
        return pl.BlockSpec((128, D), lambda i, m: (m[1] * tiles + 2 * i + j, 0))

    whole = pl.BlockSpec((tokens, D), lambda i, m: (0, 0))
    halves = pl.BlockSpec((half, D), lambda i, m: (0, 0))
    tile = pl.BlockSpec((tokens, 256), lambda i, m: (0, i))
    hidden = jax.ShapeDtypeStruct((tokens, width), bf16)
    return pl.pallas_call(
        lambda *refs: mlp_kernel(half, *refs),
        out_shape=[
            jax.ShapeDtypeStruct((D, tokens), bf16),
            jax.ShapeDtypeStruct((width, tokens), bf16),
            hidden,
            hidden,
            jax.ShapeDtypeStruct((half, D), f32),
            jax.ShapeDtypeStruct((half, D), f32),
            jax.ShapeDtypeStruct((tokens, D), bf16),
        ],
        grid_spec=pltpu.PrefetchScalarGridSpec(
            num_scalar_prefetch=1,
            grid=(steps,),
            in_specs=[whole, whole, columns(0), columns(1), columns(0), columns(1), rows(0), rows(1)],
            out_specs=[
                pl.BlockSpec((D, tokens), lambda i, m: (0, 0)),
                pl.BlockSpec((256, tokens), lambda i, m: (i, 0)),
                tile,
                tile,
                halves,
                halves,
                whole,
            ],
            scratch_shapes=[pltpu.VMEM((D, width), bf16)] * 2
            + [pltpu.VMEM((width, D), bf16)]
            + [pltpu.VMEM((tokens, width), bf16)] * 3,
        ),
        compiler_params=pltpu.CompilerParams(vmem_limit_bytes=VMEM_BYTES),
        cost_estimate=pl.CostEstimate(
            flops=12 * tokens * width * D, bytes_accessed=6 * width * D, transcendentals=0
        ),
    )(meta, x, gy, w_gate, w_gate, w_up, w_up, w_down, w_down)


def mlp_grad_kernel(
    down_rows, main, meta_ref, xt_ref, gy_ref, midt_ref, gg_ref, gu_ref,
    out_ref, head_ref, tail_ref, mlp_acc, down_acc,
):
    step = pl.program_id(0)
    core = meta_ref[1]
    at_main = pl.ds(pl.multiple_of(core * 128, 128), main)
    at_tile = pl.ds(pl.multiple_of((1 - core) * main, 128), 128)

    @pl.when(step == 0)
    def products():
        xt = xt_ref[...]
        mlp_acc[:, :main] = jnp.dot(
            xt, gg_ref[:, at_main], preferred_element_type=f32
        ).astype(bf16)
        mlp_acc[:, main : 2 * main] = jnp.dot(
            xt, gu_ref[:, at_main], preferred_element_type=f32
        ).astype(bf16)
        mixed = gg_ref[:, at_tile].astype(f32) + pltpu.roll(gu_ref[:, at_tile].astype(f32), 64, 1)
        mlp_acc[:, 2 * main :] = jnp.dot(
            xt, mixed.astype(bf16), preferred_element_type=f32
        ).astype(bf16)
        down_acc[...] = jnp.dot(midt_ref[...], gy_ref[...], preferred_element_type=f32)

    mlp_rows = mlp_acc.shape[0] // pl.num_programs(0)
    columns = mlp_acc.shape[1] // 128
    block = mlp_acc[pl.ds(pl.multiple_of(step * mlp_rows, 16), mlp_rows), :]
    for j in range(columns):
        for i in range(mlp_rows // 16):
            out_ref[0, j * 16 : (j + 1) * 16, i * 128 : (i + 1) * 128] = block[
                i * 16 : (i + 1) * 16, j * 128 : (j + 1) * 128
            ]
    first = pl.multiple_of(core * 64 + step * down_rows, 8)
    out_ref[0, columns * 16 :, :] = down_acc[pl.ds(first, down_rows), :].astype(bf16)

    @pl.when(meta_ref[4 + step] == pl.num_programs(0) // 2)
    def far():
        head_ref[...] = out_ref[0, : head_ref.shape[0], :]
        tail_ref[...] = out_ref[0, head_ref.shape[0] :, :]


def mlp_gradients(meta, xt, gy, midt, gg, gu, chips, down_rows, main):
    tokens = gy.shape[0]
    columns = (2 * main + 128) // 128
    cut = columns * 16
    rows = cut + down_rows

    def whole(x):
        return pl.BlockSpec(x.shape, lambda i, m: (0, 0))

    return pl.pallas_call(
        lambda *refs: mlp_grad_kernel(down_rows, main, *refs),
        out_shape=[
            jax.ShapeDtypeStruct((chips, rows, D), bf16),
            jax.ShapeDtypeStruct((cut, D), bf16),
            jax.ShapeDtypeStruct((rows - cut, D), bf16),
        ],
        grid_spec=pltpu.PrefetchScalarGridSpec(
            num_scalar_prefetch=1,
            grid=(chips,),
            in_specs=[whole(x) for x in (xt, gy, midt, gg, gu)],
            out_specs=[
                pl.BlockSpec((1, rows, D), lambda i, m: (m[4 + i], 0, 0)),
                pl.BlockSpec((cut, D), lambda i, m: (0, 0)),
                pl.BlockSpec((rows - cut, D), lambda i, m: (0, 0)),
            ],
            scratch_shapes=[
                pltpu.VMEM((D, columns * 128), bf16),
                pltpu.VMEM((midt.shape[0], D), f32),
            ],
        ),
        compiler_params=pltpu.CompilerParams(vmem_limit_bytes=VMEM_BYTES),
        cost_estimate=pl.CostEstimate(
            flops=6 * tokens * midt.shape[0] * D, bytes_accessed=4 * chips * rows * D,
            transcendentals=0,
        ),
    )(meta, xt, gy, midt, gg, gu)


def small_grad_kernel(chips, q_rows, meta_ref, norm_ref, joint_ref, att_ref, ga_ref, *refs):
    out_refs, acc = refs[:-1], refs[-1]
    cols = joint_ref.shape[1]
    acc[:, :cols] = dot_tn(norm_ref[...], joint_ref[...])
    acc[:, cols:] = dot_tn(att_ref[...], ga_ref[...])
    first = pl.multiple_of((2 * meta_ref[0] + meta_ref[1]) * q_rows, 16)
    width = acc.shape[1] // chips
    for out_ref, slot in zip(out_refs, range(chips)):
        column = pl.multiple_of(meta_ref[12 + slot] * width, 128)
        block = acc[pl.ds(first, q_rows), pl.ds(column, width)]
        tall = jnp.concatenate(
            [block[:, i * 128 : (i + 1) * 128] for i in range(width // 128)], 0
        ).astype(bf16)
        piece = out_ref.shape[0]
        for i in range(D // 128):
            out_ref[:, i * 128 : (i + 1) * 128] = tall[i * piece : (i + 1) * piece]


def place_all(meta, slots, pairs, old, sizes):
    main, ff_loc, q_rows, cols, down_rows, chips = sizes
    mlp_rows = D // chips
    columns = (2 * main + 128) // 128
    tiles = main // 128
    lanes_out = D // 128
    top = columns * 16
    blocks = [x for pair in pairs for x in pair]
    count = len(blocks)
    piece = blocks[0].shape[0] - top - down_rows
    parts = (cols + D) // chips // 128
    keep = [] if old is None else list(old)

    def kernel(meta_ref, *refs):
        ins = refs[:count]
        gate_out, up_out, down_out, joint_out, proj_out, token_ref = refs[
            count + len(keep) : count + len(keep) + 6
        ]
        gate_buf, up_buf, down_buf, small_buf, sems, small_sems = refs[count + len(keep) + 6 :]
        core_zero = meta_ref[1] == 0
        copies = []

        def send(src, dst, sem):
            copy = pltpu.make_async_copy(src, dst, sem)
            copy.start()
            copies.append(copy)

        def column(ref, j):
            found = [
                ref[j * 16 : (j + 1) * 16, i * 128 : (i + 1) * 128] for i in range(mlp_rows // 16)
            ]
            return jnp.concatenate(found, 0).astype(f32)

        for k, slot in enumerate(slots):
            for j in range(columns):
                got = column(ins[2 * k], j)
                other = column(ins[2 * k + 1], j)
                zero = jnp.where(core_zero, got, other)
                one = jnp.where(core_zero, other, got)
                if j < 2 * tiles:
                    buf = gate_buf if j < tiles else up_buf
                    at = (j % tiles) * 128
                    buf[k, :, at : at + 128] = zero
                    buf[k, :, at + main + 128 : at + main + 256] = one
                else:
                    left = lanes(zero.shape) < 64
                    gate_buf[k, :, main : main + 128] = jnp.where(left, zero, one)
                    up_buf[k, :, main : main + 128] = pltpu.roll(jnp.where(left, one, zero), 64, 1)
            owner = meta_ref[12 + slot]
            here = pl.ds(pl.multiple_of(owner * mlp_rows, 8), mlp_rows)
            send(gate_buf.at[k], gate_out.at[here, :], sems.at[4 * k])
            send(up_buf.at[k], up_out.at[here, :], sems.at[4 * k + 1])
            for side in range(2):
                b = 2 * k + side
                core = meta_ref[1] if side == 0 else 1 - meta_ref[1]
                down_buf[b] = ins[b][top + piece :, :].astype(f32)
                here = pl.ds(pl.multiple_of((core * chips + owner) * down_rows, 8), down_rows)
                send(down_buf.at[b], down_out.at[here, :], sems.at[4 * k + 2 + side])
                tall = jnp.concatenate(
                    [ins[b][top : top + piece, i * 128 : (i + 1) * 128] for i in range(lanes_out)], 0
                ).astype(f32)
                rows = pl.ds(pl.multiple_of(core * q_rows, 8), q_rows)
                for i in range(parts):
                    small_buf[b, i] = tall[i * q_rows : (i + 1) * q_rows]
                    block = owner * parts + i

                    @pl.when(block < cols // 128)
                    def joint(b=b, i=i, rows=rows, block=block):
                        at = pl.ds(pl.multiple_of(block * 128, 128), 128)
                        pltpu.make_async_copy(
                            small_buf.at[b, i], joint_out.at[rows, at], small_sems.at[b, i]
                        ).start()

                    @pl.when(block >= cols // 128)
                    def proj(b=b, i=i, rows=rows, block=block):
                        at = pl.ds(pl.multiple_of((block - cols // 128) * 128, 128), 128)
                        pltpu.make_async_copy(
                            small_buf.at[b, i], proj_out.at[rows, at], small_sems.at[b, i]
                        ).start()

        token_ref[...] = jnp.zeros(token_ref.shape, f32)
        for copy in copies:
            copy.wait()
        for b in range(count):
            for i in range(parts):
                pltpu.make_async_copy(
                    small_buf.at[b, i],
                    proj_out.at[pl.ds(0, q_rows), pl.ds(0, 128)],
                    small_sems.at[b, i],
                ).wait()

    anywhere = pl.BlockSpec(memory_space=pl.ANY)
    result = pl.pallas_call(
        kernel,
        out_shape=[
            jax.ShapeDtypeStruct((D, ff_loc), f32),
            jax.ShapeDtypeStruct((D, ff_loc), f32),
            jax.ShapeDtypeStruct((ff_loc, D), f32),
            jax.ShapeDtypeStruct((2 * q_rows, cols), f32),
            jax.ShapeDtypeStruct((2 * q_rows, D), f32),
            jax.ShapeDtypeStruct((8, 128), f32),
        ],
        in_specs=[pl.BlockSpec(memory_space=pltpu.SMEM)]
        + [pl.BlockSpec(memory_space=pltpu.VMEM)] * count
        + [anywhere] * len(keep),
        out_specs=[anywhere] * 5 + [pl.BlockSpec(memory_space=pltpu.VMEM)],
        scratch_shapes=[
            pltpu.VMEM((len(slots), mlp_rows, ff_loc), f32),
            pltpu.VMEM((len(slots), mlp_rows, ff_loc), f32),
            pltpu.VMEM((count, down_rows, D), f32),
            pltpu.VMEM((count, parts, q_rows, 128), f32),
            pltpu.SemaphoreType.DMA((4 * len(slots),)),
            pltpu.SemaphoreType.DMA((count, parts)),
        ],
        input_output_aliases={1 + count + i: i for i in range(len(keep))},
        compiler_params=pltpu.CompilerParams(vmem_limit_bytes=VMEM_BYTES),
        cost_estimate=pl.CostEstimate(
            flops=0, bytes_accessed=8 * sum(x.size for x in blocks), transcendentals=0
        ),
    )(meta, *blocks, *keep)
    return list(result[:5]), result[5]


def place_blocks(blocks, spots, out_shape, old=None):
    shape = blocks[0].shape
    count = len(blocks)
    if shape[0] % 8 or shape[1] % 128:
        out = jnp.zeros(out_shape, f32) if old is None else old
        for block, (i, j) in zip(blocks, spots):
            out = lax.dynamic_update_slice(
                out, block.astype(f32), (i * shape[0], j * shape[1])
            )
        return out

    def kernel(spots_ref, *refs):
        step = pl.program_id(0)
        out_ref = refs[-1]
        for i in range(count):

            @pl.when(step == i)
            def write(i=i):
                out_ref[...] = refs[i][...].astype(f32)

    keep = [] if old is None else [old]
    return pl.pallas_call(
        kernel,
        out_shape=jax.ShapeDtypeStruct(out_shape, f32),
        grid_spec=pltpu.PrefetchScalarGridSpec(
            num_scalar_prefetch=1,
            grid=(count,),
            in_specs=[pl.BlockSpec(shape, lambda i, spots: (0, 0))] * count
            + [pl.BlockSpec(memory_space=pl.ANY)] * len(keep),
            out_specs=pl.BlockSpec(shape, lambda i, spots: (spots[i, 0], spots[i, 1])),
        ),
        input_output_aliases={} if old is None else {count + 1: 0},
        compiler_params=pltpu.CompilerParams(vmem_limit_bytes=VMEM_BYTES),
    )(jnp.stack([jnp.stack(s) for s in spots]).astype(jnp.int32), *blocks, *keep)


def local(tokens, w_qkv, b_qkv, w_out, gain_attn, gain_mlp, w_gate, w_up, w_down, cotangent):
    net = Net()
    rows = tokens.shape[1]
    half_rows = rows // 2
    ctx_count = net.ctx
    core = net.core
    chips = net.chips
    part_rows = GROUP * half_rows
    x = tokens[0]
    gain_one = gain_attn[None]
    gain_two = gain_mlp[None]

    w_qkv_full = net.full_rows(w_qkv)

    ff_loc = w_gate.shape[1]
    ff_half = ff_loc // 2
    main = (ff_half // 128) * 128
    rest = ff_half - main
    width = main + 2 * rest
    first = core * main
    tiled = 2 * rest == 128 and width % 256 == 0 and chips == 8 and ff_half == chips * RING_ROWS
    ring = jnp.arange(chips, dtype=jnp.int32)
    owners_of = (net.pos - ring) % chips
    spots = jnp.concatenate(
        [jnp.stack([net.d, core, first, jnp.int32(ff_half)]), owners_of, owners_of]
    ).astype(jnp.int32)

    row_ids = jnp.arange(half_rows, dtype=jnp.int32)
    place = jnp.concatenate(
        [net.c * half_rows + row_ids, (2 * ctx_count - 1 - net.c) * half_rows + row_ids]
    )
    freq = ROPE_BASE ** (-((jnp.arange(128) % (HD // 2)).astype(f32) * (2.0 / HD)))
    angle = place.astype(f32)[:, None] * freq[None, :]
    cosine, sine = jnp.cos(angle), jnp.sin(angle)
    normed_one, queries, pairs = call(
        qkv_kernel,
        [
            jax.ShapeDtypeStruct((rows, D), bf16),
            jax.ShapeDtypeStruct((rows, WIDTH_Q), bf16),
            jax.ShapeDtypeStruct((rows, 2 * WIDTH_K), bf16),
        ],
        [x, gain_one, w_qkv_full, b_qkv[None], cosine, sine],
        flops=2 * rows * D * 1152,
    )

    slots = net.ring_gather(pairs)
    mine = jnp.concatenate(slots, 0)
    other = net.swap(mine)
    order = jnp.array(net.order, jnp.int32)
    chip_ids = order[(net.pos - jnp.arange(chips, dtype=jnp.int32)) % chips]
    meta = jnp.concatenate([net.c[None], 2 * chip_ids + core, 2 * chip_ids + 1 - core])
    meta = meta.astype(jnp.int32)

    late_w, late_g, late_n, unused = lax.optimization_barrier((w_out, cotangent[0], normed_one, pairs))
    w_out_full = net.full_rows(late_w)
    early_group = net.group_gather(jnp.concatenate([late_g, late_n], 1))
    grad_out_group = early_group[:, :D]
    normed_one_group = early_group[:, D:]

    total_keys = rows * ctx_count
    padded = (KH, 2 * part_rows, 128)
    attended_low, attended, lse, spread, keys, values, hidden, normed_two = call(
        lambda *refs: forward_kernel(ctx_count, *refs),
        [
            jax.ShapeDtypeStruct((rows, WIDTH_Q), bf16),
            jax.ShapeDtypeStruct(padded, f32),
            jax.ShapeDtypeStruct((KH, 2, 8, part_rows), f32),
            jax.ShapeDtypeStruct(padded, bf16),
            jax.ShapeDtypeStruct((total_keys, WIDTH_K), bf16),
            jax.ShapeDtypeStruct((total_keys, WIDTH_K), bf16),
            jax.ShapeDtypeStruct((rows, D), f32),
            jax.ShapeDtypeStruct((rows, D), bf16),
        ],
        [meta, queries, mine, other, x, w_out_full, gain_two],
        smem=1,
        scratch=[
            pltpu.VMEM((KH, total_keys // KEYS, part_rows, KEYS), f32),
            pltpu.VMEM((KH, part_rows, 128), f32),
            pltpu.VMEM((KH, part_rows, 128), f32),
        ],
        flops=8 * KH * part_rows * total_keys * 128,
    )

    normed_two_group = net.group_gather(normed_two)
    chip_rows = net.dp * rows
    down_rows = ff_half // chips
    mlp_rows = D // chips
    if tiled:
        x_turned, mid_turned, gate_low, up_low, grad_mine, out_mine, sent = feed_forward(
            spots, normed_two_group, grad_out_group, w_gate, w_up, w_down, width
        )
    else:
        own_cols = (jnp.arange(width) + first < ff_half) == (core == 0)
        wg = lax.dynamic_slice(w_gate, (0, first), (D, width))
        wu = lax.dynamic_slice(w_up, (0, first), (D, width))
        wd = lax.dynamic_slice(w_down, (first, 0), (width, D))
        gate = jnp.dot(normed_two_group, wg, preferred_element_type=f32)
        upper = jnp.dot(normed_two_group, wu, preferred_element_type=f32)
        sigma = jax.nn.sigmoid(gate)
        activated = gate * sigma
        middle = jnp.where(own_cols, activated * upper, 0.0).astype(bf16)
        grad_middle = jnp.einsum("td,fd->tf", grad_out_group, wd, preferred_element_type=f32)
        slope = sigma * (1.0 + gate * (1.0 - sigma))
        grad_gate_low = jnp.where(own_cols, grad_middle * upper * slope, 0.0).astype(bf16)
        grad_up_low = jnp.where(own_cols, grad_middle * activated, 0.0).astype(bf16)

        grad_normed_two = jnp.einsum(
            "tf,df->td", grad_gate_low, wg, preferred_element_type=f32
        ) + jnp.einsum("tf,df->td", grad_up_low, wu, preferred_element_type=f32)
        mlp_out = jnp.dot(middle, wd, preferred_element_type=f32)
        grad_mine, out_mine = grad_normed_two[:chip_rows], mlp_out[:chip_rows]
        sent = jnp.concatenate([grad_normed_two[chip_rows:], mlp_out[chip_rows:]], 0).astype(bf16)
    swapped = net.swap(sent)
    grad_chip = grad_mine + swapped[:chip_rows].astype(f32)
    mlp_chip = out_mine + swapped[chip_rows:].astype(f32)
    grad_two = grad_chip[:rows]
    for s in range(1, net.dp):
        piece = grad_chip[s * rows : (s + 1) * rows].astype(bf16)
        grad_two = grad_two + net.shift(piece, net.dp - s).astype(f32)

    def attention_back(*after):
        grad_hidden, grad_attn_low, grad_gain_two, grad_queries, terms_mine, terms_other = call(
            lambda *refs: backward_kernel(ctx_count, *refs),
            [
                jax.ShapeDtypeStruct((rows, D), f32),
                jax.ShapeDtypeStruct((rows, D), bf16),
                jax.ShapeDtypeStruct((1, D), f32),
                jax.ShapeDtypeStruct((rows, WIDTH_Q), f32),
                jax.ShapeDtypeStruct((chips * rows, 2 * WIDTH_K), f32),
                jax.ShapeDtypeStruct((chips * rows, 2 * WIDTH_K), bf16),
            ],
            [
                meta, grad_two, hidden, cotangent[0], gain_two, w_out_full, spread, keys, values, lse,
                attended,
            ] + list(after),
            smem=1,
            loose=len(after),
            scratch=[
                pltpu.VMEM(padded, bf16),
                pltpu.VMEM(padded, f32),
                pltpu.VMEM((total_keys, WIDTH_K), f32),
                pltpu.VMEM((total_keys, WIDTH_K), f32),
            ],
            flops=20 * KH * part_rows * total_keys * 128,
        )
        pair_sums = call(
            pair_kernel,
            [jax.ShapeDtypeStruct((rows, 2 * WIDTH_K), f32)]
            + [jax.ShapeDtypeStruct((rows, 2 * WIDTH_K), bf16)] * (chips - 1),
            [terms_mine, net.swap(terms_other)],
        )
        grad_pairs = net.ring_parts(pair_sums)
        grad_joint_low, grad_input, grad_gain_one, grad_bias = call(
            finish_kernel,
            [
                jax.ShapeDtypeStruct((rows, 1152), bf16),
                jax.ShapeDtypeStruct((rows, D), f32),
                jax.ShapeDtypeStruct((1, D), f32),
                jax.ShapeDtypeStruct((1, 1152), f32),
            ],
            [grad_queries, x, gain_one, w_qkv_full, cosine, sine, grad_hidden] + grad_pairs,
            flops=2 * rows * D * 1152,
        )
        return (
            grad_hidden, grad_attn_low, grad_gain_two, grad_joint_low, grad_input, grad_gain_one,
            grad_bias,
        )

    found = []
    if tiled:

        def middle(*after):
            found.extend(attention_back(*after))
            return found[3]

        terms, head, tail = mlp_gradients(
            spots, x_turned, grad_out_group, mid_turned, gate_low, up_low, chips, down_rows, main
        )
        sum_mlp, sum_down = net.ring_sum(
            head, tail, terms, terms.shape[1] - down_rows, middle
        )
    else:
        part_down = jnp.einsum(
            "tf,td->fd", middle, grad_out_group, preferred_element_type=f32
        ).astype(bf16)
        part_down = lax.dynamic_slice(part_down, (core * rest, 0), (ff_half, D))

        def down_chunk(slot):
            return lax.dynamic_slice(part_down, (net.owner(slot) * down_rows, 0), (down_rows, D))

        sum_down = net.ring_scatter([down_chunk(s) for s in range(chips)]).astype(bf16)

        def split_main(x):
            left = (x[:, :main], x[:, main:])
            right = (x[:, 2 * rest :], x[:, : 2 * rest])
            return (
                jnp.where(core == 0, left[0], right[0]),
                jnp.where(core == 0, left[1], right[1]),
            )

        gate_main, gate_tile = split_main(grad_gate_low)
        up_main, up_tile = split_main(grad_up_low)
        packed = jnp.concatenate(
            [gate_main, up_main, gate_tile + jnp.roll(up_tile, rest, 1)], 1
        )
        part_mlp = jnp.einsum(
            "td,tf->df", normed_two_group, packed, preferred_element_type=f32
        ).astype(bf16)

        def mlp_chunk(slot):
            return lax.dynamic_slice(
                part_mlp, (net.owner(slot) * mlp_rows, 0), (mlp_rows, 2 * ff_half)
            )

        sum_mlp = net.ring_scatter([mlp_chunk(s) for s in range(chips)]).astype(bf16)
        sum_mlp = lax.optimization_barrier(sum_mlp)
        found.extend(attention_back())
    grad_hidden, grad_attn_low, grad_gain_two, grad_joint_low, grad_input = found[:5]
    grad_gain_one, grad_bias = found[5:]

    out_sum = mlp_chip[:rows]
    sent = jnp.concatenate([attended_low, grad_attn_low], 0)
    gathered = [sent]
    for s in range(1, net.dp):
        got = net.shift(
            jnp.concatenate([mlp_chip[s * rows : (s + 1) * rows].astype(bf16), sent], 0),
            net.dp - s,
        )
        out_sum = out_sum + got[:rows].astype(f32)
        gathered.append(got[rows:])
    output = (hidden + out_sum).astype(bf16)
    gathered = jnp.concatenate(gathered, 0)
    gathered = jnp.concatenate([gathered, net.swap(gathered)], 0).reshape(2 * net.dp, 2, rows, D)
    attended_group = gathered[:, 0].reshape(2 * net.dp * rows, D)
    grad_attn_group = gathered[:, 1].reshape(2 * net.dp * rows, D)

    q_rows = w_qkv.shape[0] // 2
    qkv_cols = w_qkv.shape[1]
    joint_group = net.group_gather(grad_joint_low)
    if tiled:
        piece = q_rows * (qkv_cols + D) // chips // D
        terms_small = call(
            lambda *refs: small_grad_kernel(chips, q_rows, *refs),
            [jax.ShapeDtypeStruct((piece, D), bf16)] * chips,
            [spots, normed_one_group, joint_group, attended_group, grad_attn_group],
            smem=1,
            scratch=[pltpu.VMEM((D, qkv_cols + D), f32)],
            flops=4 * chip_rows * D * (qkv_cols + D),
        )
        block = call(
            block_kernel,
            [jax.ShapeDtypeStruct((sum_mlp.shape[0] + piece + down_rows, D), bf16)],
            [sum_mlp, sum_down] + net.ring_parts(terms_small),
        )[0]
        sizes = (main, ff_loc, q_rows, qkv_cols, down_rows, chips)
        grad_gate, grad_up, grad_down, grad_joint, grad_out_proj = net.gather_placed(
            block, lambda slots, pairs, old: place_all(spots, slots, pairs, old, sizes)
        )
    else:
        q_first = net.d * (2 * q_rows) + core * q_rows
        group_rows = 2 * net.dp * rows
        part_out = jnp.einsum(
            "tc,td->cd",
            lax.dynamic_slice(attended_group, (0, q_first), (group_rows, q_rows)),
            grad_attn_group,
            preferred_element_type=f32,
        )
        part_joint = jnp.einsum(
            "td,tc->dc",
            lax.dynamic_slice(normed_one_group, (0, q_first), (group_rows, q_rows)),
            joint_group,
            preferred_element_type=f32,
        )
        part_small = jnp.concatenate([part_joint, part_out], 1).astype(bf16)
        small_cols = part_small.shape[1] // chips

        def small_chunk(slot):
            return lax.dynamic_slice(part_small, (0, net.owner(slot) * small_cols), (q_rows, small_cols))

        sum_small = net.ring_scatter([small_chunk(s) for s in range(chips)]).astype(bf16)

        tall = jnp.concatenate(
            [sum_small[:, i * 128 : (i + 1) * 128] for i in range(small_cols // 128)], 0
        )
        piece = tall.shape[0] // (D // 128)
        wide = jnp.concatenate([tall[i * piece : (i + 1) * piece] for i in range(D // 128)], 1)
        both = lax.optimization_barrier(jnp.concatenate([sum_down, wide], 0))

        owners = [net.owner(s) for s in range(chips)]
        got_mlp = net.ring_gather(sum_mlp)
        got_both = net.ring_gather(both)
        pairs_mlp = [(got, net.swap(got)) for got in got_mlp]
        pairs_both = [(got, net.swap(got)) for got in got_both]

        down_blocks, down_spots, small_blocks, small_spots = [], [], [], []
        for owner, pair in zip(owners, pairs_both):
            for which, got in zip((core, 1 - core), pair):
                down_blocks.append(got[:down_rows])
                down_spots.append((which * chips + owner, jnp.int32(0)))
                wide = got[down_rows:]
                tall = jnp.concatenate([wide[:, i * 128 : (i + 1) * 128] for i in range(D // 128)], 0)
                small_blocks.append(
                    jnp.concatenate(
                        [tall[i * q_rows : (i + 1) * q_rows] for i in range(small_cols // 128)], 1
                    )
                )
                small_spots.append((which, owner))
        grad_down = place_blocks(down_blocks, down_spots, (ff_loc, D))
        grad_small = place_blocks(small_blocks, small_spots, (2 * q_rows, part_small.shape[1]))
        grad_gate = jnp.zeros((D, ff_loc), f32)
        grad_up = jnp.zeros((D, ff_loc), f32)
        left_lane = jnp.arange(2 * rest) < rest
        for owner, (got, swapped) in zip(owners, pairs_mlp):
            zero = jnp.where(core == 0, got, swapped).astype(f32)
            one = jnp.where(core == 0, swapped, got).astype(f32)
            tile_zero, tile_one = zero[:, 2 * main :], one[:, 2 * main :]
            mid_gate = jnp.where(left_lane, tile_zero, tile_one)
            mid_up = jnp.roll(jnp.where(left_lane, tile_one, tile_zero), rest, 1)
            base = owner * mlp_rows
            grad_gate = lax.dynamic_update_slice(
                grad_gate, jnp.concatenate([zero[:, :main], mid_gate, one[:, :main]], 1), (base, 0)
            )
            grad_up = lax.dynamic_update_slice(
                grad_up,
                jnp.concatenate([zero[:, main : 2 * main], mid_up, one[:, main : 2 * main]], 1),
                (base, 0),
            )

        grad_joint, grad_out_proj = grad_small[:, :qkv_cols], grad_small[:, qkv_cols:]

    small = net.total(jnp.concatenate([grad_gain_one, grad_gain_two, grad_bias], 1))[0]
    return (
        output[None],
        grad_input[None],
        grad_joint,
        small[2 * D :],
        grad_out_proj,
        small[:D],
        small[D : 2 * D],
        grad_gate,
        grad_up,
        grad_down,
    )


def solution(mesh):
    placed = (
        P("dp", "ctx", None),
        P("dp", None),
        P(),
        P("dp", None),
        P(),
        P(),
        P(None, "dp"),
        P(None, "dp"),
        P("dp", None),
        P("dp", "ctx", None),
    )
    return jax.shard_map(
        local,
        mesh=mesh,
        in_specs=placed,
        out_specs=(
            P("dp", "ctx", None),
            P("dp", "ctx", None),
            P("dp", None),
            P(),
            P("dp", None),
            P(),
            P(),
            P(None, "dp"),
            P(None, "dp"),
            P("dp", None),
        ),
        check_vma=False,
    )
```

```python
import jax
import jax.numpy as jnp
from jax import lax
from jax.experimental import pallas as pl
from jax.experimental.pallas import tpu as pltpu
from jax.sharding import PartitionSpec as P

D = 896
QH = 14
KH = 2
HD = 64
GROUP = QH // KH
WIDTH_Q = QH * HD
WIDTH_K = KH * HD

EPS = 1e-06
ROPE_BASE = 1000000.0

f32 = jnp.float32
bf16 = jnp.bfloat16


def ring_order(chips):
    if chips % 2:
        return list(range(chips))
    rows = chips // 2
    return [2 * i for i in range(rows)] + [2 * i + 1 for i in reversed(range(rows))]


def half_cut(rows):
    cut = (rows // 2 + 7) // 8 * 8
    return cut if cut < rows else rows // 2


class Net:
    def __init__(self):
        self.dp = lax.axis_size("dp")
        self.ctx = lax.axis_size("ctx")
        self.chips = self.ctx // 2
        self.order = ring_order(self.chips)
        self.d = lax.axis_index("dp")
        self.c = lax.axis_index("ctx")
        self.core = self.c % 2
        place = [0] * self.chips
        for spot, chip in enumerate(self.order):
            place[chip] = spot
        self.pos = jnp.array(place, jnp.int32)[self.c // 2]

    def swap(self, x):
        return lax.ppermute(x, "ctx", [(i, i ^ 1) for i in range(self.ctx)])

    def shift(self, x, step):
        n = self.dp
        return lax.ppermute(x, "dp", [(i, (i + step) % n) for i in range(n)])

    def hop(self, x, step):
        n = self.chips
        perm = []
        for spot in range(n):
            for core in range(2):
                perm.append((2 * self.order[spot] + core, 2 * self.order[(spot + step) % n] + core))
        return lax.ppermute(x, "ctx", perm)

    def owner(self, slot):
        return (self.pos - slot) % self.chips

    def group_gather(self, x):
        chip = jnp.concatenate([x] + [self.shift(x, s) for s in range(1, self.dp)], 0)
        return jnp.concatenate([chip, self.swap(chip)], 0)

    def ring_gather(self, x):
        n = self.chips
        half = n // 2
        cut = half_cut(x.shape[0])
        found = [x] + [None] * (n - 1)
        fwd, back = x, x
        for s in range(1, half):
            fwd = self.hop(fwd, 1)
            back = self.hop(back, -1)
            found[s] = fwd
            found[n - s] = back
        found[half] = jnp.concatenate([self.hop(fwd[:cut], 1), self.hop(back[cut:], -1)], 0)
        return found

    def ring_scatter(self, local):
        n = self.chips
        half = n // 2
        cut = half_cut(local[half].shape[0])

        def add(got, mine):
            return (got.astype(f32) + mine.astype(f32)).astype(bf16)

        fwd = self.hop(local[half][:cut], 1)
        back = self.hop(local[half][cut:], -1)
        for s in range(1, half):
            mine_f = local[half + s]
            mine_b = local[half - s]
            if s == 1:
                mine_f = jnp.concatenate([add(fwd, mine_f[:cut]), mine_f[cut:]], 0)
                mine_b = jnp.concatenate([mine_b[:cut], add(back, mine_b[cut:])], 0)
            else:
                mine_f = add(fwd, mine_f)
                mine_b = add(back, mine_b)
            fwd = self.hop(mine_f, 1)
            back = self.hop(mine_b, -1)
        return fwd.astype(f32) + back.astype(f32) + local[0].astype(f32)

    def full_rows(self, shard):
        rows = shard.shape[0]
        half = rows // 2
        piece = lax.dynamic_slice(shard, (self.core * half, 0), (half, shard.shape[1]))
        blocks = [shard]
        for s in range(1, self.dp):
            got = self.shift(piece, s)
            other = self.swap(got)
            low = jnp.where(self.core == 0, got, other)
            high = jnp.where(self.core == 0, other, got)
            blocks.append(jnp.concatenate([low, high], 0))
        if self.dp == 2:
            first = jnp.where(self.d == 0, blocks[0], blocks[1])
            second = jnp.where(self.d == 0, blocks[1], blocks[0])
            return jnp.concatenate([first, second], 0)
        ranked = jnp.stack(blocks)[(self.d - jnp.arange(self.dp)) % self.dp]
        return ranked.reshape(self.dp * rows, shard.shape[1])

    def total(self, x):
        x = x + self.swap(x)
        bit = 1
        while bit < self.chips:
            x = x + lax.ppermute(x, "ctx", [(i, i ^ (2 * bit)) for i in range(self.ctx)])
            bit *= 2
        bit = 1
        while bit < self.dp:
            x = x + lax.ppermute(x, "dp", [(i, i ^ bit) for i in range(self.dp)])
            bit *= 2
        return x

    def ring_parts(self, local):
        n = self.chips
        half = n // 2
        cut = half_cut(local[half].shape[0])

        def add(got, mine):
            return (got.astype(f32) + mine.astype(f32)).astype(bf16)

        fwd, back = self.hop(local[half][:cut], 1), self.hop(local[half][cut:], -1)
        for s in range(1, half):
            mine_f, mine_b = local[half + s], local[half - s]
            if s == 1:
                mine_f = jnp.concatenate([add(fwd, mine_f[:cut]), mine_f[cut:]], 0)
                mine_b = jnp.concatenate([mine_b[:cut], add(back, mine_b[cut:])], 0)
            else:
                mine_f, mine_b = add(fwd, mine_f), add(back, mine_b)
            fwd, back = self.hop(mine_f, 1), self.hop(mine_b, -1)
        return [local[0], fwd, back]

    def ring_sum(self, terms, stages):
        n = self.chips
        half = n // 2
        fwd, back = self.hop(terms[half], 1), self.hop(terms[half - 1], -1)

        def add(got, slot):
            return (got.astype(f32) + terms[slot].astype(f32)).astype(bf16)

        for s in range(1, half):
            fwd = add(fwd, half + s)
            if s < half - 1:
                back = add(back, half - 1 - s)
                stages[s - 1](fwd, back)
                fwd, back = self.hop(fwd, 1), self.hop(back, -1)
            else:
                stages[s - 1](fwd)
                fwd = self.hop(fwd, 1)
        return fwd, back

    def gather_placed(self, x, place):
        n = self.chips
        half = n // 2
        fwd = back = x
        placed = None
        waiting = ([0], [(x, self.swap(x))])
        for s in range(1, half + 1):
            if s > 1:
                placed, token = place(*waiting, placed)
                fwd, back = gate(token, fwd, back)
                waiting = ([s - 1, n - s + 1], [(fwd, self.swap(fwd)), (back, self.swap(back))])
            if s < half:
                fwd, back = self.hop(fwd, 1), self.hop(back, -1)
            else:
                cut = half_cut(fwd.shape[0])
                fwd, back = self.hop(fwd[:cut], 1), self.hop(back[cut:], -1)
        placed, token = place(*waiting, placed)
        far = join(fwd, back, token)
        return place([half], [(far, self.swap(far))], placed)[0]


VMEM_BYTES = 56 * 1024 * 1024
KEYS = 256
RING_ROWS = 152


def full_spec(shape):
    return pl.BlockSpec(shape, lambda: (0,) * len(shape))


def call(kernel, outs, args, smem=0, scratch=(), flops=0, loose=0):
    tight = len(args) - loose
    specs = [pl.BlockSpec(memory_space=pltpu.SMEM)] * smem
    specs += [pl.BlockSpec(memory_space=pltpu.VMEM)] * (tight - smem)
    specs += [pl.BlockSpec(memory_space=pl.ANY)] * loose

    def body(*refs):
        kernel(*refs[:tight], *refs[tight + loose :])

    moved = sum(x.size * x.dtype.itemsize for x in list(args) + list(outs))
    return pl.pallas_call(
        body,
        out_shape=list(outs),
        in_specs=specs,
        out_specs=[pl.BlockSpec(memory_space=pltpu.VMEM)] * len(outs),
        scratch_shapes=list(scratch),
        compiler_params=pltpu.CompilerParams(vmem_limit_bytes=VMEM_BYTES),
        cost_estimate=pl.CostEstimate(flops=flops, bytes_accessed=moved, transcendentals=0),
    )(*args)


def lanes(shape):
    return lax.broadcasted_iota(jnp.int32, shape, len(shape) - 1)


def dot_nt(a, b, precision=None):
    return lax.dot_general(
        a, b, (((1,), (1,)), ((), ())), preferred_element_type=f32, precision=precision
    )


def dot_tn(a, b):
    return lax.dot_general(a, b, (((0,), (0,)), ((), ())), preferred_element_type=f32)


def gate(token, *blocks):
    count = len(blocks)
    anywhere = pl.BlockSpec(memory_space=pl.ANY)

    def kernel(*refs):
        return None

    return pl.pallas_call(
        kernel,
        out_shape=[jax.ShapeDtypeStruct(x.shape, x.dtype) for x in blocks],
        in_specs=[anywhere] * (count + 1),
        out_specs=[anywhere] * count,
        input_output_aliases={i + 1: i for i in range(count)},
        cost_estimate=pl.CostEstimate(flops=0, bytes_accessed=1024, transcendentals=0),
    )(token, *blocks)


def join(first, second, token):
    cut = first.shape[0]

    def kernel(first_ref, second_ref, out_ref):
        out_ref[:cut, :] = first_ref[...]
        out_ref[cut:, :] = second_ref[...]

    shape = (cut + second.shape[0], first.shape[1])
    return call(
        kernel, [jax.ShapeDtypeStruct(shape, first.dtype)], [first, second, token], loose=1
    )[0]


def ring_end(fwd, back, terms, split):
    rows, columns = terms.shape[1:]

    def kernel(fwd_ref, back_ref, term_ref, first_ref, rest_ref):
        for ref, here in ((first_ref, slice(0, split)), (rest_ref, slice(split, rows))):
            total = fwd_ref[here, :].astype(f32) + back_ref[here, :].astype(f32)
            ref[...] = (total + term_ref[0, here, :].astype(f32)).astype(bf16)

    whole = pl.BlockSpec((rows, columns), lambda i: (0, 0))
    return pl.pallas_call(
        kernel,
        out_shape=[
            jax.ShapeDtypeStruct((split, columns), bf16),
            jax.ShapeDtypeStruct((rows - split, columns), bf16),
        ],
        grid=(1,),
        in_specs=[whole, whole, pl.BlockSpec((1, rows, columns), lambda i: (0, 0, 0))],
        out_specs=[
            pl.BlockSpec((split, columns), lambda i: (0, 0)),
            pl.BlockSpec((rows - split, columns), lambda i: (0, 0)),
        ],
        compiler_params=pltpu.CompilerParams(vmem_limit_bytes=VMEM_BYTES),
        cost_estimate=pl.CostEstimate(
            flops=0, bytes_accessed=8 * rows * columns, transcendentals=0
        ),
    )(fwd, back, terms)


def pair_kernel(mine_ref, got_ref, *out_refs):
    rows = out_refs[0].shape[0]
    for s, out_ref in enumerate(out_refs):
        here = slice(s * rows, (s + 1) * rows)
        out_ref[...] = (mine_ref[here, :] + got_ref[here, :].astype(f32)).astype(out_ref.dtype)


def block_kernel(mlp_ref, down_ref, *refs):
    small = refs[0][...].astype(f32)
    for ref in refs[1:-1]:
        small = small + ref[...].astype(f32)
    out_ref = refs[-1]
    top = mlp_ref.shape[0]
    piece = small.shape[0]
    out_ref[:top, :] = mlp_ref[...]
    out_ref[top : top + piece, :] = small.astype(bf16)
    out_ref[top + piece :, :] = down_ref[...]


def qkv_kernel(x_ref, gain_ref, w_ref, b_ref, cos_ref, sin_ref, norm_ref, q_ref, pair_ref):
    x = x_ref[...].astype(f32)
    inverse = lax.rsqrt(jnp.mean(x * x, -1, keepdims=True) + EPS)
    normed = (x * inverse * gain_ref[...]).astype(bf16)
    norm_ref[...] = normed
    joint = jnp.dot(normed, w_ref[...], preferred_element_type=f32) + b_ref[...]
    cosine = cos_ref[...]
    sine = sin_ref[...]
    early = lanes(cosine.shape) % HD < HD // 2
    for i in range((WIDTH_Q + WIDTH_K) // 128):
        tile = joint[:, i * 128 : (i + 1) * 128]
        turned = jnp.where(early, -pltpu.roll(tile, 96, 1), pltpu.roll(tile, 32, 1))
        turned = tile * cosine + turned * sine
        if i * 128 < WIDTH_Q:
            q_ref[:, i * 128 : (i + 1) * 128] = turned.astype(bf16)
        else:
            pair_ref[:, :WIDTH_K] = turned.astype(bf16)
    pair_ref[:, WIDTH_K:] = joint[:, WIDTH_Q + WIDTH_K :].astype(bf16)


def spread_heads(x, out_ref, factor):
    rows = x.shape[0]
    half = rows // 2
    for head in range(QH):
        kh, g = divmod(head, GROUP)
        tile = x[:, (head // 2) * 128 : (head // 2 + 1) * 128].astype(f32)
        if head % 2 != kh:
            tile = pltpu.roll(tile, HD, 1)
        tile = jnp.where(lanes(tile.shape) // HD == kh, tile * factor, 0.0).astype(out_ref.dtype)
        for part in range(2):
            start = (part * GROUP + g) * half
            out_ref[kh, start : start + half, :] = tile[part * half : (part + 1) * half]


def join_heads(src_ref, half, tile):
    sides = []
    for side in range(2):
        kh, g = divmod(2 * tile + side, GROUP)
        parts = [
            src_ref[kh, (part * GROUP + g) * half : (part * GROUP + g + 1) * half, :]
            for part in range(2)
        ]
        both = jnp.concatenate(parts, 0)
        sides.append(both if side == kh else pltpu.roll(both, HD, 1))
    return jnp.where(lanes(sides[0].shape) < HD, sides[0], sides[1])


def forward_kernel(
    ctx, meta_ref, q_ref, mine_ref, other_ref, x_ref, w_ref, gain_ref,
    low_ref, o_ref, lse_ref, spread_ref, k_ref, v_ref, hidden_ref, normed_ref,
    s_ref, max_ref, sum_ref,
):
    rows = q_ref.shape[0]
    half = rows // 2
    part_rows = GROUP * half
    me = meta_ref[0]
    chips = ctx // 2
    for j in range(ctx):
        src = mine_ref if j < chips else other_ref
        at = (j % chips) * rows
        owner = meta_ref[1 + j]
        for part in range(2):
            place = owner if part == 0 else 2 * ctx - 1 - owner
            to = pl.ds(pl.multiple_of(place * half, half), half)
            block = src[at + part * half : at + (part + 1) * half, :]
            k_ref[to, :] = block[:, :WIDTH_K]
            v_ref[to, :] = block[:, WIDTH_K:]
    spread_heads(q_ref[...], spread_ref, HD ** (-0.5))
    for part in range(2):
        span = slice(part * part_rows, (part + 1) * part_rows)
        start = (me if part == 0 else 2 * ctx - 1 - me) * half
        last = start // KEYS

        def keys_of(ref, i):
            return ref[pl.ds(pl.multiple_of(i * KEYS, KEYS), KEYS), :]

        for kh in range(KH):
            scores = dot_nt(spread_ref[kh, span, :], keys_of(k_ref, last))
            row = lax.broadcasted_iota(jnp.int32, scores.shape, 0) % half + start
            scores = jnp.where(lanes(scores.shape) + last * KEYS <= row, scores, -1e30)
            s_ref[kh, last] = scores
            max_ref[kh] = jnp.maximum(scores[:, :128], scores[:, 128:])

        def score(i, carry):
            for kh in range(KH):
                s = dot_nt(spread_ref[kh, span, :], keys_of(k_ref, i))
                s_ref[kh, i] = s
                max_ref[kh] = jnp.maximum(max_ref[kh], jnp.maximum(s[:, :128], s[:, 128:]))
            return carry

        lax.fori_loop(0, last, score, 0)
        for kh in range(KH):
            top = jnp.max(max_ref[kh], -1, keepdims=True)
            max_ref[kh] = jnp.broadcast_to(top, (part_rows, 128))
            sum_ref[kh] = jnp.zeros((part_rows, 128), f32)
            o_ref[kh, span, :] = jnp.zeros((part_rows, 128), f32)

        def weigh(i, carry):
            for kh in range(KH):
                s = s_ref[kh, i]
                top = max_ref[kh]
                left = jnp.exp(s[:, :128] - top)
                right = jnp.exp(s[:, 128:] - top)
                sum_ref[kh] += left + right
                o_ref[kh, span, :] += jnp.dot(
                    jnp.concatenate([left, right], 1).astype(bf16),
                    keys_of(v_ref, i),
                    preferred_element_type=f32,
                )
            return carry

        lax.fori_loop(0, last + 1, weigh, 0)
        for kh in range(KH):
            total = jnp.sum(sum_ref[kh], -1, keepdims=True)
            o_ref[kh, span, :] = o_ref[kh, span, :] / total
            lse_ref[kh, part] = dot_nt(
                jnp.full((8, 128), 1.0 / 128, f32),
                max_ref[kh] + jnp.log(total),
                lax.Precision.HIGHEST,
            )
    for tile in range(WIDTH_Q // 128):
        low_ref[:, tile * 128 : (tile + 1) * 128] = join_heads(o_ref, half, tile).astype(bf16)
    hidden = x_ref[...].astype(f32) + jnp.dot(low_ref[...], w_ref[...], preferred_element_type=f32)
    hidden_ref[...] = hidden
    inverse = lax.rsqrt(jnp.mean(hidden * hidden, -1, keepdims=True) + EPS)
    normed_ref[...] = (hidden * inverse * gain_ref[...]).astype(bf16)


def backward_kernel(
    ctx, meta_ref, gn_ref, hidden_ref, gout_ref, gain_ref, w_ref, spread_ref, k_ref, v_ref, lse_ref,
    o_ref,
    gh_ref, ga_ref, gain_grad_ref, gq_ref, mine_ref, other_ref,
    go_ref, gqs_ref, gk_ref, gv_ref,
):
    rows = gn_ref.shape[0]
    half = rows // 2
    part_rows = GROUP * half
    me = meta_ref[0]
    chips = ctx // 2
    hidden = hidden_ref[...]
    inverse = lax.rsqrt(jnp.mean(hidden * hidden, -1, keepdims=True) + EPS)
    unit = hidden * inverse
    grad = gn_ref[...]
    gain_grad_ref[...] = jnp.sum(grad * unit, 0, keepdims=True)
    scaled = grad * gain_ref[...]
    gh = gout_ref[...].astype(f32) + inverse * (
        scaled - unit * jnp.mean(scaled * unit, -1, keepdims=True)
    )
    gh_ref[...] = gh
    ga = gh.astype(bf16)
    ga_ref[...] = ga
    spread_heads(dot_nt(ga, w_ref[...]).astype(bf16), go_ref, 1.0)
    gqs_ref[...] = jnp.zeros_like(gqs_ref)
    gk_ref[...] = jnp.zeros_like(gk_ref)
    gv_ref[...] = jnp.zeros_like(gv_ref)
    for part in range(2):
        span = slice(part * part_rows, (part + 1) * part_rows)
        start = (me if part == 0 else 2 * ctx - 1 - me) * half
        last = start // KEYS
        deltas = [
            dot_nt(
                jnp.ones((8, 128), f32),
                go_ref[kh, span, :].astype(f32) * o_ref[kh, span, :],
                lax.Precision.HIGHEST,
            )[:1]
            for kh in range(KH)
        ]

        def step(i, masked):
            at = pl.ds(pl.multiple_of(i * KEYS, KEYS), KEYS)
            keys = k_ref[at, :]
            grad_k = gk_ref[at, :]
            grad_v = gv_ref[at, :]
            for kh in range(KH):
                queries = spread_ref[kh, span, :]
                heads = go_ref[kh, span, :]
                p = jnp.exp(dot_nt(keys, queries) - lse_ref[kh, part][:1])
                if masked:
                    row = lanes(p.shape) % half + start
                    key = lax.broadcasted_iota(jnp.int32, p.shape, 0) + i * KEYS
                    p = jnp.where(key <= row, p, 0.0)
                gs = (p * (dot_nt(v_ref[at, :], heads) - deltas[kh])).astype(bf16)
                grad_v += jnp.dot(p.astype(bf16), heads, preferred_element_type=f32)
                grad_k += jnp.dot(gs, queries, preferred_element_type=f32)
                gqs_ref[kh, span, :] += dot_tn(gs, keys)
            gk_ref[at, :] = grad_k
            gv_ref[at, :] = grad_v

        def body(i, carry):
            step(i, False)
            return carry

        lax.fori_loop(0, last, body, 0)
        step(last, True)
    for tile in range(WIDTH_Q // 128):
        gq_ref[:, tile * 128 : (tile + 1) * 128] = join_heads(gqs_ref, half, tile) * HD ** (-0.5)
    for j in range(ctx):
        dst = mine_ref if j < chips else other_ref
        at = (j % chips) * rows
        owner = meta_ref[1 + j]
        for part in range(2):
            place = owner if part == 0 else 2 * ctx - 1 - owner
            frm = pl.ds(pl.multiple_of(place * half, half), half)
            to = slice(at + part * half, at + (part + 1) * half)
            dst[to, :WIDTH_K] = gk_ref[frm, :].astype(dst.dtype)
            dst[to, WIDTH_K:] = gv_ref[frm, :].astype(dst.dtype)


def finish_kernel(
    gq_ref, x_ref, gain_ref, w_ref, cos_ref, sin_ref, gh_ref, gain_two_ref, *refs
):
    sent_ref, gx_ref, gain_grad_ref, bias_ref = refs[-4:]
    pair = refs[0][...]
    for ref in refs[1:-4]:
        pair = pair + ref[...].astype(f32)
    rows = pair.shape[0]
    joint_ref = sent_ref.at[:rows, :]
    cosine = cos_ref[...]
    sine = sin_ref[...]
    early = lanes(cosine.shape) % HD < HD // 2
    for i in range((WIDTH_Q + WIDTH_K) // 128):
        at = slice(i * 128, (i + 1) * 128)
        grad = gq_ref[:, at] if i * 128 < WIDTH_Q else pair[:, :WIDTH_K]
        scaled = grad * sine
        turned = jnp.where(early, pltpu.roll(scaled, 96, 1), -pltpu.roll(scaled, 32, 1))
        joint_ref[:, at] = (grad * cosine + turned).astype(bf16)
    joint_ref[:, WIDTH_Q + WIDTH_K :] = pair[:, WIDTH_K:].astype(bf16)
    joint = joint_ref[...]
    bias = jnp.sum(joint.astype(f32), 0, keepdims=True)
    bias_ref[...] = bias
    grad = dot_nt(joint, w_ref[...])
    x = x_ref[...].astype(f32)
    inverse = lax.rsqrt(jnp.mean(x * x, -1, keepdims=True) + EPS)
    unit = x * inverse
    gain = jnp.sum(grad * unit, 0, keepdims=True)
    gain_grad_ref[...] = gain
    wide = [jnp.zeros((1, bias.shape[1] - gain.shape[1]), f32)]
    found = []
    for row in (jnp.concatenate([gain] + wide, 1), jnp.concatenate([gain_two_ref[...]] + wide, 1), bias):
        high = row.astype(bf16)
        found += [high.astype(f32), row - high.astype(f32)]
    found.append(jnp.zeros((sent_ref.shape[0] - rows - len(found), bias.shape[1]), f32))
    sent_ref[rows:, :] = jnp.concatenate(found, 0).astype(bf16)
    scaled = grad * gain_ref[...]
    gx_ref[...] = gh_ref[...] + inverse * (
        scaled - unit * jnp.mean(scaled * unit, -1, keepdims=True)
    )


def mlp_kernel(
    half_rows, spots_ref, x_ref, gy_ref, gate_a, gate_b, up_a, up_b, down_a, down_b,
    xt_ref, midt_ref, gg_ref, gu_ref, gx_ref, out_ref, send_ref,
    wg_all, wu_all, wd_all, mid_all, gg_all, gu_all,
):
    step = pl.program_id(0)
    here = pl.ds(pl.multiple_of(step * 256, 256), 256)
    wg = jnp.concatenate([gate_a[...], gate_b[...]], 1)
    wu = jnp.concatenate([up_a[...], up_b[...]], 1)
    wd = jnp.concatenate([down_a[...], down_b[...]], 0)
    wg_all[:, here] = wg
    wu_all[:, here] = wu
    wd_all[here, :] = wd
    core = spots_ref[1]
    column = lanes((1, 256)) + (step * 256 + spots_ref[2])
    own = (column < spots_ref[3]) == (core == 0)
    tokens = x_ref.shape[0]
    for r in range(0, tokens, 256):
        rows = slice(r, r + 256)
        x = x_ref[rows, :]
        gate = jnp.dot(x, wg, preferred_element_type=f32)
        up = jnp.dot(x, wu, preferred_element_type=f32)
        grad = jnp.where(own, dot_nt(gy_ref[rows, :], wd), 0.0)
        sigma = jax.nn.sigmoid(gate)
        active = gate * sigma
        middle = jnp.where(own, active * up, 0.0).astype(bf16)
        grad_gate = (grad * up * (sigma + active * (1.0 - sigma))).astype(bf16)
        grad_up = (grad * active).astype(bf16)
        midt_ref[:, rows] = middle.T
        gg_ref[rows, :] = grad_gate
        gu_ref[rows, :] = grad_up
        mid_all[rows, here] = middle
        gg_all[rows, here] = grad_gate
        gu_all[rows, here] = grad_up

    @pl.when(step == 0)
    def transpose():
        xt_ref[...] = x_ref[...].T

    @pl.when(step == pl.num_programs(0) - 1)
    def end():
        gx = dot_nt(gg_all[...], wg_all[...]) + dot_nt(gu_all[...], wu_all[...])
        gx_ref[...] = gx[:half_rows]
        send_ref[:half_rows] = gx[half_rows:].astype(bf16)
        out = jnp.dot(mid_all[...], wd_all[...], preferred_element_type=f32)
        out_ref[...] = out[:half_rows]
        send_ref[half_rows:] = out[half_rows:].astype(bf16)


def feed_forward(meta, x, gy, w_gate, w_up, w_down, width):
    tokens = x.shape[0]
    half = tokens // 2
    steps = width // 256
    tiles = width // 128 - 1

    def columns(j):
        return pl.BlockSpec((D, 128), lambda i, m: (0, m[1] * tiles + 2 * i + j))

    def rows(j):
        return pl.BlockSpec((128, D), lambda i, m: (m[1] * tiles + 2 * i + j, 0))

    whole = pl.BlockSpec((tokens, D), lambda i, m: (0, 0))
    halves = pl.BlockSpec((half, D), lambda i, m: (0, 0))
    tile = pl.BlockSpec((tokens, 256), lambda i, m: (0, i))
    hidden = jax.ShapeDtypeStruct((tokens, width), bf16)
    return pl.pallas_call(
        lambda *refs: mlp_kernel(half, *refs),
        out_shape=[
            jax.ShapeDtypeStruct((D, tokens), bf16),
            jax.ShapeDtypeStruct((width, tokens), bf16),
            hidden,
            hidden,
            jax.ShapeDtypeStruct((half, D), f32),
            jax.ShapeDtypeStruct((half, D), f32),
            jax.ShapeDtypeStruct((tokens, D), bf16),
        ],
        grid_spec=pltpu.PrefetchScalarGridSpec(
            num_scalar_prefetch=1,
            grid=(steps,),
            in_specs=[whole, whole, columns(0), columns(1), columns(0), columns(1), rows(0), rows(1)],
            out_specs=[
                pl.BlockSpec((D, tokens), lambda i, m: (0, 0)),
                pl.BlockSpec((256, tokens), lambda i, m: (i, 0)),
                tile,
                tile,
                halves,
                halves,
                whole,
            ],
            scratch_shapes=[pltpu.VMEM((D, width), bf16)] * 2
            + [pltpu.VMEM((width, D), bf16)]
            + [pltpu.VMEM((tokens, width), bf16)] * 3,
        ),
        compiler_params=pltpu.CompilerParams(vmem_limit_bytes=VMEM_BYTES),
        cost_estimate=pl.CostEstimate(
            flops=12 * tokens * width * D, bytes_accessed=6 * width * D, transcendentals=0
        ),
    )(meta, x, gy, w_gate, w_gate, w_up, w_up, w_down, w_down)


def mlp_grad_kernel(
    down_rows, main, meta_ref, xt_ref, gy_ref, midt_ref, gg_ref, gu_ref,
    out_ref, mlp_acc, down_acc,
):
    step = pl.program_id(0)
    core = meta_ref[1]
    at_main = pl.ds(pl.multiple_of(core * 128, 128), main)
    at_tile = pl.ds(pl.multiple_of((1 - core) * main, 128), 128)

    @pl.when(step == 0)
    def products():
        xt = xt_ref[...]
        mlp_acc[:, :main] = jnp.dot(
            xt, gg_ref[:, at_main], preferred_element_type=f32
        ).astype(bf16)
        mlp_acc[:, main : 2 * main] = jnp.dot(
            xt, gu_ref[:, at_main], preferred_element_type=f32
        ).astype(bf16)
        mixed = gg_ref[:, at_tile].astype(f32) + pltpu.roll(gu_ref[:, at_tile].astype(f32), 64, 1)
        mlp_acc[:, 2 * main :] = jnp.dot(
            xt, mixed.astype(bf16), preferred_element_type=f32
        ).astype(bf16)
        down_acc[...] = jnp.dot(midt_ref[...], gy_ref[...], preferred_element_type=f32)

    mlp_rows = mlp_acc.shape[0] // pl.num_programs(0)
    columns = mlp_acc.shape[1] // 128
    block = mlp_acc[pl.ds(pl.multiple_of(step * mlp_rows, 16), mlp_rows), :]
    for j in range(columns):
        for i in range(mlp_rows // 16):
            out_ref[0, j * 16 : (j + 1) * 16, i * 128 : (i + 1) * 128] = block[
                i * 16 : (i + 1) * 16, j * 128 : (j + 1) * 128
            ]
    first = pl.multiple_of(core * 64 + step * down_rows, 8)
    out_ref[0, columns * 16 :, :] = down_acc[pl.ds(first, down_rows), :].astype(bf16)


def mlp_gradients(meta, xt, gy, midt, gg, gu, chips, down_rows, main):
    tokens = gy.shape[0]
    columns = (2 * main + 128) // 128
    rows = columns * 16 + down_rows

    def whole(x):
        return pl.BlockSpec(x.shape, lambda i, m: (0, 0))

    return pl.pallas_call(
        lambda *refs: mlp_grad_kernel(down_rows, main, *refs),
        out_shape=jax.ShapeDtypeStruct((chips, rows, D), bf16),
        grid_spec=pltpu.PrefetchScalarGridSpec(
            num_scalar_prefetch=1,
            grid=(chips,),
            in_specs=[whole(x) for x in (xt, gy, midt, gg, gu)],
            out_specs=pl.BlockSpec((1, rows, D), lambda i, m: (m[4 + i], 0, 0)),
            scratch_shapes=[
                pltpu.VMEM((D, columns * 128), bf16),
                pltpu.VMEM((midt.shape[0], D), f32),
            ],
        ),
        compiler_params=pltpu.CompilerParams(vmem_limit_bytes=VMEM_BYTES),
        cost_estimate=pl.CostEstimate(
            flops=6 * tokens * midt.shape[0] * D, bytes_accessed=4 * chips * rows * D,
            transcendentals=0,
        ),
    )(meta, xt, gy, midt, gg, gu)


def small_grad_kernel(
    chips, q_rows, rows, meta_ref, norm_ref, joint_ref, att_ref, ga_ref, *refs
):
    out_refs, acc, sums_ref = refs[:-2], refs[-2], refs[-1]
    cols = joint_ref.shape[1]
    blocks = joint_ref.shape[0] // (rows + 16)
    tokens = [joint_ref[b * (rows + 16) : b * (rows + 16) + rows, :] for b in range(blocks)]
    sums = []
    for b in range(blocks):
        found = joint_ref[b * (rows + 16) + rows : (b + 1) * (rows + 16), :].astype(f32)
        sums.append([found[2 * i : 2 * i + 1] + found[2 * i + 1 : 2 * i + 2] for i in range(3)])
    sums = [(sums[0][i] + sums[1][i]) + (sums[2][i] + sums[3][i]) for i in range(3)]
    sums_ref[...] = jnp.zeros_like(sums_ref)
    sums_ref[:1, :D] = sums[0][:, :D]
    sums_ref[:1, D : 2 * D] = sums[1][:, :D]
    sums_ref[:1, 2 * D : 2 * D + cols] = sums[2]
    acc[:, :cols] = dot_tn(norm_ref[...], jnp.concatenate(tokens, 0))
    acc[:, cols:] = dot_tn(att_ref[...], ga_ref[...])
    first = pl.multiple_of((2 * meta_ref[0] + meta_ref[1]) * q_rows, 16)
    width = acc.shape[1] // chips
    share = sums_ref.shape[1] // chips
    for out_ref, slot in zip(out_refs, range(chips)):
        owner = meta_ref[12 + slot]
        block = acc[pl.ds(first, q_rows), pl.ds(pl.multiple_of(owner * width, 128), width)]
        tall = jnp.concatenate(
            [block[:, i * 128 : (i + 1) * 128] for i in range(width // 128)], 0
        ).astype(bf16)
        piece = out_ref.shape[0] - 16
        for i in range(D // 128):
            out_ref[:piece, i * 128 : (i + 1) * 128] = tall[i * piece : (i + 1) * piece]
        vector = sums_ref[:, pl.ds(pl.multiple_of(owner * share, 128), share)]
        out_ref[piece:, :] = jnp.zeros((16, D), bf16)
        out_ref[piece:, :share] = jnp.concatenate([vector, vector], 0).astype(bf16)


def place_all(meta, slots, pairs, old, sizes):
    main, ff_loc, q_rows, cols, down_rows, chips = sizes
    mlp_rows = D // chips
    columns = (2 * main + 128) // 128
    tiles = main // 128
    lanes_out = D // 128
    top = columns * 16
    blocks = [x for pair in pairs for x in pair]
    count = len(blocks)
    piece = blocks[0].shape[0] - top - down_rows - 16
    share = 3 * 128
    parts = (cols + D) // chips // 128
    keep = [] if old is None else list(old)

    def kernel(meta_ref, *refs):
        ins = refs[:count]
        gate_out, up_out, down_out, joint_out, proj_out, sums_out, token_ref = refs[
            count + len(keep) : count + len(keep) + 7
        ]
        gate_buf, up_buf, down_buf, small_buf, sums_buf, sems, small_sems = refs[
            count + len(keep) + 7 :
        ]
        core_zero = meta_ref[1] == 0
        copies = []

        def send(src, dst, sem):
            copy = pltpu.make_async_copy(src, dst, sem)
            copy.start()
            copies.append(copy)

        def column(ref, j):
            found = [
                ref[j * 16 : (j + 1) * 16, i * 128 : (i + 1) * 128] for i in range(mlp_rows // 16)
            ]
            return jnp.concatenate(found, 0).astype(f32)

        for k, slot in enumerate(slots):
            for j in range(columns):
                got = column(ins[2 * k], j)
                other = column(ins[2 * k + 1], j)
                zero = jnp.where(core_zero, got, other)
                one = jnp.where(core_zero, other, got)
                if j < 2 * tiles:
                    buf = gate_buf if j < tiles else up_buf
                    at = (j % tiles) * 128
                    buf[k, :, at : at + 128] = zero
                    buf[k, :, at + main + 128 : at + main + 256] = one
                else:
                    left = lanes(zero.shape) < 64
                    gate_buf[k, :, main : main + 128] = jnp.where(left, zero, one)
                    up_buf[k, :, main : main + 128] = pltpu.roll(jnp.where(left, one, zero), 64, 1)
            owner = meta_ref[12 + slot]
            here = pl.ds(pl.multiple_of(owner * mlp_rows, 8), mlp_rows)
            send(gate_buf.at[k], gate_out.at[here, :], sems.at[5 * k])
            send(up_buf.at[k], up_out.at[here, :], sems.at[5 * k + 1])
            sums_buf[k] = ins[2 * k][top + piece : top + piece + 16, :share].astype(f32)[:8]
            here = pl.ds(pl.multiple_of(owner * 8, 8), 8)
            send(sums_buf.at[k], sums_out.at[here, :], sems.at[5 * k + 4])
            for side in range(2):
                b = 2 * k + side
                core = meta_ref[1] if side == 0 else 1 - meta_ref[1]
                down_buf[b] = ins[b][top + piece + 16 :, :].astype(f32)
                here = pl.ds(pl.multiple_of((core * chips + owner) * down_rows, 8), down_rows)
                send(down_buf.at[b], down_out.at[here, :], sems.at[5 * k + 2 + side])
                tall = jnp.concatenate(
                    [ins[b][top : top + piece, i * 128 : (i + 1) * 128] for i in range(lanes_out)], 0
                ).astype(f32)
                rows = pl.ds(pl.multiple_of(core * q_rows, 8), q_rows)
                for i in range(parts):
                    small_buf[b, i] = tall[i * q_rows : (i + 1) * q_rows]
                    block = owner * parts + i

                    @pl.when(block < cols // 128)
                    def joint(b=b, i=i, rows=rows, block=block):
                        at = pl.ds(pl.multiple_of(block * 128, 128), 128)
                        pltpu.make_async_copy(
                            small_buf.at[b, i], joint_out.at[rows, at], small_sems.at[b, i]
                        ).start()

                    @pl.when(block >= cols // 128)
                    def proj(b=b, i=i, rows=rows, block=block):
                        at = pl.ds(pl.multiple_of((block - cols // 128) * 128, 128), 128)
                        pltpu.make_async_copy(
                            small_buf.at[b, i], proj_out.at[rows, at], small_sems.at[b, i]
                        ).start()

        token_ref[...] = jnp.zeros(token_ref.shape, f32)
        for copy in copies:
            copy.wait()
        for b in range(count):
            for i in range(parts):
                pltpu.make_async_copy(
                    small_buf.at[b, i],
                    proj_out.at[pl.ds(0, q_rows), pl.ds(0, 128)],
                    small_sems.at[b, i],
                ).wait()

    anywhere = pl.BlockSpec(memory_space=pl.ANY)
    result = pl.pallas_call(
        kernel,
        out_shape=[
            jax.ShapeDtypeStruct((D, ff_loc), f32),
            jax.ShapeDtypeStruct((D, ff_loc), f32),
            jax.ShapeDtypeStruct((ff_loc, D), f32),
            jax.ShapeDtypeStruct((2 * q_rows, cols), f32),
            jax.ShapeDtypeStruct((2 * q_rows, D), f32),
            jax.ShapeDtypeStruct((8 * chips, share), f32),
            jax.ShapeDtypeStruct((8, 128), f32),
        ],
        in_specs=[pl.BlockSpec(memory_space=pltpu.SMEM)]
        + [pl.BlockSpec(memory_space=pltpu.VMEM)] * count
        + [anywhere] * len(keep),
        out_specs=[anywhere] * 6 + [pl.BlockSpec(memory_space=pltpu.VMEM)],
        scratch_shapes=[
            pltpu.VMEM((len(slots), mlp_rows, ff_loc), f32),
            pltpu.VMEM((len(slots), mlp_rows, ff_loc), f32),
            pltpu.VMEM((count, down_rows, D), f32),
            pltpu.VMEM((count, parts, q_rows, 128), f32),
            pltpu.VMEM((len(slots), 8, share), f32),
            pltpu.SemaphoreType.DMA((5 * len(slots),)),
            pltpu.SemaphoreType.DMA((count, parts)),
        ],
        input_output_aliases={1 + count + i: i for i in range(len(keep))},
        compiler_params=pltpu.CompilerParams(vmem_limit_bytes=VMEM_BYTES),
        cost_estimate=pl.CostEstimate(
            flops=0, bytes_accessed=8 * sum(x.size for x in blocks), transcendentals=0
        ),
    )(meta, *blocks, *keep)
    return list(result[:6]), result[6]


def place_blocks(blocks, spots, out_shape, old=None):
    shape = blocks[0].shape
    count = len(blocks)
    if shape[0] % 8 or shape[1] % 128:
        out = jnp.zeros(out_shape, f32) if old is None else old
        for block, (i, j) in zip(blocks, spots):
            out = lax.dynamic_update_slice(
                out, block.astype(f32), (i * shape[0], j * shape[1])
            )
        return out

    def kernel(spots_ref, *refs):
        step = pl.program_id(0)
        out_ref = refs[-1]
        for i in range(count):

            @pl.when(step == i)
            def write(i=i):
                out_ref[...] = refs[i][...].astype(f32)

    keep = [] if old is None else [old]
    return pl.pallas_call(
        kernel,
        out_shape=jax.ShapeDtypeStruct(out_shape, f32),
        grid_spec=pltpu.PrefetchScalarGridSpec(
            num_scalar_prefetch=1,
            grid=(count,),
            in_specs=[pl.BlockSpec(shape, lambda i, spots: (0, 0))] * count
            + [pl.BlockSpec(memory_space=pl.ANY)] * len(keep),
            out_specs=pl.BlockSpec(shape, lambda i, spots: (spots[i, 0], spots[i, 1])),
        ),
        input_output_aliases={} if old is None else {count + 1: 0},
        compiler_params=pltpu.CompilerParams(vmem_limit_bytes=VMEM_BYTES),
    )(jnp.stack([jnp.stack(s) for s in spots]).astype(jnp.int32), *blocks, *keep)


def local(tokens, w_qkv, b_qkv, w_out, gain_attn, gain_mlp, w_gate, w_up, w_down, cotangent):
    net = Net()
    rows = tokens.shape[1]
    half_rows = rows // 2
    ctx_count = net.ctx
    core = net.core
    chips = net.chips
    part_rows = GROUP * half_rows
    x = tokens[0]
    gain_one = gain_attn[None]
    gain_two = gain_mlp[None]

    w_qkv_full = net.full_rows(w_qkv)

    ff_loc = w_gate.shape[1]
    ff_half = ff_loc // 2
    main = (ff_half // 128) * 128
    rest = ff_half - main
    width = main + 2 * rest
    first = core * main
    tiled = net.dp == 2 and 2 * rest == 128 and width % 256 == 0 and chips == 8 and ff_half == chips * RING_ROWS
    ring = jnp.arange(chips, dtype=jnp.int32)
    owners_of = (net.pos - ring) % chips
    spots = jnp.concatenate(
        [jnp.stack([net.d, core, first, jnp.int32(ff_half)]), owners_of, owners_of]
    ).astype(jnp.int32)

    row_ids = jnp.arange(half_rows, dtype=jnp.int32)
    place = jnp.concatenate(
        [net.c * half_rows + row_ids, (2 * ctx_count - 1 - net.c) * half_rows + row_ids]
    )
    freq = ROPE_BASE ** (-((jnp.arange(128) % (HD // 2)).astype(f32) * (2.0 / HD)))
    angle = place.astype(f32)[:, None] * freq[None, :]
    cosine, sine = jnp.cos(angle), jnp.sin(angle)
    normed_one, queries, pairs = call(
        qkv_kernel,
        [
            jax.ShapeDtypeStruct((rows, D), bf16),
            jax.ShapeDtypeStruct((rows, WIDTH_Q), bf16),
            jax.ShapeDtypeStruct((rows, 2 * WIDTH_K), bf16),
        ],
        [x, gain_one, w_qkv_full, b_qkv[None], cosine, sine],
        flops=2 * rows * D * 1152,
    )

    slots = net.ring_gather(pairs)
    mine = jnp.concatenate(slots, 0)
    other = net.swap(mine)
    order = jnp.array(net.order, jnp.int32)
    chip_ids = order[(net.pos - jnp.arange(chips, dtype=jnp.int32)) % chips]
    meta = jnp.concatenate([net.c[None], 2 * chip_ids + core, 2 * chip_ids + 1 - core])
    meta = meta.astype(jnp.int32)

    late_w, late_g, late_n, unused = lax.optimization_barrier((w_out, cotangent[0], normed_one, pairs))
    w_out_full = net.full_rows(late_w)
    early_group = net.group_gather(jnp.concatenate([late_g, late_n], 1))
    grad_out_group = early_group[:, :D]
    normed_one_group = early_group[:, D:]

    total_keys = rows * ctx_count
    padded = (KH, 2 * part_rows, 128)
    attended_low, attended, lse, spread, keys, values, hidden, normed_two = call(
        lambda *refs: forward_kernel(ctx_count, *refs),
        [
            jax.ShapeDtypeStruct((rows, WIDTH_Q), bf16),
            jax.ShapeDtypeStruct(padded, f32),
            jax.ShapeDtypeStruct((KH, 2, 8, part_rows), f32),
            jax.ShapeDtypeStruct(padded, bf16),
            jax.ShapeDtypeStruct((total_keys, WIDTH_K), bf16),
            jax.ShapeDtypeStruct((total_keys, WIDTH_K), bf16),
            jax.ShapeDtypeStruct((rows, D), f32),
            jax.ShapeDtypeStruct((rows, D), bf16),
        ],
        [meta, queries, mine, other, x, w_out_full, gain_two],
        smem=1,
        scratch=[
            pltpu.VMEM((KH, total_keys // KEYS, part_rows, KEYS), f32),
            pltpu.VMEM((KH, part_rows, 128), f32),
            pltpu.VMEM((KH, part_rows, 128), f32),
        ],
        flops=8 * KH * part_rows * total_keys * 128,
    )

    normed_two_group = net.group_gather(normed_two)
    chip_rows = net.dp * rows
    down_rows = ff_half // chips
    mlp_rows = D // chips
    if tiled:
        x_turned, mid_turned, gate_low, up_low, grad_mine, out_mine, sent = feed_forward(
            spots, normed_two_group, grad_out_group, w_gate, w_up, w_down, width
        )
    else:
        own_cols = (jnp.arange(width) + first < ff_half) == (core == 0)
        wg = lax.dynamic_slice(w_gate, (0, first), (D, width))
        wu = lax.dynamic_slice(w_up, (0, first), (D, width))
        wd = lax.dynamic_slice(w_down, (first, 0), (width, D))
        gate = jnp.dot(normed_two_group, wg, preferred_element_type=f32)
        upper = jnp.dot(normed_two_group, wu, preferred_element_type=f32)
        sigma = jax.nn.sigmoid(gate)
        activated = gate * sigma
        middle = jnp.where(own_cols, activated * upper, 0.0).astype(bf16)
        grad_middle = jnp.einsum("td,fd->tf", grad_out_group, wd, preferred_element_type=f32)
        slope = sigma * (1.0 + gate * (1.0 - sigma))
        grad_gate_low = jnp.where(own_cols, grad_middle * upper * slope, 0.0).astype(bf16)
        grad_up_low = jnp.where(own_cols, grad_middle * activated, 0.0).astype(bf16)

        grad_normed_two = jnp.einsum(
            "tf,df->td", grad_gate_low, wg, preferred_element_type=f32
        ) + jnp.einsum("tf,df->td", grad_up_low, wu, preferred_element_type=f32)
        mlp_out = jnp.dot(middle, wd, preferred_element_type=f32)
        grad_mine, out_mine = grad_normed_two[:chip_rows], mlp_out[:chip_rows]
        sent = jnp.concatenate([grad_normed_two[chip_rows:], mlp_out[chip_rows:]], 0).astype(bf16)
    swapped = net.swap(sent)
    grad_chip = grad_mine + swapped[:chip_rows].astype(f32)
    mlp_chip = out_mine + swapped[chip_rows:].astype(f32)
    grad_two = grad_chip[:rows]
    for s in range(1, net.dp):
        piece = grad_chip[s * rows : (s + 1) * rows].astype(bf16)
        grad_two = grad_two + net.shift(piece, net.dp - s).astype(f32)

    def attention_back():
        grad_hidden, grad_attn_low, grad_gain_two, grad_queries, terms_mine, terms_other = call(
            lambda *refs: backward_kernel(ctx_count, *refs),
            [
                jax.ShapeDtypeStruct((rows, D), f32),
                jax.ShapeDtypeStruct((rows, D), bf16),
                jax.ShapeDtypeStruct((1, D), f32),
                jax.ShapeDtypeStruct((rows, WIDTH_Q), f32),
                jax.ShapeDtypeStruct((chips * rows, 2 * WIDTH_K), f32),
                jax.ShapeDtypeStruct((chips * rows, 2 * WIDTH_K), bf16),
            ],
            [
                meta, grad_two, hidden, cotangent[0], gain_two, w_out_full, spread, keys, values, lse,
                attended,
            ],
            smem=1,
            scratch=[
                pltpu.VMEM(padded, bf16),
                pltpu.VMEM(padded, f32),
                pltpu.VMEM((total_keys, WIDTH_K), f32),
                pltpu.VMEM((total_keys, WIDTH_K), f32),
            ],
            flops=20 * KH * part_rows * total_keys * 128,
        )
        swapped_terms = net.swap(terms_other)

        def finish(wait_pairs=()):
            pair_sums = call(
                pair_kernel,
                [jax.ShapeDtypeStruct((rows, 2 * WIDTH_K), f32)]
                + [jax.ShapeDtypeStruct((rows, 2 * WIDTH_K), bf16)] * (chips - 1),
                [terms_mine, swapped_terms] + list(wait_pairs),
                loose=len(wait_pairs),
            )
            grad_pairs = net.ring_parts(pair_sums)

            def last(wait_finish=()):
                joint, grad_input, grad_gain_one, grad_bias = call(
                    finish_kernel,
                    [
                        jax.ShapeDtypeStruct((rows + 16, 1152), bf16),
                        jax.ShapeDtypeStruct((rows, D), f32),
                        jax.ShapeDtypeStruct((1, D), f32),
                        jax.ShapeDtypeStruct((1, 1152), f32),
                    ],
                    [grad_queries, x, gain_one, w_qkv_full, cosine, sine, grad_hidden, grad_gain_two]
                    + grad_pairs
                    + list(wait_finish),
                    flops=2 * rows * D * 1152,
                    loose=len(wait_finish),
                )
                return (grad_attn_low, grad_gain_two, joint, grad_input, grad_gain_one, grad_bias)

            return last

        return finish

    found = []
    steps = [attention_back()]
    if tiled:

        def pairs_stage(*blocks):
            steps.append(steps[0](blocks))

        def finish_stage(*blocks):
            found.extend(steps[1](blocks))

        def small_stage(*blocks):
            found.append(blocks)

        terms = mlp_gradients(
            spots, x_turned, grad_out_group, mid_turned, gate_low, up_low, chips, down_rows, main
        )
        fwd, back = net.ring_sum(terms, [pairs_stage, finish_stage, small_stage])
        wait_small = found.pop()
        sum_mlp, sum_down = ring_end(fwd, back, terms, terms.shape[1] - down_rows)
    else:
        part_down = jnp.einsum(
            "tf,td->fd", middle, grad_out_group, preferred_element_type=f32
        ).astype(bf16)
        part_down = lax.dynamic_slice(part_down, (core * rest, 0), (ff_half, D))

        def down_chunk(slot):
            return lax.dynamic_slice(part_down, (net.owner(slot) * down_rows, 0), (down_rows, D))

        sum_down = net.ring_scatter([down_chunk(s) for s in range(chips)]).astype(bf16)

        def split_main(x):
            left = (x[:, :main], x[:, main:])
            right = (x[:, 2 * rest :], x[:, : 2 * rest])
            return (
                jnp.where(core == 0, left[0], right[0]),
                jnp.where(core == 0, left[1], right[1]),
            )

        gate_main, gate_tile = split_main(grad_gate_low)
        up_main, up_tile = split_main(grad_up_low)
        packed = jnp.concatenate(
            [gate_main, up_main, gate_tile + jnp.roll(up_tile, rest, 1)], 1
        )
        part_mlp = jnp.einsum(
            "td,tf->df", normed_two_group, packed, preferred_element_type=f32
        ).astype(bf16)

        def mlp_chunk(slot):
            return lax.dynamic_slice(
                part_mlp, (net.owner(slot) * mlp_rows, 0), (mlp_rows, 2 * ff_half)
            )

        sum_mlp = net.ring_scatter([mlp_chunk(s) for s in range(chips)]).astype(bf16)
        sum_mlp = lax.optimization_barrier(sum_mlp)
        found.extend(steps[0]()())
    grad_attn_low, grad_gain_two, grad_joint_low, grad_input, grad_gain_one, grad_bias = found

    out_sum = mlp_chip[:rows]
    sent = jnp.concatenate([attended_low, grad_attn_low], 0)
    gathered = [sent]
    for s in range(1, net.dp):
        got = net.shift(
            jnp.concatenate([mlp_chip[s * rows : (s + 1) * rows].astype(bf16), sent], 0),
            net.dp - s,
        )
        out_sum = out_sum + got[:rows].astype(f32)
        gathered.append(got[rows:])
    output = (hidden + out_sum).astype(bf16)
    gathered = jnp.concatenate(gathered, 0)
    gathered = jnp.concatenate([gathered, net.swap(gathered)], 0).reshape(2 * net.dp, 2, rows, D)
    attended_group = gathered[:, 0].reshape(2 * net.dp * rows, D)
    grad_attn_group = gathered[:, 1].reshape(2 * net.dp * rows, D)

    q_rows = w_qkv.shape[0] // 2
    qkv_cols = w_qkv.shape[1]
    if not tiled:
        grad_joint_low = grad_joint_low[:rows]
    joint_group = net.group_gather(grad_joint_low)
    if tiled:
        piece = q_rows * (qkv_cols + D) // chips // D
        terms_small = call(
            lambda *refs: small_grad_kernel(chips, q_rows, rows, *refs),
            [jax.ShapeDtypeStruct((piece + 16, D), bf16)] * chips,
            [spots, normed_one_group, joint_group, attended_group, grad_attn_group, *wait_small],
            smem=1,
            loose=len(wait_small),
            scratch=[pltpu.VMEM((D, qkv_cols + D), f32), pltpu.VMEM((8, 3 * 128 * chips), f32)],
            flops=4 * chip_rows * D * (qkv_cols + D),
        )
        block = call(
            block_kernel,
            [jax.ShapeDtypeStruct((sum_mlp.shape[0] + piece + 16 + down_rows, D), bf16)],
            [sum_mlp, sum_down] + net.ring_parts(terms_small),
        )[0]
        sizes = (main, ff_loc, q_rows, qkv_cols, down_rows, chips)
        grad_gate, grad_up, grad_down, grad_joint, grad_out_proj, sums = net.gather_placed(
            block, lambda slots, pairs, old: place_all(spots, slots, pairs, old, sizes)
        )
        small = sums.reshape(chips, 8, 384)[:, 0].reshape(-1)[: 2 * D + qkv_cols]
    else:
        q_first = net.d * (2 * q_rows) + core * q_rows
        group_rows = 2 * net.dp * rows
        part_out = jnp.einsum(
            "tc,td->cd",
            lax.dynamic_slice(attended_group, (0, q_first), (group_rows, q_rows)),
            grad_attn_group,
            preferred_element_type=f32,
        )
        part_joint = jnp.einsum(
            "td,tc->dc",
            lax.dynamic_slice(normed_one_group, (0, q_first), (group_rows, q_rows)),
            joint_group,
            preferred_element_type=f32,
        )
        part_small = jnp.concatenate([part_joint, part_out], 1).astype(bf16)
        small_cols = part_small.shape[1] // chips

        def small_chunk(slot):
            return lax.dynamic_slice(part_small, (0, net.owner(slot) * small_cols), (q_rows, small_cols))

        sum_small = net.ring_scatter([small_chunk(s) for s in range(chips)]).astype(bf16)

        tall = jnp.concatenate(
            [sum_small[:, i * 128 : (i + 1) * 128] for i in range(small_cols // 128)], 0
        )
        piece = tall.shape[0] // (D // 128)
        wide = jnp.concatenate([tall[i * piece : (i + 1) * piece] for i in range(D // 128)], 1)
        both = lax.optimization_barrier(jnp.concatenate([sum_down, wide], 0))

        owners = [net.owner(s) for s in range(chips)]
        got_mlp = net.ring_gather(sum_mlp)
        got_both = net.ring_gather(both)
        pairs_mlp = [(got, net.swap(got)) for got in got_mlp]
        pairs_both = [(got, net.swap(got)) for got in got_both]

        down_blocks, down_spots, small_blocks, small_spots = [], [], [], []
        for owner, pair in zip(owners, pairs_both):
            for which, got in zip((core, 1 - core), pair):
                down_blocks.append(got[:down_rows])
                down_spots.append((which * chips + owner, jnp.int32(0)))
                wide = got[down_rows:]
                tall = jnp.concatenate([wide[:, i * 128 : (i + 1) * 128] for i in range(D // 128)], 0)
                small_blocks.append(
                    jnp.concatenate(
                        [tall[i * q_rows : (i + 1) * q_rows] for i in range(small_cols // 128)], 1
                    )
                )
                small_spots.append((which, owner))
        grad_down = place_blocks(down_blocks, down_spots, (ff_loc, D))
        grad_small = place_blocks(small_blocks, small_spots, (2 * q_rows, part_small.shape[1]))
        grad_gate = jnp.zeros((D, ff_loc), f32)
        grad_up = jnp.zeros((D, ff_loc), f32)
        left_lane = jnp.arange(2 * rest) < rest
        for owner, (got, swapped) in zip(owners, pairs_mlp):
            zero = jnp.where(core == 0, got, swapped).astype(f32)
            one = jnp.where(core == 0, swapped, got).astype(f32)
            tile_zero, tile_one = zero[:, 2 * main :], one[:, 2 * main :]
            mid_gate = jnp.where(left_lane, tile_zero, tile_one)
            mid_up = jnp.roll(jnp.where(left_lane, tile_one, tile_zero), rest, 1)
            base = owner * mlp_rows
            grad_gate = lax.dynamic_update_slice(
                grad_gate, jnp.concatenate([zero[:, :main], mid_gate, one[:, :main]], 1), (base, 0)
            )
            grad_up = lax.dynamic_update_slice(
                grad_up,
                jnp.concatenate([zero[:, main : 2 * main], mid_up, one[:, main : 2 * main]], 1),
                (base, 0),
            )

        grad_joint, grad_out_proj = grad_small[:, :qkv_cols], grad_small[:, qkv_cols:]
        small = net.total(jnp.concatenate([grad_gain_one, grad_gain_two, grad_bias], 1))[0]
    return (
        output[None],
        grad_input[None],
        grad_joint,
        small[2 * D :],
        grad_out_proj,
        small[:D],
        small[D : 2 * D],
        grad_gate,
        grad_up,
        grad_down,
    )


def solution(mesh):
    placed = (
        P("dp", "ctx", None),
        P("dp", None),
        P(),
        P("dp", None),
        P(),
        P(),
        P(None, "dp"),
        P(None, "dp"),
        P("dp", None),
        P("dp", "ctx", None),
    )
    return jax.shard_map(
        local,
        mesh=mesh,
        in_specs=placed,
        out_specs=(
            P("dp", "ctx", None),
            P("dp", "ctx", None),
            P("dp", None),
            P(),
            P("dp", None),
            P(),
            P(),
            P(None, "dp"),
            P(None, "dp"),
            P("dp", None),
        ),
        check_vma=False,
    )
```

```python
import jax
import jax.numpy as jnp
from jax import lax
from jax.experimental import pallas as pl
from jax.experimental.pallas import tpu as pltpu
from jax.sharding import PartitionSpec as P

D = 896
QH = 14
KH = 2
HD = 64
GROUP = QH // KH
WIDTH_Q = QH * HD
WIDTH_K = KH * HD

EPS = 1e-06
ROPE_BASE = 1000000.0

f32 = jnp.float32
bf16 = jnp.bfloat16


def ring_order(chips):
    if chips % 2:
        return list(range(chips))
    rows = chips // 2
    return [2 * i for i in range(rows)] + [2 * i + 1 for i in reversed(range(rows))]


def half_cut(rows):
    cut = (rows // 2 + 7) // 8 * 8
    return cut if cut < rows else rows // 2


class Net:
    def __init__(self):
        self.dp = lax.axis_size("dp")
        self.ctx = lax.axis_size("ctx")
        self.chips = self.ctx // 2
        self.order = ring_order(self.chips)
        self.d = lax.axis_index("dp")
        self.c = lax.axis_index("ctx")
        self.core = self.c % 2
        place = [0] * self.chips
        for spot, chip in enumerate(self.order):
            place[chip] = spot
        self.pos = jnp.array(place, jnp.int32)[self.c // 2]

    def swap(self, x):
        return lax.ppermute(x, "ctx", [(i, i ^ 1) for i in range(self.ctx)])

    def shift(self, x, step):
        n = self.dp
        return lax.ppermute(x, "dp", [(i, (i + step) % n) for i in range(n)])

    def hop(self, x, step):
        n = self.chips
        perm = []
        for spot in range(n):
            for core in range(2):
                perm.append((2 * self.order[spot] + core, 2 * self.order[(spot + step) % n] + core))
        return lax.ppermute(x, "ctx", perm)

    def owner(self, slot):
        return (self.pos - slot) % self.chips

    def group_parts(self, x):
        chip = jnp.concatenate([x] + [self.shift(x, s) for s in range(1, self.dp)], 0)
        return chip, self.swap(chip)

    def group_gather(self, x):
        return jnp.concatenate(self.group_parts(x), 0)

    def ring_gather(self, x):
        n = self.chips
        half = n // 2
        cut = half_cut(x.shape[0])
        found = [x] + [None] * (n - 1)
        fwd, back = x, x
        for s in range(1, half):
            fwd = self.hop(fwd, 1)
            back = self.hop(back, -1)
            found[s] = fwd
            found[n - s] = back
        found[half] = jnp.concatenate([self.hop(fwd[:cut], 1), self.hop(back[cut:], -1)], 0)
        return found

    def ring_scatter(self, local):
        n = self.chips
        half = n // 2
        cut = half_cut(local[half].shape[0])

        def add(got, mine):
            return (got.astype(f32) + mine.astype(f32)).astype(bf16)

        fwd = self.hop(local[half][:cut], 1)
        back = self.hop(local[half][cut:], -1)
        for s in range(1, half):
            mine_f = local[half + s]
            mine_b = local[half - s]
            if s == 1:
                mine_f = jnp.concatenate([add(fwd, mine_f[:cut]), mine_f[cut:]], 0)
                mine_b = jnp.concatenate([mine_b[:cut], add(back, mine_b[cut:])], 0)
            else:
                mine_f = add(fwd, mine_f)
                mine_b = add(back, mine_b)
            fwd = self.hop(mine_f, 1)
            back = self.hop(mine_b, -1)
        return fwd.astype(f32) + back.astype(f32) + local[0].astype(f32)

    def full_rows(self, shard):
        rows = shard.shape[0]
        half = rows // 2
        piece = lax.dynamic_slice(shard, (self.core * half, 0), (half, shard.shape[1]))
        blocks = [shard]
        for s in range(1, self.dp):
            got = self.shift(piece, s)
            other = self.swap(got)
            low = jnp.where(self.core == 0, got, other)
            high = jnp.where(self.core == 0, other, got)
            blocks.append(jnp.concatenate([low, high], 0))
        if self.dp == 2:
            first = jnp.where(self.d == 0, blocks[0], blocks[1])
            second = jnp.where(self.d == 0, blocks[1], blocks[0])
            return jnp.concatenate([first, second], 0)
        ranked = jnp.stack(blocks)[(self.d - jnp.arange(self.dp)) % self.dp]
        return ranked.reshape(self.dp * rows, shard.shape[1])

    def total(self, x):
        x = x + self.swap(x)
        bit = 1
        while bit < self.chips:
            x = x + lax.ppermute(x, "ctx", [(i, i ^ (2 * bit)) for i in range(self.ctx)])
            bit *= 2
        bit = 1
        while bit < self.dp:
            x = x + lax.ppermute(x, "dp", [(i, i ^ bit) for i in range(self.dp)])
            bit *= 2
        return x

    def ring_parts(self, local):
        n = self.chips
        half = n // 2
        cut = half_cut(local[half].shape[0])

        def add(got, mine):
            return (got.astype(f32) + mine.astype(f32)).astype(bf16)

        fwd, back = self.hop(local[half][:cut], 1), self.hop(local[half][cut:], -1)
        for s in range(1, half):
            mine_f, mine_b = local[half + s], local[half - s]
            if s == 1:
                mine_f = jnp.concatenate([add(fwd, mine_f[:cut]), mine_f[cut:]], 0)
                mine_b = jnp.concatenate([mine_b[:cut], add(back, mine_b[cut:])], 0)
            else:
                mine_f, mine_b = add(fwd, mine_f), add(back, mine_b)
            fwd, back = self.hop(mine_f, 1), self.hop(mine_b, -1)
        return [local[0], fwd, back]

    def ring_sum(self, terms, stages):
        n = self.chips
        half = n // 2
        fwd, back = self.hop(terms[half], 1), self.hop(terms[half - 1], -1)

        def add(got, slot):
            return (got.astype(f32) + terms[slot].astype(f32)).astype(bf16)

        for s in range(1, half):
            fwd = add(fwd, half + s)
            if s < half - 1:
                back = add(back, half - 1 - s)
                stages[s - 1](fwd, back)
                fwd, back = self.hop(fwd, 1), self.hop(back, -1)
            else:
                stages[s - 1](fwd)
                fwd = self.hop(fwd, 1)
        return fwd, back

    def gather_placed(self, x, place):
        n = self.chips
        half = n // 2
        fwd = back = x
        placed = None
        waiting = ([0], [(x, self.swap(x))])
        for s in range(1, half + 1):
            if s > 1:
                placed, token = place(*waiting, placed)
                fwd, back = gate(token, fwd, back)
                waiting = ([s - 1, n - s + 1], [(fwd, self.swap(fwd)), (back, self.swap(back))])
            if s < half:
                fwd, back = self.hop(fwd, 1), self.hop(back, -1)
            else:
                cut = half_cut(fwd.shape[0])
                fwd, back = self.hop(fwd[:cut], 1), self.hop(back[cut:], -1)
        placed, token = place(*waiting, placed)
        far = join(fwd, back, token)
        return place([half], [(far, self.swap(far))], placed)[0]


VMEM_BYTES = 56 * 1024 * 1024
KEYS = 256
RING_ROWS = 152


def full_spec(shape):
    return pl.BlockSpec(shape, lambda: (0,) * len(shape))


def call(kernel, outs, args, smem=0, scratch=(), flops=0, loose=0):
    tight = len(args) - loose
    specs = [pl.BlockSpec(memory_space=pltpu.SMEM)] * smem
    specs += [pl.BlockSpec(memory_space=pltpu.VMEM)] * (tight - smem)
    specs += [pl.BlockSpec(memory_space=pl.ANY)] * loose

    def body(*refs):
        kernel(*refs[:tight], *refs[tight + loose :])

    moved = sum(x.size * x.dtype.itemsize for x in list(args) + list(outs))
    return pl.pallas_call(
        body,
        out_shape=list(outs),
        in_specs=specs,
        out_specs=[pl.BlockSpec(memory_space=pltpu.VMEM)] * len(outs),
        scratch_shapes=list(scratch),
        compiler_params=pltpu.CompilerParams(vmem_limit_bytes=VMEM_BYTES),
        cost_estimate=pl.CostEstimate(flops=flops, bytes_accessed=moved, transcendentals=0),
    )(*args)


def lanes(shape):
    return lax.broadcasted_iota(jnp.int32, shape, len(shape) - 1)


def dot_nt(a, b, precision=None):
    return lax.dot_general(
        a, b, (((1,), (1,)), ((), ())), preferred_element_type=f32, precision=precision
    )


def dot_tn(a, b):
    return lax.dot_general(a, b, (((0,), (0,)), ((), ())), preferred_element_type=f32)


def gate(token, *blocks):
    count = len(blocks)
    anywhere = pl.BlockSpec(memory_space=pl.ANY)

    def kernel(*refs):
        return None

    return pl.pallas_call(
        kernel,
        out_shape=[jax.ShapeDtypeStruct(x.shape, x.dtype) for x in blocks],
        in_specs=[anywhere] * (count + 1),
        out_specs=[anywhere] * count,
        input_output_aliases={i + 1: i for i in range(count)},
        cost_estimate=pl.CostEstimate(flops=0, bytes_accessed=1024, transcendentals=0),
    )(token, *blocks)


def join(first, second, token):
    cut = first.shape[0]

    def kernel(first_ref, second_ref, out_ref):
        out_ref[:cut, :] = first_ref[...]
        out_ref[cut:, :] = second_ref[...]

    shape = (cut + second.shape[0], first.shape[1])
    return call(
        kernel, [jax.ShapeDtypeStruct(shape, first.dtype)], [first, second, token], loose=1
    )[0]


def ring_end(fwd, back, term, split):
    rows, columns = term.shape

    def kernel(fwd_ref, back_ref, term_ref, first_ref, rest_ref):
        for ref, here in ((first_ref, slice(0, split)), (rest_ref, slice(split, rows))):
            total = fwd_ref[here, :].astype(f32) + back_ref[here, :].astype(f32)
            ref[...] = (total + term_ref[here, :].astype(f32)).astype(bf16)

    outs = [
        jax.ShapeDtypeStruct((split, columns), bf16),
        jax.ShapeDtypeStruct((rows - split, columns), bf16),
    ]
    return call(kernel, outs, [fwd, back, term])


def pair_kernel(mine_ref, got_ref, *out_refs):
    rows = out_refs[0].shape[0]
    for s, out_ref in enumerate(out_refs):
        here = slice(s * rows, (s + 1) * rows)
        out_ref[...] = (mine_ref[here, :] + got_ref[here, :].astype(f32)).astype(out_ref.dtype)


def block_kernel(mlp_ref, down_ref, *refs):
    small = refs[0][...].astype(f32)
    for ref in refs[1:-1]:
        small = small + ref[...].astype(f32)
    out_ref = refs[-1]
    top = mlp_ref.shape[0]
    piece = small.shape[0]
    out_ref[:top, :] = mlp_ref[...]
    out_ref[top : top + piece, :] = small.astype(bf16)
    out_ref[top + piece :, :] = down_ref[...]


def qkv_kernel(x_ref, gain_ref, w_ref, b_ref, cos_ref, sin_ref, norm_ref, q_ref, pair_ref):
    x = x_ref[...].astype(f32)
    inverse = lax.rsqrt(jnp.mean(x * x, -1, keepdims=True) + EPS)
    normed = (x * inverse * gain_ref[...]).astype(bf16)
    norm_ref[...] = normed
    joint = jnp.dot(normed, w_ref[...], preferred_element_type=f32) + b_ref[...]
    cosine = cos_ref[...]
    sine = sin_ref[...]
    early = lanes(cosine.shape) % HD < HD // 2
    for i in range((WIDTH_Q + WIDTH_K) // 128):
        tile = joint[:, i * 128 : (i + 1) * 128]
        turned = jnp.where(early, -pltpu.roll(tile, 96, 1), pltpu.roll(tile, 32, 1))
        turned = tile * cosine + turned * sine
        if i * 128 < WIDTH_Q:
            q_ref[:, i * 128 : (i + 1) * 128] = turned.astype(bf16)
        else:
            pair_ref[:, :WIDTH_K] = turned.astype(bf16)
    pair_ref[:, WIDTH_K:] = joint[:, WIDTH_Q + WIDTH_K :].astype(bf16)


def spread_heads(x, out_ref, factor):
    rows = x.shape[0]
    half = rows // 2
    for head in range(QH):
        kh, g = divmod(head, GROUP)
        tile = x[:, (head // 2) * 128 : (head // 2 + 1) * 128].astype(f32)
        if head % 2 != kh:
            tile = pltpu.roll(tile, HD, 1)
        tile = jnp.where(lanes(tile.shape) // HD == kh, tile * factor, 0.0).astype(out_ref.dtype)
        for part in range(2):
            start = (part * GROUP + g) * half
            out_ref[kh, start : start + half, :] = tile[part * half : (part + 1) * half]


def join_heads(src_ref, half, tile):
    sides = []
    for side in range(2):
        kh, g = divmod(2 * tile + side, GROUP)
        parts = [
            src_ref[kh, (part * GROUP + g) * half : (part * GROUP + g + 1) * half, :]
            for part in range(2)
        ]
        both = jnp.concatenate(parts, 0)
        sides.append(both if side == kh else pltpu.roll(both, HD, 1))
    return jnp.where(lanes(sides[0].shape) < HD, sides[0], sides[1])


def forward_kernel(
    ctx, meta_ref, q_ref, mine_ref, other_ref, x_ref, w_ref, gain_ref,
    low_ref, o_ref, lse_ref, spread_ref, k_ref, v_ref, hidden_ref, normed_ref,
    s_ref, max_ref, sum_ref,
):
    rows = q_ref.shape[0]
    half = rows // 2
    part_rows = GROUP * half
    me = meta_ref[0]
    chips = ctx // 2
    for j in range(ctx):
        src = mine_ref if j < chips else other_ref
        at = (j % chips) * rows
        owner = meta_ref[1 + j]
        for part in range(2):
            place = owner if part == 0 else 2 * ctx - 1 - owner
            to = pl.ds(pl.multiple_of(place * half, half), half)
            block = src[at + part * half : at + (part + 1) * half, :]
            k_ref[to, :] = block[:, :WIDTH_K]
            v_ref[to, :] = block[:, WIDTH_K:]
    spread_heads(q_ref[...], spread_ref, HD ** (-0.5))
    for part in range(2):
        span = slice(part * part_rows, (part + 1) * part_rows)
        start = (me if part == 0 else 2 * ctx - 1 - me) * half
        last = start // KEYS

        def keys_of(ref, i):
            return ref[pl.ds(pl.multiple_of(i * KEYS, KEYS), KEYS), :]

        for kh in range(KH):
            scores = dot_nt(spread_ref[kh, span, :], keys_of(k_ref, last))
            row = lax.broadcasted_iota(jnp.int32, scores.shape, 0) % half + start
            scores = jnp.where(lanes(scores.shape) + last * KEYS <= row, scores, -1e30)
            s_ref[kh, last] = scores
            max_ref[kh] = jnp.maximum(scores[:, :128], scores[:, 128:])

        def score(i, carry):
            for kh in range(KH):
                s = dot_nt(spread_ref[kh, span, :], keys_of(k_ref, i))
                s_ref[kh, i] = s
                max_ref[kh] = jnp.maximum(max_ref[kh], jnp.maximum(s[:, :128], s[:, 128:]))
            return carry

        lax.fori_loop(0, last, score, 0)
        for kh in range(KH):
            top = jnp.max(max_ref[kh], -1, keepdims=True)
            max_ref[kh] = jnp.broadcast_to(top, (part_rows, 128))
            sum_ref[kh] = jnp.zeros((part_rows, 128), f32)
            o_ref[kh, span, :] = jnp.zeros((part_rows, 128), f32)

        def weigh(i, carry):
            for kh in range(KH):
                s = s_ref[kh, i]
                top = max_ref[kh]
                left = jnp.exp(s[:, :128] - top)
                right = jnp.exp(s[:, 128:] - top)
                sum_ref[kh] += left + right
                o_ref[kh, span, :] += jnp.dot(
                    jnp.concatenate([left, right], 1).astype(bf16),
                    keys_of(v_ref, i),
                    preferred_element_type=f32,
                )
            return carry

        lax.fori_loop(0, last + 1, weigh, 0)
        for kh in range(KH):
            total = jnp.sum(sum_ref[kh], -1, keepdims=True)
            o_ref[kh, span, :] = o_ref[kh, span, :] / total
            lse_ref[kh, part] = dot_nt(
                jnp.full((8, 128), 1.0 / 128, f32),
                max_ref[kh] + jnp.log(total),
                lax.Precision.HIGHEST,
            )
    for tile in range(WIDTH_Q // 128):
        low_ref[:, tile * 128 : (tile + 1) * 128] = join_heads(o_ref, half, tile).astype(bf16)
    hidden = x_ref[...].astype(f32) + jnp.dot(low_ref[...], w_ref[...], preferred_element_type=f32)
    hidden_ref[...] = hidden
    inverse = lax.rsqrt(jnp.mean(hidden * hidden, -1, keepdims=True) + EPS)
    normed_ref[...] = (hidden * inverse * gain_ref[...]).astype(bf16)


def backward_kernel(
    ctx, meta_ref, gn_ref, hidden_ref, gout_ref, gain_ref, w_ref, spread_ref, k_ref, v_ref, lse_ref,
    o_ref,
    gh_ref, ga_ref, gain_grad_ref, gq_ref, mine_ref, other_ref,
    go_ref, gqs_ref, gk_ref, gv_ref,
):
    rows = gn_ref.shape[0]
    half = rows // 2
    part_rows = GROUP * half
    me = meta_ref[0]
    chips = ctx // 2
    hidden = hidden_ref[...]
    inverse = lax.rsqrt(jnp.mean(hidden * hidden, -1, keepdims=True) + EPS)
    unit = hidden * inverse
    grad = gn_ref[...]
    gain_grad_ref[...] = jnp.sum(grad * unit, 0, keepdims=True)
    scaled = grad * gain_ref[...]
    gh = gout_ref[...].astype(f32) + inverse * (
        scaled - unit * jnp.mean(scaled * unit, -1, keepdims=True)
    )
    gh_ref[...] = gh
    ga = gh.astype(bf16)
    ga_ref[...] = ga
    spread_heads(dot_nt(ga, w_ref[...]).astype(bf16), go_ref, 1.0)
    gqs_ref[...] = jnp.zeros_like(gqs_ref)
    gk_ref[...] = jnp.zeros_like(gk_ref)
    gv_ref[...] = jnp.zeros_like(gv_ref)
    for part in range(2):
        span = slice(part * part_rows, (part + 1) * part_rows)
        start = (me if part == 0 else 2 * ctx - 1 - me) * half
        last = start // KEYS
        deltas = [
            dot_nt(
                jnp.ones((8, 128), f32),
                go_ref[kh, span, :].astype(f32) * o_ref[kh, span, :],
                lax.Precision.HIGHEST,
            )[:1]
            for kh in range(KH)
        ]

        def step(i, masked):
            at = pl.ds(pl.multiple_of(i * KEYS, KEYS), KEYS)
            keys = k_ref[at, :]
            grad_k = gk_ref[at, :]
            grad_v = gv_ref[at, :]
            for kh in range(KH):
                queries = spread_ref[kh, span, :]
                heads = go_ref[kh, span, :]
                p = jnp.exp(dot_nt(keys, queries) - lse_ref[kh, part][:1])
                if masked:
                    row = lanes(p.shape) % half + start
                    key = lax.broadcasted_iota(jnp.int32, p.shape, 0) + i * KEYS
                    p = jnp.where(key <= row, p, 0.0)
                gs = (p * (dot_nt(v_ref[at, :], heads) - deltas[kh])).astype(bf16)
                grad_v += jnp.dot(p.astype(bf16), heads, preferred_element_type=f32)
                grad_k += jnp.dot(gs, queries, preferred_element_type=f32)
                gqs_ref[kh, span, :] += dot_tn(gs, keys)
            gk_ref[at, :] = grad_k
            gv_ref[at, :] = grad_v

        def body(i, carry):
            step(i, False)
            return carry

        lax.fori_loop(0, last, body, 0)
        step(last, True)
    for tile in range(WIDTH_Q // 128):
        gq_ref[:, tile * 128 : (tile + 1) * 128] = join_heads(gqs_ref, half, tile) * HD ** (-0.5)
    for j in range(ctx):
        dst = mine_ref if j < chips else other_ref
        at = (j % chips) * rows
        owner = meta_ref[1 + j]
        for part in range(2):
            place = owner if part == 0 else 2 * ctx - 1 - owner
            frm = pl.ds(pl.multiple_of(place * half, half), half)
            to = slice(at + part * half, at + (part + 1) * half)
            dst[to, :WIDTH_K] = gk_ref[frm, :].astype(dst.dtype)
            dst[to, WIDTH_K:] = gv_ref[frm, :].astype(dst.dtype)


def finish_kernel(
    gq_ref, x_ref, gain_ref, w_ref, cos_ref, sin_ref, gh_ref, gain_two_ref, *refs
):
    sent_ref, gx_ref, gain_grad_ref, bias_ref = refs[-4:]
    pair = refs[0][...]
    for ref in refs[1:-4]:
        pair = pair + ref[...].astype(f32)
    rows = pair.shape[0]
    joint_ref = sent_ref.at[:rows, :]
    cosine = cos_ref[...]
    sine = sin_ref[...]
    early = lanes(cosine.shape) % HD < HD // 2
    for i in range((WIDTH_Q + WIDTH_K) // 128):
        at = slice(i * 128, (i + 1) * 128)
        grad = gq_ref[:, at] if i * 128 < WIDTH_Q else pair[:, :WIDTH_K]
        scaled = grad * sine
        turned = jnp.where(early, pltpu.roll(scaled, 96, 1), -pltpu.roll(scaled, 32, 1))
        joint_ref[:, at] = (grad * cosine + turned).astype(bf16)
    joint_ref[:, WIDTH_Q + WIDTH_K :] = pair[:, WIDTH_K:].astype(bf16)
    joint = joint_ref[...]
    bias = jnp.sum(joint.astype(f32), 0, keepdims=True)
    bias_ref[...] = bias
    grad = dot_nt(joint, w_ref[...])
    x = x_ref[...].astype(f32)
    inverse = lax.rsqrt(jnp.mean(x * x, -1, keepdims=True) + EPS)
    unit = x * inverse
    gain = jnp.sum(grad * unit, 0, keepdims=True)
    gain_grad_ref[...] = gain
    wide = [jnp.zeros((1, bias.shape[1] - gain.shape[1]), f32)]
    found = []
    for row in (jnp.concatenate([gain] + wide, 1), jnp.concatenate([gain_two_ref[...]] + wide, 1), bias):
        high = row.astype(bf16)
        found += [high.astype(f32), row - high.astype(f32)]
    found.append(jnp.zeros((sent_ref.shape[0] - rows - len(found), bias.shape[1]), f32))
    sent_ref[rows:, :] = jnp.concatenate(found, 0).astype(bf16)
    scaled = grad * gain_ref[...]
    gx_ref[...] = gh_ref[...] + inverse * (
        scaled - unit * jnp.mean(scaled * unit, -1, keepdims=True)
    )


def mlp_kernel(
    half_rows, spots_ref, x_a, x_b, gy_a, gy_b, gate_a, gate_b, up_a, up_b, down_a, down_b,
    xt_ref, midt_ref, gg_ref, gu_ref, gx_ref, out_ref, send_ref,
    x_all, gy_all, wg_all, wu_all, wd_all, mid_all, gg_all, gu_all,
):
    step = pl.program_id(0)

    @pl.when(step == 0)
    def start():
        x_all[:half_rows] = x_a[...]
        x_all[half_rows:] = x_b[...]
        gy_all[:half_rows] = gy_a[...]
        gy_all[half_rows:] = gy_b[...]
        xt_ref[...] = x_all[...].T

    here = pl.ds(pl.multiple_of(step * 256, 256), 256)
    wg = jnp.concatenate([gate_a[...], gate_b[...]], 1)
    wu = jnp.concatenate([up_a[...], up_b[...]], 1)
    wd = jnp.concatenate([down_a[...], down_b[...]], 0)
    wg_all[:, here] = wg
    wu_all[:, here] = wu
    wd_all[here, :] = wd
    core = spots_ref[1]
    column = lanes((1, 256)) + (step * 256 + spots_ref[2])
    own = (column < spots_ref[3]) == (core == 0)
    x = x_all[...]
    gate = jnp.dot(x, wg, preferred_element_type=f32)
    up = jnp.dot(x, wu, preferred_element_type=f32)
    grad = jnp.where(own, dot_nt(gy_all[...], wd), 0.0)
    sigma = jax.nn.sigmoid(gate)
    active = gate * sigma
    middle = jnp.where(own, active * up, 0.0).astype(bf16)
    grad_gate = (grad * up * (sigma + active * (1.0 - sigma))).astype(bf16)
    grad_up = (grad * active).astype(bf16)
    midt_ref[...] = middle.T
    gg_ref[...] = grad_gate
    gu_ref[...] = grad_up
    mid_all[:, here] = middle
    gg_all[:, here] = grad_gate
    gu_all[:, here] = grad_up

    @pl.when(step == pl.num_programs(0) - 1)
    def end():
        gx = dot_nt(gg_all[...], wg_all[...]) + dot_nt(gu_all[...], wu_all[...])
        gx_ref[...] = gx[:half_rows]
        send_ref[:half_rows] = gx[half_rows:].astype(bf16)
        out = jnp.dot(mid_all[...], wd_all[...], preferred_element_type=f32)
        out_ref[...] = out[:half_rows]
        send_ref[half_rows:] = out[half_rows:].astype(bf16)


def feed_forward(meta, x, early, w_gate, w_up, w_down, width):
    half = x[0].shape[0]
    tokens = 2 * half
    steps = width // 256
    tiles = width // 128 - 1

    def columns(j):
        return pl.BlockSpec((D, 128), lambda i, m: (0, m[1] * tiles + 2 * i + j))

    def rows(j):
        return pl.BlockSpec((128, D), lambda i, m: (m[1] * tiles + 2 * i + j, 0))

    whole = pl.BlockSpec((tokens, D), lambda i, m: (0, 0))
    halves = pl.BlockSpec((half, D), lambda i, m: (0, 0))
    tile = pl.BlockSpec((tokens, 256), lambda i, m: (0, i))
    hidden = jax.ShapeDtypeStruct((tokens, width), bf16)
    return pl.pallas_call(
        lambda *refs: mlp_kernel(half, *refs),
        out_shape=[
            jax.ShapeDtypeStruct((D, tokens), bf16),
            jax.ShapeDtypeStruct((width, tokens), bf16),
            hidden,
            hidden,
            jax.ShapeDtypeStruct((half, D), f32),
            jax.ShapeDtypeStruct((half, D), f32),
            jax.ShapeDtypeStruct((tokens, D), bf16),
        ],
        grid_spec=pltpu.PrefetchScalarGridSpec(
            num_scalar_prefetch=1,
            grid=(steps,),
            in_specs=[halves] * 4
            + [columns(0), columns(1), columns(0), columns(1), rows(0), rows(1)],
            out_specs=[
                pl.BlockSpec((D, tokens), lambda i, m: (0, 0)),
                pl.BlockSpec((256, tokens), lambda i, m: (i, 0)),
                tile,
                tile,
                halves,
                halves,
                whole,
            ],
            scratch_shapes=[pltpu.VMEM((tokens, D), bf16)] * 2
            + [pltpu.VMEM((D, width), bf16)] * 2
            + [pltpu.VMEM((width, D), bf16)]
            + [pltpu.VMEM((tokens, width), bf16)] * 3,
        ),
        compiler_params=pltpu.CompilerParams(vmem_limit_bytes=VMEM_BYTES),
        cost_estimate=pl.CostEstimate(
            flops=12 * tokens * width * D, bytes_accessed=6 * width * D, transcendentals=0
        ),
    )(meta, *x, *early, w_gate, w_gate, w_up, w_up, w_down, w_down)


def mlp_grad_kernel(chips, down_rows, main, meta_ref, xt_ref, gy_a, gy_b, midt_ref, gg_ref, gu_ref, *refs):
    out_refs = refs[:chips]
    mlp_acc, down_acc, blocks, sems = refs[chips:]
    core = meta_ref[1]
    at_main = pl.ds(pl.multiple_of(core * 128, 128), main)
    at_tile = pl.ds(pl.multiple_of((1 - core) * main, 128), 128)
    xt = xt_ref[...]
    mlp_acc[:, :main] = jnp.dot(xt, gg_ref[:, at_main], preferred_element_type=f32).astype(bf16)
    mlp_acc[:, main : 2 * main] = jnp.dot(
        xt, gu_ref[:, at_main], preferred_element_type=f32
    ).astype(bf16)
    mixed = gg_ref[:, at_tile].astype(f32) + pltpu.roll(gu_ref[:, at_tile].astype(f32), 64, 1)
    mlp_acc[:, 2 * main :] = jnp.dot(
        xt, mixed.astype(bf16), preferred_element_type=f32
    ).astype(bf16)
    gy = jnp.concatenate([gy_a[:, :D], gy_b[:, :D]], 0)
    down_acc[...] = jnp.dot(midt_ref[...], gy, preferred_element_type=f32)

    mlp_rows = mlp_acc.shape[0] // chips
    columns = mlp_acc.shape[1] // 128
    half = chips // 2
    copies = []
    for slot in sorted(range(chips), key=lambda s: abs(s - half) if s else chips):
        owner = meta_ref[12 + slot]
        block = mlp_acc[pl.ds(pl.multiple_of(owner * mlp_rows, 16), mlp_rows), :]
        for j in range(columns):
            for i in range(mlp_rows // 16):
                blocks[slot, j * 16 : (j + 1) * 16, i * 128 : (i + 1) * 128] = block[
                    i * 16 : (i + 1) * 16, j * 128 : (j + 1) * 128
                ]
        first = pl.multiple_of(core * 64 + owner * down_rows, 8)
        blocks[slot, columns * 16 :, :] = down_acc[pl.ds(first, down_rows), :].astype(bf16)
        copy = pltpu.make_async_copy(blocks.at[slot], out_refs[slot], sems.at[slot])
        copy.start()
        copies.append(copy)
    for copy in copies:
        copy.wait()


def mlp_gradients(meta, xt, early, midt, gg, gu, after, chips, down_rows, main):
    tokens = gg.shape[0]
    columns = (2 * main + 128) // 128
    rows = columns * 16 + down_rows
    args = [meta, xt, *early, midt, gg, gu]
    anywhere = pl.BlockSpec(memory_space=pl.ANY)

    def kernel(*refs):
        mlp_grad_kernel(chips, down_rows, main, *refs[: len(args)], *refs[len(args) + 1 :])

    return pl.pallas_call(
        kernel,
        out_shape=[jax.ShapeDtypeStruct((rows, D), bf16)] * chips,
        in_specs=[pl.BlockSpec(memory_space=pltpu.SMEM)]
        + [pl.BlockSpec(memory_space=pltpu.VMEM)] * (len(args) - 1)
        + [anywhere],
        out_specs=[anywhere] * chips,
        scratch_shapes=[
            pltpu.VMEM((D, columns * 128), bf16),
            pltpu.VMEM((midt.shape[0], D), f32),
            pltpu.VMEM((chips, rows, D), bf16),
            pltpu.SemaphoreType.DMA((chips,)),
        ],
        compiler_params=pltpu.CompilerParams(vmem_limit_bytes=VMEM_BYTES),
        cost_estimate=pl.CostEstimate(
            flops=6 * tokens * midt.shape[0] * D, bytes_accessed=4 * chips * rows * D,
            transcendentals=0,
        ),
    )(*args, after)


def small_grad_kernel(
    chips, q_rows, rows, meta_ref, norm_a, norm_b, joint_a, joint_b, near_a, near_b, *refs
):
    out_refs, acc, sums_ref = refs[:-2], refs[-2], refs[-1]
    cols = joint_a.shape[1]
    tokens, sums, attended, grads = [], [], [], []
    for joint_ref, near_ref in ((joint_a, near_a), (joint_b, near_b)):
        for b in range(2):
            at = b * (rows + 16)
            tokens.append(joint_ref[at : at + rows, :])
            found = joint_ref[at + rows : at + rows + 16, :].astype(f32)
            sums.append([found[2 * i : 2 * i + 1] + found[2 * i + 1 : 2 * i + 2] for i in range(3)])
            attended.append(near_ref[2 * b * rows : (2 * b + 1) * rows, :])
            grads.append(near_ref[(2 * b + 1) * rows : (2 * b + 2) * rows, :])
    norm = jnp.concatenate([norm_a[:, D:], norm_b[:, D:]], 0)
    sums = [(sums[0][i] + sums[1][i]) + (sums[2][i] + sums[3][i]) for i in range(3)]
    sums_ref[...] = jnp.zeros_like(sums_ref)
    sums_ref[:1, :D] = sums[0][:, :D]
    sums_ref[:1, D : 2 * D] = sums[1][:, :D]
    sums_ref[:1, 2 * D : 2 * D + cols] = sums[2]
    acc[:, :cols] = dot_tn(norm, jnp.concatenate(tokens, 0))
    acc[:, cols:] = dot_tn(jnp.concatenate(attended, 0), jnp.concatenate(grads, 0))
    first = pl.multiple_of((2 * meta_ref[0] + meta_ref[1]) * q_rows, 16)
    width = acc.shape[1] // chips
    share = sums_ref.shape[1] // chips
    for out_ref, slot in zip(out_refs, range(chips)):
        owner = meta_ref[12 + slot]
        block = acc[pl.ds(first, q_rows), pl.ds(pl.multiple_of(owner * width, 128), width)]
        tall = jnp.concatenate(
            [block[:, i * 128 : (i + 1) * 128] for i in range(width // 128)], 0
        ).astype(bf16)
        piece = out_ref.shape[0] - 16
        for i in range(D // 128):
            out_ref[:piece, i * 128 : (i + 1) * 128] = tall[i * piece : (i + 1) * piece]
        vector = sums_ref[:, pl.ds(pl.multiple_of(owner * share, 128), share)]
        out_ref[piece:, :] = jnp.zeros((16, D), bf16)
        out_ref[piece:, :share] = jnp.concatenate([vector, vector], 0).astype(bf16)


def place_all(meta, slots, pairs, old, sizes):
    main, ff_loc, q_rows, cols, down_rows, chips = sizes
    mlp_rows = D // chips
    columns = (2 * main + 128) // 128
    tiles = main // 128
    lanes_out = D // 128
    top = columns * 16
    blocks = [x for pair in pairs for x in pair]
    count = len(blocks)
    piece = blocks[0].shape[0] - top - down_rows - 16
    share = 3 * 128
    parts = (cols + D) // chips // 128
    keep = [] if old is None else list(old)

    def kernel(meta_ref, *refs):
        ins = refs[:count]
        gate_out, up_out, down_out, joint_out, proj_out, sums_out, token_ref = refs[
            count + len(keep) : count + len(keep) + 7
        ]
        gate_buf, up_buf, down_buf, small_buf, sums_buf, sems, small_sems = refs[
            count + len(keep) + 7 :
        ]
        core_zero = meta_ref[1] == 0
        copies = []

        def send(src, dst, sem):
            copy = pltpu.make_async_copy(src, dst, sem)
            copy.start()
            copies.append(copy)

        def column(ref, j):
            found = [
                ref[j * 16 : (j + 1) * 16, i * 128 : (i + 1) * 128] for i in range(mlp_rows // 16)
            ]
            return jnp.concatenate(found, 0).astype(f32)

        for k, slot in enumerate(slots):
            for j in range(columns):
                got = column(ins[2 * k], j)
                other = column(ins[2 * k + 1], j)
                zero = jnp.where(core_zero, got, other)
                one = jnp.where(core_zero, other, got)
                if j < 2 * tiles:
                    buf = gate_buf if j < tiles else up_buf
                    at = (j % tiles) * 128
                    buf[k, :, at : at + 128] = zero
                    buf[k, :, at + main + 128 : at + main + 256] = one
                else:
                    left = lanes(zero.shape) < 64
                    gate_buf[k, :, main : main + 128] = jnp.where(left, zero, one)
                    up_buf[k, :, main : main + 128] = pltpu.roll(jnp.where(left, one, zero), 64, 1)
            owner = meta_ref[12 + slot]
            here = pl.ds(pl.multiple_of(owner * mlp_rows, 8), mlp_rows)
            send(gate_buf.at[k], gate_out.at[here, :], sems.at[5 * k])
            send(up_buf.at[k], up_out.at[here, :], sems.at[5 * k + 1])
            sums_buf[k] = ins[2 * k][top + piece : top + piece + 16, :share].astype(f32)[:8]
            here = pl.ds(pl.multiple_of(owner * 8, 8), 8)
            send(sums_buf.at[k], sums_out.at[here, :], sems.at[5 * k + 4])
            for side in range(2):
                b = 2 * k + side
                core = meta_ref[1] if side == 0 else 1 - meta_ref[1]
                down_buf[b] = ins[b][top + piece + 16 :, :].astype(f32)
                here = pl.ds(pl.multiple_of((core * chips + owner) * down_rows, 8), down_rows)
                send(down_buf.at[b], down_out.at[here, :], sems.at[5 * k + 2 + side])
                tall = jnp.concatenate(
                    [ins[b][top : top + piece, i * 128 : (i + 1) * 128] for i in range(lanes_out)], 0
                ).astype(f32)
                rows = pl.ds(pl.multiple_of(core * q_rows, 8), q_rows)
                for i in range(parts):
                    small_buf[b, i] = tall[i * q_rows : (i + 1) * q_rows]
                    block = owner * parts + i

                    @pl.when(block < cols // 128)
                    def joint(b=b, i=i, rows=rows, block=block):
                        at = pl.ds(pl.multiple_of(block * 128, 128), 128)
                        pltpu.make_async_copy(
                            small_buf.at[b, i], joint_out.at[rows, at], small_sems.at[b, i]
                        ).start()

                    @pl.when(block >= cols // 128)
                    def proj(b=b, i=i, rows=rows, block=block):
                        at = pl.ds(pl.multiple_of((block - cols // 128) * 128, 128), 128)
                        pltpu.make_async_copy(
                            small_buf.at[b, i], proj_out.at[rows, at], small_sems.at[b, i]
                        ).start()

        token_ref[...] = jnp.zeros(token_ref.shape, f32)
        for copy in copies:
            copy.wait()
        for b in range(count):
            for i in range(parts):
                pltpu.make_async_copy(
                    small_buf.at[b, i],
                    proj_out.at[pl.ds(0, q_rows), pl.ds(0, 128)],
                    small_sems.at[b, i],
                ).wait()

    anywhere = pl.BlockSpec(memory_space=pl.ANY)
    result = pl.pallas_call(
        kernel,
        out_shape=[
            jax.ShapeDtypeStruct((D, ff_loc), f32),
            jax.ShapeDtypeStruct((D, ff_loc), f32),
            jax.ShapeDtypeStruct((ff_loc, D), f32),
            jax.ShapeDtypeStruct((2 * q_rows, cols), f32),
            jax.ShapeDtypeStruct((2 * q_rows, D), f32),
            jax.ShapeDtypeStruct((8 * chips, share), f32),
            jax.ShapeDtypeStruct((8, 128), f32),
        ],
        in_specs=[pl.BlockSpec(memory_space=pltpu.SMEM)]
        + [pl.BlockSpec(memory_space=pltpu.VMEM)] * count
        + [anywhere] * len(keep),
        out_specs=[anywhere] * 6 + [pl.BlockSpec(memory_space=pltpu.VMEM)],
        scratch_shapes=[
            pltpu.VMEM((len(slots), mlp_rows, ff_loc), f32),
            pltpu.VMEM((len(slots), mlp_rows, ff_loc), f32),
            pltpu.VMEM((count, down_rows, D), f32),
            pltpu.VMEM((count, parts, q_rows, 128), f32),
            pltpu.VMEM((len(slots), 8, share), f32),
            pltpu.SemaphoreType.DMA((5 * len(slots),)),
            pltpu.SemaphoreType.DMA((count, parts)),
        ],
        input_output_aliases={1 + count + i: i for i in range(len(keep))},
        compiler_params=pltpu.CompilerParams(vmem_limit_bytes=VMEM_BYTES),
        cost_estimate=pl.CostEstimate(
            flops=0, bytes_accessed=8 * sum(x.size for x in blocks), transcendentals=0
        ),
    )(meta, *blocks, *keep)
    return list(result[:6]), result[6]


def place_blocks(blocks, spots, out_shape, old=None):
    shape = blocks[0].shape
    count = len(blocks)
    if shape[0] % 8 or shape[1] % 128:
        out = jnp.zeros(out_shape, f32) if old is None else old
        for block, (i, j) in zip(blocks, spots):
            out = lax.dynamic_update_slice(
                out, block.astype(f32), (i * shape[0], j * shape[1])
            )
        return out

    def kernel(spots_ref, *refs):
        step = pl.program_id(0)
        out_ref = refs[-1]
        for i in range(count):

            @pl.when(step == i)
            def write(i=i):
                out_ref[...] = refs[i][...].astype(f32)

    keep = [] if old is None else [old]
    return pl.pallas_call(
        kernel,
        out_shape=jax.ShapeDtypeStruct(out_shape, f32),
        grid_spec=pltpu.PrefetchScalarGridSpec(
            num_scalar_prefetch=1,
            grid=(count,),
            in_specs=[pl.BlockSpec(shape, lambda i, spots: (0, 0))] * count
            + [pl.BlockSpec(memory_space=pl.ANY)] * len(keep),
            out_specs=pl.BlockSpec(shape, lambda i, spots: (spots[i, 0], spots[i, 1])),
        ),
        input_output_aliases={} if old is None else {count + 1: 0},
        compiler_params=pltpu.CompilerParams(vmem_limit_bytes=VMEM_BYTES),
    )(jnp.stack([jnp.stack(s) for s in spots]).astype(jnp.int32), *blocks, *keep)


def local(tokens, w_qkv, b_qkv, w_out, gain_attn, gain_mlp, w_gate, w_up, w_down, cotangent):
    net = Net()
    rows = tokens.shape[1]
    half_rows = rows // 2
    ctx_count = net.ctx
    core = net.core
    chips = net.chips
    part_rows = GROUP * half_rows
    x = tokens[0]
    gain_one = gain_attn[None]
    gain_two = gain_mlp[None]

    w_qkv_full = net.full_rows(w_qkv)

    ff_loc = w_gate.shape[1]
    ff_half = ff_loc // 2
    main = (ff_half // 128) * 128
    rest = ff_half - main
    width = main + 2 * rest
    first = core * main
    tiled = net.dp == 2 and 2 * rest == 128 and width % 256 == 0 and chips == 8 and ff_half == chips * RING_ROWS
    ring = jnp.arange(chips, dtype=jnp.int32)
    owners_of = (net.pos - ring) % chips
    spots = jnp.concatenate(
        [jnp.stack([net.d, core, first, jnp.int32(ff_half)]), owners_of, owners_of]
    ).astype(jnp.int32)

    row_ids = jnp.arange(half_rows, dtype=jnp.int32)
    place = jnp.concatenate(
        [net.c * half_rows + row_ids, (2 * ctx_count - 1 - net.c) * half_rows + row_ids]
    )
    freq = ROPE_BASE ** (-((jnp.arange(128) % (HD // 2)).astype(f32) * (2.0 / HD)))
    angle = place.astype(f32)[:, None] * freq[None, :]
    cosine, sine = jnp.cos(angle), jnp.sin(angle)
    normed_one, queries, pairs = call(
        qkv_kernel,
        [
            jax.ShapeDtypeStruct((rows, D), bf16),
            jax.ShapeDtypeStruct((rows, WIDTH_Q), bf16),
            jax.ShapeDtypeStruct((rows, 2 * WIDTH_K), bf16),
        ],
        [x, gain_one, w_qkv_full, b_qkv[None], cosine, sine],
        flops=2 * rows * D * 1152,
    )

    slots = net.ring_gather(pairs)
    mine = jnp.concatenate(slots, 0)
    other = net.swap(mine)
    order = jnp.array(net.order, jnp.int32)
    chip_ids = order[(net.pos - jnp.arange(chips, dtype=jnp.int32)) % chips]
    meta = jnp.concatenate([net.c[None], 2 * chip_ids + core, 2 * chip_ids + 1 - core])
    meta = meta.astype(jnp.int32)

    late_w, late_g, late_n, unused = lax.optimization_barrier((w_out, cotangent[0], normed_one, pairs))
    w_out_full = net.full_rows(late_w)
    early = net.group_parts(jnp.concatenate([late_g, late_n], 1))

    total_keys = rows * ctx_count
    padded = (KH, 2 * part_rows, 128)
    attended_low, attended, lse, spread, keys, values, hidden, normed_two = call(
        lambda *refs: forward_kernel(ctx_count, *refs),
        [
            jax.ShapeDtypeStruct((rows, WIDTH_Q), bf16),
            jax.ShapeDtypeStruct(padded, f32),
            jax.ShapeDtypeStruct((KH, 2, 8, part_rows), f32),
            jax.ShapeDtypeStruct(padded, bf16),
            jax.ShapeDtypeStruct((total_keys, WIDTH_K), bf16),
            jax.ShapeDtypeStruct((total_keys, WIDTH_K), bf16),
            jax.ShapeDtypeStruct((rows, D), f32),
            jax.ShapeDtypeStruct((rows, D), bf16),
        ],
        [meta, queries, mine, other, x, w_out_full, gain_two],
        smem=1,
        scratch=[
            pltpu.VMEM((KH, total_keys // KEYS, part_rows, KEYS), f32),
            pltpu.VMEM((KH, part_rows, 128), f32),
            pltpu.VMEM((KH, part_rows, 128), f32),
        ],
        flops=8 * KH * part_rows * total_keys * 128,
    )

    normed_two_parts = net.group_parts(normed_two)
    chip_rows = net.dp * rows
    down_rows = ff_half // chips
    mlp_rows = D // chips
    if tiled:
        x_turned, mid_turned, gate_low, up_low, grad_mine, out_mine, sent = feed_forward(
            spots, normed_two_parts, early, w_gate, w_up, w_down, width
        )
    else:
        normed_two_group = jnp.concatenate(normed_two_parts, 0)
        grad_out_group = jnp.concatenate(early, 0)[:, :D]
        own_cols = (jnp.arange(width) + first < ff_half) == (core == 0)
        wg = lax.dynamic_slice(w_gate, (0, first), (D, width))
        wu = lax.dynamic_slice(w_up, (0, first), (D, width))
        wd = lax.dynamic_slice(w_down, (first, 0), (width, D))
        gate = jnp.dot(normed_two_group, wg, preferred_element_type=f32)
        upper = jnp.dot(normed_two_group, wu, preferred_element_type=f32)
        sigma = jax.nn.sigmoid(gate)
        activated = gate * sigma
        middle = jnp.where(own_cols, activated * upper, 0.0).astype(bf16)
        grad_middle = jnp.einsum("td,fd->tf", grad_out_group, wd, preferred_element_type=f32)
        slope = sigma * (1.0 + gate * (1.0 - sigma))
        grad_gate_low = jnp.where(own_cols, grad_middle * upper * slope, 0.0).astype(bf16)
        grad_up_low = jnp.where(own_cols, grad_middle * activated, 0.0).astype(bf16)

        grad_normed_two = jnp.einsum(
            "tf,df->td", grad_gate_low, wg, preferred_element_type=f32
        ) + jnp.einsum("tf,df->td", grad_up_low, wu, preferred_element_type=f32)
        mlp_out = jnp.dot(middle, wd, preferred_element_type=f32)
        grad_mine, out_mine = grad_normed_two[:chip_rows], mlp_out[:chip_rows]
        sent = jnp.concatenate([grad_normed_two[chip_rows:], mlp_out[chip_rows:]], 0).astype(bf16)
    swapped = net.swap(sent)
    grad_chip = grad_mine + swapped[:chip_rows].astype(f32)
    mlp_chip = out_mine + swapped[chip_rows:].astype(f32)
    grad_two = grad_chip[:rows]
    for s in range(1, net.dp):
        sent_two = grad_chip[s * rows : (s + 1) * rows].astype(bf16)
        grad_two = grad_two + net.shift(sent_two, net.dp - s).astype(f32)

    def attention_back():
        grad_hidden, grad_attn_low, grad_gain_two, grad_queries, terms_mine, terms_other = call(
            lambda *refs: backward_kernel(ctx_count, *refs),
            [
                jax.ShapeDtypeStruct((rows, D), f32),
                jax.ShapeDtypeStruct((rows, D), bf16),
                jax.ShapeDtypeStruct((1, D), f32),
                jax.ShapeDtypeStruct((rows, WIDTH_Q), f32),
                jax.ShapeDtypeStruct((chips * rows, 2 * WIDTH_K), f32),
                jax.ShapeDtypeStruct((chips * rows, 2 * WIDTH_K), bf16),
            ],
            [
                meta, grad_two, hidden, cotangent[0], gain_two, w_out_full, spread, keys, values, lse,
                attended,
            ],
            smem=1,
            scratch=[
                pltpu.VMEM(padded, bf16),
                pltpu.VMEM(padded, f32),
                pltpu.VMEM((total_keys, WIDTH_K), f32),
                pltpu.VMEM((total_keys, WIDTH_K), f32),
            ],
            flops=20 * KH * part_rows * total_keys * 128,
        )
        swapped_terms = net.swap(terms_other)

        def finish(wait_pairs=()):
            pair_sums = call(
                pair_kernel,
                [jax.ShapeDtypeStruct((rows, 2 * WIDTH_K), f32)]
                + [jax.ShapeDtypeStruct((rows, 2 * WIDTH_K), bf16)] * (chips - 1),
                [terms_mine, swapped_terms] + list(wait_pairs),
                loose=len(wait_pairs),
            )
            grad_pairs = net.ring_parts(pair_sums)

            def last(wait_finish=()):
                joint, grad_input, grad_gain_one, grad_bias = call(
                    finish_kernel,
                    [
                        jax.ShapeDtypeStruct((rows + 16, 1152), bf16),
                        jax.ShapeDtypeStruct((rows, D), f32),
                        jax.ShapeDtypeStruct((1, D), f32),
                        jax.ShapeDtypeStruct((1, 1152), f32),
                    ],
                    [grad_queries, x, gain_one, w_qkv_full, cosine, sine, grad_hidden, grad_gain_two]
                    + grad_pairs
                    + list(wait_finish),
                    flops=2 * rows * D * 1152,
                    loose=len(wait_finish),
                )
                return (grad_attn_low, grad_gain_two, joint, grad_input, grad_gain_one, grad_bias)

            return last

        return finish

    found = []
    steps = [attention_back()]
    if tiled:

        def pairs_stage(*blocks):
            steps.append(steps[0](blocks))

        def finish_stage(*blocks):
            found.extend(steps[1](blocks))

        def small_stage(*blocks):
            found.append(blocks)

        terms = mlp_gradients(
            spots, x_turned, early, mid_turned, gate_low, up_low, sent_two, chips, down_rows, main
        )
        fwd, back = net.ring_sum(terms, [pairs_stage, finish_stage, small_stage])
        wait_small = found.pop()
        sum_mlp, sum_down = ring_end(fwd, back, terms[0], terms[0].shape[0] - down_rows)
    else:
        part_down = jnp.einsum(
            "tf,td->fd", middle, grad_out_group, preferred_element_type=f32
        ).astype(bf16)
        part_down = lax.dynamic_slice(part_down, (core * rest, 0), (ff_half, D))

        def down_chunk(slot):
            return lax.dynamic_slice(part_down, (net.owner(slot) * down_rows, 0), (down_rows, D))

        sum_down = net.ring_scatter([down_chunk(s) for s in range(chips)]).astype(bf16)

        def split_main(x):
            left = (x[:, :main], x[:, main:])
            right = (x[:, 2 * rest :], x[:, : 2 * rest])
            return (
                jnp.where(core == 0, left[0], right[0]),
                jnp.where(core == 0, left[1], right[1]),
            )

        gate_main, gate_tile = split_main(grad_gate_low)
        up_main, up_tile = split_main(grad_up_low)
        packed = jnp.concatenate(
            [gate_main, up_main, gate_tile + jnp.roll(up_tile, rest, 1)], 1
        )
        part_mlp = jnp.einsum(
            "td,tf->df", normed_two_group, packed, preferred_element_type=f32
        ).astype(bf16)

        def mlp_chunk(slot):
            return lax.dynamic_slice(
                part_mlp, (net.owner(slot) * mlp_rows, 0), (mlp_rows, 2 * ff_half)
            )

        sum_mlp = net.ring_scatter([mlp_chunk(s) for s in range(chips)]).astype(bf16)
        sum_mlp = lax.optimization_barrier(sum_mlp)
        found.extend(steps[0]()())
    grad_attn_low, grad_gain_two, grad_joint_low, grad_input, grad_gain_one, grad_bias = found

    out_sum = mlp_chip[:rows]
    sent = jnp.concatenate([attended_low, grad_attn_low], 0)
    gathered = [sent]
    for s in range(1, net.dp):
        got = net.shift(
            jnp.concatenate([mlp_chip[s * rows : (s + 1) * rows].astype(bf16), sent], 0),
            net.dp - s,
        )
        out_sum = out_sum + got[:rows].astype(f32)
        gathered.append(got[rows:])
    output = (hidden + out_sum).astype(bf16)
    gathered = jnp.concatenate(gathered, 0)
    near = (gathered, net.swap(gathered))

    q_rows = w_qkv.shape[0] // 2
    qkv_cols = w_qkv.shape[1]
    if tiled:
        piece = q_rows * (qkv_cols + D) // chips // D
        terms_small = call(
            lambda *refs: small_grad_kernel(chips, q_rows, rows, *refs),
            [jax.ShapeDtypeStruct((piece + 16, D), bf16)] * chips,
            [spots, *early, *net.group_parts(grad_joint_low), *near, *wait_small],
            smem=1,
            loose=len(wait_small),
            scratch=[pltpu.VMEM((D, qkv_cols + D), f32), pltpu.VMEM((8, 3 * 128 * chips), f32)],
            flops=4 * chip_rows * D * (qkv_cols + D),
        )
        block = call(
            block_kernel,
            [jax.ShapeDtypeStruct((sum_mlp.shape[0] + piece + 16 + down_rows, D), bf16)],
            [sum_mlp, sum_down] + net.ring_parts(terms_small),
        )[0]
        sizes = (main, ff_loc, q_rows, qkv_cols, down_rows, chips)
        grad_gate, grad_up, grad_down, grad_joint, grad_out_proj, sums = net.gather_placed(
            block, lambda slots, pairs, old: place_all(spots, slots, pairs, old, sizes)
        )
        small = sums.reshape(chips, 8, 384)[:, 0].reshape(-1)[: 2 * D + qkv_cols]
    else:
        gathered = jnp.concatenate(near, 0).reshape(2 * net.dp, 2, rows, D)
        attended_group = gathered[:, 0].reshape(2 * net.dp * rows, D)
        grad_attn_group = gathered[:, 1].reshape(2 * net.dp * rows, D)
        normed_one_group = jnp.concatenate(early, 0)[:, D:]
        joint_group = net.group_gather(grad_joint_low[:rows])
        q_first = net.d * (2 * q_rows) + core * q_rows
        group_rows = 2 * net.dp * rows
        part_out = jnp.einsum(
            "tc,td->cd",
            lax.dynamic_slice(attended_group, (0, q_first), (group_rows, q_rows)),
            grad_attn_group,
            preferred_element_type=f32,
        )
        part_joint = jnp.einsum(
            "td,tc->dc",
            lax.dynamic_slice(normed_one_group, (0, q_first), (group_rows, q_rows)),
            joint_group,
            preferred_element_type=f32,
        )
        part_small = jnp.concatenate([part_joint, part_out], 1).astype(bf16)
        small_cols = part_small.shape[1] // chips

        def small_chunk(slot):
            return lax.dynamic_slice(part_small, (0, net.owner(slot) * small_cols), (q_rows, small_cols))

        sum_small = net.ring_scatter([small_chunk(s) for s in range(chips)]).astype(bf16)

        tall = jnp.concatenate(
            [sum_small[:, i * 128 : (i + 1) * 128] for i in range(small_cols // 128)], 0
        )
        piece = tall.shape[0] // (D // 128)
        wide = jnp.concatenate([tall[i * piece : (i + 1) * piece] for i in range(D // 128)], 1)
        both = lax.optimization_barrier(jnp.concatenate([sum_down, wide], 0))

        owners = [net.owner(s) for s in range(chips)]
        got_mlp = net.ring_gather(sum_mlp)
        got_both = net.ring_gather(both)
        pairs_mlp = [(got, net.swap(got)) for got in got_mlp]
        pairs_both = [(got, net.swap(got)) for got in got_both]

        down_blocks, down_spots, small_blocks, small_spots = [], [], [], []
        for owner, pair in zip(owners, pairs_both):
            for which, got in zip((core, 1 - core), pair):
                down_blocks.append(got[:down_rows])
                down_spots.append((which * chips + owner, jnp.int32(0)))
                wide = got[down_rows:]
                tall = jnp.concatenate([wide[:, i * 128 : (i + 1) * 128] for i in range(D // 128)], 0)
                small_blocks.append(
                    jnp.concatenate(
                        [tall[i * q_rows : (i + 1) * q_rows] for i in range(small_cols // 128)], 1
                    )
                )
                small_spots.append((which, owner))
        grad_down = place_blocks(down_blocks, down_spots, (ff_loc, D))
        grad_small = place_blocks(small_blocks, small_spots, (2 * q_rows, part_small.shape[1]))
        grad_gate = jnp.zeros((D, ff_loc), f32)
        grad_up = jnp.zeros((D, ff_loc), f32)
        left_lane = jnp.arange(2 * rest) < rest
        for owner, (got, swapped) in zip(owners, pairs_mlp):
            zero = jnp.where(core == 0, got, swapped).astype(f32)
            one = jnp.where(core == 0, swapped, got).astype(f32)
            tile_zero, tile_one = zero[:, 2 * main :], one[:, 2 * main :]
            mid_gate = jnp.where(left_lane, tile_zero, tile_one)
            mid_up = jnp.roll(jnp.where(left_lane, tile_one, tile_zero), rest, 1)
            base = owner * mlp_rows
            grad_gate = lax.dynamic_update_slice(
                grad_gate, jnp.concatenate([zero[:, :main], mid_gate, one[:, :main]], 1), (base, 0)
            )
            grad_up = lax.dynamic_update_slice(
                grad_up,
                jnp.concatenate([zero[:, main : 2 * main], mid_up, one[:, main : 2 * main]], 1),
                (base, 0),
            )

        grad_joint, grad_out_proj = grad_small[:, :qkv_cols], grad_small[:, qkv_cols:]
        small = net.total(jnp.concatenate([grad_gain_one, grad_gain_two, grad_bias], 1))[0]
    return (
        output[None],
        grad_input[None],
        grad_joint,
        small[2 * D :],
        grad_out_proj,
        small[:D],
        small[D : 2 * D],
        grad_gate,
        grad_up,
        grad_down,
    )


def solution(mesh):
    placed = (
        P("dp", "ctx", None),
        P("dp", None),
        P(),
        P("dp", None),
        P(),
        P(),
        P(None, "dp"),
        P(None, "dp"),
        P("dp", None),
        P("dp", "ctx", None),
    )
    return jax.shard_map(
        local,
        mesh=mesh,
        in_specs=placed,
        out_specs=(
            P("dp", "ctx", None),
            P("dp", "ctx", None),
            P("dp", None),
            P(),
            P("dp", None),
            P(),
            P(),
            P(None, "dp"),
            P(None, "dp"),
            P("dp", None),
        ),
        check_vma=False,
    )
```

```python
import jax
import jax.numpy as jnp
from jax import lax
from jax.experimental import pallas as pl
from jax.experimental.pallas import tpu as pltpu
from jax.sharding import PartitionSpec as P

D = 896
QH = 14
KH = 2
HD = 64
GROUP = QH // KH
WIDTH_Q = QH * HD
WIDTH_K = KH * HD

EPS = 1e-06
ROPE_BASE = 1000000.0

f32 = jnp.float32
bf16 = jnp.bfloat16


def ring_order(chips):
    if chips % 2:
        return list(range(chips))
    rows = chips // 2
    return [2 * i for i in range(rows)] + [2 * i + 1 for i in reversed(range(rows))]


def half_cut(rows):
    cut = (rows // 2 + 7) // 8 * 8
    return cut if cut < rows else rows // 2


class Net:
    def __init__(self):
        self.dp = lax.axis_size("dp")
        self.ctx = lax.axis_size("ctx")
        self.chips = self.ctx // 2
        self.order = ring_order(self.chips)
        self.d = lax.axis_index("dp")
        self.c = lax.axis_index("ctx")
        self.core = self.c % 2
        place = [0] * self.chips
        for spot, chip in enumerate(self.order):
            place[chip] = spot
        self.pos = jnp.array(place, jnp.int32)[self.c // 2]

    def swap(self, x):
        return lax.ppermute(x, "ctx", [(i, i ^ 1) for i in range(self.ctx)])

    def shift(self, x, step):
        n = self.dp
        return lax.ppermute(x, "dp", [(i, (i + step) % n) for i in range(n)])

    def hop(self, x, step):
        n = self.chips
        perm = []
        for spot in range(n):
            for core in range(2):
                perm.append((2 * self.order[spot] + core, 2 * self.order[(spot + step) % n] + core))
        return lax.ppermute(x, "ctx", perm)

    def owner(self, slot):
        return (self.pos - slot) % self.chips

    def group_parts(self, x):
        chip = jnp.concatenate([x] + [self.shift(x, s) for s in range(1, self.dp)], 0)
        return chip, self.swap(chip)

    def group_gather(self, x):
        return jnp.concatenate(self.group_parts(x), 0)

    def ring_gather(self, x):
        n = self.chips
        half = n // 2
        cut = half_cut(x.shape[0])
        found = [x] + [None] * (n - 1)
        fwd, back = x, x
        for s in range(1, half):
            fwd = self.hop(fwd, 1)
            back = self.hop(back, -1)
            found[s] = fwd
            found[n - s] = back
        found[half] = jnp.concatenate([self.hop(fwd[:cut], 1), self.hop(back[cut:], -1)], 0)
        return found

    def ring_scatter(self, local):
        n = self.chips
        half = n // 2
        cut = half_cut(local[half].shape[0])

        def add(got, mine):
            return (got.astype(f32) + mine.astype(f32)).astype(bf16)

        fwd = self.hop(local[half][:cut], 1)
        back = self.hop(local[half][cut:], -1)
        for s in range(1, half):
            mine_f = local[half + s]
            mine_b = local[half - s]
            if s == 1:
                mine_f = jnp.concatenate([add(fwd, mine_f[:cut]), mine_f[cut:]], 0)
                mine_b = jnp.concatenate([mine_b[:cut], add(back, mine_b[cut:])], 0)
            else:
                mine_f = add(fwd, mine_f)
                mine_b = add(back, mine_b)
            fwd = self.hop(mine_f, 1)
            back = self.hop(mine_b, -1)
        return fwd.astype(f32) + back.astype(f32) + local[0].astype(f32)

    def full_rows(self, shard):
        rows = shard.shape[0]
        half = rows // 2
        piece = lax.dynamic_slice(shard, (self.core * half, 0), (half, shard.shape[1]))
        blocks = [shard]
        for s in range(1, self.dp):
            got = self.shift(piece, s)
            other = self.swap(got)
            low = jnp.where(self.core == 0, got, other)
            high = jnp.where(self.core == 0, other, got)
            blocks.append(jnp.concatenate([low, high], 0))
        if self.dp == 2:
            first = jnp.where(self.d == 0, blocks[0], blocks[1])
            second = jnp.where(self.d == 0, blocks[1], blocks[0])
            return jnp.concatenate([first, second], 0)
        ranked = jnp.stack(blocks)[(self.d - jnp.arange(self.dp)) % self.dp]
        return ranked.reshape(self.dp * rows, shard.shape[1])

    def total(self, x):
        x = x + self.swap(x)
        bit = 1
        while bit < self.chips:
            x = x + lax.ppermute(x, "ctx", [(i, i ^ (2 * bit)) for i in range(self.ctx)])
            bit *= 2
        bit = 1
        while bit < self.dp:
            x = x + lax.ppermute(x, "dp", [(i, i ^ bit) for i in range(self.dp)])
            bit *= 2
        return x

    def ring_parts(self, local):
        n = self.chips
        half = n // 2
        cut = half_cut(local[half].shape[0])

        def add(got, mine):
            return (got.astype(f32) + mine.astype(f32)).astype(bf16)

        fwd, back = self.hop(local[half][:cut], 1), self.hop(local[half][cut:], -1)
        for s in range(1, half):
            mine_f, mine_b = local[half + s], local[half - s]
            if s == 1:
                mine_f = jnp.concatenate([add(fwd, mine_f[:cut]), mine_f[cut:]], 0)
                mine_b = jnp.concatenate([mine_b[:cut], add(back, mine_b[cut:])], 0)
            else:
                mine_f, mine_b = add(fwd, mine_f), add(back, mine_b)
            fwd, back = self.hop(mine_f, 1), self.hop(mine_b, -1)
        return [local[0], fwd, back]

    def ring_sum(self, terms, stages):
        n = self.chips
        half = n // 2
        fwd, back = self.hop(terms[half], 1), self.hop(terms[half - 1], -1)

        def add(got, slot):
            return (got.astype(f32) + terms[slot].astype(f32)).astype(bf16)

        for s in range(1, half):
            fwd = add(fwd, half + s)
            if s < half - 1:
                back = add(back, half - 1 - s)
                stages[s - 1](fwd, back)
                fwd, back = self.hop(fwd, 1), self.hop(back, -1)
            else:
                stages[s - 1](fwd)
                fwd = self.hop(fwd, 1)
        return fwd, back

    def gather_placed(self, x, place):
        n = self.chips
        half = n // 2
        fwd = back = x
        placed = None
        waiting = ([0], [(x, self.swap(x))])
        for s in range(1, half + 1):
            if s > 1:
                placed, token = place(*waiting, placed)
                fwd, back = gate(token, fwd, back)
                waiting = ([s - 1, n - s + 1], [(fwd, self.swap(fwd)), (back, self.swap(back))])
            if s < half:
                fwd, back = self.hop(fwd, 1), self.hop(back, -1)
            else:
                cut = half_cut(fwd.shape[0])
                fwd, back = self.hop(fwd[:cut], 1), self.hop(back[cut:], -1)
        placed, token = place(*waiting, placed)
        far = join(fwd, back, token)
        return place([half], [(far, self.swap(far))], placed)[0]


VMEM_BYTES = 56 * 1024 * 1024
KEYS = 256
RING_ROWS = 152
LIGHT = pl.CostEstimate(flops=0, bytes_accessed=1024, transcendentals=0)


def full_spec(shape):
    return pl.BlockSpec(shape, lambda: (0,) * len(shape))


def call(kernel, outs, args, smem=0, scratch=(), flops=0, loose=0):
    tight = len(args) - loose
    specs = [pl.BlockSpec(memory_space=pltpu.SMEM)] * smem
    specs += [pl.BlockSpec(memory_space=pltpu.VMEM)] * (tight - smem)
    specs += [pl.BlockSpec(memory_space=pl.ANY)] * loose

    def body(*refs):
        kernel(*refs[:tight], *refs[tight + loose :])

    moved = sum(x.size * x.dtype.itemsize for x in list(args) + list(outs))
    return pl.pallas_call(
        body,
        out_shape=list(outs),
        in_specs=specs,
        out_specs=[pl.BlockSpec(memory_space=pltpu.VMEM)] * len(outs),
        scratch_shapes=list(scratch),
        compiler_params=pltpu.CompilerParams(vmem_limit_bytes=VMEM_BYTES),
        cost_estimate=LIGHT,
    )(*args)


def lanes(shape):
    return lax.broadcasted_iota(jnp.int32, shape, len(shape) - 1)


def dot_nt(a, b, precision=None):
    return lax.dot_general(
        a, b, (((1,), (1,)), ((), ())), preferred_element_type=f32, precision=precision
    )


def dot_tn(a, b):
    return lax.dot_general(a, b, (((0,), (0,)), ((), ())), preferred_element_type=f32)


def gate(token, *blocks):
    count = len(blocks)
    anywhere = pl.BlockSpec(memory_space=pl.ANY)

    def kernel(*refs):
        return None

    return pl.pallas_call(
        kernel,
        out_shape=[jax.ShapeDtypeStruct(x.shape, x.dtype) for x in blocks],
        in_specs=[anywhere] * (count + 1),
        out_specs=[anywhere] * count,
        input_output_aliases={i + 1: i for i in range(count)},
        cost_estimate=LIGHT,
    )(token, *blocks)


def join(first, second, token):
    cut = first.shape[0]

    def kernel(first_ref, second_ref, out_ref):
        out_ref[:cut, :] = first_ref[...]
        out_ref[cut:, :] = second_ref[...]

    shape = (cut + second.shape[0], first.shape[1])
    return call(
        kernel, [jax.ShapeDtypeStruct(shape, first.dtype)], [first, second, token], loose=1
    )[0]


def ring_end(fwd, back, term, split):
    rows, columns = term.shape

    def kernel(fwd_ref, back_ref, term_ref, first_ref, rest_ref):
        for ref, here in ((first_ref, slice(0, split)), (rest_ref, slice(split, rows))):
            total = fwd_ref[here, :].astype(f32) + back_ref[here, :].astype(f32)
            ref[...] = (total + term_ref[here, :].astype(f32)).astype(bf16)

    outs = [
        jax.ShapeDtypeStruct((split, columns), bf16),
        jax.ShapeDtypeStruct((rows - split, columns), bf16),
    ]
    return call(kernel, outs, [fwd, back, term])


def pair_kernel(mine_ref, got_ref, *out_refs):
    rows = out_refs[0].shape[0]
    for s, out_ref in enumerate(out_refs):
        here = slice(s * rows, (s + 1) * rows)
        out_ref[...] = (mine_ref[here, :] + got_ref[here, :].astype(f32)).astype(out_ref.dtype)


def block_kernel(mlp_ref, down_ref, *refs):
    small = refs[0][...].astype(f32)
    for ref in refs[1:-1]:
        small = small + ref[...].astype(f32)
    out_ref = refs[-1]
    top = mlp_ref.shape[0]
    piece = small.shape[0]
    out_ref[:top, :] = mlp_ref[...]
    out_ref[top : top + piece, :] = small.astype(bf16)
    out_ref[top + piece :, :] = down_ref[...]


def qkv_kernel(x_ref, gain_ref, w_ref, b_ref, cos_ref, sin_ref, norm_ref, q_ref, pair_ref):
    x = x_ref[...].astype(f32)
    inverse = lax.rsqrt(jnp.mean(x * x, -1, keepdims=True) + EPS)
    normed = (x * inverse * gain_ref[...]).astype(bf16)
    norm_ref[...] = normed
    joint = jnp.dot(normed, w_ref[...], preferred_element_type=f32) + b_ref[...]
    cosine = cos_ref[...]
    sine = sin_ref[...]
    early = lanes(cosine.shape) % HD < HD // 2
    for i in range((WIDTH_Q + WIDTH_K) // 128):
        tile = joint[:, i * 128 : (i + 1) * 128]
        turned = jnp.where(early, -pltpu.roll(tile, 96, 1), pltpu.roll(tile, 32, 1))
        turned = tile * cosine + turned * sine
        if i * 128 < WIDTH_Q:
            q_ref[:, i * 128 : (i + 1) * 128] = turned.astype(bf16)
        else:
            pair_ref[:, :WIDTH_K] = turned.astype(bf16)
    pair_ref[:, WIDTH_K:] = joint[:, WIDTH_Q + WIDTH_K :].astype(bf16)


def spread_heads(x, out_ref, factor):
    rows = x.shape[0]
    half = rows // 2
    for head in range(QH):
        kh, g = divmod(head, GROUP)
        tile = x[:, (head // 2) * 128 : (head // 2 + 1) * 128].astype(f32)
        if head % 2 != kh:
            tile = pltpu.roll(tile, HD, 1)
        tile = jnp.where(lanes(tile.shape) // HD == kh, tile * factor, 0.0).astype(out_ref.dtype)
        for part in range(2):
            start = (part * GROUP + g) * half
            out_ref[kh, start : start + half, :] = tile[part * half : (part + 1) * half]


def join_heads(src_ref, half, tile):
    sides = []
    for side in range(2):
        kh, g = divmod(2 * tile + side, GROUP)
        parts = [
            src_ref[kh, (part * GROUP + g) * half : (part * GROUP + g + 1) * half, :]
            for part in range(2)
        ]
        both = jnp.concatenate(parts, 0)
        sides.append(both if side == kh else pltpu.roll(both, HD, 1))
    return jnp.where(lanes(sides[0].shape) < HD, sides[0], sides[1])


def forward_kernel(
    ctx, meta_ref, q_ref, mine_ref, other_ref, x_ref, w_ref, gain_ref,
    low_ref, o_ref, lse_ref, spread_ref, k_ref, v_ref, hidden_ref, normed_ref,
    s_ref, max_ref, sum_ref,
):
    rows = q_ref.shape[0]
    half = rows // 2
    part_rows = GROUP * half
    me = meta_ref[0]
    chips = ctx // 2
    for j in range(ctx):
        src = mine_ref if j < chips else other_ref
        at = (j % chips) * rows
        owner = meta_ref[1 + j]
        for part in range(2):
            place = owner if part == 0 else 2 * ctx - 1 - owner
            to = pl.ds(pl.multiple_of(place * half, half), half)
            block = src[at + part * half : at + (part + 1) * half, :]
            k_ref[to, :] = block[:, :WIDTH_K]
            v_ref[to, :] = block[:, WIDTH_K:]
    spread_heads(q_ref[...], spread_ref, HD ** (-0.5))
    for part in range(2):
        span = slice(part * part_rows, (part + 1) * part_rows)
        start = (me if part == 0 else 2 * ctx - 1 - me) * half
        last = start // KEYS

        def keys_of(ref, i):
            return ref[pl.ds(pl.multiple_of(i * KEYS, KEYS), KEYS), :]

        for kh in range(KH):
            scores = dot_nt(spread_ref[kh, span, :], keys_of(k_ref, last))
            row = lax.broadcasted_iota(jnp.int32, scores.shape, 0) % half + start
            scores = jnp.where(lanes(scores.shape) + last * KEYS <= row, scores, -1e30)
            s_ref[kh, last] = scores
            max_ref[kh] = jnp.maximum(scores[:, :128], scores[:, 128:])

        def score(i, carry):
            for kh in range(KH):
                s = dot_nt(spread_ref[kh, span, :], keys_of(k_ref, i))
                s_ref[kh, i] = s
                max_ref[kh] = jnp.maximum(max_ref[kh], jnp.maximum(s[:, :128], s[:, 128:]))
            return carry

        lax.fori_loop(0, last, score, 0)
        for kh in range(KH):
            top = jnp.max(max_ref[kh], -1, keepdims=True)
            max_ref[kh] = jnp.broadcast_to(top, (part_rows, 128))
            sum_ref[kh] = jnp.zeros((part_rows, 128), f32)
            o_ref[kh, span, :] = jnp.zeros((part_rows, 128), f32)

        def weigh(i, carry):
            for kh in range(KH):
                s = s_ref[kh, i]
                top = max_ref[kh]
                left = jnp.exp(s[:, :128] - top)
                right = jnp.exp(s[:, 128:] - top)
                sum_ref[kh] += left + right
                o_ref[kh, span, :] += jnp.dot(
                    jnp.concatenate([left, right], 1).astype(bf16),
                    keys_of(v_ref, i),
                    preferred_element_type=f32,
                )
            return carry

        lax.fori_loop(0, last + 1, weigh, 0)
        for kh in range(KH):
            total = jnp.sum(sum_ref[kh], -1, keepdims=True)
            o_ref[kh, span, :] = o_ref[kh, span, :] / total
            lse_ref[kh, part] = dot_nt(
                jnp.full((8, 128), 1.0 / 128, f32),
                max_ref[kh] + jnp.log(total),
                lax.Precision.HIGHEST,
            )
    for tile in range(WIDTH_Q // 128):
        low_ref[:, tile * 128 : (tile + 1) * 128] = join_heads(o_ref, half, tile).astype(bf16)
    hidden = x_ref[...].astype(f32) + jnp.dot(low_ref[...], w_ref[...], preferred_element_type=f32)
    hidden_ref[...] = hidden
    inverse = lax.rsqrt(jnp.mean(hidden * hidden, -1, keepdims=True) + EPS)
    normed_ref[...] = (hidden * inverse * gain_ref[...]).astype(bf16)


def backward_kernel(
    ctx, meta_ref, gn_ref, hidden_ref, gout_ref, gain_ref, w_ref, spread_ref, k_ref, v_ref, lse_ref,
    o_ref,
    gh_ref, ga_ref, gain_grad_ref, gq_ref, mine_ref, other_ref,
    go_ref, gqs_ref, gk_ref, gv_ref,
):
    rows = gn_ref.shape[0]
    half = rows // 2
    part_rows = GROUP * half
    me = meta_ref[0]
    chips = ctx // 2
    hidden = hidden_ref[...]
    inverse = lax.rsqrt(jnp.mean(hidden * hidden, -1, keepdims=True) + EPS)
    unit = hidden * inverse
    grad = gn_ref[...]
    gain_grad_ref[...] = jnp.sum(grad * unit, 0, keepdims=True)
    scaled = grad * gain_ref[...]
    gh = gout_ref[...].astype(f32) + inverse * (
        scaled - unit * jnp.mean(scaled * unit, -1, keepdims=True)
    )
    gh_ref[...] = gh
    ga = gh.astype(bf16)
    ga_ref[...] = ga
    spread_heads(dot_nt(ga, w_ref[...]).astype(bf16), go_ref, 1.0)
    gqs_ref[...] = jnp.zeros_like(gqs_ref)
    gk_ref[...] = jnp.zeros_like(gk_ref)
    gv_ref[...] = jnp.zeros_like(gv_ref)
    for part in range(2):
        span = slice(part * part_rows, (part + 1) * part_rows)
        start = (me if part == 0 else 2 * ctx - 1 - me) * half
        last = start // KEYS
        deltas = [
            dot_nt(
                jnp.ones((8, 128), f32),
                go_ref[kh, span, :].astype(f32) * o_ref[kh, span, :],
                lax.Precision.HIGHEST,
            )[:1]
            for kh in range(KH)
        ]

        def step(i, masked):
            at = pl.ds(pl.multiple_of(i * KEYS, KEYS), KEYS)
            keys = k_ref[at, :]
            grad_k = gk_ref[at, :]
            grad_v = gv_ref[at, :]
            for kh in range(KH):
                queries = spread_ref[kh, span, :]
                heads = go_ref[kh, span, :]
                p = jnp.exp(dot_nt(keys, queries) - lse_ref[kh, part][:1])
                if masked:
                    row = lanes(p.shape) % half + start
                    key = lax.broadcasted_iota(jnp.int32, p.shape, 0) + i * KEYS
                    p = jnp.where(key <= row, p, 0.0)
                gs = (p * (dot_nt(v_ref[at, :], heads) - deltas[kh])).astype(bf16)
                grad_v += jnp.dot(p.astype(bf16), heads, preferred_element_type=f32)
                grad_k += jnp.dot(gs, queries, preferred_element_type=f32)
                gqs_ref[kh, span, :] += dot_tn(gs, keys)
            gk_ref[at, :] = grad_k
            gv_ref[at, :] = grad_v

        def body(i, carry):
            step(i, False)
            return carry

        lax.fori_loop(0, last, body, 0)
        step(last, True)
    for tile in range(WIDTH_Q // 128):
        gq_ref[:, tile * 128 : (tile + 1) * 128] = join_heads(gqs_ref, half, tile) * HD ** (-0.5)
    for j in range(ctx):
        dst = mine_ref if j < chips else other_ref
        at = (j % chips) * rows
        owner = meta_ref[1 + j]
        for part in range(2):
            place = owner if part == 0 else 2 * ctx - 1 - owner
            frm = pl.ds(pl.multiple_of(place * half, half), half)
            to = slice(at + part * half, at + (part + 1) * half)
            dst[to, :WIDTH_K] = gk_ref[frm, :].astype(dst.dtype)
            dst[to, WIDTH_K:] = gv_ref[frm, :].astype(dst.dtype)


def finish_kernel(
    gq_ref, x_ref, gain_ref, w_ref, cos_ref, sin_ref, gh_ref, gain_two_ref, *refs
):
    sent_ref, gx_ref, gain_grad_ref, bias_ref = refs[-4:]
    pair = refs[0][...]
    for ref in refs[1:-4]:
        pair = pair + ref[...].astype(f32)
    rows = pair.shape[0]
    joint_ref = sent_ref.at[:rows, :]
    cosine = cos_ref[...]
    sine = sin_ref[...]
    early = lanes(cosine.shape) % HD < HD // 2
    for i in range((WIDTH_Q + WIDTH_K) // 128):
        at = slice(i * 128, (i + 1) * 128)
        grad = gq_ref[:, at] if i * 128 < WIDTH_Q else pair[:, :WIDTH_K]
        scaled = grad * sine
        turned = jnp.where(early, pltpu.roll(scaled, 96, 1), -pltpu.roll(scaled, 32, 1))
        joint_ref[:, at] = (grad * cosine + turned).astype(bf16)
    joint_ref[:, WIDTH_Q + WIDTH_K :] = pair[:, WIDTH_K:].astype(bf16)
    joint = joint_ref[...]
    bias = jnp.sum(joint.astype(f32), 0, keepdims=True)
    bias_ref[...] = bias
    grad = dot_nt(joint, w_ref[...])
    x = x_ref[...].astype(f32)
    inverse = lax.rsqrt(jnp.mean(x * x, -1, keepdims=True) + EPS)
    unit = x * inverse
    gain = jnp.sum(grad * unit, 0, keepdims=True)
    gain_grad_ref[...] = gain
    wide = [jnp.zeros((1, bias.shape[1] - gain.shape[1]), f32)]
    found = []
    for row in (jnp.concatenate([gain] + wide, 1), jnp.concatenate([gain_two_ref[...]] + wide, 1), bias):
        high = row.astype(bf16)
        found += [high.astype(f32), row - high.astype(f32)]
    found.append(jnp.zeros((sent_ref.shape[0] - rows - len(found), bias.shape[1]), f32))
    sent_ref[rows:, :] = jnp.concatenate(found, 0).astype(bf16)
    scaled = grad * gain_ref[...]
    gx_ref[...] = gh_ref[...] + inverse * (
        scaled - unit * jnp.mean(scaled * unit, -1, keepdims=True)
    )


def mlp_kernel(
    half_rows, spots_ref, x_a, x_b, gy_a, gy_b, gate_a, gate_b, up_a, up_b, down_a, down_b,
    xt_ref, midt_ref, gg_ref, gu_ref, gx_ref, out_ref, send_ref,
    x_all, gy_all, wg_all, wu_all, wd_all, mid_all, gg_all, gu_all,
):
    step = pl.program_id(0)

    @pl.when(step == 0)
    def start():
        x_all[:half_rows] = x_a[...]
        x_all[half_rows:] = x_b[...]
        gy_all[:half_rows] = gy_a[...]
        gy_all[half_rows:] = gy_b[...]
        xt_ref[...] = x_all[...].T

    here = pl.ds(pl.multiple_of(step * 256, 256), 256)
    wg = jnp.concatenate([gate_a[...], gate_b[...]], 1)
    wu = jnp.concatenate([up_a[...], up_b[...]], 1)
    wd = jnp.concatenate([down_a[...], down_b[...]], 0)
    wg_all[:, here] = wg
    wu_all[:, here] = wu
    wd_all[here, :] = wd
    core = spots_ref[1]
    column = lanes((1, 256)) + (step * 256 + spots_ref[2])
    own = (column < spots_ref[3]) == (core == 0)
    x = x_all[...]
    gate = jnp.dot(x, wg, preferred_element_type=f32)
    up = jnp.dot(x, wu, preferred_element_type=f32)
    grad = jnp.where(own, dot_nt(gy_all[...], wd), 0.0)
    sigma = jax.nn.sigmoid(gate)
    active = gate * sigma
    middle = jnp.where(own, active * up, 0.0).astype(bf16)
    grad_gate = (grad * up * (sigma + active * (1.0 - sigma))).astype(bf16)
    grad_up = (grad * active).astype(bf16)
    midt_ref[...] = middle.T
    gg_ref[...] = grad_gate
    gu_ref[...] = grad_up
    mid_all[:, here] = middle
    gg_all[:, here] = grad_gate
    gu_all[:, here] = grad_up

    @pl.when(step == pl.num_programs(0) - 1)
    def end():
        gx = dot_nt(gg_all[...], wg_all[...]) + dot_nt(gu_all[...], wu_all[...])
        gx_ref[...] = gx[:half_rows]
        send_ref[:half_rows] = gx[half_rows:].astype(bf16)
        out = jnp.dot(mid_all[...], wd_all[...], preferred_element_type=f32)
        out_ref[...] = out[:half_rows]
        send_ref[half_rows:] = out[half_rows:].astype(bf16)


def feed_forward(meta, x, early, w_gate, w_up, w_down, width):
    half = x[0].shape[0]
    tokens = 2 * half
    steps = width // 256
    tiles = width // 128 - 1

    def columns(j):
        return pl.BlockSpec((D, 128), lambda i, m: (0, m[1] * tiles + 2 * i + j))

    def rows(j):
        return pl.BlockSpec((128, D), lambda i, m: (m[1] * tiles + 2 * i + j, 0))

    whole = pl.BlockSpec((tokens, D), lambda i, m: (0, 0))
    halves = pl.BlockSpec((half, D), lambda i, m: (0, 0))
    tile = pl.BlockSpec((tokens, 256), lambda i, m: (0, i))
    hidden = jax.ShapeDtypeStruct((tokens, width), bf16)
    return pl.pallas_call(
        lambda *refs: mlp_kernel(half, *refs),
        out_shape=[
            jax.ShapeDtypeStruct((D, tokens), bf16),
            jax.ShapeDtypeStruct((width, tokens), bf16),
            hidden,
            hidden,
            jax.ShapeDtypeStruct((half, D), f32),
            jax.ShapeDtypeStruct((half, D), f32),
            jax.ShapeDtypeStruct((tokens, D), bf16),
        ],
        grid_spec=pltpu.PrefetchScalarGridSpec(
            num_scalar_prefetch=1,
            grid=(steps,),
            in_specs=[halves] * 4
            + [columns(0), columns(1), columns(0), columns(1), rows(0), rows(1)],
            out_specs=[
                pl.BlockSpec((D, tokens), lambda i, m: (0, 0)),
                pl.BlockSpec((256, tokens), lambda i, m: (i, 0)),
                tile,
                tile,
                halves,
                halves,
                whole,
            ],
            scratch_shapes=[pltpu.VMEM((tokens, D), bf16)] * 2
            + [pltpu.VMEM((D, width), bf16)] * 2
            + [pltpu.VMEM((width, D), bf16)]
            + [pltpu.VMEM((tokens, width), bf16)] * 3,
        ),
        compiler_params=pltpu.CompilerParams(vmem_limit_bytes=VMEM_BYTES),
        cost_estimate=LIGHT,
    )(meta, *x, *early, w_gate, w_gate, w_up, w_up, w_down, w_down)


def mlp_grad_kernel(chips, down_rows, main, meta_ref, xt_ref, gy_a, gy_b, midt_ref, gg_ref, gu_ref, *refs):
    out_refs = refs[:chips]
    mlp_acc, down_acc, blocks, sems = refs[chips:]
    core = meta_ref[1]
    at_main = pl.ds(pl.multiple_of(core * 128, 128), main)
    at_tile = pl.ds(pl.multiple_of((1 - core) * main, 128), 128)
    xt = xt_ref[...]
    mlp_acc[:, :main] = jnp.dot(xt, gg_ref[:, at_main], preferred_element_type=f32).astype(bf16)
    mlp_acc[:, main : 2 * main] = jnp.dot(
        xt, gu_ref[:, at_main], preferred_element_type=f32
    ).astype(bf16)
    mixed = gg_ref[:, at_tile].astype(f32) + pltpu.roll(gu_ref[:, at_tile].astype(f32), 64, 1)
    mlp_acc[:, 2 * main :] = jnp.dot(
        xt, mixed.astype(bf16), preferred_element_type=f32
    ).astype(bf16)
    gy = jnp.concatenate([gy_a[:, :D], gy_b[:, :D]], 0)
    down_acc[...] = jnp.dot(midt_ref[...], gy, preferred_element_type=f32)

    mlp_rows = mlp_acc.shape[0] // chips
    columns = mlp_acc.shape[1] // 128
    half = chips // 2
    copies = []
    for slot in sorted(range(chips), key=lambda s: abs(s - half) if s else chips):
        owner = meta_ref[12 + slot]
        block = mlp_acc[pl.ds(pl.multiple_of(owner * mlp_rows, 16), mlp_rows), :]
        for j in range(columns):
            for i in range(mlp_rows // 16):
                blocks[slot, j * 16 : (j + 1) * 16, i * 128 : (i + 1) * 128] = block[
                    i * 16 : (i + 1) * 16, j * 128 : (j + 1) * 128
                ]
        first = pl.multiple_of(core * 64 + owner * down_rows, 8)
        blocks[slot, columns * 16 :, :] = down_acc[pl.ds(first, down_rows), :].astype(bf16)
        copy = pltpu.make_async_copy(blocks.at[slot], out_refs[slot], sems.at[slot])
        copy.start()
        copies.append(copy)
    for copy in copies:
        copy.wait()


def mlp_gradients(meta, xt, early, midt, gg, gu, after, chips, down_rows, main):
    tokens = gg.shape[0]
    columns = (2 * main + 128) // 128
    rows = columns * 16 + down_rows
    args = [meta, xt, *early, midt, gg, gu]
    anywhere = pl.BlockSpec(memory_space=pl.ANY)

    def kernel(*refs):
        mlp_grad_kernel(chips, down_rows, main, *refs[: len(args)], *refs[len(args) + 1 :])

    return pl.pallas_call(
        kernel,
        out_shape=[jax.ShapeDtypeStruct((rows, D), bf16)] * chips,
        in_specs=[pl.BlockSpec(memory_space=pltpu.SMEM)]
        + [pl.BlockSpec(memory_space=pltpu.VMEM)] * (len(args) - 1)
        + [anywhere],
        out_specs=[anywhere] * chips,
        scratch_shapes=[
            pltpu.VMEM((D, columns * 128), bf16),
            pltpu.VMEM((midt.shape[0], D), f32),
            pltpu.VMEM((chips, rows, D), bf16),
            pltpu.SemaphoreType.DMA((chips,)),
        ],
        compiler_params=pltpu.CompilerParams(vmem_limit_bytes=VMEM_BYTES),
        cost_estimate=LIGHT,
    )(*args, after)


def small_grad_kernel(
    chips, q_rows, rows, meta_ref, norm_a, norm_b, joint_a, joint_b, near_a, near_b, *refs
):
    out_refs, acc, sums_ref = refs[:-2], refs[-2], refs[-1]
    cols = joint_a.shape[1]
    tokens, sums, attended, grads = [], [], [], []
    for joint_ref, near_ref in ((joint_a, near_a), (joint_b, near_b)):
        for b in range(2):
            at = b * (rows + 16)
            tokens.append(joint_ref[at : at + rows, :])
            found = joint_ref[at + rows : at + rows + 16, :].astype(f32)
            sums.append([found[2 * i : 2 * i + 1] + found[2 * i + 1 : 2 * i + 2] for i in range(3)])
            attended.append(near_ref[2 * b * rows : (2 * b + 1) * rows, :])
            grads.append(near_ref[(2 * b + 1) * rows : (2 * b + 2) * rows, :])
    norm = jnp.concatenate([norm_a[:, D:], norm_b[:, D:]], 0)
    sums = [(sums[0][i] + sums[1][i]) + (sums[2][i] + sums[3][i]) for i in range(3)]
    sums_ref[...] = jnp.zeros_like(sums_ref)
    sums_ref[:1, :D] = sums[0][:, :D]
    sums_ref[:1, D : 2 * D] = sums[1][:, :D]
    sums_ref[:1, 2 * D : 2 * D + cols] = sums[2]
    acc[:, :cols] = dot_tn(norm, jnp.concatenate(tokens, 0))
    acc[:, cols:] = dot_tn(jnp.concatenate(attended, 0), jnp.concatenate(grads, 0))
    first = pl.multiple_of((2 * meta_ref[0] + meta_ref[1]) * q_rows, 16)
    width = acc.shape[1] // chips
    share = sums_ref.shape[1] // chips
    for out_ref, slot in zip(out_refs, range(chips)):
        owner = meta_ref[12 + slot]
        block = acc[pl.ds(first, q_rows), pl.ds(pl.multiple_of(owner * width, 128), width)]
        tall = jnp.concatenate(
            [block[:, i * 128 : (i + 1) * 128] for i in range(width // 128)], 0
        ).astype(bf16)
        piece = out_ref.shape[0] - 16
        for i in range(D // 128):
            out_ref[:piece, i * 128 : (i + 1) * 128] = tall[i * piece : (i + 1) * piece]
        vector = sums_ref[:, pl.ds(pl.multiple_of(owner * share, 128), share)]
        out_ref[piece:, :] = jnp.zeros((16, D), bf16)
        out_ref[piece:, :share] = jnp.concatenate([vector, vector], 0).astype(bf16)


def place_all(meta, slots, pairs, old, sizes):
    main, ff_loc, q_rows, cols, down_rows, chips = sizes
    mlp_rows = D // chips
    columns = (2 * main + 128) // 128
    tiles = main // 128
    lanes_out = D // 128
    top = columns * 16
    blocks = [x for pair in pairs for x in pair]
    count = len(blocks)
    piece = blocks[0].shape[0] - top - down_rows - 16
    share = 3 * 128
    parts = (cols + D) // chips // 128
    keep = [] if old is None else list(old)

    def kernel(meta_ref, *refs):
        ins = refs[:count]
        gate_out, up_out, down_out, joint_out, proj_out, sums_out, token_ref = refs[
            count + len(keep) : count + len(keep) + 7
        ]
        gate_buf, up_buf, down_buf, small_buf, sums_buf, sems, small_sems = refs[
            count + len(keep) + 7 :
        ]
        core_zero = meta_ref[1] == 0
        copies = []

        def send(src, dst, sem):
            copy = pltpu.make_async_copy(src, dst, sem)
            copy.start()
            copies.append(copy)

        def column(ref, j):
            found = [
                ref[j * 16 : (j + 1) * 16, i * 128 : (i + 1) * 128] for i in range(mlp_rows // 16)
            ]
            return jnp.concatenate(found, 0).astype(f32)

        for k, slot in enumerate(slots):
            for j in range(columns):
                got = column(ins[2 * k], j)
                other = column(ins[2 * k + 1], j)
                zero = jnp.where(core_zero, got, other)
                one = jnp.where(core_zero, other, got)
                if j < 2 * tiles:
                    buf = gate_buf if j < tiles else up_buf
                    at = (j % tiles) * 128
                    buf[k, :, at : at + 128] = zero
                    buf[k, :, at + main + 128 : at + main + 256] = one
                else:
                    left = lanes(zero.shape) < 64
                    gate_buf[k, :, main : main + 128] = jnp.where(left, zero, one)
                    up_buf[k, :, main : main + 128] = pltpu.roll(jnp.where(left, one, zero), 64, 1)
            owner = meta_ref[12 + slot]
            here = pl.ds(pl.multiple_of(owner * mlp_rows, 8), mlp_rows)
            send(gate_buf.at[k], gate_out.at[here, :], sems.at[5 * k])
            send(up_buf.at[k], up_out.at[here, :], sems.at[5 * k + 1])
            sums_buf[k] = ins[2 * k][top + piece : top + piece + 16, :share].astype(f32)[:8]
            here = pl.ds(pl.multiple_of(owner * 8, 8), 8)
            send(sums_buf.at[k], sums_out.at[here, :], sems.at[5 * k + 4])
            for side in range(2):
                b = 2 * k + side
                core = meta_ref[1] if side == 0 else 1 - meta_ref[1]
                down_buf[b] = ins[b][top + piece + 16 :, :].astype(f32)
                here = pl.ds(pl.multiple_of((core * chips + owner) * down_rows, 8), down_rows)
                send(down_buf.at[b], down_out.at[here, :], sems.at[5 * k + 2 + side])
                tall = jnp.concatenate(
                    [ins[b][top : top + piece, i * 128 : (i + 1) * 128] for i in range(lanes_out)], 0
                ).astype(f32)
                rows = pl.ds(pl.multiple_of(core * q_rows, 8), q_rows)
                for i in range(parts):
                    small_buf[b, i] = tall[i * q_rows : (i + 1) * q_rows]
                    block = owner * parts + i

                    @pl.when(block < cols // 128)
                    def joint(b=b, i=i, rows=rows, block=block):
                        at = pl.ds(pl.multiple_of(block * 128, 128), 128)
                        pltpu.make_async_copy(
                            small_buf.at[b, i], joint_out.at[rows, at], small_sems.at[b, i]
                        ).start()

                    @pl.when(block >= cols // 128)
                    def proj(b=b, i=i, rows=rows, block=block):
                        at = pl.ds(pl.multiple_of((block - cols // 128) * 128, 128), 128)
                        pltpu.make_async_copy(
                            small_buf.at[b, i], proj_out.at[rows, at], small_sems.at[b, i]
                        ).start()

        token_ref[...] = jnp.zeros(token_ref.shape, f32)
        for copy in copies:
            copy.wait()
        for b in range(count):
            for i in range(parts):
                pltpu.make_async_copy(
                    small_buf.at[b, i],
                    proj_out.at[pl.ds(0, q_rows), pl.ds(0, 128)],
                    small_sems.at[b, i],
                ).wait()

    anywhere = pl.BlockSpec(memory_space=pl.ANY)
    result = pl.pallas_call(
        kernel,
        out_shape=[
            jax.ShapeDtypeStruct((D, ff_loc), f32),
            jax.ShapeDtypeStruct((D, ff_loc), f32),
            jax.ShapeDtypeStruct((ff_loc, D), f32),
            jax.ShapeDtypeStruct((2 * q_rows, cols), f32),
            jax.ShapeDtypeStruct((2 * q_rows, D), f32),
            jax.ShapeDtypeStruct((8 * chips, share), f32),
            jax.ShapeDtypeStruct((8, 128), f32),
        ],
        in_specs=[pl.BlockSpec(memory_space=pltpu.SMEM)]
        + [pl.BlockSpec(memory_space=pltpu.VMEM)] * count
        + [anywhere] * len(keep),
        out_specs=[anywhere] * 6 + [pl.BlockSpec(memory_space=pltpu.VMEM)],
        scratch_shapes=[
            pltpu.VMEM((len(slots), mlp_rows, ff_loc), f32),
            pltpu.VMEM((len(slots), mlp_rows, ff_loc), f32),
            pltpu.VMEM((count, down_rows, D), f32),
            pltpu.VMEM((count, parts, q_rows, 128), f32),
            pltpu.VMEM((len(slots), 8, share), f32),
            pltpu.SemaphoreType.DMA((5 * len(slots),)),
            pltpu.SemaphoreType.DMA((count, parts)),
        ],
        input_output_aliases={1 + count + i: i for i in range(len(keep))},
        compiler_params=pltpu.CompilerParams(vmem_limit_bytes=VMEM_BYTES),
        cost_estimate=LIGHT,
    )(meta, *blocks, *keep)
    return list(result[:6]), result[6]


def place_blocks(blocks, spots, out_shape, old=None):
    shape = blocks[0].shape
    count = len(blocks)
    if shape[0] % 8 or shape[1] % 128:
        out = jnp.zeros(out_shape, f32) if old is None else old
        for block, (i, j) in zip(blocks, spots):
            out = lax.dynamic_update_slice(
                out, block.astype(f32), (i * shape[0], j * shape[1])
            )
        return out

    def kernel(spots_ref, *refs):
        step = pl.program_id(0)
        out_ref = refs[-1]
        for i in range(count):

            @pl.when(step == i)
            def write(i=i):
                out_ref[...] = refs[i][...].astype(f32)

    keep = [] if old is None else [old]
    return pl.pallas_call(
        kernel,
        out_shape=jax.ShapeDtypeStruct(out_shape, f32),
        grid_spec=pltpu.PrefetchScalarGridSpec(
            num_scalar_prefetch=1,
            grid=(count,),
            in_specs=[pl.BlockSpec(shape, lambda i, spots: (0, 0))] * count
            + [pl.BlockSpec(memory_space=pl.ANY)] * len(keep),
            out_specs=pl.BlockSpec(shape, lambda i, spots: (spots[i, 0], spots[i, 1])),
        ),
        input_output_aliases={} if old is None else {count + 1: 0},
        compiler_params=pltpu.CompilerParams(vmem_limit_bytes=VMEM_BYTES),
    )(jnp.stack([jnp.stack(s) for s in spots]).astype(jnp.int32), *blocks, *keep)


def local(tokens, w_qkv, b_qkv, w_out, gain_attn, gain_mlp, w_gate, w_up, w_down, cotangent):
    net = Net()
    rows = tokens.shape[1]
    half_rows = rows // 2
    ctx_count = net.ctx
    core = net.core
    chips = net.chips
    part_rows = GROUP * half_rows
    x = tokens[0]
    gain_one = gain_attn[None]
    gain_two = gain_mlp[None]

    w_qkv_full = net.full_rows(w_qkv)

    ff_loc = w_gate.shape[1]
    ff_half = ff_loc // 2
    main = (ff_half // 128) * 128
    rest = ff_half - main
    width = main + 2 * rest
    first = core * main
    tiled = net.dp == 2 and 2 * rest == 128 and width % 256 == 0 and chips == 8 and ff_half == chips * RING_ROWS
    ring = jnp.arange(chips, dtype=jnp.int32)
    owners_of = (net.pos - ring) % chips
    spots = jnp.concatenate(
        [jnp.stack([net.d, core, first, jnp.int32(ff_half)]), owners_of, owners_of]
    ).astype(jnp.int32)

    row_ids = jnp.arange(half_rows, dtype=jnp.int32)
    place = jnp.concatenate(
        [net.c * half_rows + row_ids, (2 * ctx_count - 1 - net.c) * half_rows + row_ids]
    )
    freq = ROPE_BASE ** (-((jnp.arange(128) % (HD // 2)).astype(f32) * (2.0 / HD)))
    angle = place.astype(f32)[:, None] * freq[None, :]
    cosine, sine = jnp.cos(angle), jnp.sin(angle)
    normed_one, queries, pairs = call(
        qkv_kernel,
        [
            jax.ShapeDtypeStruct((rows, D), bf16),
            jax.ShapeDtypeStruct((rows, WIDTH_Q), bf16),
            jax.ShapeDtypeStruct((rows, 2 * WIDTH_K), bf16),
        ],
        [x, gain_one, w_qkv_full, b_qkv[None], cosine, sine],
        flops=2 * rows * D * 1152,
    )

    slots = net.ring_gather(pairs)
    mine = jnp.concatenate(slots, 0)
    other = net.swap(mine)
    order = jnp.array(net.order, jnp.int32)
    chip_ids = order[(net.pos - jnp.arange(chips, dtype=jnp.int32)) % chips]
    meta = jnp.concatenate([net.c[None], 2 * chip_ids + core, 2 * chip_ids + 1 - core])
    meta = meta.astype(jnp.int32)

    late_w, late_g, late_n, unused = lax.optimization_barrier((w_out, cotangent[0], normed_one, pairs))
    w_out_full = net.full_rows(late_w)
    early = net.group_parts(jnp.concatenate([late_g, late_n], 1))

    total_keys = rows * ctx_count
    padded = (KH, 2 * part_rows, 128)
    attended_low, attended, lse, spread, keys, values, hidden, normed_two = call(
        lambda *refs: forward_kernel(ctx_count, *refs),
        [
            jax.ShapeDtypeStruct((rows, WIDTH_Q), bf16),
            jax.ShapeDtypeStruct(padded, f32),
            jax.ShapeDtypeStruct((KH, 2, 8, part_rows), f32),
            jax.ShapeDtypeStruct(padded, bf16),
            jax.ShapeDtypeStruct((total_keys, WIDTH_K), bf16),
            jax.ShapeDtypeStruct((total_keys, WIDTH_K), bf16),
            jax.ShapeDtypeStruct((rows, D), f32),
            jax.ShapeDtypeStruct((rows, D), bf16),
        ],
        [meta, queries, mine, other, x, w_out_full, gain_two],
        smem=1,
        scratch=[
            pltpu.VMEM((KH, total_keys // KEYS, part_rows, KEYS), f32),
            pltpu.VMEM((KH, part_rows, 128), f32),
            pltpu.VMEM((KH, part_rows, 128), f32),
        ],
        flops=8 * KH * part_rows * total_keys * 128,
    )

    normed_two_parts = net.group_parts(normed_two)
    chip_rows = net.dp * rows
    down_rows = ff_half // chips
    mlp_rows = D // chips
    if tiled:
        x_turned, mid_turned, gate_low, up_low, grad_mine, out_mine, sent = feed_forward(
            spots, normed_two_parts, early, w_gate, w_up, w_down, width
        )
    else:
        normed_two_group = jnp.concatenate(normed_two_parts, 0)
        grad_out_group = jnp.concatenate(early, 0)[:, :D]
        own_cols = (jnp.arange(width) + first < ff_half) == (core == 0)
        wg = lax.dynamic_slice(w_gate, (0, first), (D, width))
        wu = lax.dynamic_slice(w_up, (0, first), (D, width))
        wd = lax.dynamic_slice(w_down, (first, 0), (width, D))
        gate = jnp.dot(normed_two_group, wg, preferred_element_type=f32)
        upper = jnp.dot(normed_two_group, wu, preferred_element_type=f32)
        sigma = jax.nn.sigmoid(gate)
        activated = gate * sigma
        middle = jnp.where(own_cols, activated * upper, 0.0).astype(bf16)
        grad_middle = jnp.einsum("td,fd->tf", grad_out_group, wd, preferred_element_type=f32)
        slope = sigma * (1.0 + gate * (1.0 - sigma))
        grad_gate_low = jnp.where(own_cols, grad_middle * upper * slope, 0.0).astype(bf16)
        grad_up_low = jnp.where(own_cols, grad_middle * activated, 0.0).astype(bf16)

        grad_normed_two = jnp.einsum(
            "tf,df->td", grad_gate_low, wg, preferred_element_type=f32
        ) + jnp.einsum("tf,df->td", grad_up_low, wu, preferred_element_type=f32)
        mlp_out = jnp.dot(middle, wd, preferred_element_type=f32)
        grad_mine, out_mine = grad_normed_two[:chip_rows], mlp_out[:chip_rows]
        sent = jnp.concatenate([grad_normed_two[chip_rows:], mlp_out[chip_rows:]], 0).astype(bf16)
    swapped = net.swap(sent)
    grad_chip = grad_mine + swapped[:chip_rows].astype(f32)
    mlp_chip = out_mine + swapped[chip_rows:].astype(f32)
    grad_two = grad_chip[:rows]
    for s in range(1, net.dp):
        sent_two = grad_chip[s * rows : (s + 1) * rows].astype(bf16)
        grad_two = grad_two + net.shift(sent_two, net.dp - s).astype(f32)

    def attention_back():
        grad_hidden, grad_attn_low, grad_gain_two, grad_queries, terms_mine, terms_other = call(
            lambda *refs: backward_kernel(ctx_count, *refs),
            [
                jax.ShapeDtypeStruct((rows, D), f32),
                jax.ShapeDtypeStruct((rows, D), bf16),
                jax.ShapeDtypeStruct((1, D), f32),
                jax.ShapeDtypeStruct((rows, WIDTH_Q), f32),
                jax.ShapeDtypeStruct((chips * rows, 2 * WIDTH_K), f32),
                jax.ShapeDtypeStruct((chips * rows, 2 * WIDTH_K), bf16),
            ],
            [
                meta, grad_two, hidden, cotangent[0], gain_two, w_out_full, spread, keys, values, lse,
                attended,
            ],
            smem=1,
            scratch=[
                pltpu.VMEM(padded, bf16),
                pltpu.VMEM(padded, f32),
                pltpu.VMEM((total_keys, WIDTH_K), f32),
                pltpu.VMEM((total_keys, WIDTH_K), f32),
            ],
            flops=20 * KH * part_rows * total_keys * 128,
        )
        swapped_terms = net.swap(terms_other)

        def finish(wait_pairs=()):
            pair_sums = call(
                pair_kernel,
                [jax.ShapeDtypeStruct((rows, 2 * WIDTH_K), f32)]
                + [jax.ShapeDtypeStruct((rows, 2 * WIDTH_K), bf16)] * (chips - 1),
                [terms_mine, swapped_terms] + list(wait_pairs),
                loose=len(wait_pairs),
            )
            grad_pairs = net.ring_parts(pair_sums)

            def last(wait_finish=()):
                joint, grad_input, grad_gain_one, grad_bias = call(
                    finish_kernel,
                    [
                        jax.ShapeDtypeStruct((rows + 16, 1152), bf16),
                        jax.ShapeDtypeStruct((rows, D), f32),
                        jax.ShapeDtypeStruct((1, D), f32),
                        jax.ShapeDtypeStruct((1, 1152), f32),
                    ],
                    [grad_queries, x, gain_one, w_qkv_full, cosine, sine, grad_hidden, grad_gain_two]
                    + grad_pairs
                    + list(wait_finish),
                    flops=2 * rows * D * 1152,
                    loose=len(wait_finish),
                )
                return (grad_attn_low, grad_gain_two, joint, grad_input, grad_gain_one, grad_bias)

            return last

        return finish

    found = []
    steps = [attention_back()]
    if tiled:

        def pairs_stage(*blocks):
            steps.append(steps[0](blocks))

        def finish_stage(*blocks):
            found.extend(steps[1](blocks))

        def small_stage(*blocks):
            found.append(blocks)

        terms = mlp_gradients(
            spots, x_turned, early, mid_turned, gate_low, up_low, sent_two, chips, down_rows, main
        )
        fwd, back = net.ring_sum(terms, [pairs_stage, finish_stage, small_stage])
        wait_small = found.pop()
        sum_mlp, sum_down = ring_end(fwd, back, terms[0], terms[0].shape[0] - down_rows)
    else:
        part_down = jnp.einsum(
            "tf,td->fd", middle, grad_out_group, preferred_element_type=f32
        ).astype(bf16)
        part_down = lax.dynamic_slice(part_down, (core * rest, 0), (ff_half, D))

        def down_chunk(slot):
            return lax.dynamic_slice(part_down, (net.owner(slot) * down_rows, 0), (down_rows, D))

        sum_down = net.ring_scatter([down_chunk(s) for s in range(chips)]).astype(bf16)

        def split_main(x):
            left = (x[:, :main], x[:, main:])
            right = (x[:, 2 * rest :], x[:, : 2 * rest])
            return (
                jnp.where(core == 0, left[0], right[0]),
                jnp.where(core == 0, left[1], right[1]),
            )

        gate_main, gate_tile = split_main(grad_gate_low)
        up_main, up_tile = split_main(grad_up_low)
        packed = jnp.concatenate(
            [gate_main, up_main, gate_tile + jnp.roll(up_tile, rest, 1)], 1
        )
        part_mlp = jnp.einsum(
            "td,tf->df", normed_two_group, packed, preferred_element_type=f32
        ).astype(bf16)

        def mlp_chunk(slot):
            return lax.dynamic_slice(
                part_mlp, (net.owner(slot) * mlp_rows, 0), (mlp_rows, 2 * ff_half)
            )

        sum_mlp = net.ring_scatter([mlp_chunk(s) for s in range(chips)]).astype(bf16)
        sum_mlp = lax.optimization_barrier(sum_mlp)
        found.extend(steps[0]()())
    grad_attn_low, grad_gain_two, grad_joint_low, grad_input, grad_gain_one, grad_bias = found

    out_sum = mlp_chip[:rows]
    sent = jnp.concatenate([attended_low, grad_attn_low], 0)
    gathered = [sent]
    for s in range(1, net.dp):
        got = net.shift(
            jnp.concatenate([mlp_chip[s * rows : (s + 1) * rows].astype(bf16), sent], 0),
            net.dp - s,
        )
        out_sum = out_sum + got[:rows].astype(f32)
        gathered.append(got[rows:])
    output = (hidden + out_sum).astype(bf16)
    gathered = jnp.concatenate(gathered, 0)
    near = (gathered, net.swap(gathered))

    q_rows = w_qkv.shape[0] // 2
    qkv_cols = w_qkv.shape[1]
    if tiled:
        piece = q_rows * (qkv_cols + D) // chips // D
        terms_small = call(
            lambda *refs: small_grad_kernel(chips, q_rows, rows, *refs),
            [jax.ShapeDtypeStruct((piece + 16, D), bf16)] * chips,
            [spots, *early, *net.group_parts(grad_joint_low), *near, *wait_small],
            smem=1,
            loose=len(wait_small),
            scratch=[pltpu.VMEM((D, qkv_cols + D), f32), pltpu.VMEM((8, 3 * 128 * chips), f32)],
            flops=4 * chip_rows * D * (qkv_cols + D),
        )
        block = call(
            block_kernel,
            [jax.ShapeDtypeStruct((sum_mlp.shape[0] + piece + 16 + down_rows, D), bf16)],
            [sum_mlp, sum_down] + net.ring_parts(terms_small),
        )[0]
        sizes = (main, ff_loc, q_rows, qkv_cols, down_rows, chips)
        grad_gate, grad_up, grad_down, grad_joint, grad_out_proj, sums = net.gather_placed(
            block, lambda slots, pairs, old: place_all(spots, slots, pairs, old, sizes)
        )
        small = sums.reshape(chips, 8, 384)[:, 0].reshape(-1)[: 2 * D + qkv_cols]
    else:
        gathered = jnp.concatenate(near, 0).reshape(2 * net.dp, 2, rows, D)
        attended_group = gathered[:, 0].reshape(2 * net.dp * rows, D)
        grad_attn_group = gathered[:, 1].reshape(2 * net.dp * rows, D)
        normed_one_group = jnp.concatenate(early, 0)[:, D:]
        joint_group = net.group_gather(grad_joint_low[:rows])
        q_first = net.d * (2 * q_rows) + core * q_rows
        group_rows = 2 * net.dp * rows
        part_out = jnp.einsum(
            "tc,td->cd",
            lax.dynamic_slice(attended_group, (0, q_first), (group_rows, q_rows)),
            grad_attn_group,
            preferred_element_type=f32,
        )
        part_joint = jnp.einsum(
            "td,tc->dc",
            lax.dynamic_slice(normed_one_group, (0, q_first), (group_rows, q_rows)),
            joint_group,
            preferred_element_type=f32,
        )
        part_small = jnp.concatenate([part_joint, part_out], 1).astype(bf16)
        small_cols = part_small.shape[1] // chips

        def small_chunk(slot):
            return lax.dynamic_slice(part_small, (0, net.owner(slot) * small_cols), (q_rows, small_cols))

        sum_small = net.ring_scatter([small_chunk(s) for s in range(chips)]).astype(bf16)

        tall = jnp.concatenate(
            [sum_small[:, i * 128 : (i + 1) * 128] for i in range(small_cols // 128)], 0
        )
        piece = tall.shape[0] // (D // 128)
        wide = jnp.concatenate([tall[i * piece : (i + 1) * piece] for i in range(D // 128)], 1)
        both = lax.optimization_barrier(jnp.concatenate([sum_down, wide], 0))

        owners = [net.owner(s) for s in range(chips)]
        got_mlp = net.ring_gather(sum_mlp)
        got_both = net.ring_gather(both)
        pairs_mlp = [(got, net.swap(got)) for got in got_mlp]
        pairs_both = [(got, net.swap(got)) for got in got_both]

        down_blocks, down_spots, small_blocks, small_spots = [], [], [], []
        for owner, pair in zip(owners, pairs_both):
            for which, got in zip((core, 1 - core), pair):
                down_blocks.append(got[:down_rows])
                down_spots.append((which * chips + owner, jnp.int32(0)))
                wide = got[down_rows:]
                tall = jnp.concatenate([wide[:, i * 128 : (i + 1) * 128] for i in range(D // 128)], 0)
                small_blocks.append(
                    jnp.concatenate(
                        [tall[i * q_rows : (i + 1) * q_rows] for i in range(small_cols // 128)], 1
                    )
                )
                small_spots.append((which, owner))
        grad_down = place_blocks(down_blocks, down_spots, (ff_loc, D))
        grad_small = place_blocks(small_blocks, small_spots, (2 * q_rows, part_small.shape[1]))
        grad_gate = jnp.zeros((D, ff_loc), f32)
        grad_up = jnp.zeros((D, ff_loc), f32)
        left_lane = jnp.arange(2 * rest) < rest
        for owner, (got, swapped) in zip(owners, pairs_mlp):
            zero = jnp.where(core == 0, got, swapped).astype(f32)
            one = jnp.where(core == 0, swapped, got).astype(f32)
            tile_zero, tile_one = zero[:, 2 * main :], one[:, 2 * main :]
            mid_gate = jnp.where(left_lane, tile_zero, tile_one)
            mid_up = jnp.roll(jnp.where(left_lane, tile_one, tile_zero), rest, 1)
            base = owner * mlp_rows
            grad_gate = lax.dynamic_update_slice(
                grad_gate, jnp.concatenate([zero[:, :main], mid_gate, one[:, :main]], 1), (base, 0)
            )
            grad_up = lax.dynamic_update_slice(
                grad_up,
                jnp.concatenate([zero[:, main : 2 * main], mid_up, one[:, main : 2 * main]], 1),
                (base, 0),
            )

        grad_joint, grad_out_proj = grad_small[:, :qkv_cols], grad_small[:, qkv_cols:]
        small = net.total(jnp.concatenate([grad_gain_one, grad_gain_two, grad_bias], 1))[0]
    return (
        output[None],
        grad_input[None],
        grad_joint,
        small[2 * D :],
        grad_out_proj,
        small[:D],
        small[D : 2 * D],
        grad_gate,
        grad_up,
        grad_down,
    )


def solution(mesh):
    placed = (
        P("dp", "ctx", None),
        P("dp", None),
        P(),
        P("dp", None),
        P(),
        P(),
        P(None, "dp"),
        P(None, "dp"),
        P("dp", None),
        P("dp", "ctx", None),
    )
    return jax.shard_map(
        local,
        mesh=mesh,
        in_specs=placed,
        out_specs=(
            P("dp", "ctx", None),
            P("dp", "ctx", None),
            P("dp", None),
            P(),
            P("dp", None),
            P(),
            P(),
            P(None, "dp"),
            P(None, "dp"),
            P("dp", None),
        ),
        check_vma=False,
    )
```

```python
import jax
import jax.numpy as jnp
from jax import lax
from jax.experimental import pallas as pl
from jax.experimental.pallas import tpu as pltpu
from jax.sharding import PartitionSpec as P

D = 896
QH = 14
KH = 2
HD = 64
GROUP = QH // KH
WIDTH_Q = QH * HD
WIDTH_K = KH * HD

EPS = 1e-06
ROPE_BASE = 1000000.0

f32 = jnp.float32
bf16 = jnp.bfloat16


def ring_order(chips):
    if chips % 2:
        return list(range(chips))
    rows = chips // 2
    return [2 * i for i in range(rows)] + [2 * i + 1 for i in reversed(range(rows))]


def half_cut(rows):
    cut = (rows // 2 + 7) // 8 * 8
    return cut if cut < rows else rows // 2


class Net:
    def __init__(self):
        self.dp = lax.axis_size("dp")
        self.ctx = lax.axis_size("ctx")
        self.chips = self.ctx // 2
        self.order = ring_order(self.chips)
        self.d = lax.axis_index("dp")
        self.c = lax.axis_index("ctx")
        self.core = self.c % 2
        place = [0] * self.chips
        for spot, chip in enumerate(self.order):
            place[chip] = spot
        self.pos = jnp.array(place, jnp.int32)[self.c // 2]

    def swap(self, x):
        return lax.ppermute(x, "ctx", [(i, i ^ 1) for i in range(self.ctx)])

    def shift(self, x, step):
        n = self.dp
        return lax.ppermute(x, "dp", [(i, (i + step) % n) for i in range(n)])

    def hop(self, x, step):
        n = self.chips
        perm = []
        for spot in range(n):
            for core in range(2):
                perm.append((2 * self.order[spot] + core, 2 * self.order[(spot + step) % n] + core))
        return lax.ppermute(x, "ctx", perm)

    def owner(self, slot):
        return (self.pos - slot) % self.chips

    def group_parts(self, x):
        chip = jnp.concatenate([x] + [self.shift(x, s) for s in range(1, self.dp)], 0)
        return chip, self.swap(chip)

    def group_gather(self, x):
        return jnp.concatenate(self.group_parts(x), 0)

    def ring_gather(self, x):
        n = self.chips
        half = n // 2
        cut = half_cut(x.shape[0])
        found = [x] + [None] * (n - 1)
        fwd, back = x, x
        for s in range(1, half):
            fwd = self.hop(fwd, 1)
            back = self.hop(back, -1)
            found[s] = fwd
            found[n - s] = back
        found[half] = jnp.concatenate([self.hop(fwd[:cut], 1), self.hop(back[cut:], -1)], 0)
        return found

    def ring_scatter(self, local):
        n = self.chips
        half = n // 2
        cut = half_cut(local[half].shape[0])

        def add(got, mine):
            return (got.astype(f32) + mine.astype(f32)).astype(bf16)

        fwd = self.hop(local[half][:cut], 1)
        back = self.hop(local[half][cut:], -1)
        for s in range(1, half):
            mine_f = local[half + s]
            mine_b = local[half - s]
            if s == 1:
                mine_f = jnp.concatenate([add(fwd, mine_f[:cut]), mine_f[cut:]], 0)
                mine_b = jnp.concatenate([mine_b[:cut], add(back, mine_b[cut:])], 0)
            else:
                mine_f = add(fwd, mine_f)
                mine_b = add(back, mine_b)
            fwd = self.hop(mine_f, 1)
            back = self.hop(mine_b, -1)
        return fwd.astype(f32) + back.astype(f32) + local[0].astype(f32)

    def full_rows(self, shard):
        rows = shard.shape[0]
        half = rows // 2
        piece = lax.dynamic_slice(shard, (self.core * half, 0), (half, shard.shape[1]))
        blocks = [shard]
        for s in range(1, self.dp):
            got = self.shift(piece, s)
            other = self.swap(got)
            low = jnp.where(self.core == 0, got, other)
            high = jnp.where(self.core == 0, other, got)
            blocks.append(jnp.concatenate([low, high], 0))
        if self.dp == 2:
            first = jnp.where(self.d == 0, blocks[0], blocks[1])
            second = jnp.where(self.d == 0, blocks[1], blocks[0])
            return jnp.concatenate([first, second], 0)
        ranked = jnp.stack(blocks)[(self.d - jnp.arange(self.dp)) % self.dp]
        return ranked.reshape(self.dp * rows, shard.shape[1])

    def total(self, x):
        x = x + self.swap(x)
        bit = 1
        while bit < self.chips:
            x = x + lax.ppermute(x, "ctx", [(i, i ^ (2 * bit)) for i in range(self.ctx)])
            bit *= 2
        bit = 1
        while bit < self.dp:
            x = x + lax.ppermute(x, "dp", [(i, i ^ bit) for i in range(self.dp)])
            bit *= 2
        return x

    def ring_parts(self, local):
        n = self.chips
        half = n // 2
        cut = half_cut(local[half].shape[0])

        def add(got, mine):
            return (got.astype(f32) + mine.astype(f32)).astype(bf16)

        fwd, back = self.hop(local[half][:cut], 1), self.hop(local[half][cut:], -1)
        for s in range(1, half):
            mine_f, mine_b = local[half + s], local[half - s]
            if s == 1:
                mine_f = jnp.concatenate([add(fwd, mine_f[:cut]), mine_f[cut:]], 0)
                mine_b = jnp.concatenate([mine_b[:cut], add(back, mine_b[cut:])], 0)
            else:
                mine_f, mine_b = add(fwd, mine_f), add(back, mine_b)
            fwd, back = self.hop(mine_f, 1), self.hop(mine_b, -1)
        return [local[0], fwd, back]

    def ring_sum(self, terms):
        half = self.chips // 2
        fwd, back = self.hop(terms[half], 1), self.hop(terms[half - 1], -1)

        def add(got, slot):
            return (got.astype(f32) + terms[slot].astype(f32)).astype(bf16)

        for s in range(1, half):
            fwd = self.hop(add(fwd, half + s), 1)
            if s < half - 1:
                back = self.hop(add(back, half - 1 - s), -1)
        return fwd, back

    def gather_placed(self, x, place, rest):
        n = self.chips
        half = n // 2
        fwd = back = x
        placed = None
        waiting = ([0], [(x, self.swap(x))])
        for s in range(1, half + 1):
            if s > 1:
                placed, token = place(*waiting, placed)
                fwd, back = gate(token, fwd, back)
                waiting = ([s - 1, n - s + 1], [(fwd, self.swap(fwd)), (back, self.swap(back))])
            if s < half:
                fwd, back = self.hop(fwd, 1), self.hop(back, -1)
            else:
                cut = half_cut(fwd.shape[0])
                fwd, back = self.hop(fwd[:cut], 1), self.hop(back[cut:], -1)
        placed, token = place(*waiting, placed)
        far = join(fwd, back, token)
        return place([half], [(far, self.swap(far))], placed, rest)[0]


VMEM_BYTES = 56 * 1024 * 1024
KEYS = 256
RING_ROWS = 152


def full_spec(shape):
    return pl.BlockSpec(shape, lambda: (0,) * len(shape))


def call(kernel, outs, args, smem=0, scratch=(), flops=0, loose=0):
    tight = len(args) - loose
    specs = [pl.BlockSpec(memory_space=pltpu.SMEM)] * smem
    specs += [pl.BlockSpec(memory_space=pltpu.VMEM)] * (tight - smem)
    specs += [pl.BlockSpec(memory_space=pl.ANY)] * loose

    def body(*refs):
        kernel(*refs[:tight], *refs[tight + loose :])

    moved = sum(x.size * x.dtype.itemsize for x in list(args) + list(outs))
    return pl.pallas_call(
        body,
        out_shape=list(outs),
        in_specs=specs,
        out_specs=[pl.BlockSpec(memory_space=pltpu.VMEM)] * len(outs),
        scratch_shapes=list(scratch),
        compiler_params=pltpu.CompilerParams(vmem_limit_bytes=VMEM_BYTES),
        cost_estimate=pl.CostEstimate(flops=flops, bytes_accessed=moved, transcendentals=0),
    )(*args)


def lanes(shape):
    return lax.broadcasted_iota(jnp.int32, shape, len(shape) - 1)


def dot_nt(a, b, precision=None):
    return lax.dot_general(
        a, b, (((1,), (1,)), ((), ())), preferred_element_type=f32, precision=precision
    )


def dot_tn(a, b):
    return lax.dot_general(a, b, (((0,), (0,)), ((), ())), preferred_element_type=f32)


def gate(token, *blocks):
    count = len(blocks)
    anywhere = pl.BlockSpec(memory_space=pl.ANY)

    def kernel(*refs):
        return None

    return pl.pallas_call(
        kernel,
        out_shape=[jax.ShapeDtypeStruct(x.shape, x.dtype) for x in blocks],
        in_specs=[anywhere] * (count + 1),
        out_specs=[anywhere] * count,
        input_output_aliases={i + 1: i for i in range(count)},
        cost_estimate=pl.CostEstimate(flops=0, bytes_accessed=1024, transcendentals=0),
    )(token, *blocks)


def join(first, second, token):
    cut = first.shape[0]

    def kernel(first_ref, second_ref, out_ref):
        out_ref[:cut, :] = first_ref[...]
        out_ref[cut:, :] = second_ref[...]

    shape = (cut + second.shape[0], first.shape[1])
    return call(
        kernel, [jax.ShapeDtypeStruct(shape, first.dtype)], [first, second, token], loose=1
    )[0]


def ring_end(fwd, back, term, split):
    rows, columns = term.shape

    def kernel(fwd_ref, back_ref, term_ref, first_ref, rest_ref):
        for ref, here in ((first_ref, slice(0, split)), (rest_ref, slice(split, rows))):
            total = fwd_ref[here, :].astype(f32) + back_ref[here, :].astype(f32)
            ref[...] = (total + term_ref[here, :].astype(f32)).astype(bf16)

    outs = [
        jax.ShapeDtypeStruct((split, columns), bf16),
        jax.ShapeDtypeStruct((rows - split, columns), bf16),
    ]
    return call(kernel, outs, [fwd, back, term])


def pair_kernel(mine_ref, got_ref, *out_refs):
    rows = out_refs[0].shape[0]
    for s, out_ref in enumerate(out_refs):
        here = slice(s * rows, (s + 1) * rows)
        out_ref[...] = (mine_ref[here, :] + got_ref[here, :].astype(f32)).astype(out_ref.dtype)


def block_kernel(mlp_ref, down_ref, *refs):
    small = refs[0][...].astype(f32)
    for ref in refs[1:-1]:
        small = small + ref[...].astype(f32)
    out_ref = refs[-1]
    top = mlp_ref.shape[0]
    piece = small.shape[0]
    out_ref[:top, :] = mlp_ref[...]
    out_ref[top : top + piece, :] = small.astype(bf16)
    out_ref[top + piece :, :] = down_ref[...]


def qkv_kernel(x_ref, gain_ref, w_ref, b_ref, cos_ref, sin_ref, norm_ref, q_ref, pair_ref):
    x = x_ref[...].astype(f32)
    inverse = lax.rsqrt(jnp.mean(x * x, -1, keepdims=True) + EPS)
    normed = (x * inverse * gain_ref[...]).astype(bf16)
    norm_ref[...] = normed
    joint = jnp.dot(normed, w_ref[...], preferred_element_type=f32) + b_ref[...]
    cosine = cos_ref[...]
    sine = sin_ref[...]
    early = lanes(cosine.shape) % HD < HD // 2
    for i in range((WIDTH_Q + WIDTH_K) // 128):
        tile = joint[:, i * 128 : (i + 1) * 128]
        turned = jnp.where(early, -pltpu.roll(tile, 96, 1), pltpu.roll(tile, 32, 1))
        turned = tile * cosine + turned * sine
        if i * 128 < WIDTH_Q:
            q_ref[:, i * 128 : (i + 1) * 128] = turned.astype(bf16)
        else:
            pair_ref[:, :WIDTH_K] = turned.astype(bf16)
    pair_ref[:, WIDTH_K:] = joint[:, WIDTH_Q + WIDTH_K :].astype(bf16)


def spread_heads(x, out_ref, factor):
    rows = x.shape[0]
    half = rows // 2
    for head in range(QH):
        kh, g = divmod(head, GROUP)
        tile = x[:, (head // 2) * 128 : (head // 2 + 1) * 128].astype(f32)
        if head % 2 != kh:
            tile = pltpu.roll(tile, HD, 1)
        tile = jnp.where(lanes(tile.shape) // HD == kh, tile * factor, 0.0).astype(out_ref.dtype)
        for part in range(2):
            start = (part * GROUP + g) * half
            out_ref[kh, start : start + half, :] = tile[part * half : (part + 1) * half]


def join_heads(src_ref, half, tile):
    sides = []
    for side in range(2):
        kh, g = divmod(2 * tile + side, GROUP)
        parts = [
            src_ref[kh, (part * GROUP + g) * half : (part * GROUP + g + 1) * half, :]
            for part in range(2)
        ]
        both = jnp.concatenate(parts, 0)
        sides.append(both if side == kh else pltpu.roll(both, HD, 1))
    return jnp.where(lanes(sides[0].shape) < HD, sides[0], sides[1])


def forward_kernel(
    ctx, meta_ref, q_ref, mine_ref, other_ref, x_ref, w_ref, gain_ref,
    low_ref, o_ref, lse_ref, spread_ref, k_ref, v_ref, hidden_ref, normed_ref,
    s_ref, max_ref, sum_ref,
):
    rows = q_ref.shape[0]
    half = rows // 2
    part_rows = GROUP * half
    me = meta_ref[0]
    chips = ctx // 2
    for j in range(ctx):
        src = mine_ref if j < chips else other_ref
        at = (j % chips) * rows
        owner = meta_ref[1 + j]
        for part in range(2):
            place = owner if part == 0 else 2 * ctx - 1 - owner
            to = pl.ds(pl.multiple_of(place * half, half), half)
            block = src[at + part * half : at + (part + 1) * half, :]
            k_ref[to, :] = block[:, :WIDTH_K]
            v_ref[to, :] = block[:, WIDTH_K:]
    spread_heads(q_ref[...], spread_ref, HD ** (-0.5))
    for part in range(2):
        span = slice(part * part_rows, (part + 1) * part_rows)
        start = (me if part == 0 else 2 * ctx - 1 - me) * half
        last = start // KEYS

        def keys_of(ref, i):
            return ref[pl.ds(pl.multiple_of(i * KEYS, KEYS), KEYS), :]

        for kh in range(KH):
            scores = dot_nt(spread_ref[kh, span, :], keys_of(k_ref, last))
            row = lax.broadcasted_iota(jnp.int32, scores.shape, 0) % half + start
            scores = jnp.where(lanes(scores.shape) + last * KEYS <= row, scores, -1e30)
            s_ref[kh, last] = scores
            max_ref[kh] = jnp.maximum(scores[:, :128], scores[:, 128:])

        def score(i, carry):
            for kh in range(KH):
                s = dot_nt(spread_ref[kh, span, :], keys_of(k_ref, i))
                s_ref[kh, i] = s
                max_ref[kh] = jnp.maximum(max_ref[kh], jnp.maximum(s[:, :128], s[:, 128:]))
            return carry

        lax.fori_loop(0, last, score, 0)
        for kh in range(KH):
            top = jnp.max(max_ref[kh], -1, keepdims=True)
            max_ref[kh] = jnp.broadcast_to(top, (part_rows, 128))
            sum_ref[kh] = jnp.zeros((part_rows, 128), f32)
            o_ref[kh, span, :] = jnp.zeros((part_rows, 128), f32)

        def weigh(i, carry):
            for kh in range(KH):
                s = s_ref[kh, i]
                top = max_ref[kh]
                left = jnp.exp(s[:, :128] - top)
                right = jnp.exp(s[:, 128:] - top)
                sum_ref[kh] += left + right
                o_ref[kh, span, :] += jnp.dot(
                    jnp.concatenate([left, right], 1).astype(bf16),
                    keys_of(v_ref, i),
                    preferred_element_type=f32,
                )
            return carry

        lax.fori_loop(0, last + 1, weigh, 0)
        for kh in range(KH):
            total = jnp.sum(sum_ref[kh], -1, keepdims=True)
            o_ref[kh, span, :] = o_ref[kh, span, :] / total
            lse_ref[kh, part] = dot_nt(
                jnp.full((8, 128), 1.0 / 128, f32),
                max_ref[kh] + jnp.log(total),
                lax.Precision.HIGHEST,
            )
    for tile in range(WIDTH_Q // 128):
        low_ref[:, tile * 128 : (tile + 1) * 128] = join_heads(o_ref, half, tile).astype(bf16)
    hidden = x_ref[...].astype(f32) + jnp.dot(low_ref[...], w_ref[...], preferred_element_type=f32)
    hidden_ref[...] = hidden
    inverse = lax.rsqrt(jnp.mean(hidden * hidden, -1, keepdims=True) + EPS)
    normed_ref[...] = (hidden * inverse * gain_ref[...]).astype(bf16)


def turn_back(grad, cos_ref, sin_ref):
    scaled = grad * sin_ref[...]
    early = lanes(grad.shape) % HD < HD // 2
    turned = jnp.where(early, pltpu.roll(scaled, 96, 1), -pltpu.roll(scaled, 32, 1))
    return grad * cos_ref[...] + turned


def backward_kernel(
    ctx, meta_ref, gn_ref, hidden_ref, gout_ref, gain_ref, w_ref, spread_ref, k_ref, v_ref, lse_ref,
    o_ref, cos_ref, sin_ref,
    gh_ref, ga_ref, gain_grad_ref, gq_ref, mine_ref, other_ref,
    go_ref, gqs_ref, gk_ref, gv_ref,
):
    rows = gn_ref.shape[0]
    half = rows // 2
    part_rows = GROUP * half
    me = meta_ref[0]
    chips = ctx // 2
    hidden = hidden_ref[...]
    inverse = lax.rsqrt(jnp.mean(hidden * hidden, -1, keepdims=True) + EPS)
    unit = hidden * inverse
    grad = gn_ref[...]
    gain_grad_ref[...] = jnp.sum(grad * unit, 0, keepdims=True)
    scaled = grad * gain_ref[...]
    gh = gout_ref[...].astype(f32) + inverse * (
        scaled - unit * jnp.mean(scaled * unit, -1, keepdims=True)
    )
    gh_ref[...] = gh
    ga = gh.astype(bf16)
    ga_ref[...] = ga
    spread_heads(dot_nt(ga, w_ref[...]).astype(bf16), go_ref, 1.0)
    gqs_ref[...] = jnp.zeros_like(gqs_ref)
    gk_ref[...] = jnp.zeros_like(gk_ref)
    gv_ref[...] = jnp.zeros_like(gv_ref)
    for part in range(2):
        span = slice(part * part_rows, (part + 1) * part_rows)
        start = (me if part == 0 else 2 * ctx - 1 - me) * half
        last = start // KEYS
        deltas = [
            dot_nt(
                jnp.ones((8, 128), f32),
                go_ref[kh, span, :].astype(f32) * o_ref[kh, span, :],
                lax.Precision.HIGHEST,
            )[:1]
            for kh in range(KH)
        ]

        def step(i, masked):
            at = pl.ds(pl.multiple_of(i * KEYS, KEYS), KEYS)
            keys = k_ref[at, :]
            grad_k = gk_ref[at, :]
            grad_v = gv_ref[at, :]
            for kh in range(KH):
                queries = spread_ref[kh, span, :]
                heads = go_ref[kh, span, :]
                p = jnp.exp(dot_nt(keys, queries) - lse_ref[kh, part][:1])
                if masked:
                    row = lanes(p.shape) % half + start
                    key = lax.broadcasted_iota(jnp.int32, p.shape, 0) + i * KEYS
                    p = jnp.where(key <= row, p, 0.0)
                gs = (p * (dot_nt(v_ref[at, :], heads) - deltas[kh])).astype(bf16)
                grad_v += jnp.dot(p.astype(bf16), heads, preferred_element_type=f32)
                grad_k += jnp.dot(gs, queries, preferred_element_type=f32)
                gqs_ref[kh, span, :] += dot_tn(gs, keys)
            gk_ref[at, :] = grad_k
            gv_ref[at, :] = grad_v

        def body(i, carry):
            step(i, False)
            return carry

        lax.fori_loop(0, last, body, 0)
        step(last, True)
    for tile in range(WIDTH_Q // 128):
        grad = join_heads(gqs_ref, half, tile) * HD ** (-0.5)
        gq_ref[:, tile * 128 : (tile + 1) * 128] = turn_back(grad, cos_ref, sin_ref).astype(bf16)
    for j in range(ctx):
        dst = mine_ref if j < chips else other_ref
        at = (j % chips) * rows
        owner = meta_ref[1 + j]
        for part in range(2):
            place = owner if part == 0 else 2 * ctx - 1 - owner
            frm = pl.ds(pl.multiple_of(place * half, half), half)
            to = slice(at + part * half, at + (part + 1) * half)
            dst[to, :WIDTH_K] = gk_ref[frm, :].astype(dst.dtype)
            dst[to, WIDTH_K:] = gv_ref[frm, :].astype(dst.dtype)


SUM_ROWS = 16


def finish_kernel(
    gq_ref, x_ref, gain_ref, w_ref, cos_ref, sin_ref, gh_ref, gain_two_ref, *refs
):
    sent_ref, gx_ref, gain_grad_ref, bias_ref = refs[-4:]
    pair = refs[0][...]
    for ref in refs[1:-4]:
        pair = pair + ref[...].astype(f32)
    rows = pair.shape[0]
    keys = turn_back(pair[:, :WIDTH_K], cos_ref, sin_ref)
    pair = jnp.concatenate([keys, pair[:, WIDTH_K:]], 1).astype(bf16)
    sent_ref[:rows, :] = pair
    joint = jnp.concatenate([gq_ref[...], pair], 1)
    bias = jnp.sum(joint.astype(f32), 0, keepdims=True)
    bias_ref[...] = bias
    grad = dot_nt(joint, w_ref[...])
    x = x_ref[...].astype(f32)
    inverse = lax.rsqrt(jnp.mean(x * x, -1, keepdims=True) + EPS)
    unit = x * inverse
    gain = jnp.sum(grad * unit, 0, keepdims=True)
    gain_grad_ref[...] = gain
    scaled = grad * gain_ref[...]
    gx_ref[...] = gh_ref[...] + inverse * (
        scaled - unit * jnp.mean(scaled * unit, -1, keepdims=True)
    )
    sums = jnp.concatenate([gain, gain_two_ref[...], bias], 1)
    width = pair.shape[1]
    sums = jnp.concatenate([sums, jnp.zeros((1, -sums.shape[1] % width), f32)], 1)
    found = [sums[:, i : i + width] for i in range(0, sums.shape[1], width)]
    found += [jnp.zeros((1, width), f32)] * (SUM_ROWS - len(found))
    sums = jnp.concatenate(found, 0)
    high = sums.astype(bf16)
    sent_ref[rows : rows + SUM_ROWS, :] = high
    sent_ref[rows + SUM_ROWS :, :] = (sums - high.astype(f32)).astype(bf16)


def pair_grad_kernel(rows, half_width, meta_ref, norm_ref, own_ref, peer_ref, out_ref, turned_ref):
    turned_ref[...] = norm_ref[:, D:].T
    first = pl.multiple_of(meta_ref[0] * half_width, 16)
    both = jnp.concatenate([own_ref[:rows, :], peer_ref[:rows, :]], 0)
    part = jnp.dot(turned_ref[pl.ds(first, half_width), :], both, preferred_element_type=f32)
    out_ref[:half_width, :] = part.astype(bf16)

    def sums(ref):
        high = ref[rows : rows + SUM_ROWS, :].astype(f32)
        return high + ref[rows + SUM_ROWS :, :].astype(f32)

    out_ref[half_width:, :] = (sums(own_ref) + sums(peer_ref)).astype(bf16)


def mlp_kernel(
    half_rows, spots_ref, x_a, x_b, gy_a, gy_b, gate_a, gate_b, up_a, up_b, down_a, down_b,
    xt_ref, midt_ref, gg_ref, gu_ref, gx_ref, out_ref, send_ref,
    x_all, gy_all, wg_all, wu_all, wd_all, mid_all, gg_all, gu_all,
):
    step = pl.program_id(0)

    @pl.when(step == 0)
    def start():
        x_all[:half_rows] = x_a[...]
        x_all[half_rows:] = x_b[...]
        gy_all[:half_rows] = gy_a[...]
        gy_all[half_rows:] = gy_b[...]
        xt_ref[...] = x_all[...].T

    here = pl.ds(pl.multiple_of(step * 256, 256), 256)
    wg = jnp.concatenate([gate_a[...], gate_b[...]], 1)
    wu = jnp.concatenate([up_a[...], up_b[...]], 1)
    wd = jnp.concatenate([down_a[...], down_b[...]], 0)
    wg_all[:, here] = wg
    wu_all[:, here] = wu
    wd_all[here, :] = wd
    core = spots_ref[1]
    column = lanes((1, 256)) + (step * 256 + spots_ref[2])
    own = (column < spots_ref[3]) == (core == 0)
    x = x_all[...]
    gate = jnp.dot(x, wg, preferred_element_type=f32)
    up = jnp.dot(x, wu, preferred_element_type=f32)
    grad = jnp.where(own, dot_nt(gy_all[...], wd), 0.0)
    sigma = jax.nn.sigmoid(gate)
    active = gate * sigma
    middle = jnp.where(own, active * up, 0.0).astype(bf16)
    grad_gate = (grad * up * (sigma + active * (1.0 - sigma))).astype(bf16)
    grad_up = (grad * active).astype(bf16)
    midt_ref[...] = middle.T
    gg_ref[...] = grad_gate
    gu_ref[...] = grad_up
    mid_all[:, here] = middle
    gg_all[:, here] = grad_gate
    gu_all[:, here] = grad_up

    @pl.when(step == pl.num_programs(0) - 1)
    def end():
        gx = dot_nt(gg_all[...], wg_all[...]) + dot_nt(gu_all[...], wu_all[...])
        gx_ref[...] = gx[:half_rows]
        send_ref[:half_rows] = gx[half_rows:].astype(bf16)
        out = jnp.dot(mid_all[...], wd_all[...], preferred_element_type=f32)
        out_ref[...] = out[:half_rows]
        send_ref[half_rows:] = out[half_rows:].astype(bf16)


def feed_forward(meta, x, early, w_gate, w_up, w_down, width):
    half = x[0].shape[0]
    tokens = 2 * half
    steps = width // 256
    tiles = width // 128 - 1

    def columns(j):
        return pl.BlockSpec((D, 128), lambda i, m: (0, m[1] * tiles + 2 * i + j))

    def rows(j):
        return pl.BlockSpec((128, D), lambda i, m: (m[1] * tiles + 2 * i + j, 0))

    whole = pl.BlockSpec((tokens, D), lambda i, m: (0, 0))
    halves = pl.BlockSpec((half, D), lambda i, m: (0, 0))
    tile = pl.BlockSpec((tokens, 256), lambda i, m: (0, i))
    hidden = jax.ShapeDtypeStruct((tokens, width), bf16)
    return pl.pallas_call(
        lambda *refs: mlp_kernel(half, *refs),
        out_shape=[
            jax.ShapeDtypeStruct((D, tokens), bf16),
            jax.ShapeDtypeStruct((width, tokens), bf16),
            hidden,
            hidden,
            jax.ShapeDtypeStruct((half, D), f32),
            jax.ShapeDtypeStruct((half, D), f32),
            jax.ShapeDtypeStruct((tokens, D), bf16),
        ],
        grid_spec=pltpu.PrefetchScalarGridSpec(
            num_scalar_prefetch=1,
            grid=(steps,),
            in_specs=[halves] * 4
            + [columns(0), columns(1), columns(0), columns(1), rows(0), rows(1)],
            out_specs=[
                pl.BlockSpec((D, tokens), lambda i, m: (0, 0)),
                pl.BlockSpec((256, tokens), lambda i, m: (i, 0)),
                tile,
                tile,
                halves,
                halves,
                whole,
            ],
            scratch_shapes=[pltpu.VMEM((tokens, D), bf16)] * 2
            + [pltpu.VMEM((D, width), bf16)] * 2
            + [pltpu.VMEM((width, D), bf16)]
            + [pltpu.VMEM((tokens, width), bf16)] * 3,
        ),
        compiler_params=pltpu.CompilerParams(vmem_limit_bytes=VMEM_BYTES),
        cost_estimate=pl.CostEstimate(
            flops=12 * tokens * width * D, bytes_accessed=6 * width * D, transcendentals=0
        ),
    )(meta, *x, *early, w_gate, w_gate, w_up, w_up, w_down, w_down)


def mlp_grad_kernel(chips, down_rows, main, meta_ref, xt_ref, gy_a, gy_b, midt_ref, gg_ref, gu_ref, *refs):
    out_refs = refs[:chips]
    mlp_acc, down_acc, blocks, sems = refs[chips:]
    core = meta_ref[1]
    at_main = pl.ds(pl.multiple_of(core * 128, 128), main)
    at_tile = pl.ds(pl.multiple_of((1 - core) * main, 128), 128)
    xt = xt_ref[...]
    mlp_acc[:, :main] = jnp.dot(xt, gg_ref[:, at_main], preferred_element_type=f32).astype(bf16)
    mlp_acc[:, main : 2 * main] = jnp.dot(
        xt, gu_ref[:, at_main], preferred_element_type=f32
    ).astype(bf16)
    mixed = gg_ref[:, at_tile].astype(f32) + pltpu.roll(gu_ref[:, at_tile].astype(f32), 64, 1)
    mlp_acc[:, 2 * main :] = jnp.dot(
        xt, mixed.astype(bf16), preferred_element_type=f32
    ).astype(bf16)
    gy = jnp.concatenate([gy_a[:, :D], gy_b[:, :D]], 0)
    down_acc[...] = jnp.dot(midt_ref[...], gy, preferred_element_type=f32)

    mlp_rows = mlp_acc.shape[0] // chips
    columns = mlp_acc.shape[1] // 128
    half = chips // 2
    copies = []
    for slot in sorted(range(chips), key=lambda s: abs(s - half) if s else chips):
        owner = meta_ref[12 + slot]
        block = mlp_acc[pl.ds(pl.multiple_of(owner * mlp_rows, 16), mlp_rows), :]
        for j in range(columns):
            for i in range(mlp_rows // 16):
                blocks[slot, j * 16 : (j + 1) * 16, i * 128 : (i + 1) * 128] = block[
                    i * 16 : (i + 1) * 16, j * 128 : (j + 1) * 128
                ]
        first = pl.multiple_of(core * 64 + owner * down_rows, 8)
        blocks[slot, columns * 16 :, :] = down_acc[pl.ds(first, down_rows), :].astype(bf16)
        copy = pltpu.make_async_copy(blocks.at[slot], out_refs[slot], sems.at[slot])
        copy.start()
        copies.append(copy)
    for copy in copies:
        copy.wait()


def mlp_gradients(meta, xt, early, midt, gg, gu, after, chips, down_rows, main):
    tokens = gg.shape[0]
    columns = (2 * main + 128) // 128
    rows = columns * 16 + down_rows
    args = [meta, xt, *early, midt, gg, gu]
    anywhere = pl.BlockSpec(memory_space=pl.ANY)

    def kernel(*refs):
        mlp_grad_kernel(chips, down_rows, main, *refs[: len(args)], *refs[len(args) + 1 :])

    return pl.pallas_call(
        kernel,
        out_shape=[jax.ShapeDtypeStruct((rows, D), bf16)] * chips,
        in_specs=[pl.BlockSpec(memory_space=pltpu.SMEM)]
        + [pl.BlockSpec(memory_space=pltpu.VMEM)] * (len(args) - 1)
        + [anywhere],
        out_specs=[anywhere] * chips,
        scratch_shapes=[
            pltpu.VMEM((D, columns * 128), bf16),
            pltpu.VMEM((midt.shape[0], D), f32),
            pltpu.VMEM((chips, rows, D), bf16),
            pltpu.SemaphoreType.DMA((chips,)),
        ],
        compiler_params=pltpu.CompilerParams(vmem_limit_bytes=VMEM_BYTES),
        cost_estimate=pl.CostEstimate(
            flops=6 * tokens * midt.shape[0] * D, bytes_accessed=4 * chips * rows * D,
            transcendentals=0,
        ),
    )(*args, after)


def small_grad_kernel(
    chips, q_rows, rows, cols, meta_ref, norm_a, norm_b, att_a, att_b, near_a, near_b, *refs
):
    out_refs, acc, turned_ref = refs[:-2], refs[-2], refs[-1]
    first = pl.multiple_of((2 * meta_ref[0] + meta_ref[1]) * q_rows, 16)
    grads, queries = [], []
    for near_ref in (near_a, near_b):
        for b in range(2):
            grads.append(near_ref[2 * b * rows : (2 * b + 1) * rows, :])
            queries.append(near_ref[(2 * b + 1) * rows : (2 * b + 2) * rows, :])
    turned_ref[...] = jnp.concatenate([norm_a[:, D:], norm_b[:, D:]], 0).T
    acc[:, :WIDTH_Q] = jnp.dot(
        turned_ref[pl.ds(first, q_rows), :],
        jnp.concatenate(queries, 0),
        preferred_element_type=f32,
    ).astype(bf16)
    acc[:, WIDTH_Q:cols] = jnp.zeros((q_rows, cols - WIDTH_Q), bf16)
    turned_ref[...] = jnp.concatenate([att_a[...], att_b[...]], 0).T
    acc[:, cols:] = jnp.dot(
        turned_ref[pl.ds(first, q_rows), :], jnp.concatenate(grads, 0), preferred_element_type=f32
    ).astype(bf16)
    width = acc.shape[1] // chips
    for out_ref, slot in zip(out_refs, range(chips)):
        owner = meta_ref[12 + slot]
        block = acc[:, pl.ds(pl.multiple_of(owner * width, 128), width)]
        tall = jnp.concatenate([block[:, i * 128 : (i + 1) * 128] for i in range(width // 128)], 0)
        piece = out_ref.shape[0]
        for i in range(D // 128):
            out_ref[:, i * 128 : (i + 1) * 128] = tall[i * piece : (i + 1) * piece]


def place_all(meta, slots, pairs, old, sizes, rest=None):
    main, ff_loc, q_rows, cols, down_rows, chips = sizes
    mlp_rows = D // chips
    columns = (2 * main + 128) // 128
    tiles = main // 128
    lanes_out = D // 128
    top = columns * 16
    blocks = [x for pair in pairs for x in pair]
    count = len(blocks)
    piece = blocks[0].shape[0] - top - down_rows
    parts = (cols + D) // chips // 128
    keep = [] if old is None else list(old)
    last = [] if rest is None else [rest]
    known = WIDTH_Q // 128

    def kernel(meta_ref, *refs):
        ins = refs[:count]
        outs_at = count + len(last) + len(keep)
        gate_out, up_out, down_out, joint_out, proj_out, token_ref = refs[outs_at : outs_at + 6]
        gate_buf, up_buf, down_buf, small_buf, rest_buf, sems, small_sems, rest_sem = refs[
            outs_at + 6 :
        ]
        core_zero = meta_ref[1] == 0
        copies = []

        def send(src, dst, sem):
            copy = pltpu.make_async_copy(src, dst, sem)
            copy.start()
            copies.append(copy)

        def column(ref, j):
            found = [
                ref[j * 16 : (j + 1) * 16, i * 128 : (i + 1) * 128] for i in range(mlp_rows // 16)
            ]
            return jnp.concatenate(found, 0).astype(f32)

        for k, slot in enumerate(slots):
            for j in range(columns):
                got = column(ins[2 * k], j)
                other = column(ins[2 * k + 1], j)
                zero = jnp.where(core_zero, got, other)
                one = jnp.where(core_zero, other, got)
                if j < 2 * tiles:
                    buf = gate_buf if j < tiles else up_buf
                    at = (j % tiles) * 128
                    buf[k, :, at : at + 128] = zero
                    buf[k, :, at + main + 128 : at + main + 256] = one
                else:
                    left = lanes(zero.shape) < 64
                    gate_buf[k, :, main : main + 128] = jnp.where(left, zero, one)
                    up_buf[k, :, main : main + 128] = pltpu.roll(jnp.where(left, one, zero), 64, 1)
            owner = meta_ref[12 + slot]
            here = pl.ds(pl.multiple_of(owner * mlp_rows, 8), mlp_rows)
            send(gate_buf.at[k], gate_out.at[here, :], sems.at[4 * k])
            send(up_buf.at[k], up_out.at[here, :], sems.at[4 * k + 1])
            for side in range(2):
                b = 2 * k + side
                core = meta_ref[1] if side == 0 else 1 - meta_ref[1]
                down_buf[b] = ins[b][top + piece :, :].astype(f32)
                here = pl.ds(pl.multiple_of((core * chips + owner) * down_rows, 8), down_rows)
                send(down_buf.at[b], down_out.at[here, :], sems.at[4 * k + 2 + side])
                tall = jnp.concatenate(
                    [ins[b][top : top + piece, i * 128 : (i + 1) * 128] for i in range(lanes_out)], 0
                ).astype(f32)
                rows = pl.ds(pl.multiple_of(core * q_rows, 8), q_rows)
                for i in range(parts):
                    small_buf[b, i] = tall[i * q_rows : (i + 1) * q_rows]
                    block = owner * parts + i

                    @pl.when(block < known)
                    def joint(b=b, i=i, rows=rows, block=block):
                        at = pl.ds(pl.multiple_of(block * 128, 128), 128)
                        pltpu.make_async_copy(
                            small_buf.at[b, i], joint_out.at[rows, at], small_sems.at[b, i]
                        ).start()

                    @pl.when(block >= cols // 128)
                    def proj(b=b, i=i, rows=rows, block=block):
                        at = pl.ds(pl.multiple_of((block - cols // 128) * 128, 128), 128)
                        pltpu.make_async_copy(
                            small_buf.at[b, i], proj_out.at[rows, at], small_sems.at[b, i]
                        ).start()

        token_ref[...] = jnp.zeros(token_ref.shape, f32)
        if last:
            rest_buf[...] = refs[count][: 2 * q_rows, :].astype(f32)
            send(rest_buf, joint_out.at[:, WIDTH_Q:cols], rest_sem)
        for copy in copies:
            copy.wait()
        for b in range(count):
            for i in range(parts):
                block = meta_ref[12 + slots[b // 2]] * parts + i

                @pl.when((block < known) | (block >= cols // 128))
                def done(b=b, i=i):
                    pltpu.make_async_copy(
                        small_buf.at[b, i],
                        proj_out.at[pl.ds(0, q_rows), pl.ds(0, 128)],
                        small_sems.at[b, i],
                    ).wait()

    anywhere = pl.BlockSpec(memory_space=pl.ANY)
    result = pl.pallas_call(
        kernel,
        out_shape=[
            jax.ShapeDtypeStruct((D, ff_loc), f32),
            jax.ShapeDtypeStruct((D, ff_loc), f32),
            jax.ShapeDtypeStruct((ff_loc, D), f32),
            jax.ShapeDtypeStruct((2 * q_rows, cols), f32),
            jax.ShapeDtypeStruct((2 * q_rows, D), f32),
            jax.ShapeDtypeStruct((8, 128), f32),
        ],
        in_specs=[pl.BlockSpec(memory_space=pltpu.SMEM)]
        + [pl.BlockSpec(memory_space=pltpu.VMEM)] * (count + len(last))
        + [anywhere] * len(keep),
        out_specs=[anywhere] * 5 + [pl.BlockSpec(memory_space=pltpu.VMEM)],
        scratch_shapes=[
            pltpu.VMEM((len(slots), mlp_rows, ff_loc), f32),
            pltpu.VMEM((len(slots), mlp_rows, ff_loc), f32),
            pltpu.VMEM((count, down_rows, D), f32),
            pltpu.VMEM((count, parts, q_rows, 128), f32),
            pltpu.VMEM((2 * q_rows, cols - WIDTH_Q), f32),
            pltpu.SemaphoreType.DMA((4 * len(slots),)),
            pltpu.SemaphoreType.DMA((count, parts)),
            pltpu.SemaphoreType.DMA,
        ],
        input_output_aliases={1 + count + len(last) + i: i for i in range(len(keep))},
        compiler_params=pltpu.CompilerParams(vmem_limit_bytes=VMEM_BYTES),
        cost_estimate=pl.CostEstimate(
            flops=0, bytes_accessed=8 * sum(x.size for x in blocks), transcendentals=0
        ),
    )(meta, *blocks, *last, *keep)
    return list(result[:5]), result[5]


def place_blocks(blocks, spots, out_shape, old=None):
    shape = blocks[0].shape
    count = len(blocks)
    if shape[0] % 8 or shape[1] % 128:
        out = jnp.zeros(out_shape, f32) if old is None else old
        for block, (i, j) in zip(blocks, spots):
            out = lax.dynamic_update_slice(
                out, block.astype(f32), (i * shape[0], j * shape[1])
            )
        return out

    def kernel(spots_ref, *refs):
        step = pl.program_id(0)
        out_ref = refs[-1]
        for i in range(count):

            @pl.when(step == i)
            def write(i=i):
                out_ref[...] = refs[i][...].astype(f32)

    keep = [] if old is None else [old]
    return pl.pallas_call(
        kernel,
        out_shape=jax.ShapeDtypeStruct(out_shape, f32),
        grid_spec=pltpu.PrefetchScalarGridSpec(
            num_scalar_prefetch=1,
            grid=(count,),
            in_specs=[pl.BlockSpec(shape, lambda i, spots: (0, 0))] * count
            + [pl.BlockSpec(memory_space=pl.ANY)] * len(keep),
            out_specs=pl.BlockSpec(shape, lambda i, spots: (spots[i, 0], spots[i, 1])),
        ),
        input_output_aliases={} if old is None else {count + 1: 0},
        compiler_params=pltpu.CompilerParams(vmem_limit_bytes=VMEM_BYTES),
    )(jnp.stack([jnp.stack(s) for s in spots]).astype(jnp.int32), *blocks, *keep)


def local(tokens, w_qkv, b_qkv, w_out, gain_attn, gain_mlp, w_gate, w_up, w_down, cotangent):
    net = Net()
    rows = tokens.shape[1]
    half_rows = rows // 2
    ctx_count = net.ctx
    core = net.core
    chips = net.chips
    part_rows = GROUP * half_rows
    x = tokens[0]
    gain_one = gain_attn[None]
    gain_two = gain_mlp[None]

    w_qkv_full = net.full_rows(w_qkv)

    ff_loc = w_gate.shape[1]
    ff_half = ff_loc // 2
    main = (ff_half // 128) * 128
    rest = ff_half - main
    width = main + 2 * rest
    first = core * main
    tiled = net.dp == 2 and 2 * rest == 128 and width % 256 == 0 and chips == 8 and ff_half == chips * RING_ROWS
    ring = jnp.arange(chips, dtype=jnp.int32)
    owners_of = (net.pos - ring) % chips
    spots = jnp.concatenate(
        [jnp.stack([net.d, core, first, jnp.int32(ff_half)]), owners_of, owners_of]
    ).astype(jnp.int32)

    row_ids = jnp.arange(half_rows, dtype=jnp.int32)
    place = jnp.concatenate(
        [net.c * half_rows + row_ids, (2 * ctx_count - 1 - net.c) * half_rows + row_ids]
    )
    freq = ROPE_BASE ** (-((jnp.arange(128) % (HD // 2)).astype(f32) * (2.0 / HD)))
    angle = place.astype(f32)[:, None] * freq[None, :]
    cosine, sine = jnp.cos(angle), jnp.sin(angle)
    normed_one, queries, pairs = call(
        qkv_kernel,
        [
            jax.ShapeDtypeStruct((rows, D), bf16),
            jax.ShapeDtypeStruct((rows, WIDTH_Q), bf16),
            jax.ShapeDtypeStruct((rows, 2 * WIDTH_K), bf16),
        ],
        [x, gain_one, w_qkv_full, b_qkv[None], cosine, sine],
        flops=2 * rows * D * 1152,
    )

    slots = net.ring_gather(pairs)
    mine = jnp.concatenate(slots, 0)
    other = net.swap(mine)
    order = jnp.array(net.order, jnp.int32)
    chip_ids = order[(net.pos - jnp.arange(chips, dtype=jnp.int32)) % chips]
    meta = jnp.concatenate([net.c[None], 2 * chip_ids + core, 2 * chip_ids + 1 - core])
    meta = meta.astype(jnp.int32)

    late_w, late_g, late_n, unused = lax.optimization_barrier((w_out, cotangent[0], normed_one, pairs))
    w_out_full = net.full_rows(late_w)
    early = net.group_parts(jnp.concatenate([late_g, late_n], 1))

    total_keys = rows * ctx_count
    padded = (KH, 2 * part_rows, 128)
    attended_low, attended, lse, spread, keys, values, hidden, normed_two = call(
        lambda *refs: forward_kernel(ctx_count, *refs),
        [
            jax.ShapeDtypeStruct((rows, WIDTH_Q), bf16),
            jax.ShapeDtypeStruct(padded, f32),
            jax.ShapeDtypeStruct((KH, 2, 8, part_rows), f32),
            jax.ShapeDtypeStruct(padded, bf16),
            jax.ShapeDtypeStruct((total_keys, WIDTH_K), bf16),
            jax.ShapeDtypeStruct((total_keys, WIDTH_K), bf16),
            jax.ShapeDtypeStruct((rows, D), f32),
            jax.ShapeDtypeStruct((rows, D), bf16),
        ],
        [meta, queries, mine, other, x, w_out_full, gain_two],
        smem=1,
        scratch=[
            pltpu.VMEM((KH, total_keys // KEYS, part_rows, KEYS), f32),
            pltpu.VMEM((KH, part_rows, 128), f32),
            pltpu.VMEM((KH, part_rows, 128), f32),
        ],
        flops=8 * KH * part_rows * total_keys * 128,
    )

    normed_two_parts = net.group_parts(normed_two)
    chip_rows = net.dp * rows
    down_rows = ff_half // chips
    mlp_rows = D // chips
    if tiled:
        x_turned, mid_turned, gate_low, up_low, grad_mine, out_mine, sent = feed_forward(
            spots, normed_two_parts, early, w_gate, w_up, w_down, width
        )
    else:
        normed_two_group = jnp.concatenate(normed_two_parts, 0)
        grad_out_group = jnp.concatenate(early, 0)[:, :D]
        own_cols = (jnp.arange(width) + first < ff_half) == (core == 0)
        wg = lax.dynamic_slice(w_gate, (0, first), (D, width))
        wu = lax.dynamic_slice(w_up, (0, first), (D, width))
        wd = lax.dynamic_slice(w_down, (first, 0), (width, D))
        gate = jnp.dot(normed_two_group, wg, preferred_element_type=f32)
        upper = jnp.dot(normed_two_group, wu, preferred_element_type=f32)
        sigma = jax.nn.sigmoid(gate)
        activated = gate * sigma
        middle = jnp.where(own_cols, activated * upper, 0.0).astype(bf16)
        grad_middle = jnp.einsum("td,fd->tf", grad_out_group, wd, preferred_element_type=f32)
        slope = sigma * (1.0 + gate * (1.0 - sigma))
        grad_gate_low = jnp.where(own_cols, grad_middle * upper * slope, 0.0).astype(bf16)
        grad_up_low = jnp.where(own_cols, grad_middle * activated, 0.0).astype(bf16)

        grad_normed_two = jnp.einsum(
            "tf,df->td", grad_gate_low, wg, preferred_element_type=f32
        ) + jnp.einsum("tf,df->td", grad_up_low, wu, preferred_element_type=f32)
        mlp_out = jnp.dot(middle, wd, preferred_element_type=f32)
        grad_mine, out_mine = grad_normed_two[:chip_rows], mlp_out[:chip_rows]
        sent = jnp.concatenate([grad_normed_two[chip_rows:], mlp_out[chip_rows:]], 0).astype(bf16)
    swapped = net.swap(sent)
    grad_chip = grad_mine + swapped[:chip_rows].astype(f32)
    mlp_chip = out_mine + swapped[chip_rows:].astype(f32)
    grad_two = grad_chip[:rows]
    for s in range(1, net.dp):
        sent_two = grad_chip[s * rows : (s + 1) * rows].astype(bf16)
        grad_two = grad_two + net.shift(sent_two, net.dp - s).astype(f32)

    def attention_back():
        grad_hidden, grad_attn_low, grad_gain_two, grad_queries, terms_mine, terms_other = call(
            lambda *refs: backward_kernel(ctx_count, *refs),
            [
                jax.ShapeDtypeStruct((rows, D), f32),
                jax.ShapeDtypeStruct((rows, D), bf16),
                jax.ShapeDtypeStruct((1, D), f32),
                jax.ShapeDtypeStruct((rows, WIDTH_Q), bf16),
                jax.ShapeDtypeStruct((chips * rows, 2 * WIDTH_K), f32),
                jax.ShapeDtypeStruct((chips * rows, 2 * WIDTH_K), bf16),
            ],
            [
                meta, grad_two, hidden, cotangent[0], gain_two, w_out_full, spread, keys, values, lse,
                attended, cosine, sine,
            ],
            smem=1,
            scratch=[
                pltpu.VMEM(padded, bf16),
                pltpu.VMEM(padded, f32),
                pltpu.VMEM((total_keys, WIDTH_K), f32),
                pltpu.VMEM((total_keys, WIDTH_K), f32),
            ],
            flops=20 * KH * part_rows * total_keys * 128,
        )
        pair_sums = call(
            pair_kernel,
            [jax.ShapeDtypeStruct((rows, 2 * WIDTH_K), f32)]
            + [jax.ShapeDtypeStruct((rows, 2 * WIDTH_K), bf16)] * (chips - 1),
            [terms_mine, net.swap(terms_other)],
        )
        grad_pairs = net.ring_parts(pair_sums)

        def finish(*after):
            return call(
                finish_kernel,
                [
                    jax.ShapeDtypeStruct((rows + 2 * SUM_ROWS, 2 * WIDTH_K), bf16),
                    jax.ShapeDtypeStruct((rows, D), f32),
                    jax.ShapeDtypeStruct((1, D), f32),
                    jax.ShapeDtypeStruct((1, w_qkv.shape[1]), f32),
                ],
                [grad_queries, x, gain_one, w_qkv_full, cosine, sine, grad_hidden, grad_gain_two]
                + grad_pairs
                + list(after),
                loose=len(after),
            )

        return grad_attn_low, grad_gain_two, grad_queries, finish

    grad_attn_low, grad_gain_two, grad_queries, finish = attention_back()
    if tiled:
        terms = mlp_gradients(
            spots, x_turned, early, mid_turned, gate_low, up_low, sent_two, chips, down_rows, main
        )
        fwd, back = net.ring_sum(terms)
        sum_mlp, sum_down = ring_end(fwd, back, terms[0], terms[0].shape[0] - down_rows)
        pair_sent, grad_input, grad_gain_one, grad_bias = finish(sum_down)
    else:
        part_down = jnp.einsum(
            "tf,td->fd", middle, grad_out_group, preferred_element_type=f32
        ).astype(bf16)
        part_down = lax.dynamic_slice(part_down, (core * rest, 0), (ff_half, D))

        def down_chunk(slot):
            return lax.dynamic_slice(part_down, (net.owner(slot) * down_rows, 0), (down_rows, D))

        sum_down = net.ring_scatter([down_chunk(s) for s in range(chips)]).astype(bf16)

        def split_main(x):
            left = (x[:, :main], x[:, main:])
            right = (x[:, 2 * rest :], x[:, : 2 * rest])
            return (
                jnp.where(core == 0, left[0], right[0]),
                jnp.where(core == 0, left[1], right[1]),
            )

        gate_main, gate_tile = split_main(grad_gate_low)
        up_main, up_tile = split_main(grad_up_low)
        packed = jnp.concatenate(
            [gate_main, up_main, gate_tile + jnp.roll(up_tile, rest, 1)], 1
        )
        part_mlp = jnp.einsum(
            "td,tf->df", normed_two_group, packed, preferred_element_type=f32
        ).astype(bf16)

        def mlp_chunk(slot):
            return lax.dynamic_slice(
                part_mlp, (net.owner(slot) * mlp_rows, 0), (mlp_rows, 2 * ff_half)
            )

        sum_mlp = net.ring_scatter([mlp_chunk(s) for s in range(chips)]).astype(bf16)
        sum_mlp = lax.optimization_barrier(sum_mlp)
        pair_sent, grad_input, grad_gain_one, grad_bias = finish()

    out_sum = mlp_chip[:rows]
    for s in range(1, net.dp):
        got = net.shift(mlp_chip[s * rows : (s + 1) * rows].astype(bf16), net.dp - s)
        out_sum = out_sum + got.astype(f32)
    output = (hidden + out_sum).astype(bf16)
    near = net.group_parts(jnp.concatenate([grad_attn_low, grad_queries], 0))
    attended_parts = net.group_parts(attended_low)

    q_rows = w_qkv.shape[0] // 2
    qkv_cols = w_qkv.shape[1]
    if tiled:
        piece = q_rows * (qkv_cols + D) // chips // D
        terms_small = call(
            lambda *refs: small_grad_kernel(chips, q_rows, rows, qkv_cols, *refs),
            [jax.ShapeDtypeStruct((piece, D), bf16)] * chips,
            [spots, *early, *attended_parts, *near],
            smem=1,
            scratch=[
                pltpu.VMEM((q_rows, qkv_cols + D), bf16),
                pltpu.VMEM((D, 2 * chip_rows), bf16),
            ],
            flops=4 * chip_rows * D * (qkv_cols + D),
        )
        block = call(
            block_kernel,
            [jax.ShapeDtypeStruct((sum_mlp.shape[0] + piece + down_rows, D), bf16)],
            [sum_mlp, sum_down] + net.ring_parts(terms_small),
        )[0]
        part_pair = call(
            lambda *refs: pair_grad_kernel(rows, 2 * q_rows, *refs),
            [jax.ShapeDtypeStruct((2 * q_rows + SUM_ROWS, 2 * WIDTH_K), bf16)],
            [spots, early[0], pair_sent, net.shift(pair_sent, 1)],
            smem=1,
            scratch=[pltpu.VMEM((D, chip_rows), bf16)],
        )[0]
        grad_pair = lax.psum(part_pair, "ctx")
        small = grad_pair[2 * q_rows :].reshape(-1)[: 2 * D + qkv_cols].astype(f32)
        sizes = (main, ff_loc, q_rows, qkv_cols, down_rows, chips)
        grad_gate, grad_up, grad_down, grad_joint, grad_out_proj = net.gather_placed(
            block,
            lambda slots, pairs, old, rest=None: place_all(spots, slots, pairs, old, sizes, rest),
            grad_pair,
        )
    else:
        gathered = jnp.concatenate(near, 0).reshape(2 * net.dp, 2, rows, D)
        grad_attn_group = gathered[:, 0].reshape(2 * net.dp * rows, D)
        attended_group = jnp.concatenate(attended_parts, 0)
        normed_one_group = jnp.concatenate(early, 0)[:, D:]
        joint_group = net.group_gather(jnp.concatenate([grad_queries, pair_sent[:rows]], 1))
        q_first = net.d * (2 * q_rows) + core * q_rows
        group_rows = 2 * net.dp * rows
        part_out = jnp.einsum(
            "tc,td->cd",
            lax.dynamic_slice(attended_group, (0, q_first), (group_rows, q_rows)),
            grad_attn_group,
            preferred_element_type=f32,
        )
        part_joint = jnp.einsum(
            "td,tc->dc",
            lax.dynamic_slice(normed_one_group, (0, q_first), (group_rows, q_rows)),
            joint_group,
            preferred_element_type=f32,
        )
        part_small = jnp.concatenate([part_joint, part_out], 1).astype(bf16)
        small_cols = part_small.shape[1] // chips

        def small_chunk(slot):
            return lax.dynamic_slice(part_small, (0, net.owner(slot) * small_cols), (q_rows, small_cols))

        sum_small = net.ring_scatter([small_chunk(s) for s in range(chips)]).astype(bf16)

        tall = jnp.concatenate(
            [sum_small[:, i * 128 : (i + 1) * 128] for i in range(small_cols // 128)], 0
        )
        piece = tall.shape[0] // (D // 128)
        wide = jnp.concatenate([tall[i * piece : (i + 1) * piece] for i in range(D // 128)], 1)
        both = lax.optimization_barrier(jnp.concatenate([sum_down, wide], 0))

        owners = [net.owner(s) for s in range(chips)]
        got_mlp = net.ring_gather(sum_mlp)
        got_both = net.ring_gather(both)
        pairs_mlp = [(got, net.swap(got)) for got in got_mlp]
        pairs_both = [(got, net.swap(got)) for got in got_both]

        down_blocks, down_spots, small_blocks, small_spots = [], [], [], []
        for owner, pair in zip(owners, pairs_both):
            for which, got in zip((core, 1 - core), pair):
                down_blocks.append(got[:down_rows])
                down_spots.append((which * chips + owner, jnp.int32(0)))
                wide = got[down_rows:]
                tall = jnp.concatenate([wide[:, i * 128 : (i + 1) * 128] for i in range(D // 128)], 0)
                small_blocks.append(
                    jnp.concatenate(
                        [tall[i * q_rows : (i + 1) * q_rows] for i in range(small_cols // 128)], 1
                    )
                )
                small_spots.append((which, owner))
        grad_down = place_blocks(down_blocks, down_spots, (ff_loc, D))
        grad_small = place_blocks(small_blocks, small_spots, (2 * q_rows, part_small.shape[1]))
        grad_gate = jnp.zeros((D, ff_loc), f32)
        grad_up = jnp.zeros((D, ff_loc), f32)
        left_lane = jnp.arange(2 * rest) < rest
        for owner, (got, swapped) in zip(owners, pairs_mlp):
            zero = jnp.where(core == 0, got, swapped).astype(f32)
            one = jnp.where(core == 0, swapped, got).astype(f32)
            tile_zero, tile_one = zero[:, 2 * main :], one[:, 2 * main :]
            mid_gate = jnp.where(left_lane, tile_zero, tile_one)
            mid_up = jnp.roll(jnp.where(left_lane, tile_one, tile_zero), rest, 1)
            base = owner * mlp_rows
            grad_gate = lax.dynamic_update_slice(
                grad_gate, jnp.concatenate([zero[:, :main], mid_gate, one[:, :main]], 1), (base, 0)
            )
            grad_up = lax.dynamic_update_slice(
                grad_up,
                jnp.concatenate([zero[:, main : 2 * main], mid_up, one[:, main : 2 * main]], 1),
                (base, 0),
            )

        grad_joint, grad_out_proj = grad_small[:, :qkv_cols], grad_small[:, qkv_cols:]
        small = net.total(jnp.concatenate([grad_gain_one, grad_gain_two, grad_bias], 1))[0]
    return (
        output[None],
        grad_input[None],
        grad_joint,
        small[2 * D :],
        grad_out_proj,
        small[:D],
        small[D : 2 * D],
        grad_gate,
        grad_up,
        grad_down,
    )


def solution(mesh):
    placed = (
        P("dp", "ctx", None),
        P("dp", None),
        P(),
        P("dp", None),
        P(),
        P(),
        P(None, "dp"),
        P(None, "dp"),
        P("dp", None),
        P("dp", "ctx", None),
    )
    return jax.shard_map(
        local,
        mesh=mesh,
        in_specs=placed,
        out_specs=(
            P("dp", "ctx", None),
            P("dp", "ctx", None),
            P("dp", None),
            P(),
            P("dp", None),
            P(),
            P(),
            P(None, "dp"),
            P(None, "dp"),
            P("dp", None),
        ),
        check_vma=False,
    )
```

```python
import jax
import jax.numpy as jnp
from jax import lax
from jax.experimental import pallas as pl
from jax.experimental.pallas import tpu as pltpu
from jax.sharding import PartitionSpec as P

D = 896
QH = 14
KH = 2
HD = 64
GROUP = QH // KH
WIDTH_Q = QH * HD
WIDTH_K = KH * HD

EPS = 1e-06
ROPE_BASE = 1000000.0

f32 = jnp.float32
bf16 = jnp.bfloat16


def ring_order(chips):
    if chips % 2:
        return list(range(chips))
    rows = chips // 2
    return [2 * i for i in range(rows)] + [2 * i + 1 for i in reversed(range(rows))]


def half_cut(rows):
    cut = (rows // 2 + 7) // 8 * 8
    return cut if cut < rows else rows // 2


class Net:
    def __init__(self):
        self.dp = lax.axis_size("dp")
        self.ctx = lax.axis_size("ctx")
        self.chips = self.ctx // 2
        self.order = ring_order(self.chips)
        self.d = lax.axis_index("dp")
        self.c = lax.axis_index("ctx")
        self.core = self.c % 2
        place = [0] * self.chips
        for spot, chip in enumerate(self.order):
            place[chip] = spot
        self.pos = jnp.array(place, jnp.int32)[self.c // 2]

    def swap(self, x):
        return lax.ppermute(x, "ctx", [(i, i ^ 1) for i in range(self.ctx)])

    def shift(self, x, step):
        n = self.dp
        return lax.ppermute(x, "dp", [(i, (i + step) % n) for i in range(n)])

    def hop(self, x, step):
        n = self.chips
        perm = []
        for spot in range(n):
            for core in range(2):
                perm.append((2 * self.order[spot] + core, 2 * self.order[(spot + step) % n] + core))
        return lax.ppermute(x, "ctx", perm)

    def owner(self, slot):
        return (self.pos - slot) % self.chips

    def group_parts(self, x):
        chip = jnp.concatenate([x] + [self.shift(x, s) for s in range(1, self.dp)], 0)
        return chip, self.swap(chip)

    def group_gather(self, x):
        return jnp.concatenate(self.group_parts(x), 0)

    def ring_gather(self, x):
        n = self.chips
        half = n // 2
        cut = half_cut(x.shape[0])
        found = [x] + [None] * (n - 1)
        fwd, back = x, x
        for s in range(1, half):
            fwd = self.hop(fwd, 1)
            back = self.hop(back, -1)
            found[s] = fwd
            found[n - s] = back
        found[half] = jnp.concatenate([self.hop(fwd[:cut], 1), self.hop(back[cut:], -1)], 0)
        return found

    def ring_scatter(self, local):
        n = self.chips
        half = n // 2
        cut = half_cut(local[half].shape[0])

        def add(got, mine):
            return (got.astype(f32) + mine.astype(f32)).astype(bf16)

        fwd = self.hop(local[half][:cut], 1)
        back = self.hop(local[half][cut:], -1)
        for s in range(1, half):
            mine_f = local[half + s]
            mine_b = local[half - s]
            if s == 1:
                mine_f = jnp.concatenate([add(fwd, mine_f[:cut]), mine_f[cut:]], 0)
                mine_b = jnp.concatenate([mine_b[:cut], add(back, mine_b[cut:])], 0)
            else:
                mine_f = add(fwd, mine_f)
                mine_b = add(back, mine_b)
            fwd = self.hop(mine_f, 1)
            back = self.hop(mine_b, -1)
        return fwd.astype(f32) + back.astype(f32) + local[0].astype(f32)

    def full_rows(self, shard):
        rows = shard.shape[0]
        half = rows // 2
        piece = lax.dynamic_slice(shard, (self.core * half, 0), (half, shard.shape[1]))
        blocks = [shard]
        for s in range(1, self.dp):
            got = self.shift(piece, s)
            other = self.swap(got)
            low = jnp.where(self.core == 0, got, other)
            high = jnp.where(self.core == 0, other, got)
            blocks.append(jnp.concatenate([low, high], 0))
        if self.dp == 2:
            first = jnp.where(self.d == 0, blocks[0], blocks[1])
            second = jnp.where(self.d == 0, blocks[1], blocks[0])
            return jnp.concatenate([first, second], 0)
        ranked = jnp.stack(blocks)[(self.d - jnp.arange(self.dp)) % self.dp]
        return ranked.reshape(self.dp * rows, shard.shape[1])

    def total(self, x):
        x = x + self.swap(x)
        bit = 1
        while bit < self.chips:
            x = x + lax.ppermute(x, "ctx", [(i, i ^ (2 * bit)) for i in range(self.ctx)])
            bit *= 2
        bit = 1
        while bit < self.dp:
            x = x + lax.ppermute(x, "dp", [(i, i ^ bit) for i in range(self.dp)])
            bit *= 2
        return x

    def ring_parts(self, local):
        n = self.chips
        half = n // 2
        cut = half_cut(local[half].shape[0])

        def add(got, mine):
            return (got.astype(f32) + mine.astype(f32)).astype(bf16)

        fwd, back = self.hop(local[half][:cut], 1), self.hop(local[half][cut:], -1)
        marks = [(fwd, back)]
        for s in range(1, half):
            mine_f, mine_b = local[half + s], local[half - s]
            if s == 1:
                mine_f = jnp.concatenate([add(fwd, mine_f[:cut]), mine_f[cut:]], 0)
                mine_b = jnp.concatenate([mine_b[:cut], add(back, mine_b[cut:])], 0)
            else:
                mine_f, mine_b = add(fwd, mine_f), add(back, mine_b)
            fwd, back = self.hop(mine_f, 1), self.hop(mine_b, -1)
            marks.append((fwd, back))
        return [local[0], fwd, back], marks

    def exchange_sum(self, x):
        half = x.shape[0] // 2

        def add(a, b):
            return (a.astype(f32) + b.astype(f32)).astype(bf16)

        x = add(x, self.swap(x))
        x = lax.dynamic_slice(x, (self.core * half, 0), (half, x.shape[1]))
        marks = [x]
        bit = 1
        while bit < self.chips:
            x = add(x, lax.ppermute(x, "ctx", [(i, i ^ (2 * bit)) for i in range(self.ctx)]))
            marks.append(x)
            bit *= 2
        return x, marks

    def ring_sum(self, terms, marks):
        half = self.chips // 2
        fwd, back = self.hop(terms[half], 1), self.hop(terms[half - 1], -1)

        def add(got, slot):
            return (got.astype(f32) + terms[slot].astype(f32)).astype(bf16)

        for s in range(1, half):
            blocks = [add(fwd, half + s)]
            if s < half - 1:
                blocks.append(add(back, half - 1 - s))
            if s > 1:
                blocks = gate(marks[s - 2], blocks)
            fwd = self.hop(blocks[0], 1)
            if s < half - 1:
                back = self.hop(blocks[1], -1)
        return fwd, back

    def gather_placed(self, x, place, rest, marks):
        n = self.chips
        half = n // 2
        fwd = back = x
        placed = None
        waiting = ([0], [(x, self.swap(x))])
        for s in range(1, half + 1):
            if s > 1:
                placed, token = place(*waiting, placed)
                fwd, back = gate([token] + marks[s - 2], [fwd, back])
                waiting = ([s - 1, n - s + 1], [(fwd, self.swap(fwd)), (back, self.swap(back))])
            if s < half:
                fwd, back = self.hop(fwd, 1), self.hop(back, -1)
            else:
                cut = half_cut(fwd.shape[0])
                fwd, back = self.hop(fwd[:cut], 1), self.hop(back[cut:], -1)
        placed, token = place(*waiting, placed)
        far = join(fwd, back, token)
        return place([half], [(far, self.swap(far))], placed, rest)[0]


VMEM_BYTES = 56 * 1024 * 1024
KEYS = 256
RING_ROWS = 152


def full_spec(shape):
    return pl.BlockSpec(shape, lambda: (0,) * len(shape))


def call(kernel, outs, args, smem=0, scratch=(), flops=0, loose=0):
    tight = len(args) - loose
    specs = [pl.BlockSpec(memory_space=pltpu.SMEM)] * smem
    specs += [pl.BlockSpec(memory_space=pltpu.VMEM)] * (tight - smem)
    specs += [pl.BlockSpec(memory_space=pl.ANY)] * loose

    def body(*refs):
        kernel(*refs[:tight], *refs[tight + loose :])

    moved = sum(x.size * x.dtype.itemsize for x in list(args) + list(outs))
    return pl.pallas_call(
        body,
        out_shape=list(outs),
        in_specs=specs,
        out_specs=[pl.BlockSpec(memory_space=pltpu.VMEM)] * len(outs),
        scratch_shapes=list(scratch),
        compiler_params=pltpu.CompilerParams(vmem_limit_bytes=VMEM_BYTES),
        cost_estimate=pl.CostEstimate(flops=flops, bytes_accessed=moved, transcendentals=0),
    )(*args)


def lanes(shape):
    return lax.broadcasted_iota(jnp.int32, shape, len(shape) - 1)


def dot_nt(a, b, precision=None):
    return lax.dot_general(
        a, b, (((1,), (1,)), ((), ())), preferred_element_type=f32, precision=precision
    )


def dot_tn(a, b):
    return lax.dot_general(a, b, (((0,), (0,)), ((), ())), preferred_element_type=f32)


def gate(tokens, blocks):
    count, before = len(blocks), len(tokens)
    anywhere = pl.BlockSpec(memory_space=pl.ANY)

    def kernel(*refs):
        return None

    return pl.pallas_call(
        kernel,
        out_shape=[jax.ShapeDtypeStruct(x.shape, x.dtype) for x in blocks],
        in_specs=[anywhere] * (before + count),
        out_specs=[anywhere] * count,
        input_output_aliases={before + i: i for i in range(count)},
        cost_estimate=pl.CostEstimate(flops=0, bytes_accessed=1024, transcendentals=0),
    )(*tokens, *blocks)


def join(first, second, token):
    cut = first.shape[0]

    def kernel(first_ref, second_ref, out_ref):
        out_ref[:cut, :] = first_ref[...]
        out_ref[cut:, :] = second_ref[...]

    shape = (cut + second.shape[0], first.shape[1])
    return call(
        kernel, [jax.ShapeDtypeStruct(shape, first.dtype)], [first, second, token], loose=1
    )[0]


def ring_end(fwd, back, term, split):
    rows, columns = term.shape

    def kernel(fwd_ref, back_ref, term_ref, first_ref, rest_ref):
        for ref, here in ((first_ref, slice(0, split)), (rest_ref, slice(split, rows))):
            total = fwd_ref[here, :].astype(f32) + back_ref[here, :].astype(f32)
            ref[...] = (total + term_ref[here, :].astype(f32)).astype(bf16)

    outs = [
        jax.ShapeDtypeStruct((split, columns), bf16),
        jax.ShapeDtypeStruct((rows - split, columns), bf16),
    ]
    return call(kernel, outs, [fwd, back, term])


def pair_kernel(mine_ref, got_ref, *out_refs):
    rows = out_refs[0].shape[0]
    for s, out_ref in enumerate(out_refs):
        here = slice(s * rows, (s + 1) * rows)
        out_ref[...] = (mine_ref[here, :] + got_ref[here, :].astype(f32)).astype(out_ref.dtype)


def block_kernel(mlp_ref, down_ref, *refs):
    small = refs[0][...].astype(f32)
    for ref in refs[1:-1]:
        small = small + ref[...].astype(f32)
    out_ref = refs[-1]
    top = mlp_ref.shape[0]
    piece = small.shape[0]
    out_ref[:top, :] = mlp_ref[...]
    out_ref[top : top + piece, :] = small.astype(bf16)
    out_ref[top + piece :, :] = down_ref[...]


def qkv_kernel(x_ref, gain_ref, w_ref, b_ref, cos_ref, sin_ref, norm_ref, q_ref, pair_ref):
    x = x_ref[...].astype(f32)
    inverse = lax.rsqrt(jnp.mean(x * x, -1, keepdims=True) + EPS)
    normed = (x * inverse * gain_ref[...]).astype(bf16)
    norm_ref[...] = normed
    joint = jnp.dot(normed, w_ref[...], preferred_element_type=f32) + b_ref[...]
    cosine = cos_ref[...]
    sine = sin_ref[...]
    early = lanes(cosine.shape) % HD < HD // 2
    for i in range((WIDTH_Q + WIDTH_K) // 128):
        tile = joint[:, i * 128 : (i + 1) * 128]
        turned = jnp.where(early, -pltpu.roll(tile, 96, 1), pltpu.roll(tile, 32, 1))
        turned = tile * cosine + turned * sine
        if i * 128 < WIDTH_Q:
            q_ref[:, i * 128 : (i + 1) * 128] = turned.astype(bf16)
        else:
            pair_ref[:, :WIDTH_K] = turned.astype(bf16)
    pair_ref[:, WIDTH_K:] = joint[:, WIDTH_Q + WIDTH_K :].astype(bf16)


def spread_heads(x, out_ref, factor):
    rows = x.shape[0]
    half = rows // 2
    for head in range(QH):
        kh, g = divmod(head, GROUP)
        tile = x[:, (head // 2) * 128 : (head // 2 + 1) * 128].astype(f32)
        if head % 2 != kh:
            tile = pltpu.roll(tile, HD, 1)
        tile = jnp.where(lanes(tile.shape) // HD == kh, tile * factor, 0.0).astype(out_ref.dtype)
        for part in range(2):
            start = (part * GROUP + g) * half
            out_ref[kh, start : start + half, :] = tile[part * half : (part + 1) * half]


def join_heads(src_ref, half, tile):
    sides = []
    for side in range(2):
        kh, g = divmod(2 * tile + side, GROUP)
        parts = [
            src_ref[kh, (part * GROUP + g) * half : (part * GROUP + g + 1) * half, :]
            for part in range(2)
        ]
        both = jnp.concatenate(parts, 0)
        sides.append(both if side == kh else pltpu.roll(both, HD, 1))
    return jnp.where(lanes(sides[0].shape) < HD, sides[0], sides[1])


def forward_kernel(
    ctx, meta_ref, q_ref, mine_ref, other_ref, x_ref, w_ref, gain_ref,
    low_ref, o_ref, lse_ref, spread_ref, k_ref, v_ref, hidden_ref, normed_ref,
    s_ref, max_ref, sum_ref,
):
    rows = q_ref.shape[0]
    half = rows // 2
    part_rows = GROUP * half
    me = meta_ref[0]
    chips = ctx // 2
    for j in range(ctx):
        src = mine_ref if j < chips else other_ref
        at = (j % chips) * rows
        owner = meta_ref[1 + j]
        for part in range(2):
            place = owner if part == 0 else 2 * ctx - 1 - owner
            to = pl.ds(pl.multiple_of(place * half, half), half)
            block = src[at + part * half : at + (part + 1) * half, :]
            k_ref[to, :] = block[:, :WIDTH_K]
            v_ref[to, :] = block[:, WIDTH_K:]
    spread_heads(q_ref[...], spread_ref, HD ** (-0.5))
    for part in range(2):
        span = slice(part * part_rows, (part + 1) * part_rows)
        start = (me if part == 0 else 2 * ctx - 1 - me) * half
        last = start // KEYS

        def keys_of(ref, i):
            return ref[pl.ds(pl.multiple_of(i * KEYS, KEYS), KEYS), :]

        for kh in range(KH):
            scores = dot_nt(spread_ref[kh, span, :], keys_of(k_ref, last))
            row = lax.broadcasted_iota(jnp.int32, scores.shape, 0) % half + start
            scores = jnp.where(lanes(scores.shape) + last * KEYS <= row, scores, -1e30)
            s_ref[kh, last] = scores
            max_ref[kh] = jnp.maximum(scores[:, :128], scores[:, 128:])

        def score(i, carry):
            for kh in range(KH):
                s = dot_nt(spread_ref[kh, span, :], keys_of(k_ref, i))
                s_ref[kh, i] = s
                max_ref[kh] = jnp.maximum(max_ref[kh], jnp.maximum(s[:, :128], s[:, 128:]))
            return carry

        lax.fori_loop(0, last, score, 0)
        for kh in range(KH):
            top = jnp.max(max_ref[kh], -1, keepdims=True)
            max_ref[kh] = jnp.broadcast_to(top, (part_rows, 128))
            sum_ref[kh] = jnp.zeros((part_rows, 128), f32)
            o_ref[kh, span, :] = jnp.zeros((part_rows, 128), f32)

        def weigh(i, carry):
            for kh in range(KH):
                s = s_ref[kh, i]
                top = max_ref[kh]
                left = jnp.exp(s[:, :128] - top)
                right = jnp.exp(s[:, 128:] - top)
                sum_ref[kh] += left + right
                o_ref[kh, span, :] += jnp.dot(
                    jnp.concatenate([left, right], 1).astype(bf16),
                    keys_of(v_ref, i),
                    preferred_element_type=f32,
                )
            return carry

        lax.fori_loop(0, last + 1, weigh, 0)
        for kh in range(KH):
            total = jnp.sum(sum_ref[kh], -1, keepdims=True)
            o_ref[kh, span, :] = o_ref[kh, span, :] / total
            lse_ref[kh, part] = dot_nt(
                jnp.full((8, 128), 1.0 / 128, f32),
                max_ref[kh] + jnp.log(total),
                lax.Precision.HIGHEST,
            )
    for tile in range(WIDTH_Q // 128):
        low_ref[:, tile * 128 : (tile + 1) * 128] = join_heads(o_ref, half, tile).astype(bf16)
    hidden = x_ref[...].astype(f32) + jnp.dot(low_ref[...], w_ref[...], preferred_element_type=f32)
    hidden_ref[...] = hidden
    inverse = lax.rsqrt(jnp.mean(hidden * hidden, -1, keepdims=True) + EPS)
    normed_ref[...] = (hidden * inverse * gain_ref[...]).astype(bf16)


def turn_back(grad, cos_ref, sin_ref):
    scaled = grad * sin_ref[...]
    early = lanes(grad.shape) % HD < HD // 2
    turned = jnp.where(early, pltpu.roll(scaled, 96, 1), -pltpu.roll(scaled, 32, 1))
    return grad * cos_ref[...] + turned


def backward_kernel(
    ctx, meta_ref, gn_ref, hidden_ref, gout_ref, gain_ref, w_ref, spread_ref, k_ref, v_ref, lse_ref,
    o_ref, cos_ref, sin_ref,
    gh_ref, ga_ref, gain_grad_ref, gq_ref, mine_ref, other_ref,
    go_ref, gqs_ref, gk_ref, gv_ref,
):
    rows = gn_ref.shape[0]
    half = rows // 2
    part_rows = GROUP * half
    me = meta_ref[0]
    chips = ctx // 2
    hidden = hidden_ref[...]
    inverse = lax.rsqrt(jnp.mean(hidden * hidden, -1, keepdims=True) + EPS)
    unit = hidden * inverse
    grad = gn_ref[...]
    gain_grad_ref[...] = jnp.sum(grad * unit, 0, keepdims=True)
    scaled = grad * gain_ref[...]
    gh = gout_ref[...].astype(f32) + inverse * (
        scaled - unit * jnp.mean(scaled * unit, -1, keepdims=True)
    )
    gh_ref[...] = gh
    ga = gh.astype(bf16)
    ga_ref[...] = ga
    spread_heads(dot_nt(ga, w_ref[...]).astype(bf16), go_ref, 1.0)
    gqs_ref[...] = jnp.zeros_like(gqs_ref)
    gk_ref[...] = jnp.zeros_like(gk_ref)
    gv_ref[...] = jnp.zeros_like(gv_ref)
    for part in range(2):
        span = slice(part * part_rows, (part + 1) * part_rows)
        start = (me if part == 0 else 2 * ctx - 1 - me) * half
        last = start // KEYS
        deltas = [
            dot_nt(
                jnp.ones((8, 128), f32),
                go_ref[kh, span, :].astype(f32) * o_ref[kh, span, :],
                lax.Precision.HIGHEST,
            )[:1]
            for kh in range(KH)
        ]

        def step(i, masked):
            at = pl.ds(pl.multiple_of(i * KEYS, KEYS), KEYS)
            keys = k_ref[at, :]
            grad_k = gk_ref[at, :]
            grad_v = gv_ref[at, :]
            for kh in range(KH):
                queries = spread_ref[kh, span, :]
                heads = go_ref[kh, span, :]
                p = jnp.exp(dot_nt(keys, queries) - lse_ref[kh, part][:1])
                if masked:
                    row = lanes(p.shape) % half + start
                    key = lax.broadcasted_iota(jnp.int32, p.shape, 0) + i * KEYS
                    p = jnp.where(key <= row, p, 0.0)
                gs = (p * (dot_nt(v_ref[at, :], heads) - deltas[kh])).astype(bf16)
                grad_v += jnp.dot(p.astype(bf16), heads, preferred_element_type=f32)
                grad_k += jnp.dot(gs, queries, preferred_element_type=f32)
                gqs_ref[kh, span, :] += dot_tn(gs, keys)
            gk_ref[at, :] = grad_k
            gv_ref[at, :] = grad_v

        def body(i, carry):
            step(i, False)
            return carry

        lax.fori_loop(0, last, body, 0)
        step(last, True)
    for tile in range(WIDTH_Q // 128):
        grad = join_heads(gqs_ref, half, tile) * HD ** (-0.5)
        gq_ref[:, tile * 128 : (tile + 1) * 128] = turn_back(grad, cos_ref, sin_ref).astype(bf16)
    for j in range(ctx):
        dst = mine_ref if j < chips else other_ref
        at = (j % chips) * rows
        owner = meta_ref[1 + j]
        for part in range(2):
            place = owner if part == 0 else 2 * ctx - 1 - owner
            frm = pl.ds(pl.multiple_of(place * half, half), half)
            to = slice(at + part * half, at + (part + 1) * half)
            dst[to, :WIDTH_K] = gk_ref[frm, :].astype(dst.dtype)
            dst[to, WIDTH_K:] = gv_ref[frm, :].astype(dst.dtype)


SUM_ROWS = 16


def finish_kernel(
    gq_ref, x_ref, gain_ref, w_ref, cos_ref, sin_ref, gh_ref, gain_two_ref, *refs
):
    sent_ref, gx_ref, gain_grad_ref, bias_ref = refs[-4:]
    pair = refs[0][...]
    for ref in refs[1:-4]:
        pair = pair + ref[...].astype(f32)
    rows = pair.shape[0]
    keys = turn_back(pair[:, :WIDTH_K], cos_ref, sin_ref)
    pair = jnp.concatenate([keys, pair[:, WIDTH_K:]], 1).astype(bf16)
    sent_ref[:rows, :] = pair
    joint = jnp.concatenate([gq_ref[...], pair], 1)
    bias = jnp.sum(joint.astype(f32), 0, keepdims=True)
    bias_ref[...] = bias
    grad = dot_nt(joint, w_ref[...])
    x = x_ref[...].astype(f32)
    inverse = lax.rsqrt(jnp.mean(x * x, -1, keepdims=True) + EPS)
    unit = x * inverse
    gain = jnp.sum(grad * unit, 0, keepdims=True)
    gain_grad_ref[...] = gain
    scaled = grad * gain_ref[...]
    gx_ref[...] = gh_ref[...] + inverse * (
        scaled - unit * jnp.mean(scaled * unit, -1, keepdims=True)
    )
    sums = jnp.concatenate([gain, gain_two_ref[...], bias], 1)
    width = pair.shape[1]
    sums = jnp.concatenate([sums, jnp.zeros((1, -sums.shape[1] % width), f32)], 1)
    found = [sums[:, i : i + width] for i in range(0, sums.shape[1], width)]
    found += [jnp.zeros((1, width), f32)] * (SUM_ROWS - len(found))
    sums = jnp.concatenate(found, 0)
    high = sums.astype(bf16)
    sent_ref[rows : rows + SUM_ROWS, :] = high
    sent_ref[rows + SUM_ROWS :, :] = (sums - high.astype(f32)).astype(bf16)


def pair_grad_kernel(rows, half_width, meta_ref, norm_ref, own_ref, peer_ref, out_ref, turned_ref):
    turned_ref[...] = norm_ref[:, D:].T
    first = pl.multiple_of(meta_ref[0] * half_width, 16)
    both = jnp.concatenate([own_ref[:rows, :], peer_ref[:rows, :]], 0)
    part = jnp.dot(turned_ref[pl.ds(first, half_width), :], both, preferred_element_type=f32)
    out_ref[:half_width, :] = part.astype(bf16)

    def sums(ref):
        high = ref[rows : rows + SUM_ROWS, :].astype(f32)
        return high + ref[rows + SUM_ROWS :, :].astype(f32)

    out_ref[half_width:, :] = (sums(own_ref) + sums(peer_ref)).astype(bf16)


def mlp_kernel(
    half_rows, spots_ref, x_a, x_b, gy_a, gy_b, gate_a, gate_b, up_a, up_b, down_a, down_b,
    xt_ref, midt_ref, gg_ref, gu_ref, gx_ref, out_ref, send_ref,
    x_all, gy_all, wg_all, wu_all, wd_all, mid_all, gg_all, gu_all,
):
    step = pl.program_id(0)

    @pl.when(step == 0)
    def start():
        x_all[:half_rows] = x_a[...]
        x_all[half_rows:] = x_b[...]
        gy_all[:half_rows] = gy_a[...]
        gy_all[half_rows:] = gy_b[...]
        xt_ref[...] = x_all[...].T

    here = pl.ds(pl.multiple_of(step * 256, 256), 256)
    wg = jnp.concatenate([gate_a[...], gate_b[...]], 1)
    wu = jnp.concatenate([up_a[...], up_b[...]], 1)
    wd = jnp.concatenate([down_a[...], down_b[...]], 0)
    wg_all[:, here] = wg
    wu_all[:, here] = wu
    wd_all[here, :] = wd
    core = spots_ref[1]
    column = lanes((1, 256)) + (step * 256 + spots_ref[2])
    own = (column < spots_ref[3]) == (core == 0)
    x = x_all[...]
    gate = jnp.dot(x, wg, preferred_element_type=f32)
    up = jnp.dot(x, wu, preferred_element_type=f32)
    grad = jnp.where(own, dot_nt(gy_all[...], wd), 0.0)
    sigma = jax.nn.sigmoid(gate)
    active = gate * sigma
    middle = jnp.where(own, active * up, 0.0).astype(bf16)
    grad_gate = (grad * up * (sigma + active * (1.0 - sigma))).astype(bf16)
    grad_up = (grad * active).astype(bf16)
    midt_ref[...] = middle.T
    gg_ref[...] = grad_gate
    gu_ref[...] = grad_up
    mid_all[:, here] = middle
    gg_all[:, here] = grad_gate
    gu_all[:, here] = grad_up

    @pl.when(step == pl.num_programs(0) - 1)
    def end():
        gx = dot_nt(gg_all[...], wg_all[...]) + dot_nt(gu_all[...], wu_all[...])
        gx_ref[...] = gx[:half_rows]
        send_ref[:half_rows] = gx[half_rows:].astype(bf16)
        out = jnp.dot(mid_all[...], wd_all[...], preferred_element_type=f32)
        out_ref[...] = out[:half_rows]
        send_ref[half_rows:] = out[half_rows:].astype(bf16)


def feed_forward(meta, x, early, w_gate, w_up, w_down, width):
    half = x[0].shape[0]
    tokens = 2 * half
    steps = width // 256
    tiles = width // 128 - 1

    def columns(j):
        return pl.BlockSpec((D, 128), lambda i, m: (0, m[1] * tiles + 2 * i + j))

    def rows(j):
        return pl.BlockSpec((128, D), lambda i, m: (m[1] * tiles + 2 * i + j, 0))

    whole = pl.BlockSpec((tokens, D), lambda i, m: (0, 0))
    halves = pl.BlockSpec((half, D), lambda i, m: (0, 0))
    tile = pl.BlockSpec((tokens, 256), lambda i, m: (0, i))
    hidden = jax.ShapeDtypeStruct((tokens, width), bf16)
    return pl.pallas_call(
        lambda *refs: mlp_kernel(half, *refs),
        out_shape=[
            jax.ShapeDtypeStruct((D, tokens), bf16),
            jax.ShapeDtypeStruct((width, tokens), bf16),
            hidden,
            hidden,
            jax.ShapeDtypeStruct((half, D), f32),
            jax.ShapeDtypeStruct((half, D), f32),
            jax.ShapeDtypeStruct((tokens, D), bf16),
        ],
        grid_spec=pltpu.PrefetchScalarGridSpec(
            num_scalar_prefetch=1,
            grid=(steps,),
            in_specs=[halves] * 4
            + [columns(0), columns(1), columns(0), columns(1), rows(0), rows(1)],
            out_specs=[
                pl.BlockSpec((D, tokens), lambda i, m: (0, 0)),
                pl.BlockSpec((256, tokens), lambda i, m: (i, 0)),
                tile,
                tile,
                halves,
                halves,
                whole,
            ],
            scratch_shapes=[pltpu.VMEM((tokens, D), bf16)] * 2
            + [pltpu.VMEM((D, width), bf16)] * 2
            + [pltpu.VMEM((width, D), bf16)]
            + [pltpu.VMEM((tokens, width), bf16)] * 3,
        ),
        compiler_params=pltpu.CompilerParams(vmem_limit_bytes=VMEM_BYTES),
        cost_estimate=pl.CostEstimate(
            flops=12 * tokens * width * D, bytes_accessed=6 * width * D, transcendentals=0
        ),
    )(meta, *x, *early, w_gate, w_gate, w_up, w_up, w_down, w_down)


def mlp_grad_kernel(chips, down_rows, main, meta_ref, xt_ref, gy_a, gy_b, midt_ref, gg_ref, gu_ref, *refs):
    out_refs = refs[:chips]
    mlp_acc, down_acc, blocks, sems = refs[chips:]
    core = meta_ref[1]
    at_main = pl.ds(pl.multiple_of(core * 128, 128), main)
    at_tile = pl.ds(pl.multiple_of((1 - core) * main, 128), 128)
    xt = xt_ref[...]
    mlp_acc[:, :main] = jnp.dot(xt, gg_ref[:, at_main], preferred_element_type=f32).astype(bf16)
    mlp_acc[:, main : 2 * main] = jnp.dot(
        xt, gu_ref[:, at_main], preferred_element_type=f32
    ).astype(bf16)
    mixed = gg_ref[:, at_tile].astype(f32) + pltpu.roll(gu_ref[:, at_tile].astype(f32), 64, 1)
    mlp_acc[:, 2 * main :] = jnp.dot(
        xt, mixed.astype(bf16), preferred_element_type=f32
    ).astype(bf16)
    gy = jnp.concatenate([gy_a[:, :D], gy_b[:, :D]], 0)
    down_acc[...] = jnp.dot(midt_ref[...], gy, preferred_element_type=f32)

    mlp_rows = mlp_acc.shape[0] // chips
    columns = mlp_acc.shape[1] // 128
    half = chips // 2
    copies = []
    for slot in sorted(range(chips), key=lambda s: abs(s - half) if s else chips):
        owner = meta_ref[12 + slot]
        block = mlp_acc[pl.ds(pl.multiple_of(owner * mlp_rows, 16), mlp_rows), :]
        for j in range(columns):
            for i in range(mlp_rows // 16):
                blocks[slot, j * 16 : (j + 1) * 16, i * 128 : (i + 1) * 128] = block[
                    i * 16 : (i + 1) * 16, j * 128 : (j + 1) * 128
                ]
        first = pl.multiple_of(core * 64 + owner * down_rows, 8)
        blocks[slot, columns * 16 :, :] = down_acc[pl.ds(first, down_rows), :].astype(bf16)
        copy = pltpu.make_async_copy(blocks.at[slot], out_refs[slot], sems.at[slot])
        copy.start()
        copies.append(copy)
    for copy in copies:
        copy.wait()


def mlp_gradients(meta, xt, early, midt, gg, gu, after, chips, down_rows, main):
    tokens = gg.shape[0]
    columns = (2 * main + 128) // 128
    rows = columns * 16 + down_rows
    args = [meta, xt, *early, midt, gg, gu]
    anywhere = pl.BlockSpec(memory_space=pl.ANY)

    def kernel(*refs):
        mlp_grad_kernel(chips, down_rows, main, *refs[: len(args)], *refs[len(args) + 1 :])

    return pl.pallas_call(
        kernel,
        out_shape=[jax.ShapeDtypeStruct((rows, D), bf16)] * chips,
        in_specs=[pl.BlockSpec(memory_space=pltpu.SMEM)]
        + [pl.BlockSpec(memory_space=pltpu.VMEM)] * (len(args) - 1)
        + [anywhere],
        out_specs=[anywhere] * chips,
        scratch_shapes=[
            pltpu.VMEM((D, columns * 128), bf16),
            pltpu.VMEM((midt.shape[0], D), f32),
            pltpu.VMEM((chips, rows, D), bf16),
            pltpu.SemaphoreType.DMA((chips,)),
        ],
        compiler_params=pltpu.CompilerParams(vmem_limit_bytes=VMEM_BYTES),
        cost_estimate=pl.CostEstimate(
            flops=6 * tokens * midt.shape[0] * D, bytes_accessed=4 * chips * rows * D,
            transcendentals=0,
        ),
    )(*args, after)


def small_grad_kernel(
    chips, q_rows, rows, cols, meta_ref, norm_a, norm_b, att_a, att_b, near_a, near_b, *refs
):
    out_refs, acc, turned_ref = refs[:-2], refs[-2], refs[-1]
    first = pl.multiple_of((2 * meta_ref[0] + meta_ref[1]) * q_rows, 16)
    grads, queries = [], []
    for near_ref in (near_a, near_b):
        for b in range(2):
            grads.append(near_ref[2 * b * rows : (2 * b + 1) * rows, :])
            queries.append(near_ref[(2 * b + 1) * rows : (2 * b + 2) * rows, :])
    turned_ref[...] = jnp.concatenate([norm_a[:, D:], norm_b[:, D:]], 0).T
    acc[:, :WIDTH_Q] = jnp.dot(
        turned_ref[pl.ds(first, q_rows), :],
        jnp.concatenate(queries, 0),
        preferred_element_type=f32,
    ).astype(bf16)
    acc[:, WIDTH_Q:cols] = jnp.zeros((q_rows, cols - WIDTH_Q), bf16)
    turned_ref[...] = jnp.concatenate([att_a[...], att_b[...]], 0).T
    acc[:, cols:] = jnp.dot(
        turned_ref[pl.ds(first, q_rows), :], jnp.concatenate(grads, 0), preferred_element_type=f32
    ).astype(bf16)
    width = acc.shape[1] // chips
    for out_ref, slot in zip(out_refs, range(chips)):
        owner = meta_ref[12 + slot]
        block = acc[:, pl.ds(pl.multiple_of(owner * width, 128), width)]
        tall = jnp.concatenate([block[:, i * 128 : (i + 1) * 128] for i in range(width // 128)], 0)
        piece = out_ref.shape[0]
        for i in range(D // 128):
            out_ref[:, i * 128 : (i + 1) * 128] = tall[i * piece : (i + 1) * piece]


def place_all(meta, slots, pairs, old, sizes, rest=None):
    main, ff_loc, q_rows, cols, down_rows, chips = sizes
    mlp_rows = D // chips
    columns = (2 * main + 128) // 128
    tiles = main // 128
    lanes_out = D // 128
    top = columns * 16
    blocks = [x for pair in pairs for x in pair]
    count = len(blocks)
    piece = blocks[0].shape[0] - top - down_rows
    parts = (cols + D) // chips // 128
    keep = [] if old is None else list(old)
    last = [] if rest is None else list(rest)
    known = WIDTH_Q // 128

    def kernel(meta_ref, *refs):
        ins = refs[:count]
        outs_at = count + len(last) + len(keep)
        gate_out, up_out, down_out, joint_out, proj_out, token_ref = refs[outs_at : outs_at + 6]
        gate_buf, up_buf, down_buf, small_buf, rest_buf, sems, small_sems, rest_sem = refs[
            outs_at + 6 :
        ]
        core_zero = meta_ref[1] == 0
        copies = []

        def send(src, dst, sem):
            copy = pltpu.make_async_copy(src, dst, sem)
            copy.start()
            copies.append(copy)

        def column(ref, j):
            found = [
                ref[j * 16 : (j + 1) * 16, i * 128 : (i + 1) * 128] for i in range(mlp_rows // 16)
            ]
            return jnp.concatenate(found, 0).astype(f32)

        for k, slot in enumerate(slots):
            for j in range(columns):
                got = column(ins[2 * k], j)
                other = column(ins[2 * k + 1], j)
                zero = jnp.where(core_zero, got, other)
                one = jnp.where(core_zero, other, got)
                if j < 2 * tiles:
                    buf = gate_buf if j < tiles else up_buf
                    at = (j % tiles) * 128
                    buf[k, :, at : at + 128] = zero
                    buf[k, :, at + main + 128 : at + main + 256] = one
                else:
                    left = lanes(zero.shape) < 64
                    gate_buf[k, :, main : main + 128] = jnp.where(left, zero, one)
                    up_buf[k, :, main : main + 128] = pltpu.roll(jnp.where(left, one, zero), 64, 1)
            owner = meta_ref[12 + slot]
            here = pl.ds(pl.multiple_of(owner * mlp_rows, 8), mlp_rows)
            send(gate_buf.at[k], gate_out.at[here, :], sems.at[4 * k])
            send(up_buf.at[k], up_out.at[here, :], sems.at[4 * k + 1])
            for side in range(2):
                b = 2 * k + side
                core = meta_ref[1] if side == 0 else 1 - meta_ref[1]
                down_buf[b] = ins[b][top + piece :, :].astype(f32)
                here = pl.ds(pl.multiple_of((core * chips + owner) * down_rows, 8), down_rows)
                send(down_buf.at[b], down_out.at[here, :], sems.at[4 * k + 2 + side])
                tall = jnp.concatenate(
                    [ins[b][top : top + piece, i * 128 : (i + 1) * 128] for i in range(lanes_out)], 0
                ).astype(f32)
                rows = pl.ds(pl.multiple_of(core * q_rows, 8), q_rows)
                for i in range(parts):
                    small_buf[b, i] = tall[i * q_rows : (i + 1) * q_rows]
                    block = owner * parts + i

                    @pl.when(block < known)
                    def joint(b=b, i=i, rows=rows, block=block):
                        at = pl.ds(pl.multiple_of(block * 128, 128), 128)
                        pltpu.make_async_copy(
                            small_buf.at[b, i], joint_out.at[rows, at], small_sems.at[b, i]
                        ).start()

                    @pl.when(block >= cols // 128)
                    def proj(b=b, i=i, rows=rows, block=block):
                        at = pl.ds(pl.multiple_of((block - cols // 128) * 128, 128), 128)
                        pltpu.make_async_copy(
                            small_buf.at[b, i], proj_out.at[rows, at], small_sems.at[b, i]
                        ).start()

        token_ref[...] = jnp.zeros(token_ref.shape, f32)
        if last:
            rows = last[0].shape[0]
            for core, ref in ((meta_ref[1], refs[count]), (1 - meta_ref[1], refs[count + 1])):
                rest_buf[pl.ds(pl.multiple_of(core * rows, 8), rows), :] = ref[...].astype(f32)
            send(rest_buf.at[: 2 * q_rows, :], joint_out.at[:, WIDTH_Q:cols], rest_sem)
        for copy in copies:
            copy.wait()
        for b in range(count):
            for i in range(parts):
                block = meta_ref[12 + slots[b // 2]] * parts + i

                @pl.when((block < known) | (block >= cols // 128))
                def done(b=b, i=i):
                    pltpu.make_async_copy(
                        small_buf.at[b, i],
                        proj_out.at[pl.ds(0, q_rows), pl.ds(0, 128)],
                        small_sems.at[b, i],
                    ).wait()

    anywhere = pl.BlockSpec(memory_space=pl.ANY)
    result = pl.pallas_call(
        kernel,
        out_shape=[
            jax.ShapeDtypeStruct((D, ff_loc), f32),
            jax.ShapeDtypeStruct((D, ff_loc), f32),
            jax.ShapeDtypeStruct((ff_loc, D), f32),
            jax.ShapeDtypeStruct((2 * q_rows, cols), f32),
            jax.ShapeDtypeStruct((2 * q_rows, D), f32),
            jax.ShapeDtypeStruct((8, 128), f32),
        ],
        in_specs=[pl.BlockSpec(memory_space=pltpu.SMEM)]
        + [pl.BlockSpec(memory_space=pltpu.VMEM)] * (count + len(last))
        + [anywhere] * len(keep),
        out_specs=[anywhere] * 5 + [pl.BlockSpec(memory_space=pltpu.VMEM)],
        scratch_shapes=[
            pltpu.VMEM((len(slots), mlp_rows, ff_loc), f32),
            pltpu.VMEM((len(slots), mlp_rows, ff_loc), f32),
            pltpu.VMEM((count, down_rows, D), f32),
            pltpu.VMEM((count, parts, q_rows, 128), f32),
            pltpu.VMEM((2 * q_rows + SUM_ROWS, cols - WIDTH_Q), f32),
            pltpu.SemaphoreType.DMA((4 * len(slots),)),
            pltpu.SemaphoreType.DMA((count, parts)),
            pltpu.SemaphoreType.DMA,
        ],
        input_output_aliases={1 + count + len(last) + i: i for i in range(len(keep))},
        compiler_params=pltpu.CompilerParams(vmem_limit_bytes=VMEM_BYTES),
        cost_estimate=pl.CostEstimate(
            flops=0, bytes_accessed=8 * sum(x.size for x in blocks), transcendentals=0
        ),
    )(meta, *blocks, *last, *keep)
    return list(result[:5]), result[5]


def place_blocks(blocks, spots, out_shape, old=None):
    shape = blocks[0].shape
    count = len(blocks)
    if shape[0] % 8 or shape[1] % 128:
        out = jnp.zeros(out_shape, f32) if old is None else old
        for block, (i, j) in zip(blocks, spots):
            out = lax.dynamic_update_slice(
                out, block.astype(f32), (i * shape[0], j * shape[1])
            )
        return out

    def kernel(spots_ref, *refs):
        step = pl.program_id(0)
        out_ref = refs[-1]
        for i in range(count):

            @pl.when(step == i)
            def write(i=i):
                out_ref[...] = refs[i][...].astype(f32)

    keep = [] if old is None else [old]
    return pl.pallas_call(
        kernel,
        out_shape=jax.ShapeDtypeStruct(out_shape, f32),
        grid_spec=pltpu.PrefetchScalarGridSpec(
            num_scalar_prefetch=1,
            grid=(count,),
            in_specs=[pl.BlockSpec(shape, lambda i, spots: (0, 0))] * count
            + [pl.BlockSpec(memory_space=pl.ANY)] * len(keep),
            out_specs=pl.BlockSpec(shape, lambda i, spots: (spots[i, 0], spots[i, 1])),
        ),
        input_output_aliases={} if old is None else {count + 1: 0},
        compiler_params=pltpu.CompilerParams(vmem_limit_bytes=VMEM_BYTES),
    )(jnp.stack([jnp.stack(s) for s in spots]).astype(jnp.int32), *blocks, *keep)


def local(tokens, w_qkv, b_qkv, w_out, gain_attn, gain_mlp, w_gate, w_up, w_down, cotangent):
    net = Net()
    rows = tokens.shape[1]
    half_rows = rows // 2
    ctx_count = net.ctx
    core = net.core
    chips = net.chips
    part_rows = GROUP * half_rows
    x = tokens[0]
    gain_one = gain_attn[None]
    gain_two = gain_mlp[None]

    w_qkv_full = net.full_rows(w_qkv)

    ff_loc = w_gate.shape[1]
    ff_half = ff_loc // 2
    main = (ff_half // 128) * 128
    rest = ff_half - main
    width = main + 2 * rest
    first = core * main
    tiled = net.dp == 2 and 2 * rest == 128 and width % 256 == 0 and chips == 8 and ff_half == chips * RING_ROWS
    ring = jnp.arange(chips, dtype=jnp.int32)
    owners_of = (net.pos - ring) % chips
    spots = jnp.concatenate(
        [jnp.stack([net.d, core, first, jnp.int32(ff_half)]), owners_of, owners_of]
    ).astype(jnp.int32)

    row_ids = jnp.arange(half_rows, dtype=jnp.int32)
    place = jnp.concatenate(
        [net.c * half_rows + row_ids, (2 * ctx_count - 1 - net.c) * half_rows + row_ids]
    )
    freq = ROPE_BASE ** (-((jnp.arange(128) % (HD // 2)).astype(f32) * (2.0 / HD)))
    angle = place.astype(f32)[:, None] * freq[None, :]
    cosine, sine = jnp.cos(angle), jnp.sin(angle)
    normed_one, queries, pairs = call(
        qkv_kernel,
        [
            jax.ShapeDtypeStruct((rows, D), bf16),
            jax.ShapeDtypeStruct((rows, WIDTH_Q), bf16),
            jax.ShapeDtypeStruct((rows, 2 * WIDTH_K), bf16),
        ],
        [x, gain_one, w_qkv_full, b_qkv[None], cosine, sine],
        flops=2 * rows * D * 1152,
    )

    slots = net.ring_gather(pairs)
    mine = jnp.concatenate(slots, 0)
    other = net.swap(mine)
    order = jnp.array(net.order, jnp.int32)
    chip_ids = order[(net.pos - jnp.arange(chips, dtype=jnp.int32)) % chips]
    meta = jnp.concatenate([net.c[None], 2 * chip_ids + core, 2 * chip_ids + 1 - core])
    meta = meta.astype(jnp.int32)

    late_w, late_g, late_n, unused = lax.optimization_barrier((w_out, cotangent[0], normed_one, pairs))
    w_out_full = net.full_rows(late_w)
    early = net.group_parts(jnp.concatenate([late_g, late_n], 1))

    total_keys = rows * ctx_count
    padded = (KH, 2 * part_rows, 128)
    attended_low, attended, lse, spread, keys, values, hidden, normed_two = call(
        lambda *refs: forward_kernel(ctx_count, *refs),
        [
            jax.ShapeDtypeStruct((rows, WIDTH_Q), bf16),
            jax.ShapeDtypeStruct(padded, f32),
            jax.ShapeDtypeStruct((KH, 2, 8, part_rows), f32),
            jax.ShapeDtypeStruct(padded, bf16),
            jax.ShapeDtypeStruct((total_keys, WIDTH_K), bf16),
            jax.ShapeDtypeStruct((total_keys, WIDTH_K), bf16),
            jax.ShapeDtypeStruct((rows, D), f32),
            jax.ShapeDtypeStruct((rows, D), bf16),
        ],
        [meta, queries, mine, other, x, w_out_full, gain_two],
        smem=1,
        scratch=[
            pltpu.VMEM((KH, total_keys // KEYS, part_rows, KEYS), f32),
            pltpu.VMEM((KH, part_rows, 128), f32),
            pltpu.VMEM((KH, part_rows, 128), f32),
        ],
        flops=8 * KH * part_rows * total_keys * 128,
    )

    normed_two_parts = net.group_parts(normed_two)
    chip_rows = net.dp * rows
    down_rows = ff_half // chips
    mlp_rows = D // chips
    if tiled:
        x_turned, mid_turned, gate_low, up_low, grad_mine, out_mine, sent = feed_forward(
            spots, normed_two_parts, early, w_gate, w_up, w_down, width
        )
    else:
        normed_two_group = jnp.concatenate(normed_two_parts, 0)
        grad_out_group = jnp.concatenate(early, 0)[:, :D]
        own_cols = (jnp.arange(width) + first < ff_half) == (core == 0)
        wg = lax.dynamic_slice(w_gate, (0, first), (D, width))
        wu = lax.dynamic_slice(w_up, (0, first), (D, width))
        wd = lax.dynamic_slice(w_down, (first, 0), (width, D))
        gate = jnp.dot(normed_two_group, wg, preferred_element_type=f32)
        upper = jnp.dot(normed_two_group, wu, preferred_element_type=f32)
        sigma = jax.nn.sigmoid(gate)
        activated = gate * sigma
        middle = jnp.where(own_cols, activated * upper, 0.0).astype(bf16)
        grad_middle = jnp.einsum("td,fd->tf", grad_out_group, wd, preferred_element_type=f32)
        slope = sigma * (1.0 + gate * (1.0 - sigma))
        grad_gate_low = jnp.where(own_cols, grad_middle * upper * slope, 0.0).astype(bf16)
        grad_up_low = jnp.where(own_cols, grad_middle * activated, 0.0).astype(bf16)

        grad_normed_two = jnp.einsum(
            "tf,df->td", grad_gate_low, wg, preferred_element_type=f32
        ) + jnp.einsum("tf,df->td", grad_up_low, wu, preferred_element_type=f32)
        mlp_out = jnp.dot(middle, wd, preferred_element_type=f32)
        grad_mine, out_mine = grad_normed_two[:chip_rows], mlp_out[:chip_rows]
        sent = jnp.concatenate([grad_normed_two[chip_rows:], mlp_out[chip_rows:]], 0).astype(bf16)
    swapped = net.swap(sent)
    grad_chip = grad_mine + swapped[:chip_rows].astype(f32)
    mlp_chip = out_mine + swapped[chip_rows:].astype(f32)
    grad_two = grad_chip[:rows]
    for s in range(1, net.dp):
        sent_two = grad_chip[s * rows : (s + 1) * rows].astype(bf16)
        grad_two = grad_two + net.shift(sent_two, net.dp - s).astype(f32)

    def attention_back(*after):
        grad_hidden, grad_attn_low, grad_gain_two, grad_queries, terms_mine, terms_other = call(
            lambda *refs: backward_kernel(ctx_count, *refs),
            [
                jax.ShapeDtypeStruct((rows, D), f32),
                jax.ShapeDtypeStruct((rows, D), bf16),
                jax.ShapeDtypeStruct((1, D), f32),
                jax.ShapeDtypeStruct((rows, WIDTH_Q), bf16),
                jax.ShapeDtypeStruct((chips * rows, 2 * WIDTH_K), f32),
                jax.ShapeDtypeStruct((chips * rows, 2 * WIDTH_K), bf16),
            ],
            [
                meta, grad_two, hidden, cotangent[0], gain_two, w_out_full, spread, keys, values, lse,
                attended, cosine, sine, *after,
            ],
            smem=1,
            loose=len(after),
            scratch=[
                pltpu.VMEM(padded, bf16),
                pltpu.VMEM(padded, f32),
                pltpu.VMEM((total_keys, WIDTH_K), f32),
                pltpu.VMEM((total_keys, WIDTH_K), f32),
            ],
            flops=20 * KH * part_rows * total_keys * 128,
        )
        pair_sums = call(
            pair_kernel,
            [jax.ShapeDtypeStruct((rows, 2 * WIDTH_K), f32)]
            + [jax.ShapeDtypeStruct((rows, 2 * WIDTH_K), bf16)] * (chips - 1),
            [terms_mine, net.swap(terms_other)],
        )
        grad_pairs, marks = net.ring_parts(pair_sums)

        def finish():
            return call(
                finish_kernel,
                [
                    jax.ShapeDtypeStruct((rows + 2 * SUM_ROWS, 2 * WIDTH_K), bf16),
                    jax.ShapeDtypeStruct((rows, D), f32),
                    jax.ShapeDtypeStruct((1, D), f32),
                    jax.ShapeDtypeStruct((1, w_qkv.shape[1]), f32),
                ],
                [grad_queries, x, gain_one, w_qkv_full, cosine, sine, grad_hidden, grad_gain_two]
                + grad_pairs,
            )

        return grad_attn_low, grad_gain_two, grad_queries, finish, marks

    if tiled:
        terms = mlp_gradients(
            spots, x_turned, early, mid_turned, gate_low, up_low, sent_two, chips, down_rows, main
        )
        grad_attn_low, grad_gain_two, grad_queries, finish, marks = attention_back(terms[0])
        fwd, back = net.ring_sum(terms, marks)
        sum_mlp, sum_down = ring_end(fwd, back, terms[0], terms[0].shape[0] - down_rows)
    else:
        part_down = jnp.einsum(
            "tf,td->fd", middle, grad_out_group, preferred_element_type=f32
        ).astype(bf16)
        part_down = lax.dynamic_slice(part_down, (core * rest, 0), (ff_half, D))

        def down_chunk(slot):
            return lax.dynamic_slice(part_down, (net.owner(slot) * down_rows, 0), (down_rows, D))

        sum_down = net.ring_scatter([down_chunk(s) for s in range(chips)]).astype(bf16)

        def split_main(x):
            left = (x[:, :main], x[:, main:])
            right = (x[:, 2 * rest :], x[:, : 2 * rest])
            return (
                jnp.where(core == 0, left[0], right[0]),
                jnp.where(core == 0, left[1], right[1]),
            )

        gate_main, gate_tile = split_main(grad_gate_low)
        up_main, up_tile = split_main(grad_up_low)
        packed = jnp.concatenate(
            [gate_main, up_main, gate_tile + jnp.roll(up_tile, rest, 1)], 1
        )
        part_mlp = jnp.einsum(
            "td,tf->df", normed_two_group, packed, preferred_element_type=f32
        ).astype(bf16)

        def mlp_chunk(slot):
            return lax.dynamic_slice(
                part_mlp, (net.owner(slot) * mlp_rows, 0), (mlp_rows, 2 * ff_half)
            )

        sum_mlp = net.ring_scatter([mlp_chunk(s) for s in range(chips)]).astype(bf16)
        sum_mlp = lax.optimization_barrier(sum_mlp)
        grad_attn_low, grad_gain_two, grad_queries, finish, marks = attention_back()
    pair_sent, grad_input, grad_gain_one, grad_bias = finish()

    out_sum = mlp_chip[:rows]
    for s in range(1, net.dp):
        got = net.shift(mlp_chip[s * rows : (s + 1) * rows].astype(bf16), net.dp - s)
        out_sum = out_sum + got.astype(f32)
    output = (hidden + out_sum).astype(bf16)
    near = net.group_parts(jnp.concatenate([grad_attn_low, grad_queries], 0))
    attended_parts = net.group_parts(attended_low)

    q_rows = w_qkv.shape[0] // 2
    qkv_cols = w_qkv.shape[1]
    if tiled:
        piece = q_rows * (qkv_cols + D) // chips // D
        terms_small = call(
            lambda *refs: small_grad_kernel(chips, q_rows, rows, qkv_cols, *refs),
            [jax.ShapeDtypeStruct((piece, D), bf16)] * chips,
            [spots, *early, *attended_parts, *near],
            smem=1,
            scratch=[
                pltpu.VMEM((q_rows, qkv_cols + D), bf16),
                pltpu.VMEM((D, 2 * chip_rows), bf16),
            ],
            flops=4 * chip_rows * D * (qkv_cols + D),
        )
        block = call(
            block_kernel,
            [jax.ShapeDtypeStruct((sum_mlp.shape[0] + piece + down_rows, D), bf16)],
            [sum_mlp, sum_down] + net.ring_parts(terms_small)[0] + list(marks[2]),
            loose=2,
        )[0]
        part_pair = call(
            lambda *refs: pair_grad_kernel(rows, 2 * q_rows, *refs),
            [jax.ShapeDtypeStruct((2 * q_rows + SUM_ROWS, 2 * WIDTH_K), bf16)],
            [spots, early[0], pair_sent, net.shift(pair_sent, 1)],
            smem=1,
            scratch=[pltpu.VMEM((D, chip_rows), bf16)],
        )[0]
        grad_pair, steps = net.exchange_sum(part_pair)
        pair_halves = (grad_pair, net.swap(grad_pair))
        sums = jnp.where(core == 1, *pair_halves)[-SUM_ROWS:]
        small = sums.reshape(-1)[: 2 * D + qkv_cols].astype(f32)
        sizes = (main, ff_loc, q_rows, qkv_cols, down_rows, chips)
        grad_gate, grad_up, grad_down, grad_joint, grad_out_proj = net.gather_placed(
            block,
            lambda slots, pairs, old, rest=None: place_all(spots, slots, pairs, old, sizes, rest),
            pair_halves,
            [[part_pair], [steps[1]], [steps[2]]],
        )
    else:
        gathered = jnp.concatenate(near, 0).reshape(2 * net.dp, 2, rows, D)
        grad_attn_group = gathered[:, 0].reshape(2 * net.dp * rows, D)
        attended_group = jnp.concatenate(attended_parts, 0)
        normed_one_group = jnp.concatenate(early, 0)[:, D:]
        joint_group = net.group_gather(jnp.concatenate([grad_queries, pair_sent[:rows]], 1))
        q_first = net.d * (2 * q_rows) + core * q_rows
        group_rows = 2 * net.dp * rows
        part_out = jnp.einsum(
            "tc,td->cd",
            lax.dynamic_slice(attended_group, (0, q_first), (group_rows, q_rows)),
            grad_attn_group,
            preferred_element_type=f32,
        )
        part_joint = jnp.einsum(
            "td,tc->dc",
            lax.dynamic_slice(normed_one_group, (0, q_first), (group_rows, q_rows)),
            joint_group,
            preferred_element_type=f32,
        )
        part_small = jnp.concatenate([part_joint, part_out], 1).astype(bf16)
        small_cols = part_small.shape[1] // chips

        def small_chunk(slot):
            return lax.dynamic_slice(part_small, (0, net.owner(slot) * small_cols), (q_rows, small_cols))

        sum_small = net.ring_scatter([small_chunk(s) for s in range(chips)]).astype(bf16)

        tall = jnp.concatenate(
            [sum_small[:, i * 128 : (i + 1) * 128] for i in range(small_cols // 128)], 0
        )
        piece = tall.shape[0] // (D // 128)
        wide = jnp.concatenate([tall[i * piece : (i + 1) * piece] for i in range(D // 128)], 1)
        both = lax.optimization_barrier(jnp.concatenate([sum_down, wide], 0))

        owners = [net.owner(s) for s in range(chips)]
        got_mlp = net.ring_gather(sum_mlp)
        got_both = net.ring_gather(both)
        pairs_mlp = [(got, net.swap(got)) for got in got_mlp]
        pairs_both = [(got, net.swap(got)) for got in got_both]

        down_blocks, down_spots, small_blocks, small_spots = [], [], [], []
        for owner, pair in zip(owners, pairs_both):
            for which, got in zip((core, 1 - core), pair):
                down_blocks.append(got[:down_rows])
                down_spots.append((which * chips + owner, jnp.int32(0)))
                wide = got[down_rows:]
                tall = jnp.concatenate([wide[:, i * 128 : (i + 1) * 128] for i in range(D // 128)], 0)
                small_blocks.append(
                    jnp.concatenate(
                        [tall[i * q_rows : (i + 1) * q_rows] for i in range(small_cols // 128)], 1
                    )
                )
                small_spots.append((which, owner))
        grad_down = place_blocks(down_blocks, down_spots, (ff_loc, D))
        grad_small = place_blocks(small_blocks, small_spots, (2 * q_rows, part_small.shape[1]))
        grad_gate = jnp.zeros((D, ff_loc), f32)
        grad_up = jnp.zeros((D, ff_loc), f32)
        left_lane = jnp.arange(2 * rest) < rest
        for owner, (got, swapped) in zip(owners, pairs_mlp):
            zero = jnp.where(core == 0, got, swapped).astype(f32)
            one = jnp.where(core == 0, swapped, got).astype(f32)
            tile_zero, tile_one = zero[:, 2 * main :], one[:, 2 * main :]
            mid_gate = jnp.where(left_lane, tile_zero, tile_one)
            mid_up = jnp.roll(jnp.where(left_lane, tile_one, tile_zero), rest, 1)
            base = owner * mlp_rows
            grad_gate = lax.dynamic_update_slice(
                grad_gate, jnp.concatenate([zero[:, :main], mid_gate, one[:, :main]], 1), (base, 0)
            )
            grad_up = lax.dynamic_update_slice(
                grad_up,
                jnp.concatenate([zero[:, main : 2 * main], mid_up, one[:, main : 2 * main]], 1),
                (base, 0),
            )

        grad_joint, grad_out_proj = grad_small[:, :qkv_cols], grad_small[:, qkv_cols:]
        small = net.total(jnp.concatenate([grad_gain_one, grad_gain_two, grad_bias], 1))[0]
    return (
        output[None],
        grad_input[None],
        grad_joint,
        small[2 * D :],
        grad_out_proj,
        small[:D],
        small[D : 2 * D],
        grad_gate,
        grad_up,
        grad_down,
    )


def solution(mesh):
    placed = (
        P("dp", "ctx", None),
        P("dp", None),
        P(),
        P("dp", None),
        P(),
        P(),
        P(None, "dp"),
        P(None, "dp"),
        P("dp", None),
        P("dp", "ctx", None),
    )
    return jax.shard_map(
        local,
        mesh=mesh,
        in_specs=placed,
        out_specs=(
            P("dp", "ctx", None),
            P("dp", "ctx", None),
            P("dp", None),
            P(),
            P("dp", None),
            P(),
            P(),
            P(None, "dp"),
            P(None, "dp"),
            P("dp", None),
        ),
        check_vma=False,
    )
```

```python
import jax
import jax.numpy as jnp
from jax import lax
from jax.experimental import pallas as pl
from jax.experimental.pallas import tpu as pltpu
from jax.sharding import PartitionSpec as P

D = 896
QH = 14
KH = 2
HD = 64
GROUP = QH // KH
WIDTH_Q = QH * HD
WIDTH_K = KH * HD

EPS = 1e-06
ROPE_BASE = 1000000.0

f32 = jnp.float32
bf16 = jnp.bfloat16


def ring_order(chips):
    if chips % 2:
        return list(range(chips))
    rows = chips // 2
    return [2 * i for i in range(rows)] + [2 * i + 1 for i in reversed(range(rows))]


def half_cut(rows):
    cut = (rows // 2 + 7) // 8 * 8
    return cut if cut < rows else rows // 2


class Net:
    def __init__(self):
        self.dp = lax.axis_size("dp")
        self.ctx = lax.axis_size("ctx")
        self.chips = self.ctx // 2
        self.order = ring_order(self.chips)
        self.d = lax.axis_index("dp")
        self.c = lax.axis_index("ctx")
        self.core = self.c % 2
        place = [0] * self.chips
        for spot, chip in enumerate(self.order):
            place[chip] = spot
        self.pos = jnp.array(place, jnp.int32)[self.c // 2]

    def swap(self, x):
        return lax.ppermute(x, "ctx", [(i, i ^ 1) for i in range(self.ctx)])

    def shift(self, x, step):
        n = self.dp
        return lax.ppermute(x, "dp", [(i, (i + step) % n) for i in range(n)])

    def hop(self, x, step):
        n = self.chips
        perm = []
        for spot in range(n):
            for core in range(2):
                perm.append((2 * self.order[spot] + core, 2 * self.order[(spot + step) % n] + core))
        return lax.ppermute(x, "ctx", perm)

    def owner(self, slot):
        return (self.pos - slot) % self.chips

    def group_parts(self, x):
        chip = jnp.concatenate([x] + [self.shift(x, s) for s in range(1, self.dp)], 0)
        return chip, self.swap(chip)

    def group_gather(self, x):
        return jnp.concatenate(self.group_parts(x), 0)

    def ring_gather(self, x):
        n = self.chips
        half = n // 2
        cut = half_cut(x.shape[0])
        found = [x] + [None] * (n - 1)
        fwd, back = x, x
        for s in range(1, half):
            fwd = self.hop(fwd, 1)
            back = self.hop(back, -1)
            found[s] = fwd
            found[n - s] = back
        found[half] = jnp.concatenate([self.hop(fwd[:cut], 1), self.hop(back[cut:], -1)], 0)
        return found

    def ring_scatter(self, local):
        n = self.chips
        half = n // 2
        cut = half_cut(local[half].shape[0])

        def add(got, mine):
            return (got.astype(f32) + mine.astype(f32)).astype(bf16)

        fwd = self.hop(local[half][:cut], 1)
        back = self.hop(local[half][cut:], -1)
        for s in range(1, half):
            mine_f = local[half + s]
            mine_b = local[half - s]
            if s == 1:
                mine_f = jnp.concatenate([add(fwd, mine_f[:cut]), mine_f[cut:]], 0)
                mine_b = jnp.concatenate([mine_b[:cut], add(back, mine_b[cut:])], 0)
            else:
                mine_f = add(fwd, mine_f)
                mine_b = add(back, mine_b)
            fwd = self.hop(mine_f, 1)
            back = self.hop(mine_b, -1)
        return fwd.astype(f32) + back.astype(f32) + local[0].astype(f32)

    def full_rows(self, shard):
        rows = shard.shape[0]
        half = rows // 2
        piece = lax.dynamic_slice(shard, (self.core * half, 0), (half, shard.shape[1]))
        blocks = [shard]
        for s in range(1, self.dp):
            got = self.shift(piece, s)
            other = self.swap(got)
            low = jnp.where(self.core == 0, got, other)
            high = jnp.where(self.core == 0, other, got)
            blocks.append(jnp.concatenate([low, high], 0))
        if self.dp == 2:
            first = jnp.where(self.d == 0, blocks[0], blocks[1])
            second = jnp.where(self.d == 0, blocks[1], blocks[0])
            return jnp.concatenate([first, second], 0)
        ranked = jnp.stack(blocks)[(self.d - jnp.arange(self.dp)) % self.dp]
        return ranked.reshape(self.dp * rows, shard.shape[1])

    def total(self, x):
        x = x + self.swap(x)
        bit = 1
        while bit < self.chips:
            x = x + lax.ppermute(x, "ctx", [(i, i ^ (2 * bit)) for i in range(self.ctx)])
            bit *= 2
        bit = 1
        while bit < self.dp:
            x = x + lax.ppermute(x, "dp", [(i, i ^ bit) for i in range(self.dp)])
            bit *= 2
        return x

    def ring_parts(self, local):
        n = self.chips
        half = n // 2
        cut = half_cut(local[half].shape[0])

        def add(got, mine):
            return (got.astype(f32) + mine.astype(f32)).astype(bf16)

        fwd, back = self.hop(local[half][:cut], 1), self.hop(local[half][cut:], -1)
        marks = [(fwd, back)]
        for s in range(1, half):
            mine_f, mine_b = local[half + s], local[half - s]
            if s == 1:
                mine_f = jnp.concatenate([add(fwd, mine_f[:cut]), mine_f[cut:]], 0)
                mine_b = jnp.concatenate([mine_b[:cut], add(back, mine_b[cut:])], 0)
            else:
                mine_f, mine_b = add(fwd, mine_f), add(back, mine_b)
            fwd, back = self.hop(mine_f, 1), self.hop(mine_b, -1)
            marks.append((fwd, back))
        return [local[0], fwd, back], marks

    def exchange_sum(self, x):
        half = x.shape[0] // 2

        def add(a, b):
            return (a.astype(f32) + b.astype(f32)).astype(bf16)

        x = add(x, self.swap(x))
        x = lax.dynamic_slice(x, (self.core * half, 0), (half, x.shape[1]))
        marks = [x]
        bit = 1
        while bit < self.chips:
            x = add(x, lax.ppermute(x, "ctx", [(i, i ^ (2 * bit)) for i in range(self.ctx)]))
            marks.append(x)
            bit *= 2
        return x, marks

    def ring_sum(self, terms, between):
        half = self.chips // 2
        fwd, back = self.hop(terms[half], 1), self.hop(terms[half - 1], -1)

        def add(got, slot):
            return (got.astype(f32) + terms[slot].astype(f32)).astype(bf16)

        for s in range(1, half):
            blocks = [add(fwd, half + s)]
            if s < half - 1:
                blocks.append(add(back, half - 1 - s))
            if s == 1:
                marks = between(*blocks)
            else:
                blocks = gate(marks[s - 2], blocks)
            fwd = self.hop(blocks[0], 1)
            if s < half - 1:
                back = self.hop(blocks[1], -1)
        return fwd, back

    def gather_placed(self, x, place, rest, marks):
        n = self.chips
        half = n // 2
        fwd = back = x
        placed = None
        waiting = ([0], [(x, self.swap(x))])
        for s in range(1, half + 1):
            if s > 1:
                placed, token = place(*waiting, placed)
                fwd, back = gate([token] + marks[s - 2], [fwd, back])
                waiting = ([s - 1, n - s + 1], [(fwd, self.swap(fwd)), (back, self.swap(back))])
            if s < half:
                fwd, back = self.hop(fwd, 1), self.hop(back, -1)
            else:
                cut = half_cut(fwd.shape[0])
                fwd, back = self.hop(fwd[:cut], 1), self.hop(back[cut:], -1)
        placed, token = place(*waiting, placed)
        far = join(fwd, back, token)
        return place([half], [(far, self.swap(far))], placed, rest)[0]


VMEM_BYTES = 56 * 1024 * 1024
KEYS = 256
RING_ROWS = 152


def full_spec(shape):
    return pl.BlockSpec(shape, lambda: (0,) * len(shape))


def call(kernel, outs, args, smem=0, scratch=(), flops=0, loose=0):
    tight = len(args) - loose
    specs = [pl.BlockSpec(memory_space=pltpu.SMEM)] * smem
    specs += [pl.BlockSpec(memory_space=pltpu.VMEM)] * (tight - smem)
    specs += [pl.BlockSpec(memory_space=pl.ANY)] * loose

    def body(*refs):
        kernel(*refs[:tight], *refs[tight + loose :])

    moved = sum(x.size * x.dtype.itemsize for x in list(args) + list(outs))
    return pl.pallas_call(
        body,
        out_shape=list(outs),
        in_specs=specs,
        out_specs=[pl.BlockSpec(memory_space=pltpu.VMEM)] * len(outs),
        scratch_shapes=list(scratch),
        compiler_params=pltpu.CompilerParams(vmem_limit_bytes=VMEM_BYTES),
        cost_estimate=pl.CostEstimate(flops=flops, bytes_accessed=moved, transcendentals=0),
    )(*args)


def lanes(shape):
    return lax.broadcasted_iota(jnp.int32, shape, len(shape) - 1)


def dot_nt(a, b, precision=None):
    return lax.dot_general(
        a, b, (((1,), (1,)), ((), ())), preferred_element_type=f32, precision=precision
    )


def dot_tn(a, b):
    return lax.dot_general(a, b, (((0,), (0,)), ((), ())), preferred_element_type=f32)


def gate(tokens, blocks):
    count, before = len(blocks), len(tokens)
    anywhere = pl.BlockSpec(memory_space=pl.ANY)

    def kernel(*refs):
        return None

    return pl.pallas_call(
        kernel,
        out_shape=[jax.ShapeDtypeStruct(x.shape, x.dtype) for x in blocks],
        in_specs=[anywhere] * (before + count),
        out_specs=[anywhere] * count,
        input_output_aliases={before + i: i for i in range(count)},
        cost_estimate=pl.CostEstimate(flops=0, bytes_accessed=1024, transcendentals=0),
    )(*tokens, *blocks)


def join(first, second, token):
    cut = first.shape[0]

    def kernel(first_ref, second_ref, out_ref):
        out_ref[:cut, :] = first_ref[...]
        out_ref[cut:, :] = second_ref[...]

    shape = (cut + second.shape[0], first.shape[1])
    return call(
        kernel, [jax.ShapeDtypeStruct(shape, first.dtype)], [first, second, token], loose=1
    )[0]


def ring_end(fwd, back, term, split):
    rows, columns = term.shape

    def kernel(fwd_ref, back_ref, term_ref, first_ref, rest_ref):
        for ref, here in ((first_ref, slice(0, split)), (rest_ref, slice(split, rows))):
            total = fwd_ref[here, :].astype(f32) + back_ref[here, :].astype(f32)
            ref[...] = (total + term_ref[here, :].astype(f32)).astype(bf16)

    outs = [
        jax.ShapeDtypeStruct((split, columns), bf16),
        jax.ShapeDtypeStruct((rows - split, columns), bf16),
    ]
    return call(kernel, outs, [fwd, back, term])


def pair_kernel(mine_ref, got_ref, *out_refs):
    rows = out_refs[0].shape[0]
    for s, out_ref in enumerate(out_refs):
        here = slice(s * rows, (s + 1) * rows)
        out_ref[...] = (mine_ref[here, :] + got_ref[here, :].astype(f32)).astype(out_ref.dtype)


def block_kernel(mlp_ref, down_ref, *refs):
    small = refs[0][...].astype(f32)
    for ref in refs[1:-1]:
        small = small + ref[...].astype(f32)
    out_ref = refs[-1]
    top = mlp_ref.shape[0]
    piece = small.shape[0]
    out_ref[:top, :] = mlp_ref[...]
    out_ref[top : top + piece, :] = small.astype(bf16)
    out_ref[top + piece :, :] = down_ref[...]


def qkv_kernel(x_ref, gain_ref, w_ref, b_ref, cos_ref, sin_ref, norm_ref, q_ref, pair_ref):
    x = x_ref[...].astype(f32)
    inverse = lax.rsqrt(jnp.mean(x * x, -1, keepdims=True) + EPS)
    normed = (x * inverse * gain_ref[...]).astype(bf16)
    norm_ref[...] = normed
    joint = jnp.dot(normed, w_ref[...], preferred_element_type=f32) + b_ref[...]
    cosine = cos_ref[...]
    sine = sin_ref[...]
    early = lanes(cosine.shape) % HD < HD // 2
    for i in range((WIDTH_Q + WIDTH_K) // 128):
        tile = joint[:, i * 128 : (i + 1) * 128]
        turned = jnp.where(early, -pltpu.roll(tile, 96, 1), pltpu.roll(tile, 32, 1))
        turned = tile * cosine + turned * sine
        if i * 128 < WIDTH_Q:
            q_ref[:, i * 128 : (i + 1) * 128] = turned.astype(bf16)
        else:
            pair_ref[:, :WIDTH_K] = turned.astype(bf16)
    pair_ref[:, WIDTH_K:] = joint[:, WIDTH_Q + WIDTH_K :].astype(bf16)


def spread_heads(x, out_ref, factor):
    rows = x.shape[0]
    half = rows // 2
    for head in range(QH):
        kh, g = divmod(head, GROUP)
        tile = x[:, (head // 2) * 128 : (head // 2 + 1) * 128].astype(f32)
        if head % 2 != kh:
            tile = pltpu.roll(tile, HD, 1)
        tile = jnp.where(lanes(tile.shape) // HD == kh, tile * factor, 0.0).astype(out_ref.dtype)
        for part in range(2):
            start = (part * GROUP + g) * half
            out_ref[kh, start : start + half, :] = tile[part * half : (part + 1) * half]


def join_heads(src_ref, half, tile):
    sides = []
    for side in range(2):
        kh, g = divmod(2 * tile + side, GROUP)
        parts = [
            src_ref[kh, (part * GROUP + g) * half : (part * GROUP + g + 1) * half, :]
            for part in range(2)
        ]
        both = jnp.concatenate(parts, 0)
        sides.append(both if side == kh else pltpu.roll(both, HD, 1))
    return jnp.where(lanes(sides[0].shape) < HD, sides[0], sides[1])


def forward_kernel(
    ctx, meta_ref, q_ref, mine_ref, other_ref, x_ref, w_ref, gain_ref,
    low_ref, o_ref, lse_ref, spread_ref, k_ref, v_ref, hidden_ref, normed_ref,
    s_ref, max_ref, sum_ref,
):
    rows = q_ref.shape[0]
    half = rows // 2
    part_rows = GROUP * half
    me = meta_ref[0]
    chips = ctx // 2
    for j in range(ctx):
        src = mine_ref if j < chips else other_ref
        at = (j % chips) * rows
        owner = meta_ref[1 + j]
        for part in range(2):
            place = owner if part == 0 else 2 * ctx - 1 - owner
            to = pl.ds(pl.multiple_of(place * half, half), half)
            block = src[at + part * half : at + (part + 1) * half, :]
            k_ref[to, :] = block[:, :WIDTH_K]
            v_ref[to, :] = block[:, WIDTH_K:]
    spread_heads(q_ref[...], spread_ref, HD ** (-0.5))
    for part in range(2):
        span = slice(part * part_rows, (part + 1) * part_rows)
        start = (me if part == 0 else 2 * ctx - 1 - me) * half
        last = start // KEYS

        def keys_of(ref, i):
            return ref[pl.ds(pl.multiple_of(i * KEYS, KEYS), KEYS), :]

        for kh in range(KH):
            scores = dot_nt(spread_ref[kh, span, :], keys_of(k_ref, last))
            row = lax.broadcasted_iota(jnp.int32, scores.shape, 0) % half + start
            scores = jnp.where(lanes(scores.shape) + last * KEYS <= row, scores, -1e30)
            s_ref[kh, last] = scores
            max_ref[kh] = jnp.maximum(scores[:, :128], scores[:, 128:])

        def score(i, carry):
            for kh in range(KH):
                s = dot_nt(spread_ref[kh, span, :], keys_of(k_ref, i))
                s_ref[kh, i] = s
                max_ref[kh] = jnp.maximum(max_ref[kh], jnp.maximum(s[:, :128], s[:, 128:]))
            return carry

        lax.fori_loop(0, last, score, 0)
        for kh in range(KH):
            top = jnp.max(max_ref[kh], -1, keepdims=True)
            max_ref[kh] = jnp.broadcast_to(top, (part_rows, 128))
            sum_ref[kh] = jnp.zeros((part_rows, 128), f32)
            o_ref[kh, span, :] = jnp.zeros((part_rows, 128), f32)

        def weigh(i, carry):
            for kh in range(KH):
                s = s_ref[kh, i]
                top = max_ref[kh]
                left = jnp.exp(s[:, :128] - top)
                right = jnp.exp(s[:, 128:] - top)
                sum_ref[kh] += left + right
                o_ref[kh, span, :] += jnp.dot(
                    jnp.concatenate([left, right], 1).astype(bf16),
                    keys_of(v_ref, i),
                    preferred_element_type=f32,
                )
            return carry

        lax.fori_loop(0, last + 1, weigh, 0)
        for kh in range(KH):
            total = jnp.sum(sum_ref[kh], -1, keepdims=True)
            o_ref[kh, span, :] = o_ref[kh, span, :] / total
            lse_ref[kh, part] = dot_nt(
                jnp.full((8, 128), 1.0 / 128, f32),
                max_ref[kh] + jnp.log(total),
                lax.Precision.HIGHEST,
            )
    for tile in range(WIDTH_Q // 128):
        low_ref[:, tile * 128 : (tile + 1) * 128] = join_heads(o_ref, half, tile).astype(bf16)
    hidden = x_ref[...].astype(f32) + jnp.dot(low_ref[...], w_ref[...], preferred_element_type=f32)
    hidden_ref[...] = hidden
    inverse = lax.rsqrt(jnp.mean(hidden * hidden, -1, keepdims=True) + EPS)
    normed_ref[...] = (hidden * inverse * gain_ref[...]).astype(bf16)


def turn_back(grad, cos_ref, sin_ref):
    scaled = grad * sin_ref[...]
    early = lanes(grad.shape) % HD < HD // 2
    turned = jnp.where(early, pltpu.roll(scaled, 96, 1), -pltpu.roll(scaled, 32, 1))
    return grad * cos_ref[...] + turned


def backward_kernel(
    ctx, meta_ref, gn_ref, hidden_ref, gout_ref, gain_ref, w_ref, spread_ref, k_ref, v_ref, lse_ref,
    o_ref, cos_ref, sin_ref,
    gh_ref, ga_ref, gain_grad_ref, gq_ref, mine_ref, other_ref,
    go_ref, gqs_ref, gk_ref, gv_ref,
):
    rows = gn_ref.shape[0]
    half = rows // 2
    part_rows = GROUP * half
    me = meta_ref[0]
    chips = ctx // 2
    hidden = hidden_ref[...]
    inverse = lax.rsqrt(jnp.mean(hidden * hidden, -1, keepdims=True) + EPS)
    unit = hidden * inverse
    grad = gn_ref[...]
    gain_grad_ref[...] = jnp.sum(grad * unit, 0, keepdims=True)
    scaled = grad * gain_ref[...]
    gh = gout_ref[...].astype(f32) + inverse * (
        scaled - unit * jnp.mean(scaled * unit, -1, keepdims=True)
    )
    gh_ref[...] = gh
    ga = gh.astype(bf16)
    ga_ref[...] = ga
    spread_heads(dot_nt(ga, w_ref[...]).astype(bf16), go_ref, 1.0)
    gqs_ref[...] = jnp.zeros_like(gqs_ref)
    gk_ref[...] = jnp.zeros_like(gk_ref)
    gv_ref[...] = jnp.zeros_like(gv_ref)
    for part in range(2):
        span = slice(part * part_rows, (part + 1) * part_rows)
        start = (me if part == 0 else 2 * ctx - 1 - me) * half
        last = start // KEYS
        deltas = [
            dot_nt(
                jnp.ones((8, 128), f32),
                go_ref[kh, span, :].astype(f32) * o_ref[kh, span, :],
                lax.Precision.HIGHEST,
            )[:1]
            for kh in range(KH)
        ]

        def step(i, masked):
            at = pl.ds(pl.multiple_of(i * KEYS, KEYS), KEYS)
            keys = k_ref[at, :]
            grad_k = gk_ref[at, :]
            grad_v = gv_ref[at, :]
            for kh in range(KH):
                queries = spread_ref[kh, span, :]
                heads = go_ref[kh, span, :]
                p = jnp.exp(dot_nt(keys, queries) - lse_ref[kh, part][:1])
                if masked:
                    row = lanes(p.shape) % half + start
                    key = lax.broadcasted_iota(jnp.int32, p.shape, 0) + i * KEYS
                    p = jnp.where(key <= row, p, 0.0)
                gs = (p * (dot_nt(v_ref[at, :], heads) - deltas[kh])).astype(bf16)
                grad_v += jnp.dot(p.astype(bf16), heads, preferred_element_type=f32)
                grad_k += jnp.dot(gs, queries, preferred_element_type=f32)
                gqs_ref[kh, span, :] += dot_tn(gs, keys)
            gk_ref[at, :] = grad_k
            gv_ref[at, :] = grad_v

        def body(i, carry):
            step(i, False)
            return carry

        lax.fori_loop(0, last, body, 0)
        step(last, True)
    for tile in range(WIDTH_Q // 128):
        grad = join_heads(gqs_ref, half, tile) * HD ** (-0.5)
        gq_ref[:, tile * 128 : (tile + 1) * 128] = turn_back(grad, cos_ref, sin_ref).astype(bf16)
    for j in range(ctx):
        dst = mine_ref if j < chips else other_ref
        at = (j % chips) * rows
        owner = meta_ref[1 + j]
        for part in range(2):
            place = owner if part == 0 else 2 * ctx - 1 - owner
            frm = pl.ds(pl.multiple_of(place * half, half), half)
            to = slice(at + part * half, at + (part + 1) * half)
            dst[to, :WIDTH_K] = gk_ref[frm, :].astype(dst.dtype)
            dst[to, WIDTH_K:] = gv_ref[frm, :].astype(dst.dtype)


SUM_ROWS = 16


def finish_kernel(
    gq_ref, x_ref, gain_ref, w_ref, cos_ref, sin_ref, gh_ref, gain_two_ref, *refs
):
    sent_ref, gx_ref, gain_grad_ref, bias_ref = refs[-4:]
    pair = refs[0][...]
    for ref in refs[1:-4]:
        pair = pair + ref[...].astype(f32)
    rows = pair.shape[0]
    keys = turn_back(pair[:, :WIDTH_K], cos_ref, sin_ref)
    pair = jnp.concatenate([keys, pair[:, WIDTH_K:]], 1).astype(bf16)
    sent_ref[:rows, :] = pair
    joint = jnp.concatenate([gq_ref[...], pair], 1)
    bias = jnp.sum(joint.astype(f32), 0, keepdims=True)
    bias_ref[...] = bias
    grad = dot_nt(joint, w_ref[...])
    x = x_ref[...].astype(f32)
    inverse = lax.rsqrt(jnp.mean(x * x, -1, keepdims=True) + EPS)
    unit = x * inverse
    gain = jnp.sum(grad * unit, 0, keepdims=True)
    gain_grad_ref[...] = gain
    scaled = grad * gain_ref[...]
    gx_ref[...] = gh_ref[...] + inverse * (
        scaled - unit * jnp.mean(scaled * unit, -1, keepdims=True)
    )
    sums = jnp.concatenate([gain, gain_two_ref[...], bias], 1)
    width = pair.shape[1]
    sums = jnp.concatenate([sums, jnp.zeros((1, -sums.shape[1] % width), f32)], 1)
    found = [sums[:, i : i + width] for i in range(0, sums.shape[1], width)]
    found += [jnp.zeros((1, width), f32)] * (SUM_ROWS - len(found))
    sums = jnp.concatenate(found, 0)
    high = sums.astype(bf16)
    sent_ref[rows : rows + SUM_ROWS, :] = high
    sent_ref[rows + SUM_ROWS :, :] = (sums - high.astype(f32)).astype(bf16)


def pair_grad_kernel(rows, half_width, meta_ref, norm_ref, own_ref, peer_ref, out_ref, turned_ref):
    turned_ref[...] = norm_ref[:, D:].T
    first = pl.multiple_of(meta_ref[0] * half_width, 16)
    both = jnp.concatenate([own_ref[:rows, :], peer_ref[:rows, :]], 0)
    part = jnp.dot(turned_ref[pl.ds(first, half_width), :], both, preferred_element_type=f32)
    out_ref[:half_width, :] = part.astype(bf16)

    def sums(ref):
        high = ref[rows : rows + SUM_ROWS, :].astype(f32)
        return high + ref[rows + SUM_ROWS :, :].astype(f32)

    out_ref[half_width:, :] = (sums(own_ref) + sums(peer_ref)).astype(bf16)


def mlp_kernel(
    half_rows, spots_ref, x_a, x_b, gy_a, gy_b, gate_a, gate_b, up_a, up_b, down_a, down_b,
    xt_ref, midt_ref, gg_ref, gu_ref, gx_ref, out_ref, send_ref,
    x_all, gy_all, wg_all, wu_all, wd_all, mid_all, gg_all, gu_all,
):
    step = pl.program_id(0)

    @pl.when(step == 0)
    def start():
        x_all[:half_rows] = x_a[...]
        x_all[half_rows:] = x_b[...]
        gy_all[:half_rows] = gy_a[...]
        gy_all[half_rows:] = gy_b[...]
        xt_ref[...] = x_all[...].T

    here = pl.ds(pl.multiple_of(step * 256, 256), 256)
    wg = jnp.concatenate([gate_a[...], gate_b[...]], 1)
    wu = jnp.concatenate([up_a[...], up_b[...]], 1)
    wd = jnp.concatenate([down_a[...], down_b[...]], 0)
    wg_all[:, here] = wg
    wu_all[:, here] = wu
    wd_all[here, :] = wd
    core = spots_ref[1]
    column = lanes((1, 256)) + (step * 256 + spots_ref[2])
    own = (column < spots_ref[3]) == (core == 0)
    x = x_all[...]
    gate = jnp.dot(x, wg, preferred_element_type=f32)
    up = jnp.dot(x, wu, preferred_element_type=f32)
    grad = jnp.where(own, dot_nt(gy_all[...], wd), 0.0)
    sigma = jax.nn.sigmoid(gate)
    active = gate * sigma
    middle = jnp.where(own, active * up, 0.0).astype(bf16)
    grad_gate = (grad * up * (sigma + active * (1.0 - sigma))).astype(bf16)
    grad_up = (grad * active).astype(bf16)
    midt_ref[...] = middle.T
    gg_ref[...] = grad_gate
    gu_ref[...] = grad_up
    mid_all[:, here] = middle
    gg_all[:, here] = grad_gate
    gu_all[:, here] = grad_up

    @pl.when(step == pl.num_programs(0) - 1)
    def end():
        gx = dot_nt(gg_all[...], wg_all[...]) + dot_nt(gu_all[...], wu_all[...])
        gx_ref[...] = gx[:half_rows]
        send_ref[:half_rows] = gx[half_rows:].astype(bf16)
        out = jnp.dot(mid_all[...], wd_all[...], preferred_element_type=f32)
        out_ref[...] = out[:half_rows]
        send_ref[half_rows:] = out[half_rows:].astype(bf16)


def feed_forward(meta, x, early, w_gate, w_up, w_down, width):
    half = x[0].shape[0]
    tokens = 2 * half
    steps = width // 256
    tiles = width // 128 - 1

    def columns(j):
        return pl.BlockSpec((D, 128), lambda i, m: (0, m[1] * tiles + 2 * i + j))

    def rows(j):
        return pl.BlockSpec((128, D), lambda i, m: (m[1] * tiles + 2 * i + j, 0))

    whole = pl.BlockSpec((tokens, D), lambda i, m: (0, 0))
    halves = pl.BlockSpec((half, D), lambda i, m: (0, 0))
    tile = pl.BlockSpec((tokens, 256), lambda i, m: (0, i))
    hidden = jax.ShapeDtypeStruct((tokens, width), bf16)
    return pl.pallas_call(
        lambda *refs: mlp_kernel(half, *refs),
        out_shape=[
            jax.ShapeDtypeStruct((D, tokens), bf16),
            jax.ShapeDtypeStruct((width, tokens), bf16),
            hidden,
            hidden,
            jax.ShapeDtypeStruct((half, D), f32),
            jax.ShapeDtypeStruct((half, D), f32),
            jax.ShapeDtypeStruct((tokens, D), bf16),
        ],
        grid_spec=pltpu.PrefetchScalarGridSpec(
            num_scalar_prefetch=1,
            grid=(steps,),
            in_specs=[halves] * 4
            + [columns(0), columns(1), columns(0), columns(1), rows(0), rows(1)],
            out_specs=[
                pl.BlockSpec((D, tokens), lambda i, m: (0, 0)),
                pl.BlockSpec((256, tokens), lambda i, m: (i, 0)),
                tile,
                tile,
                halves,
                halves,
                whole,
            ],
            scratch_shapes=[pltpu.VMEM((tokens, D), bf16)] * 2
            + [pltpu.VMEM((D, width), bf16)] * 2
            + [pltpu.VMEM((width, D), bf16)]
            + [pltpu.VMEM((tokens, width), bf16)] * 3,
        ),
        compiler_params=pltpu.CompilerParams(vmem_limit_bytes=VMEM_BYTES),
        cost_estimate=pl.CostEstimate(
            flops=12 * tokens * width * D, bytes_accessed=6 * width * D, transcendentals=0
        ),
    )(meta, *x, *early, w_gate, w_gate, w_up, w_up, w_down, w_down)


def mlp_grad_kernel(chips, down_rows, main, meta_ref, xt_ref, gy_a, gy_b, midt_ref, gg_ref, gu_ref, *refs):
    out_refs = refs[:chips]
    mlp_acc, down_acc, blocks, sems = refs[chips:]
    core = meta_ref[1]
    at_main = pl.ds(pl.multiple_of(core * 128, 128), main)
    at_tile = pl.ds(pl.multiple_of((1 - core) * main, 128), 128)
    xt = xt_ref[...]
    mlp_acc[:, :main] = jnp.dot(xt, gg_ref[:, at_main], preferred_element_type=f32).astype(bf16)
    mlp_acc[:, main : 2 * main] = jnp.dot(
        xt, gu_ref[:, at_main], preferred_element_type=f32
    ).astype(bf16)
    mixed = gg_ref[:, at_tile].astype(f32) + pltpu.roll(gu_ref[:, at_tile].astype(f32), 64, 1)
    mlp_acc[:, 2 * main :] = jnp.dot(
        xt, mixed.astype(bf16), preferred_element_type=f32
    ).astype(bf16)
    gy = jnp.concatenate([gy_a[:, :D], gy_b[:, :D]], 0)
    down_acc[...] = jnp.dot(midt_ref[...], gy, preferred_element_type=f32)

    mlp_rows = mlp_acc.shape[0] // chips
    columns = mlp_acc.shape[1] // 128
    half = chips // 2
    copies = []
    for slot in sorted(range(chips), key=lambda s: abs(s - half) if s else chips):
        owner = meta_ref[12 + slot]
        block = mlp_acc[pl.ds(pl.multiple_of(owner * mlp_rows, 16), mlp_rows), :]
        for j in range(columns):
            for i in range(mlp_rows // 16):
                blocks[slot, j * 16 : (j + 1) * 16, i * 128 : (i + 1) * 128] = block[
                    i * 16 : (i + 1) * 16, j * 128 : (j + 1) * 128
                ]
        first = pl.multiple_of(core * 64 + owner * down_rows, 8)
        blocks[slot, columns * 16 :, :] = down_acc[pl.ds(first, down_rows), :].astype(bf16)
        copy = pltpu.make_async_copy(blocks.at[slot], out_refs[slot], sems.at[slot])
        copy.start()
        copies.append(copy)
    for copy in copies:
        copy.wait()


def mlp_gradients(meta, xt, early, midt, gg, gu, after, chips, down_rows, main):
    tokens = gg.shape[0]
    columns = (2 * main + 128) // 128
    rows = columns * 16 + down_rows
    args = [meta, xt, *early, midt, gg, gu]
    anywhere = pl.BlockSpec(memory_space=pl.ANY)

    def kernel(*refs):
        mlp_grad_kernel(chips, down_rows, main, *refs[: len(args)], *refs[len(args) + 1 :])

    return pl.pallas_call(
        kernel,
        out_shape=[jax.ShapeDtypeStruct((rows, D), bf16)] * chips,
        in_specs=[pl.BlockSpec(memory_space=pltpu.SMEM)]
        + [pl.BlockSpec(memory_space=pltpu.VMEM)] * (len(args) - 1)
        + [anywhere],
        out_specs=[anywhere] * chips,
        scratch_shapes=[
            pltpu.VMEM((D, columns * 128), bf16),
            pltpu.VMEM((midt.shape[0], D), f32),
            pltpu.VMEM((chips, rows, D), bf16),
            pltpu.SemaphoreType.DMA((chips,)),
        ],
        compiler_params=pltpu.CompilerParams(vmem_limit_bytes=VMEM_BYTES),
        cost_estimate=pl.CostEstimate(
            flops=6 * tokens * midt.shape[0] * D, bytes_accessed=4 * chips * rows * D,
            transcendentals=0,
        ),
    )(*args, after)


def small_grad_kernel(
    chips, q_rows, rows, cols, meta_ref, norm_a, norm_b, att_a, att_b, near_a, near_b, *refs
):
    out_refs, acc, turned_ref = refs[:-2], refs[-2], refs[-1]
    first = pl.multiple_of((2 * meta_ref[0] + meta_ref[1]) * q_rows, 16)
    grads, queries = [], []
    for near_ref in (near_a, near_b):
        for b in range(2):
            grads.append(near_ref[2 * b * rows : (2 * b + 1) * rows, :])
            queries.append(near_ref[(2 * b + 1) * rows : (2 * b + 2) * rows, :])
    turned_ref[...] = jnp.concatenate([norm_a[:, D:], norm_b[:, D:]], 0).T
    acc[:, :WIDTH_Q] = jnp.dot(
        turned_ref[pl.ds(first, q_rows), :],
        jnp.concatenate(queries, 0),
        preferred_element_type=f32,
    ).astype(bf16)
    acc[:, WIDTH_Q:cols] = jnp.zeros((q_rows, cols - WIDTH_Q), bf16)
    turned_ref[...] = jnp.concatenate([att_a[...], att_b[...]], 0).T
    acc[:, cols:] = jnp.dot(
        turned_ref[pl.ds(first, q_rows), :], jnp.concatenate(grads, 0), preferred_element_type=f32
    ).astype(bf16)
    width = acc.shape[1] // chips
    for out_ref, slot in zip(out_refs, range(chips)):
        owner = meta_ref[12 + slot]
        block = acc[:, pl.ds(pl.multiple_of(owner * width, 128), width)]
        tall = jnp.concatenate([block[:, i * 128 : (i + 1) * 128] for i in range(width // 128)], 0)
        piece = out_ref.shape[0]
        for i in range(D // 128):
            out_ref[:, i * 128 : (i + 1) * 128] = tall[i * piece : (i + 1) * piece]


def place_all(meta, slots, pairs, old, sizes, rest=None):
    main, ff_loc, q_rows, cols, down_rows, chips = sizes
    mlp_rows = D // chips
    columns = (2 * main + 128) // 128
    tiles = main // 128
    lanes_out = D // 128
    top = columns * 16
    blocks = [x for pair in pairs for x in pair]
    count = len(blocks)
    piece = blocks[0].shape[0] - top - down_rows
    parts = (cols + D) // chips // 128
    keep = [] if old is None else list(old)
    last = [] if rest is None else list(rest)
    known = WIDTH_Q // 128

    def kernel(meta_ref, *refs):
        ins = refs[:count]
        outs_at = count + len(last) + len(keep)
        gate_out, up_out, down_out, joint_out, proj_out, token_ref = refs[outs_at : outs_at + 6]
        gate_buf, up_buf, down_buf, small_buf, rest_buf, sems, small_sems, rest_sem = refs[
            outs_at + 6 :
        ]
        core_zero = meta_ref[1] == 0
        copies = []

        def send(src, dst, sem):
            copy = pltpu.make_async_copy(src, dst, sem)
            copy.start()
            copies.append(copy)

        def column(ref, j):
            found = [
                ref[j * 16 : (j + 1) * 16, i * 128 : (i + 1) * 128] for i in range(mlp_rows // 16)
            ]
            return jnp.concatenate(found, 0).astype(f32)

        for k, slot in enumerate(slots):
            for j in range(columns):
                got = column(ins[2 * k], j)
                other = column(ins[2 * k + 1], j)
                zero = jnp.where(core_zero, got, other)
                one = jnp.where(core_zero, other, got)
                if j < 2 * tiles:
                    buf = gate_buf if j < tiles else up_buf
                    at = (j % tiles) * 128
                    buf[k, :, at : at + 128] = zero
                    buf[k, :, at + main + 128 : at + main + 256] = one
                else:
                    left = lanes(zero.shape) < 64
                    gate_buf[k, :, main : main + 128] = jnp.where(left, zero, one)
                    up_buf[k, :, main : main + 128] = pltpu.roll(jnp.where(left, one, zero), 64, 1)
            owner = meta_ref[12 + slot]
            here = pl.ds(pl.multiple_of(owner * mlp_rows, 8), mlp_rows)
            send(gate_buf.at[k], gate_out.at[here, :], sems.at[4 * k])
            send(up_buf.at[k], up_out.at[here, :], sems.at[4 * k + 1])
            for side in range(2):
                b = 2 * k + side
                core = meta_ref[1] if side == 0 else 1 - meta_ref[1]
                down_buf[b] = ins[b][top + piece :, :].astype(f32)
                here = pl.ds(pl.multiple_of((core * chips + owner) * down_rows, 8), down_rows)
                send(down_buf.at[b], down_out.at[here, :], sems.at[4 * k + 2 + side])
                tall = jnp.concatenate(
                    [ins[b][top : top + piece, i * 128 : (i + 1) * 128] for i in range(lanes_out)], 0
                ).astype(f32)
                rows = pl.ds(pl.multiple_of(core * q_rows, 8), q_rows)
                for i in range(parts):
                    small_buf[b, i] = tall[i * q_rows : (i + 1) * q_rows]
                    block = owner * parts + i

                    @pl.when(block < known)
                    def joint(b=b, i=i, rows=rows, block=block):
                        at = pl.ds(pl.multiple_of(block * 128, 128), 128)
                        pltpu.make_async_copy(
                            small_buf.at[b, i], joint_out.at[rows, at], small_sems.at[b, i]
                        ).start()

                    @pl.when(block >= cols // 128)
                    def proj(b=b, i=i, rows=rows, block=block):
                        at = pl.ds(pl.multiple_of((block - cols // 128) * 128, 128), 128)
                        pltpu.make_async_copy(
                            small_buf.at[b, i], proj_out.at[rows, at], small_sems.at[b, i]
                        ).start()

        token_ref[...] = jnp.zeros(token_ref.shape, f32)
        if last:
            rows = last[0].shape[0]
            for core, ref in ((meta_ref[1], refs[count]), (1 - meta_ref[1], refs[count + 1])):
                rest_buf[pl.ds(pl.multiple_of(core * rows, 8), rows), :] = ref[...].astype(f32)
            send(rest_buf.at[: 2 * q_rows, :], joint_out.at[:, WIDTH_Q:cols], rest_sem)
        for copy in copies:
            copy.wait()
        for b in range(count):
            for i in range(parts):
                block = meta_ref[12 + slots[b // 2]] * parts + i

                @pl.when((block < known) | (block >= cols // 128))
                def done(b=b, i=i):
                    pltpu.make_async_copy(
                        small_buf.at[b, i],
                        proj_out.at[pl.ds(0, q_rows), pl.ds(0, 128)],
                        small_sems.at[b, i],
                    ).wait()

    anywhere = pl.BlockSpec(memory_space=pl.ANY)
    result = pl.pallas_call(
        kernel,
        out_shape=[
            jax.ShapeDtypeStruct((D, ff_loc), f32),
            jax.ShapeDtypeStruct((D, ff_loc), f32),
            jax.ShapeDtypeStruct((ff_loc, D), f32),
            jax.ShapeDtypeStruct((2 * q_rows, cols), f32),
            jax.ShapeDtypeStruct((2 * q_rows, D), f32),
            jax.ShapeDtypeStruct((8, 128), f32),
        ],
        in_specs=[pl.BlockSpec(memory_space=pltpu.SMEM)]
        + [pl.BlockSpec(memory_space=pltpu.VMEM)] * (count + len(last))
        + [anywhere] * len(keep),
        out_specs=[anywhere] * 5 + [pl.BlockSpec(memory_space=pltpu.VMEM)],
        scratch_shapes=[
            pltpu.VMEM((len(slots), mlp_rows, ff_loc), f32),
            pltpu.VMEM((len(slots), mlp_rows, ff_loc), f32),
            pltpu.VMEM((count, down_rows, D), f32),
            pltpu.VMEM((count, parts, q_rows, 128), f32),
            pltpu.VMEM((2 * q_rows + SUM_ROWS, cols - WIDTH_Q), f32),
            pltpu.SemaphoreType.DMA((4 * len(slots),)),
            pltpu.SemaphoreType.DMA((count, parts)),
            pltpu.SemaphoreType.DMA,
        ],
        input_output_aliases={1 + count + len(last) + i: i for i in range(len(keep))},
        compiler_params=pltpu.CompilerParams(vmem_limit_bytes=VMEM_BYTES),
        cost_estimate=pl.CostEstimate(
            flops=0, bytes_accessed=8 * sum(x.size for x in blocks), transcendentals=0
        ),
    )(meta, *blocks, *last, *keep)
    return list(result[:5]), result[5]


def place_blocks(blocks, spots, out_shape, old=None):
    shape = blocks[0].shape
    count = len(blocks)
    if shape[0] % 8 or shape[1] % 128:
        out = jnp.zeros(out_shape, f32) if old is None else old
        for block, (i, j) in zip(blocks, spots):
            out = lax.dynamic_update_slice(
                out, block.astype(f32), (i * shape[0], j * shape[1])
            )
        return out

    def kernel(spots_ref, *refs):
        step = pl.program_id(0)
        out_ref = refs[-1]
        for i in range(count):

            @pl.when(step == i)
            def write(i=i):
                out_ref[...] = refs[i][...].astype(f32)

    keep = [] if old is None else [old]
    return pl.pallas_call(
        kernel,
        out_shape=jax.ShapeDtypeStruct(out_shape, f32),
        grid_spec=pltpu.PrefetchScalarGridSpec(
            num_scalar_prefetch=1,
            grid=(count,),
            in_specs=[pl.BlockSpec(shape, lambda i, spots: (0, 0))] * count
            + [pl.BlockSpec(memory_space=pl.ANY)] * len(keep),
            out_specs=pl.BlockSpec(shape, lambda i, spots: (spots[i, 0], spots[i, 1])),
        ),
        input_output_aliases={} if old is None else {count + 1: 0},
        compiler_params=pltpu.CompilerParams(vmem_limit_bytes=VMEM_BYTES),
    )(jnp.stack([jnp.stack(s) for s in spots]).astype(jnp.int32), *blocks, *keep)


def local(tokens, w_qkv, b_qkv, w_out, gain_attn, gain_mlp, w_gate, w_up, w_down, cotangent):
    net = Net()
    rows = tokens.shape[1]
    half_rows = rows // 2
    ctx_count = net.ctx
    core = net.core
    chips = net.chips
    part_rows = GROUP * half_rows
    x = tokens[0]
    gain_one = gain_attn[None]
    gain_two = gain_mlp[None]

    w_qkv_full = net.full_rows(w_qkv)

    ff_loc = w_gate.shape[1]
    ff_half = ff_loc // 2
    main = (ff_half // 128) * 128
    rest = ff_half - main
    width = main + 2 * rest
    first = core * main
    tiled = net.dp == 2 and 2 * rest == 128 and width % 256 == 0 and chips == 8 and ff_half == chips * RING_ROWS
    ring = jnp.arange(chips, dtype=jnp.int32)
    owners_of = (net.pos - ring) % chips
    spots = jnp.concatenate(
        [jnp.stack([net.d, core, first, jnp.int32(ff_half)]), owners_of, owners_of]
    ).astype(jnp.int32)

    row_ids = jnp.arange(half_rows, dtype=jnp.int32)
    place = jnp.concatenate(
        [net.c * half_rows + row_ids, (2 * ctx_count - 1 - net.c) * half_rows + row_ids]
    )
    freq = ROPE_BASE ** (-((jnp.arange(128) % (HD // 2)).astype(f32) * (2.0 / HD)))
    angle = place.astype(f32)[:, None] * freq[None, :]
    cosine, sine = jnp.cos(angle), jnp.sin(angle)
    normed_one, queries, pairs = call(
        qkv_kernel,
        [
            jax.ShapeDtypeStruct((rows, D), bf16),
            jax.ShapeDtypeStruct((rows, WIDTH_Q), bf16),
            jax.ShapeDtypeStruct((rows, 2 * WIDTH_K), bf16),
        ],
        [x, gain_one, w_qkv_full, b_qkv[None], cosine, sine],
        flops=2 * rows * D * 1152,
    )

    slots = net.ring_gather(pairs)
    mine = jnp.concatenate(slots, 0)
    other = net.swap(mine)
    order = jnp.array(net.order, jnp.int32)
    chip_ids = order[(net.pos - jnp.arange(chips, dtype=jnp.int32)) % chips]
    meta = jnp.concatenate([net.c[None], 2 * chip_ids + core, 2 * chip_ids + 1 - core])
    meta = meta.astype(jnp.int32)

    late_w, late_g, late_n, unused = lax.optimization_barrier((w_out, cotangent[0], normed_one, pairs))
    w_out_full = net.full_rows(late_w)
    early = net.group_parts(jnp.concatenate([late_g, late_n], 1))

    total_keys = rows * ctx_count
    padded = (KH, 2 * part_rows, 128)
    attended_low, attended, lse, spread, keys, values, hidden, normed_two = call(
        lambda *refs: forward_kernel(ctx_count, *refs),
        [
            jax.ShapeDtypeStruct((rows, WIDTH_Q), bf16),
            jax.ShapeDtypeStruct(padded, f32),
            jax.ShapeDtypeStruct((KH, 2, 8, part_rows), f32),
            jax.ShapeDtypeStruct(padded, bf16),
            jax.ShapeDtypeStruct((total_keys, WIDTH_K), bf16),
            jax.ShapeDtypeStruct((total_keys, WIDTH_K), bf16),
            jax.ShapeDtypeStruct((rows, D), f32),
            jax.ShapeDtypeStruct((rows, D), bf16),
        ],
        [meta, queries, mine, other, x, w_out_full, gain_two],
        smem=1,
        scratch=[
            pltpu.VMEM((KH, total_keys // KEYS, part_rows, KEYS), f32),
            pltpu.VMEM((KH, part_rows, 128), f32),
            pltpu.VMEM((KH, part_rows, 128), f32),
        ],
        flops=8 * KH * part_rows * total_keys * 128,
    )

    normed_two_parts = net.group_parts(normed_two)
    chip_rows = net.dp * rows
    down_rows = ff_half // chips
    mlp_rows = D // chips
    if tiled:
        x_turned, mid_turned, gate_low, up_low, grad_mine, out_mine, sent = feed_forward(
            spots, normed_two_parts, early, w_gate, w_up, w_down, width
        )
    else:
        normed_two_group = jnp.concatenate(normed_two_parts, 0)
        grad_out_group = jnp.concatenate(early, 0)[:, :D]
        own_cols = (jnp.arange(width) + first < ff_half) == (core == 0)
        wg = lax.dynamic_slice(w_gate, (0, first), (D, width))
        wu = lax.dynamic_slice(w_up, (0, first), (D, width))
        wd = lax.dynamic_slice(w_down, (first, 0), (width, D))
        gate = jnp.dot(normed_two_group, wg, preferred_element_type=f32)
        upper = jnp.dot(normed_two_group, wu, preferred_element_type=f32)
        sigma = jax.nn.sigmoid(gate)
        activated = gate * sigma
        middle = jnp.where(own_cols, activated * upper, 0.0).astype(bf16)
        grad_middle = jnp.einsum("td,fd->tf", grad_out_group, wd, preferred_element_type=f32)
        slope = sigma * (1.0 + gate * (1.0 - sigma))
        grad_gate_low = jnp.where(own_cols, grad_middle * upper * slope, 0.0).astype(bf16)
        grad_up_low = jnp.where(own_cols, grad_middle * activated, 0.0).astype(bf16)

        grad_normed_two = jnp.einsum(
            "tf,df->td", grad_gate_low, wg, preferred_element_type=f32
        ) + jnp.einsum("tf,df->td", grad_up_low, wu, preferred_element_type=f32)
        mlp_out = jnp.dot(middle, wd, preferred_element_type=f32)
        grad_mine, out_mine = grad_normed_two[:chip_rows], mlp_out[:chip_rows]
        sent = jnp.concatenate([grad_normed_two[chip_rows:], mlp_out[chip_rows:]], 0).astype(bf16)
    swapped = net.swap(sent)
    grad_chip = grad_mine + swapped[:chip_rows].astype(f32)
    mlp_chip = out_mine + swapped[chip_rows:].astype(f32)
    grad_two = grad_chip[:rows]
    for s in range(1, net.dp):
        sent_two = grad_chip[s * rows : (s + 1) * rows].astype(bf16)
        grad_two = grad_two + net.shift(sent_two, net.dp - s).astype(f32)

    def attention_back(*after):
        grad_hidden, grad_attn_low, grad_gain_two, grad_queries, terms_mine, terms_other = call(
            lambda *refs: backward_kernel(ctx_count, *refs),
            [
                jax.ShapeDtypeStruct((rows, D), f32),
                jax.ShapeDtypeStruct((rows, D), bf16),
                jax.ShapeDtypeStruct((1, D), f32),
                jax.ShapeDtypeStruct((rows, WIDTH_Q), bf16),
                jax.ShapeDtypeStruct((chips * rows, 2 * WIDTH_K), f32),
                jax.ShapeDtypeStruct((chips * rows, 2 * WIDTH_K), bf16),
            ],
            [
                meta, grad_two, hidden, cotangent[0], gain_two, w_out_full, spread, keys, values, lse,
                attended, cosine, sine, *after,
            ],
            smem=1,
            loose=len(after),
            scratch=[
                pltpu.VMEM(padded, bf16),
                pltpu.VMEM(padded, f32),
                pltpu.VMEM((total_keys, WIDTH_K), f32),
                pltpu.VMEM((total_keys, WIDTH_K), f32),
            ],
            flops=20 * KH * part_rows * total_keys * 128,
        )
        other_terms = net.swap(terms_other)

        def row_sums(*after):
            pair_sums = call(
                pair_kernel,
                [jax.ShapeDtypeStruct((rows, 2 * WIDTH_K), f32)]
                + [jax.ShapeDtypeStruct((rows, 2 * WIDTH_K), bf16)] * (chips - 1),
                [terms_mine, other_terms, *after],
                loose=len(after),
            )
            return net.ring_parts(pair_sums)

        def finish(grad_pairs):
            return call(
                finish_kernel,
                [
                    jax.ShapeDtypeStruct((rows + 2 * SUM_ROWS, 2 * WIDTH_K), bf16),
                    jax.ShapeDtypeStruct((rows, D), f32),
                    jax.ShapeDtypeStruct((1, D), f32),
                    jax.ShapeDtypeStruct((1, w_qkv.shape[1]), f32),
                ],
                [grad_queries, x, gain_one, w_qkv_full, cosine, sine, grad_hidden, grad_gain_two]
                + grad_pairs,
            )

        return grad_attn_low, grad_gain_two, grad_queries, row_sums, finish

    if tiled:
        terms = mlp_gradients(
            spots, x_turned, early, mid_turned, gate_low, up_low, sent_two, chips, down_rows, main
        )
        grad_attn_low, grad_gain_two, grad_queries, row_sums, finish = attention_back(terms[0])
        found = []

        def between(*blocks):
            found.extend(row_sums(*blocks))
            return found[1]

        fwd, back = net.ring_sum(terms, between)
        grad_pairs, marks = found
        sum_mlp, sum_down = ring_end(fwd, back, terms[0], terms[0].shape[0] - down_rows)
    else:
        part_down = jnp.einsum(
            "tf,td->fd", middle, grad_out_group, preferred_element_type=f32
        ).astype(bf16)
        part_down = lax.dynamic_slice(part_down, (core * rest, 0), (ff_half, D))

        def down_chunk(slot):
            return lax.dynamic_slice(part_down, (net.owner(slot) * down_rows, 0), (down_rows, D))

        sum_down = net.ring_scatter([down_chunk(s) for s in range(chips)]).astype(bf16)

        def split_main(x):
            left = (x[:, :main], x[:, main:])
            right = (x[:, 2 * rest :], x[:, : 2 * rest])
            return (
                jnp.where(core == 0, left[0], right[0]),
                jnp.where(core == 0, left[1], right[1]),
            )

        gate_main, gate_tile = split_main(grad_gate_low)
        up_main, up_tile = split_main(grad_up_low)
        packed = jnp.concatenate(
            [gate_main, up_main, gate_tile + jnp.roll(up_tile, rest, 1)], 1
        )
        part_mlp = jnp.einsum(
            "td,tf->df", normed_two_group, packed, preferred_element_type=f32
        ).astype(bf16)

        def mlp_chunk(slot):
            return lax.dynamic_slice(
                part_mlp, (net.owner(slot) * mlp_rows, 0), (mlp_rows, 2 * ff_half)
            )

        sum_mlp = net.ring_scatter([mlp_chunk(s) for s in range(chips)]).astype(bf16)
        sum_mlp = lax.optimization_barrier(sum_mlp)
        grad_attn_low, grad_gain_two, grad_queries, row_sums, finish = attention_back()
        grad_pairs, marks = row_sums()
    pair_sent, grad_input, grad_gain_one, grad_bias = finish(grad_pairs)

    out_sum = mlp_chip[:rows]
    for s in range(1, net.dp):
        got = net.shift(mlp_chip[s * rows : (s + 1) * rows].astype(bf16), net.dp - s)
        out_sum = out_sum + got.astype(f32)
    output = (hidden + out_sum).astype(bf16)
    near = net.group_parts(jnp.concatenate([grad_attn_low, grad_queries], 0))
    attended_parts = net.group_parts(attended_low)

    q_rows = w_qkv.shape[0] // 2
    qkv_cols = w_qkv.shape[1]
    if tiled:
        piece = q_rows * (qkv_cols + D) // chips // D
        terms_small = call(
            lambda *refs: small_grad_kernel(chips, q_rows, rows, qkv_cols, *refs),
            [jax.ShapeDtypeStruct((piece, D), bf16)] * chips,
            [spots, *early, *attended_parts, *near],
            smem=1,
            scratch=[
                pltpu.VMEM((q_rows, qkv_cols + D), bf16),
                pltpu.VMEM((D, 2 * chip_rows), bf16),
            ],
            flops=4 * chip_rows * D * (qkv_cols + D),
        )
        block = call(
            block_kernel,
            [jax.ShapeDtypeStruct((sum_mlp.shape[0] + piece + down_rows, D), bf16)],
            [sum_mlp, sum_down] + net.ring_parts(terms_small)[0] + list(marks[2]),
            loose=2,
        )[0]
        part_pair = call(
            lambda *refs: pair_grad_kernel(rows, 2 * q_rows, *refs),
            [jax.ShapeDtypeStruct((2 * q_rows + SUM_ROWS, 2 * WIDTH_K), bf16)],
            [spots, early[0], pair_sent, net.shift(pair_sent, 1)],
            smem=1,
            scratch=[pltpu.VMEM((D, chip_rows), bf16)],
        )[0]
        grad_pair, steps = net.exchange_sum(part_pair)
        pair_halves = (grad_pair, net.swap(grad_pair))
        sums = jnp.where(core == 1, *pair_halves)[-SUM_ROWS:]
        small = sums.reshape(-1)[: 2 * D + qkv_cols].astype(f32)
        sizes = (main, ff_loc, q_rows, qkv_cols, down_rows, chips)
        grad_gate, grad_up, grad_down, grad_joint, grad_out_proj = net.gather_placed(
            block,
            lambda slots, pairs, old, rest=None: place_all(spots, slots, pairs, old, sizes, rest),
            pair_halves,
            [[part_pair], [steps[1]], [steps[2]]],
        )
    else:
        gathered = jnp.concatenate(near, 0).reshape(2 * net.dp, 2, rows, D)
        grad_attn_group = gathered[:, 0].reshape(2 * net.dp * rows, D)
        attended_group = jnp.concatenate(attended_parts, 0)
        normed_one_group = jnp.concatenate(early, 0)[:, D:]
        joint_group = net.group_gather(jnp.concatenate([grad_queries, pair_sent[:rows]], 1))
        q_first = net.d * (2 * q_rows) + core * q_rows
        group_rows = 2 * net.dp * rows
        part_out = jnp.einsum(
            "tc,td->cd",
            lax.dynamic_slice(attended_group, (0, q_first), (group_rows, q_rows)),
            grad_attn_group,
            preferred_element_type=f32,
        )
        part_joint = jnp.einsum(
            "td,tc->dc",
            lax.dynamic_slice(normed_one_group, (0, q_first), (group_rows, q_rows)),
            joint_group,
            preferred_element_type=f32,
        )
        part_small = jnp.concatenate([part_joint, part_out], 1).astype(bf16)
        small_cols = part_small.shape[1] // chips

        def small_chunk(slot):
            return lax.dynamic_slice(part_small, (0, net.owner(slot) * small_cols), (q_rows, small_cols))

        sum_small = net.ring_scatter([small_chunk(s) for s in range(chips)]).astype(bf16)

        tall = jnp.concatenate(
            [sum_small[:, i * 128 : (i + 1) * 128] for i in range(small_cols // 128)], 0
        )
        piece = tall.shape[0] // (D // 128)
        wide = jnp.concatenate([tall[i * piece : (i + 1) * piece] for i in range(D // 128)], 1)
        both = lax.optimization_barrier(jnp.concatenate([sum_down, wide], 0))

        owners = [net.owner(s) for s in range(chips)]
        got_mlp = net.ring_gather(sum_mlp)
        got_both = net.ring_gather(both)
        pairs_mlp = [(got, net.swap(got)) for got in got_mlp]
        pairs_both = [(got, net.swap(got)) for got in got_both]

        down_blocks, down_spots, small_blocks, small_spots = [], [], [], []
        for owner, pair in zip(owners, pairs_both):
            for which, got in zip((core, 1 - core), pair):
                down_blocks.append(got[:down_rows])
                down_spots.append((which * chips + owner, jnp.int32(0)))
                wide = got[down_rows:]
                tall = jnp.concatenate([wide[:, i * 128 : (i + 1) * 128] for i in range(D // 128)], 0)
                small_blocks.append(
                    jnp.concatenate(
                        [tall[i * q_rows : (i + 1) * q_rows] for i in range(small_cols // 128)], 1
                    )
                )
                small_spots.append((which, owner))
        grad_down = place_blocks(down_blocks, down_spots, (ff_loc, D))
        grad_small = place_blocks(small_blocks, small_spots, (2 * q_rows, part_small.shape[1]))
        grad_gate = jnp.zeros((D, ff_loc), f32)
        grad_up = jnp.zeros((D, ff_loc), f32)
        left_lane = jnp.arange(2 * rest) < rest
        for owner, (got, swapped) in zip(owners, pairs_mlp):
            zero = jnp.where(core == 0, got, swapped).astype(f32)
            one = jnp.where(core == 0, swapped, got).astype(f32)
            tile_zero, tile_one = zero[:, 2 * main :], one[:, 2 * main :]
            mid_gate = jnp.where(left_lane, tile_zero, tile_one)
            mid_up = jnp.roll(jnp.where(left_lane, tile_one, tile_zero), rest, 1)
            base = owner * mlp_rows
            grad_gate = lax.dynamic_update_slice(
                grad_gate, jnp.concatenate([zero[:, :main], mid_gate, one[:, :main]], 1), (base, 0)
            )
            grad_up = lax.dynamic_update_slice(
                grad_up,
                jnp.concatenate([zero[:, main : 2 * main], mid_up, one[:, main : 2 * main]], 1),
                (base, 0),
            )

        grad_joint, grad_out_proj = grad_small[:, :qkv_cols], grad_small[:, qkv_cols:]
        small = net.total(jnp.concatenate([grad_gain_one, grad_gain_two, grad_bias], 1))[0]
    return (
        output[None],
        grad_input[None],
        grad_joint,
        small[2 * D :],
        grad_out_proj,
        small[:D],
        small[D : 2 * D],
        grad_gate,
        grad_up,
        grad_down,
    )


def solution(mesh):
    placed = (
        P("dp", "ctx", None),
        P("dp", None),
        P(),
        P("dp", None),
        P(),
        P(),
        P(None, "dp"),
        P(None, "dp"),
        P("dp", None),
        P("dp", "ctx", None),
    )
    return jax.shard_map(
        local,
        mesh=mesh,
        in_specs=placed,
        out_specs=(
            P("dp", "ctx", None),
            P("dp", "ctx", None),
            P("dp", None),
            P(),
            P("dp", None),
            P(),
            P(),
            P(None, "dp"),
            P(None, "dp"),
            P("dp", None),
        ),
        check_vma=False,
    )
```

```python
import jax
import jax.numpy as jnp
from jax import lax
from jax.experimental import pallas as pl
from jax.experimental.pallas import tpu as pltpu
from jax.sharding import PartitionSpec as P

D = 896
QH = 14
KH = 2
HD = 64
GROUP = QH // KH
WIDTH_Q = QH * HD
WIDTH_K = KH * HD

EPS = 1e-06
ROPE_BASE = 1000000.0

f32 = jnp.float32
bf16 = jnp.bfloat16


def ring_order(chips):
    if chips % 2:
        return list(range(chips))
    rows = chips // 2
    return [2 * i for i in range(rows)] + [2 * i + 1 for i in reversed(range(rows))]


def half_cut(rows):
    cut = (rows // 2 + 7) // 8 * 8
    return cut if cut < rows else rows // 2


class Net:
    def __init__(self):
        self.dp = lax.axis_size("dp")
        self.ctx = lax.axis_size("ctx")
        self.chips = self.ctx // 2
        self.order = ring_order(self.chips)
        self.d = lax.axis_index("dp")
        self.c = lax.axis_index("ctx")
        self.core = self.c % 2
        place = [0] * self.chips
        for spot, chip in enumerate(self.order):
            place[chip] = spot
        self.pos = jnp.array(place, jnp.int32)[self.c // 2]

    def swap(self, x):
        return lax.ppermute(x, "ctx", [(i, i ^ 1) for i in range(self.ctx)])

    def shift(self, x, step):
        n = self.dp
        return lax.ppermute(x, "dp", [(i, (i + step) % n) for i in range(n)])

    def hop(self, x, step):
        n = self.chips
        perm = []
        for spot in range(n):
            for core in range(2):
                perm.append((2 * self.order[spot] + core, 2 * self.order[(spot + step) % n] + core))
        return lax.ppermute(x, "ctx", perm)

    def owner(self, slot):
        return (self.pos - slot) % self.chips

    def group_parts(self, x):
        chip = jnp.concatenate([x] + [self.shift(x, s) for s in range(1, self.dp)], 0)
        return chip, self.swap(chip)

    def group_gather(self, x):
        return jnp.concatenate(self.group_parts(x), 0)

    def ring_gather(self, x):
        n = self.chips
        half = n // 2
        cut = half_cut(x.shape[0])
        found = [x] + [None] * (n - 1)
        fwd, back = x, x
        for s in range(1, half):
            fwd = self.hop(fwd, 1)
            back = self.hop(back, -1)
            found[s] = fwd
            found[n - s] = back
        found[half] = jnp.concatenate([self.hop(fwd[:cut], 1), self.hop(back[cut:], -1)], 0)
        return found

    def ring_scatter(self, local):
        n = self.chips
        half = n // 2
        cut = half_cut(local[half].shape[0])

        def add(got, mine):
            return (got.astype(f32) + mine.astype(f32)).astype(bf16)

        fwd = self.hop(local[half][:cut], 1)
        back = self.hop(local[half][cut:], -1)
        for s in range(1, half):
            mine_f = local[half + s]
            mine_b = local[half - s]
            if s == 1:
                mine_f = jnp.concatenate([add(fwd, mine_f[:cut]), mine_f[cut:]], 0)
                mine_b = jnp.concatenate([mine_b[:cut], add(back, mine_b[cut:])], 0)
            else:
                mine_f = add(fwd, mine_f)
                mine_b = add(back, mine_b)
            fwd = self.hop(mine_f, 1)
            back = self.hop(mine_b, -1)
        return fwd.astype(f32) + back.astype(f32) + local[0].astype(f32)

    def full_rows(self, shard):
        rows = shard.shape[0]
        half = rows // 2
        piece = lax.dynamic_slice(shard, (self.core * half, 0), (half, shard.shape[1]))
        blocks = [shard]
        for s in range(1, self.dp):
            got = self.shift(piece, s)
            other = self.swap(got)
            low = jnp.where(self.core == 0, got, other)
            high = jnp.where(self.core == 0, other, got)
            blocks.append(jnp.concatenate([low, high], 0))
        if self.dp == 2:
            first = jnp.where(self.d == 0, blocks[0], blocks[1])
            second = jnp.where(self.d == 0, blocks[1], blocks[0])
            return jnp.concatenate([first, second], 0)
        ranked = jnp.stack(blocks)[(self.d - jnp.arange(self.dp)) % self.dp]
        return ranked.reshape(self.dp * rows, shard.shape[1])

    def total(self, x):
        x = x + self.swap(x)
        bit = 1
        while bit < self.chips:
            x = x + lax.ppermute(x, "ctx", [(i, i ^ (2 * bit)) for i in range(self.ctx)])
            bit *= 2
        bit = 1
        while bit < self.dp:
            x = x + lax.ppermute(x, "dp", [(i, i ^ bit) for i in range(self.dp)])
            bit *= 2
        return x

    def ring_parts(self, local):
        n = self.chips
        half = n // 2
        cut = half_cut(local[half].shape[0])

        def add(got, mine):
            return (got.astype(f32) + mine.astype(f32)).astype(bf16)

        fwd, back = self.hop(local[half][:cut], 1), self.hop(local[half][cut:], -1)
        marks = [(fwd, back)]
        for s in range(1, half):
            mine_f, mine_b = local[half + s], local[half - s]
            if s == 1:
                mine_f = jnp.concatenate([add(fwd, mine_f[:cut]), mine_f[cut:]], 0)
                mine_b = jnp.concatenate([mine_b[:cut], add(back, mine_b[cut:])], 0)
            else:
                mine_f, mine_b = add(fwd, mine_f), add(back, mine_b)
            fwd, back = self.hop(mine_f, 1), self.hop(mine_b, -1)
            marks.append((fwd, back))
        return [local[0], fwd, back], marks

    def exchange_sum(self, x):
        half = x.shape[0] // 2

        def add(a, b):
            return (a.astype(f32) + b.astype(f32)).astype(bf16)

        x = add(x, self.swap(x))
        x = lax.dynamic_slice(x, (self.core * half, 0), (half, x.shape[1]))
        marks = [x]
        bit = 1
        while bit < self.chips:
            x = add(x, lax.ppermute(x, "ctx", [(i, i ^ (2 * bit)) for i in range(self.ctx)]))
            marks.append(x)
            bit *= 2
        return x, marks

    def ring_sum(self, terms, between):
        half = self.chips // 2
        fwd, back = self.hop(terms[half], 1), self.hop(terms[half - 1], -1)

        def add(got, slot):
            return (got.astype(f32) + terms[slot].astype(f32)).astype(bf16)

        for s in range(1, half):
            blocks = [add(fwd, half + s)]
            if s < half - 1:
                blocks.append(add(back, half - 1 - s))
            if s == 1:
                marks = between(*blocks)
            else:
                blocks = gate(marks[s - 2], blocks)
            fwd = self.hop(blocks[0], 1)
            if s < half - 1:
                back = self.hop(blocks[1], -1)
        return fwd, back

    def gather_placed(self, x, place, rest, marks):
        n = self.chips
        half = n // 2
        fwd = back = x
        placed = None
        waiting = ([0], [(x, self.swap(x))])
        for s in range(1, half + 1):
            if s > 1:
                placed, token = place(*waiting, placed)
                fwd, back = gate([token] + marks[s - 2], [fwd, back])
                waiting = ([s - 1, n - s + 1], [(fwd, self.swap(fwd)), (back, self.swap(back))])
            if s < half:
                fwd, back = self.hop(fwd, 1), self.hop(back, -1)
            else:
                cut = half_cut(fwd.shape[0])
                fwd, back = self.hop(fwd[:cut], 1), self.hop(back[cut:], -1)
        placed, token = place(*waiting, placed)
        far = join(fwd, back, token)
        return place([half], [(far, self.swap(far))], placed, rest)[0]


VMEM_BYTES = 56 * 1024 * 1024
KEYS = 256
RING_ROWS = 152


def full_spec(shape):
    return pl.BlockSpec(shape, lambda: (0,) * len(shape))


def call(kernel, outs, args, smem=0, scratch=(), flops=0, loose=0):
    tight = len(args) - loose
    specs = [pl.BlockSpec(memory_space=pltpu.SMEM)] * smem
    specs += [pl.BlockSpec(memory_space=pltpu.VMEM)] * (tight - smem)
    specs += [pl.BlockSpec(memory_space=pl.ANY)] * loose

    def body(*refs):
        kernel(*refs[:tight], *refs[tight + loose :])

    moved = sum(x.size * x.dtype.itemsize for x in list(args) + list(outs))
    return pl.pallas_call(
        body,
        out_shape=list(outs),
        in_specs=specs,
        out_specs=[pl.BlockSpec(memory_space=pltpu.VMEM)] * len(outs),
        scratch_shapes=list(scratch),
        compiler_params=pltpu.CompilerParams(vmem_limit_bytes=VMEM_BYTES),
        cost_estimate=pl.CostEstimate(flops=flops, bytes_accessed=moved, transcendentals=0),
    )(*args)


def lanes(shape):
    return lax.broadcasted_iota(jnp.int32, shape, len(shape) - 1)


def dot_nt(a, b, precision=None):
    return lax.dot_general(
        a, b, (((1,), (1,)), ((), ())), preferred_element_type=f32, precision=precision
    )


def dot_tn(a, b):
    return lax.dot_general(a, b, (((0,), (0,)), ((), ())), preferred_element_type=f32)


def gate(tokens, blocks):
    count, before = len(blocks), len(tokens)
    anywhere = pl.BlockSpec(memory_space=pl.ANY)

    def kernel(*refs):
        return None

    return pl.pallas_call(
        kernel,
        out_shape=[jax.ShapeDtypeStruct(x.shape, x.dtype) for x in blocks],
        in_specs=[anywhere] * (before + count),
        out_specs=[anywhere] * count,
        input_output_aliases={before + i: i for i in range(count)},
        cost_estimate=pl.CostEstimate(flops=0, bytes_accessed=1024, transcendentals=0),
    )(*tokens, *blocks)


def join(first, second, token):
    cut = first.shape[0]

    def kernel(first_ref, second_ref, out_ref):
        out_ref[:cut, :] = first_ref[...]
        out_ref[cut:, :] = second_ref[...]

    shape = (cut + second.shape[0], first.shape[1])
    return call(
        kernel, [jax.ShapeDtypeStruct(shape, first.dtype)], [first, second, token], loose=1
    )[0]


def ring_end(fwd, back, term, split):
    rows, columns = term.shape

    def kernel(fwd_ref, back_ref, term_ref, first_ref, rest_ref):
        for ref, here in ((first_ref, slice(0, split)), (rest_ref, slice(split, rows))):
            total = fwd_ref[here, :].astype(f32) + back_ref[here, :].astype(f32)
            ref[...] = (total + term_ref[here, :].astype(f32)).astype(bf16)

    outs = [
        jax.ShapeDtypeStruct((split, columns), bf16),
        jax.ShapeDtypeStruct((rows - split, columns), bf16),
    ]
    return call(kernel, outs, [fwd, back, term])


def pair_kernel(mine_ref, got_ref, *out_refs):
    rows = out_refs[0].shape[0]
    for s, out_ref in enumerate(out_refs):
        here = slice(s * rows, (s + 1) * rows)
        out_ref[...] = (mine_ref[here, :] + got_ref[here, :].astype(f32)).astype(out_ref.dtype)


def block_kernel(mlp_ref, down_ref, *refs):
    small = refs[0][...].astype(f32)
    for ref in refs[1:-1]:
        small = small + ref[...].astype(f32)
    out_ref = refs[-1]
    top = mlp_ref.shape[0]
    piece = small.shape[0]
    out_ref[:top, :] = mlp_ref[...]
    out_ref[top : top + piece, :] = small.astype(bf16)
    out_ref[top + piece :, :] = down_ref[...]


def qkv_kernel(x_ref, gain_ref, w_ref, b_ref, cos_ref, sin_ref, norm_ref, q_ref, pair_ref):
    x = x_ref[...].astype(f32)
    inverse = lax.rsqrt(jnp.mean(x * x, -1, keepdims=True) + EPS)
    normed = (x * inverse * gain_ref[...]).astype(bf16)
    norm_ref[...] = normed
    joint = jnp.dot(normed, w_ref[...], preferred_element_type=f32) + b_ref[...]
    cosine = cos_ref[...]
    sine = sin_ref[...]
    early = lanes(cosine.shape) % HD < HD // 2
    for i in range((WIDTH_Q + WIDTH_K) // 128):
        tile = joint[:, i * 128 : (i + 1) * 128]
        turned = jnp.where(early, -pltpu.roll(tile, 96, 1), pltpu.roll(tile, 32, 1))
        turned = tile * cosine + turned * sine
        if i * 128 < WIDTH_Q:
            q_ref[:, i * 128 : (i + 1) * 128] = turned.astype(bf16)
        else:
            pair_ref[:, :WIDTH_K] = turned.astype(bf16)
    pair_ref[:, WIDTH_K:] = joint[:, WIDTH_Q + WIDTH_K :].astype(bf16)


def spread_heads(x, out_ref, factor):
    rows = x.shape[0]
    half = rows // 2
    for head in range(QH):
        kh, g = divmod(head, GROUP)
        tile = x[:, (head // 2) * 128 : (head // 2 + 1) * 128].astype(f32)
        if head % 2 != kh:
            tile = pltpu.roll(tile, HD, 1)
        tile = jnp.where(lanes(tile.shape) // HD == kh, tile * factor, 0.0).astype(out_ref.dtype)
        for part in range(2):
            start = (part * GROUP + g) * half
            out_ref[kh, start : start + half, :] = tile[part * half : (part + 1) * half]


def join_heads(src_ref, half, tile):
    sides = []
    for side in range(2):
        kh, g = divmod(2 * tile + side, GROUP)
        parts = [
            src_ref[kh, (part * GROUP + g) * half : (part * GROUP + g + 1) * half, :]
            for part in range(2)
        ]
        both = jnp.concatenate(parts, 0)
        sides.append(both if side == kh else pltpu.roll(both, HD, 1))
    return jnp.where(lanes(sides[0].shape) < HD, sides[0], sides[1])


def forward_kernel(
    ctx, meta_ref, q_ref, mine_ref, other_ref, x_ref, w_ref, gain_ref,
    low_ref, o_ref, lse_ref, spread_ref, k_ref, v_ref, hidden_ref, normed_ref,
    s_ref, max_ref, sum_ref,
):
    rows = q_ref.shape[0]
    half = rows // 2
    part_rows = GROUP * half
    me = meta_ref[0]
    chips = ctx // 2
    for j in range(ctx):
        src = mine_ref if j < chips else other_ref
        at = (j % chips) * rows
        owner = meta_ref[1 + j]
        for part in range(2):
            place = owner if part == 0 else 2 * ctx - 1 - owner
            to = pl.ds(pl.multiple_of(place * half, half), half)
            block = src[at + part * half : at + (part + 1) * half, :]
            k_ref[to, :] = block[:, :WIDTH_K]
            v_ref[to, :] = block[:, WIDTH_K:]
    spread_heads(q_ref[...], spread_ref, HD ** (-0.5))
    for part in range(2):
        span = slice(part * part_rows, (part + 1) * part_rows)
        start = (me if part == 0 else 2 * ctx - 1 - me) * half
        last = start // KEYS

        def keys_of(ref, i):
            return ref[pl.ds(pl.multiple_of(i * KEYS, KEYS), KEYS), :]

        for kh in range(KH):
            scores = dot_nt(spread_ref[kh, span, :], keys_of(k_ref, last))
            row = lax.broadcasted_iota(jnp.int32, scores.shape, 0) % half + start
            scores = jnp.where(lanes(scores.shape) + last * KEYS <= row, scores, -1e30)
            s_ref[kh, last] = scores
            max_ref[kh] = jnp.maximum(scores[:, :128], scores[:, 128:])

        def score(i, carry):
            for kh in range(KH):
                s = dot_nt(spread_ref[kh, span, :], keys_of(k_ref, i))
                s_ref[kh, i] = s
                max_ref[kh] = jnp.maximum(max_ref[kh], jnp.maximum(s[:, :128], s[:, 128:]))
            return carry

        lax.fori_loop(0, last, score, 0)
        for kh in range(KH):
            top = jnp.max(max_ref[kh], -1, keepdims=True)
            max_ref[kh] = jnp.broadcast_to(top, (part_rows, 128))
            sum_ref[kh] = jnp.zeros((part_rows, 128), f32)
            o_ref[kh, span, :] = jnp.zeros((part_rows, 128), f32)

        def weigh(i, carry):
            for kh in range(KH):
                s = s_ref[kh, i]
                top = max_ref[kh]
                left = jnp.exp(s[:, :128] - top)
                right = jnp.exp(s[:, 128:] - top)
                sum_ref[kh] += left + right
                o_ref[kh, span, :] += jnp.dot(
                    jnp.concatenate([left, right], 1).astype(bf16),
                    keys_of(v_ref, i),
                    preferred_element_type=f32,
                )
            return carry

        lax.fori_loop(0, last + 1, weigh, 0)
        for kh in range(KH):
            total = jnp.sum(sum_ref[kh], -1, keepdims=True)
            o_ref[kh, span, :] = o_ref[kh, span, :] / total
            lse_ref[kh, part] = dot_nt(
                jnp.full((8, 128), 1.0 / 128, f32),
                max_ref[kh] + jnp.log(total),
                lax.Precision.HIGHEST,
            )
    for tile in range(WIDTH_Q // 128):
        low_ref[:, tile * 128 : (tile + 1) * 128] = join_heads(o_ref, half, tile).astype(bf16)
    hidden = x_ref[...].astype(f32) + jnp.dot(low_ref[...], w_ref[...], preferred_element_type=f32)
    hidden_ref[...] = hidden
    inverse = lax.rsqrt(jnp.mean(hidden * hidden, -1, keepdims=True) + EPS)
    normed_ref[...] = (hidden * inverse * gain_ref[...]).astype(bf16)


def turn_back(grad, cos_ref, sin_ref):
    scaled = grad * sin_ref[...]
    early = lanes(grad.shape) % HD < HD // 2
    turned = jnp.where(early, pltpu.roll(scaled, 96, 1), -pltpu.roll(scaled, 32, 1))
    return grad * cos_ref[...] + turned


def backward_kernel(
    ctx, meta_ref, gn_ref, hidden_ref, gout_ref, gain_ref, w_ref, spread_ref, k_ref, v_ref, lse_ref,
    o_ref, cos_ref, sin_ref,
    gh_ref, ga_ref, gain_grad_ref, gq_ref, mine_ref, other_ref,
    go_ref, gqs_ref, gk_ref, gv_ref,
):
    rows = gn_ref.shape[0]
    half = rows // 2
    part_rows = GROUP * half
    me = meta_ref[0]
    chips = ctx // 2
    hidden = hidden_ref[...]
    inverse = lax.rsqrt(jnp.mean(hidden * hidden, -1, keepdims=True) + EPS)
    unit = hidden * inverse
    grad = gn_ref[...]
    gain_grad_ref[...] = jnp.sum(grad * unit, 0, keepdims=True)
    scaled = grad * gain_ref[...]
    gh = gout_ref[...].astype(f32) + inverse * (
        scaled - unit * jnp.mean(scaled * unit, -1, keepdims=True)
    )
    gh_ref[...] = gh
    ga = gh.astype(bf16)
    ga_ref[...] = ga
    spread_heads(dot_nt(ga, w_ref[...]).astype(bf16), go_ref, 1.0)
    gqs_ref[...] = jnp.zeros_like(gqs_ref)
    gk_ref[...] = jnp.zeros_like(gk_ref)
    gv_ref[...] = jnp.zeros_like(gv_ref)
    for part in range(2):
        span = slice(part * part_rows, (part + 1) * part_rows)
        start = (me if part == 0 else 2 * ctx - 1 - me) * half
        last = start // KEYS
        deltas = [
            dot_nt(
                jnp.ones((8, 128), f32),
                go_ref[kh, span, :].astype(f32) * o_ref[kh, span, :],
                lax.Precision.HIGHEST,
            )[:1]
            for kh in range(KH)
        ]

        def step(i, masked):
            at = pl.ds(pl.multiple_of(i * KEYS, KEYS), KEYS)
            keys = k_ref[at, :]
            grad_k = gk_ref[at, :]
            grad_v = gv_ref[at, :]
            for kh in range(KH):
                queries = spread_ref[kh, span, :]
                heads = go_ref[kh, span, :]
                p = jnp.exp(dot_nt(keys, queries) - lse_ref[kh, part][:1])
                if masked:
                    row = lanes(p.shape) % half + start
                    key = lax.broadcasted_iota(jnp.int32, p.shape, 0) + i * KEYS
                    p = jnp.where(key <= row, p, 0.0)
                gs = (p * (dot_nt(v_ref[at, :], heads) - deltas[kh])).astype(bf16)
                grad_v += jnp.dot(p.astype(bf16), heads, preferred_element_type=f32)
                grad_k += jnp.dot(gs, queries, preferred_element_type=f32)
                gqs_ref[kh, span, :] += dot_tn(gs, keys)
            gk_ref[at, :] = grad_k
            gv_ref[at, :] = grad_v

        def body(i, carry):
            step(i, False)
            return carry

        lax.fori_loop(0, last, body, 0)
        step(last, True)
    for tile in range(WIDTH_Q // 128):
        grad = join_heads(gqs_ref, half, tile) * HD ** (-0.5)
        gq_ref[:, tile * 128 : (tile + 1) * 128] = turn_back(grad, cos_ref, sin_ref).astype(bf16)
    for j in range(ctx):
        dst = mine_ref if j < chips else other_ref
        at = (j % chips) * rows
        owner = meta_ref[1 + j]
        for part in range(2):
            place = owner if part == 0 else 2 * ctx - 1 - owner
            frm = pl.ds(pl.multiple_of(place * half, half), half)
            to = slice(at + part * half, at + (part + 1) * half)
            dst[to, :WIDTH_K] = gk_ref[frm, :].astype(dst.dtype)
            dst[to, WIDTH_K:] = gv_ref[frm, :].astype(dst.dtype)


SUM_ROWS = 16


def finish_kernel(
    gq_ref, x_ref, gain_ref, w_ref, cos_ref, sin_ref, gh_ref, gain_two_ref, *refs
):
    sent_ref, gx_ref, gain_grad_ref, bias_ref = refs[-4:]
    pair = refs[0][...]
    for ref in refs[1:-4]:
        pair = pair + ref[...].astype(f32)
    rows = pair.shape[0]
    keys = turn_back(pair[:, :WIDTH_K], cos_ref, sin_ref)
    pair = jnp.concatenate([keys, pair[:, WIDTH_K:]], 1).astype(bf16)
    sent_ref[:rows, :] = pair
    joint = jnp.concatenate([gq_ref[...], pair], 1)
    bias = jnp.sum(joint.astype(f32), 0, keepdims=True)
    bias_ref[...] = bias
    grad = dot_nt(joint, w_ref[...])
    x = x_ref[...].astype(f32)
    inverse = lax.rsqrt(jnp.mean(x * x, -1, keepdims=True) + EPS)
    unit = x * inverse
    gain = jnp.sum(grad * unit, 0, keepdims=True)
    gain_grad_ref[...] = gain
    scaled = grad * gain_ref[...]
    gx_ref[...] = gh_ref[...] + inverse * (
        scaled - unit * jnp.mean(scaled * unit, -1, keepdims=True)
    )
    sums = jnp.concatenate([gain, gain_two_ref[...], bias], 1)
    width = pair.shape[1]
    sums = jnp.concatenate([sums, jnp.zeros((1, -sums.shape[1] % width), f32)], 1)
    found = [sums[:, i : i + width] for i in range(0, sums.shape[1], width)]
    found += [jnp.zeros((1, width), f32)] * (SUM_ROWS - len(found))
    sums = jnp.concatenate(found, 0)
    high = sums.astype(bf16)
    sent_ref[rows : rows + SUM_ROWS, :] = high
    sent_ref[rows + SUM_ROWS :, :] = (sums - high.astype(f32)).astype(bf16)


def pair_grad_kernel(rows, half_width, meta_ref, norm_ref, own_ref, peer_ref, out_ref, turned_ref):
    turned_ref[...] = norm_ref[:, D:].T
    first = pl.multiple_of(meta_ref[0] * half_width, 16)
    both = jnp.concatenate([own_ref[:rows, :], peer_ref[:rows, :]], 0)
    part = jnp.dot(turned_ref[pl.ds(first, half_width), :], both, preferred_element_type=f32)
    out_ref[:half_width, :] = part.astype(bf16)

    def sums(ref):
        high = ref[rows : rows + SUM_ROWS, :].astype(f32)
        return high + ref[rows + SUM_ROWS :, :].astype(f32)

    out_ref[half_width:, :] = (sums(own_ref) + sums(peer_ref)).astype(bf16)


def mlp_kernel(
    half_rows, spots_ref, x_a, x_b, gy_a, gy_b, gate_a, gate_b, up_a, up_b, down_a, down_b,
    xt_ref, midt_ref, gg_ref, gu_ref, gx_ref, out_ref, send_ref,
    x_all, gy_all, wg_all, wu_all, wd_all, mid_all, gg_all, gu_all,
):
    step = pl.program_id(0)

    @pl.when(step == 0)
    def start():
        x_all[:half_rows] = x_a[...]
        x_all[half_rows:] = x_b[...]
        gy_all[:half_rows] = gy_a[...]
        gy_all[half_rows:] = gy_b[...]
        xt_ref[...] = x_all[...].T

    here = pl.ds(pl.multiple_of(step * 256, 256), 256)
    wg = jnp.concatenate([gate_a[...], gate_b[...]], 1)
    wu = jnp.concatenate([up_a[...], up_b[...]], 1)
    wd = jnp.concatenate([down_a[...], down_b[...]], 0)
    wg_all[:, here] = wg
    wu_all[:, here] = wu
    wd_all[here, :] = wd
    core = spots_ref[1]
    column = lanes((1, 256)) + (step * 256 + spots_ref[2])
    own = (column < spots_ref[3]) == (core == 0)
    x = x_all[...]
    gate = jnp.dot(x, wg, preferred_element_type=f32)
    up = jnp.dot(x, wu, preferred_element_type=f32)
    grad = jnp.where(own, dot_nt(gy_all[...], wd), 0.0)
    sigma = jax.nn.sigmoid(gate)
    active = gate * sigma
    middle = jnp.where(own, active * up, 0.0).astype(bf16)
    grad_gate = (grad * up * (sigma + active * (1.0 - sigma))).astype(bf16)
    grad_up = (grad * active).astype(bf16)
    midt_ref[...] = middle.T
    gg_ref[...] = grad_gate
    gu_ref[...] = grad_up
    mid_all[:, here] = middle
    gg_all[:, here] = grad_gate
    gu_all[:, here] = grad_up

    @pl.when(step == pl.num_programs(0) - 1)
    def end():
        gx = dot_nt(gg_all[...], wg_all[...]) + dot_nt(gu_all[...], wu_all[...])
        gx_ref[...] = gx[:half_rows]
        send_ref[:half_rows] = gx[half_rows:].astype(bf16)
        out = jnp.dot(mid_all[...], wd_all[...], preferred_element_type=f32)
        out_ref[...] = out[:half_rows]
        send_ref[half_rows:] = out[half_rows:].astype(bf16)


def feed_forward(meta, x, early, w_gate, w_up, w_down, width):
    half = x[0].shape[0]
    tokens = 2 * half
    steps = width // 256
    tiles = width // 128 - 1

    def columns(j):
        return pl.BlockSpec((D, 128), lambda i, m: (0, m[1] * tiles + 2 * i + j))

    def rows(j):
        return pl.BlockSpec((128, D), lambda i, m: (m[1] * tiles + 2 * i + j, 0))

    whole = pl.BlockSpec((tokens, D), lambda i, m: (0, 0))
    halves = pl.BlockSpec((half, D), lambda i, m: (0, 0))
    tile = pl.BlockSpec((tokens, 256), lambda i, m: (0, i))
    hidden = jax.ShapeDtypeStruct((tokens, width), bf16)
    return pl.pallas_call(
        lambda *refs: mlp_kernel(half, *refs),
        out_shape=[
            jax.ShapeDtypeStruct((D, tokens), bf16),
            jax.ShapeDtypeStruct((width, tokens), bf16),
            hidden,
            hidden,
            jax.ShapeDtypeStruct((half, D), f32),
            jax.ShapeDtypeStruct((half, D), f32),
            jax.ShapeDtypeStruct((tokens, D), bf16),
        ],
        grid_spec=pltpu.PrefetchScalarGridSpec(
            num_scalar_prefetch=1,
            grid=(steps,),
            in_specs=[halves] * 4
            + [columns(0), columns(1), columns(0), columns(1), rows(0), rows(1)],
            out_specs=[
                pl.BlockSpec((D, tokens), lambda i, m: (0, 0)),
                pl.BlockSpec((256, tokens), lambda i, m: (i, 0)),
                tile,
                tile,
                halves,
                halves,
                whole,
            ],
            scratch_shapes=[pltpu.VMEM((tokens, D), bf16)] * 2
            + [pltpu.VMEM((D, width), bf16)] * 2
            + [pltpu.VMEM((width, D), bf16)]
            + [pltpu.VMEM((tokens, width), bf16)] * 3,
        ),
        compiler_params=pltpu.CompilerParams(vmem_limit_bytes=VMEM_BYTES),
        cost_estimate=pl.CostEstimate(
            flops=12 * tokens * width * D, bytes_accessed=6 * width * D, transcendentals=0
        ),
    )(meta, *x, *early, w_gate, w_gate, w_up, w_up, w_down, w_down)


def mlp_grad_kernel(chips, down_rows, main, meta_ref, xt_ref, gy_a, gy_b, midt_ref, gg_ref, gu_ref, *refs):
    out_refs = refs[:chips]
    mlp_acc, down_acc, blocks, sems = refs[chips:]
    core = meta_ref[1]
    at_main = pl.ds(pl.multiple_of(core * 128, 128), main)
    at_tile = pl.ds(pl.multiple_of((1 - core) * main, 128), 128)
    xt = xt_ref[...]
    mlp_acc[:, :main] = jnp.dot(xt, gg_ref[:, at_main], preferred_element_type=f32).astype(bf16)
    mlp_acc[:, main : 2 * main] = jnp.dot(
        xt, gu_ref[:, at_main], preferred_element_type=f32
    ).astype(bf16)
    mixed = gg_ref[:, at_tile].astype(f32) + pltpu.roll(gu_ref[:, at_tile].astype(f32), 64, 1)
    mlp_acc[:, 2 * main :] = jnp.dot(
        xt, mixed.astype(bf16), preferred_element_type=f32
    ).astype(bf16)
    gy = jnp.concatenate([gy_a[:, :D], gy_b[:, :D]], 0)
    down_acc[...] = jnp.dot(midt_ref[...], gy, preferred_element_type=f32)

    mlp_rows = mlp_acc.shape[0] // chips
    columns = mlp_acc.shape[1] // 128
    half = chips // 2
    copies = []
    for slot in sorted(range(chips), key=lambda s: abs(s - half) if s else chips):
        owner = meta_ref[12 + slot]
        block = mlp_acc[pl.ds(pl.multiple_of(owner * mlp_rows, 16), mlp_rows), :]
        for j in range(columns):
            for i in range(mlp_rows // 16):
                blocks[slot, j * 16 : (j + 1) * 16, i * 128 : (i + 1) * 128] = block[
                    i * 16 : (i + 1) * 16, j * 128 : (j + 1) * 128
                ]
        first = pl.multiple_of(core * 64 + owner * down_rows, 8)
        blocks[slot, columns * 16 :, :] = down_acc[pl.ds(first, down_rows), :].astype(bf16)
        copy = pltpu.make_async_copy(blocks.at[slot], out_refs[slot], sems.at[slot])
        copy.start()
        copies.append(copy)
    for copy in copies:
        copy.wait()


def mlp_gradients(meta, xt, early, midt, gg, gu, after, chips, down_rows, main):
    tokens = gg.shape[0]
    columns = (2 * main + 128) // 128
    rows = columns * 16 + down_rows
    args = [meta, xt, *early, midt, gg, gu]
    anywhere = pl.BlockSpec(memory_space=pl.ANY)

    def kernel(*refs):
        mlp_grad_kernel(chips, down_rows, main, *refs[: len(args)], *refs[len(args) + 1 :])

    return pl.pallas_call(
        kernel,
        out_shape=[jax.ShapeDtypeStruct((rows, D), bf16)] * chips,
        in_specs=[pl.BlockSpec(memory_space=pltpu.SMEM)]
        + [pl.BlockSpec(memory_space=pltpu.VMEM)] * (len(args) - 1)
        + [anywhere],
        out_specs=[anywhere] * chips,
        scratch_shapes=[
            pltpu.VMEM((D, columns * 128), bf16),
            pltpu.VMEM((midt.shape[0], D), f32),
            pltpu.VMEM((chips, rows, D), bf16),
            pltpu.SemaphoreType.DMA((chips,)),
        ],
        compiler_params=pltpu.CompilerParams(vmem_limit_bytes=VMEM_BYTES),
        cost_estimate=pl.CostEstimate(
            flops=6 * tokens * midt.shape[0] * D, bytes_accessed=4 * chips * rows * D,
            transcendentals=0,
        ),
    )(*args, after)


def small_grad_kernel(
    chips, q_rows, rows, cols, meta_ref, norm_a, norm_b, near_a, near_b, *refs
):
    out_refs, acc, turned_ref = refs[:-2], refs[-2], refs[-1]
    first = pl.multiple_of((2 * meta_ref[0] + meta_ref[1]) * q_rows, 16)
    grads, queries, attended = [], [], []
    for near_ref in (near_a, near_b):
        for b in range(2):
            for i, found in enumerate((grads, queries, attended)):
                found.append(near_ref[(3 * b + i) * rows : (3 * b + i + 1) * rows, :])
    turned_ref[...] = jnp.concatenate([norm_a[:, D:], norm_b[:, D:]], 0).T
    acc[:, :WIDTH_Q] = jnp.dot(
        turned_ref[pl.ds(first, q_rows), :],
        jnp.concatenate(queries, 0),
        preferred_element_type=f32,
    ).astype(bf16)
    acc[:, WIDTH_Q:cols] = jnp.zeros((q_rows, cols - WIDTH_Q), bf16)
    turned_ref[...] = jnp.concatenate(attended, 0).T
    acc[:, cols:] = jnp.dot(
        turned_ref[pl.ds(first, q_rows), :], jnp.concatenate(grads, 0), preferred_element_type=f32
    ).astype(bf16)
    width = acc.shape[1] // chips
    for out_ref, slot in zip(out_refs, range(chips)):
        owner = meta_ref[12 + slot]
        block = acc[:, pl.ds(pl.multiple_of(owner * width, 128), width)]
        tall = jnp.concatenate([block[:, i * 128 : (i + 1) * 128] for i in range(width // 128)], 0)
        piece = out_ref.shape[0]
        for i in range(D // 128):
            out_ref[:, i * 128 : (i + 1) * 128] = tall[i * piece : (i + 1) * piece]


def place_all(meta, slots, pairs, old, sizes, rest=None):
    main, ff_loc, q_rows, cols, down_rows, chips = sizes
    mlp_rows = D // chips
    columns = (2 * main + 128) // 128
    tiles = main // 128
    lanes_out = D // 128
    top = columns * 16
    blocks = [x for pair in pairs for x in pair]
    count = len(blocks)
    piece = blocks[0].shape[0] - top - down_rows
    parts = (cols + D) // chips // 128
    keep = [] if old is None else list(old)
    last = [] if rest is None else list(rest)
    known = WIDTH_Q // 128

    def kernel(meta_ref, *refs):
        ins = refs[:count]
        outs_at = count + len(last) + len(keep)
        gate_out, up_out, down_out, joint_out, proj_out, token_ref = refs[outs_at : outs_at + 6]
        gate_buf, up_buf, down_buf, small_buf, rest_buf, sems, small_sems, rest_sem = refs[
            outs_at + 6 :
        ]
        core_zero = meta_ref[1] == 0
        copies = []

        def send(src, dst, sem):
            copy = pltpu.make_async_copy(src, dst, sem)
            copy.start()
            copies.append(copy)

        def column(ref, j):
            found = [
                ref[j * 16 : (j + 1) * 16, i * 128 : (i + 1) * 128] for i in range(mlp_rows // 16)
            ]
            return jnp.concatenate(found, 0).astype(f32)

        for k, slot in enumerate(slots):
            for j in range(columns):
                got = column(ins[2 * k], j)
                other = column(ins[2 * k + 1], j)
                zero = jnp.where(core_zero, got, other)
                one = jnp.where(core_zero, other, got)
                if j < 2 * tiles:
                    buf = gate_buf if j < tiles else up_buf
                    at = (j % tiles) * 128
                    buf[k, :, at : at + 128] = zero
                    buf[k, :, at + main + 128 : at + main + 256] = one
                else:
                    left = lanes(zero.shape) < 64
                    gate_buf[k, :, main : main + 128] = jnp.where(left, zero, one)
                    up_buf[k, :, main : main + 128] = pltpu.roll(jnp.where(left, one, zero), 64, 1)
            owner = meta_ref[12 + slot]
            here = pl.ds(pl.multiple_of(owner * mlp_rows, 8), mlp_rows)
            send(gate_buf.at[k], gate_out.at[here, :], sems.at[4 * k])
            send(up_buf.at[k], up_out.at[here, :], sems.at[4 * k + 1])
            for side in range(2):
                b = 2 * k + side
                core = meta_ref[1] if side == 0 else 1 - meta_ref[1]
                down_buf[b] = ins[b][top + piece :, :].astype(f32)
                here = pl.ds(pl.multiple_of((core * chips + owner) * down_rows, 8), down_rows)
                send(down_buf.at[b], down_out.at[here, :], sems.at[4 * k + 2 + side])
                tall = jnp.concatenate(
                    [ins[b][top : top + piece, i * 128 : (i + 1) * 128] for i in range(lanes_out)], 0
                ).astype(f32)
                rows = pl.ds(pl.multiple_of(core * q_rows, 8), q_rows)
                for i in range(parts):
                    small_buf[b, i] = tall[i * q_rows : (i + 1) * q_rows]
                    block = owner * parts + i

                    @pl.when(block < known)
                    def joint(b=b, i=i, rows=rows, block=block):
                        at = pl.ds(pl.multiple_of(block * 128, 128), 128)
                        pltpu.make_async_copy(
                            small_buf.at[b, i], joint_out.at[rows, at], small_sems.at[b, i]
                        ).start()

                    @pl.when(block >= cols // 128)
                    def proj(b=b, i=i, rows=rows, block=block):
                        at = pl.ds(pl.multiple_of((block - cols // 128) * 128, 128), 128)
                        pltpu.make_async_copy(
                            small_buf.at[b, i], proj_out.at[rows, at], small_sems.at[b, i]
                        ).start()

        token_ref[...] = jnp.zeros(token_ref.shape, f32)
        if last:
            rows = last[0].shape[0]
            for core, ref in ((meta_ref[1], refs[count]), (1 - meta_ref[1], refs[count + 1])):
                rest_buf[pl.ds(pl.multiple_of(core * rows, 8), rows), :] = ref[...].astype(f32)
            send(rest_buf.at[: 2 * q_rows, :], joint_out.at[:, WIDTH_Q:cols], rest_sem)
        for copy in copies:
            copy.wait()
        for b in range(count):
            for i in range(parts):
                block = meta_ref[12 + slots[b // 2]] * parts + i

                @pl.when((block < known) | (block >= cols // 128))
                def done(b=b, i=i):
                    pltpu.make_async_copy(
                        small_buf.at[b, i],
                        proj_out.at[pl.ds(0, q_rows), pl.ds(0, 128)],
                        small_sems.at[b, i],
                    ).wait()

    anywhere = pl.BlockSpec(memory_space=pl.ANY)
    result = pl.pallas_call(
        kernel,
        out_shape=[
            jax.ShapeDtypeStruct((D, ff_loc), f32),
            jax.ShapeDtypeStruct((D, ff_loc), f32),
            jax.ShapeDtypeStruct((ff_loc, D), f32),
            jax.ShapeDtypeStruct((2 * q_rows, cols), f32),
            jax.ShapeDtypeStruct((2 * q_rows, D), f32),
            jax.ShapeDtypeStruct((8, 128), f32),
        ],
        in_specs=[pl.BlockSpec(memory_space=pltpu.SMEM)]
        + [pl.BlockSpec(memory_space=pltpu.VMEM)] * (count + len(last))
        + [anywhere] * len(keep),
        out_specs=[anywhere] * 5 + [pl.BlockSpec(memory_space=pltpu.VMEM)],
        scratch_shapes=[
            pltpu.VMEM((len(slots), mlp_rows, ff_loc), f32),
            pltpu.VMEM((len(slots), mlp_rows, ff_loc), f32),
            pltpu.VMEM((count, down_rows, D), f32),
            pltpu.VMEM((count, parts, q_rows, 128), f32),
            pltpu.VMEM((2 * q_rows + SUM_ROWS, cols - WIDTH_Q), f32),
            pltpu.SemaphoreType.DMA((4 * len(slots),)),
            pltpu.SemaphoreType.DMA((count, parts)),
            pltpu.SemaphoreType.DMA,
        ],
        input_output_aliases={1 + count + len(last) + i: i for i in range(len(keep))},
        compiler_params=pltpu.CompilerParams(vmem_limit_bytes=VMEM_BYTES),
        cost_estimate=pl.CostEstimate(
            flops=0, bytes_accessed=8 * sum(x.size for x in blocks), transcendentals=0
        ),
    )(meta, *blocks, *last, *keep)
    return list(result[:5]), result[5]


def place_blocks(blocks, spots, out_shape, old=None):
    shape = blocks[0].shape
    count = len(blocks)
    if shape[0] % 8 or shape[1] % 128:
        out = jnp.zeros(out_shape, f32) if old is None else old
        for block, (i, j) in zip(blocks, spots):
            out = lax.dynamic_update_slice(
                out, block.astype(f32), (i * shape[0], j * shape[1])
            )
        return out

    def kernel(spots_ref, *refs):
        step = pl.program_id(0)
        out_ref = refs[-1]
        for i in range(count):

            @pl.when(step == i)
            def write(i=i):
                out_ref[...] = refs[i][...].astype(f32)

    keep = [] if old is None else [old]
    return pl.pallas_call(
        kernel,
        out_shape=jax.ShapeDtypeStruct(out_shape, f32),
        grid_spec=pltpu.PrefetchScalarGridSpec(
            num_scalar_prefetch=1,
            grid=(count,),
            in_specs=[pl.BlockSpec(shape, lambda i, spots: (0, 0))] * count
            + [pl.BlockSpec(memory_space=pl.ANY)] * len(keep),
            out_specs=pl.BlockSpec(shape, lambda i, spots: (spots[i, 0], spots[i, 1])),
        ),
        input_output_aliases={} if old is None else {count + 1: 0},
        compiler_params=pltpu.CompilerParams(vmem_limit_bytes=VMEM_BYTES),
    )(jnp.stack([jnp.stack(s) for s in spots]).astype(jnp.int32), *blocks, *keep)


def local(tokens, w_qkv, b_qkv, w_out, gain_attn, gain_mlp, w_gate, w_up, w_down, cotangent):
    net = Net()
    rows = tokens.shape[1]
    half_rows = rows // 2
    ctx_count = net.ctx
    core = net.core
    chips = net.chips
    part_rows = GROUP * half_rows
    x = tokens[0]
    gain_one = gain_attn[None]
    gain_two = gain_mlp[None]

    w_qkv_full = net.full_rows(w_qkv)

    ff_loc = w_gate.shape[1]
    ff_half = ff_loc // 2
    main = (ff_half // 128) * 128
    rest = ff_half - main
    width = main + 2 * rest
    first = core * main
    tiled = net.dp == 2 and 2 * rest == 128 and width % 256 == 0 and chips == 8 and ff_half == chips * RING_ROWS
    ring = jnp.arange(chips, dtype=jnp.int32)
    owners_of = (net.pos - ring) % chips
    spots = jnp.concatenate(
        [jnp.stack([net.d, core, first, jnp.int32(ff_half)]), owners_of, owners_of]
    ).astype(jnp.int32)

    row_ids = jnp.arange(half_rows, dtype=jnp.int32)
    place = jnp.concatenate(
        [net.c * half_rows + row_ids, (2 * ctx_count - 1 - net.c) * half_rows + row_ids]
    )
    freq = ROPE_BASE ** (-((jnp.arange(128) % (HD // 2)).astype(f32) * (2.0 / HD)))
    angle = place.astype(f32)[:, None] * freq[None, :]
    cosine, sine = jnp.cos(angle), jnp.sin(angle)
    normed_one, queries, pairs = call(
        qkv_kernel,
        [
            jax.ShapeDtypeStruct((rows, D), bf16),
            jax.ShapeDtypeStruct((rows, WIDTH_Q), bf16),
            jax.ShapeDtypeStruct((rows, 2 * WIDTH_K), bf16),
        ],
        [x, gain_one, w_qkv_full, b_qkv[None], cosine, sine],
        flops=2 * rows * D * 1152,
    )

    slots = net.ring_gather(pairs)
    mine = jnp.concatenate(slots, 0)
    other = net.swap(mine)
    order = jnp.array(net.order, jnp.int32)
    chip_ids = order[(net.pos - jnp.arange(chips, dtype=jnp.int32)) % chips]
    meta = jnp.concatenate([net.c[None], 2 * chip_ids + core, 2 * chip_ids + 1 - core])
    meta = meta.astype(jnp.int32)

    late_w, late_g, late_n, unused = lax.optimization_barrier((w_out, cotangent[0], normed_one, pairs))
    w_out_full = net.full_rows(late_w)
    early = net.group_parts(jnp.concatenate([late_g, late_n], 1))

    total_keys = rows * ctx_count
    padded = (KH, 2 * part_rows, 128)
    attended_low, attended, lse, spread, keys, values, hidden, normed_two = call(
        lambda *refs: forward_kernel(ctx_count, *refs),
        [
            jax.ShapeDtypeStruct((rows, WIDTH_Q), bf16),
            jax.ShapeDtypeStruct(padded, f32),
            jax.ShapeDtypeStruct((KH, 2, 8, part_rows), f32),
            jax.ShapeDtypeStruct(padded, bf16),
            jax.ShapeDtypeStruct((total_keys, WIDTH_K), bf16),
            jax.ShapeDtypeStruct((total_keys, WIDTH_K), bf16),
            jax.ShapeDtypeStruct((rows, D), f32),
            jax.ShapeDtypeStruct((rows, D), bf16),
        ],
        [meta, queries, mine, other, x, w_out_full, gain_two],
        smem=1,
        scratch=[
            pltpu.VMEM((KH, total_keys // KEYS, part_rows, KEYS), f32),
            pltpu.VMEM((KH, part_rows, 128), f32),
            pltpu.VMEM((KH, part_rows, 128), f32),
        ],
        flops=8 * KH * part_rows * total_keys * 128,
    )

    normed_two_parts = net.group_parts(normed_two)
    chip_rows = net.dp * rows
    down_rows = ff_half // chips
    mlp_rows = D // chips
    if tiled:
        x_turned, mid_turned, gate_low, up_low, grad_mine, out_mine, sent = feed_forward(
            spots, normed_two_parts, early, w_gate, w_up, w_down, width
        )
    else:
        normed_two_group = jnp.concatenate(normed_two_parts, 0)
        grad_out_group = jnp.concatenate(early, 0)[:, :D]
        own_cols = (jnp.arange(width) + first < ff_half) == (core == 0)
        wg = lax.dynamic_slice(w_gate, (0, first), (D, width))
        wu = lax.dynamic_slice(w_up, (0, first), (D, width))
        wd = lax.dynamic_slice(w_down, (first, 0), (width, D))
        gate = jnp.dot(normed_two_group, wg, preferred_element_type=f32)
        upper = jnp.dot(normed_two_group, wu, preferred_element_type=f32)
        sigma = jax.nn.sigmoid(gate)
        activated = gate * sigma
        middle = jnp.where(own_cols, activated * upper, 0.0).astype(bf16)
        grad_middle = jnp.einsum("td,fd->tf", grad_out_group, wd, preferred_element_type=f32)
        slope = sigma * (1.0 + gate * (1.0 - sigma))
        grad_gate_low = jnp.where(own_cols, grad_middle * upper * slope, 0.0).astype(bf16)
        grad_up_low = jnp.where(own_cols, grad_middle * activated, 0.0).astype(bf16)

        grad_normed_two = jnp.einsum(
            "tf,df->td", grad_gate_low, wg, preferred_element_type=f32
        ) + jnp.einsum("tf,df->td", grad_up_low, wu, preferred_element_type=f32)
        mlp_out = jnp.dot(middle, wd, preferred_element_type=f32)
        grad_mine, out_mine = grad_normed_two[:chip_rows], mlp_out[:chip_rows]
        sent = jnp.concatenate([grad_normed_two[chip_rows:], mlp_out[chip_rows:]], 0).astype(bf16)
    swapped = net.swap(sent)
    grad_chip = grad_mine + swapped[:chip_rows].astype(f32)
    mlp_chip = out_mine + swapped[chip_rows:].astype(f32)
    grad_two = grad_chip[:rows]
    for s in range(1, net.dp):
        sent_two = grad_chip[s * rows : (s + 1) * rows].astype(bf16)
        grad_two = grad_two + net.shift(sent_two, net.dp - s).astype(f32)

    def attention_back(*after):
        grad_hidden, grad_attn_low, grad_gain_two, grad_queries, terms_mine, terms_other = call(
            lambda *refs: backward_kernel(ctx_count, *refs),
            [
                jax.ShapeDtypeStruct((rows, D), f32),
                jax.ShapeDtypeStruct((rows, D), bf16),
                jax.ShapeDtypeStruct((1, D), f32),
                jax.ShapeDtypeStruct((rows, WIDTH_Q), bf16),
                jax.ShapeDtypeStruct((chips * rows, 2 * WIDTH_K), f32),
                jax.ShapeDtypeStruct((chips * rows, 2 * WIDTH_K), bf16),
            ],
            [
                meta, grad_two, hidden, cotangent[0], gain_two, w_out_full, spread, keys, values, lse,
                attended, cosine, sine, *after,
            ],
            smem=1,
            loose=len(after),
            scratch=[
                pltpu.VMEM(padded, bf16),
                pltpu.VMEM(padded, f32),
                pltpu.VMEM((total_keys, WIDTH_K), f32),
                pltpu.VMEM((total_keys, WIDTH_K), f32),
            ],
            flops=20 * KH * part_rows * total_keys * 128,
        )
        other_terms = net.swap(terms_other)

        def row_sums(*after):
            pair_sums = call(
                pair_kernel,
                [jax.ShapeDtypeStruct((rows, 2 * WIDTH_K), f32)]
                + [jax.ShapeDtypeStruct((rows, 2 * WIDTH_K), bf16)] * (chips - 1),
                [terms_mine, other_terms, *after],
                loose=len(after),
            )
            return net.ring_parts(pair_sums)

        def finish(grad_pairs):
            return call(
                finish_kernel,
                [
                    jax.ShapeDtypeStruct((rows + 2 * SUM_ROWS, 2 * WIDTH_K), bf16),
                    jax.ShapeDtypeStruct((rows, D), f32),
                    jax.ShapeDtypeStruct((1, D), f32),
                    jax.ShapeDtypeStruct((1, w_qkv.shape[1]), f32),
                ],
                [grad_queries, x, gain_one, w_qkv_full, cosine, sine, grad_hidden, grad_gain_two]
                + grad_pairs,
            )

        return grad_attn_low, grad_gain_two, grad_queries, row_sums, finish

    if tiled:
        terms = mlp_gradients(
            spots, x_turned, early, mid_turned, gate_low, up_low, sent_two, chips, down_rows, main
        )
        grad_attn_low, grad_gain_two, grad_queries, row_sums, finish = attention_back(terms[0])
        found = []

        def between(*blocks):
            found.extend(row_sums(*blocks))
            return found[1]

        fwd, back = net.ring_sum(terms, between)
        grad_pairs, marks = found
        sum_mlp, sum_down = ring_end(fwd, back, terms[0], terms[0].shape[0] - down_rows)
    else:
        part_down = jnp.einsum(
            "tf,td->fd", middle, grad_out_group, preferred_element_type=f32
        ).astype(bf16)
        part_down = lax.dynamic_slice(part_down, (core * rest, 0), (ff_half, D))

        def down_chunk(slot):
            return lax.dynamic_slice(part_down, (net.owner(slot) * down_rows, 0), (down_rows, D))

        sum_down = net.ring_scatter([down_chunk(s) for s in range(chips)]).astype(bf16)

        def split_main(x):
            left = (x[:, :main], x[:, main:])
            right = (x[:, 2 * rest :], x[:, : 2 * rest])
            return (
                jnp.where(core == 0, left[0], right[0]),
                jnp.where(core == 0, left[1], right[1]),
            )

        gate_main, gate_tile = split_main(grad_gate_low)
        up_main, up_tile = split_main(grad_up_low)
        packed = jnp.concatenate(
            [gate_main, up_main, gate_tile + jnp.roll(up_tile, rest, 1)], 1
        )
        part_mlp = jnp.einsum(
            "td,tf->df", normed_two_group, packed, preferred_element_type=f32
        ).astype(bf16)

        def mlp_chunk(slot):
            return lax.dynamic_slice(
                part_mlp, (net.owner(slot) * mlp_rows, 0), (mlp_rows, 2 * ff_half)
            )

        sum_mlp = net.ring_scatter([mlp_chunk(s) for s in range(chips)]).astype(bf16)
        sum_mlp = lax.optimization_barrier(sum_mlp)
        grad_attn_low, grad_gain_two, grad_queries, row_sums, finish = attention_back()
        grad_pairs, marks = row_sums()
    pair_sent, grad_input, grad_gain_one, grad_bias = finish(grad_pairs)

    out_sum = mlp_chip[:rows]
    for s in range(1, net.dp):
        got = net.shift(mlp_chip[s * rows : (s + 1) * rows].astype(bf16), net.dp - s)
        out_sum = out_sum + got.astype(f32)
    output = (hidden + out_sum).astype(bf16)
    near = net.group_parts(jnp.concatenate([grad_attn_low, grad_queries, attended_low], 0))

    q_rows = w_qkv.shape[0] // 2
    qkv_cols = w_qkv.shape[1]
    if tiled:
        piece = q_rows * (qkv_cols + D) // chips // D
        terms_small = call(
            lambda *refs: small_grad_kernel(chips, q_rows, rows, qkv_cols, *refs),
            [jax.ShapeDtypeStruct((piece, D), bf16)] * chips,
            [spots, *early, *near],
            smem=1,
            scratch=[
                pltpu.VMEM((q_rows, qkv_cols + D), bf16),
                pltpu.VMEM((D, 2 * chip_rows), bf16),
            ],
            flops=4 * chip_rows * D * (qkv_cols + D),
        )
        block = call(
            block_kernel,
            [jax.ShapeDtypeStruct((sum_mlp.shape[0] + piece + down_rows, D), bf16)],
            [sum_mlp, sum_down] + net.ring_parts(terms_small)[0] + list(marks[3]),
            loose=2,
        )[0]
        part_pair = call(
            lambda *refs: pair_grad_kernel(rows, 2 * q_rows, *refs),
            [jax.ShapeDtypeStruct((2 * q_rows + SUM_ROWS, 2 * WIDTH_K), bf16)],
            [spots, early[0], pair_sent, net.shift(pair_sent, 1)],
            smem=1,
            scratch=[pltpu.VMEM((D, chip_rows), bf16)],
        )[0]
        grad_pair, steps = net.exchange_sum(part_pair)
        pair_halves = (grad_pair, net.swap(grad_pair))
        sums = jnp.where(core == 1, *pair_halves)[-SUM_ROWS:]
        small = sums.reshape(-1)[: 2 * D + qkv_cols].astype(f32)
        sizes = (main, ff_loc, q_rows, qkv_cols, down_rows, chips)
        grad_gate, grad_up, grad_down, grad_joint, grad_out_proj = net.gather_placed(
            block,
            lambda slots, pairs, old, rest=None: place_all(spots, slots, pairs, old, sizes, rest),
            pair_halves,
            [[part_pair], [steps[1]], [steps[2]]],
        )
    else:
        gathered = jnp.concatenate(near, 0).reshape(2 * net.dp, 3, rows, D)
        grad_attn_group = gathered[:, 0].reshape(2 * net.dp * rows, D)
        attended_group = gathered[:, 2].reshape(2 * net.dp * rows, D)
        normed_one_group = jnp.concatenate(early, 0)[:, D:]
        joint_group = net.group_gather(jnp.concatenate([grad_queries, pair_sent[:rows]], 1))
        q_first = net.d * (2 * q_rows) + core * q_rows
        group_rows = 2 * net.dp * rows
        part_out = jnp.einsum(
            "tc,td->cd",
            lax.dynamic_slice(attended_group, (0, q_first), (group_rows, q_rows)),
            grad_attn_group,
            preferred_element_type=f32,
        )
        part_joint = jnp.einsum(
            "td,tc->dc",
            lax.dynamic_slice(normed_one_group, (0, q_first), (group_rows, q_rows)),
            joint_group,
            preferred_element_type=f32,
        )
        part_small = jnp.concatenate([part_joint, part_out], 1).astype(bf16)
        small_cols = part_small.shape[1] // chips

        def small_chunk(slot):
            return lax.dynamic_slice(part_small, (0, net.owner(slot) * small_cols), (q_rows, small_cols))

        sum_small = net.ring_scatter([small_chunk(s) for s in range(chips)]).astype(bf16)

        tall = jnp.concatenate(
            [sum_small[:, i * 128 : (i + 1) * 128] for i in range(small_cols // 128)], 0
        )
        piece = tall.shape[0] // (D // 128)
        wide = jnp.concatenate([tall[i * piece : (i + 1) * piece] for i in range(D // 128)], 1)
        both = lax.optimization_barrier(jnp.concatenate([sum_down, wide], 0))

        owners = [net.owner(s) for s in range(chips)]
        got_mlp = net.ring_gather(sum_mlp)
        got_both = net.ring_gather(both)
        pairs_mlp = [(got, net.swap(got)) for got in got_mlp]
        pairs_both = [(got, net.swap(got)) for got in got_both]

        down_blocks, down_spots, small_blocks, small_spots = [], [], [], []
        for owner, pair in zip(owners, pairs_both):
            for which, got in zip((core, 1 - core), pair):
                down_blocks.append(got[:down_rows])
                down_spots.append((which * chips + owner, jnp.int32(0)))
                wide = got[down_rows:]
                tall = jnp.concatenate([wide[:, i * 128 : (i + 1) * 128] for i in range(D // 128)], 0)
                small_blocks.append(
                    jnp.concatenate(
                        [tall[i * q_rows : (i + 1) * q_rows] for i in range(small_cols // 128)], 1
                    )
                )
                small_spots.append((which, owner))
        grad_down = place_blocks(down_blocks, down_spots, (ff_loc, D))
        grad_small = place_blocks(small_blocks, small_spots, (2 * q_rows, part_small.shape[1]))
        grad_gate = jnp.zeros((D, ff_loc), f32)
        grad_up = jnp.zeros((D, ff_loc), f32)
        left_lane = jnp.arange(2 * rest) < rest
        for owner, (got, swapped) in zip(owners, pairs_mlp):
            zero = jnp.where(core == 0, got, swapped).astype(f32)
            one = jnp.where(core == 0, swapped, got).astype(f32)
            tile_zero, tile_one = zero[:, 2 * main :], one[:, 2 * main :]
            mid_gate = jnp.where(left_lane, tile_zero, tile_one)
            mid_up = jnp.roll(jnp.where(left_lane, tile_one, tile_zero), rest, 1)
            base = owner * mlp_rows
            grad_gate = lax.dynamic_update_slice(
                grad_gate, jnp.concatenate([zero[:, :main], mid_gate, one[:, :main]], 1), (base, 0)
            )
            grad_up = lax.dynamic_update_slice(
                grad_up,
                jnp.concatenate([zero[:, main : 2 * main], mid_up, one[:, main : 2 * main]], 1),
                (base, 0),
            )

        grad_joint, grad_out_proj = grad_small[:, :qkv_cols], grad_small[:, qkv_cols:]
        small = net.total(jnp.concatenate([grad_gain_one, grad_gain_two, grad_bias], 1))[0]
    return (
        output[None],
        grad_input[None],
        grad_joint,
        small[2 * D :],
        grad_out_proj,
        small[:D],
        small[D : 2 * D],
        grad_gate,
        grad_up,
        grad_down,
    )


def solution(mesh):
    placed = (
        P("dp", "ctx", None),
        P("dp", None),
        P(),
        P("dp", None),
        P(),
        P(),
        P(None, "dp"),
        P(None, "dp"),
        P("dp", None),
        P("dp", "ctx", None),
    )
    return jax.shard_map(
        local,
        mesh=mesh,
        in_specs=placed,
        out_specs=(
            P("dp", "ctx", None),
            P("dp", "ctx", None),
            P("dp", None),
            P(),
            P("dp", None),
            P(),
            P(),
            P(None, "dp"),
            P(None, "dp"),
            P("dp", None),
        ),
        check_vma=False,
    )
```

```python
import jax
import jax.numpy as jnp
from jax import lax
from jax.experimental import pallas as pl
from jax.experimental.pallas import tpu as pltpu
from jax.sharding import PartitionSpec as P

D = 896
QH = 14
KH = 2
HD = 64
GROUP = QH // KH
WIDTH_Q = QH * HD
WIDTH_K = KH * HD

EPS = 1e-06
ROPE_BASE = 1000000.0

f32 = jnp.float32
bf16 = jnp.bfloat16


def ring_order(chips):
    if chips % 2:
        return list(range(chips))
    rows = chips // 2
    return [2 * i for i in range(rows)] + [2 * i + 1 for i in reversed(range(rows))]


def half_cut(rows):
    cut = (rows // 2 + 7) // 8 * 8
    return cut if cut < rows else rows // 2


class Net:
    def __init__(self):
        self.dp = lax.axis_size("dp")
        self.ctx = lax.axis_size("ctx")
        self.chips = self.ctx // 2
        self.order = ring_order(self.chips)
        self.d = lax.axis_index("dp")
        self.c = lax.axis_index("ctx")
        self.core = self.c % 2
        place = [0] * self.chips
        for spot, chip in enumerate(self.order):
            place[chip] = spot
        self.pos = jnp.array(place, jnp.int32)[self.c // 2]

    def swap(self, x):
        return lax.ppermute(x, "ctx", [(i, i ^ 1) for i in range(self.ctx)])

    def shift(self, x, step):
        n = self.dp
        return lax.ppermute(x, "dp", [(i, (i + step) % n) for i in range(n)])

    def hop(self, x, step):
        n = self.chips
        perm = []
        for spot in range(n):
            for core in range(2):
                perm.append((2 * self.order[spot] + core, 2 * self.order[(spot + step) % n] + core))
        return lax.ppermute(x, "ctx", perm)

    def owner(self, slot):
        return (self.pos - slot) % self.chips

    def group_parts(self, x):
        chip = jnp.concatenate([x] + [self.shift(x, s) for s in range(1, self.dp)], 0)
        return chip, self.swap(chip)

    def group_gather(self, x):
        return jnp.concatenate(self.group_parts(x), 0)

    def ring_gather(self, x):
        n = self.chips
        half = n // 2
        cut = half_cut(x.shape[0])
        found = [x] + [None] * (n - 1)
        fwd, back = x, x
        for s in range(1, half):
            fwd = self.hop(fwd, 1)
            back = self.hop(back, -1)
            found[s] = fwd
            found[n - s] = back
        found[half] = jnp.concatenate([self.hop(fwd[:cut], 1), self.hop(back[cut:], -1)], 0)
        return found

    def ring_scatter(self, local):
        n = self.chips
        half = n // 2
        cut = half_cut(local[half].shape[0])

        def add(got, mine):
            return (got.astype(f32) + mine.astype(f32)).astype(bf16)

        fwd = self.hop(local[half][:cut], 1)
        back = self.hop(local[half][cut:], -1)
        for s in range(1, half):
            mine_f = local[half + s]
            mine_b = local[half - s]
            if s == 1:
                mine_f = jnp.concatenate([add(fwd, mine_f[:cut]), mine_f[cut:]], 0)
                mine_b = jnp.concatenate([mine_b[:cut], add(back, mine_b[cut:])], 0)
            else:
                mine_f = add(fwd, mine_f)
                mine_b = add(back, mine_b)
            fwd = self.hop(mine_f, 1)
            back = self.hop(mine_b, -1)
        return fwd.astype(f32) + back.astype(f32) + local[0].astype(f32)

    def full_rows(self, shard):
        rows = shard.shape[0]
        half = rows // 2
        piece = lax.dynamic_slice(shard, (self.core * half, 0), (half, shard.shape[1]))
        blocks = [shard]
        for s in range(1, self.dp):
            got = self.shift(piece, s)
            other = self.swap(got)
            low = jnp.where(self.core == 0, got, other)
            high = jnp.where(self.core == 0, other, got)
            blocks.append(jnp.concatenate([low, high], 0))
        if self.dp == 2:
            first = jnp.where(self.d == 0, blocks[0], blocks[1])
            second = jnp.where(self.d == 0, blocks[1], blocks[0])
            return jnp.concatenate([first, second], 0)
        ranked = jnp.stack(blocks)[(self.d - jnp.arange(self.dp)) % self.dp]
        return ranked.reshape(self.dp * rows, shard.shape[1])

    def total(self, x):
        x = x + self.swap(x)
        bit = 1
        while bit < self.chips:
            x = x + lax.ppermute(x, "ctx", [(i, i ^ (2 * bit)) for i in range(self.ctx)])
            bit *= 2
        bit = 1
        while bit < self.dp:
            x = x + lax.ppermute(x, "dp", [(i, i ^ bit) for i in range(self.dp)])
            bit *= 2
        return x

    def ring_parts(self, local):
        n = self.chips
        half = n // 2
        cut = half_cut(local[half].shape[0])

        def add(got, mine):
            return (got.astype(f32) + mine.astype(f32)).astype(bf16)

        fwd, back = self.hop(local[half][:cut], 1), self.hop(local[half][cut:], -1)
        marks = [(fwd, back)]
        for s in range(1, half):
            mine_f, mine_b = local[half + s], local[half - s]
            if s == 1:
                mine_f = jnp.concatenate([add(fwd, mine_f[:cut]), mine_f[cut:]], 0)
                mine_b = jnp.concatenate([mine_b[:cut], add(back, mine_b[cut:])], 0)
            else:
                mine_f, mine_b = add(fwd, mine_f), add(back, mine_b)
            fwd, back = self.hop(mine_f, 1), self.hop(mine_b, -1)
            marks.append((fwd, back))
        return [local[0], fwd, back], marks

    def exchange_sum(self, x):
        half = x.shape[0] // 2

        def add(a, b):
            return (a.astype(f32) + b.astype(f32)).astype(bf16)

        x = add(x, self.swap(x))
        x = lax.dynamic_slice(x, (self.core * half, 0), (half, x.shape[1]))
        bit = 1
        while bit < self.chips:
            x = add(x, lax.ppermute(x, "ctx", [(i, i ^ (2 * bit)) for i in range(self.ctx)]))
            bit *= 2
        return x

    def ring_sum(self, terms, between):
        half = self.chips // 2
        fwd, back = self.hop(terms[half], 1), self.hop(terms[half - 1], -1)

        def add(got, slot):
            return (got.astype(f32) + terms[slot].astype(f32)).astype(bf16)

        for s in range(1, half):
            blocks = [add(fwd, half + s)]
            if s < half - 1:
                blocks.append(add(back, half - 1 - s))
            if s == 1:
                marks = between(*blocks)
            else:
                blocks = gate(marks[s - 2], blocks)
            fwd = self.hop(blocks[0], 1)
            if s < half - 1:
                back = self.hop(blocks[1], -1)
        return fwd, back

    def gather_placed(self, x, place, rest, marks):
        n = self.chips
        half = n // 2
        fwd = back = x
        placed = None
        waiting = ([0], [(x, self.swap(x))])
        for s in range(1, half + 1):
            if s > 1:
                placed, token = place(*waiting, placed)
                fwd, back = gate([token] + marks[s - 2], [fwd, back])
                waiting = ([s - 1, n - s + 1], [(fwd, self.swap(fwd)), (back, self.swap(back))])
            if s < half:
                fwd, back = self.hop(fwd, 1), self.hop(back, -1)
            else:
                cut = half_cut(fwd.shape[0])
                fwd, back = self.hop(fwd[:cut], 1), self.hop(back[cut:], -1)
        placed, token = place(*waiting, placed)
        far = join(fwd, back, token)
        return place([half], [(far, self.swap(far))], placed, rest)[0]


VMEM_BYTES = 56 * 1024 * 1024
KEYS = 256
RING_ROWS = 152


def full_spec(shape):
    return pl.BlockSpec(shape, lambda: (0,) * len(shape))


def call(kernel, outs, args, smem=0, scratch=(), flops=0, loose=0):
    tight = len(args) - loose
    specs = [pl.BlockSpec(memory_space=pltpu.SMEM)] * smem
    specs += [pl.BlockSpec(memory_space=pltpu.VMEM)] * (tight - smem)
    specs += [pl.BlockSpec(memory_space=pl.ANY)] * loose

    def body(*refs):
        kernel(*refs[:tight], *refs[tight + loose :])

    moved = sum(x.size * x.dtype.itemsize for x in list(args) + list(outs))
    return pl.pallas_call(
        body,
        out_shape=list(outs),
        in_specs=specs,
        out_specs=[pl.BlockSpec(memory_space=pltpu.VMEM)] * len(outs),
        scratch_shapes=list(scratch),
        compiler_params=pltpu.CompilerParams(vmem_limit_bytes=VMEM_BYTES),
        cost_estimate=pl.CostEstimate(flops=flops, bytes_accessed=moved, transcendentals=0),
    )(*args)


def lanes(shape):
    return lax.broadcasted_iota(jnp.int32, shape, len(shape) - 1)


def dot_nt(a, b, precision=None):
    return lax.dot_general(
        a, b, (((1,), (1,)), ((), ())), preferred_element_type=f32, precision=precision
    )


def dot_tn(a, b):
    return lax.dot_general(a, b, (((0,), (0,)), ((), ())), preferred_element_type=f32)


def gate(tokens, blocks):
    count, before = len(blocks), len(tokens)
    anywhere = pl.BlockSpec(memory_space=pl.ANY)

    def kernel(*refs):
        return None

    return pl.pallas_call(
        kernel,
        out_shape=[jax.ShapeDtypeStruct(x.shape, x.dtype) for x in blocks],
        in_specs=[anywhere] * (before + count),
        out_specs=[anywhere] * count,
        input_output_aliases={before + i: i for i in range(count)},
        cost_estimate=pl.CostEstimate(flops=0, bytes_accessed=1024, transcendentals=0),
    )(*tokens, *blocks)


def join(first, second, token):
    cut = first.shape[0]

    def kernel(first_ref, second_ref, out_ref):
        out_ref[:cut, :] = first_ref[...]
        out_ref[cut:, :] = second_ref[...]

    shape = (cut + second.shape[0], first.shape[1])
    return call(
        kernel, [jax.ShapeDtypeStruct(shape, first.dtype)], [first, second, token], loose=1
    )[0]


def ring_end(fwd, back, term, split):
    rows, columns = term.shape

    def kernel(fwd_ref, back_ref, term_ref, first_ref, rest_ref):
        for ref, here in ((first_ref, slice(0, split)), (rest_ref, slice(split, rows))):
            total = fwd_ref[here, :].astype(f32) + back_ref[here, :].astype(f32)
            ref[...] = (total + term_ref[here, :].astype(f32)).astype(bf16)

    outs = [
        jax.ShapeDtypeStruct((split, columns), bf16),
        jax.ShapeDtypeStruct((rows - split, columns), bf16),
    ]
    return call(kernel, outs, [fwd, back, term])


def pair_kernel(mine_ref, got_ref, *out_refs):
    rows = out_refs[0].shape[0]
    for s, out_ref in enumerate(out_refs):
        here = slice(s * rows, (s + 1) * rows)
        out_ref[...] = (mine_ref[here, :] + got_ref[here, :].astype(f32)).astype(out_ref.dtype)


def block_kernel(mlp_ref, down_ref, *refs):
    small = refs[0][...].astype(f32)
    for ref in refs[1:-1]:
        small = small + ref[...].astype(f32)
    out_ref = refs[-1]
    top = mlp_ref.shape[0]
    piece = small.shape[0]
    out_ref[:top, :] = mlp_ref[...]
    out_ref[top : top + piece, :] = small.astype(bf16)
    out_ref[top + piece :, :] = down_ref[...]


def qkv_kernel(x_ref, gain_ref, w_ref, b_ref, cos_ref, sin_ref, norm_ref, q_ref, pair_ref):
    x = x_ref[...].astype(f32)
    inverse = lax.rsqrt(jnp.mean(x * x, -1, keepdims=True) + EPS)
    normed = (x * inverse * gain_ref[...]).astype(bf16)
    norm_ref[...] = normed
    joint = jnp.dot(normed, w_ref[...], preferred_element_type=f32) + b_ref[...]
    cosine = cos_ref[...]
    sine = sin_ref[...]
    early = lanes(cosine.shape) % HD < HD // 2
    for i in range((WIDTH_Q + WIDTH_K) // 128):
        tile = joint[:, i * 128 : (i + 1) * 128]
        turned = jnp.where(early, -pltpu.roll(tile, 96, 1), pltpu.roll(tile, 32, 1))
        turned = tile * cosine + turned * sine
        if i * 128 < WIDTH_Q:
            q_ref[:, i * 128 : (i + 1) * 128] = turned.astype(bf16)
        else:
            pair_ref[:, :WIDTH_K] = turned.astype(bf16)
    pair_ref[:, WIDTH_K:] = joint[:, WIDTH_Q + WIDTH_K :].astype(bf16)


def spread_heads(x, out_ref, factor):
    rows = x.shape[0]
    half = rows // 2
    for head in range(QH):
        kh, g = divmod(head, GROUP)
        tile = x[:, (head // 2) * 128 : (head // 2 + 1) * 128].astype(f32)
        if head % 2 != kh:
            tile = pltpu.roll(tile, HD, 1)
        tile = jnp.where(lanes(tile.shape) // HD == kh, tile * factor, 0.0).astype(out_ref.dtype)
        for part in range(2):
            start = (part * GROUP + g) * half
            out_ref[kh, start : start + half, :] = tile[part * half : (part + 1) * half]


def join_heads(src_ref, half, tile):
    sides = []
    for side in range(2):
        kh, g = divmod(2 * tile + side, GROUP)
        parts = [
            src_ref[kh, (part * GROUP + g) * half : (part * GROUP + g + 1) * half, :]
            for part in range(2)
        ]
        both = jnp.concatenate(parts, 0)
        sides.append(both if side == kh else pltpu.roll(both, HD, 1))
    return jnp.where(lanes(sides[0].shape) < HD, sides[0], sides[1])


def forward_kernel(
    ctx, meta_ref, q_ref, mine_ref, other_ref, x_ref, w_ref, gain_ref,
    low_ref, o_ref, lse_ref, spread_ref, k_ref, v_ref, hidden_ref, normed_ref,
    s_ref, max_ref, sum_ref,
):
    rows = q_ref.shape[0]
    half = rows // 2
    part_rows = GROUP * half
    me = meta_ref[0]
    chips = ctx // 2
    for j in range(ctx):
        src = mine_ref if j < chips else other_ref
        at = (j % chips) * rows
        owner = meta_ref[1 + j]
        for part in range(2):
            place = owner if part == 0 else 2 * ctx - 1 - owner
            to = pl.ds(pl.multiple_of(place * half, half), half)
            block = src[at + part * half : at + (part + 1) * half, :]
            k_ref[to, :] = block[:, :WIDTH_K]
            v_ref[to, :] = block[:, WIDTH_K:]
    spread_heads(q_ref[...], spread_ref, HD ** (-0.5))
    for part in range(2):
        span = slice(part * part_rows, (part + 1) * part_rows)
        start = (me if part == 0 else 2 * ctx - 1 - me) * half
        last = start // KEYS

        def keys_of(ref, i):
            return ref[pl.ds(pl.multiple_of(i * KEYS, KEYS), KEYS), :]

        for kh in range(KH):
            scores = dot_nt(spread_ref[kh, span, :], keys_of(k_ref, last))
            row = lax.broadcasted_iota(jnp.int32, scores.shape, 0) % half + start
            scores = jnp.where(lanes(scores.shape) + last * KEYS <= row, scores, -1e30)
            s_ref[kh, last] = scores
            max_ref[kh] = jnp.maximum(scores[:, :128], scores[:, 128:])

        def score(i, carry):
            for kh in range(KH):
                s = dot_nt(spread_ref[kh, span, :], keys_of(k_ref, i))
                s_ref[kh, i] = s
                max_ref[kh] = jnp.maximum(max_ref[kh], jnp.maximum(s[:, :128], s[:, 128:]))
            return carry

        lax.fori_loop(0, last, score, 0)
        for kh in range(KH):
            top = jnp.max(max_ref[kh], -1, keepdims=True)
            max_ref[kh] = jnp.broadcast_to(top, (part_rows, 128))
            sum_ref[kh] = jnp.zeros((part_rows, 128), f32)
            o_ref[kh, span, :] = jnp.zeros((part_rows, 128), f32)

        def weigh(i, carry):
            for kh in range(KH):
                s = s_ref[kh, i]
                top = max_ref[kh]
                left = jnp.exp(s[:, :128] - top)
                right = jnp.exp(s[:, 128:] - top)
                sum_ref[kh] += left + right
                o_ref[kh, span, :] += jnp.dot(
                    jnp.concatenate([left, right], 1).astype(bf16),
                    keys_of(v_ref, i),
                    preferred_element_type=f32,
                )
            return carry

        lax.fori_loop(0, last + 1, weigh, 0)
        for kh in range(KH):
            total = jnp.sum(sum_ref[kh], -1, keepdims=True)
            o_ref[kh, span, :] = o_ref[kh, span, :] / total
            lse_ref[kh, part] = dot_nt(
                jnp.full((8, 128), 1.0 / 128, f32),
                max_ref[kh] + jnp.log(total),
                lax.Precision.HIGHEST,
            )
    for tile in range(WIDTH_Q // 128):
        low_ref[:, tile * 128 : (tile + 1) * 128] = join_heads(o_ref, half, tile).astype(bf16)
    hidden = x_ref[...].astype(f32) + jnp.dot(low_ref[...], w_ref[...], preferred_element_type=f32)
    hidden_ref[...] = hidden
    inverse = lax.rsqrt(jnp.mean(hidden * hidden, -1, keepdims=True) + EPS)
    normed_ref[...] = (hidden * inverse * gain_ref[...]).astype(bf16)


def turn_back(grad, cos_ref, sin_ref):
    scaled = grad * sin_ref[...]
    early = lanes(grad.shape) % HD < HD // 2
    turned = jnp.where(early, pltpu.roll(scaled, 96, 1), -pltpu.roll(scaled, 32, 1))
    return grad * cos_ref[...] + turned


def backward_kernel(
    ctx, meta_ref, gn_ref, hidden_ref, gout_ref, gain_ref, w_ref, spread_ref, k_ref, v_ref, lse_ref,
    o_ref, cos_ref, sin_ref,
    gh_ref, ga_ref, gain_grad_ref, gq_ref, mine_ref, other_ref,
    go_ref, gqs_ref, gk_ref, gv_ref,
):
    rows = gn_ref.shape[0]
    half = rows // 2
    part_rows = GROUP * half
    me = meta_ref[0]
    chips = ctx // 2
    hidden = hidden_ref[...]
    inverse = lax.rsqrt(jnp.mean(hidden * hidden, -1, keepdims=True) + EPS)
    unit = hidden * inverse
    grad = gn_ref[...]
    gain_grad_ref[...] = jnp.sum(grad * unit, 0, keepdims=True)
    scaled = grad * gain_ref[...]
    gh = gout_ref[...].astype(f32) + inverse * (
        scaled - unit * jnp.mean(scaled * unit, -1, keepdims=True)
    )
    gh_ref[...] = gh
    ga = gh.astype(bf16)
    ga_ref[...] = ga
    spread_heads(dot_nt(ga, w_ref[...]).astype(bf16), go_ref, 1.0)
    gqs_ref[...] = jnp.zeros_like(gqs_ref)
    gk_ref[...] = jnp.zeros_like(gk_ref)
    gv_ref[...] = jnp.zeros_like(gv_ref)
    for part in range(2):
        span = slice(part * part_rows, (part + 1) * part_rows)
        start = (me if part == 0 else 2 * ctx - 1 - me) * half
        last = start // KEYS
        deltas = [
            dot_nt(
                jnp.ones((8, 128), f32),
                go_ref[kh, span, :].astype(f32) * o_ref[kh, span, :],
                lax.Precision.HIGHEST,
            )[:1]
            for kh in range(KH)
        ]

        def step(i, masked):
            at = pl.ds(pl.multiple_of(i * KEYS, KEYS), KEYS)
            keys = k_ref[at, :]
            grad_k = gk_ref[at, :]
            grad_v = gv_ref[at, :]
            for kh in range(KH):
                queries = spread_ref[kh, span, :]
                heads = go_ref[kh, span, :]
                p = jnp.exp(dot_nt(keys, queries) - lse_ref[kh, part][:1])
                if masked:
                    row = lanes(p.shape) % half + start
                    key = lax.broadcasted_iota(jnp.int32, p.shape, 0) + i * KEYS
                    p = jnp.where(key <= row, p, 0.0)
                gs = (p * (dot_nt(v_ref[at, :], heads) - deltas[kh])).astype(bf16)
                grad_v += jnp.dot(p.astype(bf16), heads, preferred_element_type=f32)
                grad_k += jnp.dot(gs, queries, preferred_element_type=f32)
                gqs_ref[kh, span, :] += dot_tn(gs, keys)
            gk_ref[at, :] = grad_k
            gv_ref[at, :] = grad_v

        def body(i, carry):
            step(i, False)
            return carry

        lax.fori_loop(0, last, body, 0)
        step(last, True)
    for tile in range(WIDTH_Q // 128):
        grad = join_heads(gqs_ref, half, tile) * HD ** (-0.5)
        gq_ref[:, tile * 128 : (tile + 1) * 128] = turn_back(grad, cos_ref, sin_ref).astype(bf16)
    for j in range(ctx):
        dst = mine_ref if j < chips else other_ref
        at = (j % chips) * rows
        owner = meta_ref[1 + j]
        for part in range(2):
            place = owner if part == 0 else 2 * ctx - 1 - owner
            frm = pl.ds(pl.multiple_of(place * half, half), half)
            to = slice(at + part * half, at + (part + 1) * half)
            dst[to, :WIDTH_K] = gk_ref[frm, :].astype(dst.dtype)
            dst[to, WIDTH_K:] = gv_ref[frm, :].astype(dst.dtype)


SUM_ROWS = 16


def finish_kernel(
    gq_ref, x_ref, gain_ref, w_ref, cos_ref, sin_ref, gh_ref, gain_two_ref, *refs
):
    sent_ref, gx_ref, gain_grad_ref, bias_ref = refs[-4:]
    pair = refs[0][...]
    for ref in refs[1:-4]:
        pair = pair + ref[...].astype(f32)
    rows = pair.shape[0]
    keys = turn_back(pair[:, :WIDTH_K], cos_ref, sin_ref)
    pair = jnp.concatenate([keys, pair[:, WIDTH_K:]], 1).astype(bf16)
    sent_ref[:rows, :] = pair
    joint = jnp.concatenate([gq_ref[...], pair], 1)
    bias = jnp.sum(joint.astype(f32), 0, keepdims=True)
    bias_ref[...] = bias
    grad = dot_nt(joint, w_ref[...])
    x = x_ref[...].astype(f32)
    inverse = lax.rsqrt(jnp.mean(x * x, -1, keepdims=True) + EPS)
    unit = x * inverse
    gain = jnp.sum(grad * unit, 0, keepdims=True)
    gain_grad_ref[...] = gain
    scaled = grad * gain_ref[...]
    gx_ref[...] = gh_ref[...] + inverse * (
        scaled - unit * jnp.mean(scaled * unit, -1, keepdims=True)
    )
    sums = jnp.concatenate([gain, gain_two_ref[...], bias], 1)
    width = pair.shape[1]
    sums = jnp.concatenate([sums, jnp.zeros((1, -sums.shape[1] % width), f32)], 1)
    found = [sums[:, i : i + width] for i in range(0, sums.shape[1], width)]
    found += [jnp.zeros((1, width), f32)] * (SUM_ROWS - len(found))
    sums = jnp.concatenate(found, 0)
    high = sums.astype(bf16)
    sent_ref[rows : rows + SUM_ROWS, :] = high
    sent_ref[rows + SUM_ROWS :, :] = (sums - high.astype(f32)).astype(bf16)


def pair_grad_kernel(rows, half_width, meta_ref, norm_ref, own_ref, peer_ref, out_ref, turned_ref):
    turned_ref[...] = norm_ref[:, D:].T
    first = pl.multiple_of(meta_ref[0] * half_width, 16)
    both = jnp.concatenate([own_ref[:rows, :], peer_ref[:rows, :]], 0)
    part = jnp.dot(turned_ref[pl.ds(first, half_width), :], both, preferred_element_type=f32)
    out_ref[:half_width, :] = part.astype(bf16)

    def sums(ref):
        high = ref[rows : rows + SUM_ROWS, :].astype(f32)
        return high + ref[rows + SUM_ROWS :, :].astype(f32)

    out_ref[half_width:, :] = (sums(own_ref) + sums(peer_ref)).astype(bf16)


def mlp_kernel(
    half_rows, spots_ref, x_a, x_b, gy_a, gy_b, gate_a, gate_b, up_a, up_b, down_a, down_b,
    xt_ref, midt_ref, gg_ref, gu_ref, gx_ref, out_ref, send_ref,
    x_all, gy_all, wg_all, wu_all, wd_all, mid_all, gg_all, gu_all,
):
    step = pl.program_id(0)

    @pl.when(step == 0)
    def start():
        x_all[:half_rows] = x_a[...]
        x_all[half_rows:] = x_b[...]
        gy_all[:half_rows] = gy_a[...]
        gy_all[half_rows:] = gy_b[...]
        xt_ref[...] = x_all[...].T

    here = pl.ds(pl.multiple_of(step * 256, 256), 256)
    wg = jnp.concatenate([gate_a[...], gate_b[...]], 1)
    wu = jnp.concatenate([up_a[...], up_b[...]], 1)
    wd = jnp.concatenate([down_a[...], down_b[...]], 0)
    wg_all[:, here] = wg
    wu_all[:, here] = wu
    wd_all[here, :] = wd
    core = spots_ref[1]
    column = lanes((1, 256)) + (step * 256 + spots_ref[2])
    own = (column < spots_ref[3]) == (core == 0)
    x = x_all[...]
    gate = jnp.dot(x, wg, preferred_element_type=f32)
    up = jnp.dot(x, wu, preferred_element_type=f32)
    grad = jnp.where(own, dot_nt(gy_all[...], wd), 0.0)
    sigma = jax.nn.sigmoid(gate)
    active = gate * sigma
    middle = jnp.where(own, active * up, 0.0).astype(bf16)
    grad_gate = (grad * up * (sigma + active * (1.0 - sigma))).astype(bf16)
    grad_up = (grad * active).astype(bf16)
    midt_ref[...] = middle.T
    gg_ref[...] = grad_gate
    gu_ref[...] = grad_up
    mid_all[:, here] = middle
    gg_all[:, here] = grad_gate
    gu_all[:, here] = grad_up

    @pl.when(step == pl.num_programs(0) - 1)
    def end():
        gx = dot_nt(gg_all[...], wg_all[...]) + dot_nt(gu_all[...], wu_all[...])
        gx_ref[...] = gx[:half_rows]
        send_ref[:half_rows] = gx[half_rows:].astype(bf16)
        out = jnp.dot(mid_all[...], wd_all[...], preferred_element_type=f32)
        out_ref[...] = out[:half_rows]
        send_ref[half_rows:] = out[half_rows:].astype(bf16)


def feed_forward(meta, x, early, w_gate, w_up, w_down, width):
    half = x[0].shape[0]
    tokens = 2 * half
    steps = width // 256
    tiles = width // 128 - 1

    def columns(j):
        return pl.BlockSpec((D, 128), lambda i, m: (0, m[1] * tiles + 2 * i + j))

    def rows(j):
        return pl.BlockSpec((128, D), lambda i, m: (m[1] * tiles + 2 * i + j, 0))

    whole = pl.BlockSpec((tokens, D), lambda i, m: (0, 0))
    halves = pl.BlockSpec((half, D), lambda i, m: (0, 0))
    tile = pl.BlockSpec((tokens, 256), lambda i, m: (0, i))
    hidden = jax.ShapeDtypeStruct((tokens, width), bf16)
    return pl.pallas_call(
        lambda *refs: mlp_kernel(half, *refs),
        out_shape=[
            jax.ShapeDtypeStruct((D, tokens), bf16),
            jax.ShapeDtypeStruct((width, tokens), bf16),
            hidden,
            hidden,
            jax.ShapeDtypeStruct((half, D), f32),
            jax.ShapeDtypeStruct((half, D), f32),
            jax.ShapeDtypeStruct((tokens, D), bf16),
        ],
        grid_spec=pltpu.PrefetchScalarGridSpec(
            num_scalar_prefetch=1,
            grid=(steps,),
            in_specs=[halves] * 4
            + [columns(0), columns(1), columns(0), columns(1), rows(0), rows(1)],
            out_specs=[
                pl.BlockSpec((D, tokens), lambda i, m: (0, 0)),
                pl.BlockSpec((256, tokens), lambda i, m: (i, 0)),
                tile,
                tile,
                halves,
                halves,
                whole,
            ],
            scratch_shapes=[pltpu.VMEM((tokens, D), bf16)] * 2
            + [pltpu.VMEM((D, width), bf16)] * 2
            + [pltpu.VMEM((width, D), bf16)]
            + [pltpu.VMEM((tokens, width), bf16)] * 3,
        ),
        compiler_params=pltpu.CompilerParams(vmem_limit_bytes=VMEM_BYTES),
        cost_estimate=pl.CostEstimate(
            flops=12 * tokens * width * D, bytes_accessed=6 * width * D, transcendentals=0
        ),
    )(meta, *x, *early, w_gate, w_gate, w_up, w_up, w_down, w_down)


def mlp_grad_kernel(chips, down_rows, main, meta_ref, xt_ref, gy_a, gy_b, midt_ref, gg_ref, gu_ref, *refs):
    out_refs = refs[:chips]
    mlp_acc, down_acc, blocks, sems = refs[chips:]
    core = meta_ref[1]
    at_main = pl.ds(pl.multiple_of(core * 128, 128), main)
    at_tile = pl.ds(pl.multiple_of((1 - core) * main, 128), 128)
    xt = xt_ref[...]
    mlp_acc[:, :main] = jnp.dot(xt, gg_ref[:, at_main], preferred_element_type=f32).astype(bf16)
    mlp_acc[:, main : 2 * main] = jnp.dot(
        xt, gu_ref[:, at_main], preferred_element_type=f32
    ).astype(bf16)
    mixed = gg_ref[:, at_tile].astype(f32) + pltpu.roll(gu_ref[:, at_tile].astype(f32), 64, 1)
    mlp_acc[:, 2 * main :] = jnp.dot(
        xt, mixed.astype(bf16), preferred_element_type=f32
    ).astype(bf16)
    gy = jnp.concatenate([gy_a[:, :D], gy_b[:, :D]], 0)
    down_acc[...] = jnp.dot(midt_ref[...], gy, preferred_element_type=f32)

    mlp_rows = mlp_acc.shape[0] // chips
    columns = mlp_acc.shape[1] // 128
    half = chips // 2
    copies = []
    for slot in sorted(range(chips), key=lambda s: abs(s - half) if s else chips):
        owner = meta_ref[12 + slot]
        block = mlp_acc[pl.ds(pl.multiple_of(owner * mlp_rows, 16), mlp_rows), :]
        for j in range(columns):
            for i in range(mlp_rows // 16):
                blocks[slot, j * 16 : (j + 1) * 16, i * 128 : (i + 1) * 128] = block[
                    i * 16 : (i + 1) * 16, j * 128 : (j + 1) * 128
                ]
        first = pl.multiple_of(core * 64 + owner * down_rows, 8)
        blocks[slot, columns * 16 :, :] = down_acc[pl.ds(first, down_rows), :].astype(bf16)
        copy = pltpu.make_async_copy(blocks.at[slot], out_refs[slot], sems.at[slot])
        copy.start()
        copies.append(copy)
    for copy in copies:
        copy.wait()


def mlp_gradients(meta, xt, early, midt, gg, gu, after, chips, down_rows, main):
    tokens = gg.shape[0]
    columns = (2 * main + 128) // 128
    rows = columns * 16 + down_rows
    args = [meta, xt, *early, midt, gg, gu]
    anywhere = pl.BlockSpec(memory_space=pl.ANY)

    def kernel(*refs):
        mlp_grad_kernel(chips, down_rows, main, *refs[: len(args)], *refs[len(args) + 1 :])

    return pl.pallas_call(
        kernel,
        out_shape=[jax.ShapeDtypeStruct((rows, D), bf16)] * chips,
        in_specs=[pl.BlockSpec(memory_space=pltpu.SMEM)]
        + [pl.BlockSpec(memory_space=pltpu.VMEM)] * (len(args) - 1)
        + [anywhere],
        out_specs=[anywhere] * chips,
        scratch_shapes=[
            pltpu.VMEM((D, columns * 128), bf16),
            pltpu.VMEM((midt.shape[0], D), f32),
            pltpu.VMEM((chips, rows, D), bf16),
            pltpu.SemaphoreType.DMA((chips,)),
        ],
        compiler_params=pltpu.CompilerParams(vmem_limit_bytes=VMEM_BYTES),
        cost_estimate=pl.CostEstimate(
            flops=6 * tokens * midt.shape[0] * D, bytes_accessed=4 * chips * rows * D,
            transcendentals=0,
        ),
    )(*args, after)


def small_grad_kernel(
    chips, q_rows, rows, cols, meta_ref, norm_a, norm_b, near_a, near_b, *refs
):
    out_refs, acc, turned_ref = refs[:-2], refs[-2], refs[-1]
    first = pl.multiple_of((2 * meta_ref[0] + meta_ref[1]) * q_rows, 16)
    grads, queries, attended = [], [], []
    for near_ref in (near_a, near_b):
        for b in range(2):
            for i, found in enumerate((grads, queries, attended)):
                found.append(near_ref[(3 * b + i) * rows : (3 * b + i + 1) * rows, :])
    turned_ref[...] = jnp.concatenate([norm_a[:, D:], norm_b[:, D:]], 0).T
    acc[:, :WIDTH_Q] = jnp.dot(
        turned_ref[pl.ds(first, q_rows), :],
        jnp.concatenate(queries, 0),
        preferred_element_type=f32,
    ).astype(bf16)
    acc[:, WIDTH_Q:cols] = jnp.zeros((q_rows, cols - WIDTH_Q), bf16)
    turned_ref[...] = jnp.concatenate(attended, 0).T
    acc[:, cols:] = jnp.dot(
        turned_ref[pl.ds(first, q_rows), :], jnp.concatenate(grads, 0), preferred_element_type=f32
    ).astype(bf16)
    width = acc.shape[1] // chips
    for out_ref, slot in zip(out_refs, range(chips)):
        owner = meta_ref[12 + slot]
        block = acc[:, pl.ds(pl.multiple_of(owner * width, 128), width)]
        tall = jnp.concatenate([block[:, i * 128 : (i + 1) * 128] for i in range(width // 128)], 0)
        piece = out_ref.shape[0]
        for i in range(D // 128):
            out_ref[:, i * 128 : (i + 1) * 128] = tall[i * piece : (i + 1) * piece]


def place_all(meta, slots, pairs, old, sizes, rest=None):
    main, ff_loc, q_rows, cols, down_rows, chips = sizes
    mlp_rows = D // chips
    columns = (2 * main + 128) // 128
    tiles = main // 128
    lanes_out = D // 128
    top = columns * 16
    blocks = [x for pair in pairs for x in pair]
    count = len(blocks)
    piece = blocks[0].shape[0] - top - down_rows
    parts = (cols + D) // chips // 128
    keep = [] if old is None else list(old)
    last = [] if rest is None else list(rest)
    known = WIDTH_Q // 128

    def kernel(meta_ref, *refs):
        ins = refs[:count]
        outs_at = count + len(last) + len(keep)
        gate_out, up_out, down_out, joint_out, proj_out, token_ref = refs[outs_at : outs_at + 6]
        gate_buf, up_buf, down_buf, small_buf, rest_buf, sems, small_sems, rest_sem = refs[
            outs_at + 6 :
        ]
        core_zero = meta_ref[1] == 0
        copies = []

        def send(src, dst, sem):
            copy = pltpu.make_async_copy(src, dst, sem)
            copy.start()
            copies.append(copy)

        def column(ref, j):
            found = [
                ref[j * 16 : (j + 1) * 16, i * 128 : (i + 1) * 128] for i in range(mlp_rows // 16)
            ]
            return jnp.concatenate(found, 0).astype(f32)

        for k, slot in enumerate(slots):
            for j in range(columns):
                got = column(ins[2 * k], j)
                other = column(ins[2 * k + 1], j)
                zero = jnp.where(core_zero, got, other)
                one = jnp.where(core_zero, other, got)
                if j < 2 * tiles:
                    buf = gate_buf if j < tiles else up_buf
                    at = (j % tiles) * 128
                    buf[k, :, at : at + 128] = zero
                    buf[k, :, at + main + 128 : at + main + 256] = one
                else:
                    left = lanes(zero.shape) < 64
                    gate_buf[k, :, main : main + 128] = jnp.where(left, zero, one)
                    up_buf[k, :, main : main + 128] = pltpu.roll(jnp.where(left, one, zero), 64, 1)
            owner = meta_ref[12 + slot]
            here = pl.ds(pl.multiple_of(owner * mlp_rows, 8), mlp_rows)
            send(gate_buf.at[k], gate_out.at[here, :], sems.at[4 * k])
            send(up_buf.at[k], up_out.at[here, :], sems.at[4 * k + 1])
            for side in range(2):
                b = 2 * k + side
                core = meta_ref[1] if side == 0 else 1 - meta_ref[1]
                down_buf[b] = ins[b][top + piece :, :].astype(f32)
                here = pl.ds(pl.multiple_of((core * chips + owner) * down_rows, 8), down_rows)
                send(down_buf.at[b], down_out.at[here, :], sems.at[4 * k + 2 + side])
                tall = jnp.concatenate(
                    [ins[b][top : top + piece, i * 128 : (i + 1) * 128] for i in range(lanes_out)], 0
                ).astype(f32)
                rows = pl.ds(pl.multiple_of(core * q_rows, 8), q_rows)
                for i in range(parts):
                    small_buf[b, i] = tall[i * q_rows : (i + 1) * q_rows]
                    block = owner * parts + i

                    @pl.when(block < known)
                    def joint(b=b, i=i, rows=rows, block=block):
                        at = pl.ds(pl.multiple_of(block * 128, 128), 128)
                        pltpu.make_async_copy(
                            small_buf.at[b, i], joint_out.at[rows, at], small_sems.at[b, i]
                        ).start()

                    @pl.when(block >= cols // 128)
                    def proj(b=b, i=i, rows=rows, block=block):
                        at = pl.ds(pl.multiple_of((block - cols // 128) * 128, 128), 128)
                        pltpu.make_async_copy(
                            small_buf.at[b, i], proj_out.at[rows, at], small_sems.at[b, i]
                        ).start()

        token_ref[...] = jnp.zeros(token_ref.shape, f32)
        if last:
            rows = last[0].shape[0]
            for core, ref in ((meta_ref[1], refs[count]), (1 - meta_ref[1], refs[count + 1])):
                rest_buf[pl.ds(pl.multiple_of(core * rows, 8), rows), :] = ref[...].astype(f32)
            send(rest_buf.at[: 2 * q_rows, :], joint_out.at[:, WIDTH_Q:cols], rest_sem)
        for copy in copies:
            copy.wait()
        for b in range(count):
            for i in range(parts):
                block = meta_ref[12 + slots[b // 2]] * parts + i

                @pl.when((block < known) | (block >= cols // 128))
                def done(b=b, i=i):
                    pltpu.make_async_copy(
                        small_buf.at[b, i],
                        proj_out.at[pl.ds(0, q_rows), pl.ds(0, 128)],
                        small_sems.at[b, i],
                    ).wait()

    anywhere = pl.BlockSpec(memory_space=pl.ANY)
    result = pl.pallas_call(
        kernel,
        out_shape=[
            jax.ShapeDtypeStruct((D, ff_loc), f32),
            jax.ShapeDtypeStruct((D, ff_loc), f32),
            jax.ShapeDtypeStruct((ff_loc, D), f32),
            jax.ShapeDtypeStruct((2 * q_rows, cols), f32),
            jax.ShapeDtypeStruct((2 * q_rows, D), f32),
            jax.ShapeDtypeStruct((8, 128), f32),
        ],
        in_specs=[pl.BlockSpec(memory_space=pltpu.SMEM)]
        + [pl.BlockSpec(memory_space=pltpu.VMEM)] * (count + len(last))
        + [anywhere] * len(keep),
        out_specs=[anywhere] * 5 + [pl.BlockSpec(memory_space=pltpu.VMEM)],
        scratch_shapes=[
            pltpu.VMEM((len(slots), mlp_rows, ff_loc), f32),
            pltpu.VMEM((len(slots), mlp_rows, ff_loc), f32),
            pltpu.VMEM((count, down_rows, D), f32),
            pltpu.VMEM((count, parts, q_rows, 128), f32),
            pltpu.VMEM((2 * q_rows + SUM_ROWS, cols - WIDTH_Q), f32),
            pltpu.SemaphoreType.DMA((4 * len(slots),)),
            pltpu.SemaphoreType.DMA((count, parts)),
            pltpu.SemaphoreType.DMA,
        ],
        input_output_aliases={1 + count + len(last) + i: i for i in range(len(keep))},
        compiler_params=pltpu.CompilerParams(vmem_limit_bytes=VMEM_BYTES),
        cost_estimate=pl.CostEstimate(
            flops=0, bytes_accessed=8 * sum(x.size for x in blocks), transcendentals=0
        ),
    )(meta, *blocks, *last, *keep)
    return list(result[:5]), result[5]


def place_blocks(blocks, spots, out_shape, old=None):
    shape = blocks[0].shape
    count = len(blocks)
    if shape[0] % 8 or shape[1] % 128:
        out = jnp.zeros(out_shape, f32) if old is None else old
        for block, (i, j) in zip(blocks, spots):
            out = lax.dynamic_update_slice(
                out, block.astype(f32), (i * shape[0], j * shape[1])
            )
        return out

    def kernel(spots_ref, *refs):
        step = pl.program_id(0)
        out_ref = refs[-1]
        for i in range(count):

            @pl.when(step == i)
            def write(i=i):
                out_ref[...] = refs[i][...].astype(f32)

    keep = [] if old is None else [old]
    return pl.pallas_call(
        kernel,
        out_shape=jax.ShapeDtypeStruct(out_shape, f32),
        grid_spec=pltpu.PrefetchScalarGridSpec(
            num_scalar_prefetch=1,
            grid=(count,),
            in_specs=[pl.BlockSpec(shape, lambda i, spots: (0, 0))] * count
            + [pl.BlockSpec(memory_space=pl.ANY)] * len(keep),
            out_specs=pl.BlockSpec(shape, lambda i, spots: (spots[i, 0], spots[i, 1])),
        ),
        input_output_aliases={} if old is None else {count + 1: 0},
        compiler_params=pltpu.CompilerParams(vmem_limit_bytes=VMEM_BYTES),
    )(jnp.stack([jnp.stack(s) for s in spots]).astype(jnp.int32), *blocks, *keep)


def local(tokens, w_qkv, b_qkv, w_out, gain_attn, gain_mlp, w_gate, w_up, w_down, cotangent):
    net = Net()
    rows = tokens.shape[1]
    half_rows = rows // 2
    ctx_count = net.ctx
    core = net.core
    chips = net.chips
    part_rows = GROUP * half_rows
    x = tokens[0]
    gain_one = gain_attn[None]
    gain_two = gain_mlp[None]

    w_qkv_full = net.full_rows(w_qkv)

    ff_loc = w_gate.shape[1]
    ff_half = ff_loc // 2
    main = (ff_half // 128) * 128
    rest = ff_half - main
    width = main + 2 * rest
    first = core * main
    tiled = net.dp == 2 and 2 * rest == 128 and width % 256 == 0 and chips == 8 and ff_half == chips * RING_ROWS
    ring = jnp.arange(chips, dtype=jnp.int32)
    owners_of = (net.pos - ring) % chips
    spots = jnp.concatenate(
        [jnp.stack([net.d, core, first, jnp.int32(ff_half)]), owners_of, owners_of]
    ).astype(jnp.int32)

    row_ids = jnp.arange(half_rows, dtype=jnp.int32)
    place = jnp.concatenate(
        [net.c * half_rows + row_ids, (2 * ctx_count - 1 - net.c) * half_rows + row_ids]
    )
    freq = ROPE_BASE ** (-((jnp.arange(128) % (HD // 2)).astype(f32) * (2.0 / HD)))
    angle = place.astype(f32)[:, None] * freq[None, :]
    cosine, sine = jnp.cos(angle), jnp.sin(angle)
    normed_one, queries, pairs = call(
        qkv_kernel,
        [
            jax.ShapeDtypeStruct((rows, D), bf16),
            jax.ShapeDtypeStruct((rows, WIDTH_Q), bf16),
            jax.ShapeDtypeStruct((rows, 2 * WIDTH_K), bf16),
        ],
        [x, gain_one, w_qkv_full, b_qkv[None], cosine, sine],
        flops=2 * rows * D * 1152,
    )

    slots = net.ring_gather(pairs)
    mine = jnp.concatenate(slots, 0)
    other = net.swap(mine)
    order = jnp.array(net.order, jnp.int32)
    chip_ids = order[(net.pos - jnp.arange(chips, dtype=jnp.int32)) % chips]
    meta = jnp.concatenate([net.c[None], 2 * chip_ids + core, 2 * chip_ids + 1 - core])
    meta = meta.astype(jnp.int32)

    late_w, late_g, late_n, unused = lax.optimization_barrier((w_out, cotangent[0], normed_one, pairs))
    w_out_full = net.full_rows(late_w)
    early = net.group_parts(jnp.concatenate([late_g, late_n], 1))

    total_keys = rows * ctx_count
    padded = (KH, 2 * part_rows, 128)
    attended_low, attended, lse, spread, keys, values, hidden, normed_two = call(
        lambda *refs: forward_kernel(ctx_count, *refs),
        [
            jax.ShapeDtypeStruct((rows, WIDTH_Q), bf16),
            jax.ShapeDtypeStruct(padded, f32),
            jax.ShapeDtypeStruct((KH, 2, 8, part_rows), f32),
            jax.ShapeDtypeStruct(padded, bf16),
            jax.ShapeDtypeStruct((total_keys, WIDTH_K), bf16),
            jax.ShapeDtypeStruct((total_keys, WIDTH_K), bf16),
            jax.ShapeDtypeStruct((rows, D), f32),
            jax.ShapeDtypeStruct((rows, D), bf16),
        ],
        [meta, queries, mine, other, x, w_out_full, gain_two],
        smem=1,
        scratch=[
            pltpu.VMEM((KH, total_keys // KEYS, part_rows, KEYS), f32),
            pltpu.VMEM((KH, part_rows, 128), f32),
            pltpu.VMEM((KH, part_rows, 128), f32),
        ],
        flops=8 * KH * part_rows * total_keys * 128,
    )

    normed_two_parts = net.group_parts(normed_two)
    chip_rows = net.dp * rows
    down_rows = ff_half // chips
    mlp_rows = D // chips
    if tiled:
        x_turned, mid_turned, gate_low, up_low, grad_mine, out_mine, sent = feed_forward(
            spots, normed_two_parts, early, w_gate, w_up, w_down, width
        )
    else:
        normed_two_group = jnp.concatenate(normed_two_parts, 0)
        grad_out_group = jnp.concatenate(early, 0)[:, :D]
        own_cols = (jnp.arange(width) + first < ff_half) == (core == 0)
        wg = lax.dynamic_slice(w_gate, (0, first), (D, width))
        wu = lax.dynamic_slice(w_up, (0, first), (D, width))
        wd = lax.dynamic_slice(w_down, (first, 0), (width, D))
        gate = jnp.dot(normed_two_group, wg, preferred_element_type=f32)
        upper = jnp.dot(normed_two_group, wu, preferred_element_type=f32)
        sigma = jax.nn.sigmoid(gate)
        activated = gate * sigma
        middle = jnp.where(own_cols, activated * upper, 0.0).astype(bf16)
        grad_middle = jnp.einsum("td,fd->tf", grad_out_group, wd, preferred_element_type=f32)
        slope = sigma * (1.0 + gate * (1.0 - sigma))
        grad_gate_low = jnp.where(own_cols, grad_middle * upper * slope, 0.0).astype(bf16)
        grad_up_low = jnp.where(own_cols, grad_middle * activated, 0.0).astype(bf16)

        grad_normed_two = jnp.einsum(
            "tf,df->td", grad_gate_low, wg, preferred_element_type=f32
        ) + jnp.einsum("tf,df->td", grad_up_low, wu, preferred_element_type=f32)
        mlp_out = jnp.dot(middle, wd, preferred_element_type=f32)
        grad_mine, out_mine = grad_normed_two[:chip_rows], mlp_out[:chip_rows]
        sent = jnp.concatenate([grad_normed_two[chip_rows:], mlp_out[chip_rows:]], 0).astype(bf16)
    swapped = net.swap(sent)
    grad_chip = grad_mine + swapped[:chip_rows].astype(f32)
    mlp_chip = out_mine + swapped[chip_rows:].astype(f32)
    grad_two = grad_chip[:rows]
    for s in range(1, net.dp):
        sent_two = grad_chip[s * rows : (s + 1) * rows].astype(bf16)
        grad_two = grad_two + net.shift(sent_two, net.dp - s).astype(f32)

    def attention_back(*after):
        grad_hidden, grad_attn_low, grad_gain_two, grad_queries, terms_mine, terms_other = call(
            lambda *refs: backward_kernel(ctx_count, *refs),
            [
                jax.ShapeDtypeStruct((rows, D), f32),
                jax.ShapeDtypeStruct((rows, D), bf16),
                jax.ShapeDtypeStruct((1, D), f32),
                jax.ShapeDtypeStruct((rows, WIDTH_Q), bf16),
                jax.ShapeDtypeStruct((chips * rows, 2 * WIDTH_K), f32),
                jax.ShapeDtypeStruct((chips * rows, 2 * WIDTH_K), bf16),
            ],
            [
                meta, grad_two, hidden, cotangent[0], gain_two, w_out_full, spread, keys, values, lse,
                attended, cosine, sine, *after,
            ],
            smem=1,
            loose=len(after),
            scratch=[
                pltpu.VMEM(padded, bf16),
                pltpu.VMEM(padded, f32),
                pltpu.VMEM((total_keys, WIDTH_K), f32),
                pltpu.VMEM((total_keys, WIDTH_K), f32),
            ],
            flops=20 * KH * part_rows * total_keys * 128,
        )
        other_terms = net.swap(terms_other)

        def row_sums(*after):
            pair_sums = call(
                pair_kernel,
                [jax.ShapeDtypeStruct((rows, 2 * WIDTH_K), f32)]
                + [jax.ShapeDtypeStruct((rows, 2 * WIDTH_K), bf16)] * (chips - 1),
                [terms_mine, other_terms, *after],
                loose=len(after),
            )
            return net.ring_parts(pair_sums)

        def finish(grad_pairs):
            return call(
                finish_kernel,
                [
                    jax.ShapeDtypeStruct((rows + 2 * SUM_ROWS, 2 * WIDTH_K), bf16),
                    jax.ShapeDtypeStruct((rows, D), f32),
                    jax.ShapeDtypeStruct((1, D), f32),
                    jax.ShapeDtypeStruct((1, w_qkv.shape[1]), f32),
                ],
                [grad_queries, x, gain_one, w_qkv_full, cosine, sine, grad_hidden, grad_gain_two]
                + grad_pairs,
            )

        return grad_attn_low, grad_gain_two, grad_queries, row_sums, finish

    if tiled:
        terms = mlp_gradients(
            spots, x_turned, early, mid_turned, gate_low, up_low, sent_two, chips, down_rows, main
        )
        grad_attn_low, grad_gain_two, grad_queries, row_sums, finish = attention_back(terms[0])
        found = []

        def between(*blocks):
            found.extend(row_sums(*blocks))
            return found[1]

        fwd, back = net.ring_sum(terms, between)
        grad_pairs, marks = found
        sum_mlp, sum_down = ring_end(fwd, back, terms[0], terms[0].shape[0] - down_rows)
    else:
        part_down = jnp.einsum(
            "tf,td->fd", middle, grad_out_group, preferred_element_type=f32
        ).astype(bf16)
        part_down = lax.dynamic_slice(part_down, (core * rest, 0), (ff_half, D))

        def down_chunk(slot):
            return lax.dynamic_slice(part_down, (net.owner(slot) * down_rows, 0), (down_rows, D))

        sum_down = net.ring_scatter([down_chunk(s) for s in range(chips)]).astype(bf16)

        def split_main(x):
            left = (x[:, :main], x[:, main:])
            right = (x[:, 2 * rest :], x[:, : 2 * rest])
            return (
                jnp.where(core == 0, left[0], right[0]),
                jnp.where(core == 0, left[1], right[1]),
            )

        gate_main, gate_tile = split_main(grad_gate_low)
        up_main, up_tile = split_main(grad_up_low)
        packed = jnp.concatenate(
            [gate_main, up_main, gate_tile + jnp.roll(up_tile, rest, 1)], 1
        )
        part_mlp = jnp.einsum(
            "td,tf->df", normed_two_group, packed, preferred_element_type=f32
        ).astype(bf16)

        def mlp_chunk(slot):
            return lax.dynamic_slice(
                part_mlp, (net.owner(slot) * mlp_rows, 0), (mlp_rows, 2 * ff_half)
            )

        sum_mlp = net.ring_scatter([mlp_chunk(s) for s in range(chips)]).astype(bf16)
        sum_mlp = lax.optimization_barrier(sum_mlp)
        grad_attn_low, grad_gain_two, grad_queries, row_sums, finish = attention_back()
        grad_pairs, marks = row_sums()
    pair_sent, grad_input, grad_gain_one, grad_bias = finish(grad_pairs)

    out_sum = mlp_chip[:rows]
    for s in range(1, net.dp):
        got = net.shift(mlp_chip[s * rows : (s + 1) * rows].astype(bf16), net.dp - s)
        out_sum = out_sum + got.astype(f32)
    output = (hidden + out_sum).astype(bf16)
    near = net.group_parts(jnp.concatenate([grad_attn_low, grad_queries, attended_low], 0))

    q_rows = w_qkv.shape[0] // 2
    qkv_cols = w_qkv.shape[1]
    if tiled:
        piece = q_rows * (qkv_cols + D) // chips // D
        terms_small = call(
            lambda *refs: small_grad_kernel(chips, q_rows, rows, qkv_cols, *refs),
            [jax.ShapeDtypeStruct((piece, D), bf16)] * chips,
            [spots, *early, *near],
            smem=1,
            scratch=[
                pltpu.VMEM((q_rows, qkv_cols + D), bf16),
                pltpu.VMEM((D, 2 * chip_rows), bf16),
            ],
            flops=4 * chip_rows * D * (qkv_cols + D),
        )
        block = call(
            block_kernel,
            [jax.ShapeDtypeStruct((sum_mlp.shape[0] + piece + down_rows, D), bf16)],
            [sum_mlp, sum_down] + net.ring_parts(terms_small)[0] + list(marks[3]),
            loose=2,
        )[0]
        part_pair = call(
            lambda *refs: pair_grad_kernel(rows, 2 * q_rows, *refs),
            [jax.ShapeDtypeStruct((2 * q_rows + SUM_ROWS, 2 * WIDTH_K), bf16)],
            [spots, early[0], pair_sent, net.shift(pair_sent, 1)],
            smem=1,
            scratch=[pltpu.VMEM((D, chip_rows), bf16)],
        )[0]
        grad_pair = net.exchange_sum(part_pair)
        pair_halves = (grad_pair, net.swap(grad_pair))
        sums = jnp.where(core == 1, *pair_halves)[-SUM_ROWS:]
        small = sums.reshape(-1)[: 2 * D + qkv_cols].astype(f32)
        sizes = (main, ff_loc, q_rows, qkv_cols, down_rows, chips)
        grad_gate, grad_up, grad_down, grad_joint, grad_out_proj = net.gather_placed(
            block,
            lambda slots, pairs, old, rest=None: place_all(spots, slots, pairs, old, sizes, rest),
            pair_halves,
            [[part_pair], [], []],
        )
    else:
        gathered = jnp.concatenate(near, 0).reshape(2 * net.dp, 3, rows, D)
        grad_attn_group = gathered[:, 0].reshape(2 * net.dp * rows, D)
        attended_group = gathered[:, 2].reshape(2 * net.dp * rows, D)
        normed_one_group = jnp.concatenate(early, 0)[:, D:]
        joint_group = net.group_gather(jnp.concatenate([grad_queries, pair_sent[:rows]], 1))
        q_first = net.d * (2 * q_rows) + core * q_rows
        group_rows = 2 * net.dp * rows
        part_out = jnp.einsum(
            "tc,td->cd",
            lax.dynamic_slice(attended_group, (0, q_first), (group_rows, q_rows)),
            grad_attn_group,
            preferred_element_type=f32,
        )
        part_joint = jnp.einsum(
            "td,tc->dc",
            lax.dynamic_slice(normed_one_group, (0, q_first), (group_rows, q_rows)),
            joint_group,
            preferred_element_type=f32,
        )
        part_small = jnp.concatenate([part_joint, part_out], 1).astype(bf16)
        small_cols = part_small.shape[1] // chips

        def small_chunk(slot):
            return lax.dynamic_slice(part_small, (0, net.owner(slot) * small_cols), (q_rows, small_cols))

        sum_small = net.ring_scatter([small_chunk(s) for s in range(chips)]).astype(bf16)

        tall = jnp.concatenate(
            [sum_small[:, i * 128 : (i + 1) * 128] for i in range(small_cols // 128)], 0
        )
        piece = tall.shape[0] // (D // 128)
        wide = jnp.concatenate([tall[i * piece : (i + 1) * piece] for i in range(D // 128)], 1)
        both = lax.optimization_barrier(jnp.concatenate([sum_down, wide], 0))

        owners = [net.owner(s) for s in range(chips)]
        got_mlp = net.ring_gather(sum_mlp)
        got_both = net.ring_gather(both)
        pairs_mlp = [(got, net.swap(got)) for got in got_mlp]
        pairs_both = [(got, net.swap(got)) for got in got_both]

        down_blocks, down_spots, small_blocks, small_spots = [], [], [], []
        for owner, pair in zip(owners, pairs_both):
            for which, got in zip((core, 1 - core), pair):
                down_blocks.append(got[:down_rows])
                down_spots.append((which * chips + owner, jnp.int32(0)))
                wide = got[down_rows:]
                tall = jnp.concatenate([wide[:, i * 128 : (i + 1) * 128] for i in range(D // 128)], 0)
                small_blocks.append(
                    jnp.concatenate(
                        [tall[i * q_rows : (i + 1) * q_rows] for i in range(small_cols // 128)], 1
                    )
                )
                small_spots.append((which, owner))
        grad_down = place_blocks(down_blocks, down_spots, (ff_loc, D))
        grad_small = place_blocks(small_blocks, small_spots, (2 * q_rows, part_small.shape[1]))
        grad_gate = jnp.zeros((D, ff_loc), f32)
        grad_up = jnp.zeros((D, ff_loc), f32)
        left_lane = jnp.arange(2 * rest) < rest
        for owner, (got, swapped) in zip(owners, pairs_mlp):
            zero = jnp.where(core == 0, got, swapped).astype(f32)
            one = jnp.where(core == 0, swapped, got).astype(f32)
            tile_zero, tile_one = zero[:, 2 * main :], one[:, 2 * main :]
            mid_gate = jnp.where(left_lane, tile_zero, tile_one)
            mid_up = jnp.roll(jnp.where(left_lane, tile_one, tile_zero), rest, 1)
            base = owner * mlp_rows
            grad_gate = lax.dynamic_update_slice(
                grad_gate, jnp.concatenate([zero[:, :main], mid_gate, one[:, :main]], 1), (base, 0)
            )
            grad_up = lax.dynamic_update_slice(
                grad_up,
                jnp.concatenate([zero[:, main : 2 * main], mid_up, one[:, main : 2 * main]], 1),
                (base, 0),
            )

        grad_joint, grad_out_proj = grad_small[:, :qkv_cols], grad_small[:, qkv_cols:]
        small = net.total(jnp.concatenate([grad_gain_one, grad_gain_two, grad_bias], 1))[0]
    return (
        output[None],
        grad_input[None],
        grad_joint,
        small[2 * D :],
        grad_out_proj,
        small[:D],
        small[D : 2 * D],
        grad_gate,
        grad_up,
        grad_down,
    )


def solution(mesh):
    placed = (
        P("dp", "ctx", None),
        P("dp", None),
        P(),
        P("dp", None),
        P(),
        P(),
        P(None, "dp"),
        P(None, "dp"),
        P("dp", None),
        P("dp", "ctx", None),
    )
    return jax.shard_map(
        local,
        mesh=mesh,
        in_specs=placed,
        out_specs=(
            P("dp", "ctx", None),
            P("dp", "ctx", None),
            P("dp", None),
            P(),
            P("dp", None),
            P(),
            P(),
            P(None, "dp"),
            P(None, "dp"),
            P("dp", None),
        ),
        check_vma=False,
    )
```

```python
import jax
import jax.numpy as jnp
from jax import lax
from jax.experimental import pallas as pl
from jax.experimental.pallas import tpu as pltpu
from jax.sharding import PartitionSpec as P

D = 896
QH = 14
KH = 2
HD = 64
GROUP = QH // KH
WIDTH_Q = QH * HD
WIDTH_K = KH * HD

EPS = 1e-06
ROPE_BASE = 1000000.0

f32 = jnp.float32
bf16 = jnp.bfloat16


def ring_order(chips):
    if chips % 2:
        return list(range(chips))
    rows = chips // 2
    return [2 * i for i in range(rows)] + [2 * i + 1 for i in reversed(range(rows))]


def half_cut(rows):
    cut = (rows // 2 + 7) // 8 * 8
    return cut if cut < rows else rows // 2


def add_low(a, b):
    return (a.astype(f32) + b.astype(f32)).astype(bf16)


class Net:
    def __init__(self):
        self.dp = lax.axis_size("dp")
        self.ctx = lax.axis_size("ctx")
        self.chips = self.ctx // 2
        self.order = ring_order(self.chips)
        self.d = lax.axis_index("dp")
        self.c = lax.axis_index("ctx")
        self.core = self.c % 2
        place = [0] * self.chips
        for spot, chip in enumerate(self.order):
            place[chip] = spot
        self.pos = jnp.array(place, jnp.int32)[self.c // 2]

    def swap(self, x):
        return lax.ppermute(x, "ctx", [(i, i ^ 1) for i in range(self.ctx)])

    def shift(self, x, step):
        n = self.dp
        return lax.ppermute(x, "dp", [(i, (i + step) % n) for i in range(n)])

    def hop(self, x, step):
        n = self.chips
        perm = []
        for spot in range(n):
            for core in range(2):
                perm.append((2 * self.order[spot] + core, 2 * self.order[(spot + step) % n] + core))
        return lax.ppermute(x, "ctx", perm)

    def owner(self, slot):
        return (self.pos - slot) % self.chips

    def group_parts(self, x):
        chip = jnp.concatenate([x] + [self.shift(x, s) for s in range(1, self.dp)], 0)
        return chip, self.swap(chip)

    def group_gather(self, x):
        return jnp.concatenate(self.group_parts(x), 0)

    def ring_gather(self, x):
        n = self.chips
        half = n // 2
        cut = half_cut(x.shape[0])
        found = [x] + [None] * (n - 1)
        fwd, back = x, x
        for s in range(1, half):
            fwd = self.hop(fwd, 1)
            back = self.hop(back, -1)
            found[s] = fwd
            found[n - s] = back
        found[half] = jnp.concatenate([self.hop(fwd[:cut], 1), self.hop(back[cut:], -1)], 0)
        return found

    def ring_scatter(self, local):
        n = self.chips
        half = n // 2
        cut = half_cut(local[half].shape[0])

        def add(got, mine):
            return (got.astype(f32) + mine.astype(f32)).astype(bf16)

        fwd = self.hop(local[half][:cut], 1)
        back = self.hop(local[half][cut:], -1)
        for s in range(1, half):
            mine_f = local[half + s]
            mine_b = local[half - s]
            if s == 1:
                mine_f = jnp.concatenate([add(fwd, mine_f[:cut]), mine_f[cut:]], 0)
                mine_b = jnp.concatenate([mine_b[:cut], add(back, mine_b[cut:])], 0)
            else:
                mine_f = add(fwd, mine_f)
                mine_b = add(back, mine_b)
            fwd = self.hop(mine_f, 1)
            back = self.hop(mine_b, -1)
        return fwd.astype(f32) + back.astype(f32) + local[0].astype(f32)

    def full_rows(self, shard):
        rows = shard.shape[0]
        half = rows // 2
        piece = lax.dynamic_slice(shard, (self.core * half, 0), (half, shard.shape[1]))
        blocks = [shard]
        for s in range(1, self.dp):
            got = self.shift(piece, s)
            other = self.swap(got)
            low = jnp.where(self.core == 0, got, other)
            high = jnp.where(self.core == 0, other, got)
            blocks.append(jnp.concatenate([low, high], 0))
        if self.dp == 2:
            first = jnp.where(self.d == 0, blocks[0], blocks[1])
            second = jnp.where(self.d == 0, blocks[1], blocks[0])
            return jnp.concatenate([first, second], 0)
        ranked = jnp.stack(blocks)[(self.d - jnp.arange(self.dp)) % self.dp]
        return ranked.reshape(self.dp * rows, shard.shape[1])

    def total(self, x):
        x = x + self.swap(x)
        bit = 1
        while bit < self.chips:
            x = x + lax.ppermute(x, "ctx", [(i, i ^ (2 * bit)) for i in range(self.ctx)])
            bit *= 2
        bit = 1
        while bit < self.dp:
            x = x + lax.ppermute(x, "dp", [(i, i ^ bit) for i in range(self.dp)])
            bit *= 2
        return x

    def ring_parts(self, local):
        n = self.chips
        half = n // 2
        cut = half_cut(local[half].shape[0])

        def add(got, mine):
            return (got.astype(f32) + mine.astype(f32)).astype(bf16)

        fwd, back = self.hop(local[half][:cut], 1), self.hop(local[half][cut:], -1)
        marks = [(fwd, back)]
        for s in range(1, half):
            mine_f, mine_b = local[half + s], local[half - s]
            if s == 1:
                mine_f = jnp.concatenate([add(fwd, mine_f[:cut]), mine_f[cut:]], 0)
                mine_b = jnp.concatenate([mine_b[:cut], add(back, mine_b[cut:])], 0)
            else:
                mine_f, mine_b = add(fwd, mine_f), add(back, mine_b)
            fwd, back = self.hop(mine_f, 1), self.hop(mine_b, -1)
            marks.append((fwd, back))
        return [local[0], fwd, back], marks

    def exchange_start(self, x):
        half = x.shape[0] // 2
        x = add_low(x, self.swap(x))
        x = lax.dynamic_slice(x, (self.core * half, 0), (half, x.shape[1]))
        bit = 1
        while 2 * bit < self.chips:
            x = self.exchange(x, bit)
            bit *= 2
        return x

    def exchange(self, x, bit):
        return add_low(x, lax.ppermute(x, "ctx", [(i, i ^ (2 * bit)) for i in range(self.ctx)]))

    def ring_sum(self, terms, between):
        half = self.chips // 2
        fwd, back = self.hop(terms[half], 1), self.hop(terms[half - 1], -1)

        def add(got, slot):
            return (got.astype(f32) + terms[slot].astype(f32)).astype(bf16)

        for s in range(1, half):
            blocks = [add(fwd, half + s)]
            if s < half - 1:
                blocks.append(add(back, half - 1 - s))
            if s == 1:
                marks = between(*blocks)
            else:
                blocks = gate(marks[s - 2], blocks)
            fwd = self.hop(blocks[0], 1)
            if s < half - 1:
                back = self.hop(blocks[1], -1)
        return fwd, back

    def gather_placed(self, x, place, rest, marks):
        n = self.chips
        half = n // 2
        fwd = back = x
        placed = None
        waiting = ([0], [(x, self.swap(x))])
        for s in range(1, half + 1):
            if s > 1:
                placed, token = place(*waiting, placed)
                fwd, back = gate([token] + marks[s - 2], [fwd, back])
                waiting = ([s - 1, n - s + 1], [(fwd, self.swap(fwd)), (back, self.swap(back))])
            if s < half:
                fwd, back = self.hop(fwd, 1), self.hop(back, -1)
            else:
                cut = half_cut(fwd.shape[0])
                fwd, back = self.hop(fwd[:cut], 1), self.hop(back[cut:], -1)
        placed, token = place(*waiting, placed)
        far = join(fwd, back, token)
        rest = gate([token], [rest])[0]
        rest = self.exchange(rest, half)
        halves = (rest, self.swap(rest))
        return place([half], [(far, self.swap(far))], placed, halves)[0], halves


VMEM_BYTES = 56 * 1024 * 1024
KEYS = 256
RING_ROWS = 152


def full_spec(shape):
    return pl.BlockSpec(shape, lambda: (0,) * len(shape))


def call(kernel, outs, args, smem=0, scratch=(), flops=0, loose=0):
    tight = len(args) - loose
    specs = [pl.BlockSpec(memory_space=pltpu.SMEM)] * smem
    specs += [pl.BlockSpec(memory_space=pltpu.VMEM)] * (tight - smem)
    specs += [pl.BlockSpec(memory_space=pl.ANY)] * loose

    def body(*refs):
        kernel(*refs[:tight], *refs[tight + loose :])

    moved = sum(x.size * x.dtype.itemsize for x in list(args) + list(outs))
    return pl.pallas_call(
        body,
        out_shape=list(outs),
        in_specs=specs,
        out_specs=[pl.BlockSpec(memory_space=pltpu.VMEM)] * len(outs),
        scratch_shapes=list(scratch),
        compiler_params=pltpu.CompilerParams(vmem_limit_bytes=VMEM_BYTES),
        cost_estimate=pl.CostEstimate(flops=flops, bytes_accessed=moved, transcendentals=0),
    )(*args)


def lanes(shape):
    return lax.broadcasted_iota(jnp.int32, shape, len(shape) - 1)


def dot_nt(a, b, precision=None):
    return lax.dot_general(
        a, b, (((1,), (1,)), ((), ())), preferred_element_type=f32, precision=precision
    )


def dot_tn(a, b):
    return lax.dot_general(a, b, (((0,), (0,)), ((), ())), preferred_element_type=f32)


def gate(tokens, blocks):
    count, before = len(blocks), len(tokens)
    anywhere = pl.BlockSpec(memory_space=pl.ANY)

    def kernel(*refs):
        return None

    return pl.pallas_call(
        kernel,
        out_shape=[jax.ShapeDtypeStruct(x.shape, x.dtype) for x in blocks],
        in_specs=[anywhere] * (before + count),
        out_specs=[anywhere] * count,
        input_output_aliases={before + i: i for i in range(count)},
        cost_estimate=pl.CostEstimate(flops=0, bytes_accessed=1024, transcendentals=0),
    )(*tokens, *blocks)


def join(first, second, token):
    cut = first.shape[0]

    def kernel(first_ref, second_ref, out_ref):
        out_ref[:cut, :] = first_ref[...]
        out_ref[cut:, :] = second_ref[...]

    shape = (cut + second.shape[0], first.shape[1])
    return call(
        kernel, [jax.ShapeDtypeStruct(shape, first.dtype)], [first, second, token], loose=1
    )[0]


def ring_end(fwd, back, term, split):
    rows, columns = term.shape

    def kernel(fwd_ref, back_ref, term_ref, first_ref, rest_ref):
        for ref, here in ((first_ref, slice(0, split)), (rest_ref, slice(split, rows))):
            total = fwd_ref[here, :].astype(f32) + back_ref[here, :].astype(f32)
            ref[...] = (total + term_ref[here, :].astype(f32)).astype(bf16)

    outs = [
        jax.ShapeDtypeStruct((split, columns), bf16),
        jax.ShapeDtypeStruct((rows - split, columns), bf16),
    ]
    return call(kernel, outs, [fwd, back, term])


def pair_kernel(mine_ref, got_ref, *out_refs):
    rows = out_refs[0].shape[0]
    for s, out_ref in enumerate(out_refs):
        here = slice(s * rows, (s + 1) * rows)
        out_ref[...] = (mine_ref[here, :] + got_ref[here, :].astype(f32)).astype(out_ref.dtype)


def block_kernel(mlp_ref, down_ref, *refs):
    small = refs[0][...].astype(f32)
    for ref in refs[1:-1]:
        small = small + ref[...].astype(f32)
    out_ref = refs[-1]
    top = mlp_ref.shape[0]
    piece = small.shape[0]
    out_ref[:top, :] = mlp_ref[...]
    out_ref[top : top + piece, :] = small.astype(bf16)
    out_ref[top + piece :, :] = down_ref[...]


def qkv_kernel(x_ref, gain_ref, w_ref, b_ref, cos_ref, sin_ref, norm_ref, q_ref, pair_ref):
    x = x_ref[...].astype(f32)
    inverse = lax.rsqrt(jnp.mean(x * x, -1, keepdims=True) + EPS)
    normed = (x * inverse * gain_ref[...]).astype(bf16)
    norm_ref[...] = normed
    joint = jnp.dot(normed, w_ref[...], preferred_element_type=f32) + b_ref[...]
    cosine = cos_ref[...]
    sine = sin_ref[...]
    early = lanes(cosine.shape) % HD < HD // 2
    for i in range((WIDTH_Q + WIDTH_K) // 128):
        tile = joint[:, i * 128 : (i + 1) * 128]
        turned = jnp.where(early, -pltpu.roll(tile, 96, 1), pltpu.roll(tile, 32, 1))
        turned = tile * cosine + turned * sine
        if i * 128 < WIDTH_Q:
            q_ref[:, i * 128 : (i + 1) * 128] = turned.astype(bf16)
        else:
            pair_ref[:, :WIDTH_K] = turned.astype(bf16)
    pair_ref[:, WIDTH_K:] = joint[:, WIDTH_Q + WIDTH_K :].astype(bf16)


def spread_heads(x, out_ref, factor):
    rows = x.shape[0]
    half = rows // 2
    for head in range(QH):
        kh, g = divmod(head, GROUP)
        tile = x[:, (head // 2) * 128 : (head // 2 + 1) * 128].astype(f32)
        if head % 2 != kh:
            tile = pltpu.roll(tile, HD, 1)
        tile = jnp.where(lanes(tile.shape) // HD == kh, tile * factor, 0.0).astype(out_ref.dtype)
        for part in range(2):
            start = (part * GROUP + g) * half
            out_ref[kh, start : start + half, :] = tile[part * half : (part + 1) * half]


def join_heads(src_ref, half, tile):
    sides = []
    for side in range(2):
        kh, g = divmod(2 * tile + side, GROUP)
        parts = [
            src_ref[kh, (part * GROUP + g) * half : (part * GROUP + g + 1) * half, :]
            for part in range(2)
        ]
        both = jnp.concatenate(parts, 0)
        sides.append(both if side == kh else pltpu.roll(both, HD, 1))
    return jnp.where(lanes(sides[0].shape) < HD, sides[0], sides[1])


def forward_kernel(
    ctx, meta_ref, q_ref, mine_ref, other_ref, x_ref, w_ref, gain_ref,
    low_ref, o_ref, lse_ref, spread_ref, k_ref, v_ref, hidden_ref, normed_ref,
    s_ref, max_ref, sum_ref,
):
    rows = q_ref.shape[0]
    half = rows // 2
    part_rows = GROUP * half
    me = meta_ref[0]
    chips = ctx // 2
    for j in range(ctx):
        src = mine_ref if j < chips else other_ref
        at = (j % chips) * rows
        owner = meta_ref[1 + j]
        for part in range(2):
            place = owner if part == 0 else 2 * ctx - 1 - owner
            to = pl.ds(pl.multiple_of(place * half, half), half)
            block = src[at + part * half : at + (part + 1) * half, :]
            k_ref[to, :] = block[:, :WIDTH_K]
            v_ref[to, :] = block[:, WIDTH_K:]
    spread_heads(q_ref[...], spread_ref, HD ** (-0.5))
    for part in range(2):
        span = slice(part * part_rows, (part + 1) * part_rows)
        start = (me if part == 0 else 2 * ctx - 1 - me) * half
        last = start // KEYS

        def keys_of(ref, i):
            return ref[pl.ds(pl.multiple_of(i * KEYS, KEYS), KEYS), :]

        for kh in range(KH):
            scores = dot_nt(spread_ref[kh, span, :], keys_of(k_ref, last))
            row = lax.broadcasted_iota(jnp.int32, scores.shape, 0) % half + start
            scores = jnp.where(lanes(scores.shape) + last * KEYS <= row, scores, -1e30)
            s_ref[kh, last] = scores
            max_ref[kh] = jnp.maximum(scores[:, :128], scores[:, 128:])

        def score(i, carry):
            for kh in range(KH):
                s = dot_nt(spread_ref[kh, span, :], keys_of(k_ref, i))
                s_ref[kh, i] = s
                max_ref[kh] = jnp.maximum(max_ref[kh], jnp.maximum(s[:, :128], s[:, 128:]))
            return carry

        lax.fori_loop(0, last, score, 0)
        for kh in range(KH):
            top = jnp.max(max_ref[kh], -1, keepdims=True)
            max_ref[kh] = jnp.broadcast_to(top, (part_rows, 128))
            sum_ref[kh] = jnp.zeros((part_rows, 128), f32)
            o_ref[kh, span, :] = jnp.zeros((part_rows, 128), f32)

        def weigh(i, carry):
            for kh in range(KH):
                s = s_ref[kh, i]
                top = max_ref[kh]
                left = jnp.exp(s[:, :128] - top)
                right = jnp.exp(s[:, 128:] - top)
                sum_ref[kh] += left + right
                o_ref[kh, span, :] += jnp.dot(
                    jnp.concatenate([left, right], 1).astype(bf16),
                    keys_of(v_ref, i),
                    preferred_element_type=f32,
                )
            return carry

        lax.fori_loop(0, last + 1, weigh, 0)
        for kh in range(KH):
            total = jnp.sum(sum_ref[kh], -1, keepdims=True)
            o_ref[kh, span, :] = o_ref[kh, span, :] / total
            lse_ref[kh, part] = dot_nt(
                jnp.full((8, 128), 1.0 / 128, f32),
                max_ref[kh] + jnp.log(total),
                lax.Precision.HIGHEST,
            )
    for tile in range(WIDTH_Q // 128):
        low_ref[:, tile * 128 : (tile + 1) * 128] = join_heads(o_ref, half, tile).astype(bf16)
    hidden = x_ref[...].astype(f32) + jnp.dot(low_ref[...], w_ref[...], preferred_element_type=f32)
    hidden_ref[...] = hidden
    inverse = lax.rsqrt(jnp.mean(hidden * hidden, -1, keepdims=True) + EPS)
    normed_ref[...] = (hidden * inverse * gain_ref[...]).astype(bf16)


def turn_back(grad, cos_ref, sin_ref):
    scaled = grad * sin_ref[...]
    early = lanes(grad.shape) % HD < HD // 2
    turned = jnp.where(early, pltpu.roll(scaled, 96, 1), -pltpu.roll(scaled, 32, 1))
    return grad * cos_ref[...] + turned


def backward_kernel(
    ctx, meta_ref, gn_ref, hidden_ref, gout_ref, gain_ref, w_ref, spread_ref, k_ref, v_ref, lse_ref,
    o_ref, cos_ref, sin_ref,
    gh_ref, ga_ref, gain_grad_ref, gq_ref, mine_ref, other_ref,
    go_ref, gqs_ref, gk_ref, gv_ref,
):
    rows = gn_ref.shape[0]
    half = rows // 2
    part_rows = GROUP * half
    me = meta_ref[0]
    chips = ctx // 2
    hidden = hidden_ref[...]
    inverse = lax.rsqrt(jnp.mean(hidden * hidden, -1, keepdims=True) + EPS)
    unit = hidden * inverse
    grad = gn_ref[...]
    gain_grad_ref[...] = jnp.sum(grad * unit, 0, keepdims=True)
    scaled = grad * gain_ref[...]
    gh = gout_ref[...].astype(f32) + inverse * (
        scaled - unit * jnp.mean(scaled * unit, -1, keepdims=True)
    )
    gh_ref[...] = gh
    ga = gh.astype(bf16)
    ga_ref[...] = ga
    spread_heads(dot_nt(ga, w_ref[...]).astype(bf16), go_ref, 1.0)
    gqs_ref[...] = jnp.zeros_like(gqs_ref)
    gk_ref[...] = jnp.zeros_like(gk_ref)
    gv_ref[...] = jnp.zeros_like(gv_ref)
    for part in range(2):
        span = slice(part * part_rows, (part + 1) * part_rows)
        start = (me if part == 0 else 2 * ctx - 1 - me) * half
        last = start // KEYS
        deltas = [
            dot_nt(
                jnp.ones((8, 128), f32),
                go_ref[kh, span, :].astype(f32) * o_ref[kh, span, :],
                lax.Precision.HIGHEST,
            )[:1]
            for kh in range(KH)
        ]

        def step(i, masked):
            at = pl.ds(pl.multiple_of(i * KEYS, KEYS), KEYS)
            keys = k_ref[at, :]
            grad_k = gk_ref[at, :]
            grad_v = gv_ref[at, :]
            for kh in range(KH):
                queries = spread_ref[kh, span, :]
                heads = go_ref[kh, span, :]
                p = jnp.exp(dot_nt(keys, queries) - lse_ref[kh, part][:1])
                if masked:
                    row = lanes(p.shape) % half + start
                    key = lax.broadcasted_iota(jnp.int32, p.shape, 0) + i * KEYS
                    p = jnp.where(key <= row, p, 0.0)
                gs = (p * (dot_nt(v_ref[at, :], heads) - deltas[kh])).astype(bf16)
                grad_v += jnp.dot(p.astype(bf16), heads, preferred_element_type=f32)
                grad_k += jnp.dot(gs, queries, preferred_element_type=f32)
                gqs_ref[kh, span, :] += dot_tn(gs, keys)
            gk_ref[at, :] = grad_k
            gv_ref[at, :] = grad_v

        def body(i, carry):
            step(i, False)
            return carry

        lax.fori_loop(0, last, body, 0)
        step(last, True)
    for tile in range(WIDTH_Q // 128):
        grad = join_heads(gqs_ref, half, tile) * HD ** (-0.5)
        gq_ref[:, tile * 128 : (tile + 1) * 128] = turn_back(grad, cos_ref, sin_ref).astype(bf16)
    for j in range(ctx):
        dst = mine_ref if j < chips else other_ref
        at = (j % chips) * rows
        owner = meta_ref[1 + j]
        for part in range(2):
            place = owner if part == 0 else 2 * ctx - 1 - owner
            frm = pl.ds(pl.multiple_of(place * half, half), half)
            to = slice(at + part * half, at + (part + 1) * half)
            dst[to, :WIDTH_K] = gk_ref[frm, :].astype(dst.dtype)
            dst[to, WIDTH_K:] = gv_ref[frm, :].astype(dst.dtype)


SUM_ROWS = 16


def finish_kernel(
    gq_ref, x_ref, gain_ref, w_ref, cos_ref, sin_ref, gh_ref, gain_two_ref, *refs
):
    sent_ref, gx_ref, gain_grad_ref, bias_ref = refs[-4:]
    pair = refs[0][...]
    for ref in refs[1:-4]:
        pair = pair + ref[...].astype(f32)
    rows = pair.shape[0]
    keys = turn_back(pair[:, :WIDTH_K], cos_ref, sin_ref)
    pair = jnp.concatenate([keys, pair[:, WIDTH_K:]], 1).astype(bf16)
    sent_ref[:rows, :] = pair
    joint = jnp.concatenate([gq_ref[...], pair], 1)
    bias = jnp.sum(joint.astype(f32), 0, keepdims=True)
    bias_ref[...] = bias
    grad = dot_nt(joint, w_ref[...])
    x = x_ref[...].astype(f32)
    inverse = lax.rsqrt(jnp.mean(x * x, -1, keepdims=True) + EPS)
    unit = x * inverse
    gain = jnp.sum(grad * unit, 0, keepdims=True)
    gain_grad_ref[...] = gain
    scaled = grad * gain_ref[...]
    gx_ref[...] = gh_ref[...] + inverse * (
        scaled - unit * jnp.mean(scaled * unit, -1, keepdims=True)
    )
    sums = jnp.concatenate([gain, gain_two_ref[...], bias], 1)
    width = pair.shape[1]
    sums = jnp.concatenate([sums, jnp.zeros((1, -sums.shape[1] % width), f32)], 1)
    found = [sums[:, i : i + width] for i in range(0, sums.shape[1], width)]
    found += [jnp.zeros((1, width), f32)] * (SUM_ROWS - len(found))
    sums = jnp.concatenate(found, 0)
    high = sums.astype(bf16)
    sent_ref[rows : rows + SUM_ROWS, :] = high
    sent_ref[rows + SUM_ROWS :, :] = (sums - high.astype(f32)).astype(bf16)


def pair_grad_kernel(rows, half_width, meta_ref, norm_ref, own_ref, peer_ref, out_ref, turned_ref):
    turned_ref[...] = norm_ref[:, D:].T
    first = pl.multiple_of(meta_ref[0] * half_width, 16)
    both = jnp.concatenate([own_ref[:rows, :], peer_ref[:rows, :]], 0)
    part = jnp.dot(turned_ref[pl.ds(first, half_width), :], both, preferred_element_type=f32)
    out_ref[:half_width, :] = part.astype(bf16)

    def sums(ref):
        high = ref[rows : rows + SUM_ROWS, :].astype(f32)
        return high + ref[rows + SUM_ROWS :, :].astype(f32)

    out_ref[half_width:, :] = (sums(own_ref) + sums(peer_ref)).astype(bf16)


def mlp_kernel(
    half_rows, spots_ref, x_a, x_b, gy_a, gy_b, gate_a, gate_b, up_a, up_b, down_a, down_b,
    xt_ref, midt_ref, gg_ref, gu_ref, gx_ref, out_ref, send_ref,
    x_all, gy_all, wg_all, wu_all, wd_all, mid_all, gg_all, gu_all,
):
    step = pl.program_id(0)

    @pl.when(step == 0)
    def start():
        x_all[:half_rows] = x_a[...]
        x_all[half_rows:] = x_b[...]
        gy_all[:half_rows] = gy_a[...]
        gy_all[half_rows:] = gy_b[...]
        xt_ref[...] = x_all[...].T

    here = pl.ds(pl.multiple_of(step * 256, 256), 256)
    wg = jnp.concatenate([gate_a[...], gate_b[...]], 1)
    wu = jnp.concatenate([up_a[...], up_b[...]], 1)
    wd = jnp.concatenate([down_a[...], down_b[...]], 0)
    wg_all[:, here] = wg
    wu_all[:, here] = wu
    wd_all[here, :] = wd
    core = spots_ref[1]
    column = lanes((1, 256)) + (step * 256 + spots_ref[2])
    own = (column < spots_ref[3]) == (core == 0)
    x = x_all[...]
    gate = jnp.dot(x, wg, preferred_element_type=f32)
    up = jnp.dot(x, wu, preferred_element_type=f32)
    grad = jnp.where(own, dot_nt(gy_all[...], wd), 0.0)
    sigma = jax.nn.sigmoid(gate)
    active = gate * sigma
    middle = jnp.where(own, active * up, 0.0).astype(bf16)
    grad_gate = (grad * up * (sigma + active * (1.0 - sigma))).astype(bf16)
    grad_up = (grad * active).astype(bf16)
    midt_ref[...] = middle.T
    gg_ref[...] = grad_gate
    gu_ref[...] = grad_up
    mid_all[:, here] = middle
    gg_all[:, here] = grad_gate
    gu_all[:, here] = grad_up

    @pl.when(step == pl.num_programs(0) - 1)
    def end():
        gx = dot_nt(gg_all[...], wg_all[...]) + dot_nt(gu_all[...], wu_all[...])
        gx_ref[...] = gx[:half_rows]
        send_ref[:half_rows] = gx[half_rows:].astype(bf16)
        out = jnp.dot(mid_all[...], wd_all[...], preferred_element_type=f32)
        out_ref[...] = out[:half_rows]
        send_ref[half_rows:] = out[half_rows:].astype(bf16)


def feed_forward(meta, x, early, w_gate, w_up, w_down, width):
    half = x[0].shape[0]
    tokens = 2 * half
    steps = width // 256
    tiles = width // 128 - 1

    def columns(j):
        return pl.BlockSpec((D, 128), lambda i, m: (0, m[1] * tiles + 2 * i + j))

    def rows(j):
        return pl.BlockSpec((128, D), lambda i, m: (m[1] * tiles + 2 * i + j, 0))

    whole = pl.BlockSpec((tokens, D), lambda i, m: (0, 0))
    halves = pl.BlockSpec((half, D), lambda i, m: (0, 0))
    tile = pl.BlockSpec((tokens, 256), lambda i, m: (0, i))
    hidden = jax.ShapeDtypeStruct((tokens, width), bf16)
    return pl.pallas_call(
        lambda *refs: mlp_kernel(half, *refs),
        out_shape=[
            jax.ShapeDtypeStruct((D, tokens), bf16),
            jax.ShapeDtypeStruct((width, tokens), bf16),
            hidden,
            hidden,
            jax.ShapeDtypeStruct((half, D), f32),
            jax.ShapeDtypeStruct((half, D), f32),
            jax.ShapeDtypeStruct((tokens, D), bf16),
        ],
        grid_spec=pltpu.PrefetchScalarGridSpec(
            num_scalar_prefetch=1,
            grid=(steps,),
            in_specs=[halves] * 4
            + [columns(0), columns(1), columns(0), columns(1), rows(0), rows(1)],
            out_specs=[
                pl.BlockSpec((D, tokens), lambda i, m: (0, 0)),
                pl.BlockSpec((256, tokens), lambda i, m: (i, 0)),
                tile,
                tile,
                halves,
                halves,
                whole,
            ],
            scratch_shapes=[pltpu.VMEM((tokens, D), bf16)] * 2
            + [pltpu.VMEM((D, width), bf16)] * 2
            + [pltpu.VMEM((width, D), bf16)]
            + [pltpu.VMEM((tokens, width), bf16)] * 3,
        ),
        compiler_params=pltpu.CompilerParams(vmem_limit_bytes=VMEM_BYTES),
        cost_estimate=pl.CostEstimate(
            flops=12 * tokens * width * D, bytes_accessed=6 * width * D, transcendentals=0
        ),
    )(meta, *x, *early, w_gate, w_gate, w_up, w_up, w_down, w_down)


def mlp_grad_kernel(chips, down_rows, main, meta_ref, xt_ref, gy_a, gy_b, midt_ref, gg_ref, gu_ref, *refs):
    out_refs = refs[:chips]
    mlp_acc, down_acc, blocks, sems = refs[chips:]
    core = meta_ref[1]
    at_main = pl.ds(pl.multiple_of(core * 128, 128), main)
    at_tile = pl.ds(pl.multiple_of((1 - core) * main, 128), 128)
    xt = xt_ref[...]
    mlp_acc[:, :main] = jnp.dot(xt, gg_ref[:, at_main], preferred_element_type=f32).astype(bf16)
    mlp_acc[:, main : 2 * main] = jnp.dot(
        xt, gu_ref[:, at_main], preferred_element_type=f32
    ).astype(bf16)
    mixed = gg_ref[:, at_tile].astype(f32) + pltpu.roll(gu_ref[:, at_tile].astype(f32), 64, 1)
    mlp_acc[:, 2 * main :] = jnp.dot(
        xt, mixed.astype(bf16), preferred_element_type=f32
    ).astype(bf16)
    gy = jnp.concatenate([gy_a[:, :D], gy_b[:, :D]], 0)
    down_acc[...] = jnp.dot(midt_ref[...], gy, preferred_element_type=f32)

    mlp_rows = mlp_acc.shape[0] // chips
    columns = mlp_acc.shape[1] // 128
    half = chips // 2
    copies = []
    for slot in sorted(range(chips), key=lambda s: abs(s - half) if s else chips):
        owner = meta_ref[12 + slot]
        block = mlp_acc[pl.ds(pl.multiple_of(owner * mlp_rows, 16), mlp_rows), :]
        for j in range(columns):
            for i in range(mlp_rows // 16):
                blocks[slot, j * 16 : (j + 1) * 16, i * 128 : (i + 1) * 128] = block[
                    i * 16 : (i + 1) * 16, j * 128 : (j + 1) * 128
                ]
        first = pl.multiple_of(core * 64 + owner * down_rows, 8)
        blocks[slot, columns * 16 :, :] = down_acc[pl.ds(first, down_rows), :].astype(bf16)
        copy = pltpu.make_async_copy(blocks.at[slot], out_refs[slot], sems.at[slot])
        copy.start()
        copies.append(copy)
    for copy in copies:
        copy.wait()


def mlp_gradients(meta, xt, early, midt, gg, gu, after, chips, down_rows, main):
    tokens = gg.shape[0]
    columns = (2 * main + 128) // 128
    rows = columns * 16 + down_rows
    args = [meta, xt, *early, midt, gg, gu]
    anywhere = pl.BlockSpec(memory_space=pl.ANY)

    def kernel(*refs):
        mlp_grad_kernel(chips, down_rows, main, *refs[: len(args)], *refs[len(args) + 1 :])

    return pl.pallas_call(
        kernel,
        out_shape=[jax.ShapeDtypeStruct((rows, D), bf16)] * chips,
        in_specs=[pl.BlockSpec(memory_space=pltpu.SMEM)]
        + [pl.BlockSpec(memory_space=pltpu.VMEM)] * (len(args) - 1)
        + [anywhere],
        out_specs=[anywhere] * chips,
        scratch_shapes=[
            pltpu.VMEM((D, columns * 128), bf16),
            pltpu.VMEM((midt.shape[0], D), f32),
            pltpu.VMEM((chips, rows, D), bf16),
            pltpu.SemaphoreType.DMA((chips,)),
        ],
        compiler_params=pltpu.CompilerParams(vmem_limit_bytes=VMEM_BYTES),
        cost_estimate=pl.CostEstimate(
            flops=6 * tokens * midt.shape[0] * D, bytes_accessed=4 * chips * rows * D,
            transcendentals=0,
        ),
    )(*args, after)


def small_grad_kernel(
    chips, q_rows, rows, cols, meta_ref, norm_a, norm_b, near_a, near_b, *refs
):
    out_refs, acc, turned_ref = refs[:-2], refs[-2], refs[-1]
    first = pl.multiple_of((2 * meta_ref[0] + meta_ref[1]) * q_rows, 16)
    grads, queries, attended = [], [], []
    for near_ref in (near_a, near_b):
        for b in range(2):
            for i, found in enumerate((grads, queries, attended)):
                found.append(near_ref[(3 * b + i) * rows : (3 * b + i + 1) * rows, :])
    turned_ref[...] = jnp.concatenate([norm_a[:, D:], norm_b[:, D:]], 0).T
    acc[:, :WIDTH_Q] = jnp.dot(
        turned_ref[pl.ds(first, q_rows), :],
        jnp.concatenate(queries, 0),
        preferred_element_type=f32,
    ).astype(bf16)
    acc[:, WIDTH_Q:cols] = jnp.zeros((q_rows, cols - WIDTH_Q), bf16)
    turned_ref[...] = jnp.concatenate(attended, 0).T
    acc[:, cols:] = jnp.dot(
        turned_ref[pl.ds(first, q_rows), :], jnp.concatenate(grads, 0), preferred_element_type=f32
    ).astype(bf16)
    width = acc.shape[1] // chips
    for out_ref, slot in zip(out_refs, range(chips)):
        owner = meta_ref[12 + slot]
        block = acc[:, pl.ds(pl.multiple_of(owner * width, 128), width)]
        tall = jnp.concatenate([block[:, i * 128 : (i + 1) * 128] for i in range(width // 128)], 0)
        piece = out_ref.shape[0]
        for i in range(D // 128):
            out_ref[:, i * 128 : (i + 1) * 128] = tall[i * piece : (i + 1) * piece]


def place_all(meta, slots, pairs, old, sizes, rest=None):
    main, ff_loc, q_rows, cols, down_rows, chips = sizes
    mlp_rows = D // chips
    columns = (2 * main + 128) // 128
    tiles = main // 128
    lanes_out = D // 128
    top = columns * 16
    blocks = [x for pair in pairs for x in pair]
    count = len(blocks)
    piece = blocks[0].shape[0] - top - down_rows
    parts = (cols + D) // chips // 128
    keep = [] if old is None else list(old)
    last = [] if rest is None else list(rest)
    known = WIDTH_Q // 128

    def kernel(meta_ref, *refs):
        ins = refs[:count]
        outs_at = count + len(last) + len(keep)
        gate_out, up_out, down_out, joint_out, proj_out, token_ref = refs[outs_at : outs_at + 6]
        gate_buf, up_buf, down_buf, small_buf, rest_buf, sems, small_sems, rest_sem = refs[
            outs_at + 6 :
        ]
        core_zero = meta_ref[1] == 0
        copies = []

        def send(src, dst, sem):
            copy = pltpu.make_async_copy(src, dst, sem)
            copy.start()
            copies.append(copy)

        def column(ref, j):
            found = [
                ref[j * 16 : (j + 1) * 16, i * 128 : (i + 1) * 128] for i in range(mlp_rows // 16)
            ]
            return jnp.concatenate(found, 0).astype(f32)

        for k, slot in enumerate(slots):
            for j in range(columns):
                got = column(ins[2 * k], j)
                other = column(ins[2 * k + 1], j)
                zero = jnp.where(core_zero, got, other)
                one = jnp.where(core_zero, other, got)
                if j < 2 * tiles:
                    buf = gate_buf if j < tiles else up_buf
                    at = (j % tiles) * 128
                    buf[k, :, at : at + 128] = zero
                    buf[k, :, at + main + 128 : at + main + 256] = one
                else:
                    left = lanes(zero.shape) < 64
                    gate_buf[k, :, main : main + 128] = jnp.where(left, zero, one)
                    up_buf[k, :, main : main + 128] = pltpu.roll(jnp.where(left, one, zero), 64, 1)
            owner = meta_ref[12 + slot]
            here = pl.ds(pl.multiple_of(owner * mlp_rows, 8), mlp_rows)
            send(gate_buf.at[k], gate_out.at[here, :], sems.at[4 * k])
            send(up_buf.at[k], up_out.at[here, :], sems.at[4 * k + 1])
            for side in range(2):
                b = 2 * k + side
                core = meta_ref[1] if side == 0 else 1 - meta_ref[1]
                down_buf[b] = ins[b][top + piece :, :].astype(f32)
                here = pl.ds(pl.multiple_of((core * chips + owner) * down_rows, 8), down_rows)
                send(down_buf.at[b], down_out.at[here, :], sems.at[4 * k + 2 + side])
                tall = jnp.concatenate(
                    [ins[b][top : top + piece, i * 128 : (i + 1) * 128] for i in range(lanes_out)], 0
                ).astype(f32)
                rows = pl.ds(pl.multiple_of(core * q_rows, 8), q_rows)
                for i in range(parts):
                    small_buf[b, i] = tall[i * q_rows : (i + 1) * q_rows]
                    block = owner * parts + i

                    @pl.when(block < known)
                    def joint(b=b, i=i, rows=rows, block=block):
                        at = pl.ds(pl.multiple_of(block * 128, 128), 128)
                        pltpu.make_async_copy(
                            small_buf.at[b, i], joint_out.at[rows, at], small_sems.at[b, i]
                        ).start()

                    @pl.when(block >= cols // 128)
                    def proj(b=b, i=i, rows=rows, block=block):
                        at = pl.ds(pl.multiple_of((block - cols // 128) * 128, 128), 128)
                        pltpu.make_async_copy(
                            small_buf.at[b, i], proj_out.at[rows, at], small_sems.at[b, i]
                        ).start()

        token_ref[...] = jnp.zeros(token_ref.shape, f32)
        if last:
            rows = last[0].shape[0]
            for core, ref in ((meta_ref[1], refs[count]), (1 - meta_ref[1], refs[count + 1])):
                rest_buf[pl.ds(pl.multiple_of(core * rows, 8), rows), :] = ref[...].astype(f32)
            send(rest_buf.at[: 2 * q_rows, :], joint_out.at[:, WIDTH_Q:cols], rest_sem)
        for copy in copies:
            copy.wait()
        for b in range(count):
            for i in range(parts):
                block = meta_ref[12 + slots[b // 2]] * parts + i

                @pl.when((block < known) | (block >= cols // 128))
                def done(b=b, i=i):
                    pltpu.make_async_copy(
                        small_buf.at[b, i],
                        proj_out.at[pl.ds(0, q_rows), pl.ds(0, 128)],
                        small_sems.at[b, i],
                    ).wait()

    anywhere = pl.BlockSpec(memory_space=pl.ANY)
    result = pl.pallas_call(
        kernel,
        out_shape=[
            jax.ShapeDtypeStruct((D, ff_loc), f32),
            jax.ShapeDtypeStruct((D, ff_loc), f32),
            jax.ShapeDtypeStruct((ff_loc, D), f32),
            jax.ShapeDtypeStruct((2 * q_rows, cols), f32),
            jax.ShapeDtypeStruct((2 * q_rows, D), f32),
            jax.ShapeDtypeStruct((8, 128), f32),
        ],
        in_specs=[pl.BlockSpec(memory_space=pltpu.SMEM)]
        + [pl.BlockSpec(memory_space=pltpu.VMEM)] * (count + len(last))
        + [anywhere] * len(keep),
        out_specs=[anywhere] * 5 + [pl.BlockSpec(memory_space=pltpu.VMEM)],
        scratch_shapes=[
            pltpu.VMEM((len(slots), mlp_rows, ff_loc), f32),
            pltpu.VMEM((len(slots), mlp_rows, ff_loc), f32),
            pltpu.VMEM((count, down_rows, D), f32),
            pltpu.VMEM((count, parts, q_rows, 128), f32),
            pltpu.VMEM((2 * q_rows + SUM_ROWS, cols - WIDTH_Q), f32),
            pltpu.SemaphoreType.DMA((4 * len(slots),)),
            pltpu.SemaphoreType.DMA((count, parts)),
            pltpu.SemaphoreType.DMA,
        ],
        input_output_aliases={1 + count + len(last) + i: i for i in range(len(keep))},
        compiler_params=pltpu.CompilerParams(vmem_limit_bytes=VMEM_BYTES),
        cost_estimate=pl.CostEstimate(
            flops=0, bytes_accessed=8 * sum(x.size for x in blocks), transcendentals=0
        ),
    )(meta, *blocks, *last, *keep)
    return list(result[:5]), result[5]


def place_blocks(blocks, spots, out_shape, old=None):
    shape = blocks[0].shape
    count = len(blocks)
    if shape[0] % 8 or shape[1] % 128:
        out = jnp.zeros(out_shape, f32) if old is None else old
        for block, (i, j) in zip(blocks, spots):
            out = lax.dynamic_update_slice(
                out, block.astype(f32), (i * shape[0], j * shape[1])
            )
        return out

    def kernel(spots_ref, *refs):
        step = pl.program_id(0)
        out_ref = refs[-1]
        for i in range(count):

            @pl.when(step == i)
            def write(i=i):
                out_ref[...] = refs[i][...].astype(f32)

    keep = [] if old is None else [old]
    return pl.pallas_call(
        kernel,
        out_shape=jax.ShapeDtypeStruct(out_shape, f32),
        grid_spec=pltpu.PrefetchScalarGridSpec(
            num_scalar_prefetch=1,
            grid=(count,),
            in_specs=[pl.BlockSpec(shape, lambda i, spots: (0, 0))] * count
            + [pl.BlockSpec(memory_space=pl.ANY)] * len(keep),
            out_specs=pl.BlockSpec(shape, lambda i, spots: (spots[i, 0], spots[i, 1])),
        ),
        input_output_aliases={} if old is None else {count + 1: 0},
        compiler_params=pltpu.CompilerParams(vmem_limit_bytes=VMEM_BYTES),
    )(jnp.stack([jnp.stack(s) for s in spots]).astype(jnp.int32), *blocks, *keep)


def local(tokens, w_qkv, b_qkv, w_out, gain_attn, gain_mlp, w_gate, w_up, w_down, cotangent):
    net = Net()
    rows = tokens.shape[1]
    half_rows = rows // 2
    ctx_count = net.ctx
    core = net.core
    chips = net.chips
    part_rows = GROUP * half_rows
    x = tokens[0]
    gain_one = gain_attn[None]
    gain_two = gain_mlp[None]

    w_qkv_full = net.full_rows(w_qkv)

    ff_loc = w_gate.shape[1]
    ff_half = ff_loc // 2
    main = (ff_half // 128) * 128
    rest = ff_half - main
    width = main + 2 * rest
    first = core * main
    tiled = net.dp == 2 and 2 * rest == 128 and width % 256 == 0 and chips == 8 and ff_half == chips * RING_ROWS
    ring = jnp.arange(chips, dtype=jnp.int32)
    owners_of = (net.pos - ring) % chips
    spots = jnp.concatenate(
        [jnp.stack([net.d, core, first, jnp.int32(ff_half)]), owners_of, owners_of]
    ).astype(jnp.int32)

    row_ids = jnp.arange(half_rows, dtype=jnp.int32)
    place = jnp.concatenate(
        [net.c * half_rows + row_ids, (2 * ctx_count - 1 - net.c) * half_rows + row_ids]
    )
    freq = ROPE_BASE ** (-((jnp.arange(128) % (HD // 2)).astype(f32) * (2.0 / HD)))
    angle = place.astype(f32)[:, None] * freq[None, :]
    cosine, sine = jnp.cos(angle), jnp.sin(angle)
    normed_one, queries, pairs = call(
        qkv_kernel,
        [
            jax.ShapeDtypeStruct((rows, D), bf16),
            jax.ShapeDtypeStruct((rows, WIDTH_Q), bf16),
            jax.ShapeDtypeStruct((rows, 2 * WIDTH_K), bf16),
        ],
        [x, gain_one, w_qkv_full, b_qkv[None], cosine, sine],
        flops=2 * rows * D * 1152,
    )

    slots = net.ring_gather(pairs)
    mine = jnp.concatenate(slots, 0)
    other = net.swap(mine)
    order = jnp.array(net.order, jnp.int32)
    chip_ids = order[(net.pos - jnp.arange(chips, dtype=jnp.int32)) % chips]
    meta = jnp.concatenate([net.c[None], 2 * chip_ids + core, 2 * chip_ids + 1 - core])
    meta = meta.astype(jnp.int32)

    late_w, late_g, late_n, unused = lax.optimization_barrier((w_out, cotangent[0], normed_one, pairs))
    w_out_full = net.full_rows(late_w)
    early = net.group_parts(jnp.concatenate([late_g, late_n], 1))

    total_keys = rows * ctx_count
    padded = (KH, 2 * part_rows, 128)
    attended_low, attended, lse, spread, keys, values, hidden, normed_two = call(
        lambda *refs: forward_kernel(ctx_count, *refs),
        [
            jax.ShapeDtypeStruct((rows, WIDTH_Q), bf16),
            jax.ShapeDtypeStruct(padded, f32),
            jax.ShapeDtypeStruct((KH, 2, 8, part_rows), f32),
            jax.ShapeDtypeStruct(padded, bf16),
            jax.ShapeDtypeStruct((total_keys, WIDTH_K), bf16),
            jax.ShapeDtypeStruct((total_keys, WIDTH_K), bf16),
            jax.ShapeDtypeStruct((rows, D), f32),
            jax.ShapeDtypeStruct((rows, D), bf16),
        ],
        [meta, queries, mine, other, x, w_out_full, gain_two],
        smem=1,
        scratch=[
            pltpu.VMEM((KH, total_keys // KEYS, part_rows, KEYS), f32),
            pltpu.VMEM((KH, part_rows, 128), f32),
            pltpu.VMEM((KH, part_rows, 128), f32),
        ],
        flops=8 * KH * part_rows * total_keys * 128,
    )

    normed_two_parts = net.group_parts(normed_two)
    chip_rows = net.dp * rows
    down_rows = ff_half // chips
    mlp_rows = D // chips
    if tiled:
        x_turned, mid_turned, gate_low, up_low, grad_mine, out_mine, sent = feed_forward(
            spots, normed_two_parts, early, w_gate, w_up, w_down, width
        )
    else:
        normed_two_group = jnp.concatenate(normed_two_parts, 0)
        grad_out_group = jnp.concatenate(early, 0)[:, :D]
        own_cols = (jnp.arange(width) + first < ff_half) == (core == 0)
        wg = lax.dynamic_slice(w_gate, (0, first), (D, width))
        wu = lax.dynamic_slice(w_up, (0, first), (D, width))
        wd = lax.dynamic_slice(w_down, (first, 0), (width, D))
        gate = jnp.dot(normed_two_group, wg, preferred_element_type=f32)
        upper = jnp.dot(normed_two_group, wu, preferred_element_type=f32)
        sigma = jax.nn.sigmoid(gate)
        activated = gate * sigma
        middle = jnp.where(own_cols, activated * upper, 0.0).astype(bf16)
        grad_middle = jnp.einsum("td,fd->tf", grad_out_group, wd, preferred_element_type=f32)
        slope = sigma * (1.0 + gate * (1.0 - sigma))
        grad_gate_low = jnp.where(own_cols, grad_middle * upper * slope, 0.0).astype(bf16)
        grad_up_low = jnp.where(own_cols, grad_middle * activated, 0.0).astype(bf16)

        grad_normed_two = jnp.einsum(
            "tf,df->td", grad_gate_low, wg, preferred_element_type=f32
        ) + jnp.einsum("tf,df->td", grad_up_low, wu, preferred_element_type=f32)
        mlp_out = jnp.dot(middle, wd, preferred_element_type=f32)
        grad_mine, out_mine = grad_normed_two[:chip_rows], mlp_out[:chip_rows]
        sent = jnp.concatenate([grad_normed_two[chip_rows:], mlp_out[chip_rows:]], 0).astype(bf16)
    swapped = net.swap(sent)
    grad_chip = grad_mine + swapped[:chip_rows].astype(f32)
    mlp_chip = out_mine + swapped[chip_rows:].astype(f32)
    grad_two = grad_chip[:rows]
    for s in range(1, net.dp):
        sent_two = grad_chip[s * rows : (s + 1) * rows].astype(bf16)
        grad_two = grad_two + net.shift(sent_two, net.dp - s).astype(f32)

    def attention_back(*after):
        grad_hidden, grad_attn_low, grad_gain_two, grad_queries, terms_mine, terms_other = call(
            lambda *refs: backward_kernel(ctx_count, *refs),
            [
                jax.ShapeDtypeStruct((rows, D), f32),
                jax.ShapeDtypeStruct((rows, D), bf16),
                jax.ShapeDtypeStruct((1, D), f32),
                jax.ShapeDtypeStruct((rows, WIDTH_Q), bf16),
                jax.ShapeDtypeStruct((chips * rows, 2 * WIDTH_K), f32),
                jax.ShapeDtypeStruct((chips * rows, 2 * WIDTH_K), bf16),
            ],
            [
                meta, grad_two, hidden, cotangent[0], gain_two, w_out_full, spread, keys, values, lse,
                attended, cosine, sine, *after,
            ],
            smem=1,
            loose=len(after),
            scratch=[
                pltpu.VMEM(padded, bf16),
                pltpu.VMEM(padded, f32),
                pltpu.VMEM((total_keys, WIDTH_K), f32),
                pltpu.VMEM((total_keys, WIDTH_K), f32),
            ],
            flops=20 * KH * part_rows * total_keys * 128,
        )
        other_terms = net.swap(terms_other)

        def row_sums(*after):
            pair_sums = call(
                pair_kernel,
                [jax.ShapeDtypeStruct((rows, 2 * WIDTH_K), f32)]
                + [jax.ShapeDtypeStruct((rows, 2 * WIDTH_K), bf16)] * (chips - 1),
                [terms_mine, other_terms, *after],
                loose=len(after),
            )
            return net.ring_parts(pair_sums)

        def finish(grad_pairs):
            return call(
                finish_kernel,
                [
                    jax.ShapeDtypeStruct((rows + 2 * SUM_ROWS, 2 * WIDTH_K), bf16),
                    jax.ShapeDtypeStruct((rows, D), f32),
                    jax.ShapeDtypeStruct((1, D), f32),
                    jax.ShapeDtypeStruct((1, w_qkv.shape[1]), f32),
                ],
                [grad_queries, x, gain_one, w_qkv_full, cosine, sine, grad_hidden, grad_gain_two]
                + grad_pairs,
            )

        return grad_attn_low, grad_gain_two, grad_queries, row_sums, finish

    if tiled:
        terms = mlp_gradients(
            spots, x_turned, early, mid_turned, gate_low, up_low, sent_two, chips, down_rows, main
        )
        grad_attn_low, grad_gain_two, grad_queries, row_sums, finish = attention_back(terms[0])
        found = []

        def between(*blocks):
            found.extend(row_sums(*blocks))
            return found[1]

        fwd, back = net.ring_sum(terms, between)
        grad_pairs, marks = found
        sum_mlp, sum_down = ring_end(fwd, back, terms[0], terms[0].shape[0] - down_rows)
    else:
        part_down = jnp.einsum(
            "tf,td->fd", middle, grad_out_group, preferred_element_type=f32
        ).astype(bf16)
        part_down = lax.dynamic_slice(part_down, (core * rest, 0), (ff_half, D))

        def down_chunk(slot):
            return lax.dynamic_slice(part_down, (net.owner(slot) * down_rows, 0), (down_rows, D))

        sum_down = net.ring_scatter([down_chunk(s) for s in range(chips)]).astype(bf16)

        def split_main(x):
            left = (x[:, :main], x[:, main:])
            right = (x[:, 2 * rest :], x[:, : 2 * rest])
            return (
                jnp.where(core == 0, left[0], right[0]),
                jnp.where(core == 0, left[1], right[1]),
            )

        gate_main, gate_tile = split_main(grad_gate_low)
        up_main, up_tile = split_main(grad_up_low)
        packed = jnp.concatenate(
            [gate_main, up_main, gate_tile + jnp.roll(up_tile, rest, 1)], 1
        )
        part_mlp = jnp.einsum(
            "td,tf->df", normed_two_group, packed, preferred_element_type=f32
        ).astype(bf16)

        def mlp_chunk(slot):
            return lax.dynamic_slice(
                part_mlp, (net.owner(slot) * mlp_rows, 0), (mlp_rows, 2 * ff_half)
            )

        sum_mlp = net.ring_scatter([mlp_chunk(s) for s in range(chips)]).astype(bf16)
        sum_mlp = lax.optimization_barrier(sum_mlp)
        grad_attn_low, grad_gain_two, grad_queries, row_sums, finish = attention_back()
        grad_pairs, marks = row_sums()
    pair_sent, grad_input, grad_gain_one, grad_bias = finish(grad_pairs)

    out_sum = mlp_chip[:rows]
    for s in range(1, net.dp):
        got = net.shift(mlp_chip[s * rows : (s + 1) * rows].astype(bf16), net.dp - s)
        out_sum = out_sum + got.astype(f32)
    output = (hidden + out_sum).astype(bf16)
    near = net.group_parts(jnp.concatenate([grad_attn_low, grad_queries, attended_low], 0))

    q_rows = w_qkv.shape[0] // 2
    qkv_cols = w_qkv.shape[1]
    if tiled:
        piece = q_rows * (qkv_cols + D) // chips // D
        terms_small = call(
            lambda *refs: small_grad_kernel(chips, q_rows, rows, qkv_cols, *refs),
            [jax.ShapeDtypeStruct((piece, D), bf16)] * chips,
            [spots, *early, *near],
            smem=1,
            scratch=[
                pltpu.VMEM((q_rows, qkv_cols + D), bf16),
                pltpu.VMEM((D, 2 * chip_rows), bf16),
            ],
            flops=4 * chip_rows * D * (qkv_cols + D),
        )
        block = call(
            block_kernel,
            [jax.ShapeDtypeStruct((sum_mlp.shape[0] + piece + down_rows, D), bf16)],
            [sum_mlp, sum_down] + net.ring_parts(terms_small)[0] + list(marks[3]),
            loose=2,
        )[0]
        part_pair = call(
            lambda *refs: pair_grad_kernel(rows, 2 * q_rows, *refs),
            [jax.ShapeDtypeStruct((2 * q_rows + SUM_ROWS, 2 * WIDTH_K), bf16)],
            [spots, early[0], pair_sent, net.shift(pair_sent, 1)],
            smem=1,
            scratch=[pltpu.VMEM((D, chip_rows), bf16)],
        )[0]
        sizes = (main, ff_loc, q_rows, qkv_cols, down_rows, chips)
        placed, pair_halves = net.gather_placed(
            block,
            lambda slots, pairs, old, rest=None: place_all(spots, slots, pairs, old, sizes, rest),
            net.exchange_start(part_pair),
            [[part_pair], [], []],
        )
        grad_gate, grad_up, grad_down, grad_joint, grad_out_proj = placed
        sums = jnp.where(core == 1, *pair_halves)[-SUM_ROWS:]
        small = sums.reshape(-1)[: 2 * D + qkv_cols].astype(f32)
    else:
        gathered = jnp.concatenate(near, 0).reshape(2 * net.dp, 3, rows, D)
        grad_attn_group = gathered[:, 0].reshape(2 * net.dp * rows, D)
        attended_group = gathered[:, 2].reshape(2 * net.dp * rows, D)
        normed_one_group = jnp.concatenate(early, 0)[:, D:]
        joint_group = net.group_gather(jnp.concatenate([grad_queries, pair_sent[:rows]], 1))
        q_first = net.d * (2 * q_rows) + core * q_rows
        group_rows = 2 * net.dp * rows
        part_out = jnp.einsum(
            "tc,td->cd",
            lax.dynamic_slice(attended_group, (0, q_first), (group_rows, q_rows)),
            grad_attn_group,
            preferred_element_type=f32,
        )
        part_joint = jnp.einsum(
            "td,tc->dc",
            lax.dynamic_slice(normed_one_group, (0, q_first), (group_rows, q_rows)),
            joint_group,
            preferred_element_type=f32,
        )
        part_small = jnp.concatenate([part_joint, part_out], 1).astype(bf16)
        small_cols = part_small.shape[1] // chips

        def small_chunk(slot):
            return lax.dynamic_slice(part_small, (0, net.owner(slot) * small_cols), (q_rows, small_cols))

        sum_small = net.ring_scatter([small_chunk(s) for s in range(chips)]).astype(bf16)

        tall = jnp.concatenate(
            [sum_small[:, i * 128 : (i + 1) * 128] for i in range(small_cols // 128)], 0
        )
        piece = tall.shape[0] // (D // 128)
        wide = jnp.concatenate([tall[i * piece : (i + 1) * piece] for i in range(D // 128)], 1)
        both = lax.optimization_barrier(jnp.concatenate([sum_down, wide], 0))

        owners = [net.owner(s) for s in range(chips)]
        got_mlp = net.ring_gather(sum_mlp)
        got_both = net.ring_gather(both)
        pairs_mlp = [(got, net.swap(got)) for got in got_mlp]
        pairs_both = [(got, net.swap(got)) for got in got_both]

        down_blocks, down_spots, small_blocks, small_spots = [], [], [], []
        for owner, pair in zip(owners, pairs_both):
            for which, got in zip((core, 1 - core), pair):
                down_blocks.append(got[:down_rows])
                down_spots.append((which * chips + owner, jnp.int32(0)))
                wide = got[down_rows:]
                tall = jnp.concatenate([wide[:, i * 128 : (i + 1) * 128] for i in range(D // 128)], 0)
                small_blocks.append(
                    jnp.concatenate(
                        [tall[i * q_rows : (i + 1) * q_rows] for i in range(small_cols // 128)], 1
                    )
                )
                small_spots.append((which, owner))
        grad_down = place_blocks(down_blocks, down_spots, (ff_loc, D))
        grad_small = place_blocks(small_blocks, small_spots, (2 * q_rows, part_small.shape[1]))
        grad_gate = jnp.zeros((D, ff_loc), f32)
        grad_up = jnp.zeros((D, ff_loc), f32)
        left_lane = jnp.arange(2 * rest) < rest
        for owner, (got, swapped) in zip(owners, pairs_mlp):
            zero = jnp.where(core == 0, got, swapped).astype(f32)
            one = jnp.where(core == 0, swapped, got).astype(f32)
            tile_zero, tile_one = zero[:, 2 * main :], one[:, 2 * main :]
            mid_gate = jnp.where(left_lane, tile_zero, tile_one)
            mid_up = jnp.roll(jnp.where(left_lane, tile_one, tile_zero), rest, 1)
            base = owner * mlp_rows
            grad_gate = lax.dynamic_update_slice(
                grad_gate, jnp.concatenate([zero[:, :main], mid_gate, one[:, :main]], 1), (base, 0)
            )
            grad_up = lax.dynamic_update_slice(
                grad_up,
                jnp.concatenate([zero[:, main : 2 * main], mid_up, one[:, main : 2 * main]], 1),
                (base, 0),
            )

        grad_joint, grad_out_proj = grad_small[:, :qkv_cols], grad_small[:, qkv_cols:]
        small = net.total(jnp.concatenate([grad_gain_one, grad_gain_two, grad_bias], 1))[0]
    return (
        output[None],
        grad_input[None],
        grad_joint,
        small[2 * D :],
        grad_out_proj,
        small[:D],
        small[D : 2 * D],
        grad_gate,
        grad_up,
        grad_down,
    )


def solution(mesh):
    placed = (
        P("dp", "ctx", None),
        P("dp", None),
        P(),
        P("dp", None),
        P(),
        P(),
        P(None, "dp"),
        P(None, "dp"),
        P("dp", None),
        P("dp", "ctx", None),
    )
    return jax.shard_map(
        local,
        mesh=mesh,
        in_specs=placed,
        out_specs=(
            P("dp", "ctx", None),
            P("dp", "ctx", None),
            P("dp", None),
            P(),
            P("dp", None),
            P(),
            P(),
            P(None, "dp"),
            P(None, "dp"),
            P("dp", None),
        ),
        check_vma=False,
    )
```

```python
import jax
import jax.numpy as jnp
from jax import lax
from jax.experimental import pallas as pl
from jax.experimental.pallas import tpu as pltpu
from jax.sharding import PartitionSpec as P

D = 896
QH = 14
KH = 2
HD = 64
GROUP = QH // KH
WIDTH_Q = QH * HD
WIDTH_K = KH * HD

EPS = 1e-06
ROPE_BASE = 1000000.0

f32 = jnp.float32
bf16 = jnp.bfloat16


def ring_order(chips):
    if chips % 2:
        return list(range(chips))
    rows = chips // 2
    return [2 * i for i in range(rows)] + [2 * i + 1 for i in reversed(range(rows))]


def half_cut(rows):
    cut = (rows // 2 + 7) // 8 * 8
    return cut if cut < rows else rows // 2


def add_low(a, b):
    return (a.astype(f32) + b.astype(f32)).astype(bf16)


class Net:
    def __init__(self):
        self.dp = lax.axis_size("dp")
        self.ctx = lax.axis_size("ctx")
        self.chips = self.ctx // 2
        self.order = ring_order(self.chips)
        self.d = lax.axis_index("dp")
        self.c = lax.axis_index("ctx")
        self.core = self.c % 2
        place = [0] * self.chips
        for spot, chip in enumerate(self.order):
            place[chip] = spot
        self.pos = jnp.array(place, jnp.int32)[self.c // 2]

    def swap(self, x):
        return lax.ppermute(x, "ctx", [(i, i ^ 1) for i in range(self.ctx)])

    def shift(self, x, step):
        n = self.dp
        return lax.ppermute(x, "dp", [(i, (i + step) % n) for i in range(n)])

    def hop(self, x, step):
        n = self.chips
        perm = []
        for spot in range(n):
            for core in range(2):
                perm.append((2 * self.order[spot] + core, 2 * self.order[(spot + step) % n] + core))
        return lax.ppermute(x, "ctx", perm)

    def owner(self, slot):
        return (self.pos - slot) % self.chips

    def group_parts(self, x):
        chip = jnp.concatenate([x] + [self.shift(x, s) for s in range(1, self.dp)], 0)
        return chip, self.swap(chip)

    def group_gather(self, x):
        return jnp.concatenate(self.group_parts(x), 0)

    def ring_gather(self, x):
        n = self.chips
        half = n // 2
        cut = half_cut(x.shape[0])
        found = [x] + [None] * (n - 1)
        fwd, back = x, x
        for s in range(1, half):
            fwd = self.hop(fwd, 1)
            back = self.hop(back, -1)
            found[s] = fwd
            found[n - s] = back
        found[half] = jnp.concatenate([self.hop(fwd[:cut], 1), self.hop(back[cut:], -1)], 0)
        return found

    def ring_scatter(self, local):
        n = self.chips
        half = n // 2
        cut = half_cut(local[half].shape[0])

        def add(got, mine):
            return (got.astype(f32) + mine.astype(f32)).astype(bf16)

        fwd = self.hop(local[half][:cut], 1)
        back = self.hop(local[half][cut:], -1)
        for s in range(1, half):
            mine_f = local[half + s]
            mine_b = local[half - s]
            if s == 1:
                mine_f = jnp.concatenate([add(fwd, mine_f[:cut]), mine_f[cut:]], 0)
                mine_b = jnp.concatenate([mine_b[:cut], add(back, mine_b[cut:])], 0)
            else:
                mine_f = add(fwd, mine_f)
                mine_b = add(back, mine_b)
            fwd = self.hop(mine_f, 1)
            back = self.hop(mine_b, -1)
        return fwd.astype(f32) + back.astype(f32) + local[0].astype(f32)

    def full_rows(self, shard):
        rows = shard.shape[0]
        half = rows // 2
        piece = lax.dynamic_slice(shard, (self.core * half, 0), (half, shard.shape[1]))
        blocks = [shard]
        for s in range(1, self.dp):
            got = self.shift(piece, s)
            other = self.swap(got)
            low = jnp.where(self.core == 0, got, other)
            high = jnp.where(self.core == 0, other, got)
            blocks.append(jnp.concatenate([low, high], 0))
        if self.dp == 2:
            first = jnp.where(self.d == 0, blocks[0], blocks[1])
            second = jnp.where(self.d == 0, blocks[1], blocks[0])
            return jnp.concatenate([first, second], 0)
        ranked = jnp.stack(blocks)[(self.d - jnp.arange(self.dp)) % self.dp]
        return ranked.reshape(self.dp * rows, shard.shape[1])

    def total(self, x):
        x = x + self.swap(x)
        bit = 1
        while bit < self.chips:
            x = x + lax.ppermute(x, "ctx", [(i, i ^ (2 * bit)) for i in range(self.ctx)])
            bit *= 2
        bit = 1
        while bit < self.dp:
            x = x + lax.ppermute(x, "dp", [(i, i ^ bit) for i in range(self.dp)])
            bit *= 2
        return x

    def ring_parts(self, local):
        n = self.chips
        half = n // 2
        cut = half_cut(local[half].shape[0])

        def add(got, mine):
            return (got.astype(f32) + mine.astype(f32)).astype(bf16)

        fwd, back = self.hop(local[half][:cut], 1), self.hop(local[half][cut:], -1)
        marks = [(fwd, back)]
        for s in range(1, half):
            mine_f, mine_b = local[half + s], local[half - s]
            if s == 1:
                mine_f = jnp.concatenate([add(fwd, mine_f[:cut]), mine_f[cut:]], 0)
                mine_b = jnp.concatenate([mine_b[:cut], add(back, mine_b[cut:])], 0)
            else:
                mine_f, mine_b = add(fwd, mine_f), add(back, mine_b)
            fwd, back = self.hop(mine_f, 1), self.hop(mine_b, -1)
            marks.append((fwd, back))
        return [local[0], fwd, back], marks

    def exchange_start(self, x):
        half = x.shape[0] // 2
        x = add_low(x, self.swap(x))
        return lax.dynamic_slice(x, (self.core * half, 0), (half, x.shape[1]))

    def exchange(self, x, bit):
        return add_low(x, lax.ppermute(x, "ctx", [(i, i ^ (2 * bit)) for i in range(self.ctx)]))

    def ring_sum(self, terms, between):
        half = self.chips // 2
        fwd, back = self.hop(terms[half], 1), self.hop(terms[half - 1], -1)

        def add(got, slot):
            return (got.astype(f32) + terms[slot].astype(f32)).astype(bf16)

        for s in range(1, half):
            blocks = [add(fwd, half + s)]
            if s < half - 1:
                blocks.append(add(back, half - 1 - s))
            if s == 1:
                marks = between(*blocks)
            else:
                blocks = gate(marks[s - 2], blocks)
            fwd = self.hop(blocks[0], 1)
            if s < half - 1:
                back = self.hop(blocks[1], -1)
        return fwd, back

    def gather_placed(self, x, place, rest, marks):
        n = self.chips
        half = n // 2
        fwd = back = x
        placed = None
        waiting = ([0], [(x, self.swap(x))])
        for s in range(1, half + 1):
            if s > 1:
                placed, token = place(*waiting, placed)
                before = [token] + marks[s - 2]
                if s > half - 2:
                    rest = self.exchange(gate([token], [rest])[0], 1 << (s - half + 1))
                    if s == half:
                        before.append(rest)
                fwd, back = gate(before, [fwd, back])
                waiting = ([s - 1, n - s + 1], [(fwd, self.swap(fwd)), (back, self.swap(back))])
            if s < half:
                fwd, back = self.hop(fwd, 1), self.hop(back, -1)
            else:
                cut = half_cut(fwd.shape[0])
                fwd, back = self.hop(fwd[:cut], 1), self.hop(back[cut:], -1)
        placed, token = place(*waiting, placed)
        far = join(fwd, back, token)
        rest = gate([token], [rest])[0]
        rest = self.exchange(rest, half)
        halves = (rest, self.swap(rest))
        return place([half], [(far, self.swap(far))], placed, halves)[0], halves


VMEM_BYTES = 56 * 1024 * 1024
KEYS = 256
RING_ROWS = 152


def full_spec(shape):
    return pl.BlockSpec(shape, lambda: (0,) * len(shape))


def call(kernel, outs, args, smem=0, scratch=(), flops=0, loose=0):
    tight = len(args) - loose
    specs = [pl.BlockSpec(memory_space=pltpu.SMEM)] * smem
    specs += [pl.BlockSpec(memory_space=pltpu.VMEM)] * (tight - smem)
    specs += [pl.BlockSpec(memory_space=pl.ANY)] * loose

    def body(*refs):
        kernel(*refs[:tight], *refs[tight + loose :])

    moved = sum(x.size * x.dtype.itemsize for x in list(args) + list(outs))
    return pl.pallas_call(
        body,
        out_shape=list(outs),
        in_specs=specs,
        out_specs=[pl.BlockSpec(memory_space=pltpu.VMEM)] * len(outs),
        scratch_shapes=list(scratch),
        compiler_params=pltpu.CompilerParams(vmem_limit_bytes=VMEM_BYTES),
        cost_estimate=pl.CostEstimate(flops=flops, bytes_accessed=moved, transcendentals=0),
    )(*args)


def lanes(shape):
    return lax.broadcasted_iota(jnp.int32, shape, len(shape) - 1)


def dot_nt(a, b, precision=None):
    return lax.dot_general(
        a, b, (((1,), (1,)), ((), ())), preferred_element_type=f32, precision=precision
    )


def dot_tn(a, b):
    return lax.dot_general(a, b, (((0,), (0,)), ((), ())), preferred_element_type=f32)


def gate(tokens, blocks):
    count, before = len(blocks), len(tokens)
    anywhere = pl.BlockSpec(memory_space=pl.ANY)

    def kernel(*refs):
        return None

    return pl.pallas_call(
        kernel,
        out_shape=[jax.ShapeDtypeStruct(x.shape, x.dtype) for x in blocks],
        in_specs=[anywhere] * (before + count),
        out_specs=[anywhere] * count,
        input_output_aliases={before + i: i for i in range(count)},
        cost_estimate=pl.CostEstimate(flops=0, bytes_accessed=1024, transcendentals=0),
    )(*tokens, *blocks)


def join(first, second, token):
    cut = first.shape[0]

    def kernel(first_ref, second_ref, out_ref):
        out_ref[:cut, :] = first_ref[...]
        out_ref[cut:, :] = second_ref[...]

    shape = (cut + second.shape[0], first.shape[1])
    return call(
        kernel, [jax.ShapeDtypeStruct(shape, first.dtype)], [first, second, token], loose=1
    )[0]


def ring_end(fwd, back, term, split):
    rows, columns = term.shape

    def kernel(fwd_ref, back_ref, term_ref, first_ref, rest_ref):
        for ref, here in ((first_ref, slice(0, split)), (rest_ref, slice(split, rows))):
            total = fwd_ref[here, :].astype(f32) + back_ref[here, :].astype(f32)
            ref[...] = (total + term_ref[here, :].astype(f32)).astype(bf16)

    outs = [
        jax.ShapeDtypeStruct((split, columns), bf16),
        jax.ShapeDtypeStruct((rows - split, columns), bf16),
    ]
    return call(kernel, outs, [fwd, back, term])


def pair_kernel(mine_ref, got_ref, *out_refs):
    rows = out_refs[0].shape[0]
    for s, out_ref in enumerate(out_refs):
        here = slice(s * rows, (s + 1) * rows)
        out_ref[...] = (mine_ref[here, :] + got_ref[here, :].astype(f32)).astype(out_ref.dtype)


def block_kernel(mlp_ref, down_ref, *refs):
    small = refs[0][...].astype(f32)
    for ref in refs[1:-1]:
        small = small + ref[...].astype(f32)
    out_ref = refs[-1]
    top = mlp_ref.shape[0]
    piece = small.shape[0]
    out_ref[:top, :] = mlp_ref[...]
    out_ref[top : top + piece, :] = small.astype(bf16)
    out_ref[top + piece :, :] = down_ref[...]


def qkv_kernel(x_ref, gain_ref, w_ref, b_ref, cos_ref, sin_ref, norm_ref, q_ref, pair_ref):
    x = x_ref[...].astype(f32)
    inverse = lax.rsqrt(jnp.mean(x * x, -1, keepdims=True) + EPS)
    normed = (x * inverse * gain_ref[...]).astype(bf16)
    norm_ref[...] = normed
    joint = jnp.dot(normed, w_ref[...], preferred_element_type=f32) + b_ref[...]
    cosine = cos_ref[...]
    sine = sin_ref[...]
    early = lanes(cosine.shape) % HD < HD // 2
    for i in range((WIDTH_Q + WIDTH_K) // 128):
        tile = joint[:, i * 128 : (i + 1) * 128]
        turned = jnp.where(early, -pltpu.roll(tile, 96, 1), pltpu.roll(tile, 32, 1))
        turned = tile * cosine + turned * sine
        if i * 128 < WIDTH_Q:
            q_ref[:, i * 128 : (i + 1) * 128] = turned.astype(bf16)
        else:
            pair_ref[:, :WIDTH_K] = turned.astype(bf16)
    pair_ref[:, WIDTH_K:] = joint[:, WIDTH_Q + WIDTH_K :].astype(bf16)


def spread_heads(x, out_ref, factor):
    rows = x.shape[0]
    half = rows // 2
    for head in range(QH):
        kh, g = divmod(head, GROUP)
        tile = x[:, (head // 2) * 128 : (head // 2 + 1) * 128].astype(f32)
        if head % 2 != kh:
            tile = pltpu.roll(tile, HD, 1)
        tile = jnp.where(lanes(tile.shape) // HD == kh, tile * factor, 0.0).astype(out_ref.dtype)
        for part in range(2):
            start = (part * GROUP + g) * half
            out_ref[kh, start : start + half, :] = tile[part * half : (part + 1) * half]


def join_heads(src_ref, half, tile):
    sides = []
    for side in range(2):
        kh, g = divmod(2 * tile + side, GROUP)
        parts = [
            src_ref[kh, (part * GROUP + g) * half : (part * GROUP + g + 1) * half, :]
            for part in range(2)
        ]
        both = jnp.concatenate(parts, 0)
        sides.append(both if side == kh else pltpu.roll(both, HD, 1))
    return jnp.where(lanes(sides[0].shape) < HD, sides[0], sides[1])


def forward_kernel(
    ctx, meta_ref, q_ref, mine_ref, other_ref, x_ref, w_ref, gain_ref,
    low_ref, o_ref, lse_ref, spread_ref, k_ref, v_ref, hidden_ref, normed_ref,
    s_ref, max_ref, sum_ref,
):
    rows = q_ref.shape[0]
    half = rows // 2
    part_rows = GROUP * half
    me = meta_ref[0]
    chips = ctx // 2
    for j in range(ctx):
        src = mine_ref if j < chips else other_ref
        at = (j % chips) * rows
        owner = meta_ref[1 + j]
        for part in range(2):
            place = owner if part == 0 else 2 * ctx - 1 - owner
            to = pl.ds(pl.multiple_of(place * half, half), half)
            block = src[at + part * half : at + (part + 1) * half, :]
            k_ref[to, :] = block[:, :WIDTH_K]
            v_ref[to, :] = block[:, WIDTH_K:]
    spread_heads(q_ref[...], spread_ref, HD ** (-0.5))
    for part in range(2):
        span = slice(part * part_rows, (part + 1) * part_rows)
        start = (me if part == 0 else 2 * ctx - 1 - me) * half
        last = start // KEYS

        def keys_of(ref, i):
            return ref[pl.ds(pl.multiple_of(i * KEYS, KEYS), KEYS), :]

        for kh in range(KH):
            scores = dot_nt(spread_ref[kh, span, :], keys_of(k_ref, last))
            row = lax.broadcasted_iota(jnp.int32, scores.shape, 0) % half + start
            scores = jnp.where(lanes(scores.shape) + last * KEYS <= row, scores, -1e30)
            s_ref[kh, last] = scores
            max_ref[kh] = jnp.maximum(scores[:, :128], scores[:, 128:])

        def score(i, carry):
            for kh in range(KH):
                s = dot_nt(spread_ref[kh, span, :], keys_of(k_ref, i))
                s_ref[kh, i] = s
                max_ref[kh] = jnp.maximum(max_ref[kh], jnp.maximum(s[:, :128], s[:, 128:]))
            return carry

        lax.fori_loop(0, last, score, 0)
        for kh in range(KH):
            top = jnp.max(max_ref[kh], -1, keepdims=True)
            max_ref[kh] = jnp.broadcast_to(top, (part_rows, 128))
            sum_ref[kh] = jnp.zeros((part_rows, 128), f32)
            o_ref[kh, span, :] = jnp.zeros((part_rows, 128), f32)

        def weigh(i, carry):
            for kh in range(KH):
                s = s_ref[kh, i]
                top = max_ref[kh]
                left = jnp.exp(s[:, :128] - top)
                right = jnp.exp(s[:, 128:] - top)
                sum_ref[kh] += left + right
                o_ref[kh, span, :] += jnp.dot(
                    jnp.concatenate([left, right], 1).astype(bf16),
                    keys_of(v_ref, i),
                    preferred_element_type=f32,
                )
            return carry

        lax.fori_loop(0, last + 1, weigh, 0)
        for kh in range(KH):
            total = jnp.sum(sum_ref[kh], -1, keepdims=True)
            o_ref[kh, span, :] = o_ref[kh, span, :] / total
            lse_ref[kh, part] = dot_nt(
                jnp.full((8, 128), 1.0 / 128, f32),
                max_ref[kh] + jnp.log(total),
                lax.Precision.HIGHEST,
            )
    for tile in range(WIDTH_Q // 128):
        low_ref[:, tile * 128 : (tile + 1) * 128] = join_heads(o_ref, half, tile).astype(bf16)
    hidden = x_ref[...].astype(f32) + jnp.dot(low_ref[...], w_ref[...], preferred_element_type=f32)
    hidden_ref[...] = hidden
    inverse = lax.rsqrt(jnp.mean(hidden * hidden, -1, keepdims=True) + EPS)
    normed_ref[...] = (hidden * inverse * gain_ref[...]).astype(bf16)


def turn_back(grad, cos_ref, sin_ref):
    scaled = grad * sin_ref[...]
    early = lanes(grad.shape) % HD < HD // 2
    turned = jnp.where(early, pltpu.roll(scaled, 96, 1), -pltpu.roll(scaled, 32, 1))
    return grad * cos_ref[...] + turned


def backward_kernel(
    ctx, meta_ref, gn_ref, hidden_ref, gout_ref, gain_ref, w_ref, spread_ref, k_ref, v_ref, lse_ref,
    o_ref, cos_ref, sin_ref,
    gh_ref, ga_ref, gain_grad_ref, gq_ref, mine_ref, other_ref,
    go_ref, gqs_ref, gk_ref, gv_ref,
):
    rows = gn_ref.shape[0]
    half = rows // 2
    part_rows = GROUP * half
    me = meta_ref[0]
    chips = ctx // 2
    hidden = hidden_ref[...]
    inverse = lax.rsqrt(jnp.mean(hidden * hidden, -1, keepdims=True) + EPS)
    unit = hidden * inverse
    grad = gn_ref[...]
    gain_grad_ref[...] = jnp.sum(grad * unit, 0, keepdims=True)
    scaled = grad * gain_ref[...]
    gh = gout_ref[...].astype(f32) + inverse * (
        scaled - unit * jnp.mean(scaled * unit, -1, keepdims=True)
    )
    gh_ref[...] = gh
    ga = gh.astype(bf16)
    ga_ref[...] = ga
    spread_heads(dot_nt(ga, w_ref[...]).astype(bf16), go_ref, 1.0)
    gqs_ref[...] = jnp.zeros_like(gqs_ref)
    gk_ref[...] = jnp.zeros_like(gk_ref)
    gv_ref[...] = jnp.zeros_like(gv_ref)
    for part in range(2):
        span = slice(part * part_rows, (part + 1) * part_rows)
        start = (me if part == 0 else 2 * ctx - 1 - me) * half
        last = start // KEYS
        deltas = [
            dot_nt(
                jnp.ones((8, 128), f32),
                go_ref[kh, span, :].astype(f32) * o_ref[kh, span, :],
                lax.Precision.HIGHEST,
            )[:1]
            for kh in range(KH)
        ]

        def step(i, masked):
            at = pl.ds(pl.multiple_of(i * KEYS, KEYS), KEYS)
            keys = k_ref[at, :]
            grad_k = gk_ref[at, :]
            grad_v = gv_ref[at, :]
            for kh in range(KH):
                queries = spread_ref[kh, span, :]
                heads = go_ref[kh, span, :]
                p = jnp.exp(dot_nt(keys, queries) - lse_ref[kh, part][:1])
                if masked:
                    row = lanes(p.shape) % half + start
                    key = lax.broadcasted_iota(jnp.int32, p.shape, 0) + i * KEYS
                    p = jnp.where(key <= row, p, 0.0)
                gs = (p * (dot_nt(v_ref[at, :], heads) - deltas[kh])).astype(bf16)
                grad_v += jnp.dot(p.astype(bf16), heads, preferred_element_type=f32)
                grad_k += jnp.dot(gs, queries, preferred_element_type=f32)
                gqs_ref[kh, span, :] += dot_tn(gs, keys)
            gk_ref[at, :] = grad_k
            gv_ref[at, :] = grad_v

        def body(i, carry):
            step(i, False)
            return carry

        lax.fori_loop(0, last, body, 0)
        step(last, True)
    for tile in range(WIDTH_Q // 128):
        grad = join_heads(gqs_ref, half, tile) * HD ** (-0.5)
        gq_ref[:, tile * 128 : (tile + 1) * 128] = turn_back(grad, cos_ref, sin_ref).astype(bf16)
    for j in range(ctx):
        dst = mine_ref if j < chips else other_ref
        at = (j % chips) * rows
        owner = meta_ref[1 + j]
        for part in range(2):
            place = owner if part == 0 else 2 * ctx - 1 - owner
            frm = pl.ds(pl.multiple_of(place * half, half), half)
            to = slice(at + part * half, at + (part + 1) * half)
            dst[to, :WIDTH_K] = gk_ref[frm, :].astype(dst.dtype)
            dst[to, WIDTH_K:] = gv_ref[frm, :].astype(dst.dtype)


SUM_ROWS = 16


def finish_kernel(
    gq_ref, x_ref, gain_ref, w_ref, cos_ref, sin_ref, gh_ref, gain_two_ref, *refs
):
    sent_ref, gx_ref, gain_grad_ref, bias_ref = refs[-4:]
    pair = refs[0][...]
    for ref in refs[1:-4]:
        pair = pair + ref[...].astype(f32)
    rows = pair.shape[0]
    keys = turn_back(pair[:, :WIDTH_K], cos_ref, sin_ref)
    pair = jnp.concatenate([keys, pair[:, WIDTH_K:]], 1).astype(bf16)
    sent_ref[:rows, :] = pair
    joint = jnp.concatenate([gq_ref[...], pair], 1)
    bias = jnp.sum(joint.astype(f32), 0, keepdims=True)
    bias_ref[...] = bias
    grad = dot_nt(joint, w_ref[...])
    x = x_ref[...].astype(f32)
    inverse = lax.rsqrt(jnp.mean(x * x, -1, keepdims=True) + EPS)
    unit = x * inverse
    gain = jnp.sum(grad * unit, 0, keepdims=True)
    gain_grad_ref[...] = gain
    scaled = grad * gain_ref[...]
    gx_ref[...] = gh_ref[...] + inverse * (
        scaled - unit * jnp.mean(scaled * unit, -1, keepdims=True)
    )
    sums = jnp.concatenate([gain, gain_two_ref[...], bias], 1)
    width = pair.shape[1]
    sums = jnp.concatenate([sums, jnp.zeros((1, -sums.shape[1] % width), f32)], 1)
    found = [sums[:, i : i + width] for i in range(0, sums.shape[1], width)]
    found += [jnp.zeros((1, width), f32)] * (SUM_ROWS - len(found))
    sums = jnp.concatenate(found, 0)
    high = sums.astype(bf16)
    sent_ref[rows : rows + SUM_ROWS, :] = high
    sent_ref[rows + SUM_ROWS :, :] = (sums - high.astype(f32)).astype(bf16)


def pair_grad_kernel(rows, half_width, meta_ref, norm_ref, own_ref, peer_ref, out_ref, turned_ref):
    turned_ref[...] = norm_ref[:, D:].T
    first = pl.multiple_of(meta_ref[0] * half_width, 16)
    both = jnp.concatenate([own_ref[:rows, :], peer_ref[:rows, :]], 0)
    part = jnp.dot(turned_ref[pl.ds(first, half_width), :], both, preferred_element_type=f32)
    out_ref[:half_width, :] = part.astype(bf16)

    def sums(ref):
        high = ref[rows : rows + SUM_ROWS, :].astype(f32)
        return high + ref[rows + SUM_ROWS :, :].astype(f32)

    out_ref[half_width:, :] = (sums(own_ref) + sums(peer_ref)).astype(bf16)


def mlp_kernel(
    half_rows, spots_ref, x_a, x_b, gy_a, gy_b, gate_a, gate_b, up_a, up_b, down_a, down_b,
    xt_ref, midt_ref, gg_ref, gu_ref, gx_ref, out_ref, send_ref,
    x_all, gy_all, wg_all, wu_all, wd_all, mid_all, gg_all, gu_all,
):
    step = pl.program_id(0)

    @pl.when(step == 0)
    def start():
        x_all[:half_rows] = x_a[...]
        x_all[half_rows:] = x_b[...]
        gy_all[:half_rows] = gy_a[...]
        gy_all[half_rows:] = gy_b[...]
        xt_ref[...] = x_all[...].T

    here = pl.ds(pl.multiple_of(step * 256, 256), 256)
    wg = jnp.concatenate([gate_a[...], gate_b[...]], 1)
    wu = jnp.concatenate([up_a[...], up_b[...]], 1)
    wd = jnp.concatenate([down_a[...], down_b[...]], 0)
    wg_all[:, here] = wg
    wu_all[:, here] = wu
    wd_all[here, :] = wd
    core = spots_ref[1]
    column = lanes((1, 256)) + (step * 256 + spots_ref[2])
    own = (column < spots_ref[3]) == (core == 0)
    x = x_all[...]
    gate = jnp.dot(x, wg, preferred_element_type=f32)
    up = jnp.dot(x, wu, preferred_element_type=f32)
    grad = jnp.where(own, dot_nt(gy_all[...], wd), 0.0)
    sigma = jax.nn.sigmoid(gate)
    active = gate * sigma
    middle = jnp.where(own, active * up, 0.0).astype(bf16)
    grad_gate = (grad * up * (sigma + active * (1.0 - sigma))).astype(bf16)
    grad_up = (grad * active).astype(bf16)
    midt_ref[...] = middle.T
    gg_ref[...] = grad_gate
    gu_ref[...] = grad_up
    mid_all[:, here] = middle
    gg_all[:, here] = grad_gate
    gu_all[:, here] = grad_up

    @pl.when(step == pl.num_programs(0) - 1)
    def end():
        gx = dot_nt(gg_all[...], wg_all[...]) + dot_nt(gu_all[...], wu_all[...])
        gx_ref[...] = gx[:half_rows]
        send_ref[:half_rows] = gx[half_rows:].astype(bf16)
        out = jnp.dot(mid_all[...], wd_all[...], preferred_element_type=f32)
        out_ref[...] = out[:half_rows]
        send_ref[half_rows:] = out[half_rows:].astype(bf16)


def feed_forward(meta, x, early, w_gate, w_up, w_down, width):
    half = x[0].shape[0]
    tokens = 2 * half
    steps = width // 256
    tiles = width // 128 - 1

    def columns(j):
        return pl.BlockSpec((D, 128), lambda i, m: (0, m[1] * tiles + 2 * i + j))

    def rows(j):
        return pl.BlockSpec((128, D), lambda i, m: (m[1] * tiles + 2 * i + j, 0))

    whole = pl.BlockSpec((tokens, D), lambda i, m: (0, 0))
    halves = pl.BlockSpec((half, D), lambda i, m: (0, 0))
    tile = pl.BlockSpec((tokens, 256), lambda i, m: (0, i))
    hidden = jax.ShapeDtypeStruct((tokens, width), bf16)
    return pl.pallas_call(
        lambda *refs: mlp_kernel(half, *refs),
        out_shape=[
            jax.ShapeDtypeStruct((D, tokens), bf16),
            jax.ShapeDtypeStruct((width, tokens), bf16),
            hidden,
            hidden,
            jax.ShapeDtypeStruct((half, D), f32),
            jax.ShapeDtypeStruct((half, D), f32),
            jax.ShapeDtypeStruct((tokens, D), bf16),
        ],
        grid_spec=pltpu.PrefetchScalarGridSpec(
            num_scalar_prefetch=1,
            grid=(steps,),
            in_specs=[halves] * 4
            + [columns(0), columns(1), columns(0), columns(1), rows(0), rows(1)],
            out_specs=[
                pl.BlockSpec((D, tokens), lambda i, m: (0, 0)),
                pl.BlockSpec((256, tokens), lambda i, m: (i, 0)),
                tile,
                tile,
                halves,
                halves,
                whole,
            ],
            scratch_shapes=[pltpu.VMEM((tokens, D), bf16)] * 2
            + [pltpu.VMEM((D, width), bf16)] * 2
            + [pltpu.VMEM((width, D), bf16)]
            + [pltpu.VMEM((tokens, width), bf16)] * 3,
        ),
        compiler_params=pltpu.CompilerParams(vmem_limit_bytes=VMEM_BYTES),
        cost_estimate=pl.CostEstimate(
            flops=12 * tokens * width * D, bytes_accessed=6 * width * D, transcendentals=0
        ),
    )(meta, *x, *early, w_gate, w_gate, w_up, w_up, w_down, w_down)


def mlp_grad_kernel(chips, down_rows, main, meta_ref, xt_ref, gy_a, gy_b, midt_ref, gg_ref, gu_ref, *refs):
    out_refs = refs[:chips]
    mlp_acc, down_acc, blocks, sems = refs[chips:]
    core = meta_ref[1]
    at_main = pl.ds(pl.multiple_of(core * 128, 128), main)
    at_tile = pl.ds(pl.multiple_of((1 - core) * main, 128), 128)
    xt = xt_ref[...]
    mlp_acc[:, :main] = jnp.dot(xt, gg_ref[:, at_main], preferred_element_type=f32).astype(bf16)
    mlp_acc[:, main : 2 * main] = jnp.dot(
        xt, gu_ref[:, at_main], preferred_element_type=f32
    ).astype(bf16)
    mixed = gg_ref[:, at_tile].astype(f32) + pltpu.roll(gu_ref[:, at_tile].astype(f32), 64, 1)
    mlp_acc[:, 2 * main :] = jnp.dot(
        xt, mixed.astype(bf16), preferred_element_type=f32
    ).astype(bf16)
    gy = jnp.concatenate([gy_a[:, :D], gy_b[:, :D]], 0)
    down_acc[...] = jnp.dot(midt_ref[...], gy, preferred_element_type=f32)

    mlp_rows = mlp_acc.shape[0] // chips
    columns = mlp_acc.shape[1] // 128
    half = chips // 2
    copies = []
    for slot in sorted(range(chips), key=lambda s: abs(s - half) if s else chips):
        owner = meta_ref[12 + slot]
        block = mlp_acc[pl.ds(pl.multiple_of(owner * mlp_rows, 16), mlp_rows), :]
        for j in range(columns):
            for i in range(mlp_rows // 16):
                blocks[slot, j * 16 : (j + 1) * 16, i * 128 : (i + 1) * 128] = block[
                    i * 16 : (i + 1) * 16, j * 128 : (j + 1) * 128
                ]
        first = pl.multiple_of(core * 64 + owner * down_rows, 8)
        blocks[slot, columns * 16 :, :] = down_acc[pl.ds(first, down_rows), :].astype(bf16)
        copy = pltpu.make_async_copy(blocks.at[slot], out_refs[slot], sems.at[slot])
        copy.start()
        copies.append(copy)
    for copy in copies:
        copy.wait()


def mlp_gradients(meta, xt, early, midt, gg, gu, after, chips, down_rows, main):
    tokens = gg.shape[0]
    columns = (2 * main + 128) // 128
    rows = columns * 16 + down_rows
    args = [meta, xt, *early, midt, gg, gu]
    anywhere = pl.BlockSpec(memory_space=pl.ANY)

    def kernel(*refs):
        mlp_grad_kernel(chips, down_rows, main, *refs[: len(args)], *refs[len(args) + 1 :])

    return pl.pallas_call(
        kernel,
        out_shape=[jax.ShapeDtypeStruct((rows, D), bf16)] * chips,
        in_specs=[pl.BlockSpec(memory_space=pltpu.SMEM)]
        + [pl.BlockSpec(memory_space=pltpu.VMEM)] * (len(args) - 1)
        + [anywhere],
        out_specs=[anywhere] * chips,
        scratch_shapes=[
            pltpu.VMEM((D, columns * 128), bf16),
            pltpu.VMEM((midt.shape[0], D), f32),
            pltpu.VMEM((chips, rows, D), bf16),
            pltpu.SemaphoreType.DMA((chips,)),
        ],
        compiler_params=pltpu.CompilerParams(vmem_limit_bytes=VMEM_BYTES),
        cost_estimate=pl.CostEstimate(
            flops=6 * tokens * midt.shape[0] * D, bytes_accessed=4 * chips * rows * D,
            transcendentals=0,
        ),
    )(*args, after)


def small_grad_kernel(
    chips, q_rows, rows, cols, meta_ref, norm_a, norm_b, near_a, near_b, *refs
):
    out_refs, acc, turned_ref = refs[:-2], refs[-2], refs[-1]
    first = pl.multiple_of((2 * meta_ref[0] + meta_ref[1]) * q_rows, 16)
    grads, queries, attended = [], [], []
    for near_ref in (near_a, near_b):
        for b in range(2):
            for i, found in enumerate((grads, queries, attended)):
                found.append(near_ref[(3 * b + i) * rows : (3 * b + i + 1) * rows, :])
    turned_ref[...] = jnp.concatenate([norm_a[:, D:], norm_b[:, D:]], 0).T
    acc[:, :WIDTH_Q] = jnp.dot(
        turned_ref[pl.ds(first, q_rows), :],
        jnp.concatenate(queries, 0),
        preferred_element_type=f32,
    ).astype(bf16)
    acc[:, WIDTH_Q:cols] = jnp.zeros((q_rows, cols - WIDTH_Q), bf16)
    turned_ref[...] = jnp.concatenate(attended, 0).T
    acc[:, cols:] = jnp.dot(
        turned_ref[pl.ds(first, q_rows), :], jnp.concatenate(grads, 0), preferred_element_type=f32
    ).astype(bf16)
    width = acc.shape[1] // chips
    for out_ref, slot in zip(out_refs, range(chips)):
        owner = meta_ref[12 + slot]
        block = acc[:, pl.ds(pl.multiple_of(owner * width, 128), width)]
        tall = jnp.concatenate([block[:, i * 128 : (i + 1) * 128] for i in range(width // 128)], 0)
        piece = out_ref.shape[0]
        for i in range(D // 128):
            out_ref[:, i * 128 : (i + 1) * 128] = tall[i * piece : (i + 1) * piece]


def place_all(meta, slots, pairs, old, sizes, rest=None):
    main, ff_loc, q_rows, cols, down_rows, chips = sizes
    mlp_rows = D // chips
    columns = (2 * main + 128) // 128
    tiles = main // 128
    lanes_out = D // 128
    top = columns * 16
    blocks = [x for pair in pairs for x in pair]
    count = len(blocks)
    piece = blocks[0].shape[0] - top - down_rows
    parts = (cols + D) // chips // 128
    keep = [] if old is None else list(old)
    last = [] if rest is None else list(rest)
    known = WIDTH_Q // 128

    def kernel(meta_ref, *refs):
        ins = refs[:count]
        outs_at = count + len(last) + len(keep)
        gate_out, up_out, down_out, joint_out, proj_out, token_ref = refs[outs_at : outs_at + 6]
        gate_buf, up_buf, down_buf, small_buf, rest_buf, sems, small_sems, rest_sem = refs[
            outs_at + 6 :
        ]
        core_zero = meta_ref[1] == 0
        copies = []

        def send(src, dst, sem):
            copy = pltpu.make_async_copy(src, dst, sem)
            copy.start()
            copies.append(copy)

        def column(ref, j):
            found = [
                ref[j * 16 : (j + 1) * 16, i * 128 : (i + 1) * 128] for i in range(mlp_rows // 16)
            ]
            return jnp.concatenate(found, 0).astype(f32)

        for k, slot in enumerate(slots):
            for j in range(columns):
                got = column(ins[2 * k], j)
                other = column(ins[2 * k + 1], j)
                zero = jnp.where(core_zero, got, other)
                one = jnp.where(core_zero, other, got)
                if j < 2 * tiles:
                    buf = gate_buf if j < tiles else up_buf
                    at = (j % tiles) * 128
                    buf[k, :, at : at + 128] = zero
                    buf[k, :, at + main + 128 : at + main + 256] = one
                else:
                    left = lanes(zero.shape) < 64
                    gate_buf[k, :, main : main + 128] = jnp.where(left, zero, one)
                    up_buf[k, :, main : main + 128] = pltpu.roll(jnp.where(left, one, zero), 64, 1)
            owner = meta_ref[12 + slot]
            here = pl.ds(pl.multiple_of(owner * mlp_rows, 8), mlp_rows)
            send(gate_buf.at[k], gate_out.at[here, :], sems.at[4 * k])
            send(up_buf.at[k], up_out.at[here, :], sems.at[4 * k + 1])
            for side in range(2):
                b = 2 * k + side
                core = meta_ref[1] if side == 0 else 1 - meta_ref[1]
                down_buf[b] = ins[b][top + piece :, :].astype(f32)
                here = pl.ds(pl.multiple_of((core * chips + owner) * down_rows, 8), down_rows)
                send(down_buf.at[b], down_out.at[here, :], sems.at[4 * k + 2 + side])
                tall = jnp.concatenate(
                    [ins[b][top : top + piece, i * 128 : (i + 1) * 128] for i in range(lanes_out)], 0
                ).astype(f32)
                rows = pl.ds(pl.multiple_of(core * q_rows, 8), q_rows)
                for i in range(parts):
                    small_buf[b, i] = tall[i * q_rows : (i + 1) * q_rows]
                    block = owner * parts + i

                    @pl.when(block < known)
                    def joint(b=b, i=i, rows=rows, block=block):
                        at = pl.ds(pl.multiple_of(block * 128, 128), 128)
                        pltpu.make_async_copy(
                            small_buf.at[b, i], joint_out.at[rows, at], small_sems.at[b, i]
                        ).start()

                    @pl.when(block >= cols // 128)
                    def proj(b=b, i=i, rows=rows, block=block):
                        at = pl.ds(pl.multiple_of((block - cols // 128) * 128, 128), 128)
                        pltpu.make_async_copy(
                            small_buf.at[b, i], proj_out.at[rows, at], small_sems.at[b, i]
                        ).start()

        token_ref[...] = jnp.zeros(token_ref.shape, f32)
        if last:
            rows = last[0].shape[0]
            for core, ref in ((meta_ref[1], refs[count]), (1 - meta_ref[1], refs[count + 1])):
                rest_buf[pl.ds(pl.multiple_of(core * rows, 8), rows), :] = ref[...].astype(f32)
            send(rest_buf.at[: 2 * q_rows, :], joint_out.at[:, WIDTH_Q:cols], rest_sem)
        for copy in copies:
            copy.wait()
        for b in range(count):
            for i in range(parts):
                block = meta_ref[12 + slots[b // 2]] * parts + i

                @pl.when((block < known) | (block >= cols // 128))
                def done(b=b, i=i):
                    pltpu.make_async_copy(
                        small_buf.at[b, i],
                        proj_out.at[pl.ds(0, q_rows), pl.ds(0, 128)],
                        small_sems.at[b, i],
                    ).wait()

    anywhere = pl.BlockSpec(memory_space=pl.ANY)
    result = pl.pallas_call(
        kernel,
        out_shape=[
            jax.ShapeDtypeStruct((D, ff_loc), f32),
            jax.ShapeDtypeStruct((D, ff_loc), f32),
            jax.ShapeDtypeStruct((ff_loc, D), f32),
            jax.ShapeDtypeStruct((2 * q_rows, cols), f32),
            jax.ShapeDtypeStruct((2 * q_rows, D), f32),
            jax.ShapeDtypeStruct((8, 128), f32),
        ],
        in_specs=[pl.BlockSpec(memory_space=pltpu.SMEM)]
        + [pl.BlockSpec(memory_space=pltpu.VMEM)] * (count + len(last))
        + [anywhere] * len(keep),
        out_specs=[anywhere] * 5 + [pl.BlockSpec(memory_space=pltpu.VMEM)],
        scratch_shapes=[
            pltpu.VMEM((len(slots), mlp_rows, ff_loc), f32),
            pltpu.VMEM((len(slots), mlp_rows, ff_loc), f32),
            pltpu.VMEM((count, down_rows, D), f32),
            pltpu.VMEM((count, parts, q_rows, 128), f32),
            pltpu.VMEM((2 * q_rows + SUM_ROWS, cols - WIDTH_Q), f32),
            pltpu.SemaphoreType.DMA((4 * len(slots),)),
            pltpu.SemaphoreType.DMA((count, parts)),
            pltpu.SemaphoreType.DMA,
        ],
        input_output_aliases={1 + count + len(last) + i: i for i in range(len(keep))},
        compiler_params=pltpu.CompilerParams(vmem_limit_bytes=VMEM_BYTES),
        cost_estimate=pl.CostEstimate(
            flops=0, bytes_accessed=8 * sum(x.size for x in blocks), transcendentals=0
        ),
    )(meta, *blocks, *last, *keep)
    return list(result[:5]), result[5]


def place_blocks(blocks, spots, out_shape, old=None):
    shape = blocks[0].shape
    count = len(blocks)
    if shape[0] % 8 or shape[1] % 128:
        out = jnp.zeros(out_shape, f32) if old is None else old
        for block, (i, j) in zip(blocks, spots):
            out = lax.dynamic_update_slice(
                out, block.astype(f32), (i * shape[0], j * shape[1])
            )
        return out

    def kernel(spots_ref, *refs):
        step = pl.program_id(0)
        out_ref = refs[-1]
        for i in range(count):

            @pl.when(step == i)
            def write(i=i):
                out_ref[...] = refs[i][...].astype(f32)

    keep = [] if old is None else [old]
    return pl.pallas_call(
        kernel,
        out_shape=jax.ShapeDtypeStruct(out_shape, f32),
        grid_spec=pltpu.PrefetchScalarGridSpec(
            num_scalar_prefetch=1,
            grid=(count,),
            in_specs=[pl.BlockSpec(shape, lambda i, spots: (0, 0))] * count
            + [pl.BlockSpec(memory_space=pl.ANY)] * len(keep),
            out_specs=pl.BlockSpec(shape, lambda i, spots: (spots[i, 0], spots[i, 1])),
        ),
        input_output_aliases={} if old is None else {count + 1: 0},
        compiler_params=pltpu.CompilerParams(vmem_limit_bytes=VMEM_BYTES),
    )(jnp.stack([jnp.stack(s) for s in spots]).astype(jnp.int32), *blocks, *keep)


def local(tokens, w_qkv, b_qkv, w_out, gain_attn, gain_mlp, w_gate, w_up, w_down, cotangent):
    net = Net()
    rows = tokens.shape[1]
    half_rows = rows // 2
    ctx_count = net.ctx
    core = net.core
    chips = net.chips
    part_rows = GROUP * half_rows
    x = tokens[0]
    gain_one = gain_attn[None]
    gain_two = gain_mlp[None]

    w_qkv_full = net.full_rows(w_qkv)

    ff_loc = w_gate.shape[1]
    ff_half = ff_loc // 2
    main = (ff_half // 128) * 128
    rest = ff_half - main
    width = main + 2 * rest
    first = core * main
    tiled = net.dp == 2 and 2 * rest == 128 and width % 256 == 0 and chips == 8 and ff_half == chips * RING_ROWS
    ring = jnp.arange(chips, dtype=jnp.int32)
    owners_of = (net.pos - ring) % chips
    spots = jnp.concatenate(
        [jnp.stack([net.d, core, first, jnp.int32(ff_half)]), owners_of, owners_of]
    ).astype(jnp.int32)

    row_ids = jnp.arange(half_rows, dtype=jnp.int32)
    place = jnp.concatenate(
        [net.c * half_rows + row_ids, (2 * ctx_count - 1 - net.c) * half_rows + row_ids]
    )
    freq = ROPE_BASE ** (-((jnp.arange(128) % (HD // 2)).astype(f32) * (2.0 / HD)))
    angle = place.astype(f32)[:, None] * freq[None, :]
    cosine, sine = jnp.cos(angle), jnp.sin(angle)
    normed_one, queries, pairs = call(
        qkv_kernel,
        [
            jax.ShapeDtypeStruct((rows, D), bf16),
            jax.ShapeDtypeStruct((rows, WIDTH_Q), bf16),
            jax.ShapeDtypeStruct((rows, 2 * WIDTH_K), bf16),
        ],
        [x, gain_one, w_qkv_full, b_qkv[None], cosine, sine],
        flops=2 * rows * D * 1152,
    )

    slots = net.ring_gather(pairs)
    mine = jnp.concatenate(slots, 0)
    other = net.swap(mine)
    order = jnp.array(net.order, jnp.int32)
    chip_ids = order[(net.pos - jnp.arange(chips, dtype=jnp.int32)) % chips]
    meta = jnp.concatenate([net.c[None], 2 * chip_ids + core, 2 * chip_ids + 1 - core])
    meta = meta.astype(jnp.int32)

    late_w, late_g, late_n, unused = lax.optimization_barrier((w_out, cotangent[0], normed_one, pairs))
    w_out_full = net.full_rows(late_w)
    early = net.group_parts(jnp.concatenate([late_g, late_n], 1))

    total_keys = rows * ctx_count
    padded = (KH, 2 * part_rows, 128)
    attended_low, attended, lse, spread, keys, values, hidden, normed_two = call(
        lambda *refs: forward_kernel(ctx_count, *refs),
        [
            jax.ShapeDtypeStruct((rows, WIDTH_Q), bf16),
            jax.ShapeDtypeStruct(padded, f32),
            jax.ShapeDtypeStruct((KH, 2, 8, part_rows), f32),
            jax.ShapeDtypeStruct(padded, bf16),
            jax.ShapeDtypeStruct((total_keys, WIDTH_K), bf16),
            jax.ShapeDtypeStruct((total_keys, WIDTH_K), bf16),
            jax.ShapeDtypeStruct((rows, D), f32),
            jax.ShapeDtypeStruct((rows, D), bf16),
        ],
        [meta, queries, mine, other, x, w_out_full, gain_two],
        smem=1,
        scratch=[
            pltpu.VMEM((KH, total_keys // KEYS, part_rows, KEYS), f32),
            pltpu.VMEM((KH, part_rows, 128), f32),
            pltpu.VMEM((KH, part_rows, 128), f32),
        ],
        flops=8 * KH * part_rows * total_keys * 128,
    )

    normed_two_parts = net.group_parts(normed_two)
    chip_rows = net.dp * rows
    down_rows = ff_half // chips
    mlp_rows = D // chips
    if tiled:
        x_turned, mid_turned, gate_low, up_low, grad_mine, out_mine, sent = feed_forward(
            spots, normed_two_parts, early, w_gate, w_up, w_down, width
        )
    else:
        normed_two_group = jnp.concatenate(normed_two_parts, 0)
        grad_out_group = jnp.concatenate(early, 0)[:, :D]
        own_cols = (jnp.arange(width) + first < ff_half) == (core == 0)
        wg = lax.dynamic_slice(w_gate, (0, first), (D, width))
        wu = lax.dynamic_slice(w_up, (0, first), (D, width))
        wd = lax.dynamic_slice(w_down, (first, 0), (width, D))
        gate = jnp.dot(normed_two_group, wg, preferred_element_type=f32)
        upper = jnp.dot(normed_two_group, wu, preferred_element_type=f32)
        sigma = jax.nn.sigmoid(gate)
        activated = gate * sigma
        middle = jnp.where(own_cols, activated * upper, 0.0).astype(bf16)
        grad_middle = jnp.einsum("td,fd->tf", grad_out_group, wd, preferred_element_type=f32)
        slope = sigma * (1.0 + gate * (1.0 - sigma))
        grad_gate_low = jnp.where(own_cols, grad_middle * upper * slope, 0.0).astype(bf16)
        grad_up_low = jnp.where(own_cols, grad_middle * activated, 0.0).astype(bf16)

        grad_normed_two = jnp.einsum(
            "tf,df->td", grad_gate_low, wg, preferred_element_type=f32
        ) + jnp.einsum("tf,df->td", grad_up_low, wu, preferred_element_type=f32)
        mlp_out = jnp.dot(middle, wd, preferred_element_type=f32)
        grad_mine, out_mine = grad_normed_two[:chip_rows], mlp_out[:chip_rows]
        sent = jnp.concatenate([grad_normed_two[chip_rows:], mlp_out[chip_rows:]], 0).astype(bf16)
    swapped = net.swap(sent)
    grad_chip = grad_mine + swapped[:chip_rows].astype(f32)
    mlp_chip = out_mine + swapped[chip_rows:].astype(f32)
    grad_two = grad_chip[:rows]
    for s in range(1, net.dp):
        sent_two = grad_chip[s * rows : (s + 1) * rows].astype(bf16)
        grad_two = grad_two + net.shift(sent_two, net.dp - s).astype(f32)

    def attention_back(*after):
        grad_hidden, grad_attn_low, grad_gain_two, grad_queries, terms_mine, terms_other = call(
            lambda *refs: backward_kernel(ctx_count, *refs),
            [
                jax.ShapeDtypeStruct((rows, D), f32),
                jax.ShapeDtypeStruct((rows, D), bf16),
                jax.ShapeDtypeStruct((1, D), f32),
                jax.ShapeDtypeStruct((rows, WIDTH_Q), bf16),
                jax.ShapeDtypeStruct((chips * rows, 2 * WIDTH_K), f32),
                jax.ShapeDtypeStruct((chips * rows, 2 * WIDTH_K), bf16),
            ],
            [
                meta, grad_two, hidden, cotangent[0], gain_two, w_out_full, spread, keys, values, lse,
                attended, cosine, sine, *after,
            ],
            smem=1,
            loose=len(after),
            scratch=[
                pltpu.VMEM(padded, bf16),
                pltpu.VMEM(padded, f32),
                pltpu.VMEM((total_keys, WIDTH_K), f32),
                pltpu.VMEM((total_keys, WIDTH_K), f32),
            ],
            flops=20 * KH * part_rows * total_keys * 128,
        )
        other_terms = net.swap(terms_other)

        def row_sums(*after):
            pair_sums = call(
                pair_kernel,
                [jax.ShapeDtypeStruct((rows, 2 * WIDTH_K), f32)]
                + [jax.ShapeDtypeStruct((rows, 2 * WIDTH_K), bf16)] * (chips - 1),
                [terms_mine, other_terms, *after],
                loose=len(after),
            )
            return net.ring_parts(pair_sums)

        def finish(grad_pairs):
            return call(
                finish_kernel,
                [
                    jax.ShapeDtypeStruct((rows + 2 * SUM_ROWS, 2 * WIDTH_K), bf16),
                    jax.ShapeDtypeStruct((rows, D), f32),
                    jax.ShapeDtypeStruct((1, D), f32),
                    jax.ShapeDtypeStruct((1, w_qkv.shape[1]), f32),
                ],
                [grad_queries, x, gain_one, w_qkv_full, cosine, sine, grad_hidden, grad_gain_two]
                + grad_pairs,
            )

        return grad_attn_low, grad_gain_two, grad_queries, row_sums, finish

    if tiled:
        terms = mlp_gradients(
            spots, x_turned, early, mid_turned, gate_low, up_low, sent_two, chips, down_rows, main
        )
        grad_attn_low, grad_gain_two, grad_queries, row_sums, finish = attention_back(terms[0])
        found = []

        def between(*blocks):
            found.extend(row_sums(*blocks))
            return found[1]

        fwd, back = net.ring_sum(terms, between)
        grad_pairs, marks = found
        sum_mlp, sum_down = ring_end(fwd, back, terms[0], terms[0].shape[0] - down_rows)
    else:
        part_down = jnp.einsum(
            "tf,td->fd", middle, grad_out_group, preferred_element_type=f32
        ).astype(bf16)
        part_down = lax.dynamic_slice(part_down, (core * rest, 0), (ff_half, D))

        def down_chunk(slot):
            return lax.dynamic_slice(part_down, (net.owner(slot) * down_rows, 0), (down_rows, D))

        sum_down = net.ring_scatter([down_chunk(s) for s in range(chips)]).astype(bf16)

        def split_main(x):
            left = (x[:, :main], x[:, main:])
            right = (x[:, 2 * rest :], x[:, : 2 * rest])
            return (
                jnp.where(core == 0, left[0], right[0]),
                jnp.where(core == 0, left[1], right[1]),
            )

        gate_main, gate_tile = split_main(grad_gate_low)
        up_main, up_tile = split_main(grad_up_low)
        packed = jnp.concatenate(
            [gate_main, up_main, gate_tile + jnp.roll(up_tile, rest, 1)], 1
        )
        part_mlp = jnp.einsum(
            "td,tf->df", normed_two_group, packed, preferred_element_type=f32
        ).astype(bf16)

        def mlp_chunk(slot):
            return lax.dynamic_slice(
                part_mlp, (net.owner(slot) * mlp_rows, 0), (mlp_rows, 2 * ff_half)
            )

        sum_mlp = net.ring_scatter([mlp_chunk(s) for s in range(chips)]).astype(bf16)
        sum_mlp = lax.optimization_barrier(sum_mlp)
        grad_attn_low, grad_gain_two, grad_queries, row_sums, finish = attention_back()
        grad_pairs, marks = row_sums()
    pair_sent, grad_input, grad_gain_one, grad_bias = finish(grad_pairs)

    out_sum = mlp_chip[:rows]
    for s in range(1, net.dp):
        got = net.shift(mlp_chip[s * rows : (s + 1) * rows].astype(bf16), net.dp - s)
        out_sum = out_sum + got.astype(f32)
    output = (hidden + out_sum).astype(bf16)
    near = net.group_parts(jnp.concatenate([grad_attn_low, grad_queries, attended_low], 0))

    q_rows = w_qkv.shape[0] // 2
    qkv_cols = w_qkv.shape[1]
    if tiled:
        piece = q_rows * (qkv_cols + D) // chips // D
        terms_small = call(
            lambda *refs: small_grad_kernel(chips, q_rows, rows, qkv_cols, *refs),
            [jax.ShapeDtypeStruct((piece, D), bf16)] * chips,
            [spots, *early, *near],
            smem=1,
            scratch=[
                pltpu.VMEM((q_rows, qkv_cols + D), bf16),
                pltpu.VMEM((D, 2 * chip_rows), bf16),
            ],
            flops=4 * chip_rows * D * (qkv_cols + D),
        )
        block = call(
            block_kernel,
            [jax.ShapeDtypeStruct((sum_mlp.shape[0] + piece + down_rows, D), bf16)],
            [sum_mlp, sum_down] + net.ring_parts(terms_small)[0] + list(marks[3]),
            loose=2,
        )[0]
        part_pair = call(
            lambda *refs: pair_grad_kernel(rows, 2 * q_rows, *refs),
            [jax.ShapeDtypeStruct((2 * q_rows + SUM_ROWS, 2 * WIDTH_K), bf16)],
            [spots, early[0], pair_sent, net.shift(pair_sent, 1)],
            smem=1,
            scratch=[pltpu.VMEM((D, chip_rows), bf16)],
        )[0]
        sizes = (main, ff_loc, q_rows, qkv_cols, down_rows, chips)
        placed, pair_halves = net.gather_placed(
            block,
            lambda slots, pairs, old, rest=None: place_all(spots, slots, pairs, old, sizes, rest),
            net.exchange_start(part_pair),
            [[part_pair], [], []],
        )
        grad_gate, grad_up, grad_down, grad_joint, grad_out_proj = placed
        sums = jnp.where(core == 1, *pair_halves)[-SUM_ROWS:]
        small = sums.reshape(-1)[: 2 * D + qkv_cols].astype(f32)
    else:
        gathered = jnp.concatenate(near, 0).reshape(2 * net.dp, 3, rows, D)
        grad_attn_group = gathered[:, 0].reshape(2 * net.dp * rows, D)
        attended_group = gathered[:, 2].reshape(2 * net.dp * rows, D)
        normed_one_group = jnp.concatenate(early, 0)[:, D:]
        joint_group = net.group_gather(jnp.concatenate([grad_queries, pair_sent[:rows]], 1))
        q_first = net.d * (2 * q_rows) + core * q_rows
        group_rows = 2 * net.dp * rows
        part_out = jnp.einsum(
            "tc,td->cd",
            lax.dynamic_slice(attended_group, (0, q_first), (group_rows, q_rows)),
            grad_attn_group,
            preferred_element_type=f32,
        )
        part_joint = jnp.einsum(
            "td,tc->dc",
            lax.dynamic_slice(normed_one_group, (0, q_first), (group_rows, q_rows)),
            joint_group,
            preferred_element_type=f32,
        )
        part_small = jnp.concatenate([part_joint, part_out], 1).astype(bf16)
        small_cols = part_small.shape[1] // chips

        def small_chunk(slot):
            return lax.dynamic_slice(part_small, (0, net.owner(slot) * small_cols), (q_rows, small_cols))

        sum_small = net.ring_scatter([small_chunk(s) for s in range(chips)]).astype(bf16)

        tall = jnp.concatenate(
            [sum_small[:, i * 128 : (i + 1) * 128] for i in range(small_cols // 128)], 0
        )
        piece = tall.shape[0] // (D // 128)
        wide = jnp.concatenate([tall[i * piece : (i + 1) * piece] for i in range(D // 128)], 1)
        both = lax.optimization_barrier(jnp.concatenate([sum_down, wide], 0))

        owners = [net.owner(s) for s in range(chips)]
        got_mlp = net.ring_gather(sum_mlp)
        got_both = net.ring_gather(both)
        pairs_mlp = [(got, net.swap(got)) for got in got_mlp]
        pairs_both = [(got, net.swap(got)) for got in got_both]

        down_blocks, down_spots, small_blocks, small_spots = [], [], [], []
        for owner, pair in zip(owners, pairs_both):
            for which, got in zip((core, 1 - core), pair):
                down_blocks.append(got[:down_rows])
                down_spots.append((which * chips + owner, jnp.int32(0)))
                wide = got[down_rows:]
                tall = jnp.concatenate([wide[:, i * 128 : (i + 1) * 128] for i in range(D // 128)], 0)
                small_blocks.append(
                    jnp.concatenate(
                        [tall[i * q_rows : (i + 1) * q_rows] for i in range(small_cols // 128)], 1
                    )
                )
                small_spots.append((which, owner))
        grad_down = place_blocks(down_blocks, down_spots, (ff_loc, D))
        grad_small = place_blocks(small_blocks, small_spots, (2 * q_rows, part_small.shape[1]))
        grad_gate = jnp.zeros((D, ff_loc), f32)
        grad_up = jnp.zeros((D, ff_loc), f32)
        left_lane = jnp.arange(2 * rest) < rest
        for owner, (got, swapped) in zip(owners, pairs_mlp):
            zero = jnp.where(core == 0, got, swapped).astype(f32)
            one = jnp.where(core == 0, swapped, got).astype(f32)
            tile_zero, tile_one = zero[:, 2 * main :], one[:, 2 * main :]
            mid_gate = jnp.where(left_lane, tile_zero, tile_one)
            mid_up = jnp.roll(jnp.where(left_lane, tile_one, tile_zero), rest, 1)
            base = owner * mlp_rows
            grad_gate = lax.dynamic_update_slice(
                grad_gate, jnp.concatenate([zero[:, :main], mid_gate, one[:, :main]], 1), (base, 0)
            )
            grad_up = lax.dynamic_update_slice(
                grad_up,
                jnp.concatenate([zero[:, main : 2 * main], mid_up, one[:, main : 2 * main]], 1),
                (base, 0),
            )

        grad_joint, grad_out_proj = grad_small[:, :qkv_cols], grad_small[:, qkv_cols:]
        small = net.total(jnp.concatenate([grad_gain_one, grad_gain_two, grad_bias], 1))[0]
    return (
        output[None],
        grad_input[None],
        grad_joint,
        small[2 * D :],
        grad_out_proj,
        small[:D],
        small[D : 2 * D],
        grad_gate,
        grad_up,
        grad_down,
    )


def solution(mesh):
    placed = (
        P("dp", "ctx", None),
        P("dp", None),
        P(),
        P("dp", None),
        P(),
        P(),
        P(None, "dp"),
        P(None, "dp"),
        P("dp", None),
        P("dp", "ctx", None),
    )
    return jax.shard_map(
        local,
        mesh=mesh,
        in_specs=placed,
        out_specs=(
            P("dp", "ctx", None),
            P("dp", "ctx", None),
            P("dp", None),
            P(),
            P("dp", None),
            P(),
            P(),
            P(None, "dp"),
            P(None, "dp"),
            P("dp", None),
        ),
        check_vma=False,
    )
```
